32 devices in a mesh: dp: 8 (over z, x), row: 2 (over y), col: 2 (over core).
Axes of the slice: x: 2, y: 2, z: 4, core: 2. Of those that a mesh axis runs over, the one named last changes fastest.
Arguments:
- tokens_in: bfloat16 [8192, 1536], P(('dp', 'row'), 'col'), may hold values from -6 to 6
- norm_gain_attn: float32 [1536], P('col'), may hold values from 0.5 to 1.5
- w_query: bfloat16 [1536, 1536], P('col', 'row'), may hold values from -0.15625 to 0.15625
- w_key: bfloat16 [1536, 512], P('col', 'row'), may hold values from -0.15625 to 0.15625
- w_value: bfloat16 [1536, 512], P('col', 'row'), may hold values from -0.15625 to 0.15625
- w_out: bfloat16 [1536, 1536], P('row', 'col'), may hold values from -2.5 to 2.5
- norm_gain_ffn: float32 [1536], P('col'), may hold values from 0.5 to 1.5
- w_gate: bfloat16 [16, 1536, 512], P(None, 'col', 'row'), may hold values from -0.15625 to 0.15625
- w_up: bfloat16 [16, 1536, 512], P(None, 'col', 'row'), may hold values from -0.15625 to 0.15625
- w_down: bfloat16 [16, 512, 1536], P(None, 'row', 'col'), may hold values from -1 to 1
- w_shared_gate: bfloat16 [1536, 1024], P('col', 'row'), may hold values from -0.15625 to 0.15625
- w_shared_up: bfloat16 [1536, 1024], P('col', 'row'), may hold values from -0.15625 to 0.15625
- w_shared_down: bfloat16 [1024, 1536], P('row', 'col'), may hold values from -0.375 to 0.375
- routes: int32 [8192, 6], P('dp'), may hold values from 0 to 15, all different within a row; in each aligned block of 1024 rows (0 to 1023, 1024 to 2047, ...) at most 512 rows name the same one
- gate_weights: float32 [8192, 6], P('dp'), may hold values from 0.08 to 0.32
- seq_lengths: int32 [8], P('dp'), may hold values from 256 to 1024, as said below
- out_grad: bfloat16 [8192, 1536], P(('dp', 'row'), 'col'), may hold values from -6 to 6
Outputs:
- block_out: bfloat16 [8192, 1536], P(('dp', 'row'), 'col')
- tokens_grad: bfloat16 [8192, 1536], P(('dp', 'row'), 'col')
- gain_attn_grad: float32 [1536], P('col')
- query_grad: float32 [1536, 1536], P('col', 'row')
- key_grad: float32 [1536, 512], P('col', 'row')
- value_grad: float32 [1536, 512], P('col', 'row')
- out_proj_grad: float32 [1536, 1536], P('row', 'col')
- gain_ffn_grad: float32 [1536], P('col')
- gate_grad: float32 [16, 1536, 512], P(None, 'col', 'row')
- up_grad: float32 [16, 1536, 512], P(None, 'col', 'row')
- down_grad: float32 [16, 512, 1536], P(None, 'row', 'col')
- shared_gate_grad: float32 [1536, 1024], P('col', 'row')
- shared_up_grad: float32 [1536, 1024], P('col', 'row')
- shared_down_grad: float32 [1024, 1536], P('row', 'col')
The draws below stay inside these ranges and needn't reach their ends.
Inputs may be any that keep to these rules, and one draw needn't show every extreme that they name: `routes`: each row names 6 different experts; within each data shard's 1024 rows no expert is named by more than 512 rows, and that bound is reached. `seq_lengths`: keys at or past a sequence's length are masked; some sequence has the full 1024 and some has 256.
All inputs are finite; a program needn't handle non-finite values.
Results may differ from the reference program's by a relative error of at most 0.023.
Values may be sent and summed in bfloat16 or wider, within the bound.
No kernel may reach another device: no remote copies, remote signals or barrier semaphores. Data moves between devices by JAX's collectives and lax.ppermute only.
A program may use at most 384 MiB of HBM per device.

```python
import math
import jax
import jax.numpy as jnp
import numpy as np
from jax import lax

D = 1536
HQ = 12
HK = 4
DH = 128
H = 512
HS = 1024
TOP = 6
E = 16
SEQ = 1024
SEQ_GRP = 1
GROUP_TOKENS = 1024
CAP = 512
TOKENS = 8192
SEQS = 8
N_DP = 8


def draw_seq_lengths(key, part):
    key = jax.random.fold_in(key, 7)
    first_key, second_key = jax.random.split(key)
    lengths_drawn = jax.random.randint(first_key, (SEQS,), SEQ // 4, SEQ + 1, dtype=jnp.int32)
    shuffled = jax.random.permutation(second_key, SEQS)
    lengths_drawn = lengths_drawn.at[shuffled[0]].set(SEQ)
    return lengths_drawn.at[shuffled[1]].set(SEQ // 4)


def levels(stream_key, dims, pieces, low, high):
    factor_of, own = 1.0, jax.random.fold_in(stream_key, 6)
    for axis_at, blocks in pieces:
        draws = jnp.exp(jax.random.uniform(jax.random.fold_in(own, axis_at), (blocks,), jnp.float32, low / len(pieces), high / len(pieces)))
        factor_of = factor_of * jnp.repeat(draws, dims[axis_at] // blocks).reshape([-1 if axis == axis_at else 1 for axis in range(len(dims))])
    return factor_of


def routed_block(stream_key, own, number, rows, count, top, bound, skew):
    sequence = jax.random.permutation(stream_key, count)
    heavy_load, usual = load_shares(count, rows * top, bound, skew, True), load_shares(count, rows * top, bound, skew, False)
    places = jnp.arange(count)

    def named(sizes, rotation):
        used = int((sizes > 0).sum())
        fixed = max(1, used // 4)
        moved = fixed + (places - fixed + rotation * (used - fixed)) % max(1, count - fixed)
        return jnp.zeros((count,), jnp.int32).at[sequence[jnp.where(places < fixed, places, moved)]].set(jnp.asarray(sizes, jnp.int32))

    sizes = jnp.where(number % 4 == 0, named(heavy_load, number // 4), named(usual, number - number // 4 - 1))
    mixed = jax.random.permutation(jax.random.fold_in(own, 3), count)
    giver, receiver = mixed[0:count // 2 * 2:2], mixed[1:count // 2 * 2:2]
    room = jnp.minimum(sizes[giver] - 1, bound - sizes[receiver]) // 2
    room = jnp.where((giver == sequence[0]) | (receiver == sequence[0]) | (sizes[receiver] == 0), 0, jnp.maximum(room, 0))
    moved = jax.random.randint(jax.random.fold_in(own, 4), (count // 2,), 0, 1 << 20) % (room + 1)
    sizes = sizes.at[giver].add(-moved).at[receiver].add(moved)
    labels = jnp.searchsorted(jnp.cumsum(sizes), jnp.arange(rows * top), side="right").astype(jnp.int32)
    grid = labels.reshape(top, rows).T
    grid = grid[jax.random.permutation(jax.random.fold_in(own, 1), rows)]
    rotation = jax.random.randint(jax.random.fold_in(own, 2), (rows, 1), 0, top)
    return jnp.take_along_axis(grid, (jnp.arange(top)[None, :] + rotation) % top, axis=1)


def load_shares(count, total, most, lean, full):
    portions = [(1 << 20) // math.isqrt(standing ** lean) + 1 for standing in range(1, count + 1)]
    largest = most if full else min(most, max(-(-total // count), total * portions[0] // sum(portions)))
    least = 1 if total - largest >= count - 1 else 0
    counts, spare = [largest] + [least] * (count - 1), total - largest - least * (count - 1)
    while spare > 0:
        free = [i for i in range(1, count) if counts[i] < largest] or [i for i in range(1, count) if counts[i] < most]
        mass, left = sum([portions[i] for i in free]), spare
        for i in free:
            extra = min(most - counts[i], max(1, left * portions[i] // mass), spare)
            counts[i] = counts[i] + extra
            spare = spare - extra
    return np.array(counts)


def gaussian(stream_key, shape, deviation, reach, cuts=(), held_as=jnp.bfloat16):
    factor_of = levels(stream_key, shape, cuts, -0.22, 0.18) if cuts else 1.0
    values = jax.random.normal(stream_key, shape, jnp.float32) * deviation * factor_of
    return jnp.minimum(jnp.maximum(values, -reach), reach).astype(held_as)


def setup_inputs(seed: int = 0) -> dict:
    keys = jax.random.split(jax.random.key(seed), 18)
    tokens_in = gaussian(keys[0], (TOKENS, D), 1.0, 6.0, ((0, 16), (1, 2)))
    norm_gain_attn = jnp.clip(1.0 + 0.1 * jax.random.normal(keys[1], (D,), jnp.float32), 0.5, 1.5)
    w_query = gaussian(keys[2], (D, HQ * DH), D ** -0.5, 0.15625, ((0, 2), (1, 2)))
    w_key = gaussian(keys[3], (D, HK * DH), D ** -0.5, 0.15625, ((0, 2), (1, 2)))
    w_value = gaussian(keys[4], (D, HK * DH), D ** -0.5, 0.15625, ((0, 2), (1, 2)))
    w_out = gaussian(keys[5], (HQ * DH, D), (max(HQ * DH * 4 // SEQ, 1)) ** -0.5, 2.5, ((0, 2), (1, 2)))
    norm_gain_ffn = jnp.clip(1.0 + 0.1 * jax.random.normal(keys[6], (D,), jnp.float32), 0.5, 1.5)
    w_gate = gaussian(keys[7], (E, D, H), D ** -0.5, 0.15625, ((1, 2), (2, 2)))
    w_up = gaussian(keys[8], (E, D, H), D ** -0.5, 0.15625, ((1, 2), (2, 2)))
    w_down = gaussian(keys[9], (E, H, D), (H // 16) ** -0.5, 1.0, ((1, 2), (2, 2)))
    w_shared_gate = gaussian(keys[10], (D, HS), D ** -0.5, 0.15625, ((0, 2), (1, 2)))
    w_shared_up = gaussian(keys[11], (D, HS), D ** -0.5, 0.15625, ((0, 2), (1, 2)))
    w_shared_down = gaussian(keys[12], (HS, D), (HS // 4) ** -0.5, 0.375, ((0, 2), (1, 2)))
    routes_keys = jax.random.split(jax.random.fold_in(keys[13], 1), TOKENS // GROUP_TOKENS)
    routes_turns = jax.random.permutation(jax.random.fold_in(keys[13], 3), TOKENS // GROUP_TOKENS)
    routes = jax.vmap(lambda own, number: routed_block(jax.random.fold_in(keys[13], 2), own, number, GROUP_TOKENS, E, TOP, CAP, 1))(routes_keys, routes_turns).reshape((TOKENS, TOP))
    gate_weights = jnp.clip(jnp.exp(math.log(0.32) - 1.3862944 * jax.random.uniform(keys[14], (TOKENS, TOP), jnp.float32) ** levels(keys[14], (TOKENS, TOP), ((0, 8),), -0.2, 0.2)), 0.08, 0.32)
    seq_lengths = draw_seq_lengths(jax.random.fold_in(keys[17], 71), 0)
    out_grad = gaussian(keys[16], (TOKENS, D), 1.0, 6.0, ((0, 16), (1, 2)))
    return {"tokens_in": tokens_in, "norm_gain_attn": norm_gain_attn, "w_query": w_query, "w_key": w_key, "w_value": w_value, "w_out": w_out, "norm_gain_ffn": norm_gain_ffn, "w_gate": w_gate, "w_up": w_up, "w_down": w_down, "w_shared_gate": w_shared_gate, "w_shared_up": w_shared_up, "w_shared_down": w_shared_down, "routes": routes, "gate_weights": gate_weights, "seq_lengths": seq_lengths, "out_grad": out_grad}


EPSILON = 1e-05
HIGHEST = lax.Precision.HIGHEST

@jax.custom_vjp
def low(v):
    return lax.optimization_barrier(v.astype(jnp.bfloat16)).astype(jnp.float32)

@jax.custom_vjp
def low_back(v):
    return v

def low_keep(v):
    return (low(v), None)

def low_pass(kept, grad):
    return (grad,)

def back_keep(v):
    return (v, None)

def back_low(kept, grad):
    return (low(grad),)
low.defvjp(low_keep, low_pass)
low_back.defvjp(back_keep, back_low)

def matmul(left, right):
    return jnp.dot(left, right, precision=HIGHEST, preferred_element_type=jnp.float32)

def inverse_rms(values):
    return lax.rsqrt(lax.optimization_barrier(jnp.mean(values * values, axis=-1, keepdims=True)) + EPSILON)

def slot_table(routes):
    pair_experts = routes.reshape(-1)
    onehot = (pair_experts[:, None] == jnp.arange(E, dtype=jnp.int32)[None, :]).astype(jnp.int32)
    pair_ranks = lax.optimization_barrier(jnp.sum((jnp.cumsum(onehot, axis=0) - 1) * onehot, axis=1))
    pair_slots = pair_ranks * E + pair_experts
    owners = jnp.arange(pair_experts.shape[0], dtype=jnp.int32) // TOP
    holder = jnp.full((CAP * E,), GROUP_TOKENS, jnp.int32).at[pair_slots].set(owners)
    return (pair_slots.reshape(-1, TOP), holder)

def attention(queries, key_rows, value_rows, length):
    grouped = queries.reshape(SEQ, HK, HQ // HK, DH)
    scores = low_back(jnp.einsum('qgrd,kgd->grqk', grouped, key_rows, precision=HIGHEST) * DH ** (-0.5))
    position = jnp.arange(SEQ, dtype=jnp.int32)
    allowed = (position[None, :] <= position[:, None]) & (position[None, :] < length)
    scores = jnp.where(allowed, scores, -1e+30)
    highest = lax.optimization_barrier(jnp.max(scores, axis=-1, keepdims=True))
    weights = jnp.exp(scores - highest)
    key_probs = weights / lax.optimization_barrier(jnp.sum(weights, axis=-1, keepdims=True))
    attended = jnp.einsum('grqk,kgd->qgrd', low(key_probs), value_rows, precision=HIGHEST)
    return low(low_back(attended.reshape(SEQ, HQ * DH)))

def group_forward(params, group_parts):
    gain_attn, w_query, w_key, w_value, w_out, gain_ffn, w_gate, w_up, w_down, w_shared_gate, w_shared_up, w_shared_down = params
    tokens, routes, gates, lengths = group_parts
    normed = low(tokens * inverse_rms(tokens) * gain_attn)
    queries = low(low_back(matmul(normed, w_query)))
    key_rows = low(low_back(matmul(normed, w_key)))
    value_rows = low(low_back(matmul(normed, w_value)))
    attended = jax.vmap(attention)(queries.reshape(SEQ_GRP, SEQ, HQ, DH), key_rows.reshape(SEQ_GRP, SEQ, HK, DH), value_rows.reshape(SEQ_GRP, SEQ, HK, DH), lengths)
    hidden = tokens + low_back(matmul(attended.reshape(GROUP_TOKENS, HQ * DH), w_out))
    normed_ffn = low(hidden * inverse_rms(hidden) * gain_ffn)
    pair_slots, holder = slot_table(routes)
    padded = jnp.concatenate([normed_ffn, jnp.zeros((1, D), jnp.float32)], axis=0)
    dispatched = padded[holder].reshape(CAP, E, D)
    pre_gate = low_back(jnp.einsum('ced,edh->ceh', dispatched, w_gate, precision=HIGHEST))
    pre_up = low_back(jnp.einsum('ced,edh->ceh', dispatched, w_up, precision=HIGHEST))
    inner = low(jax.nn.silu(pre_gate) * pre_up)
    expert_out = low_back(jnp.einsum('ceh,ehd->ced', inner, w_down, precision=HIGHEST)).reshape(CAP * E, D)
    routed = lax.optimization_barrier(jnp.sum(gates[:, :, None] * expert_out[pair_slots], axis=1))
    shared_gate = low_back(matmul(normed_ffn, w_shared_gate))
    shared_up = low_back(matmul(normed_ffn, w_shared_up))
    shared_inner = low(jax.nn.silu(shared_gate) * shared_up)
    shared_out = low_back(matmul(shared_inner, w_shared_down))
    return hidden + routed + shared_out

def reference(tokens_in, norm_gain_attn, w_query, w_key, w_value, w_out, norm_gain_ffn, w_gate, w_up, w_down, w_shared_gate, w_shared_up, w_shared_down, routes, gate_weights, seq_lengths, out_grad):
    params = (norm_gain_attn.astype(jnp.float32), w_query.astype(jnp.float32), w_key.astype(jnp.float32), w_value.astype(jnp.float32), w_out.astype(jnp.float32), norm_gain_ffn.astype(jnp.float32), w_gate.astype(jnp.float32), w_up.astype(jnp.float32), w_down.astype(jnp.float32), w_shared_gate.astype(jnp.float32), w_shared_up.astype(jnp.float32), w_shared_down.astype(jnp.float32))
    tokens = tokens_in.astype(jnp.float32).reshape(N_DP, GROUP_TOKENS, D)
    route_groups = routes.reshape(N_DP, GROUP_TOKENS, TOP)
    gate_groups = gate_weights.astype(jnp.float32).reshape(N_DP, GROUP_TOKENS, TOP)
    length_groups = seq_lengths.reshape(N_DP, SEQ_GRP)
    checked = jax.checkpoint(group_forward)

    def whole_layer(tokens_all, params_all):
        return lax.map(lambda group_parts: checked(params_all, group_parts), (tokens_all, route_groups, gate_groups, length_groups))
    block_rows, pullback = jax.vjp(whole_layer, tokens, params)
    tokens_back, grads = pullback(out_grad.astype(jnp.float32).reshape(N_DP, GROUP_TOKENS, D))
    return (block_rows.reshape(TOKENS, D).astype(jnp.bfloat16), tokens_back.reshape(TOKENS, D).astype(jnp.bfloat16), grads[0], grads[1], grads[2], grads[3], grads[4], grads[5], grads[6], grads[7], grads[8], grads[9], grads[10], grads[11])
```

```python
import functools

import jax
import jax.numpy as jnp
from jax import lax
from jax.experimental import pallas as pl
from jax.experimental.pallas import tpu as pltpu
from jax.sharding import PartitionSpec as P

D = 1536
HQ = 12
HK = 4
DH = 128
GROUP_HEADS = HQ // HK
LANES = 128

EPSILON = 1e-05
F32 = jnp.float32
BF16 = jnp.bfloat16
VMEM_LIMIT = 56 * 1024 * 1024


def params(*semantics):
    return pltpu.CompilerParams(
        dimension_semantics=semantics or None, vmem_limit_bytes=VMEM_LIMIT
    )


def dot(left, right):
    return jnp.dot(left, right, preferred_element_type=F32)


def dot_nt(left, right):
    return lax.dot_general(left, right, (((1,), (1,)), ((), ())), preferred_element_type=F32)


def dot_tn(left, right):
    return lax.dot_general(left, right, (((0,), (0,)), ((), ())), preferred_element_type=F32)


def swap(values, axis):
    return lax.ppermute(values, axis, [(0, 1), (1, 0)])


def halves(values, axis, mine):
    size = values.shape[axis] // 2
    low = lax.slice_in_dim(values, 0, size, axis=axis)
    high = lax.slice_in_dim(values, size, 2 * size, axis=axis)
    return jnp.where(mine == 0, low, high), jnp.where(mine == 0, high, low)


def in_order(own, other, mine, axis):
    return jnp.concatenate(
        [jnp.where(mine == 0, own, other), jnp.where(mine == 0, other, own)], axis=axis
    )


def attend_kernel(place_ref, own_ref, other_ref, out_ref, all_ref):
    row = place_ref[0]
    length = place_ref[1]
    rows = own_ref.shape[0]
    all_ref[pl.ds(pl.multiple_of(row * rows, rows), rows), :] = own_ref[...]
    all_ref[pl.ds(pl.multiple_of((1 - row) * rows, rows), rows), :] = other_ref[...]
    block = 256
    width = GROUP_HEADS * DH
    for at in range(2 * rows // block):
        first, keys = at * block, (at + 1) * block
        query = jnp.concatenate(
            [
                all_ref[first : first + block, h * DH : (h + 1) * DH]
                for h in range(GROUP_HEADS)
            ],
            axis=0,
        )
        key = all_ref[0:keys, width : width + DH]
        value = all_ref[0:keys, width + DH : width + 2 * DH]
        scores = dot_nt(query, key) * DH ** (-0.5)
        shape = (block, keys)
        query_at = lax.broadcasted_iota(jnp.int32, shape, 0) + first
        key_at = lax.broadcasted_iota(jnp.int32, shape, 1)
        allowed = (key_at <= query_at) & (key_at < length)
        allowed = jnp.concatenate([allowed] * GROUP_HEADS, axis=0)
        scores = jnp.where(allowed, scores, -1e30)
        weights = jnp.exp(scores - jnp.max(scores, axis=1, keepdims=True))
        probs = weights * (1.0 / jnp.sum(weights, axis=1, keepdims=True))
        result = dot(probs.astype(BF16), value).astype(BF16)
        for h in range(GROUP_HEADS):
            out_ref[first : first + block, h * DH : (h + 1) * DH] = result[
                h * block : (h + 1) * block
            ]


def attend(place, own, other):
    rows, width = own.shape
    spec = pl.BlockSpec(memory_space=pltpu.VMEM)
    return pl.pallas_call(
        attend_kernel,
        out_shape=jax.ShapeDtypeStruct((2 * rows, GROUP_HEADS * DH), BF16),
        in_specs=[pl.BlockSpec(memory_space=pltpu.SMEM), spec, spec],
        out_specs=spec,
        scratch_shapes=[pltpu.VMEM((2 * rows, width), BF16)],
        compiler_params=params(),
        cost_estimate=pl.CostEstimate(
            flops=4 * 2 * rows * rows * width, bytes_accessed=8 * rows * width, transcendentals=0
        ),
        name="attend",
    )(place, own, other)


def attend_back(qkv, attended_grad, length):
    seq = qkv.shape[0]
    width = GROUP_HEADS * DH
    queries = qkv[:, :width].reshape(seq, GROUP_HEADS, DH)
    key, value = qkv[:, width : width + DH], qkv[:, width + DH :]
    grads = attended_grad.reshape(seq, GROUP_HEADS, DH)
    scale = DH ** (-0.5)
    scores = jnp.einsum("qrd,kd->rqk", queries, key, preferred_element_type=F32) * scale
    position = jnp.arange(seq, dtype=jnp.int32)
    allowed = (position[None, :] <= position[:, None]) & (position[None, :] < length)
    scores = jnp.where(allowed, scores, -1e30)
    weights = jnp.exp(scores - jnp.max(scores, axis=-1, keepdims=True))
    probs = weights / jnp.sum(weights, axis=-1, keepdims=True)
    probs_grad = jnp.einsum("qrd,kd->rqk", grads, value, preferred_element_type=F32)
    carried = jnp.sum(probs * probs_grad, axis=-1, keepdims=True)
    score_grad = (probs * (probs_grad - carried)).astype(BF16)
    query_back = jnp.einsum("rqk,kd->qrd", score_grad, key, preferred_element_type=F32) * scale
    key_back = jnp.einsum("rqk,qrd->kd", score_grad, queries, preferred_element_type=F32) * scale
    value_back = jnp.einsum(
        "rqk,qrd->kd", probs.astype(BF16), grads, preferred_element_type=F32
    )
    return jnp.concatenate(
        [query_back.reshape(seq, width), key_back, value_back], axis=1
    ).astype(BF16)


def hidden_kernel(tokens_ref, a0, a1, a2, a3, w0, w1, w2, w3, hidden_ref, square_ref):
    hidden = tokens_ref[...].astype(F32)
    for a, w in ((a0, w0), (a1, w1), (a2, w2), (a3, w3)):
        hidden = hidden + dot(a[...], w[...])
    hidden_ref[...] = hidden
    square_ref[...] = jnp.sum(hidden * hidden, axis=1, keepdims=True)


def hidden_rows(tokens, attended, weights):
    rows, features = tokens.shape
    heads = attended[0].shape[1]
    tile = 256

    def rowwise(width):
        return pl.BlockSpec((tile, width), lambda i: (i, 0))

    def whole(width):
        return pl.BlockSpec((width, features), lambda i: (0, 0))

    return pl.pallas_call(
        hidden_kernel,
        grid=(rows // tile,),
        out_shape=(
            jax.ShapeDtypeStruct((rows, features), F32),
            jax.ShapeDtypeStruct((rows, 1), F32),
        ),
        in_specs=[rowwise(features)] + [rowwise(heads)] * 4 + [whole(heads)] * 4,
        out_specs=(rowwise(features), rowwise(1)),
        compiler_params=params("arbitrary"),
        cost_estimate=pl.CostEstimate(
            flops=8 * rows * features * heads,
            bytes_accessed=10 * rows * features,
            transcendentals=0,
        ),
        name="hidden_rows",
    )(tokens, *attended, *weights)


def expert_kernel(routed, order_ref, *refs):
    (x_own, x_other, x_turned, o_own, o_other, routes, gates) = refs[:7]
    weights = refs[7:15]
    grads = refs[15:17]
    pair_refs = refs[17:19]
    inner_refs = refs[19:21]
    step = pl.program_id(0)
    rows = x_own.shape[0]
    features = x_own.shape[1]
    tile = 256
    up_own = jnp.concatenate([weights[0][0], weights[4][0]], axis=1)
    up_other = jnp.concatenate([weights[1][0], weights[5][0]], axis=1)
    down_own = jnp.concatenate([weights[2][0], weights[6][0]], axis=0)
    down_other = jnp.concatenate([weights[3][0], weights[7][0]], axis=0)

    def token_tile(t, carry):
        at = pl.ds(pl.multiple_of(t * tile, tile), tile)
        pre = dot(x_own[at, :], up_own) + dot(x_other[at, :], up_other)
        back = dot_nt(o_own[at, :], down_own) + dot_nt(o_other[at, :], down_other)
        for k in range(2):
            expert = order_ref[2 * step + k]
            chosen = jnp.where(routes[at, :] == expert, gates[at, :], 0.0)
            gate = jnp.sum(chosen, axis=1, keepdims=True)
            gate = jnp.where(expert >= routed, 1.0, gate)
            pre_gate = pre[:, 2 * k * LANES : (2 * k + 1) * LANES]
            pre_up = pre[:, (2 * k + 1) * LANES : (2 * k + 2) * LANES]
            inner_grad = gate * back[:, k * LANES : (k + 1) * LANES]
            sigmoid = 1.0 / (1.0 + jnp.exp(-pre_gate))
            silu = pre_gate * sigmoid
            inner_refs[k][0, at, :] = (gate * (silu * pre_up)).astype(BF16)
            gate_grad = inner_grad * pre_up * (sigmoid * (1.0 + pre_gate * (1.0 - sigmoid)))
            pair_refs[k][0, at, 0:LANES] = gate_grad.astype(BF16)
            pair_refs[k][0, at, LANES : 2 * LANES] = (inner_grad * silu).astype(BF16)
        return carry

    lax.fori_loop(0, rows // tile, token_tile, 0)
    for k in range(2):
        pairs = pair_refs[k][0]

        def feature_tile(t, carry, k=k, pairs=pairs):
            at = pl.ds(pl.multiple_of(t * tile, tile), tile)
            grads[k][0, at, 0 : 2 * LANES] = dot(x_turned[at, :], pairs).astype(BF16)
            return carry

        lax.fori_loop(0, 2 * features // tile, feature_tile, 0)
    inner = jnp.concatenate([inner_refs[0][0], inner_refs[1][0]], axis=1)
    turned = inner.T
    for h, o in enumerate((o_own, o_other)):
        for j in range(features // tile):
            down = dot(turned, o[:, j * tile : (j + 1) * tile]).astype(BF16)
            for k in range(2):
                for b in range(tile // LANES):
                    at = h * features + j * tile + b * LANES
                    grads[k][0, at : at + LANES, 2 * LANES :] = down[
                        k * LANES : (k + 1) * LANES, b * LANES : (b + 1) * LANES
                    ]


def expert_grads(routed, order, x_own, x_other, x_turned, o_own, o_other, routes, gates, weights):
    steps = order.shape[0] // 2
    rows, features = x_own.shape
    choices = routes.shape[1]
    hidden = weights[2].shape[1]

    def fixed(*shape):
        return pl.BlockSpec(shape, lambda i, o: (0,) * len(shape))

    def picked(k, *shape):
        return pl.BlockSpec((1, *shape), lambda i, o: (o[2 * i + k], 0, 0))

    def stepped(*shape):
        return pl.BlockSpec((1, *shape), lambda i, o: (i, 0, 0))

    weight_specs = []
    for k in range(2):
        weight_specs += [
            picked(k, features, 2 * hidden),
            picked(k, features, 2 * hidden),
            picked(k, hidden, features),
            picked(k, hidden, features),
        ]
    return pl.pallas_call(
        functools.partial(expert_kernel, routed),
        grid_spec=pltpu.PrefetchScalarGridSpec(
            num_scalar_prefetch=1,
            grid=(steps,),
            in_specs=[
                fixed(rows, features),
                fixed(rows, features),
                fixed(2 * features, rows),
                fixed(rows, features),
                fixed(rows, features),
                fixed(rows, choices),
                fixed(rows, choices),
            ]
            + weight_specs,
            out_specs=[stepped(2 * features, 3 * hidden)] * 2
            + [stepped(rows, 2 * hidden)] * 2
            + [stepped(rows, hidden)] * 2,
        ),
        out_shape=[jax.ShapeDtypeStruct((steps, 2 * features, 3 * hidden), BF16)] * 2
        + [jax.ShapeDtypeStruct((steps, rows, 2 * hidden), BF16)] * 2
        + [jax.ShapeDtypeStruct((steps, rows, hidden), BF16)] * 2,
        compiler_params=params("arbitrary"),
        cost_estimate=pl.CostEstimate(
            flops=steps * 24 * rows * features * hidden * 2,
            bytes_accessed=12 * rows * features + steps * 12 * features * hidden * 2,
            transcendentals=0,
        ),
        name="expert_grads",
    )(order, x_own, x_other, x_turned, o_own, o_other, routes, gates, *weights, *weights)


def combine_kernel(order_ref, *refs):
    pairs = refs[0:2]
    inners = refs[2:4]
    weights = refs[4:12]
    out_own, out_other, back_own, back_other = refs[12:16]
    step = pl.program_id(0)
    rows, features = out_own.shape
    tile = 256
    up = [
        jnp.concatenate([weights[h][0], weights[4 + h][0]], axis=1) for h in range(2)
    ]
    down = [
        jnp.concatenate([weights[2 + h][0], weights[6 + h][0]], axis=0) for h in range(2)
    ]

    def token_tile(t, carry):
        at = pl.ds(pl.multiple_of(t * tile, tile), tile)
        pair = jnp.concatenate([pairs[0][0, at, :], pairs[1][0, at, :]], axis=1)
        inner = jnp.concatenate([inners[0][0, at, :], inners[1][0, at, :]], axis=1)
        for h, (out, back) in enumerate(((out_own, back_own), (out_other, back_other))):
            out_term = dot(inner, down[h])
            back_term = dot_nt(pair, up[h])

            @pl.when(step == 0)
            def _():
                out[at, :] = out_term
                back[at, :] = back_term

            @pl.when(step > 0)
            def _():
                out[at, :] += out_term
                back[at, :] += back_term

        return carry

    lax.fori_loop(0, rows // tile, token_tile, 0)


def combine(order, pairs, inners, weights):
    steps, rows, double = pairs[0].shape
    hidden = double // 2
    features = weights[0].shape[1]

    def picked(k, *shape):
        return pl.BlockSpec((1, *shape), lambda i, o: (o[2 * i + k], 0, 0))

    def stepped(*shape):
        return pl.BlockSpec((1, *shape), lambda i, o: (i, 0, 0))

    weight_specs = []
    for k in range(2):
        weight_specs += [
            picked(k, features, 2 * hidden),
            picked(k, features, 2 * hidden),
            picked(k, hidden, features),
            picked(k, hidden, features),
        ]
    return pl.pallas_call(
        combine_kernel,
        grid_spec=pltpu.PrefetchScalarGridSpec(
            num_scalar_prefetch=1,
            grid=(steps,),
            in_specs=[stepped(rows, 2 * hidden)] * 2
            + [stepped(rows, hidden)] * 2
            + weight_specs,
            out_specs=[pl.BlockSpec((rows, features), lambda i, o: (0, 0))] * 4,
        ),
        out_shape=[jax.ShapeDtypeStruct((rows, features), F32)] * 4,
        compiler_params=params("arbitrary"),
        cost_estimate=pl.CostEstimate(
            flops=steps * 24 * rows * features * hidden,
            bytes_accessed=16 * rows * features,
            transcendentals=0,
        ),
        name="combine",
    )(order, *pairs, *inners, *weights, *weights)


def ring_of(size):
    return list(range(0, size, 2)) + list(range(1, size, 2))[::-1]


def unpack_kernel(aliased, index_ref, *refs):
    right_ref, left_ref = refs[0:2]
    gate_ref, up_ref, down_ref = refs[2 + aliased : 5 + aliased]
    blocks = right_ref.shape[1] // LANES

    def write(chunk_ref):
        for c in range(2):
            base = 3 * LANES * c
            to = slice(c * LANES, (c + 1) * LANES)
            gate_ref[0, :, to] = chunk_ref[0, :, base : base + LANES].astype(F32)
            up_ref[0, :, to] = chunk_ref[0, :, base + LANES : base + 2 * LANES].astype(F32)
            for b in range(blocks):
                down_ref[0, to, b * LANES : (b + 1) * LANES] = chunk_ref[
                    0, b * LANES : (b + 1) * LANES, base + 2 * LANES : base + 3 * LANES
                ].astype(F32)

    pl.when(pl.program_id(1) == 0)(lambda: write(right_ref))
    pl.when(pl.program_id(1) == 1)(lambda: write(left_ref))


def unpack(index, right, left, shapes, outs):
    count, rows, width = right.shape
    chunk = pl.BlockSpec((1, rows, width), lambda i, d, n: (i, 0, 0))

    def placed(shape):
        return pl.BlockSpec((1, *shape[1:]), lambda i, d, n: (n[2 * i + d], 0, 0))

    aliased = len(outs)
    return pl.pallas_call(
        functools.partial(unpack_kernel, aliased),
        grid_spec=pltpu.PrefetchScalarGridSpec(
            num_scalar_prefetch=1,
            grid=(count, 2),
            in_specs=[chunk, chunk] + [pl.BlockSpec(memory_space=pl.ANY)] * aliased,
            out_specs=[placed(shape) for shape in shapes],
        ),
        out_shape=[jax.ShapeDtypeStruct(shape, F32) for shape in shapes],
        input_output_aliases={3 + k: k for k in range(aliased)},
        compiler_params=params("arbitrary", "arbitrary"),
        cost_estimate=pl.CostEstimate(
            flops=0, bytes_accessed=count * rows * width * 12, transcendentals=0
        ),
        name="unpack",
    )(index, right, left, *outs)


def add_rounded(left, right):
    return (left.astype(F32) + right.astype(F32)).astype(BF16)


def body(
    tokens_in,
    norm_gain_attn,
    w_query,
    w_key,
    w_value,
    w_out,
    norm_gain_ffn,
    w_gate,
    w_up,
    w_down,
    w_shared_gate,
    w_shared_up,
    w_shared_down,
    routes,
    gate_weights,
    seq_lengths,
    out_grad,
):
    row = lax.axis_index("row")
    col = lax.axis_index("col")
    dp = lax.axis_index("dp")
    dp_size = lax.axis_size("dp")
    local_rows, local_features = tokens_in.shape
    experts = w_gate.shape[0]
    hidden_part = w_gate.shape[2] // 2
    group_width = GROUP_HEADS * DH

    ring_size = min(8, dp_size)
    ring = ring_of(ring_size)
    starts = range(0, dp_size, ring_size)
    to_right = [
        (g + ring[k], g + ring[(k + 1) % ring_size]) for g in starts for k in range(ring_size)
    ]
    to_left = [(b, a) for a, b in to_right]
    place_of = [ring.index(k) for k in range(ring_size)]
    place = jnp.asarray(place_of, jnp.int32)[dp % ring_size]
    peers = [[g + k for g in starts] for k in range(ring_size)]

    def across_rings(values):
        if len(starts) == 1:
            return values
        return lax.psum(values, "dp", axis_index_groups=peers)

    def send(values, left):
        if ring_size == 1:
            return values
        return lax.ppermute(values, "dp", to_left if left else to_right)

    tokens_y = swap(tokens_in, "row")
    tokens_c = swap(tokens_in, "col")
    gains = jnp.stack([norm_gain_attn, norm_gain_ffn])
    gains_c = swap(gains, "col")

    query_own, query_send = halves(w_query, 1, col)
    key_own, key_send = halves(w_key, 1, col)
    value_own, value_send = halves(w_value, 1, col)
    project_own = jnp.concatenate([query_own, key_own, value_own], axis=1)
    project_other = swap(jnp.concatenate([query_send, key_send, value_send], axis=1), "col")

    def project(own, other):
        own, other = own.astype(F32), other.astype(F32)
        total = jnp.sum(own * own, axis=1) + jnp.sum(other * other, axis=1)
        scale = lax.rsqrt(total / D + EPSILON)[:, None]
        own = (own * scale * gains[0]).astype(BF16)
        other = (other * scale * gains_c[0]).astype(BF16)
        qkv = (dot(own, project_own) + dot(other, project_other)).astype(BF16)
        return own, other, qkv, scale

    tokens_yc = swap(tokens_y, "col")
    near = project(tokens_in, tokens_c)
    far = project(tokens_y, tokens_yc)
    grad_y = swap(out_grad, "row")
    grad_own = in_order(out_grad, grad_y, row, 0)
    grad_other = swap(grad_own, "col")

    gate_own, gate_send = halves(w_gate, 2, col)
    up_own, up_send = halves(w_up, 2, col)
    down_own, down_send = halves(w_down, 1, col)
    sgate_own, sgate_send = halves(w_shared_gate, 1, col)
    sup_own, sup_send = halves(w_shared_up, 1, col)
    sdown_own, sdown_send = halves(w_shared_down, 0, col)
    shared_blocks = sgate_own.shape[1] // hidden_part

    def blocks(values):
        return values.reshape(local_features, shared_blocks, hidden_part).transpose(1, 0, 2)

    def down_blocks(values):
        return values.reshape(shared_blocks, hidden_part, local_features)

    def widen(gate, up, shared_gate, shared_up):
        return jnp.concatenate(
            [
                jnp.concatenate([gate, up], axis=2),
                jnp.concatenate([blocks(shared_gate), blocks(shared_up)], axis=2),
            ],
            axis=0,
        )

    up_mine = widen(gate_own, up_own, sgate_own, sup_own)
    up_theirs = swap(widen(gate_send, up_send, sgate_send, sup_send), "col")
    down_mine = jnp.concatenate([down_own, down_blocks(sdown_own)], axis=0)
    down_theirs = swap(jnp.concatenate([down_send, down_blocks(sdown_send)], axis=0), "col")
    expert_weights = [up_mine, up_theirs, down_mine, down_theirs]

    where = jnp.stack([row, seq_lengths[0]])
    attended = attend(where, near[2], far[2])
    attended_y = swap(attended, "row")
    attended_c = swap(attended, "col")
    attended_yc = swap(attended_y, "col")
    out_own, out_other = halves(w_out, 0, col)
    out_y_own, out_y_other = halves(swap(w_out, "row"), 0, col)
    tokens = in_order(tokens_in, tokens_y, row, 0)
    hidden, squares = hidden_rows(
        tokens,
        [attended, attended_c, attended_y, attended_yc],
        [out_own, out_other, out_y_own, out_y_other],
    )
    squares = squares + swap(squares, "col")
    scale_ffn = lax.rsqrt(squares / D + EPSILON)
    x_own = (hidden * scale_ffn * norm_gain_ffn).astype(BF16)
    x_other = swap(x_own, "col")
    x_turned = jnp.concatenate([x_own.T, x_other.T], axis=0)

    each = experts // (2 * ring_size)
    orders = []
    for s in range(ring_size):
        right = (place - s) % ring_size
        left = (place + s) % ring_size
        for k in range(each):
            orders.append(2 * each * right + k)
            orders.append(2 * each * left + each + k)
    for k in range(shared_blocks):
        orders.append(jnp.int32(experts + k))
    order = jnp.stack(orders).astype(jnp.int32)

    def run(first, last):
        return expert_grads(
            experts,
            order[2 * first : 2 * last],
            x_own,
            x_other,
            x_turned,
            grad_own,
            grad_other,
            routes,
            gate_weights,
            expert_weights,
        )

    pairs_total = (experts + shared_blocks) // 2
    cuts = [0] + list(range(each, pairs_total, 2 * each)) + [pairs_total]
    runs = [run(a, b) for a, b in zip(cuts[:-1], cuts[1:], strict=True)]

    def part(which, first, count):
        for a, b, result in zip(cuts[:-1], cuts[1:], runs, strict=True):
            if a <= first and first + count <= b:
                return result[which][first - a : first - a + count]
        raise ValueError

    sums = []
    for left in range(2):
        total = part(left, 0, each)
        for s in range(1, ring_size):
            total = add_rounded(send(total, left), part(left, s * each, each))
        total = across_rings(total)
        mine = total[:, :local_features]
        theirs = swap(total[:, local_features:], "col")
        sums.append(in_order(mine, theirs, col, 2))

    expert_shapes = [w_gate.shape, w_up.shape, w_down.shape]
    expert_outs = ()
    right, left = sums
    for s in range(ring_size):
        at_right = (place + 1 - s) % ring_size
        at_left = (place - 1 + s) % ring_size
        index = []
        for k in range(each):
            index.append(2 * each * at_right + k)
            index.append(2 * each * at_left + each + k)
        expert_outs = unpack(
            jnp.stack(index).astype(jnp.int32), right, left, expert_shapes, expert_outs
        )
        if s + 1 < ring_size:
            right, left = send(right, 0), send(left, 1)
    gate_grad, up_grad, down_grad = expert_outs

    joined = [jnp.concatenate([result[k] for result in runs], axis=0) for k in range(2, 6)]
    sum_own, sum_other, back_own, back_other = combine(
        order, joined[0:2], joined[2:4], expert_weights
    )
    start = row * local_rows

    def my_rows(values):
        return lax.dynamic_slice_in_dim(values, start, local_rows, axis=0)

    def their_rows(values):
        return lax.dynamic_slice_in_dim(values, local_rows - start, local_rows, axis=0)

    ffn_sum = sum_own + swap(sum_other.astype(BF16), "col").astype(F32)
    ffn_rows = my_rows(ffn_sum) + swap(their_rows(ffn_sum).astype(BF16), "row").astype(F32)
    block_out = (my_rows(hidden) + ffn_rows).astype(BF16)

    normed_grad = back_own + swap(back_other.astype(BF16), "col").astype(F32)
    normed_grad = normed_grad + swap(normed_grad.astype(BF16), "row").astype(F32)
    gain_ffn_part = jnp.sum(my_rows(normed_grad * hidden * scale_ffn), axis=0)
    scaled = normed_grad * norm_gain_ffn
    products = jnp.sum(scaled * hidden, axis=1, keepdims=True)
    mean = (products + swap(products, "col")) / D
    hidden_grad = grad_own.astype(F32) + scale_ffn * scaled - hidden * scale_ffn**3 * mean
    attn_grad = hidden_grad.astype(BF16)
    attn_grad_c = swap(attn_grad, "col")

    out_back = swap(out_other, "col")
    attended_grad = (dot_nt(attn_grad, out_own) + dot_nt(attn_grad_c, out_back)).astype(BF16)
    out_grads = [dot_tn(attended, attn_grad), dot_tn(attended, attn_grad_c)]
    qkv = in_order(near[2], far[2], row, 0)
    qkv_grad = attend_back(qkv, attended_grad, seq_lengths[0])
    normed_own = in_order(near[0], far[0], row, 0)
    normed_other = in_order(near[1], far[1], row, 0)
    project_grads = [dot_tn(normed_own, qkv_grad), dot_tn(normed_other, qkv_grad)]
    tokens_back = dot_nt(qkv_grad, project_own)
    tokens_back = tokens_back + swap(
        dot_nt(qkv_grad, project_other).astype(BF16), "col"
    ).astype(F32)
    tokens_back = my_rows(tokens_back) + swap(
        their_rows(tokens_back).astype(BF16), "row"
    ).astype(F32)
    scale_attn = near[3]
    tokens_f32 = tokens_in.astype(F32)
    gain_attn_part = jnp.sum(tokens_back * tokens_f32 * scale_attn, axis=0)
    scaled = tokens_back * norm_gain_attn
    products = jnp.sum(scaled * tokens_f32, axis=1, keepdims=True)
    mean = (products + swap(products, "col")) / D
    tokens_grad = (
        my_rows(hidden_grad) + scale_attn * scaled - tokens_f32 * scale_attn**3 * mean
    ).astype(BF16)
    gain_attn_grad, gain_ffn_grad = lax.psum((gain_attn_part, gain_ffn_part), ("dp", "row"))

    share = local_features // ring_size
    shared_grads = jnp.concatenate([runs[-1][k][-1:] for k in range(2)], axis=0)
    shared_pack = shared_grads.reshape(shared_blocks, 2, ring_size, share, 3 * hidden_part)
    shared_pack = shared_pack.transpose(2, 1, 3, 0, 4).reshape(ring_size, 2, share, -1)
    project_pack = jnp.stack([g.astype(BF16) for g in project_grads])
    project_pack = project_pack.reshape(2, ring_size, share, -1).transpose(1, 0, 2, 3)
    out_pack = jnp.stack([g.astype(BF16) for g in out_grads])
    out_share = group_width // ring_size
    out_pack = out_pack.reshape(2, ring_size, out_share, 2, local_features // 2)
    out_pack = out_pack.transpose(1, 0, 3, 2, 4).reshape(ring_size, 2, share, -1)
    pack = jnp.concatenate([shared_pack, project_pack, out_pack], axis=3)
    middle = pack.shape[3] // 2
    finals = []
    for left in range(2):
        lanes = pack[..., middle:] if left else pack[..., :middle]

        def chunk(s, left=left, lanes=lanes):
            at = (place + s if left else place - s) % ring_size
            return lax.dynamic_index_in_dim(lanes, at, axis=0, keepdims=False)

        total = chunk(0)
        for s in range(1, ring_size):
            total = add_rounded(send(total, left), chunk(s))
        total = across_rings(total)
        current = jnp.stack([total[0], swap(total[1], "col")])
        final = jnp.zeros((ring_size, *current.shape), BF16)
        for s in range(ring_size):
            at = (place - 1 + s if left else place + 1 - s) % ring_size
            final = lax.dynamic_update_index_in_dim(final, current, at, 0)
            if s + 1 < ring_size:
                current = send(current, left)
        finals.append(final)
    final = jnp.concatenate(finals, axis=3)
    final = in_order(final[:, 0:1], final[:, 1:2], col, 1).astype(F32)
    lanes_shared = shared_blocks * 3 * hidden_part
    lanes_project = project_grads[0].shape[1]
    shared_final = final[..., :lanes_shared].reshape(
        ring_size, 2, share, shared_blocks, 3, hidden_part
    )

    def shared_up(which):
        picked = shared_final[:, :, :, :, which]
        return picked.transpose(0, 2, 1, 3, 4).reshape(local_features, -1)

    shared_gate_grad = shared_up(0)
    shared_up_grad = shared_up(1)
    down_final = shared_final[:, :, :, :, 2].transpose(1, 3, 0, 2, 4)
    down_final = down_final.reshape(
        2, shared_blocks, local_features // LANES, hidden_part, LANES
    )
    shared_down_grad = down_final.transpose(0, 1, 3, 2, 4).reshape(-1, local_features)
    project_final = final[..., lanes_shared : lanes_shared + lanes_project]
    project_final = project_final.transpose(0, 2, 1, 3).reshape(local_features, 2, -1)
    query_grad = project_final[:, :, :group_width].reshape(local_features, -1)
    key_grad = project_final[:, :, group_width : group_width + DH].reshape(local_features, -1)
    value_grad = project_final[:, :, group_width + DH :].reshape(local_features, -1)
    out_final = final[..., lanes_shared + lanes_project :]
    out_final = out_final.reshape(ring_size, 2, 2, out_share, local_features // 2)
    out_proj_grad = out_final.transpose(1, 0, 3, 2, 4).reshape(-1, local_features)

    return (
        block_out,
        tokens_grad,
        gain_attn_grad,
        query_grad,
        key_grad,
        value_grad,
        out_proj_grad,
        gain_ffn_grad,
        gate_grad,
        up_grad,
        down_grad,
        shared_gate_grad,
        shared_up_grad,
        shared_down_grad,
    )


def solution(mesh):
    in_specs = (
        P(("dp", "row"), "col"),
        P("col"),
        P("col", "row"),
        P("col", "row"),
        P("col", "row"),
        P("row", "col"),
        P("col"),
        P(None, "col", "row"),
        P(None, "col", "row"),
        P(None, "row", "col"),
        P("col", "row"),
        P("col", "row"),
        P("row", "col"),
        P("dp", None),
        P("dp", None),
        P("dp"),
        P(("dp", "row"), "col"),
    )
    out_specs = (
        P(("dp", "row"), "col"),
        P(("dp", "row"), "col"),
        P("col"),
        P("col", "row"),
        P("col", "row"),
        P("col", "row"),
        P("row", "col"),
        P("col"),
        P(None, "col", "row"),
        P(None, "col", "row"),
        P(None, "row", "col"),
        P("col", "row"),
        P("col", "row"),
        P("row", "col"),
    )
    return jax.shard_map(body, mesh=mesh, in_specs=in_specs, out_specs=out_specs, check_vma=False)
```

```python
import functools

import jax
import jax.numpy as jnp
from jax import lax
from jax.experimental import pallas as pl
from jax.experimental.pallas import tpu as pltpu
from jax.sharding import PartitionSpec as P

D = 1536
HQ = 12
HK = 4
DH = 128
GROUP_HEADS = HQ // HK
LANES = 128

EPSILON = 1e-05
F32 = jnp.float32
BF16 = jnp.bfloat16
VMEM_LIMIT = 56 * 1024 * 1024
SMALL = pl.CostEstimate(flops=0, bytes_accessed=0, transcendentals=0)


def params(*semantics):
    return pltpu.CompilerParams(
        dimension_semantics=semantics or None, vmem_limit_bytes=VMEM_LIMIT
    )


def dot(left, right):
    return jnp.dot(left, right, preferred_element_type=F32)


def dot_nt(left, right):
    return lax.dot_general(left, right, (((1,), (1,)), ((), ())), preferred_element_type=F32)


def dot_tn(left, right):
    return lax.dot_general(left, right, (((0,), (0,)), ((), ())), preferred_element_type=F32)


def after(values, *others):
    return lax.optimization_barrier((values, *others))[0]


def swap(values, axis):
    return lax.ppermute(values, axis, [(0, 1), (1, 0)])


def halves(values, axis, mine):
    size = values.shape[axis] // 2
    low = lax.slice_in_dim(values, 0, size, axis=axis)
    high = lax.slice_in_dim(values, size, 2 * size, axis=axis)
    return jnp.where(mine == 0, low, high), jnp.where(mine == 0, high, low)


def in_order(own, other, mine, axis):
    return jnp.concatenate(
        [jnp.where(mine == 0, own, other), jnp.where(mine == 0, other, own)], axis=axis
    )


def attend_kernel(place_ref, own_ref, other_ref, out_ref, all_ref):
    row = place_ref[0]
    length = place_ref[1]
    rows = own_ref.shape[0]
    all_ref[pl.ds(pl.multiple_of(row * rows, rows), rows), :] = own_ref[...]
    all_ref[pl.ds(pl.multiple_of((1 - row) * rows, rows), rows), :] = other_ref[...]
    block = 256
    width = GROUP_HEADS * DH
    for at in range(2 * rows // block):
        first, keys = at * block, (at + 1) * block
        query = jnp.concatenate(
            [
                all_ref[first : first + block, h * DH : (h + 1) * DH]
                for h in range(GROUP_HEADS)
            ],
            axis=0,
        )
        key = all_ref[0:keys, width : width + DH]
        value = all_ref[0:keys, width + DH : width + 2 * DH]
        scores = dot_nt(query, key) * DH ** (-0.5)
        shape = (block, keys)
        query_at = lax.broadcasted_iota(jnp.int32, shape, 0) + first
        key_at = lax.broadcasted_iota(jnp.int32, shape, 1)
        allowed = (key_at <= query_at) & (key_at < length)
        allowed = jnp.concatenate([allowed] * GROUP_HEADS, axis=0)
        scores = jnp.where(allowed, scores, -1e30)
        weights = jnp.exp(scores - jnp.max(scores, axis=1, keepdims=True))
        probs = weights * (1.0 / jnp.sum(weights, axis=1, keepdims=True))
        result = dot(probs.astype(BF16), value).astype(BF16)
        for h in range(GROUP_HEADS):
            out_ref[first : first + block, h * DH : (h + 1) * DH] = result[
                h * block : (h + 1) * block
            ]


def attend(place, own, other):
    rows, width = own.shape
    spec = pl.BlockSpec(memory_space=pltpu.VMEM)
    return pl.pallas_call(
        attend_kernel,
        out_shape=jax.ShapeDtypeStruct((2 * rows, GROUP_HEADS * DH), BF16),
        in_specs=[pl.BlockSpec(memory_space=pltpu.SMEM), spec, spec],
        out_specs=spec,
        scratch_shapes=[pltpu.VMEM((2 * rows, width), BF16)],
        compiler_params=params(),
        cost_estimate=SMALL,
        name="attend",
    )(place, own, other)


def attend_back(qkv, attended_grad, length):
    seq = qkv.shape[0]
    width = GROUP_HEADS * DH
    queries = qkv[:, :width].reshape(seq, GROUP_HEADS, DH)
    key, value = qkv[:, width : width + DH], qkv[:, width + DH :]
    grads = attended_grad.reshape(seq, GROUP_HEADS, DH)
    scale = DH ** (-0.5)
    scores = jnp.einsum("qrd,kd->rqk", queries, key, preferred_element_type=F32) * scale
    position = jnp.arange(seq, dtype=jnp.int32)
    allowed = (position[None, :] <= position[:, None]) & (position[None, :] < length)
    scores = jnp.where(allowed, scores, -1e30)
    weights = jnp.exp(scores - jnp.max(scores, axis=-1, keepdims=True))
    probs = weights / jnp.sum(weights, axis=-1, keepdims=True)
    probs_grad = jnp.einsum("qrd,kd->rqk", grads, value, preferred_element_type=F32)
    carried = jnp.sum(probs * probs_grad, axis=-1, keepdims=True)
    score_grad = (probs * (probs_grad - carried)).astype(BF16)
    query_back = jnp.einsum("rqk,kd->qrd", score_grad, key, preferred_element_type=F32) * scale
    key_back = jnp.einsum("rqk,qrd->kd", score_grad, queries, preferred_element_type=F32) * scale
    value_back = jnp.einsum(
        "rqk,qrd->kd", probs.astype(BF16), grads, preferred_element_type=F32
    )
    return jnp.concatenate(
        [query_back.reshape(seq, width), key_back, value_back], axis=1
    ).astype(BF16)


def project_kernel(col_ref, own_ref, other_ref, gains_ref, gains_c_ref, query_ref, key_ref, value_ref, there_ref, x_own_ref, x_other_ref, qkv_ref, scale_ref):
    own = own_ref[...].astype(F32)
    other = other_ref[...].astype(F32)
    total = jnp.sum(own * own, axis=1, keepdims=True)
    total = total + jnp.sum(other * other, axis=1, keepdims=True)
    scale = lax.rsqrt(total / D + EPSILON)
    own = (own * scale * gains_ref[0:1, :]).astype(BF16)
    other = (other * scale * gains_c_ref[0:1, :]).astype(BF16)
    x_own_ref[...] = own
    x_other_ref[...] = other
    scale_ref[...] = scale
    here = jnp.concatenate([query_ref[...], key_ref[...], value_ref[...]], axis=1)
    qkv_ref[...] = (dot(own, here) + dot(other, there_ref[...])).astype(BF16)


def project(col, own, other, gains, gains_c, w_query, w_key, w_value, there):
    rows, features = own.shape
    width = there.shape[1]
    group = GROUP_HEADS * DH
    tile = rows // 2

    def whole(*shape):
        return pl.BlockSpec(shape, lambda i, c: (0,) * len(shape))

    def mine(width):
        return pl.BlockSpec((features, width), lambda i, c: (0, c[0]))

    def rowwise(width):
        return pl.BlockSpec((tile, width), lambda i, c: (i, 0))

    return pl.pallas_call(
        project_kernel,
        grid_spec=pltpu.PrefetchScalarGridSpec(
            num_scalar_prefetch=1,
            grid=(rows // tile,),
            in_specs=[
                rowwise(features),
                rowwise(features),
                whole(2, features),
                whole(2, features),
                mine(group),
                mine(DH),
                mine(DH),
                whole(features, width),
            ],
            out_specs=[rowwise(features), rowwise(features), rowwise(width), rowwise(1)],
        ),
        out_shape=[
            jax.ShapeDtypeStruct((rows, features), BF16),
            jax.ShapeDtypeStruct((rows, features), BF16),
            jax.ShapeDtypeStruct((rows, width), BF16),
            jax.ShapeDtypeStruct((rows, 1), F32),
        ],
        compiler_params=params("arbitrary"),
        cost_estimate=SMALL,
        name="project",
    )(col, own, other, gains, gains_c, w_query, w_key, w_value, there)


def hidden_kernel(tiles, place_ref, *refs):
    near, near_c, far, far_c = refs[0:4]
    attended = refs[4:8]
    here = refs[8:12]
    there = refs[12:16]
    gains_ref, gains_c_ref = refs[16:18]
    hidden_ref, x_own_ref, x_other_ref, scale_ref = refs[18:22]
    is_near = (pl.program_id(0) >= tiles // 2).astype(jnp.int32) == place_ref[0]
    own = jnp.where(is_near, near[...], far[...]).astype(F32)
    other = jnp.where(is_near, near_c[...], far_c[...]).astype(F32)
    for k in range(4):
        own = own + dot(attended[k][...], here[k][...])
        other = other + dot(attended[k][...], there[k][...])
    total = jnp.sum(own * own, axis=1, keepdims=True)
    total = total + jnp.sum(other * other, axis=1, keepdims=True)
    scale = lax.rsqrt(total / D + EPSILON)
    hidden_ref[...] = own
    scale_ref[...] = scale
    x_own_ref[...] = (own * scale * gains_ref[1:2, :]).astype(BF16)
    x_other_ref[...] = (other * scale * gains_c_ref[1:2, :]).astype(BF16)


def hidden_rows(place, tokens, attended, w_here, w_there, gains, gains_c):
    half, features = tokens[0].shape
    rows, heads = attended[0].shape
    tile = 256
    tiles = rows // tile
    per_half = half // tile

    def rowwise(width):
        return pl.BlockSpec((tile, width), lambda i, p: (i, 0))

    def halfwise(width):
        return pl.BlockSpec((tile, width), lambda i, p: (i % per_half, 0))

    def whole(*shape):
        return pl.BlockSpec(shape, lambda i, p: (0,) * len(shape))

    mine = pl.BlockSpec((heads, features), lambda i, p: (p[1], 0))
    others = pl.BlockSpec((heads, features), lambda i, p: (1 - p[1], 0))
    return pl.pallas_call(
        functools.partial(hidden_kernel, tiles),
        grid_spec=pltpu.PrefetchScalarGridSpec(
            num_scalar_prefetch=1,
            grid=(tiles,),
            in_specs=[halfwise(features)] * 4
            + [rowwise(heads)] * 4
            + [mine, others, mine, others] * 2
            + [whole(2, features)] * 2,
            out_specs=[rowwise(features)] * 3 + [rowwise(1)],
        ),
        out_shape=[
            jax.ShapeDtypeStruct((rows, features), F32),
            jax.ShapeDtypeStruct((rows, features), BF16),
            jax.ShapeDtypeStruct((rows, features), BF16),
            jax.ShapeDtypeStruct((rows, 1), F32),
        ],
        compiler_params=params("arbitrary"),
        cost_estimate=SMALL,
        name="hidden_rows",
    )(
        place,
        *tokens,
        *attended,
        *[w_here[k // 2] for k in range(4)],
        *[w_there[k // 2] for k in range(4)],
        gains,
        gains_c,
    )


def expert_kernel(shared, aliased, first, order_ref, *refs):
    x_own, x_other, o_own, o_other, routes, gates = refs[0:6]
    weights = refs[6:18]
    grads = refs[18 + aliased : 20 + aliased]
    pair_ref, inner_ref = refs[20 + aliased : 22 + aliased]
    step = pl.program_id(0) + first
    rows, features = x_own.shape
    tile = 512
    up_own = jnp.concatenate([weights[k][0] for k in (0, 1, 6, 7)], axis=1)
    up_other = jnp.concatenate([weights[k][0] for k in (2, 3, 8, 9)], axis=1)
    down_own = jnp.concatenate([weights[k][0] for k in (4, 10)], axis=0)
    down_other = jnp.concatenate([weights[k][0] for k in (5, 11)], axis=0)

    def token_tile(t, carry):
        at = pl.ds(pl.multiple_of(t * tile, tile), tile)
        pre = dot(x_own[at, :], up_own) + dot(x_other[at, :], up_other)
        back = dot_nt(o_own[at, :], down_own) + dot_nt(o_other[at, :], down_other)
        for k in range(2):
            pre_gate = pre[:, 2 * k * LANES : (2 * k + 1) * LANES]
            pre_up = pre[:, (2 * k + 1) * LANES : (2 * k + 2) * LANES]
            inner_grad = back[:, k * LANES : (k + 1) * LANES]
            sigmoid = 1.0 / (1.0 + jnp.exp(-pre_gate))
            silu = pre_gate * sigmoid
            inner = silu * pre_up
            if not shared:
                chosen = jnp.where(routes[at, :] == order_ref[2 * step + k], gates[at, :], 0.0)
                gate = jnp.sum(chosen, axis=1, keepdims=True)
                inner = gate * inner
                inner_grad = gate * inner_grad
            gate_grad = inner_grad * pre_up * (sigmoid * (1.0 + pre_gate * (1.0 - sigmoid)))
            inner_ref[0, at, k * LANES : (k + 1) * LANES] = inner.astype(BF16)
            pair_ref[0, at, 2 * k * LANES : (2 * k + 1) * LANES] = gate_grad.astype(BF16)
            pair_ref[0, at, (2 * k + 1) * LANES : (2 * k + 2) * LANES] = (
                inner_grad * silu
            ).astype(BF16)
        return carry

    lax.fori_loop(0, rows // tile, token_tile, 0)
    pairs = pair_ref[0]
    for h, x in enumerate((x_own, x_other)):
        wide = dot_tn(x[...], pairs).astype(BF16)
        for k in range(2):
            grads[k][0, h * features : (h + 1) * features, 0 : 2 * LANES] = wide[
                :, 2 * k * LANES : (2 * k + 2) * LANES
            ]
    inner = inner_ref[0]
    tile = 256
    for h, o in enumerate((o_own, o_other)):
        for j in range(features // tile):
            low = dot_tn(inner, o[:, j * tile : (j + 1) * tile]).astype(BF16)
            for k in range(2):
                for b in range(tile // LANES):
                    at = h * features + j * tile + b * LANES
                    grads[k][0, at : at + LANES, 2 * LANES :] = low[
                        k * LANES : (k + 1) * LANES, b * LANES : (b + 1) * LANES
                    ]


def expert_specs(features, place, wide, low):
    specs = []
    if wide:
        block = pl.BlockSpec((1, features, LANES), lambda i, o: (place(i, o)[0], 0, place(i, o)[1]))
        specs += [block] * 4
    if low:
        block = pl.BlockSpec((1, LANES, features), lambda i, o: (*place(i, o), 0))
        specs += [block] * 2
    return specs


def expert_grads(order, first, last, total, x, o, routes, gates, weights, kept):
    shared = total is None
    steps = last - first
    rows, features = x[0].shape
    choices = routes.shape[1]
    aliased = len(kept)

    def fixed(*shape):
        return pl.BlockSpec(shape, lambda i, o: (0,) * len(shape))

    def stepped(*shape):
        return pl.BlockSpec((1, *shape), lambda i, o: (i, 0, 0))

    def placed(*shape):
        return pl.BlockSpec((1, *shape), lambda i, o: (i + first, 0, 0))

    specs = []
    for k in range(2):
        if shared:

            def picked(i, o, k=k):
                return 0, 2 * o[o.shape[0] - 1] + k

        else:

            def picked(i, o, k=k):
                return o[2 * (i + first) + k], o[o.shape[0] - 1]

        specs += expert_specs(features, picked, True, True)
    total = steps if shared else total
    return pl.pallas_call(
        functools.partial(expert_kernel, shared, aliased, first),
        grid_spec=pltpu.PrefetchScalarGridSpec(
            num_scalar_prefetch=1,
            grid=(steps,),
            in_specs=[fixed(rows, features)] * 4
            + [fixed(rows, choices)] * 2
            + specs
            + [pl.BlockSpec(memory_space=pl.ANY)] * aliased,
            out_specs=[stepped(2 * features, 3 * LANES)] * 2
            + [placed(rows, 4 * LANES), placed(rows, 2 * LANES)],
        ),
        out_shape=[jax.ShapeDtypeStruct((steps, 2 * features, 3 * LANES), BF16)] * 2
        + [
            jax.ShapeDtypeStruct((total, rows, 4 * LANES), BF16),
            jax.ShapeDtypeStruct((total, rows, 2 * LANES), BF16),
        ],
        input_output_aliases={19 + k: 2 + k for k in range(aliased)},
        compiler_params=params("arbitrary"),
        cost_estimate=SMALL,
        name="expert_grads",
    )(order, *x, *o, routes, gates, *weights, *weights, *kept)


def mix_kernel(back, group, order_ref, *refs):
    acts_ref, shared_ref = refs[0:2]
    each = 4 if back else 2
    count = 2 * group
    weights = refs[2 : 2 + each * count]
    shared = refs[2 + each * count : 2 + each * count + 2 * each]
    own_ref, other_ref, total_ref = refs[2 + each * (count + 2) :]
    step = pl.program_id(0)
    rows, features = own_ref.shape
    tile = 512

    def gathered(parts):
        if back:
            own = [p[0] for k in range(len(parts) // 4) for p in parts[4 * k : 4 * k + 2]]
            other = [p[0] for k in range(len(parts) // 4) for p in parts[4 * k + 2 : 4 * k + 4]]
            return [jnp.concatenate(own, axis=1), jnp.concatenate(other, axis=1)]
        own = [parts[2 * k][0] for k in range(len(parts) // 2)]
        other = [parts[2 * k + 1][0] for k in range(len(parts) // 2)]
        return [jnp.concatenate(own, axis=0), jnp.concatenate(other, axis=0)]

    times = dot_nt if back else dot

    @pl.when(step == 0)
    def _():
        both = gathered(shared)
        for t in range(rows // tile):
            at = slice(t * tile, (t + 1) * tile)
            for h in range(2):
                total_ref[h, at, :] = times(shared_ref[0, at, :], both[h])

    both = gathered(weights)
    for t in range(rows // tile):
        at = slice(t * tile, (t + 1) * tile)
        acts = jnp.concatenate([acts_ref[g, at, :] for g in range(group)], axis=1)
        for h in range(2):
            total_ref[h, at, :] += times(acts, both[h])

    @pl.when(step == pl.num_programs(0) - 1)
    def _():
        own_ref[...] = total_ref[0]
        other_ref[...] = total_ref[1].astype(BF16)


def mix(back, order, acts, shared_acts, weights, shared_weights):
    pairs, rows, width = acts.shape
    features = weights[0].shape[1] if back else weights[0].shape[2]
    group = 2 if pairs % 2 == 0 else 1

    specs = []
    for k in range(2 * group):

        def picked(i, o, k=k):
            return o[2 * group * i + k], o[o.shape[0] - 1]

        specs += expert_specs(features, picked, back, not back)
    for k in range(2):

        def picked(i, o, k=k):
            return 0, 2 * o[o.shape[0] - 1] + k

        specs += expert_specs(features, picked, back, not back)
    whole = pl.BlockSpec((rows, features), lambda i, o: (0, 0))
    return pl.pallas_call(
        functools.partial(mix_kernel, back, group),
        grid_spec=pltpu.PrefetchScalarGridSpec(
            num_scalar_prefetch=1,
            grid=(pairs // group,),
            in_specs=[
                pl.BlockSpec((group, rows, width), lambda i, o: (i, 0, 0)),
                pl.BlockSpec((1, rows, width), lambda i, o: (0, 0, 0)),
            ]
            + specs,
            out_specs=[whole, whole],
            scratch_shapes=[pltpu.VMEM((2, rows, features), F32)],
        ),
        out_shape=[
            jax.ShapeDtypeStruct((rows, features), F32),
            jax.ShapeDtypeStruct((rows, features), BF16),
        ],
        compiler_params=params("arbitrary"),
        cost_estimate=SMALL,
        name="mix",
    )(order, acts, shared_acts, *weights * (2 * group), *shared_weights * 2)


def ring_of(size):
    return list(range(0, size, 2)) + list(range(1, size, 2))[::-1]


def unpack_kernel(aliased, index_ref, *refs):
    first_ref, second_ref = refs[0:2]
    gate_ref, up_ref, down_ref = refs[2 + aliased : 5 + aliased]
    blocks = first_ref.shape[1] // LANES

    def write(chunk_ref):
        for c in range(2):
            base = 3 * LANES * c
            to = slice(c * LANES, (c + 1) * LANES)
            gate_ref[0, :, to] = chunk_ref[0, :, base : base + LANES].astype(F32)
            up_ref[0, :, to] = chunk_ref[0, :, base + LANES : base + 2 * LANES].astype(F32)
            for b in range(blocks):
                down_ref[0, to, b * LANES : (b + 1) * LANES] = chunk_ref[
                    0, b * LANES : (b + 1) * LANES, base + 2 * LANES : base + 3 * LANES
                ].astype(F32)

    pl.when(pl.program_id(1) == 0)(lambda: write(first_ref))
    pl.when(pl.program_id(1) == 1)(lambda: write(second_ref))


def unpack(index, first, second, shapes, outs):
    count, rows, width = first.shape
    chunk = pl.BlockSpec((1, rows, width), lambda i, d, n: (i, 0, 0))

    def placed(shape):
        return pl.BlockSpec((1, *shape[1:]), lambda i, d, n: (n[2 * i + d], 0, 0))

    aliased = len(outs)
    return pl.pallas_call(
        functools.partial(unpack_kernel, aliased),
        grid_spec=pltpu.PrefetchScalarGridSpec(
            num_scalar_prefetch=1,
            grid=(count, 2),
            in_specs=[chunk, chunk] + [pl.BlockSpec(memory_space=pl.ANY)] * aliased,
            out_specs=[placed(shape) for shape in shapes],
        ),
        out_shape=[jax.ShapeDtypeStruct(shape, F32) for shape in shapes],
        input_output_aliases={3 + k: k for k in range(aliased)},
        compiler_params=params("arbitrary", "arbitrary"),
        cost_estimate=SMALL,
        name="unpack",
    )(index, first, second, *outs)

def unpack_late_kernel(col_ref, first_ref, second_ref, *outs):
    sgate, sup, sdown, query, key, value, out = outs
    features = first_ref.shape[1]
    flipped = col_ref[0] != 0
    for c in range(2):
        for b in range(14):
            lanes = slice(b % 7 * LANES, (b % 7 + 1) * LANES)
            first, second = first_ref[c, :, lanes], second_ref[c, :, lanes]
            if b >= 7:
                first, second = second, first
            block = jnp.where(flipped, second, first).astype(F32)
            if b < 6:
                at = slice((2 * c + b // 3) * LANES, (2 * c + b // 3 + 1) * LANES)
                if b % 3 < 2:
                    (sgate, sup)[b % 3][:, at] = block
                else:
                    for k in range(features // LANES):
                        here = slice(k * LANES, (k + 1) * LANES)
                        sdown[at, here] = block[here, :]
            elif b < 9:
                at = (GROUP_HEADS * c + b - 6) * LANES
                query[:, at : at + LANES] = block
            elif b < 11:
                (key, value)[b - 9][:, c * LANES : (c + 1) * LANES] = block
            else:
                at = (GROUP_HEADS * c + b - 11) * LANES
                out[at : at + LANES, :] = block.T


def unpack_late(col, first, second, shapes):
    spec = pl.BlockSpec(memory_space=pltpu.VMEM)
    return pl.pallas_call(
        unpack_late_kernel,
        in_specs=[pl.BlockSpec(memory_space=pltpu.SMEM), spec, spec],
        out_specs=[spec] * len(shapes),
        out_shape=[jax.ShapeDtypeStruct(shape, F32) for shape in shapes],
        compiler_params=params(),
        name="unpack_late",
    )(col, first, second)


def add_rounded(left, right):
    return (left.astype(F32) + right.astype(F32)).astype(BF16)


def body(
    tokens_in,
    norm_gain_attn,
    w_query,
    w_key,
    w_value,
    w_out,
    norm_gain_ffn,
    w_gate,
    w_up,
    w_down,
    w_shared_gate,
    w_shared_up,
    w_shared_down,
    routes,
    gate_weights,
    seq_lengths,
    out_grad,
):
    row = lax.axis_index("row")
    col = lax.axis_index("col")
    dp = lax.axis_index("dp")
    dp_size = lax.axis_size("dp")
    local_rows, local_features = tokens_in.shape
    experts = w_gate.shape[0]
    group_width = GROUP_HEADS * DH
    col_ref = col.reshape(1)

    ring_size = min(8, dp_size)
    ring = ring_of(ring_size)
    starts = range(0, dp_size, ring_size)
    rights = [
        (g + ring[k], g + ring[(k + 1) % ring_size]) for g in starts for k in range(ring_size)
    ]
    lefts = [(b, a) for a, b in rights]
    routes_of = [
        [(2 * a, 2 * b) for a, b in ways[0]] + [(2 * a + 1, 2 * b + 1) for a, b in ways[1]]
        for ways in ((rights, lefts), (lefts, rights))
    ]
    place_of = [ring.index(k) for k in range(ring_size)]
    place = jnp.asarray(place_of, jnp.int32)[dp % ring_size]
    signs = [1 - 2 * col, 2 * col - 1]

    def send(values, which):
        if ring_size == 1:
            return values
        return lax.ppermute(values, ("dp", "col"), routes_of[which])

    def chunk_at(step, which):
        return (place - signs[which] * step) % ring_size

    def across_rings(values):
        if len(starts) == 1:
            return values
        peers = [[g + k for g in starts] for k in range(ring_size)]
        return lax.psum(values, "dp", axis_index_groups=peers)

    tokens_y = swap(tokens_in, "row")
    tokens_c = swap(tokens_in, "col")
    gains = jnp.stack([norm_gain_attn, norm_gain_ffn])
    gains_c = swap(gains, "col")
    there = jnp.concatenate(
        [halves(w, 1, col)[1] for w in (w_query, w_key, w_value)], axis=1
    )
    there = swap(there, "col")
    count = min(ring_size, 4)
    share = w_out.shape[0] // count
    member = dp % count
    out_share = swap(lax.dynamic_slice_in_dim(w_out, member * share, share, axis=0), "row")

    def project_half(own, other):
        return project(col_ref, own, other, gains, gains_c, w_query, w_key, w_value, there)

    near = project_half(tokens_in, tokens_c)

    shares = [after(out_share, near[2])]
    for k in range(1, count):
        pairs = [(m, m ^ k) for m in range(dp_size)]
        shares.append(lax.ppermute(shares[0], "dp", pairs))
    tokens_y = after(tokens_y, near[2], out_share)
    tokens_yc = swap(tokens_y, "col")
    grad_cut = local_rows // 8 * 3
    grad_y = [
        swap(after(part, tokens_y), "row") for part in (out_grad[:grad_cut], out_grad[grad_cut:])
    ]
    far = project_half(tokens_y, tokens_yc)

    attended = attend(
        after(jnp.stack([row, seq_lengths[0]]), grad_y[0], *shares), near[2], far[2]
    )
    out_c = swap(after(w_out, attended), "col")
    shares = jnp.stack([after(shares[0], attended)] + shares[1:])
    out_y = jnp.concatenate(
        [lax.dynamic_index_in_dim(shares, member ^ k, keepdims=False) for k in range(count)],
        axis=0,
    )
    attended_y = swap(after(attended, grad_y[1]), "row")
    attended_c = swap(attended, "col")

    w_sgate, w_sup, w_sdown = w_shared_gate[None], w_shared_up[None], w_shared_down[None]
    gate_c = swap(w_gate, "col")
    up_c, down_c, sgate_c, sup_c, sdown_c = (
        swap(after(w, attended), "col") for w in (w_up, w_down, w_sgate, w_sup, w_sdown)
    )

    grad_own = in_order(out_grad, jnp.concatenate(grad_y, axis=0), row, 0)
    grad_other = swap(grad_own, "col")
    out_yc = swap(out_y, "col")
    attended_y = after(attended_y, grad_own, out_yc)
    attended_yc = swap(attended_y, "col")
    hidden, x_own, x_other, scale_ffn = hidden_rows(
        jnp.stack([row, col]),
        [tokens_in, tokens_c, tokens_y, tokens_yc],
        [attended, attended_c, attended_y, attended_yc],
        [w_out, out_y],
        [out_c, out_yc],
        gains,
        gains_c,
    )

    each = experts // (2 * ring_size)
    orders = []
    for s in range(ring_size):
        for k in range(each):
            for which in range(2):
                second = col if which == 0 else 1 - col
                orders.append(2 * each * chunk_at(s, which) + each * second + k)
    order = jnp.stack(orders + [col]).astype(jnp.int32)
    pairs_total = experts // 2
    routed = [w_gate, w_up, gate_c, up_c, w_down, down_c]
    shared = [w_sgate, w_sup, sgate_c, sup_c, w_sdown, sdown_c]

    def run(first, last, order, kept):
        return expert_grads(
            order,
            first,
            last,
            pairs_total,
            [x_own, x_other],
            [grad_own, grad_other],
            routes,
            gate_weights,
            routed,
            kept,
        )

    first = run(0, each, order, ())
    kept = first[2:]
    sums = [first[0], first[1]]
    ready = {s: [first[0], first[1]] for s in (0,)}
    done = each
    runs = {}
    for s in range(1, ring_size):
        got = [send(sums[k], k) for k in range(2)]
        work = []
        last = min(max(done, each * s) + 2 * each, pairs_total)
        if done < last:
            result = run(done, last, after(order, *sums), tuple(kept))
            kept = result[2:]
            for at in range(done, last):
                runs[at] = (result[0], result[1], at - done)
            done = last
            work = list(kept)
        elif "shared" not in runs:
            runs["shared"] = expert_grads(
                after(order, *sums),
                0,
                1,
                None,
                [x_own, x_other],
                [grad_own, grad_other],
                routes,
                gate_weights,
                shared,
                (),
            )
            work = [runs["shared"][2]]
        elif "back" not in runs:
            runs["back"] = mix(
                True,
                after(order, *sums),
                kept[0],
                runs["shared"][2],
                routed[:4],
                shared[:4],
            )
            work = [runs["back"][1]]
        elif "out" not in runs:
            runs["out"] = mix(
                False,
                after(order, *sums),
                kept[1],
                runs["shared"][3],
                routed[4:],
                shared[4:],
            )
            work = [runs["out"][1]]
        for k in range(2):
            got[k] = after(got[k], *(sums[:1] if k else work))
            parts = [runs[at] for at in range(each * s, each * s + each)]
            mine = jnp.concatenate([p[k][p[2] : p[2] + 1] for p in parts], axis=0)
            sums[k] = add_rounded(got[k], mine)
    if "shared" not in runs:
        runs["shared"] = expert_grads(
            order, 0, 1, None, [x_own, x_other], [grad_own, grad_other], routes, gate_weights, shared, ()
        )
    if "back" not in runs:
        runs["back"] = mix(True, order, kept[0], runs["shared"][2], routed[:4], shared[:4])
    if "out" not in runs:
        runs["out"] = mix(False, order, kept[1], runs["shared"][3], routed[4:], shared[4:])

    sums = [across_rings(total) for total in sums]
    crossed = [swap(total[:, local_features:], "col") for total in sums]
    chunks = [
        in_order(sums[k][:, :local_features], crossed[1 - k], col, 2) for k in range(2)
    ]

    start = row * local_rows

    def my_rows(values):
        return lax.dynamic_slice_in_dim(values, start, local_rows, axis=0)

    def their_rows(values):
        return lax.dynamic_slice_in_dim(values, local_rows - start, local_rows, axis=0)

    back_own, back_other = runs["back"]
    normed_grad = back_own + swap(back_other, "col").astype(F32)
    normed_grad = normed_grad + swap(normed_grad.astype(BF16), "row").astype(F32)
    sum_own, sum_other = runs["out"]
    ffn_sum = sum_own + swap(sum_other, "col").astype(F32)
    ffn_rows = my_rows(ffn_sum) + swap(their_rows(ffn_sum).astype(BF16), "row").astype(F32)
    block_out = (my_rows(hidden) + ffn_rows).astype(BF16)

    gain_ffn_part = jnp.sum(my_rows(normed_grad * hidden * scale_ffn), axis=0)
    scaled = normed_grad * norm_gain_ffn
    products = jnp.sum(scaled * hidden, axis=1, keepdims=True)
    mean = (products + swap(products, "col")) / D
    hidden_grad = grad_own.astype(F32) + scale_ffn * scaled - hidden * scale_ffn**3 * mean
    attn_grad = hidden_grad.astype(BF16)
    attn_grad_c = swap(attn_grad, "col")

    out_own = lax.dynamic_slice_in_dim(w_out, col * group_width, group_width, axis=0)
    out_back = lax.dynamic_slice_in_dim(out_c, col * group_width, group_width, axis=0)
    attended_grad = (dot_nt(attn_grad, out_own) + dot_nt(attn_grad_c, out_back)).astype(BF16)
    out_grads = [dot_tn(attn_grad, attended), dot_tn(attn_grad_c, attended)]
    qkv = in_order(near[2], far[2], row, 0)
    qkv_grad = attend_back(qkv, attended_grad, seq_lengths[0])
    normed_own = in_order(near[0], far[0], row, 0)
    normed_other = in_order(near[1], far[1], row, 0)
    project_grads = [dot_tn(normed_own, qkv_grad), dot_tn(normed_other, qkv_grad)]
    here = jnp.concatenate(
        [halves(w, 1, col)[0] for w in (w_query, w_key, w_value)], axis=1
    )
    tokens_back = dot_nt(qkv_grad, here) + swap(
        dot_nt(qkv_grad, there).astype(BF16), "col"
    ).astype(F32)
    tokens_back = my_rows(tokens_back) + swap(
        their_rows(tokens_back).astype(BF16), "row"
    ).astype(F32)
    scale_attn = near[3]
    tokens_f32 = tokens_in.astype(F32)
    gain_attn_part = jnp.sum(tokens_back * tokens_f32 * scale_attn, axis=0)
    scaled = tokens_back * norm_gain_attn
    products = jnp.sum(scaled * tokens_f32, axis=1, keepdims=True)
    mean = (products + swap(products, "col")) / D
    tokens_grad = (
        my_rows(hidden_grad) + scale_attn * scaled - tokens_f32 * scale_attn**3 * mean
    ).astype(BF16)

    shared_grads = runs["shared"]
    pack = jnp.concatenate(
        [shared_grads[0][0], shared_grads[1][0]]
        + [
            jnp.concatenate(grads, axis=0).astype(BF16) for grads in (project_grads, out_grads)
        ],
        axis=1,
    )
    pack = pack.reshape(2, ring_size, local_features // ring_size, -1)
    middle = pack.shape[3] // 2

    def late_chunk(step, which):
        chunk = lax.dynamic_index_in_dim(pack, chunk_at(step, which), axis=1, keepdims=False)
        low, high = chunk[..., :middle], chunk[..., middle:]
        return jnp.where(col == which, low, high)

    def late_place(current, step, which):
        at = chunk_at(ring_size - 1 + step, which)
        return lax.dynamic_update_index_in_dim(late_out[which], current, at, 1)

    late_out = [jnp.zeros((*pack.shape[:3], middle), BF16) for _ in range(2)]
    late = [late_chunk(0, k) for k in range(2)]
    late_steps = 0

    def late_step(late_steps, late):
        late = [send(late[k], k) for k in range(2)]
        step = late_steps + 1
        if step < ring_size:
            late = [add_rounded(late[k], late_chunk(step, k)) for k in range(2)]
        else:
            for k in range(2):
                late_out[k] = late_place(late[k], step - ring_size + 1, k)
        if step == ring_size - 1:
            late = [across_rings(values) for values in late]
            others = [swap(values[1], "col") for values in late]
            late = [in_order(late[k][0:1], others[1 - k][None], col, 0) for k in range(2)]
            for k in range(2):
                late_out[k] = late_place(late[k], 0, k)
        return step, late

    shapes = [w_gate.shape, w_up.shape, w_down.shape]
    placed = ()
    late_slots = 5
    late_total = 2 * (ring_size - 1)
    for s in range(ring_size):
        index = []
        for k in range(each):
            for which in range(2):
                second = col if which == 0 else 1 - col
                at = chunk_at(ring_size - 1 + s, which)
                index.append(2 * each * at + each * second + k)
        index = jnp.stack(index).astype(jnp.int32)
        if s + 1 < ring_size:
            got = [send(chunks[k], k) for k in range(2)]
            placed = unpack(index, chunks[0], chunks[1], shapes, placed)
            slots_left = ring_size - 1 - s
            if slots_left <= late_slots:
                if late_steps == 0:
                    late = list(lax.optimization_barrier((*late, *chunks))[:2])
                until = late_total - late_total * (slots_left - 1) // late_slots
                while late_steps < until:
                    late_steps, late = late_step(late_steps, late)
            held = lax.optimization_barrier((*got, *late, *placed))
            got, late, placed = held[0:2], list(held[2:4]), held[4:]
            chunks = got
        else:
            placed = unpack(index, chunks[0], chunks[1], shapes, placed)
    while late_steps < late_total:
        late_steps, late = late_step(late_steps, late)
    if late_total == 0:
        others = [swap(values[1], "col") for values in late]
        late = [in_order(late[k][0:1], others[1 - k][None], col, 0) for k in range(2)]
        late_out = [late_place(late[k], 0, k) for k in range(2)]
    gate_grad, up_grad, down_grad = placed
    shapes = [w.shape for w in (w_shared_gate, w_shared_up, w_shared_down)]
    shapes += [w.shape for w in (w_query, w_key, w_value, w_out)]
    late_grads = unpack_late(
        col_ref,
        late_out[0].reshape(2, local_features, middle),
        late_out[1].reshape(2, local_features, middle),
        shapes,
    )
    shared_gate_grad, shared_up_grad, shared_down_grad = late_grads[0:3]
    query_grad, key_grad, value_grad, out_proj_grad = late_grads[3:7]

    gain_parts = jnp.stack([gain_attn_part, gain_ffn_part])
    bit = 1
    while bit < ring_size:
        pairs = [(g + k, g + (k ^ bit)) for g in starts for k in range(ring_size)]
        gain_parts = gain_parts + lax.ppermute(gain_parts, "dp", pairs)
        bit *= 2
    gain_parts = across_rings(gain_parts + swap(gain_parts, "row"))

    return (
        block_out,
        tokens_grad,
        gain_parts[0],
        query_grad,
        key_grad,
        value_grad,
        out_proj_grad,
        gain_parts[1],
        gate_grad,
        up_grad,
        down_grad,
        shared_gate_grad,
        shared_up_grad,
        shared_down_grad,
    )


def solution(mesh):
    in_specs = (
        P(("dp", "row"), "col"),
        P("col"),
        P("col", "row"),
        P("col", "row"),
        P("col", "row"),
        P("row", "col"),
        P("col"),
        P(None, "col", "row"),
        P(None, "col", "row"),
        P(None, "row", "col"),
        P("col", "row"),
        P("col", "row"),
        P("row", "col"),
        P("dp", None),
        P("dp", None),
        P("dp"),
        P(("dp", "row"), "col"),
    )
    out_specs = (
        P(("dp", "row"), "col"),
        P(("dp", "row"), "col"),
        P("col"),
        P("col", "row"),
        P("col", "row"),
        P("col", "row"),
        P("row", "col"),
        P("col"),
        P(None, "col", "row"),
        P(None, "col", "row"),
        P(None, "row", "col"),
        P("col", "row"),
        P("col", "row"),
        P("row", "col"),
    )
    return jax.shard_map(body, mesh=mesh, in_specs=in_specs, out_specs=out_specs, check_vma=False)
```

```python
import functools

import jax
import jax.numpy as jnp
from jax import lax
from jax.experimental import pallas as pl
from jax.experimental.pallas import tpu as pltpu
from jax.sharding import PartitionSpec as P

D = 1536
HQ = 12
HK = 4
DH = 128
GROUP_HEADS = HQ // HK
LANES = 128

EPSILON = 1e-05
F32 = jnp.float32
BF16 = jnp.bfloat16
MIB = 1024 * 1024
SMALL = pl.CostEstimate(flops=0, bytes_accessed=0, transcendentals=0)


def params(mib, *semantics):
    return pltpu.CompilerParams(
        dimension_semantics=semantics or None, vmem_limit_bytes=mib * MIB
    )


def dot(left, right):
    return jnp.dot(left, right, preferred_element_type=F32)


def dot_nt(left, right):
    return lax.dot_general(left, right, (((1,), (1,)), ((), ())), preferred_element_type=F32)


def dot_tn(left, right):
    return lax.dot_general(left, right, (((0,), (0,)), ((), ())), preferred_element_type=F32)


def after(values, *others):
    return lax.optimization_barrier((values, *others))[0]


def swap(values, axis):
    return lax.ppermute(values, axis, [(0, 1), (1, 0)])


def halves(values, axis, mine):
    size = values.shape[axis] // 2
    low = lax.slice_in_dim(values, 0, size, axis=axis)
    high = lax.slice_in_dim(values, size, 2 * size, axis=axis)
    return jnp.where(mine == 0, low, high), jnp.where(mine == 0, high, low)


def in_order(own, other, mine, axis):
    return jnp.concatenate(
        [jnp.where(mine == 0, own, other), jnp.where(mine == 0, other, own)], axis=axis
    )


def gather_rows(place_ref, own_ref, other_ref, all_ref):
    row = place_ref[0]
    rows = own_ref.shape[0]
    all_ref[pl.ds(pl.multiple_of(row * rows, rows), rows), :] = own_ref[...]
    all_ref[pl.ds(pl.multiple_of((1 - row) * rows, rows), rows), :] = other_ref[...]


def head_rows(ref, first, block):
    return jnp.concatenate(
        [ref[first : first + block, h * DH : (h + 1) * DH] for h in range(GROUP_HEADS)], axis=0
    )


def key_probs(query, key, first, length):
    block, keys = query.shape[0] // GROUP_HEADS, key.shape[0]
    scores = dot_nt(query, key) * DH ** (-0.5)
    shape = (block, keys)
    query_at = lax.broadcasted_iota(jnp.int32, shape, 0) + first
    key_at = lax.broadcasted_iota(jnp.int32, shape, 1)
    allowed = (key_at <= query_at) & (key_at < length)
    allowed = jnp.concatenate([allowed] * GROUP_HEADS, axis=0)
    scores = jnp.where(allowed, scores, -1e30)
    weights = jnp.exp(scores - jnp.max(scores, axis=1, keepdims=True))
    return weights * (1.0 / jnp.sum(weights, axis=1, keepdims=True))


def attend_kernel(place_ref, own_ref, other_ref, out_ref, all_ref):
    gather_rows(place_ref, own_ref, other_ref, all_ref)
    rows = own_ref.shape[0]
    block = 256
    width = GROUP_HEADS * DH
    for at in range(2 * rows // block):
        first, keys = at * block, (at + 1) * block
        query = head_rows(all_ref, first, block)
        key = all_ref[0:keys, width : width + DH]
        value = all_ref[0:keys, width + DH : width + 2 * DH]
        probs = key_probs(query, key, first, place_ref[1])
        result = dot(probs.astype(BF16), value).astype(BF16)
        for h in range(GROUP_HEADS):
            out_ref[first : first + block, h * DH : (h + 1) * DH] = result[
                h * block : (h + 1) * block
            ]


def attend(place, own, other):
    rows, width = own.shape
    spec = pl.BlockSpec(memory_space=pltpu.VMEM)
    return pl.pallas_call(
        attend_kernel,
        out_shape=jax.ShapeDtypeStruct((2 * rows, GROUP_HEADS * DH), BF16),
        in_specs=[pl.BlockSpec(memory_space=pltpu.SMEM), spec, spec],
        out_specs=spec,
        scratch_shapes=[pltpu.VMEM((2 * rows, width), BF16)],
        compiler_params=params(32),
        cost_estimate=SMALL,
        name="attend",
    )(place, own, other)


def attend_back_kernel(
    place_ref, own_ref, other_ref, grad_ref, grad_c_ref, out_ref, out_c_ref, result_ref, all_ref, total_ref
):
    gather_rows(place_ref, own_ref, other_ref, all_ref)
    rows = own_ref.shape[0]
    block = 256
    width = GROUP_HEADS * DH
    group = pl.ds(pl.multiple_of(place_ref[2] * width, width), width)
    blocks = 2 * rows // block
    for at in reversed(range(blocks)):
        first, keys = at * block, (at + 1) * block
        query = head_rows(all_ref, first, block)
        key = all_ref[0:keys, width : width + DH]
        value = all_ref[0:keys, width + DH : width + 2 * DH]
        probs = key_probs(query, key, first, place_ref[1])
        grad = dot_nt(grad_ref[first:keys, :], out_ref[group, :])
        grad = (grad + dot_nt(grad_c_ref[first:keys, :], out_c_ref[group, :])).astype(BF16)
        grad = jnp.concatenate(
            [grad[:, h * DH : (h + 1) * DH] for h in range(GROUP_HEADS)], axis=0
        )
        probs_grad = dot_nt(grad, value)
        carried = jnp.sum(probs * probs_grad, axis=1, keepdims=True)
        score_grad = (probs * (probs_grad - carried)).astype(BF16)
        query_back = (dot(score_grad, key) * DH ** (-0.5)).astype(BF16)
        for h in range(GROUP_HEADS):
            result_ref[first:keys, h * DH : (h + 1) * DH] = query_back[
                h * block : (h + 1) * block
            ]
        key_back = dot_tn(score_grad, query)
        value_back = dot_tn(probs.astype(BF16), grad)
        if at == blocks - 1:
            total_ref[:, 0:DH] = key_back
            total_ref[:, DH:] = value_back
        else:
            total_ref[0:keys, 0:DH] += key_back
            total_ref[0:keys, DH:] += value_back
    result_ref[:, width : width + DH] = (total_ref[:, 0:DH] * DH ** (-0.5)).astype(BF16)
    result_ref[:, width + DH :] = total_ref[:, DH:].astype(BF16)


def attend_back(place, own, other, grad, grad_c, w_out, out_c):
    rows, width = own.shape
    spec = pl.BlockSpec(memory_space=pltpu.VMEM)
    return pl.pallas_call(
        attend_back_kernel,
        out_shape=jax.ShapeDtypeStruct((2 * rows, width), BF16),
        in_specs=[pl.BlockSpec(memory_space=pltpu.SMEM)] + [spec] * 6,
        out_specs=spec,
        scratch_shapes=[
            pltpu.VMEM((2 * rows, width), BF16),
            pltpu.VMEM((2 * rows, 2 * DH), F32),
        ],
        compiler_params=params(48),
        cost_estimate=SMALL,
        name="attend_back",
    )(place, own, other, grad, grad_c, w_out, out_c)


def late_kernel(place_ref, *refs):
    near, near_c, far, far_c, qkv_ref, attended_ref, grad_ref, grad_c_ref = refs[0:8]
    shared = refs[8:10]
    outs = refs[10:12]
    rows, features = near.shape
    own_rows = pl.ds(pl.multiple_of(place_ref[0] * rows, rows), rows)
    far_rows = pl.ds(pl.multiple_of((1 - place_ref[0]) * rows, rows), rows)
    split = 7 * LANES

    def store(h, at, values):
        values = values.astype(BF16)
        for part in range(2):
            low, high = max(at, part * split), min(at + values.shape[1], (part + 1) * split)
            if low < high:
                piece = values[:, low - at : high - at]
                to = slice(low - part * split, high - part * split)

                @pl.when(place_ref[2] == 0)
                def _(part=part, to=to, piece=piece):
                    outs[part][h, :, to] = piece

                @pl.when(place_ref[2] != 0)
                def _(part=part, to=to, piece=piece):
                    outs[1 - part][h, :, to] = piece

    for h, (x, y, grad) in enumerate(((near, far, grad_ref), (near_c, far_c, grad_c_ref))):
        for k in range(2):
            store(h, 3 * LANES * k, shared[k][0, h * features : (h + 1) * features, :])
        project = dot_tn(x[...], qkv_ref[own_rows, :]) + dot_tn(y[...], qkv_ref[far_rows, :])
        store(h, 6 * LANES, project)
        store(h, 11 * LANES, dot_tn(grad[...], attended_ref[...]))


def late_grads(place, near, far, qkv_grad, attended, grad, grad_c, shared):
    features = near[0].shape[1]
    spec = pl.BlockSpec(memory_space=pltpu.VMEM)
    return pl.pallas_call(
        late_kernel,
        out_shape=[jax.ShapeDtypeStruct((2, features, 7 * LANES), BF16)] * 2,
        in_specs=[pl.BlockSpec(memory_space=pltpu.SMEM)] + [spec] * 10,
        out_specs=[spec] * 2,
        compiler_params=params(40),
        cost_estimate=SMALL,
        name="late_grads",
    )(place, *near, *far, qkv_grad, attended, grad, grad_c, *shared)


def columns_kernel(
    col_ref, query_ref, key_ref, value_ref, gain_ref, gain_ffn_ref, out_ref, gains_ref
):
    gains_ref[0:1, :] = gain_ref[...]
    gains_ref[1:2, :] = gain_ffn_ref[...]
    width = GROUP_HEADS * DH
    out_ref[:, 0:width] = query_ref[...]
    out_ref[:, width : width + DH] = key_ref[...]
    out_ref[:, width + DH :] = value_ref[...]


def their_columns(col, w_query, w_key, w_value, gain_attn, gain_ffn):
    rows = w_query.shape[0]
    width = GROUP_HEADS * DH + 2 * DH

    def theirs(width):
        return pl.BlockSpec((rows, width), lambda i, c: (0, 1 - c[0]))

    return pl.pallas_call(
        columns_kernel,
        grid_spec=pltpu.PrefetchScalarGridSpec(
            num_scalar_prefetch=1,
            grid=(1,),
            in_specs=[theirs(GROUP_HEADS * DH), theirs(DH), theirs(DH)]
            + [pl.BlockSpec(gain_attn.shape, lambda i, c: (0, 0))] * 2,
            out_specs=[
                pl.BlockSpec((rows, width), lambda i, c: (0, 0)),
                pl.BlockSpec((2, rows), lambda i, c: (0, 0)),
            ],
        ),
        out_shape=[
            jax.ShapeDtypeStruct((rows, width), BF16),
            jax.ShapeDtypeStruct((2, rows), F32),
        ],
        compiler_params=params(16, "arbitrary"),
        cost_estimate=SMALL,
        name="their_columns",
    )(col, w_query, w_key, w_value, gain_attn, gain_ffn)


def project_kernel(col_ref, own_ref, other_ref, gains_ref, gains_c_ref, query_ref, key_ref, value_ref, there_ref, x_own_ref, x_other_ref, qkv_ref, scale_ref):
    own = own_ref[...].astype(F32)
    other = other_ref[...].astype(F32)
    total = jnp.sum(own * own, axis=1, keepdims=True)
    total = total + jnp.sum(other * other, axis=1, keepdims=True)
    scale = lax.rsqrt(total / D + EPSILON)
    own = (own * scale * gains_ref[0:1, :]).astype(BF16)
    other = (other * scale * gains_c_ref[0:1, :]).astype(BF16)
    x_own_ref[...] = own
    x_other_ref[...] = other
    scale_ref[...] = scale
    here = jnp.concatenate([query_ref[...], key_ref[...], value_ref[...]], axis=1)
    qkv_ref[...] = (dot(own, here) + dot(other, there_ref[...])).astype(BF16)


def project(col, own, other, gains, gains_c, w_query, w_key, w_value, there):
    rows, features = own.shape
    width = there.shape[1]
    group = GROUP_HEADS * DH
    tile = rows // 2

    def whole(*shape):
        return pl.BlockSpec(shape, lambda i, c: (0,) * len(shape))

    def mine(width):
        return pl.BlockSpec((features, width), lambda i, c: (0, c[0]))

    def rowwise(width):
        return pl.BlockSpec((tile, width), lambda i, c: (i, 0))

    return pl.pallas_call(
        project_kernel,
        grid_spec=pltpu.PrefetchScalarGridSpec(
            num_scalar_prefetch=1,
            grid=(rows // tile,),
            in_specs=[
                rowwise(features),
                rowwise(features),
                whole(2, features),
                whole(2, features),
                mine(group),
                mine(DH),
                mine(DH),
                whole(features, width),
            ],
            out_specs=[rowwise(features), rowwise(features), rowwise(width), rowwise(1)],
        ),
        out_shape=[
            jax.ShapeDtypeStruct((rows, features), BF16),
            jax.ShapeDtypeStruct((rows, features), BF16),
            jax.ShapeDtypeStruct((rows, width), BF16),
            jax.ShapeDtypeStruct((rows, 1), F32),
        ],
        compiler_params=params(24, "arbitrary"),
        cost_estimate=SMALL,
        name="project",
    )(col, own, other, gains, gains_c, w_query, w_key, w_value, there)


def head_pair(col_ref, own, other):
    first, second = own[...], other[...]
    flipped = col_ref != 0
    return jnp.concatenate(
        [jnp.where(flipped, second, first), jnp.where(flipped, first, second)], axis=1
    )


def before_kernel(tiles, place_ref, *refs):
    near, near_c, far, far_c, attended, attended_c, here, there, own_ref, other_ref = refs
    is_near = (pl.program_id(0) >= tiles // 2).astype(jnp.int32) == place_ref[0]
    heads = head_pair(place_ref[2], attended, attended_c)
    own = jnp.where(is_near, near[...], far[...]).astype(F32)
    other = jnp.where(is_near, near_c[...], far_c[...]).astype(F32)
    own_ref[...] = own + dot(heads, here[...])
    other_ref[...] = other + dot(heads, there[...])


def after_kernel(place_ref, *refs):
    own_ref, other_ref, attended, attended_c, here, there, gains_ref, gains_c_ref = refs[0:8]
    hidden_ref, x_own_ref, x_other_ref, scale_ref = refs[8:12]
    heads = head_pair(place_ref[2], attended, attended_c)
    own = own_ref[...] + dot(heads, here[...])
    other = other_ref[...] + dot(heads, there[...])
    total = jnp.sum(own * own, axis=1, keepdims=True)
    total = total + jnp.sum(other * other, axis=1, keepdims=True)
    scale = lax.rsqrt(total / D + EPSILON)
    hidden_ref[...] = own
    scale_ref[...] = scale
    x_own_ref[...] = (own * scale * gains_ref[1:2, :]).astype(BF16)
    x_other_ref[...] = (other * scale * gains_c_ref[1:2, :]).astype(BF16)


TOKEN_TILE = 256


def rowwise(width):
    return pl.BlockSpec((TOKEN_TILE, width), lambda i, p: (i, 0))


def whole(*shape):
    return pl.BlockSpec(shape, lambda i, p: (0,) * len(shape))


def hidden_before(place, tokens, attended, here, there):
    half, features = tokens[0].shape
    rows, heads = attended[0].shape
    tiles = rows // TOKEN_TILE
    per_half = half // TOKEN_TILE
    halfwise = pl.BlockSpec((TOKEN_TILE, features), lambda i, p: (i % per_half, 0))
    return pl.pallas_call(
        functools.partial(before_kernel, tiles),
        grid_spec=pltpu.PrefetchScalarGridSpec(
            num_scalar_prefetch=1,
            grid=(tiles,),
            in_specs=[halfwise] * 4 + [rowwise(heads)] * 2 + [whole(2 * heads, features)] * 2,
            out_specs=[rowwise(features)] * 2,
        ),
        out_shape=[jax.ShapeDtypeStruct((rows, features), F32)] * 2,
        compiler_params=params(32, "arbitrary"),
        cost_estimate=pl.CostEstimate(
            flops=8 * rows * features * heads,
            bytes_accessed=16 * rows * features,
            transcendentals=0,
        ),
        name="hidden_before",
    )(place, *tokens, *attended, here, there)


def hidden_after(place, before, attended, here, there, gains, gains_c):
    rows, features = before[0].shape
    heads = attended[0].shape[1]
    return pl.pallas_call(
        after_kernel,
        grid_spec=pltpu.PrefetchScalarGridSpec(
            num_scalar_prefetch=1,
            grid=(rows // TOKEN_TILE,),
            in_specs=[rowwise(features)] * 2
            + [rowwise(heads)] * 2
            + [whole(2 * heads, features)] * 2
            + [whole(2, features)] * 2,
            out_specs=[rowwise(features)] * 3 + [rowwise(1)],
        ),
        out_shape=[
            jax.ShapeDtypeStruct((rows, features), F32),
            jax.ShapeDtypeStruct((rows, features), BF16),
            jax.ShapeDtypeStruct((rows, features), BF16),
            jax.ShapeDtypeStruct((rows, 1), F32),
        ],
        compiler_params=params(32, "arbitrary"),
        cost_estimate=SMALL,
        name="hidden_after",
    )(place, *before, *attended, here, there, gains, gains_c)


def expert_kernel(shared, aliased, first, order_ref, *refs):
    x_own, x_other, o_own, o_other, gates_ref = refs[0:5]
    weights = refs[5:17]
    grads = refs[17 + aliased : 19 + aliased]
    pair_ref, inner_ref = refs[19 + aliased : 21 + aliased]
    step = pl.program_id(0) + first
    rows, features = x_own.shape
    tile = 512
    up_own = jnp.concatenate([weights[k][0] for k in (0, 1, 6, 7)], axis=1)
    up_other = jnp.concatenate([weights[k][0] for k in (2, 3, 8, 9)], axis=1)
    down_own = jnp.concatenate([weights[k][0] for k in (4, 10)], axis=0)
    down_other = jnp.concatenate([weights[k][0] for k in (5, 11)], axis=0)

    def token_tile(t, carry):
        at = pl.ds(pl.multiple_of(t * tile, tile), tile)
        pre = dot(x_own[at, :], up_own) + dot(x_other[at, :], up_other)
        back = dot_nt(o_own[at, :], down_own) + dot_nt(o_other[at, :], down_other)
        for k in range(2):
            pre_gate = pre[:, 2 * k * LANES : (2 * k + 1) * LANES]
            pre_up = pre[:, (2 * k + 1) * LANES : (2 * k + 2) * LANES]
            inner_grad = back[:, k * LANES : (k + 1) * LANES]
            sigmoid = 1.0 / (1.0 + jnp.exp(-pre_gate))
            silu = pre_gate * sigmoid
            inner = silu * pre_up
            if not shared:
                shape = (gates_ref.shape[0], LANES)
                expert = lax.broadcasted_iota(jnp.int32, shape, 0) % (gates_ref.shape[0] // 3)
                chosen = (expert == order_ref[2 * step + k]).astype(F32).astype(BF16)
                gate = dot_tn(gates_ref[:, at], chosen)
                inner = gate * inner
                inner_grad = gate * inner_grad
            gate_grad = inner_grad * pre_up * (sigmoid * (1.0 + pre_gate * (1.0 - sigmoid)))
            inner_ref[0, at, k * LANES : (k + 1) * LANES] = inner.astype(BF16)
            pair_ref[0, at, 2 * k * LANES : (2 * k + 1) * LANES] = gate_grad.astype(BF16)
            pair_ref[0, at, (2 * k + 1) * LANES : (2 * k + 2) * LANES] = (
                inner_grad * silu
            ).astype(BF16)
        return carry

    lax.fori_loop(0, rows // tile, token_tile, 0)
    pairs = pair_ref[0]
    for h, x in enumerate((x_own, x_other)):
        wide = dot_tn(x[...], pairs).astype(BF16)
        for k in range(2):
            grads[k][0, h * features : (h + 1) * features, 0 : 2 * LANES] = wide[
                :, 2 * k * LANES : (2 * k + 2) * LANES
            ]
    inner = inner_ref[0]
    tile = 256
    for h, o in enumerate((o_own, o_other)):
        for j in range(features // tile):
            low = dot_tn(inner, o[:, j * tile : (j + 1) * tile]).astype(BF16)
            for k in range(2):
                for b in range(tile // LANES):
                    at = h * features + j * tile + b * LANES
                    grads[k][0, at : at + LANES, 2 * LANES :] = low[
                        k * LANES : (k + 1) * LANES, b * LANES : (b + 1) * LANES
                    ]


def expert_specs(features, place, wide, low):
    specs = []
    if wide:
        block = pl.BlockSpec((1, features, LANES), lambda i, o: (place(i, o)[0], 0, place(i, o)[1]))
        specs += [block] * 4
    if low:
        block = pl.BlockSpec((1, LANES, features), lambda i, o: (*place(i, o), 0))
        specs += [block] * 2
    return specs


def expert_grads(order, first, last, total, x, o, gates, weights, kept):
    shared = total is None
    steps = last - first
    rows, features = x[0].shape
    aliased = len(kept)

    def fixed(*shape):
        return pl.BlockSpec(shape, lambda i, o: (0,) * len(shape))

    def stepped(*shape):
        return pl.BlockSpec((1, *shape), lambda i, o: (i, 0, 0))

    def placed(*shape):
        return pl.BlockSpec((1, *shape), lambda i, o: (i + first, 0, 0))

    specs = []
    for k in range(2):
        if shared:

            def picked(i, o, k=k):
                return 0, 2 * o[o.shape[0] - 1] + k

        else:

            def picked(i, o, k=k):
                return o[2 * (i + first) + k], o[o.shape[0] - 1]

        specs += expert_specs(features, picked, True, True)
    total = steps if shared else total
    return pl.pallas_call(
        functools.partial(expert_kernel, shared, aliased, first),
        grid_spec=pltpu.PrefetchScalarGridSpec(
            num_scalar_prefetch=1,
            grid=(steps,),
            in_specs=[fixed(rows, features)] * 4
            + [fixed(*gates.shape)]
            + specs
            + [pl.BlockSpec(memory_space=pl.ANY)] * aliased,
            out_specs=[stepped(2 * features, 3 * LANES)] * 2
            + [placed(rows, 4 * LANES), placed(rows, 2 * LANES)],
        ),
        out_shape=[jax.ShapeDtypeStruct((steps, 2 * features, 3 * LANES), BF16)] * 2
        + [
            jax.ShapeDtypeStruct((total, rows, 4 * LANES), BF16),
            jax.ShapeDtypeStruct((total, rows, 2 * LANES), BF16),
        ],
        input_output_aliases={18 + k: 2 + k for k in range(aliased)},
        compiler_params=params(40, "arbitrary"),
        cost_estimate=SMALL,
        name="expert_grads",
    )(order, *x, *o, gates, *weights, *weights, *kept)


def mix_kernel(back, group, order_ref, *refs):
    acts_ref, shared_ref = refs[0:2]
    each = 2 if back else 1
    count = 2 * group * each
    weights = refs[2 : 2 + count]
    shared = refs[2 + count : 2 + count + 2 * each]
    out_ref, total_ref = refs[2 + count + 2 * each :]
    step = pl.program_id(0)
    rows = out_ref.shape[0]
    tile = 512
    times = dot_nt if back else dot
    along = 1 if back else 0

    @pl.when(step == 0)
    def _():
        both = jnp.concatenate([w[0] for w in shared], axis=along)
        for t in range(rows // tile):
            at = slice(t * tile, (t + 1) * tile)
            total_ref[at, :] = times(shared_ref[0, at, :], both)

    both = jnp.concatenate([w[0] for w in weights], axis=along)
    for t in range(rows // tile):
        at = slice(t * tile, (t + 1) * tile)
        acts = jnp.concatenate([acts_ref[g, at, :] for g in range(group)], axis=1)
        total_ref[at, :] += times(acts, both)

    @pl.when(step == pl.num_programs(0) - 1)
    def _():
        out_ref[...] = total_ref[...].astype(out_ref.dtype)


def mix(back, dtype, order, acts, shared_acts, weights, shared_weights):
    pairs, rows, width = acts.shape
    features = weights[0].shape[1] if back else weights[0].shape[2]
    group = 4 if pairs % 4 == 0 else 1

    def spec(place):
        if back:
            return pl.BlockSpec((1, features, LANES), lambda i, o: (place(i, o)[0], 0, place(i, o)[1]))
        return pl.BlockSpec((1, LANES, features), lambda i, o: (*place(i, o), 0))

    def routed(k):
        return spec(lambda i, o: (o[2 * group * i + k], o[o.shape[0] - 1]))

    def common(k):
        return spec(lambda i, o: (0, 2 * o[o.shape[0] - 1] + k))

    return pl.pallas_call(
        functools.partial(mix_kernel, back, group),
        grid_spec=pltpu.PrefetchScalarGridSpec(
            num_scalar_prefetch=1,
            grid=(pairs // group,),
            in_specs=[
                pl.BlockSpec((group, rows, width), lambda i, o: (i, 0, 0)),
                pl.BlockSpec((1, rows, width), lambda i, o: (0, 0, 0)),
            ]
            + [routed(k) for k in range(2 * group) for _ in weights]
            + [common(k) for k in range(2) for _ in weights],
            out_specs=pl.BlockSpec((rows, features), lambda i, o: (0, 0)),
            scratch_shapes=[pltpu.VMEM((rows, features), F32)],
        ),
        out_shape=jax.ShapeDtypeStruct((rows, features), dtype),
        compiler_params=params(48, "arbitrary"),
        cost_estimate=SMALL,
        name="mix",
    )(order, acts, shared_acts, *weights * (2 * group), *shared_weights * 2)


def ring_of(size):
    return list(range(0, size, 2)) + list(range(1, size, 2))[::-1]


def unpack_kernel(aliased, index_ref, *refs):
    chunks = refs[0:2]
    gate_ref, up_ref, down_ref = refs[2 + aliased : 5 + aliased]
    blocks = chunks[0].shape[1] // LANES

    def write(chunk_ref):
        gate_ref[0] = chunk_ref[0, :, 0:LANES].astype(F32)
        up_ref[0] = chunk_ref[0, :, LANES : 2 * LANES].astype(F32)
        for b in range(blocks):
            at = slice(b * LANES, (b + 1) * LANES)
            down_ref[0, :, at] = chunk_ref[0, at, 2 * LANES :].astype(F32)

    for k in range(2):
        pl.when(pl.program_id(1) == k)(lambda k=k: write(chunks[k]))


def unpack(index, chunks, shapes, outs):
    count, rows, width = chunks[0].shape
    chunk = pl.BlockSpec((1, rows, width), lambda i, d, n: (i, 0, 0))

    def wide(i, d, n):
        return (n[2 * i + d], 0, n[2 * count])

    def low(i, d, n):
        return (n[2 * i + d], n[2 * count], 0)

    aliased = len(outs)
    return pl.pallas_call(
        functools.partial(unpack_kernel, aliased),
        grid_spec=pltpu.PrefetchScalarGridSpec(
            num_scalar_prefetch=1,
            grid=(count, 2),
            in_specs=[chunk, chunk] + [pl.BlockSpec(memory_space=pl.ANY)] * aliased,
            out_specs=[
                pl.BlockSpec((1, rows, LANES), wide),
                pl.BlockSpec((1, rows, LANES), wide),
                pl.BlockSpec((1, LANES, rows), low),
            ],
        ),
        out_shape=[jax.ShapeDtypeStruct(shape, F32) for shape in shapes],
        input_output_aliases={3 + k: k for k in range(aliased)},
        compiler_params=params(16, "arbitrary", "arbitrary"),
        cost_estimate=SMALL,
        name="unpack",
    )(index, *chunks, *outs)


def unpack_late_kernel(col_ref, first_ref, second_ref, *outs):
    sgate, sup, sdown, query, key, value, out = outs
    features = first_ref.shape[1]
    flipped = col_ref[0] != 0
    for c in range(2):
        for b in range(14):
            lanes = slice(b % 7 * LANES, (b % 7 + 1) * LANES)
            first, second = first_ref[c, :, lanes], second_ref[c, :, lanes]
            if b >= 7:
                first, second = second, first
            block = jnp.where(flipped, second, first).astype(F32)
            if b < 6:
                at = slice((2 * c + b // 3) * LANES, (2 * c + b // 3 + 1) * LANES)
                if b % 3 < 2:
                    (sgate, sup)[b % 3][:, at] = block
                else:
                    for k in range(features // LANES):
                        here = slice(k * LANES, (k + 1) * LANES)
                        sdown[at, here] = block[here, :]
            elif b < 9:
                at = (GROUP_HEADS * c + b - 6) * LANES
                query[:, at : at + LANES] = block
            elif b < 11:
                (key, value)[b - 9][:, c * LANES : (c + 1) * LANES] = block
            else:
                at = (GROUP_HEADS * c + b - 11) * LANES
                out[at : at + LANES, :] = block.T


def unpack_late(col, first, second, shapes):
    spec = pl.BlockSpec(memory_space=pltpu.VMEM)
    return pl.pallas_call(
        unpack_late_kernel,
        in_specs=[pl.BlockSpec(memory_space=pltpu.SMEM), spec, spec],
        out_specs=[spec] * len(shapes),
        out_shape=[jax.ShapeDtypeStruct(shape, F32) for shape in shapes],
        compiler_params=params(48),
        name="unpack_late",
    )(col, first, second)


LATE_ROUND = 3


def add_rounded(left, right):
    return (left.astype(F32) + right.astype(F32)).astype(BF16)


def body(
    tokens_in,
    norm_gain_attn,
    w_query,
    w_key,
    w_value,
    w_out,
    norm_gain_ffn,
    w_gate,
    w_up,
    w_down,
    w_shared_gate,
    w_shared_up,
    w_shared_down,
    routes,
    gate_weights,
    seq_lengths,
    out_grad,
):
    row = lax.axis_index("row")
    col = lax.axis_index("col")
    dp = lax.axis_index("dp")
    dp_size = lax.axis_size("dp")
    local_rows, local_features = tokens_in.shape
    experts = w_gate.shape[0]
    group_width = GROUP_HEADS * DH
    col_ref = col.reshape(1)

    ring_size = min(8, dp_size)
    ring = ring_of(ring_size)
    starts = range(0, dp_size, ring_size)
    rights = [
        (g + ring[k], g + ring[(k + 1) % ring_size]) for g in starts for k in range(ring_size)
    ]
    lefts = [(b, a) for a, b in rights]
    routes_of = [
        [(2 * a, 2 * b) for a, b in ways[0]] + [(2 * a + 1, 2 * b + 1) for a, b in ways[1]]
        for ways in ((rights, lefts), (lefts, rights))
    ]
    place_of = [ring.index(k) for k in range(ring_size)]
    place = jnp.asarray(place_of, jnp.int32)[dp % ring_size]
    signs = [1 - 2 * col, 2 * col - 1]

    def send(values, which):
        if ring_size == 1:
            return values
        return lax.ppermute(values, ("dp", "col"), routes_of[which])

    def chunk_at(step, which):
        return (place - signs[which] * step) % ring_size

    def across_rings(values):
        if len(starts) == 1:
            return values
        peers = [[g + k for g in starts] for k in range(ring_size)]
        return lax.psum(values, "dp", axis_index_groups=peers)

    where = jnp.stack([row, seq_lengths[0], col])
    tokens_y = swap(tokens_in, "row")
    tokens_c = swap(tokens_in, "col")
    there, gains = their_columns(
        col_ref, w_query, w_key, w_value, norm_gain_attn[None], norm_gain_ffn[None]
    )
    there = swap(there, "col")
    gains_c = swap(gains, "col")

    def project_half(own, other):
        return project(col_ref, own, other, gains, gains_c, w_query, w_key, w_value, there)

    near = project_half(tokens_in, tokens_c)
    gate_c = swap(w_gate, "col")
    count = min(ring_size, 4)
    share = w_out.shape[0] // count
    member = dp % count
    out_y = lax.dynamic_slice_in_dim(w_out, member * share, share, axis=0)
    out_y = swap(out_y, "row")
    tokens_y = after(tokens_y, near[2], out_y)
    tokens_yc = swap(tokens_y, "col")
    grad_y = swap(after(out_grad, tokens_y), "row")
    far = project_half(tokens_y, tokens_yc)

    def double(part, bit, *others):
        if bit >= count:
            return part
        pairs = [(m, m ^ bit) for m in range(dp_size)]
        came = after(lax.ppermute(part, "dp", pairs), *others)
        return in_order(part, came, member // bit % 2, 0)

    out_y = double(out_y, 1)
    where = after(where, out_y)

    w_sgate, w_sup, w_sdown = w_shared_gate[None], w_shared_up[None], w_shared_down[None]
    up_c = swap(after(w_up, gate_c, tokens_yc), "col")

    attended = attend(where, near[2], far[2])
    attended_y = swap(attended, "row")
    attended_c = swap(attended, "col")
    out_c = swap(after(w_out, tokens_yc), "col")
    before = hidden_before(
        where,
        [tokens_in, tokens_c, tokens_y, tokens_yc],
        [attended, attended_c],
        w_out,
        out_c,
    )
    down_c = swap(after(w_down, up_c, attended_c, out_c, grad_y), "col")
    grad_own = in_order(out_grad, grad_y, row, 0)
    grad_other = swap(grad_own, "col")
    attended_y = after(attended_y, grad_own, before[0])
    out_y = double(out_y, 2, attended_y)
    out_yc = swap(out_y, "col")
    attended_yc = swap(attended_y, "col")
    hidden, x_own, x_other, scale_ffn = hidden_after(
        where, before, [attended_y, attended_yc], out_y, out_yc, gains, gains_c
    )
    sgate_c, sup_c, sdown_c = (
        swap(after(w, attended_yc), "col") for w in (w_sgate, w_sup, w_sdown)
    )

    choices = jnp.arange(experts, dtype=jnp.int32)[:, None]
    dense = sum(
        jnp.where(routes[:, k][None, :] == choices, gate_weights[:, k][None, :], 0.0)
        for k in range(routes.shape[1])
    )
    gates = []
    for _ in range(3):
        gates.append(lax.reduce_precision(dense, 8, 7))
        dense = dense - gates[-1]
    gates = jnp.concatenate(gates, axis=0).astype(BF16)

    each = experts // (2 * ring_size)
    orders = []
    for s in range(ring_size):
        for k in range(each):
            for which in range(2):
                second = col if which == 0 else 1 - col
                orders.append(2 * each * chunk_at(s, which) + each * second + k)
    order = jnp.stack(orders + [col]).astype(jnp.int32)
    pairs_total = experts // 2
    routed = [w_gate, w_up, gate_c, up_c, w_down, down_c]
    shared = [w_sgate, w_sup, sgate_c, sup_c, w_sdown, sdown_c]

    def run(first, last, order, kept):
        return expert_grads(
            order,
            first,
            last,
            pairs_total,
            [x_own, x_other],
            [grad_own, grad_other],
            gates,
            routed,
            kept,
        )

    first = run(0, each, order, ())
    kept = first[2:]
    sums = [first[0], first[1]]
    runs = {}
    mixed = {}

    def work_experts(first, last):
        def work(order):
            nonlocal kept
            result = run(first, last, order, tuple(kept))
            kept = result[2:]
            for at in range(first, last):
                runs[at] = (result[0], result[1], at - first)
            return kept[0]

        return work

    def work_shared(order):
        runs["shared"] = expert_grads(
            order, 0, 1, None, [x_own, x_other], [grad_own, grad_other], gates, shared, ()
        )
        return runs["shared"][2]

    def work_mix(back, half):
        def work(order):
            pick = slice(2 * half, 2 * half + 2) if back else slice(4 + half, 5 + half)
            mixed[back, half] = mix(
                back,
                BF16 if half else F32,
                order,
                kept[0 if back else 1],
                runs["shared"][2 if back else 3],
                routed[pick],
                shared[pick],
            )
            return mixed[back, half]

        return work

    bounds = list(range(each, pairs_total, 2 * each)) + [pairs_total]
    tasks = [[work_experts(a, b)] for a, b in zip(bounds[:-1], bounds[1:], strict=True)]
    if not tasks:
        tasks.append([])
    tasks[-1].append(work_shared)
    tasks += [[work_mix(True, 1)], [work_mix(True, 0)], [work_mix(False, 1)], [work_mix(False, 0)]]
    for s in range(1, ring_size):
        got = [send(sums[k], k) for k in range(2)]
        last = sums
        if s <= len(tasks):
            for task in tasks[s - 1]:
                last = [task(after(order, *last))]
        for k in range(2):
            got[k] = after(got[k], *last)
            parts = [runs[at] for at in range(each * s, each * s + each)]
            mine = [p[k][p[2] : p[2] + 1] for p in parts]
            mine = mine[0] if each == 1 else jnp.concatenate(mine, axis=0)
            sums[k] = add_rounded(got[k], mine)
            last = [sums[k]]
    for task in [task for step in tasks[ring_size - 1 :] for task in step]:
        task(after(order, *sums))
    sums = [across_rings(total) for total in sums]
    waves = [[total[:, :local_features] for total in sums]]
    crossed = [swap(total[:, local_features:], "col") for total in sums]
    waves.append([crossed[1], crossed[0]])

    start = row * local_rows

    def my_rows(values):
        return lax.dynamic_slice_in_dim(values, start, local_rows, axis=0)

    def their_rows(values):
        return lax.dynamic_slice_in_dim(values, local_rows - start, local_rows, axis=0)

    normed_grad = mixed[True, 0] + swap(mixed[True, 1], "col").astype(F32)
    normed_grad = normed_grad + swap(normed_grad.astype(BF16), "row").astype(F32)
    ffn_sum = mixed[False, 0] + swap(mixed[False, 1], "col").astype(F32)
    ffn_rows = my_rows(ffn_sum) + swap(their_rows(ffn_sum).astype(BF16), "row").astype(F32)
    block_out = (my_rows(hidden) + ffn_rows).astype(BF16)

    gain_ffn_part = jnp.sum(my_rows(normed_grad * hidden * scale_ffn), axis=0)
    scaled = normed_grad * norm_gain_ffn
    products = jnp.sum(scaled * hidden, axis=1, keepdims=True)
    mean = (products + swap(products, "col")) / D
    hidden_grad = grad_own.astype(F32) + scale_ffn * scaled - hidden * scale_ffn**3 * mean
    attn_grad = hidden_grad.astype(BF16)
    attn_grad_c = swap(attn_grad, "col")

    qkv_grad = attend_back(where, near[2], far[2], attn_grad, attn_grad_c, w_out, out_c)
    packs = late_grads(
        where,
        near[0:2],
        far[0:2],
        qkv_grad,
        attended,
        attn_grad,
        attn_grad_c,
        runs["shared"][0:2],
    )
    here = jnp.concatenate(
        [halves(w, 1, col)[0] for w in (w_query, w_key, w_value)], axis=1
    )

    packs = [
        pack.reshape(2, ring_size, local_features // ring_size, pack.shape[2]) for pack in packs
    ]

    def late_chunk(step, which):
        at = chunk_at(step, which)
        return lax.dynamic_index_in_dim(packs[which], at, axis=1, keepdims=False)

    def late_place(current, step, which):
        at = chunk_at(ring_size - 1 + step, which)
        return lax.dynamic_update_index_in_dim(late_out[which], current, at, 1)

    late_out = [jnp.zeros(pack.shape, BF16) for pack in packs]
    late = [late_chunk(0, k) for k in range(2)]
    late_done = 0
    late_total = 2 * (ring_size - 1)

    def late_turn():
        totals = [across_rings(values) for values in late]
        others = [swap(values[1], "col") for values in totals]
        for k in range(2):
            late[k] = in_order(totals[k][0:1], others[1 - k][None], col, 0)
            late_out[k] = late_place(late[k], 0, k)

    def late_finish(got, last):
        nonlocal late_done
        late_done += 1
        for k in range(2):
            values = after(got[k], *last)
            if late_done < ring_size:
                late[k] = add_rounded(values, late_chunk(late_done, k))
            else:
                late[k] = values
                late_out[k] = late_place(values, late_done - ring_size + 1, k)
            last = [late[k]]
        if late_done == ring_size - 1:
            late_turn()

    shapes = [w_gate.shape, w_up.shape, w_down.shape]
    placed = ()

    def place_chunks(wave, step, chunks, placed):
        index = []
        for k in range(each):
            for which in range(2):
                second = col if which == 0 else 1 - col
                at = chunk_at(ring_size - 1 + step, which)
                index.append(2 * each * at + each * second + k)
        index.append(col if wave == 0 else 1 - col)
        return unpack(jnp.stack(index).astype(jnp.int32), chunks, shapes, placed)

    if late_total == 0:
        late_turn()
    rounds = [(wave, step) for wave in range(2) for step in range(ring_size - 1)]
    for number, (wave, step) in enumerate(rounds):
        if step == 0:
            chunks = waves[wave]
        got = [send(chunks[k], k) for k in range(2)]
        steps = 0 if number < LATE_ROUND else 1
        if number >= len(rounds) - LATE_ROUND:
            steps = 2
        steps = min(steps, late_total - late_done)
        if number == LATE_ROUND:
            late = [after(values, *chunks) for values in late]
        late_got = [send(late[k], k) for k in range(2)] if steps else None
        placed = place_chunks(wave, step, chunks, placed)
        for k in range(2):
            got[k] = after(got[k], placed[0])
        for at in range(steps):
            if at:
                late_got = [send(late[k], k) for k in range(2)]
            late_finish(late_got, got)
        chunks = got
        if step == ring_size - 2:
            placed = place_chunks(wave, step + 1, chunks, placed)
    if not rounds:
        for wave in range(2):
            placed = place_chunks(wave, 0, waves[wave], placed)
    while late_done < late_total:
        late_finish([send(late[k], k) for k in range(2)], placed[0:1])
    gate_grad, up_grad, down_grad = placed
    shapes = [w.shape for w in (w_shared_gate, w_shared_up, w_shared_down)]
    shapes += [w.shape for w in (w_query, w_key, w_value, w_out)]
    finals = unpack_late(
        col_ref, *[out.reshape(2, local_features, out.shape[3]) for out in late_out], shapes
    )
    shared_gate_grad, shared_up_grad, shared_down_grad = finals[0:3]
    query_grad, key_grad, value_grad, out_proj_grad = finals[3:7]

    tokens_back = dot_nt(qkv_grad, here) + swap(
        dot_nt(qkv_grad, there).astype(BF16), "col"
    ).astype(F32)
    tokens_back = my_rows(tokens_back) + swap(
        their_rows(tokens_back).astype(BF16), "row"
    ).astype(F32)
    scale_attn = near[3]
    tokens_f32 = tokens_in.astype(F32)
    gain_attn_part = jnp.sum(tokens_back * tokens_f32 * scale_attn, axis=0)
    scaled = tokens_back * norm_gain_attn
    products = jnp.sum(scaled * tokens_f32, axis=1, keepdims=True)
    mean = (products + swap(products, "col")) / D
    tokens_grad = (
        my_rows(hidden_grad) + scale_attn * scaled - tokens_f32 * scale_attn**3 * mean
    ).astype(BF16)

    gain_parts = jnp.stack([gain_attn_part, gain_ffn_part])
    bit = 1
    while bit < ring_size:
        pairs = [(g + k, g + (k ^ bit)) for g in starts for k in range(ring_size)]
        gain_parts = gain_parts + lax.ppermute(gain_parts, "dp", pairs)
        bit *= 2
    gain_parts = across_rings(gain_parts + swap(gain_parts, "row"))

    return (
        block_out,
        tokens_grad,
        gain_parts[0],
        query_grad,
        key_grad,
        value_grad,
        out_proj_grad,
        gain_parts[1],
        gate_grad,
        up_grad,
        down_grad,
        shared_gate_grad,
        shared_up_grad,
        shared_down_grad,
    )


def solution(mesh):
    in_specs = (
        P(("dp", "row"), "col"),
        P("col"),
        P("col", "row"),
        P("col", "row"),
        P("col", "row"),
        P("row", "col"),
        P("col"),
        P(None, "col", "row"),
        P(None, "col", "row"),
        P(None, "row", "col"),
        P("col", "row"),
        P("col", "row"),
        P("row", "col"),
        P("dp", None),
        P("dp", None),
        P("dp"),
        P(("dp", "row"), "col"),
    )
    out_specs = (
        P(("dp", "row"), "col"),
        P(("dp", "row"), "col"),
        P("col"),
        P("col", "row"),
        P("col", "row"),
        P("col", "row"),
        P("row", "col"),
        P("col"),
        P(None, "col", "row"),
        P(None, "col", "row"),
        P(None, "row", "col"),
        P("col", "row"),
        P("col", "row"),
        P("row", "col"),
    )
    return jax.shard_map(body, mesh=mesh, in_specs=in_specs, out_specs=out_specs, check_vma=False)
```

```python
import functools

import jax
import jax.numpy as jnp
from jax import lax
from jax.experimental import pallas as pl
from jax.experimental.pallas import tpu as pltpu
from jax.sharding import PartitionSpec as P

D = 1536
HQ = 12
HK = 4
DH = 128
GROUP_HEADS = HQ // HK
LANES = 128

EPSILON = 1e-05
F32 = jnp.float32
BF16 = jnp.bfloat16
MIB = 1024 * 1024
SMALL = pl.CostEstimate(flops=0, bytes_accessed=0, transcendentals=0)


def params(mib, *semantics):
    return pltpu.CompilerParams(
        dimension_semantics=semantics or None, vmem_limit_bytes=mib * MIB
    )


def dot(left, right):
    return jnp.dot(left, right, preferred_element_type=F32)


def dot_nt(left, right):
    return lax.dot_general(left, right, (((1,), (1,)), ((), ())), preferred_element_type=F32)


def dot_tn(left, right):
    return lax.dot_general(left, right, (((0,), (0,)), ((), ())), preferred_element_type=F32)


def after(values, *others):
    return lax.optimization_barrier((values, *others))[0]


def swap(values, axis):
    return lax.ppermute(values, axis, [(0, 1), (1, 0)])


def halves(values, axis, mine):
    size = values.shape[axis] // 2
    low = lax.slice_in_dim(values, 0, size, axis=axis)
    high = lax.slice_in_dim(values, size, 2 * size, axis=axis)
    return jnp.where(mine == 0, low, high), jnp.where(mine == 0, high, low)


def in_order(own, other, mine, axis):
    return jnp.concatenate(
        [jnp.where(mine == 0, own, other), jnp.where(mine == 0, other, own)], axis=axis
    )


def gather_rows(place_ref, own_ref, other_ref, all_ref):
    row = place_ref[0]
    rows = own_ref.shape[0]
    all_ref[pl.ds(pl.multiple_of(row * rows, rows), rows), :] = own_ref[...]
    all_ref[pl.ds(pl.multiple_of((1 - row) * rows, rows), rows), :] = other_ref[...]


def head_rows(ref, first, block):
    return jnp.concatenate(
        [ref[first : first + block, h * DH : (h + 1) * DH] for h in range(GROUP_HEADS)], axis=0
    )


def key_probs(query, key, first, length):
    block, keys = query.shape[0] // GROUP_HEADS, key.shape[0]
    scores = dot_nt(query, key) * DH ** (-0.5)
    shape = (block, keys)
    query_at = lax.broadcasted_iota(jnp.int32, shape, 0) + first
    key_at = lax.broadcasted_iota(jnp.int32, shape, 1)
    allowed = (key_at <= query_at) & (key_at < length)
    allowed = jnp.concatenate([allowed] * GROUP_HEADS, axis=0)
    scores = jnp.where(allowed, scores, -1e30)
    weights = jnp.exp(scores - jnp.max(scores, axis=1, keepdims=True))
    return weights * (1.0 / jnp.sum(weights, axis=1, keepdims=True))


def attend_kernel(place_ref, own_ref, other_ref, out_ref, all_ref):
    gather_rows(place_ref, own_ref, other_ref, all_ref)
    rows = own_ref.shape[0]
    block = 256
    width = GROUP_HEADS * DH
    for at in range(2 * rows // block):
        first, keys = at * block, (at + 1) * block
        query = head_rows(all_ref, first, block)
        key = all_ref[0:keys, width : width + DH]
        value = all_ref[0:keys, width + DH : width + 2 * DH]
        probs = key_probs(query, key, first, place_ref[1])
        result = dot(probs.astype(BF16), value).astype(BF16)
        for h in range(GROUP_HEADS):
            out_ref[first : first + block, h * DH : (h + 1) * DH] = result[
                h * block : (h + 1) * block
            ]


def attend(place, own, other):
    rows, width = own.shape
    spec = pl.BlockSpec(memory_space=pltpu.VMEM)
    return pl.pallas_call(
        attend_kernel,
        out_shape=jax.ShapeDtypeStruct((2 * rows, GROUP_HEADS * DH), BF16),
        in_specs=[pl.BlockSpec(memory_space=pltpu.SMEM), spec, spec],
        out_specs=spec,
        scratch_shapes=[pltpu.VMEM((2 * rows, width), BF16)],
        compiler_params=params(32),
        cost_estimate=SMALL,
        name="attend",
    )(place, own, other)


def attend_back_kernel(
    place_ref, own_ref, other_ref, grad_ref, grad_c_ref, out_ref, out_c_ref, result_ref, all_ref, total_ref
):
    gather_rows(place_ref, own_ref, other_ref, all_ref)
    rows = own_ref.shape[0]
    block = 256
    width = GROUP_HEADS * DH
    group = pl.ds(pl.multiple_of(place_ref[2] * width, width), width)
    blocks = 2 * rows // block
    for at in reversed(range(blocks)):
        first, keys = at * block, (at + 1) * block
        query = head_rows(all_ref, first, block)
        key = all_ref[0:keys, width : width + DH]
        value = all_ref[0:keys, width + DH : width + 2 * DH]
        probs = key_probs(query, key, first, place_ref[1])
        grad = dot_nt(grad_ref[first:keys, :], out_ref[group, :])
        grad = (grad + dot_nt(grad_c_ref[first:keys, :], out_c_ref[group, :])).astype(BF16)
        grad = jnp.concatenate(
            [grad[:, h * DH : (h + 1) * DH] for h in range(GROUP_HEADS)], axis=0
        )
        probs_grad = dot_nt(grad, value)
        carried = jnp.sum(probs * probs_grad, axis=1, keepdims=True)
        score_grad = (probs * (probs_grad - carried)).astype(BF16)
        query_back = (dot(score_grad, key) * DH ** (-0.5)).astype(BF16)
        for h in range(GROUP_HEADS):
            result_ref[first:keys, h * DH : (h + 1) * DH] = query_back[
                h * block : (h + 1) * block
            ]
        key_back = dot_tn(score_grad, query)
        value_back = dot_tn(probs.astype(BF16), grad)
        if at == blocks - 1:
            total_ref[:, 0:DH] = key_back
            total_ref[:, DH:] = value_back
        else:
            total_ref[0:keys, 0:DH] += key_back
            total_ref[0:keys, DH:] += value_back
    result_ref[:, width : width + DH] = (total_ref[:, 0:DH] * DH ** (-0.5)).astype(BF16)
    result_ref[:, width + DH :] = total_ref[:, DH:].astype(BF16)


def attend_back(place, own, other, grad, grad_c, w_out, out_c):
    rows, width = own.shape
    spec = pl.BlockSpec(memory_space=pltpu.VMEM)
    return pl.pallas_call(
        attend_back_kernel,
        out_shape=jax.ShapeDtypeStruct((2 * rows, width), BF16),
        in_specs=[pl.BlockSpec(memory_space=pltpu.SMEM)] + [spec] * 6,
        out_specs=spec,
        scratch_shapes=[
            pltpu.VMEM((2 * rows, width), BF16),
            pltpu.VMEM((2 * rows, 2 * DH), F32),
        ],
        compiler_params=params(48),
        cost_estimate=SMALL,
        name="attend_back",
    )(place, own, other, grad, grad_c, w_out, out_c)


def late_kernel(place_ref, *refs):
    near, near_c, far, far_c, qkv_ref, attended_ref, grad_ref, grad_c_ref = refs[0:8]
    shared = refs[8:10]
    outs = refs[10:12]
    rows, features = near.shape
    own_rows = pl.ds(pl.multiple_of(place_ref[0] * rows, rows), rows)
    far_rows = pl.ds(pl.multiple_of((1 - place_ref[0]) * rows, rows), rows)
    split = 7 * LANES

    def store(h, at, values):
        values = values.astype(BF16)
        for part in range(2):
            low, high = max(at, part * split), min(at + values.shape[1], (part + 1) * split)
            if low < high:
                piece = values[:, low - at : high - at]
                to = slice(low - part * split, high - part * split)

                @pl.when(place_ref[2] == 0)
                def _(part=part, to=to, piece=piece):
                    outs[part][h, :, to] = piece

                @pl.when(place_ref[2] != 0)
                def _(part=part, to=to, piece=piece):
                    outs[1 - part][h, :, to] = piece

    for h, (x, y, grad) in enumerate(((near, far, grad_ref), (near_c, far_c, grad_c_ref))):
        for k in range(2):
            store(h, 3 * LANES * k, shared[k][0, h * features : (h + 1) * features, :])
        project = dot_tn(x[...], qkv_ref[own_rows, :]) + dot_tn(y[...], qkv_ref[far_rows, :])
        store(h, 6 * LANES, project)
        store(h, 11 * LANES, dot_tn(grad[...], attended_ref[...]))


def late_grads(place, near, far, qkv_grad, attended, grad, grad_c, shared):
    features = near[0].shape[1]
    spec = pl.BlockSpec(memory_space=pltpu.VMEM)
    return pl.pallas_call(
        late_kernel,
        out_shape=[jax.ShapeDtypeStruct((2, features, 7 * LANES), BF16)] * 2,
        in_specs=[pl.BlockSpec(memory_space=pltpu.SMEM)] + [spec] * 10,
        out_specs=[spec] * 2,
        compiler_params=params(40),
        cost_estimate=SMALL,
        name="late_grads",
    )(place, *near, *far, qkv_grad, attended, grad, grad_c, *shared)


def columns_kernel(
    place_ref, query_ref, key_ref, value_ref, gain_ref, gain_ffn_ref, w_out_ref, out_ref, gains_ref, share_ref
):
    share_ref[...] = w_out_ref[...]
    gains_ref[0:1, :] = gain_ref[...]
    gains_ref[1:2, :] = gain_ffn_ref[...]
    width = GROUP_HEADS * DH
    out_ref[:, 0:width] = query_ref[...]
    out_ref[:, width : width + DH] = key_ref[...]
    out_ref[:, width + DH :] = value_ref[...]


def their_columns(place, w_query, w_key, w_value, gain_attn, gain_ffn, w_out, shares):
    rows = w_query.shape[0]
    width = GROUP_HEADS * DH + 2 * DH

    def theirs(width):
        return pl.BlockSpec((rows, width), lambda i, c: (0, 1 - c[0]))

    return pl.pallas_call(
        columns_kernel,
        grid_spec=pltpu.PrefetchScalarGridSpec(
            num_scalar_prefetch=1,
            grid=(1,),
            in_specs=[theirs(GROUP_HEADS * DH), theirs(DH), theirs(DH)]
            + [pl.BlockSpec(gain_attn.shape, lambda i, c: (0, 0))] * 2
            + [pl.BlockSpec((rows // shares, rows), lambda i, c: (c[1], 0))],
            out_specs=[
                pl.BlockSpec((rows, width), lambda i, c: (0, 0)),
                pl.BlockSpec((2, rows), lambda i, c: (0, 0)),
                pl.BlockSpec((rows // shares, rows), lambda i, c: (0, 0)),
            ],
        ),
        out_shape=[
            jax.ShapeDtypeStruct((rows, width), BF16),
            jax.ShapeDtypeStruct((2, rows), F32),
            jax.ShapeDtypeStruct((rows // shares, rows), BF16),
        ],
        compiler_params=params(16, "arbitrary"),
        cost_estimate=SMALL,
        name="their_columns",
    )(place, w_query, w_key, w_value, gain_attn, gain_ffn, w_out)


def join_kernel(mine_ref, own_ref, other_ref, out_ref):
    rows = own_ref.shape[0]
    out_ref[pl.ds(pl.multiple_of(mine_ref[0] * rows, rows), rows), :] = own_ref[...]
    out_ref[pl.ds(pl.multiple_of((1 - mine_ref[0]) * rows, rows), rows), :] = other_ref[...]


def join(mine, own, other):
    rows, width = own.shape
    spec = pl.BlockSpec(memory_space=pltpu.VMEM)
    return pl.pallas_call(
        join_kernel,
        out_shape=jax.ShapeDtypeStruct((2 * rows, width), own.dtype),
        in_specs=[pl.BlockSpec(memory_space=pltpu.SMEM), spec, spec],
        out_specs=spec,
        compiler_params=params(16),
        cost_estimate=SMALL,
        name="join",
    )(mine.reshape(1), own, other)


def project_kernel(col_ref, own_ref, other_ref, gains_ref, gains_c_ref, query_ref, key_ref, value_ref, there_ref, x_own_ref, x_other_ref, qkv_ref, scale_ref):
    own = own_ref[...].astype(F32)
    other = other_ref[...].astype(F32)
    total = jnp.sum(own * own, axis=1, keepdims=True)
    total = total + jnp.sum(other * other, axis=1, keepdims=True)
    scale = lax.rsqrt(total / D + EPSILON)
    own = (own * scale * gains_ref[0:1, :]).astype(BF16)
    other = (other * scale * gains_c_ref[0:1, :]).astype(BF16)
    x_own_ref[...] = own
    x_other_ref[...] = other
    scale_ref[...] = scale
    here = jnp.concatenate([query_ref[...], key_ref[...], value_ref[...]], axis=1)
    qkv_ref[...] = (dot(own, here) + dot(other, there_ref[...])).astype(BF16)


def project(col, own, other, gains, gains_c, w_query, w_key, w_value, there):
    rows, features = own.shape
    width = there.shape[1]
    group = GROUP_HEADS * DH
    tile = rows // 2

    def whole(*shape):
        return pl.BlockSpec(shape, lambda i, c: (0,) * len(shape))

    def mine(width):
        return pl.BlockSpec((features, width), lambda i, c: (0, c[0]))

    def rowwise(width):
        return pl.BlockSpec((tile, width), lambda i, c: (i, 0))

    return pl.pallas_call(
        project_kernel,
        grid_spec=pltpu.PrefetchScalarGridSpec(
            num_scalar_prefetch=1,
            grid=(rows // tile,),
            in_specs=[
                rowwise(features),
                rowwise(features),
                whole(2, features),
                whole(2, features),
                mine(group),
                mine(DH),
                mine(DH),
                whole(features, width),
            ],
            out_specs=[rowwise(features), rowwise(features), rowwise(width), rowwise(1)],
        ),
        out_shape=[
            jax.ShapeDtypeStruct((rows, features), BF16),
            jax.ShapeDtypeStruct((rows, features), BF16),
            jax.ShapeDtypeStruct((rows, width), BF16),
            jax.ShapeDtypeStruct((rows, 1), F32),
        ],
        compiler_params=params(24, "arbitrary"),
        cost_estimate=SMALL,
        name="project",
    )(col, own, other, gains, gains_c, w_query, w_key, w_value, there)


def head_pair(col_ref, own, other):
    first, second = own[...], other[...]
    flipped = col_ref != 0
    return jnp.concatenate(
        [jnp.where(flipped, second, first), jnp.where(flipped, first, second)], axis=1
    )


def before_kernel(tiles, place_ref, *refs):
    near, near_c, far, far_c, attended, attended_c, here, there, own_ref, other_ref = refs
    is_near = (pl.program_id(0) >= tiles // 2).astype(jnp.int32) == place_ref[0]
    heads = head_pair(place_ref[2], attended, attended_c)
    own = jnp.where(is_near, near[...], far[...]).astype(F32)
    other = jnp.where(is_near, near_c[...], far_c[...]).astype(F32)
    own_ref[...] = own + dot(heads, here[...])
    other_ref[...] = other + dot(heads, there[...])


def after_kernel(place_ref, *refs):
    own_ref, other_ref, attended, attended_c, here, there, gains_ref, gains_c_ref = refs[0:8]
    hidden_ref, x_own_ref, x_other_ref, scale_ref = refs[8:12]
    heads = head_pair(place_ref[2], attended, attended_c)
    own = own_ref[...] + dot(heads, here[...])
    other = other_ref[...] + dot(heads, there[...])
    total = jnp.sum(own * own, axis=1, keepdims=True)
    total = total + jnp.sum(other * other, axis=1, keepdims=True)
    scale = lax.rsqrt(total / D + EPSILON)
    hidden_ref[...] = own
    scale_ref[...] = scale
    x_own_ref[...] = (own * scale * gains_ref[1:2, :]).astype(BF16)
    x_other_ref[...] = (other * scale * gains_c_ref[1:2, :]).astype(BF16)


TOKEN_TILE = 256


def rowwise(width):
    return pl.BlockSpec((TOKEN_TILE, width), lambda i, p: (i, 0))


def whole(*shape):
    return pl.BlockSpec(shape, lambda i, p: (0,) * len(shape))


def hidden_before(place, tokens, attended, here, there):
    half, features = tokens[0].shape
    rows, heads = attended[0].shape
    tiles = rows // TOKEN_TILE
    per_half = half // TOKEN_TILE
    halfwise = pl.BlockSpec((TOKEN_TILE, features), lambda i, p: (i % per_half, 0))
    return pl.pallas_call(
        functools.partial(before_kernel, tiles),
        grid_spec=pltpu.PrefetchScalarGridSpec(
            num_scalar_prefetch=1,
            grid=(tiles,),
            in_specs=[halfwise] * 4 + [rowwise(heads)] * 2 + [whole(2 * heads, features)] * 2,
            out_specs=[rowwise(features)] * 2,
        ),
        out_shape=[jax.ShapeDtypeStruct((rows, features), F32)] * 2,
        compiler_params=params(56, "arbitrary"),
        cost_estimate=pl.CostEstimate(
            flops=8 * rows * features * heads,
            bytes_accessed=16 * rows * features,
            transcendentals=0,
        ),
        name="hidden_before",
    )(place, *tokens, *attended, here, there)


def hidden_after(place, before, attended, here, there, gains, gains_c):
    rows, features = before[0].shape
    heads = attended[0].shape[1]
    return pl.pallas_call(
        after_kernel,
        grid_spec=pltpu.PrefetchScalarGridSpec(
            num_scalar_prefetch=1,
            grid=(rows // TOKEN_TILE,),
            in_specs=[rowwise(features)] * 2
            + [rowwise(heads)] * 2
            + [whole(2 * heads, features)] * 2
            + [whole(2, features)] * 2,
            out_specs=[rowwise(features)] * 3 + [rowwise(1)],
        ),
        out_shape=[
            jax.ShapeDtypeStruct((rows, features), F32),
            jax.ShapeDtypeStruct((rows, features), BF16),
            jax.ShapeDtypeStruct((rows, features), BF16),
            jax.ShapeDtypeStruct((rows, 1), F32),
        ],
        compiler_params=params(56, "arbitrary"),
        cost_estimate=SMALL,
        name="hidden_after",
    )(place, *before, *attended, here, there, gains, gains_c)


def expert_kernel(shared, aliased, first, order_ref, *refs):
    x_own, x_other, o_own, o_other, gates_ref = refs[0:5]
    weights = refs[5:17]
    grads = refs[17 + aliased : 19 + aliased]
    pair_ref, inner_ref = refs[19 + aliased : 21 + aliased]
    step = pl.program_id(0) + first
    rows, features = x_own.shape
    tile = 512
    up_own = jnp.concatenate([weights[k][0] for k in (0, 1, 6, 7)], axis=1)
    up_other = jnp.concatenate([weights[k][0] for k in (2, 3, 8, 9)], axis=1)
    down_own = jnp.concatenate([weights[k][0] for k in (4, 10)], axis=0)
    down_other = jnp.concatenate([weights[k][0] for k in (5, 11)], axis=0)

    def token_tile(t, carry):
        at = pl.ds(pl.multiple_of(t * tile, tile), tile)
        pre = dot(x_own[at, :], up_own) + dot(x_other[at, :], up_other)
        back = dot_nt(o_own[at, :], down_own) + dot_nt(o_other[at, :], down_other)
        for k in range(2):
            pre_gate = pre[:, 2 * k * LANES : (2 * k + 1) * LANES]
            pre_up = pre[:, (2 * k + 1) * LANES : (2 * k + 2) * LANES]
            inner_grad = back[:, k * LANES : (k + 1) * LANES]
            sigmoid = 1.0 / (1.0 + jnp.exp(-pre_gate))
            silu = pre_gate * sigmoid
            inner = silu * pre_up
            if not shared:
                shape = (gates_ref.shape[0], LANES)
                expert = lax.broadcasted_iota(jnp.int32, shape, 0) % (gates_ref.shape[0] // 3)
                chosen = (expert == order_ref[2 * step + k]).astype(F32).astype(BF16)
                gate = dot_tn(gates_ref[:, at], chosen)
                inner = gate * inner
                inner_grad = gate * inner_grad
            gate_grad = inner_grad * pre_up * (sigmoid * (1.0 + pre_gate * (1.0 - sigmoid)))
            inner_ref[0, at, k * LANES : (k + 1) * LANES] = inner.astype(BF16)
            pair_ref[0, at, 2 * k * LANES : (2 * k + 1) * LANES] = gate_grad.astype(BF16)
            pair_ref[0, at, (2 * k + 1) * LANES : (2 * k + 2) * LANES] = (
                inner_grad * silu
            ).astype(BF16)
        return carry

    lax.fori_loop(0, rows // tile, token_tile, 0)
    pairs = pair_ref[0]
    for h, x in enumerate((x_own, x_other)):
        wide = dot_tn(x[...], pairs).astype(BF16)
        for k in range(2):
            grads[k][0, h * features : (h + 1) * features, 0 : 2 * LANES] = wide[
                :, 2 * k * LANES : (2 * k + 2) * LANES
            ]
    inner = inner_ref[0]
    tile = 256
    for h, o in enumerate((o_own, o_other)):
        for j in range(features // tile):
            low = dot_tn(inner, o[:, j * tile : (j + 1) * tile]).astype(BF16)
            for k in range(2):
                for b in range(tile // LANES):
                    at = h * features + j * tile + b * LANES
                    grads[k][0, at : at + LANES, 2 * LANES :] = low[
                        k * LANES : (k + 1) * LANES, b * LANES : (b + 1) * LANES
                    ]


def expert_specs(features, place, wide, low):
    specs = []
    if wide:
        block = pl.BlockSpec((1, features, LANES), lambda i, o: (place(i, o)[0], 0, place(i, o)[1]))
        specs += [block] * 4
    if low:
        block = pl.BlockSpec((1, LANES, features), lambda i, o: (*place(i, o), 0))
        specs += [block] * 2
    return specs


def expert_grads(order, first, last, total, x, o, gates, weights, kept):
    shared = total is None
    steps = last - first
    rows, features = x[0].shape
    aliased = len(kept)

    def fixed(*shape):
        return pl.BlockSpec(shape, lambda i, o: (0,) * len(shape))

    def stepped(*shape):
        return pl.BlockSpec((1, *shape), lambda i, o: (i, 0, 0))

    def placed(*shape):
        return pl.BlockSpec((1, *shape), lambda i, o: (i + first, 0, 0))

    specs = []
    for k in range(2):
        if shared:

            def picked(i, o, k=k):
                return 0, 2 * o[o.shape[0] - 1] + k

        else:

            def picked(i, o, k=k):
                return o[2 * (i + first) + k], o[o.shape[0] - 1]

        specs += expert_specs(features, picked, True, True)
    total = steps if shared else total
    return pl.pallas_call(
        functools.partial(expert_kernel, shared, aliased, first),
        grid_spec=pltpu.PrefetchScalarGridSpec(
            num_scalar_prefetch=1,
            grid=(steps,),
            in_specs=[fixed(rows, features)] * 4
            + [fixed(*gates.shape)]
            + specs
            + [pl.BlockSpec(memory_space=pl.ANY)] * aliased,
            out_specs=[stepped(2 * features, 3 * LANES)] * 2
            + [placed(rows, 4 * LANES), placed(rows, 2 * LANES)],
        ),
        out_shape=[jax.ShapeDtypeStruct((steps, 2 * features, 3 * LANES), BF16)] * 2
        + [
            jax.ShapeDtypeStruct((total, rows, 4 * LANES), BF16),
            jax.ShapeDtypeStruct((total, rows, 2 * LANES), BF16),
        ],
        input_output_aliases={18 + k: 2 + k for k in range(aliased)},
        compiler_params=params(40, "arbitrary"),
        cost_estimate=SMALL,
        name="expert_grads",
    )(order, *x, *o, gates, *weights, *weights, *kept)


def mix_kernel(back, group, order_ref, *refs):
    acts_ref, shared_ref = refs[0:2]
    each = 2 if back else 1
    count = 2 * group * each
    weights = refs[2 : 2 + count]
    shared = refs[2 + count : 2 + count + 2 * each]
    out_ref, total_ref = refs[2 + count + 2 * each :]
    step = pl.program_id(0)
    rows = out_ref.shape[0]
    tile = 512
    times = dot_nt if back else dot
    along = 1 if back else 0

    @pl.when(step == 0)
    def _():
        both = jnp.concatenate([w[0] for w in shared], axis=along)
        for t in range(rows // tile):
            at = slice(t * tile, (t + 1) * tile)
            total_ref[at, :] = times(shared_ref[0, at, :], both)

    both = jnp.concatenate([w[0] for w in weights], axis=along)
    for t in range(rows // tile):
        at = slice(t * tile, (t + 1) * tile)
        acts = jnp.concatenate([acts_ref[g, at, :] for g in range(group)], axis=1)
        total_ref[at, :] += times(acts, both)

    @pl.when(step == pl.num_programs(0) - 1)
    def _():
        out_ref[...] = total_ref[...].astype(out_ref.dtype)


def mix(back, dtype, order, acts, shared_acts, weights, shared_weights):
    pairs, rows, width = acts.shape
    features = weights[0].shape[1] if back else weights[0].shape[2]
    group = 4 if pairs % 4 == 0 else 1

    def spec(place):
        if back:
            return pl.BlockSpec((1, features, LANES), lambda i, o: (place(i, o)[0], 0, place(i, o)[1]))
        return pl.BlockSpec((1, LANES, features), lambda i, o: (*place(i, o), 0))

    def routed(k):
        return spec(lambda i, o: (o[2 * group * i + k], o[o.shape[0] - 1]))

    def common(k):
        return spec(lambda i, o: (0, 2 * o[o.shape[0] - 1] + k))

    return pl.pallas_call(
        functools.partial(mix_kernel, back, group),
        grid_spec=pltpu.PrefetchScalarGridSpec(
            num_scalar_prefetch=1,
            grid=(pairs // group,),
            in_specs=[
                pl.BlockSpec((group, rows, width), lambda i, o: (i, 0, 0)),
                pl.BlockSpec((1, rows, width), lambda i, o: (0, 0, 0)),
            ]
            + [routed(k) for k in range(2 * group) for _ in weights]
            + [common(k) for k in range(2) for _ in weights],
            out_specs=pl.BlockSpec((rows, features), lambda i, o: (0, 0)),
            scratch_shapes=[pltpu.VMEM((rows, features), F32)],
        ),
        out_shape=jax.ShapeDtypeStruct((rows, features), dtype),
        compiler_params=params(48, "arbitrary"),
        cost_estimate=SMALL,
        name="mix",
    )(order, acts, shared_acts, *weights * (2 * group), *shared_weights * 2)


def ring_of(size):
    return list(range(0, size, 2)) + list(range(1, size, 2))[::-1]


def unpack_kernel(aliased, index_ref, *refs):
    chunks = refs[0:2]
    gate_ref, up_ref, down_ref = refs[2 + aliased : 5 + aliased]
    blocks = chunks[0].shape[1] // LANES

    def write(chunk_ref):
        gate_ref[0] = chunk_ref[0, :, 0:LANES].astype(F32)
        up_ref[0] = chunk_ref[0, :, LANES : 2 * LANES].astype(F32)
        for b in range(blocks):
            at = slice(b * LANES, (b + 1) * LANES)
            down_ref[0, :, at] = chunk_ref[0, at, 2 * LANES :].astype(F32)

    for k in range(2):
        pl.when(pl.program_id(1) == k)(lambda k=k: write(chunks[k]))


def unpack(index, chunks, shapes, outs):
    count, rows, width = chunks[0].shape
    chunk = pl.BlockSpec((1, rows, width), lambda i, d, n: (i, 0, 0))

    def wide(i, d, n):
        return (n[2 * i + d], 0, n[2 * count])

    def low(i, d, n):
        return (n[2 * i + d], n[2 * count], 0)

    aliased = len(outs)
    return pl.pallas_call(
        functools.partial(unpack_kernel, aliased),
        grid_spec=pltpu.PrefetchScalarGridSpec(
            num_scalar_prefetch=1,
            grid=(count, 2),
            in_specs=[chunk, chunk] + [pl.BlockSpec(memory_space=pl.ANY)] * aliased,
            out_specs=[
                pl.BlockSpec((1, rows, LANES), wide),
                pl.BlockSpec((1, rows, LANES), wide),
                pl.BlockSpec((1, LANES, rows), low),
            ],
        ),
        out_shape=[jax.ShapeDtypeStruct(shape, F32) for shape in shapes],
        input_output_aliases={3 + k: k for k in range(aliased)},
        compiler_params=params(16, "arbitrary", "arbitrary"),
        cost_estimate=SMALL,
        name="unpack",
    )(index, *chunks, *outs)


def unpack_late_kernel(col_ref, first_ref, second_ref, *outs):
    sgate, sup, sdown, query, key, value, out = outs
    features = first_ref.shape[1]
    flipped = col_ref[0] != 0
    for c in range(2):
        for b in range(14):
            lanes = slice(b % 7 * LANES, (b % 7 + 1) * LANES)
            first, second = first_ref[c, :, lanes], second_ref[c, :, lanes]
            if b >= 7:
                first, second = second, first
            block = jnp.where(flipped, second, first).astype(F32)
            if b < 6:
                at = slice((2 * c + b // 3) * LANES, (2 * c + b // 3 + 1) * LANES)
                if b % 3 < 2:
                    (sgate, sup)[b % 3][:, at] = block
                else:
                    for k in range(features // LANES):
                        here = slice(k * LANES, (k + 1) * LANES)
                        sdown[at, here] = block[here, :]
            elif b < 9:
                at = (GROUP_HEADS * c + b - 6) * LANES
                query[:, at : at + LANES] = block
            elif b < 11:
                (key, value)[b - 9][:, c * LANES : (c + 1) * LANES] = block
            else:
                at = (GROUP_HEADS * c + b - 11) * LANES
                out[at : at + LANES, :] = block.T


def unpack_late(col, first, second, shapes):
    spec = pl.BlockSpec(memory_space=pltpu.VMEM)
    return pl.pallas_call(
        unpack_late_kernel,
        in_specs=[pl.BlockSpec(memory_space=pltpu.SMEM), spec, spec],
        out_specs=[spec] * len(shapes),
        out_shape=[jax.ShapeDtypeStruct(shape, F32) for shape in shapes],
        compiler_params=params(48),
        name="unpack_late",
    )(col, first, second)


LATE_ROUND = 3


def add_rounded(left, right):
    return (left.astype(F32) + right.astype(F32)).astype(BF16)


def body(
    tokens_in,
    norm_gain_attn,
    w_query,
    w_key,
    w_value,
    w_out,
    norm_gain_ffn,
    w_gate,
    w_up,
    w_down,
    w_shared_gate,
    w_shared_up,
    w_shared_down,
    routes,
    gate_weights,
    seq_lengths,
    out_grad,
):
    row = lax.axis_index("row")
    col = lax.axis_index("col")
    dp = lax.axis_index("dp")
    dp_size = lax.axis_size("dp")
    local_rows, local_features = tokens_in.shape
    experts = w_gate.shape[0]
    group_width = GROUP_HEADS * DH
    col_ref = col.reshape(1)

    ring_size = min(8, dp_size)
    ring = ring_of(ring_size)
    starts = range(0, dp_size, ring_size)
    rights = [
        (g + ring[k], g + ring[(k + 1) % ring_size]) for g in starts for k in range(ring_size)
    ]
    lefts = [(b, a) for a, b in rights]
    routes_of = [
        [(2 * a, 2 * b) for a, b in ways[0]] + [(2 * a + 1, 2 * b + 1) for a, b in ways[1]]
        for ways in ((rights, lefts), (lefts, rights))
    ]
    place_of = [ring.index(k) for k in range(ring_size)]
    place = jnp.asarray(place_of, jnp.int32)[dp % ring_size]
    signs = [1 - 2 * col, 2 * col - 1]

    def send(values, which):
        if ring_size == 1:
            return values
        return lax.ppermute(values, ("dp", "col"), routes_of[which])

    def chunk_at(step, which):
        return (place - signs[which] * step) % ring_size

    def across_rings(values):
        if len(starts) == 1:
            return values
        peers = [[g + k for g in starts] for k in range(ring_size)]
        return lax.psum(values, "dp", axis_index_groups=peers)

    where = jnp.stack([row, seq_lengths[0], col])
    tokens_y = swap(tokens_in, "row")
    tokens_c = swap(tokens_in, "col")
    count = min(ring_size, 4)
    member = dp % count
    there, gains, out_y = their_columns(
        jnp.stack([col, member]),
        w_query,
        w_key,
        w_value,
        norm_gain_attn[None],
        norm_gain_ffn[None],
        w_out,
        count,
    )
    there = swap(there, "col")
    gains_c = swap(gains, "col")

    def project_half(own, other):
        return project(col_ref, own, other, gains, gains_c, w_query, w_key, w_value, there)

    near = project_half(tokens_in, tokens_c)
    gate_c = swap(w_gate, "col")
    out_y = swap(out_y, "row")
    tokens_y = after(tokens_y, near[2], out_y)
    tokens_yc = swap(tokens_y, "col")
    grad_cut = local_rows // 8 * 5
    grad_y = swap(after(out_grad[:grad_cut], tokens_y), "row")
    far = project_half(tokens_y, tokens_yc)

    def double(part, bit, *others):
        if bit >= count:
            return part
        pairs = [(m, m ^ bit) for m in range(dp_size)]
        came = after(lax.ppermute(part, "dp", pairs), *others)
        return join(member // bit % 2, part, came)

    out_y = double(out_y, 1)
    where = after(where, out_y, grad_y)

    w_sgate, w_sup, w_sdown = w_shared_gate[None], w_shared_up[None], w_shared_down[None]
    up_c = swap(after(w_up, gate_c, tokens_yc), "col")

    attended = attend(where, near[2], far[2])
    attended_y = swap(attended, "row")
    attended_c = swap(attended, "col")
    out_c = swap(after(w_out, tokens_yc), "col")
    before = hidden_before(
        where,
        [tokens_in, tokens_c, tokens_y, tokens_yc],
        [attended, attended_c],
        w_out,
        out_c,
    )
    down_c = swap(after(w_down, up_c, attended_c), "col")
    rest_y = swap(after(out_grad[grad_cut:], attended_c), "row")
    attended_y = after(attended_y, before[0])
    out_y = double(out_y, 2, attended_y)
    out_yc = swap(out_y, "col")
    attended_yc = swap(attended_y, "col")
    grad_own = join(row, out_grad, jnp.concatenate([grad_y, rest_y], axis=0))
    grad_other = swap(grad_own, "col")
    hidden, x_own, x_other, scale_ffn = hidden_after(
        where, before, [attended_y, attended_yc], out_y, out_yc, gains, gains_c
    )
    sgate_c, sup_c, sdown_c = (
        swap(after(w, attended_yc), "col") for w in (w_sgate, w_sup, w_sdown)
    )

    choices = jnp.arange(experts, dtype=jnp.int32)[:, None]
    dense = sum(
        jnp.where(routes[:, k][None, :] == choices, gate_weights[:, k][None, :], 0.0)
        for k in range(routes.shape[1])
    )
    gates = []
    for _ in range(3):
        gates.append(lax.reduce_precision(dense, 8, 7))
        dense = dense - gates[-1]
    gates = jnp.concatenate(gates, axis=0).astype(BF16)

    each = experts // (2 * ring_size)
    orders = []
    for s in range(ring_size):
        for k in range(each):
            for which in range(2):
                second = col if which == 0 else 1 - col
                orders.append(2 * each * chunk_at(s, which) + each * second + k)
    order = jnp.stack(orders + [col]).astype(jnp.int32)
    pairs_total = experts // 2
    routed = [w_gate, w_up, gate_c, up_c, w_down, down_c]
    shared = [w_sgate, w_sup, sgate_c, sup_c, w_sdown, sdown_c]

    def run(first, last, order, kept):
        return expert_grads(
            order,
            first,
            last,
            pairs_total,
            [x_own, x_other],
            [grad_own, grad_other],
            gates,
            routed,
            kept,
        )

    first = run(0, each, order, ())
    kept = first[2:]
    sums = [first[0], first[1]]
    runs = {}
    mixed = {}

    def work_experts(first, last):
        def work(order):
            nonlocal kept
            result = run(first, last, order, tuple(kept))
            kept = result[2:]
            for at in range(first, last):
                runs[at] = (result[0], result[1], at - first)
            return kept[0]

        return work

    def work_shared(order):
        runs["shared"] = expert_grads(
            order, 0, 1, None, [x_own, x_other], [grad_own, grad_other], gates, shared, ()
        )
        return runs["shared"][2]

    def work_mix(back, half):
        def work(order):
            pick = slice(2 * half, 2 * half + 2) if back else slice(4 + half, 5 + half)
            mixed[back, half] = mix(
                back,
                BF16 if half else F32,
                order,
                kept[0 if back else 1],
                runs["shared"][2 if back else 3],
                routed[pick],
                shared[pick],
            )
            return mixed[back, half]

        return work

    tasks = [work_experts(at, at + each) for at in range(each, pairs_total, each)]
    tasks += [work_shared, work_mix(True, 1), work_mix(True, 0)]
    later = [work_mix(False, 1), work_mix(False, 0)]
    got = [None, None]
    if ring_size > 1:
        got[0] = send(sums[0], 0)
        tasks.pop(0)(after(order, *sums))
        got[1] = send(after(sums[1], kept[0]), 1)
    for s in range(1, ring_size):
        for k in range(2):
            last = sums
            if tasks:
                last = [tasks.pop(0)(after(order, *last))]
            got[k] = after(got[k], *last)
            parts = [runs[at] for at in range(each * s, each * s + each)]
            mine = [p[k][p[2] : p[2] + 1] for p in parts]
            mine = mine[0] if each == 1 else jnp.concatenate(mine, axis=0)
            sums[k] = add_rounded(got[k], mine)
            if s + 1 < ring_size:
                got[k] = send(sums[k], k)
    while tasks:
        tasks.pop(0)(after(order, *sums))
    sums = [across_rings(total) for total in sums]
    waves = [[total[:, :local_features] for total in sums]]
    crossed = [swap(total[:, local_features:], "col") for total in sums]
    waves.append([crossed[1], crossed[0]])

    start = row * local_rows

    def my_rows(values):
        return lax.dynamic_slice_in_dim(values, start, local_rows, axis=0)

    def their_rows(values):
        return lax.dynamic_slice_in_dim(values, local_rows - start, local_rows, axis=0)

    normed_grad = mixed[True, 0] + swap(mixed[True, 1], "col").astype(F32)
    normed_grad = normed_grad + swap(normed_grad.astype(BF16), "row").astype(F32)
    gain_ffn_part = jnp.sum(my_rows(normed_grad * hidden * scale_ffn), axis=0)
    scaled = normed_grad * norm_gain_ffn
    products = jnp.sum(scaled * hidden, axis=1, keepdims=True)
    mean = (products + swap(products, "col")) / D
    hidden_grad = grad_own.astype(F32) + scale_ffn * scaled - hidden * scale_ffn**3 * mean
    attn_grad = hidden_grad.astype(BF16)
    attn_grad_c = swap(attn_grad, "col")

    qkv_grad = attend_back(where, near[2], far[2], attn_grad, attn_grad_c, w_out, out_c)
    packs = late_grads(
        where,
        near[0:2],
        far[0:2],
        qkv_grad,
        attended,
        attn_grad,
        attn_grad_c,
        runs["shared"][0:2],
    )

    packs = [
        pack.reshape(2, ring_size, local_features // ring_size, pack.shape[2]) for pack in packs
    ]

    def late_chunk(step, which):
        at = chunk_at(step, which)
        return lax.dynamic_index_in_dim(packs[which], at, axis=1, keepdims=False)

    def late_place(current, step, which):
        at = chunk_at(ring_size - 1 + step, which)
        return lax.dynamic_update_index_in_dim(late_out[which], current, at, 1)

    late_out = [jnp.zeros(pack.shape, BF16) for pack in packs]
    late = [late_chunk(0, k) for k in range(2)]
    late_done = 0
    late_total = 2 * (ring_size - 1)

    def late_turn():
        totals = [across_rings(values) for values in late]
        others = [swap(values[1], "col") for values in totals]
        for k in range(2):
            late[k] = in_order(totals[k][0:1], others[1 - k][None], col, 0)
            late_out[k] = late_place(late[k], 0, k)

    def late_finish(got, last):
        nonlocal late_done
        late_done += 1
        for k in range(2):
            values = after(got[k], *last)
            if late_done < ring_size:
                late[k] = add_rounded(values, late_chunk(late_done, k))
            else:
                late[k] = values
                late_out[k] = late_place(values, late_done - ring_size + 1, k)
            last = [late[k]]
        if late_done == ring_size - 1:
            late_turn()

    shapes = [w_gate.shape, w_up.shape, w_down.shape]
    placed = ()

    def place_chunks(wave, step, chunks, placed):
        index = []
        for k in range(each):
            for which in range(2):
                second = col if which == 0 else 1 - col
                at = chunk_at(ring_size - 1 + step, which)
                index.append(2 * each * at + each * second + k)
        index.append(col if wave == 0 else 1 - col)
        return unpack(jnp.stack(index).astype(jnp.int32), chunks, shapes, placed)

    if late_total == 0:
        late_turn()
    rounds = [(wave, step) for wave in range(2) for step in range(ring_size - 1)]
    for number, (wave, step) in enumerate(rounds):
        if step == 0:
            chunks = waves[wave]
        if number == LATE_ROUND:
            late = [after(values, *chunks) for values in late]
        steps = 1 if number >= LATE_ROUND else 0
        if number >= len(rounds) - LATE_ROUND:
            steps = 2
        steps = min(steps, late_total - late_done)
        got = [send(chunks[k], k) for k in range(2)]
        late_got = [send(late[k], k) for k in range(2)] if steps else None
        placed = place_chunks(wave, step, chunks, placed)
        last = placed[0:1]
        if number in (LATE_ROUND + 1, LATE_ROUND + 2):
            last = [later.pop(0)(after(order, *last))]
        if number == LATE_ROUND + 5:
            qkv_grad = after(qkv_grad, *last)
        for k in range(2):
            got[k] = after(got[k], *last)
        for at in range(steps):
            if at:
                late_got = [send(late[k], k) for k in range(2)]
            late_finish(late_got, got)
        chunks = got
        if step == ring_size - 2:
            placed = place_chunks(wave, step + 1, chunks, placed)
    while later:
        later.pop(0)(order)
    if not rounds:
        for wave in range(2):
            placed = place_chunks(wave, 0, waves[wave], placed)
    while late_done < late_total:
        late_finish([send(late[k], k) for k in range(2)], placed[0:1])
    gate_grad, up_grad, down_grad = placed
    shapes = [w.shape for w in (w_shared_gate, w_shared_up, w_shared_down)]
    shapes += [w.shape for w in (w_query, w_key, w_value, w_out)]
    finals = unpack_late(
        col_ref, *[out.reshape(2, local_features, out.shape[3]) for out in late_out], shapes
    )
    shared_gate_grad, shared_up_grad, shared_down_grad = finals[0:3]
    query_grad, key_grad, value_grad, out_proj_grad = finals[3:7]

    ffn_sum = mixed[False, 0] + swap(mixed[False, 1], "col").astype(F32)
    ffn_rows = my_rows(ffn_sum) + swap(their_rows(ffn_sum).astype(BF16), "row").astype(F32)
    block_out = (my_rows(hidden) + ffn_rows).astype(BF16)

    here = jnp.concatenate(
        [halves(w, 1, col)[0] for w in (w_query, w_key, w_value)], axis=1
    )
    tokens_back = dot_nt(qkv_grad, here) + swap(
        dot_nt(qkv_grad, there).astype(BF16), "col"
    ).astype(F32)
    tokens_back = my_rows(tokens_back) + swap(
        their_rows(tokens_back).astype(BF16), "row"
    ).astype(F32)
    scale_attn = near[3]
    tokens_f32 = tokens_in.astype(F32)
    gain_attn_part = jnp.sum(tokens_back * tokens_f32 * scale_attn, axis=0)
    scaled = tokens_back * norm_gain_attn
    products = jnp.sum(scaled * tokens_f32, axis=1, keepdims=True)
    mean = (products + swap(products, "col")) / D
    tokens_grad = (
        my_rows(hidden_grad) + scale_attn * scaled - tokens_f32 * scale_attn**3 * mean
    ).astype(BF16)

    gain_parts = jnp.stack([gain_attn_part, gain_ffn_part])
    bit = 1
    while bit < ring_size:
        pairs = [(g + k, g + (k ^ bit)) for g in starts for k in range(ring_size)]
        gain_parts = gain_parts + lax.ppermute(gain_parts, "dp", pairs)
        bit *= 2
    gain_parts = across_rings(gain_parts + swap(gain_parts, "row"))

    return (
        block_out,
        tokens_grad,
        gain_parts[0],
        query_grad,
        key_grad,
        value_grad,
        out_proj_grad,
        gain_parts[1],
        gate_grad,
        up_grad,
        down_grad,
        shared_gate_grad,
        shared_up_grad,
        shared_down_grad,
    )


def solution(mesh):
    in_specs = (
        P(("dp", "row"), "col"),
        P("col"),
        P("col", "row"),
        P("col", "row"),
        P("col", "row"),
        P("row", "col"),
        P("col"),
        P(None, "col", "row"),
        P(None, "col", "row"),
        P(None, "row", "col"),
        P("col", "row"),
        P("col", "row"),
        P("row", "col"),
        P("dp", None),
        P("dp", None),
        P("dp"),
        P(("dp", "row"), "col"),
    )
    out_specs = (
        P(("dp", "row"), "col"),
        P(("dp", "row"), "col"),
        P("col"),
        P("col", "row"),
        P("col", "row"),
        P("col", "row"),
        P("row", "col"),
        P("col"),
        P(None, "col", "row"),
        P(None, "col", "row"),
        P(None, "row", "col"),
        P("col", "row"),
        P("col", "row"),
        P("row", "col"),
    )
    return jax.shard_map(body, mesh=mesh, in_specs=in_specs, out_specs=out_specs, check_vma=False)
```

```python
import functools

import jax
import jax.numpy as jnp
import numpy as np
from jax import lax
from jax.experimental import pallas as pl
from jax.experimental.pallas import tpu as pltpu
from jax.sharding import PartitionSpec as P

D = 1536
HQ = 12
HK = 4
DH = 128
GROUP_HEADS = HQ // HK
LANES = 128

EPSILON = 1e-05
F32 = jnp.float32
BF16 = jnp.bfloat16
MIB = 1024 * 1024
SMALL = pl.CostEstimate(flops=0, bytes_accessed=0, transcendentals=0)


def params(mib, *semantics):
    return pltpu.CompilerParams(
        dimension_semantics=semantics or None, vmem_limit_bytes=mib * MIB
    )


def dot(left, right):
    return jnp.dot(left, right, preferred_element_type=F32)


def dot_nt(left, right):
    return lax.dot_general(left, right, (((1,), (1,)), ((), ())), preferred_element_type=F32)


def dot_tn(left, right):
    return lax.dot_general(left, right, (((0,), (0,)), ((), ())), preferred_element_type=F32)


def after(values, *others):
    return lax.optimization_barrier((values, *others))[0]


def swap(values, axis):
    return lax.ppermute(values, axis, [(0, 1), (1, 0)])


def halves(values, axis, mine):
    size = values.shape[axis] // 2
    low = lax.slice_in_dim(values, 0, size, axis=axis)
    high = lax.slice_in_dim(values, size, 2 * size, axis=axis)
    return jnp.where(mine == 0, low, high), jnp.where(mine == 0, high, low)


def in_order(own, other, mine, axis):
    return jnp.concatenate(
        [jnp.where(mine == 0, own, other), jnp.where(mine == 0, other, own)], axis=axis
    )


def gather_rows(place_ref, own_ref, other_ref, all_ref):
    row = place_ref[0]
    rows = own_ref.shape[0]
    all_ref[pl.ds(pl.multiple_of(row * rows, rows), rows), :] = own_ref[...]
    all_ref[pl.ds(pl.multiple_of((1 - row) * rows, rows), rows), :] = other_ref[...]


def head_rows(ref, first, block):
    return jnp.concatenate(
        [ref[first : first + block, h * DH : (h + 1) * DH] for h in range(GROUP_HEADS)], axis=0
    )


def key_probs(query, key, first, length):
    block, keys = query.shape[0] // GROUP_HEADS, key.shape[0]
    scores = dot_nt(query, key) * DH ** (-0.5)
    shape = (block, keys)
    query_at = lax.broadcasted_iota(jnp.int32, shape, 0) + first
    key_at = lax.broadcasted_iota(jnp.int32, shape, 1)
    allowed = (key_at <= query_at) & (key_at < length)
    allowed = jnp.concatenate([allowed] * GROUP_HEADS, axis=0)
    scores = jnp.where(allowed, scores, -1e30)
    weights = jnp.exp(scores - jnp.max(scores, axis=1, keepdims=True))
    return weights * (1.0 / jnp.sum(weights, axis=1, keepdims=True))


def attend_kernel(place_ref, own_ref, other_ref, out_ref, all_ref):
    gather_rows(place_ref, own_ref, other_ref, all_ref)
    rows = own_ref.shape[0]
    block = 256
    width = GROUP_HEADS * DH
    for at in range(2 * rows // block):
        first, keys = at * block, (at + 1) * block
        query = head_rows(all_ref, first, block)
        key = all_ref[0:keys, width : width + DH]
        value = all_ref[0:keys, width + DH : width + 2 * DH]
        probs = key_probs(query, key, first, place_ref[1])
        result = dot(probs.astype(BF16), value).astype(BF16)
        for h in range(GROUP_HEADS):
            out_ref[first : first + block, h * DH : (h + 1) * DH] = result[
                h * block : (h + 1) * block
            ]


def attend(place, own, other):
    rows, width = own.shape
    spec = pl.BlockSpec(memory_space=pltpu.VMEM)
    return pl.pallas_call(
        attend_kernel,
        out_shape=jax.ShapeDtypeStruct((2 * rows, GROUP_HEADS * DH), BF16),
        in_specs=[pl.BlockSpec(memory_space=pltpu.SMEM), spec, spec],
        out_specs=spec,
        scratch_shapes=[pltpu.VMEM((2 * rows, width), BF16)],
        compiler_params=params(32),
        cost_estimate=SMALL,
        name="attend",
    )(place, own, other)


def attend_back_kernel(
    place_ref, own_ref, other_ref, grad_ref, grad_c_ref, out_ref, out_c_ref, result_ref, all_ref, total_ref
):
    gather_rows(place_ref, own_ref, other_ref, all_ref)
    rows = own_ref.shape[0]
    block = 256
    width = GROUP_HEADS * DH
    group = pl.ds(pl.multiple_of(place_ref[2] * width, width), width)
    blocks = 2 * rows // block
    for at in reversed(range(blocks)):
        first, keys = at * block, (at + 1) * block
        query = head_rows(all_ref, first, block)
        key = all_ref[0:keys, width : width + DH]
        value = all_ref[0:keys, width + DH : width + 2 * DH]
        probs = key_probs(query, key, first, place_ref[1])
        grad = dot_nt(grad_ref[first:keys, :], out_ref[group, :])
        grad = (grad + dot_nt(grad_c_ref[first:keys, :], out_c_ref[group, :])).astype(BF16)
        grad = jnp.concatenate(
            [grad[:, h * DH : (h + 1) * DH] for h in range(GROUP_HEADS)], axis=0
        )
        probs_grad = dot_nt(grad, value)
        carried = jnp.sum(probs * probs_grad, axis=1, keepdims=True)
        score_grad = (probs * (probs_grad - carried)).astype(BF16)
        query_back = (dot(score_grad, key) * DH ** (-0.5)).astype(BF16)
        for h in range(GROUP_HEADS):
            result_ref[first:keys, h * DH : (h + 1) * DH] = query_back[
                h * block : (h + 1) * block
            ]
        key_back = dot_tn(score_grad, query)
        value_back = dot_tn(probs.astype(BF16), grad)
        if at == blocks - 1:
            total_ref[:, 0:DH] = key_back
            total_ref[:, DH:] = value_back
        else:
            total_ref[0:keys, 0:DH] += key_back
            total_ref[0:keys, DH:] += value_back
    result_ref[:, width : width + DH] = (total_ref[:, 0:DH] * DH ** (-0.5)).astype(BF16)
    result_ref[:, width + DH :] = total_ref[:, DH:].astype(BF16)


def attend_back(place, own, other, grad, grad_c, w_out, out_c):
    rows, width = own.shape
    spec = pl.BlockSpec(memory_space=pltpu.VMEM)
    return pl.pallas_call(
        attend_back_kernel,
        out_shape=jax.ShapeDtypeStruct((2 * rows, width), BF16),
        in_specs=[pl.BlockSpec(memory_space=pltpu.SMEM)] + [spec] * 6,
        out_specs=spec,
        scratch_shapes=[
            pltpu.VMEM((2 * rows, width), BF16),
            pltpu.VMEM((2 * rows, 2 * DH), F32),
        ],
        compiler_params=params(48),
        cost_estimate=SMALL,
        name="attend_back",
    )(place, own, other, grad, grad_c, w_out, out_c)


def late_kernel(place_ref, *refs):
    near, near_c, far, far_c, qkv_ref, attended_ref, grad_ref, grad_c_ref = refs[0:8]
    shared = refs[8:10]
    outs = refs[10:12]
    rows, features = near.shape
    own_rows = pl.ds(pl.multiple_of(place_ref[0] * rows, rows), rows)
    far_rows = pl.ds(pl.multiple_of((1 - place_ref[0]) * rows, rows), rows)
    split = 7 * LANES

    def store(h, at, values):
        values = values.astype(BF16)
        for part in range(2):
            low, high = max(at, part * split), min(at + values.shape[1], (part + 1) * split)
            if low < high:
                piece = values[:, low - at : high - at]
                to = slice(low - part * split, high - part * split)

                @pl.when(place_ref[2] == 0)
                def _(part=part, to=to, piece=piece):
                    outs[part][h, :, to] = piece

                @pl.when(place_ref[2] != 0)
                def _(part=part, to=to, piece=piece):
                    outs[1 - part][h, :, to] = piece

    for h, (x, y, grad) in enumerate(((near, far, grad_ref), (near_c, far_c, grad_c_ref))):
        for k in range(2):
            store(h, 3 * LANES * k, shared[k][0, h * features : (h + 1) * features, :])
        project = dot_tn(x[...], qkv_ref[own_rows, :]) + dot_tn(y[...], qkv_ref[far_rows, :])
        store(h, 6 * LANES, project)
        store(h, 11 * LANES, dot_tn(grad[...], attended_ref[...]))


def late_grads(place, near, far, qkv_grad, attended, grad, grad_c, shared):
    features = near[0].shape[1]
    spec = pl.BlockSpec(memory_space=pltpu.VMEM)
    return pl.pallas_call(
        late_kernel,
        out_shape=[jax.ShapeDtypeStruct((2, features, 7 * LANES), BF16)] * 2,
        in_specs=[pl.BlockSpec(memory_space=pltpu.SMEM)] + [spec] * 10,
        out_specs=[spec] * 2,
        compiler_params=params(40),
        cost_estimate=SMALL,
        name="late_grads",
    )(place, *near, *far, qkv_grad, attended, grad, grad_c, *shared)


def columns_kernel(
    place_ref, query_ref, key_ref, value_ref, gain_ref, gain_ffn_ref, w_out_ref, out_ref, gains_ref, share_ref
):
    share_ref[...] = w_out_ref[...]
    gains_ref[0:1, :] = gain_ref[...]
    gains_ref[1:2, :] = gain_ffn_ref[...]
    width = GROUP_HEADS * DH
    out_ref[:, 0:width] = query_ref[...]
    out_ref[:, width : width + DH] = key_ref[...]
    out_ref[:, width + DH :] = value_ref[...]


def their_columns(place, w_query, w_key, w_value, gain_attn, gain_ffn, w_out, shares):
    rows = w_query.shape[0]
    width = GROUP_HEADS * DH + 2 * DH

    def theirs(width):
        return pl.BlockSpec((rows, width), lambda i, c: (0, 1 - c[0]))

    return pl.pallas_call(
        columns_kernel,
        grid_spec=pltpu.PrefetchScalarGridSpec(
            num_scalar_prefetch=1,
            grid=(1,),
            in_specs=[theirs(GROUP_HEADS * DH), theirs(DH), theirs(DH)]
            + [pl.BlockSpec(gain_attn.shape, lambda i, c: (0, 0))] * 2
            + [pl.BlockSpec((rows // shares, rows), lambda i, c: (c[1], 0))],
            out_specs=[
                pl.BlockSpec((rows, width), lambda i, c: (0, 0)),
                pl.BlockSpec((2, rows), lambda i, c: (0, 0)),
                pl.BlockSpec((rows // shares, rows), lambda i, c: (0, 0)),
            ],
        ),
        out_shape=[
            jax.ShapeDtypeStruct((rows, width), BF16),
            jax.ShapeDtypeStruct((2, rows), F32),
            jax.ShapeDtypeStruct((rows // shares, rows), BF16),
        ],
        compiler_params=params(60, "arbitrary"),
        cost_estimate=SMALL,
        name="their_columns",
    )(place, w_query, w_key, w_value, gain_attn, gain_ffn, w_out)


def join_kernel(mine_ref, *refs):
    *parts, out_ref = refs
    rows = parts[0].shape[0]
    for k, part in enumerate(parts):
        at = jnp.bitwise_xor(mine_ref[0], k)
        out_ref[pl.ds(pl.multiple_of(at * rows, rows), rows), :] = part[...]


def join(mine, *parts):
    rows, width = parts[0].shape
    spec = pl.BlockSpec(memory_space=pltpu.VMEM)
    return pl.pallas_call(
        join_kernel,
        out_shape=jax.ShapeDtypeStruct((len(parts) * rows, width), parts[0].dtype),
        in_specs=[pl.BlockSpec(memory_space=pltpu.SMEM)] + [spec] * len(parts),
        out_specs=spec,
        compiler_params=params(16),
        cost_estimate=SMALL,
        name="join",
    )(mine.reshape(1), *parts)


def project_kernel(col_ref, own_ref, other_ref, gains_ref, gains_c_ref, query_ref, key_ref, value_ref, there_ref, x_own_ref, x_other_ref, qkv_ref, scale_ref):
    own = own_ref[...].astype(F32)
    other = other_ref[...].astype(F32)
    total = jnp.sum(own * own, axis=1, keepdims=True)
    total = total + jnp.sum(other * other, axis=1, keepdims=True)
    scale = lax.rsqrt(total / D + EPSILON)
    own = (own * scale * gains_ref[0:1, :]).astype(BF16)
    other = (other * scale * gains_c_ref[0:1, :]).astype(BF16)
    x_own_ref[...] = own
    x_other_ref[...] = other
    scale_ref[...] = scale
    here = jnp.concatenate([query_ref[...], key_ref[...], value_ref[...]], axis=1)
    qkv_ref[...] = (dot(own, here) + dot(other, there_ref[...])).astype(BF16)


def project(col, own, other, gains, gains_c, w_query, w_key, w_value, there):
    rows, features = own.shape
    width = there.shape[1]
    group = GROUP_HEADS * DH
    tile = rows // 2

    def whole(*shape):
        return pl.BlockSpec(shape, lambda i, c: (0,) * len(shape))

    def mine(width):
        return pl.BlockSpec((features, width), lambda i, c: (0, c[0]))

    def rowwise(width):
        return pl.BlockSpec((tile, width), lambda i, c: (i, 0))

    return pl.pallas_call(
        project_kernel,
        grid_spec=pltpu.PrefetchScalarGridSpec(
            num_scalar_prefetch=1,
            grid=(rows // tile,),
            in_specs=[
                rowwise(features),
                rowwise(features),
                whole(2, features),
                whole(2, features),
                mine(group),
                mine(DH),
                mine(DH),
                whole(features, width),
            ],
            out_specs=[rowwise(features), rowwise(features), rowwise(width), rowwise(1)],
        ),
        out_shape=[
            jax.ShapeDtypeStruct((rows, features), BF16),
            jax.ShapeDtypeStruct((rows, features), BF16),
            jax.ShapeDtypeStruct((rows, width), BF16),
            jax.ShapeDtypeStruct((rows, 1), F32),
        ],
        compiler_params=params(60, "arbitrary"),
        cost_estimate=SMALL,
        name="project",
    )(col, own, other, gains, gains_c, w_query, w_key, w_value, there)


def head_pair(col_ref, own, other):
    first, second = own[...], other[...]
    flipped = col_ref != 0
    return jnp.concatenate(
        [jnp.where(flipped, second, first), jnp.where(flipped, first, second)], axis=1
    )


def before_kernel(tiles, place_ref, *refs):
    near, near_c, far, far_c, attended, attended_c, here, there, own_ref, other_ref = refs
    is_near = (pl.program_id(0) >= tiles // 2).astype(jnp.int32) == place_ref[0]
    heads = head_pair(place_ref[2], attended, attended_c)
    own = jnp.where(is_near, near[...], far[...]).astype(F32)
    other = jnp.where(is_near, near_c[...], far_c[...]).astype(F32)
    own_ref[...] = own + dot(heads, here[...])
    other_ref[...] = other + dot(heads, there[...])


def after_kernel(place_ref, *refs):
    own_ref, other_ref, attended, attended_c, here, there, gains_ref, gains_c_ref = refs[0:8]
    hidden_ref, x_own_ref, x_other_ref, scale_ref = refs[8:12]
    heads = head_pair(place_ref[2], attended, attended_c)
    own = own_ref[...] + dot(heads, here[...])
    other = other_ref[...] + dot(heads, there[...])
    total = jnp.sum(own * own, axis=1, keepdims=True)
    total = total + jnp.sum(other * other, axis=1, keepdims=True)
    scale = lax.rsqrt(total / D + EPSILON)
    hidden_ref[...] = own
    scale_ref[...] = scale
    x_own_ref[...] = (own * scale * gains_ref[1:2, :]).astype(BF16)
    x_other_ref[...] = (other * scale * gains_c_ref[1:2, :]).astype(BF16)


TOKEN_TILE = 256


def rowwise(width):
    return pl.BlockSpec((TOKEN_TILE, width), lambda i, p: (i, 0))


def whole(*shape):
    return pl.BlockSpec(shape, lambda i, p: (0,) * len(shape))


def hidden_before(place, tokens, attended, here, there):
    half, features = tokens[0].shape
    rows, heads = attended[0].shape
    tiles = rows // TOKEN_TILE
    per_half = half // TOKEN_TILE
    halfwise = pl.BlockSpec((TOKEN_TILE, features), lambda i, p: (i % per_half, 0))
    return pl.pallas_call(
        functools.partial(before_kernel, tiles),
        grid_spec=pltpu.PrefetchScalarGridSpec(
            num_scalar_prefetch=1,
            grid=(tiles,),
            in_specs=[halfwise] * 4 + [rowwise(heads)] * 2 + [whole(2 * heads, features)] * 2,
            out_specs=[rowwise(features)] * 2,
        ),
        out_shape=[jax.ShapeDtypeStruct((rows, features), F32)] * 2,
        compiler_params=params(56, "arbitrary"),
        cost_estimate=pl.CostEstimate(
            flops=8 * rows * features * heads,
            bytes_accessed=16 * rows * features,
            transcendentals=0,
        ),
        name="hidden_before",
    )(place, *tokens, *attended, here, there)


def hidden_after(place, before, attended, here, there, gains, gains_c):
    rows, features = before[0].shape
    heads = attended[0].shape[1]
    return pl.pallas_call(
        after_kernel,
        grid_spec=pltpu.PrefetchScalarGridSpec(
            num_scalar_prefetch=1,
            grid=(rows // TOKEN_TILE,),
            in_specs=[rowwise(features)] * 2
            + [rowwise(heads)] * 2
            + [whole(2 * heads, features)] * 2
            + [whole(2, features)] * 2,
            out_specs=[rowwise(features)] * 3 + [rowwise(1)],
        ),
        out_shape=[
            jax.ShapeDtypeStruct((rows, features), F32),
            jax.ShapeDtypeStruct((rows, features), BF16),
            jax.ShapeDtypeStruct((rows, features), BF16),
            jax.ShapeDtypeStruct((rows, 1), F32),
        ],
        compiler_params=params(56, "arbitrary"),
        cost_estimate=SMALL,
        name="hidden_after",
    )(place, *before, *attended, here, there, gains, gains_c)


def expert_kernel(shared, aliased, first, order_ref, *refs):
    x_own, x_other, o_own, o_other, gates_ref = refs[0:5]
    weights = refs[5:17]
    grads = refs[17 + aliased : 19 + aliased]
    pair_ref, inner_ref = refs[19 + aliased : 21 + aliased]
    step = pl.program_id(0) + first
    rows, features = x_own.shape
    tile = 512
    up_own = jnp.concatenate([weights[k][0] for k in (0, 1, 6, 7)], axis=1)
    up_other = jnp.concatenate([weights[k][0] for k in (2, 3, 8, 9)], axis=1)
    down_own = jnp.concatenate([weights[k][0] for k in (4, 10)], axis=0)
    down_other = jnp.concatenate([weights[k][0] for k in (5, 11)], axis=0)

    def token_tile(t, carry):
        at = pl.ds(pl.multiple_of(t * tile, tile), tile)
        pre = dot(x_own[at, :], up_own) + dot(x_other[at, :], up_other)
        back = dot_nt(o_own[at, :], down_own) + dot_nt(o_other[at, :], down_other)
        for k in range(2):
            pre_gate = pre[:, 2 * k * LANES : (2 * k + 1) * LANES]
            pre_up = pre[:, (2 * k + 1) * LANES : (2 * k + 2) * LANES]
            inner_grad = back[:, k * LANES : (k + 1) * LANES]
            sigmoid = 1.0 / (1.0 + jnp.exp(-pre_gate))
            silu = pre_gate * sigmoid
            inner = silu * pre_up
            if not shared:
                shape = (gates_ref.shape[0], LANES)
                expert = lax.broadcasted_iota(jnp.int32, shape, 0) % (gates_ref.shape[0] // 3)
                chosen = (expert == order_ref[2 * step + k]).astype(F32).astype(BF16)
                gate = dot_tn(gates_ref[:, at], chosen)
                inner = gate * inner
                inner_grad = gate * inner_grad
            gate_grad = inner_grad * pre_up * (sigmoid * (1.0 + pre_gate * (1.0 - sigmoid)))
            inner_ref[0, at, k * LANES : (k + 1) * LANES] = inner.astype(BF16)
            pair_ref[0, at, 2 * k * LANES : (2 * k + 1) * LANES] = gate_grad.astype(BF16)
            pair_ref[0, at, (2 * k + 1) * LANES : (2 * k + 2) * LANES] = (
                inner_grad * silu
            ).astype(BF16)
        return carry

    lax.fori_loop(0, rows // tile, token_tile, 0)
    pairs = pair_ref[0]
    for h, x in enumerate((x_own, x_other)):
        wide = dot_tn(x[...], pairs).astype(BF16)
        for k in range(2):
            grads[k][0, h * features : (h + 1) * features, 0 : 2 * LANES] = wide[
                :, 2 * k * LANES : (2 * k + 2) * LANES
            ]
    inner = inner_ref[0]
    tile = 256
    for h, o in enumerate((o_own, o_other)):
        for j in range(features // tile):
            low = dot_tn(inner, o[:, j * tile : (j + 1) * tile]).astype(BF16)
            for k in range(2):
                for b in range(tile // LANES):
                    at = h * features + j * tile + b * LANES
                    grads[k][0, at : at + LANES, 2 * LANES :] = low[
                        k * LANES : (k + 1) * LANES, b * LANES : (b + 1) * LANES
                    ]


def expert_specs(features, place, wide, low):
    specs = []
    if wide:
        block = pl.BlockSpec((1, features, LANES), lambda i, o: (place(i, o)[0], 0, place(i, o)[1]))
        specs += [block] * 4
    if low:
        block = pl.BlockSpec((1, LANES, features), lambda i, o: (*place(i, o), 0))
        specs += [block] * 2
    return specs


def expert_grads(order, first, last, total, x, o, gates, weights, kept):
    shared = total is None
    steps = last - first
    rows, features = x[0].shape
    aliased = len(kept)

    def fixed(*shape):
        return pl.BlockSpec(shape, lambda i, o: (0,) * len(shape))

    def stepped(*shape):
        return pl.BlockSpec((1, *shape), lambda i, o: (i, 0, 0))

    def placed(*shape):
        return pl.BlockSpec((1, *shape), lambda i, o: (i + first, 0, 0))

    specs = []
    for k in range(2):
        if shared:

            def picked(i, o, k=k):
                return 0, 2 * o[o.shape[0] - 1] + k

        else:

            def picked(i, o, k=k):
                return o[2 * (i + first) + k], o[o.shape[0] - 1]

        specs += expert_specs(features, picked, True, True)
    total = steps if shared else total
    return pl.pallas_call(
        functools.partial(expert_kernel, shared, aliased, first),
        grid_spec=pltpu.PrefetchScalarGridSpec(
            num_scalar_prefetch=1,
            grid=(steps,),
            in_specs=[fixed(rows, features)] * 4
            + [fixed(*gates.shape)]
            + specs
            + [pl.BlockSpec(memory_space=pl.ANY)] * aliased,
            out_specs=[stepped(2 * features, 3 * LANES)] * 2
            + [placed(rows, 4 * LANES), placed(rows, 2 * LANES)],
        ),
        out_shape=[jax.ShapeDtypeStruct((steps, 2 * features, 3 * LANES), BF16)] * 2
        + [
            jax.ShapeDtypeStruct((total, rows, 4 * LANES), BF16),
            jax.ShapeDtypeStruct((total, rows, 2 * LANES), BF16),
        ],
        input_output_aliases={18 + k: 2 + k for k in range(aliased)},
        compiler_params=params(40, "arbitrary"),
        cost_estimate=SMALL,
        name="expert_grads",
    )(order, *x, *o, gates, *weights, *weights, *kept)


def mix_kernel(back, group, order_ref, *refs):
    acts_ref, shared_ref = refs[0:2]
    each = 2 if back else 1
    count = 2 * group * each
    weights = refs[2 : 2 + count]
    shared = refs[2 + count : 2 + count + 2 * each]
    out_ref, total_ref = refs[2 + count + 2 * each :]
    step = pl.program_id(0)
    rows = out_ref.shape[0]
    tile = 512
    times = dot_nt if back else dot
    along = 1 if back else 0

    @pl.when(step == 0)
    def _():
        both = jnp.concatenate([w[0] for w in shared], axis=along)
        for t in range(rows // tile):
            at = slice(t * tile, (t + 1) * tile)
            total_ref[at, :] = times(shared_ref[0, at, :], both)

    both = jnp.concatenate([w[0] for w in weights], axis=along)
    for t in range(rows // tile):
        at = slice(t * tile, (t + 1) * tile)
        acts = jnp.concatenate([acts_ref[g, at, :] for g in range(group)], axis=1)
        total_ref[at, :] += times(acts, both)

    @pl.when(step == pl.num_programs(0) - 1)
    def _():
        out_ref[...] = total_ref[...].astype(out_ref.dtype)


def mix(back, dtype, order, acts, shared_acts, weights, shared_weights):
    pairs, rows, width = acts.shape
    features = weights[0].shape[1] if back else weights[0].shape[2]
    group = 4 if pairs % 4 == 0 else 1

    def spec(place):
        if back:
            return pl.BlockSpec((1, features, LANES), lambda i, o: (place(i, o)[0], 0, place(i, o)[1]))
        return pl.BlockSpec((1, LANES, features), lambda i, o: (*place(i, o), 0))

    def routed(k):
        return spec(lambda i, o: (o[2 * group * i + k], o[o.shape[0] - 1]))

    def common(k):
        return spec(lambda i, o: (0, 2 * o[o.shape[0] - 1] + k))

    return pl.pallas_call(
        functools.partial(mix_kernel, back, group),
        grid_spec=pltpu.PrefetchScalarGridSpec(
            num_scalar_prefetch=1,
            grid=(pairs // group,),
            in_specs=[
                pl.BlockSpec((group, rows, width), lambda i, o: (i, 0, 0)),
                pl.BlockSpec((1, rows, width), lambda i, o: (0, 0, 0)),
            ]
            + [routed(k) for k in range(2 * group) for _ in weights]
            + [common(k) for k in range(2) for _ in weights],
            out_specs=pl.BlockSpec((rows, features), lambda i, o: (0, 0)),
            scratch_shapes=[pltpu.VMEM((rows, features), F32)],
        ),
        out_shape=jax.ShapeDtypeStruct((rows, features), dtype),
        compiler_params=params(48, "arbitrary"),
        cost_estimate=SMALL,
        name="mix",
    )(order, acts, shared_acts, *weights * (2 * group), *shared_weights * 2)


def ring_of(size):
    return list(range(0, size, 2)) + list(range(1, size, 2))[::-1]


def unpack_kernel(aliased, plan_ref, *refs):
    chunks = refs[0:2]
    gate_ref, up_ref, down_ref = refs[2 + aliased : 5 + aliased]
    blocks = chunks[0].shape[1] // LANES

    def write(chunk_ref):
        gate_ref[0] = chunk_ref[0, :, 0:LANES].astype(F32)
        up_ref[0] = chunk_ref[0, :, LANES : 2 * LANES].astype(F32)
        for b in range(blocks):
            at = slice(b * LANES, (b + 1) * LANES)
            down_ref[0, :, at] = chunk_ref[0, at, 2 * LANES :].astype(F32)

    for k in range(2):
        pl.when(pl.program_id(1) == k)(lambda k=k: write(chunks[k]))


def unpack(plan, first, wave, chunks, shapes, outs):
    count, rows, width = chunks[0].shape
    chunk = pl.BlockSpec((1, rows, width), lambda i, d, n: (i, 0, 0))

    def place(i, d, n):
        block = n[n.shape[0] - 1]
        return n[first + 2 * i + d], 1 - block if wave else block

    def wide(i, d, n):
        expert, block = place(i, d, n)
        return (expert, 0, block)

    def low(i, d, n):
        expert, block = place(i, d, n)
        return (expert, block, 0)

    aliased = len(outs)
    return pl.pallas_call(
        functools.partial(unpack_kernel, aliased),
        grid_spec=pltpu.PrefetchScalarGridSpec(
            num_scalar_prefetch=1,
            grid=(count, 2),
            in_specs=[chunk, chunk] + [pl.BlockSpec(memory_space=pl.ANY)] * aliased,
            out_specs=[
                pl.BlockSpec((1, rows, LANES), wide),
                pl.BlockSpec((1, rows, LANES), wide),
                pl.BlockSpec((1, LANES, rows), low),
            ],
        ),
        out_shape=[jax.ShapeDtypeStruct(shape, F32) for shape in shapes],
        input_output_aliases={3 + k: k for k in range(aliased)},
        compiler_params=params(16, "arbitrary", "arbitrary"),
        cost_estimate=SMALL,
        name="unpack",
    )(plan, *chunks, *outs)


def unpack_late_kernel(col_ref, first_ref, second_ref, *outs):
    sgate, sup, sdown, query, key, value, out = outs
    features = first_ref.shape[1]
    flipped = col_ref[0] != 0
    for c in range(2):
        for b in range(14):
            lanes = slice(b % 7 * LANES, (b % 7 + 1) * LANES)
            first, second = first_ref[c, :, lanes], second_ref[c, :, lanes]
            if b >= 7:
                first, second = second, first
            block = jnp.where(flipped, second, first).astype(F32)
            if b < 6:
                at = slice((2 * c + b // 3) * LANES, (2 * c + b // 3 + 1) * LANES)
                if b % 3 < 2:
                    (sgate, sup)[b % 3][:, at] = block
                else:
                    for k in range(features // LANES):
                        here = slice(k * LANES, (k + 1) * LANES)
                        sdown[at, here] = block[here, :]
            elif b < 9:
                at = (GROUP_HEADS * c + b - 6) * LANES
                query[:, at : at + LANES] = block
            elif b < 11:
                (key, value)[b - 9][:, c * LANES : (c + 1) * LANES] = block
            else:
                at = (GROUP_HEADS * c + b - 11) * LANES
                out[at : at + LANES, :] = block.T


def unpack_late(col, first, second, shapes):
    spec = pl.BlockSpec(memory_space=pltpu.VMEM)
    return pl.pallas_call(
        unpack_late_kernel,
        in_specs=[pl.BlockSpec(memory_space=pltpu.SMEM), spec, spec],
        out_specs=[spec] * len(shapes),
        out_shape=[jax.ShapeDtypeStruct(shape, F32) for shape in shapes],
        compiler_params=params(48),
        name="unpack_late",
    )(col, first, second)


def plans(ring, each):
    size = len(ring)
    rows = []
    for member in range(size):
        place = ring.index(member)
        for col in range(2):
            chunks = []
            for step in range(2 * size - 1):
                for which in range(2):
                    sign = 1 if which == col else -1
                    chunks.append((place - sign * step) % size)
            experts = []
            for start in (0, size - 1):
                for step in range(start, start + size):
                    for k in range(each):
                        for which in range(2):
                            second = col if which == 0 else 1 - col
                            experts.append(2 * each * chunks[2 * step + which] + each * second + k)
            rows.append(experts + chunks + [col])
    return np.asarray(rows, np.int32)


LATE_ROUND = 1


def add_rounded(left, right):
    return (left.astype(F32) + right.astype(F32)).astype(BF16)


def body(
    tokens_in,
    norm_gain_attn,
    w_query,
    w_key,
    w_value,
    w_out,
    norm_gain_ffn,
    w_gate,
    w_up,
    w_down,
    w_shared_gate,
    w_shared_up,
    w_shared_down,
    routes,
    gate_weights,
    seq_lengths,
    out_grad,
):
    row = lax.axis_index("row")
    col = lax.axis_index("col")
    dp = lax.axis_index("dp")
    dp_size = lax.axis_size("dp")
    local_rows, local_features = tokens_in.shape
    experts = w_gate.shape[0]
    group_width = GROUP_HEADS * DH
    col_ref = col.reshape(1)

    ring_size = min(8, dp_size)
    ring = ring_of(ring_size)
    starts = range(0, dp_size, ring_size)
    rights = [
        (g + ring[k], g + ring[(k + 1) % ring_size]) for g in starts for k in range(ring_size)
    ]
    lefts = [(b, a) for a, b in rights]
    routes_of = [
        [(2 * a, 2 * b) for a, b in ways[0]] + [(2 * a + 1, 2 * b + 1) for a, b in ways[1]]
        for ways in ((rights, lefts), (lefts, rights))
    ]
    experts_each = experts // (2 * ring_size)
    plan = jnp.asarray(plans(ring, experts_each))
    plan = lax.dynamic_slice(
        plan, (2 * (dp % ring_size) + col, jnp.int32(0)), (1, plan.shape[1])
    ).reshape(-1)

    def send(values, which):
        if ring_size == 1:
            return values
        return lax.ppermute(values, ("dp", "col"), routes_of[which])

    def chunk_at(step, which):
        return plan[2 * experts + 2 * step + which]

    def across_rings(values):
        if len(starts) == 1:
            return values
        peers = [[g + k for g in starts] for k in range(ring_size)]
        return lax.psum(values, "dp", axis_index_groups=peers)

    where = jnp.stack([row, seq_lengths[0], col])
    tokens_y = swap(tokens_in, "row")
    tokens_c = swap(tokens_in, "col")
    count = min(ring_size, 4)
    member = dp % count
    there, gains, out_y = their_columns(
        jnp.stack([col, member]),
        w_query,
        w_key,
        w_value,
        norm_gain_attn[None],
        norm_gain_ffn[None],
        w_out,
        count,
    )
    there = swap(there, "col")
    gains_c = swap(gains, "col")

    def project_half(own, other):
        return project(col_ref, own, other, gains, gains_c, w_query, w_key, w_value, there)

    near = project_half(tokens_in, tokens_c)
    gate_c = swap(w_gate, "col")
    out_y = swap(out_y, "row")
    tokens_y = after(tokens_y, near[2], out_y)
    tokens_yc = swap(tokens_y, "col")
    grad_cut = local_rows // 8 * 5
    grad_y = swap(after(out_grad[:grad_cut], tokens_y), "row")
    far = project_half(tokens_y, tokens_yc)

    shares = [out_y]
    for k in range(1, count):
        shares.append(lax.ppermute(out_y, "dp", [(m, m ^ k) for m in range(dp_size)]))
    where = after(where, grad_y, *shares)

    w_sgate, w_sup, w_sdown = w_shared_gate[None], w_shared_up[None], w_shared_down[None]
    up_c = swap(after(w_up, gate_c, tokens_yc), "col")

    attended = attend(where, near[2], far[2])
    attended_y = swap(attended, "row")
    attended_c = swap(attended, "col")
    out_c = swap(after(w_out, tokens_yc), "col")
    before = hidden_before(
        where,
        [tokens_in, tokens_c, tokens_y, tokens_yc],
        [attended, attended_c],
        w_out,
        out_c,
    )
    down_c = swap(after(w_down, tokens_yc), "col")
    rest_y = swap(after(out_grad[grad_cut:], attended_c), "row")
    attended_y = after(attended_y, before[0])
    out_y = join(member, *shares)
    out_yc = swap(out_y, "col")
    attended_yc = swap(attended_y, "col")
    grad_own = join(row, out_grad, jnp.concatenate([grad_y, rest_y], axis=0))
    grad_other = swap(grad_own, "col")
    hidden, x_own, x_other, scale_ffn = hidden_after(
        where, before, [attended_y, attended_yc], out_y, out_yc, gains, gains_c
    )
    sgate_c, sup_c, sdown_c = (
        swap(after(w, attended_yc), "col") for w in (w_sgate, w_sup, w_sdown)
    )

    choices = jnp.arange(experts, dtype=jnp.int32)[:, None]
    dense = sum(
        jnp.where(routes[:, k][None, :] == choices, gate_weights[:, k][None, :], 0.0)
        for k in range(routes.shape[1])
    )
    gates = []
    for _ in range(3):
        gates.append(lax.reduce_precision(dense, 8, 7))
        dense = dense - gates[-1]
    gates = jnp.concatenate(gates, axis=0).astype(BF16)

    each = experts_each
    order = plan
    pairs_total = experts // 2
    routed = [w_gate, w_up, gate_c, up_c, w_down, down_c]
    shared = [w_sgate, w_sup, sgate_c, sup_c, w_sdown, sdown_c]

    def run(first, last, order, kept):
        return expert_grads(
            order,
            first,
            last,
            pairs_total,
            [x_own, x_other],
            [grad_own, grad_other],
            gates,
            routed,
            kept,
        )

    first = run(0, each, order, ())
    kept = first[2:]
    sums = [first[0], first[1]]
    runs = {}
    mixed = {}

    def work_experts(first, last):
        def work(order):
            nonlocal kept
            result = run(first, last, order, tuple(kept))
            kept = result[2:]
            for at in range(first, last):
                runs[at] = (result[0], result[1], at - first)
            return kept[0]

        return work

    def work_shared(order):
        runs["shared"] = expert_grads(
            order, 0, 1, None, [x_own, x_other], [grad_own, grad_other], gates, shared, ()
        )
        return runs["shared"][2]

    def work_mix(back, half):
        def work(order):
            pick = slice(2 * half, 2 * half + 2) if back else slice(4 + half, 5 + half)
            mixed[back, half] = mix(
                back,
                BF16 if half else F32,
                order,
                kept[0 if back else 1],
                runs["shared"][2 if back else 3],
                routed[pick],
                shared[pick],
            )
            return mixed[back, half]

        return work

    start = row * local_rows

    def my_rows(values):
        return lax.dynamic_slice_in_dim(values, start, local_rows, axis=0)

    def their_rows(values):
        return lax.dynamic_slice_in_dim(values, local_rows - start, local_rows, axis=0)

    normed = {}

    def work_hidden(order):
        normed_grad = mixed[True, 0] + swap(mixed[True, 1], "col").astype(F32)
        came = swap(normed_grad.astype(BF16), "row")
        normed_grad = normed_grad + after(came, order).astype(F32)
        scaled = normed_grad * norm_gain_ffn
        products = jnp.sum(scaled * hidden, axis=1, keepdims=True)
        mean = (products + swap(products, "col")) / D
        normed["gain"] = jnp.sum(my_rows(normed_grad * hidden * scale_ffn), axis=0)
        normed["hidden"] = (
            grad_own.astype(F32) + scale_ffn * scaled - hidden * scale_ffn**3 * mean
        )
        normed["grad"] = normed["hidden"].astype(BF16)
        normed["grad_c"] = swap(normed["grad"], "col")
        return normed["grad"]

    def work_attend(order):
        normed["qkv"] = attend_back(
            after(where, order), near[2], far[2], normed["grad"], normed["grad_c"], w_out, out_c
        )
        return normed["qkv"]

    tasks = [work_experts(at, at + each) for at in range(each, pairs_total, each)]
    tasks += [work_shared, work_mix(True, 1), work_mix(True, 0), work_mix(False, 1), work_mix(False, 0)]
    tasks += [None] * (2 * ring_size - 3 - len(tasks)) + [work_hidden, work_attend]
    got = [None, None]
    if ring_size > 1:
        got[0] = send(sums[0], 0)
        tasks.pop(0)(after(order, *sums))
        got[1] = send(after(sums[1], kept[0]), 1)
    for s in range(1, ring_size):
        for k in range(2):
            last = sums
            task = tasks.pop(0) if tasks else None
            if task:
                last = [task(after(order, *last))]
            got[k] = after(got[k], *last)
            parts = [runs[at] for at in range(each * s, each * s + each)]
            mine = [p[k][p[2] : p[2] + 1] for p in parts]
            mine = mine[0] if each == 1 else jnp.concatenate(mine, axis=0)
            sums[k] = add_rounded(got[k], mine)
            if s + 1 < ring_size:
                got[k] = send(sums[k], k)
    for task in tasks:
        if task:
            task(after(order, *sums))
    sums = [across_rings(total) for total in sums]
    waves = [[total[:, :local_features] for total in sums]]
    crossed = [swap(total[:, local_features:], "col") for total in sums]
    waves.append([crossed[1], crossed[0]])

    hidden_grad, attn_grad, attn_grad_c = normed["hidden"], normed["grad"], normed["grad_c"]
    gain_ffn_part, qkv_grad = normed["gain"], normed["qkv"]
    packs = late_grads(
        where,
        near[0:2],
        far[0:2],
        qkv_grad,
        attended,
        attn_grad,
        attn_grad_c,
        runs["shared"][0:2],
    )

    packs = [
        pack.reshape(2, ring_size, local_features // ring_size, pack.shape[2]) for pack in packs
    ]

    def late_chunk(step, which):
        at = chunk_at(step, which)
        return lax.dynamic_index_in_dim(packs[which], at, axis=1, keepdims=False)

    def late_place(current, step, which):
        at = chunk_at(ring_size - 1 + step, which)
        return lax.dynamic_update_index_in_dim(late_out[which], current, at, 1)

    late_out = [jnp.zeros(pack.shape, BF16) for pack in packs]
    late = [late_chunk(0, k) for k in range(2)]
    late_done = 0
    late_total = 2 * (ring_size - 1)

    def late_turn():
        totals = [across_rings(values) for values in late]
        others = [swap(values[1], "col") for values in totals]
        for k in range(2):
            late[k] = in_order(totals[k][0:1], others[1 - k][None], col, 0)
            late_out[k] = late_place(late[k], 0, k)

    def late_finish(k, values):
        if late_done < ring_size:
            late[k] = add_rounded(values, late_chunk(late_done, k))
        else:
            late[k] = values
            late_out[k] = late_place(values, late_done - ring_size + 1, k)

    shapes = [w_gate.shape, w_up.shape, w_down.shape]
    placed = ()

    def place_chunks(wave, step, chunks, placed):
        return unpack(plan, experts + 2 * each * step, wave, chunks, shapes, placed)

    if late_total == 0:
        late_turn()
    rounds = [(wave, step) for wave in range(2) for step in range(ring_size - 1)]
    late_got = None
    last = list(sums)
    for number, (wave, step) in enumerate(rounds):
        if step == 0:
            came = list(got) if number else None
            got = list(waves[wave])
        late_done += late_got is not None
        chunks = [None, None]
        for k in range(2):
            chunks[k] = after(got[k], *last)
            got[k] = send(chunks[k], k)
            last = [chunks[k]]
            if late_got is not None:
                late_finish(k, after(late_got[k], *last))
                last = [late[k]]
        if late_got is not None and late_done == ring_size - 1:
            late_turn()
        if number >= LATE_ROUND and late_done < late_total:
            late_got = [send(after(late[k], *chunks), k) for k in range(2)]
        else:
            late_got = None
        if step == 0 and number:
            placed = place_chunks(0, ring_size - 1, came, placed)
        placed = place_chunks(wave, step, chunks, placed)
        last = placed[0:1]
        if number == LATE_ROUND + 3:
            qkv_grad = after(qkv_grad, *last)
    if rounds:
        placed = place_chunks(1, ring_size - 1, [after(got[k], *last) for k in range(2)], placed)
        last = placed[0:1]
    while late_got is not None:
        late_done += 1
        for k in range(2):
            late_finish(k, after(late_got[k], *last))
        if late_done == ring_size - 1:
            late_turn()
        late_got = [send(late[k], k) for k in range(2)] if late_done < late_total else None
    if not rounds:
        for wave in range(2):
            placed = place_chunks(wave, 0, waves[wave], placed)
    gate_grad, up_grad, down_grad = placed
    shapes = [w.shape for w in (w_shared_gate, w_shared_up, w_shared_down)]
    shapes += [w.shape for w in (w_query, w_key, w_value, w_out)]
    finals = unpack_late(
        col_ref, *[out.reshape(2, local_features, out.shape[3]) for out in late_out], shapes
    )
    shared_gate_grad, shared_up_grad, shared_down_grad = finals[0:3]
    query_grad, key_grad, value_grad, out_proj_grad = finals[3:7]

    ffn_sum = mixed[False, 0] + swap(mixed[False, 1], "col").astype(F32)
    ffn_rows = my_rows(ffn_sum) + swap(their_rows(ffn_sum).astype(BF16), "row").astype(F32)
    block_out = (my_rows(hidden) + ffn_rows).astype(BF16)

    here = jnp.concatenate(
        [halves(w, 1, col)[0] for w in (w_query, w_key, w_value)], axis=1
    )
    tokens_back = dot_nt(qkv_grad, here) + swap(
        dot_nt(qkv_grad, there).astype(BF16), "col"
    ).astype(F32)
    tokens_back = my_rows(tokens_back) + swap(
        their_rows(tokens_back).astype(BF16), "row"
    ).astype(F32)
    scale_attn = near[3]
    tokens_f32 = tokens_in.astype(F32)
    gain_attn_part = jnp.sum(tokens_back * tokens_f32 * scale_attn, axis=0)
    scaled = tokens_back * norm_gain_attn
    products = jnp.sum(scaled * tokens_f32, axis=1, keepdims=True)
    mean = (products + swap(products, "col")) / D
    tokens_grad = (
        my_rows(hidden_grad) + scale_attn * scaled - tokens_f32 * scale_attn**3 * mean
    ).astype(BF16)

    gain_parts = jnp.stack([gain_attn_part, gain_ffn_part])
    bit = 1
    while bit < ring_size:
        pairs = [(g + k, g + (k ^ bit)) for g in starts for k in range(ring_size)]
        gain_parts = gain_parts + lax.ppermute(gain_parts, "dp", pairs)
        bit *= 2
    gain_parts = across_rings(gain_parts + swap(gain_parts, "row"))

    return (
        block_out,
        tokens_grad,
        gain_parts[0],
        query_grad,
        key_grad,
        value_grad,
        out_proj_grad,
        gain_parts[1],
        gate_grad,
        up_grad,
        down_grad,
        shared_gate_grad,
        shared_up_grad,
        shared_down_grad,
    )


def solution(mesh):
    in_specs = (
        P(("dp", "row"), "col"),
        P("col"),
        P("col", "row"),
        P("col", "row"),
        P("col", "row"),
        P("row", "col"),
        P("col"),
        P(None, "col", "row"),
        P(None, "col", "row"),
        P(None, "row", "col"),
        P("col", "row"),
        P("col", "row"),
        P("row", "col"),
        P("dp", None),
        P("dp", None),
        P("dp"),
        P(("dp", "row"), "col"),
    )
    out_specs = (
        P(("dp", "row"), "col"),
        P(("dp", "row"), "col"),
        P("col"),
        P("col", "row"),
        P("col", "row"),
        P("col", "row"),
        P("row", "col"),
        P("col"),
        P(None, "col", "row"),
        P(None, "col", "row"),
        P(None, "row", "col"),
        P("col", "row"),
        P("col", "row"),
        P("row", "col"),
    )
    return jax.shard_map(body, mesh=mesh, in_specs=in_specs, out_specs=out_specs, check_vma=False)
```

```python
import functools

import jax
import jax.numpy as jnp
import numpy as np
from jax import lax
from jax.experimental import pallas as pl
from jax.experimental.pallas import tpu as pltpu
from jax.sharding import PartitionSpec as P

D = 1536
HQ = 12
HK = 4
DH = 128
GROUP_HEADS = HQ // HK
LANES = 128

EPSILON = 1e-05
F32 = jnp.float32
BF16 = jnp.bfloat16
MIB = 1024 * 1024
SMALL = pl.CostEstimate(flops=0, bytes_accessed=0, transcendentals=0)


def params(mib, *semantics):
    return pltpu.CompilerParams(
        dimension_semantics=semantics or None, vmem_limit_bytes=mib * MIB
    )


def dot(left, right):
    return jnp.dot(left, right, preferred_element_type=F32)


def dot_nt(left, right):
    return lax.dot_general(left, right, (((1,), (1,)), ((), ())), preferred_element_type=F32)


def dot_tn(left, right):
    return lax.dot_general(left, right, (((0,), (0,)), ((), ())), preferred_element_type=F32)


def after(values, *others):
    return lax.optimization_barrier((values, *others))[0]


def swap(values, axis):
    return lax.ppermute(values, axis, [(0, 1), (1, 0)])


def halves(values, axis, mine):
    size = values.shape[axis] // 2
    low = lax.slice_in_dim(values, 0, size, axis=axis)
    high = lax.slice_in_dim(values, size, 2 * size, axis=axis)
    return jnp.where(mine == 0, low, high), jnp.where(mine == 0, high, low)


def in_order(own, other, mine, axis):
    return jnp.concatenate(
        [jnp.where(mine == 0, own, other), jnp.where(mine == 0, other, own)], axis=axis
    )


def gather_rows(place_ref, own_ref, other_ref, all_ref):
    row = place_ref[0]
    rows = own_ref.shape[0]
    all_ref[pl.ds(pl.multiple_of(row * rows, rows), rows), :] = own_ref[...]
    all_ref[pl.ds(pl.multiple_of((1 - row) * rows, rows), rows), :] = other_ref[...]


def head_rows(ref, first, block):
    return jnp.concatenate(
        [ref[first : first + block, h * DH : (h + 1) * DH] for h in range(GROUP_HEADS)], axis=0
    )


def key_probs(query, key, first, length):
    block, keys = query.shape[0] // GROUP_HEADS, key.shape[0]
    scores = dot_nt(query, key) * DH ** (-0.5)
    shape = (block, keys)
    query_at = lax.broadcasted_iota(jnp.int32, shape, 0) + first
    key_at = lax.broadcasted_iota(jnp.int32, shape, 1)
    allowed = (key_at <= query_at) & (key_at < length)
    allowed = jnp.concatenate([allowed] * GROUP_HEADS, axis=0)
    scores = jnp.where(allowed, scores, -1e30)
    weights = jnp.exp(scores - jnp.max(scores, axis=1, keepdims=True))
    return weights * (1.0 / jnp.sum(weights, axis=1, keepdims=True))


def attend_kernel(place_ref, own_ref, other_ref, out_ref, all_ref):
    gather_rows(place_ref, own_ref, other_ref, all_ref)
    rows = own_ref.shape[0]
    block = 256
    width = GROUP_HEADS * DH
    for at in range(2 * rows // block):
        first, keys = at * block, (at + 1) * block
        query = head_rows(all_ref, first, block)
        key = all_ref[0:keys, width : width + DH]
        value = all_ref[0:keys, width + DH : width + 2 * DH]
        probs = key_probs(query, key, first, place_ref[1])
        result = dot(probs.astype(BF16), value).astype(BF16)
        for h in range(GROUP_HEADS):
            out_ref[first : first + block, h * DH : (h + 1) * DH] = result[
                h * block : (h + 1) * block
            ]


def attend(place, own, other):
    rows, width = own.shape
    spec = pl.BlockSpec(memory_space=pltpu.VMEM)
    return pl.pallas_call(
        attend_kernel,
        out_shape=jax.ShapeDtypeStruct((2 * rows, GROUP_HEADS * DH), BF16),
        in_specs=[pl.BlockSpec(memory_space=pltpu.SMEM), spec, spec],
        out_specs=spec,
        scratch_shapes=[pltpu.VMEM((2 * rows, width), BF16)],
        compiler_params=params(32),
        cost_estimate=SMALL,
        name="attend",
    )(place, own, other)


def attend_back_kernel(
    place_ref, own_ref, other_ref, grad_ref, grad_c_ref, out_ref, out_c_ref, result_ref, all_ref, total_ref
):
    gather_rows(place_ref, own_ref, other_ref, all_ref)
    rows = own_ref.shape[0]
    block = 256
    width = GROUP_HEADS * DH
    group = pl.ds(pl.multiple_of(place_ref[2] * width, width), width)
    blocks = 2 * rows // block
    for at in reversed(range(blocks)):
        first, keys = at * block, (at + 1) * block
        query = head_rows(all_ref, first, block)
        key = all_ref[0:keys, width : width + DH]
        value = all_ref[0:keys, width + DH : width + 2 * DH]
        probs = key_probs(query, key, first, place_ref[1])
        grad = dot_nt(grad_ref[first:keys, :], out_ref[group, :])
        grad = (grad + dot_nt(grad_c_ref[first:keys, :], out_c_ref[group, :])).astype(BF16)
        grad = jnp.concatenate(
            [grad[:, h * DH : (h + 1) * DH] for h in range(GROUP_HEADS)], axis=0
        )
        probs_grad = dot_nt(grad, value)
        carried = jnp.sum(probs * probs_grad, axis=1, keepdims=True)
        score_grad = (probs * (probs_grad - carried)).astype(BF16)
        query_back = (dot(score_grad, key) * DH ** (-0.5)).astype(BF16)
        for h in range(GROUP_HEADS):
            result_ref[first:keys, h * DH : (h + 1) * DH] = query_back[
                h * block : (h + 1) * block
            ]
        key_back = dot_tn(score_grad, query)
        value_back = dot_tn(probs.astype(BF16), grad)
        if at == blocks - 1:
            total_ref[:, 0:DH] = key_back
            total_ref[:, DH:] = value_back
        else:
            total_ref[0:keys, 0:DH] += key_back
            total_ref[0:keys, DH:] += value_back
    result_ref[:, width : width + DH] = (total_ref[:, 0:DH] * DH ** (-0.5)).astype(BF16)
    result_ref[:, width + DH :] = total_ref[:, DH:].astype(BF16)


def attend_back(place, own, other, grad, grad_c, w_out, out_c):
    rows, width = own.shape
    spec = pl.BlockSpec(memory_space=pltpu.VMEM)
    return pl.pallas_call(
        attend_back_kernel,
        out_shape=jax.ShapeDtypeStruct((2 * rows, width), BF16),
        in_specs=[pl.BlockSpec(memory_space=pltpu.SMEM)] + [spec] * 6,
        out_specs=spec,
        scratch_shapes=[
            pltpu.VMEM((2 * rows, width), BF16),
            pltpu.VMEM((2 * rows, 2 * DH), F32),
        ],
        compiler_params=params(60),
        cost_estimate=SMALL,
        name="attend_back",
    )(place, own, other, grad, grad_c, w_out, out_c)


def late_kernel(place_ref, *refs):
    near, near_c, far, far_c, qkv_ref, attended_ref, grad_ref, grad_c_ref = refs[0:8]
    shared = refs[8:10]
    outs = refs[10:12]
    rows, features = near.shape
    own_rows = pl.ds(pl.multiple_of(place_ref[0] * rows, rows), rows)
    far_rows = pl.ds(pl.multiple_of((1 - place_ref[0]) * rows, rows), rows)
    split = 7 * LANES

    def store(h, at, values):
        values = values.astype(BF16)
        for part in range(2):
            low, high = max(at, part * split), min(at + values.shape[1], (part + 1) * split)
            if low < high:
                piece = values[:, low - at : high - at]
                to = slice(low - part * split, high - part * split)

                @pl.when(place_ref[2] == 0)
                def _(part=part, to=to, piece=piece):
                    outs[part][h, :, to] = piece

                @pl.when(place_ref[2] != 0)
                def _(part=part, to=to, piece=piece):
                    outs[1 - part][h, :, to] = piece

    for h, (x, y, grad) in enumerate(((near, far, grad_ref), (near_c, far_c, grad_c_ref))):
        for k in range(2):
            store(h, 3 * LANES * k, shared[k][0, h * features : (h + 1) * features, :])
        project = dot_tn(x[...], qkv_ref[own_rows, :]) + dot_tn(y[...], qkv_ref[far_rows, :])
        store(h, 6 * LANES, project)
        store(h, 11 * LANES, dot_tn(grad[...], attended_ref[...]))


def late_grads(place, near, far, qkv_grad, attended, grad, grad_c, shared):
    features = near[0].shape[1]
    spec = pl.BlockSpec(memory_space=pltpu.VMEM)
    return pl.pallas_call(
        late_kernel,
        out_shape=[jax.ShapeDtypeStruct((2, features, 7 * LANES), BF16)] * 2,
        in_specs=[pl.BlockSpec(memory_space=pltpu.SMEM)] + [spec] * 10,
        out_specs=[spec] * 2,
        compiler_params=params(60),
        cost_estimate=SMALL,
        name="late_grads",
    )(place, *near, *far, qkv_grad, attended, grad, grad_c, *shared)


def columns_kernel(
    place_ref, query_ref, key_ref, value_ref, w_out_ref, out_ref, share_ref
):
    share_ref[...] = w_out_ref[...]
    width = GROUP_HEADS * DH
    out_ref[:, 0:width] = query_ref[...]
    out_ref[:, width : width + DH] = key_ref[...]
    out_ref[:, width + DH :] = value_ref[...]


def their_columns(place, w_query, w_key, w_value, w_out, shares):
    rows = w_query.shape[0]
    width = GROUP_HEADS * DH + 2 * DH

    def theirs(width):
        return pl.BlockSpec((rows, width), lambda i, c: (0, 1 - c[0]))

    return pl.pallas_call(
        columns_kernel,
        grid_spec=pltpu.PrefetchScalarGridSpec(
            num_scalar_prefetch=1,
            grid=(1,),
            in_specs=[theirs(GROUP_HEADS * DH), theirs(DH), theirs(DH)]
            + [pl.BlockSpec((rows // shares, rows), lambda i, c: (c[1], 0))],
            out_specs=[
                pl.BlockSpec((rows, width), lambda i, c: (0, 0)),
                pl.BlockSpec((rows // shares, rows), lambda i, c: (0, 0)),
            ],
        ),
        out_shape=[
            jax.ShapeDtypeStruct((rows, width), BF16),
            jax.ShapeDtypeStruct((rows // shares, rows), BF16),
        ],
        compiler_params=params(60, "arbitrary"),
        cost_estimate=SMALL,
        name="their_columns",
    )(place, w_query, w_key, w_value, w_out)


def join_kernel(mine_ref, *refs):
    *parts, out_ref = refs
    rows = parts[0].shape[0]
    for k, part in enumerate(parts):
        at = jnp.bitwise_xor(mine_ref[0], k)
        out_ref[pl.ds(pl.multiple_of(at * rows, rows), rows), :] = part[...]


def join(mine, *parts):
    rows, width = parts[0].shape
    spec = pl.BlockSpec(memory_space=pltpu.VMEM)
    return pl.pallas_call(
        join_kernel,
        out_shape=jax.ShapeDtypeStruct((len(parts) * rows, width), parts[0].dtype),
        in_specs=[pl.BlockSpec(memory_space=pltpu.SMEM)] + [spec] * len(parts),
        out_specs=spec,
        compiler_params=params(16),
        cost_estimate=SMALL,
        name="join",
    )(mine.reshape(1), *parts)


def project_kernel(col_ref, own_ref, other_ref, gains_ref, gains_c_ref, query_ref, key_ref, value_ref, there_ref, x_own_ref, x_other_ref, qkv_ref, scale_ref):
    own = own_ref[...].astype(F32)
    other = other_ref[...].astype(F32)
    total = jnp.sum(own * own, axis=1, keepdims=True)
    total = total + jnp.sum(other * other, axis=1, keepdims=True)
    scale = lax.rsqrt(total / D + EPSILON)
    own = (own * scale * gains_ref[0:1, :]).astype(BF16)
    other = (other * scale * gains_c_ref[0:1, :]).astype(BF16)
    x_own_ref[...] = own
    x_other_ref[...] = other
    scale_ref[...] = scale
    here = jnp.concatenate([query_ref[...], key_ref[...], value_ref[...]], axis=1)
    qkv_ref[...] = (dot(own, here) + dot(other, there_ref[...])).astype(BF16)


def project(col, own, other, gains, gains_c, w_query, w_key, w_value, there):
    rows, features = own.shape
    width = there.shape[1]
    group = GROUP_HEADS * DH
    tile = rows // 2

    def whole(*shape):
        return pl.BlockSpec(shape, lambda i, c: (0,) * len(shape))

    def mine(width):
        return pl.BlockSpec((features, width), lambda i, c: (0, c[0]))

    def rowwise(width):
        return pl.BlockSpec((tile, width), lambda i, c: (i, 0))

    return pl.pallas_call(
        project_kernel,
        grid_spec=pltpu.PrefetchScalarGridSpec(
            num_scalar_prefetch=1,
            grid=(rows // tile,),
            in_specs=[
                rowwise(features),
                rowwise(features),
                whole(2, features),
                whole(2, features),
                mine(group),
                mine(DH),
                mine(DH),
                whole(features, width),
            ],
            out_specs=[rowwise(features), rowwise(features), rowwise(width), rowwise(1)],
        ),
        out_shape=[
            jax.ShapeDtypeStruct((rows, features), BF16),
            jax.ShapeDtypeStruct((rows, features), BF16),
            jax.ShapeDtypeStruct((rows, width), BF16),
            jax.ShapeDtypeStruct((rows, 1), F32),
        ],
        compiler_params=params(60, "arbitrary"),
        cost_estimate=SMALL,
        name="project",
    )(col, own, other, gains, gains_c, w_query, w_key, w_value, there)


def head_pair(col_ref, own, other):
    first, second = own[...], other[...]
    flipped = col_ref != 0
    return jnp.concatenate(
        [jnp.where(flipped, second, first), jnp.where(flipped, first, second)], axis=1
    )


def before_kernel(tiles, place_ref, *refs):
    near, near_c, far, far_c, attended, attended_c, here, there, own_ref, other_ref = refs
    is_near = (pl.program_id(0) >= tiles // 2).astype(jnp.int32) == place_ref[0]
    heads = head_pair(place_ref[2], attended, attended_c)
    own = jnp.where(is_near, near[...], far[...]).astype(F32)
    other = jnp.where(is_near, near_c[...], far_c[...]).astype(F32)
    own_ref[...] = own + dot(heads, here[...])
    other_ref[...] = other + dot(heads, there[...])


def after_kernel(place_ref, *refs):
    own_ref, other_ref, attended, attended_c, here, there, gains_ref, gains_c_ref = refs[0:8]
    hidden_ref, x_own_ref, x_other_ref, scale_ref = refs[8:12]
    heads = head_pair(place_ref[2], attended, attended_c)
    own = own_ref[...] + dot(heads, here[...])
    other = other_ref[...] + dot(heads, there[...])
    total = jnp.sum(own * own, axis=1, keepdims=True)
    total = total + jnp.sum(other * other, axis=1, keepdims=True)
    scale = lax.rsqrt(total / D + EPSILON)
    hidden_ref[...] = own
    scale_ref[...] = scale
    x_own_ref[...] = (own * scale * gains_ref[1:2, :]).astype(BF16)
    x_other_ref[...] = (other * scale * gains_c_ref[1:2, :]).astype(BF16)


TOKEN_TILE = 256


def rowwise(width):
    return pl.BlockSpec((TOKEN_TILE, width), lambda i, p: (i, 0))


def whole(*shape):
    return pl.BlockSpec(shape, lambda i, p: (0,) * len(shape))


def hidden_before(place, tokens, attended, here, there):
    half, features = tokens[0].shape
    rows, heads = attended[0].shape
    tiles = rows // TOKEN_TILE
    per_half = half // TOKEN_TILE
    halfwise = pl.BlockSpec((TOKEN_TILE, features), lambda i, p: (i % per_half, 0))
    return pl.pallas_call(
        functools.partial(before_kernel, tiles),
        grid_spec=pltpu.PrefetchScalarGridSpec(
            num_scalar_prefetch=1,
            grid=(tiles,),
            in_specs=[halfwise] * 4 + [rowwise(heads)] * 2 + [whole(2 * heads, features)] * 2,
            out_specs=[rowwise(features)] * 2,
        ),
        out_shape=[jax.ShapeDtypeStruct((rows, features), F32)] * 2,
        compiler_params=params(56, "arbitrary"),
        cost_estimate=pl.CostEstimate(
            flops=8 * rows * features * heads,
            bytes_accessed=16 * rows * features,
            transcendentals=0,
        ),
        name="hidden_before",
    )(place, *tokens, *attended, here, there)


def hidden_after(place, before, attended, here, there, gains, gains_c):
    rows, features = before[0].shape
    heads = attended[0].shape[1]
    return pl.pallas_call(
        after_kernel,
        grid_spec=pltpu.PrefetchScalarGridSpec(
            num_scalar_prefetch=1,
            grid=(rows // TOKEN_TILE,),
            in_specs=[rowwise(features)] * 2
            + [rowwise(heads)] * 2
            + [whole(2 * heads, features)] * 2
            + [whole(2, features)] * 2,
            out_specs=[rowwise(features)] * 3 + [rowwise(1)],
        ),
        out_shape=[
            jax.ShapeDtypeStruct((rows, features), F32),
            jax.ShapeDtypeStruct((rows, features), BF16),
            jax.ShapeDtypeStruct((rows, features), BF16),
            jax.ShapeDtypeStruct((rows, 1), F32),
        ],
        compiler_params=params(56, "arbitrary"),
        cost_estimate=SMALL,
        name="hidden_after",
    )(place, *before, *attended, here, there, gains, gains_c)


def expert_kernel(shared, aliased, first, order_ref, *refs):
    x_own, x_other, o_own, o_other, gates_ref = refs[0:5]
    weights = refs[5:17]
    grads = refs[17 + aliased : 19 + aliased]
    pair_ref, inner_ref = refs[19 + aliased : 21 + aliased]
    step = pl.program_id(0) + first
    rows, features = x_own.shape
    tile = 512
    up_own = jnp.concatenate([weights[k][0] for k in (0, 1, 6, 7)], axis=1)
    up_other = jnp.concatenate([weights[k][0] for k in (2, 3, 8, 9)], axis=1)
    down_own = jnp.concatenate([weights[k][0] for k in (4, 10)], axis=0)
    down_other = jnp.concatenate([weights[k][0] for k in (5, 11)], axis=0)

    def token_tile(t, carry):
        at = pl.ds(pl.multiple_of(t * tile, tile), tile)
        pre = dot(x_own[at, :], up_own) + dot(x_other[at, :], up_other)
        back = dot_nt(o_own[at, :], down_own) + dot_nt(o_other[at, :], down_other)
        for k in range(2):
            pre_gate = pre[:, 2 * k * LANES : (2 * k + 1) * LANES]
            pre_up = pre[:, (2 * k + 1) * LANES : (2 * k + 2) * LANES]
            inner_grad = back[:, k * LANES : (k + 1) * LANES]
            sigmoid = 1.0 / (1.0 + jnp.exp(-pre_gate))
            silu = pre_gate * sigmoid
            inner = silu * pre_up
            if not shared:
                shape = (gates_ref.shape[0], LANES)
                expert = lax.broadcasted_iota(jnp.int32, shape, 0) % (gates_ref.shape[0] // 3)
                chosen = (expert == order_ref[2 * step + k]).astype(F32).astype(BF16)
                gate = dot_tn(gates_ref[:, at], chosen)
                inner = gate * inner
                inner_grad = gate * inner_grad
            gate_grad = inner_grad * pre_up * (sigmoid * (1.0 + pre_gate * (1.0 - sigmoid)))
            inner_ref[0, at, k * LANES : (k + 1) * LANES] = inner.astype(BF16)
            pair_ref[0, at, 2 * k * LANES : (2 * k + 1) * LANES] = gate_grad.astype(BF16)
            pair_ref[0, at, (2 * k + 1) * LANES : (2 * k + 2) * LANES] = (
                inner_grad * silu
            ).astype(BF16)
        return carry

    lax.fori_loop(0, rows // tile, token_tile, 0)
    pairs = pair_ref[0]
    for h, x in enumerate((x_own, x_other)):
        wide = dot_tn(x[...], pairs).astype(BF16)
        for k in range(2):
            grads[k][0, h * features : (h + 1) * features, 0 : 2 * LANES] = wide[
                :, 2 * k * LANES : (2 * k + 2) * LANES
            ]
    inner = inner_ref[0]
    tile = 256
    for h, o in enumerate((o_own, o_other)):
        for j in range(features // tile):
            low = dot_tn(inner, o[:, j * tile : (j + 1) * tile]).astype(BF16)
            for k in range(2):
                for b in range(tile // LANES):
                    at = h * features + j * tile + b * LANES
                    grads[k][0, at : at + LANES, 2 * LANES :] = low[
                        k * LANES : (k + 1) * LANES, b * LANES : (b + 1) * LANES
                    ]


def expert_specs(features, place, wide, low):
    specs = []
    if wide:
        block = pl.BlockSpec((1, features, LANES), lambda i, o: (place(i, o)[0], 0, place(i, o)[1]))
        specs += [block] * 4
    if low:
        block = pl.BlockSpec((1, LANES, features), lambda i, o: (*place(i, o), 0))
        specs += [block] * 2
    return specs


def expert_grads(order, first, last, total, x, o, gates, weights, kept):
    shared = total is None
    steps = last - first
    rows, features = x[0].shape
    aliased = len(kept)

    def fixed(*shape):
        return pl.BlockSpec(shape, lambda i, o: (0,) * len(shape))

    def stepped(*shape):
        return pl.BlockSpec((1, *shape), lambda i, o: (i, 0, 0))

    def placed(*shape):
        return pl.BlockSpec((1, *shape), lambda i, o: (i + first, 0, 0))

    specs = []
    for k in range(2):
        if shared:

            def picked(i, o, k=k):
                return 0, 2 * o[o.shape[0] - 1] + k

        else:

            def picked(i, o, k=k):
                return o[2 * (i + first) + k], o[o.shape[0] - 1]

        specs += expert_specs(features, picked, True, True)
    total = steps if shared else total
    return pl.pallas_call(
        functools.partial(expert_kernel, shared, aliased, first),
        grid_spec=pltpu.PrefetchScalarGridSpec(
            num_scalar_prefetch=1,
            grid=(steps,),
            in_specs=[fixed(rows, features)] * 4
            + [fixed(*gates.shape)]
            + specs
            + [pl.BlockSpec(memory_space=pl.ANY)] * aliased,
            out_specs=[stepped(2 * features, 3 * LANES)] * 2
            + [placed(rows, 4 * LANES), placed(rows, 2 * LANES)],
        ),
        out_shape=[jax.ShapeDtypeStruct((steps, 2 * features, 3 * LANES), BF16)] * 2
        + [
            jax.ShapeDtypeStruct((total, rows, 4 * LANES), BF16),
            jax.ShapeDtypeStruct((total, rows, 2 * LANES), BF16),
        ],
        input_output_aliases={18 + k: 2 + k for k in range(aliased)},
        compiler_params=params(40, "arbitrary"),
        cost_estimate=SMALL,
        name="expert_grads",
    )(order, *x, *o, gates, *weights, *weights, *kept)


def mix_kernel(back, group, order_ref, *refs):
    acts_ref, shared_ref = refs[0:2]
    each = 2 if back else 1
    count = 2 * group * each
    weights = refs[2 : 2 + count]
    shared = refs[2 + count : 2 + count + 2 * each]
    out_ref, total_ref = refs[2 + count + 2 * each :]
    step = pl.program_id(0)
    rows = out_ref.shape[0]
    tile = 512
    times = dot_nt if back else dot
    along = 1 if back else 0

    @pl.when(step == 0)
    def _():
        both = jnp.concatenate([w[0] for w in shared], axis=along)
        for t in range(rows // tile):
            at = slice(t * tile, (t + 1) * tile)
            total_ref[at, :] = times(shared_ref[0, at, :], both)

    both = jnp.concatenate([w[0] for w in weights], axis=along)
    for t in range(rows // tile):
        at = slice(t * tile, (t + 1) * tile)
        acts = jnp.concatenate([acts_ref[g, at, :] for g in range(group)], axis=1)
        total_ref[at, :] += times(acts, both)

    @pl.when(step == pl.num_programs(0) - 1)
    def _():
        out_ref[...] = total_ref[...].astype(out_ref.dtype)


def mix(back, dtype, order, acts, shared_acts, weights, shared_weights):
    pairs, rows, width = acts.shape
    features = weights[0].shape[1] if back else weights[0].shape[2]
    group = 4 if pairs % 4 == 0 else 1

    def spec(place):
        if back:
            return pl.BlockSpec((1, features, LANES), lambda i, o: (place(i, o)[0], 0, place(i, o)[1]))
        return pl.BlockSpec((1, LANES, features), lambda i, o: (*place(i, o), 0))

    def routed(k):
        return spec(lambda i, o: (o[2 * group * i + k], o[o.shape[0] - 1]))

    def common(k):
        return spec(lambda i, o: (0, 2 * o[o.shape[0] - 1] + k))

    return pl.pallas_call(
        functools.partial(mix_kernel, back, group),
        grid_spec=pltpu.PrefetchScalarGridSpec(
            num_scalar_prefetch=1,
            grid=(pairs // group,),
            in_specs=[
                pl.BlockSpec((group, rows, width), lambda i, o: (i, 0, 0)),
                pl.BlockSpec((1, rows, width), lambda i, o: (0, 0, 0)),
            ]
            + [routed(k) for k in range(2 * group) for _ in weights]
            + [common(k) for k in range(2) for _ in weights],
            out_specs=pl.BlockSpec((rows, features), lambda i, o: (0, 0)),
            scratch_shapes=[pltpu.VMEM((rows, features), F32)],
        ),
        out_shape=jax.ShapeDtypeStruct((rows, features), dtype),
        compiler_params=params(48, "arbitrary"),
        cost_estimate=SMALL,
        name="mix",
    )(order, acts, shared_acts, *weights * (2 * group), *shared_weights * 2)


def ring_of(size):
    return list(range(0, size, 2)) + list(range(1, size, 2))[::-1]


def unpack_kernel(aliased, plan_ref, *refs):
    chunks = refs[0:2]
    gate_ref, up_ref, down_ref = refs[2 + aliased : 5 + aliased]
    blocks = chunks[0].shape[1] // LANES

    def write(chunk_ref):
        gate_ref[0] = chunk_ref[0, :, 0:LANES].astype(F32)
        up_ref[0] = chunk_ref[0, :, LANES : 2 * LANES].astype(F32)
        for b in range(blocks):
            at = slice(b * LANES, (b + 1) * LANES)
            down_ref[0, :, at] = chunk_ref[0, at, 2 * LANES :].astype(F32)

    for k in range(2):
        pl.when(pl.program_id(1) == k)(lambda k=k: write(chunks[k]))


def unpack(plan, first, wave, chunks, shapes, outs):
    count, rows, width = chunks[0].shape
    chunk = pl.BlockSpec((1, rows, width), lambda i, d, n: (i, 0, 0))

    def place(i, d, n):
        block = n[n.shape[0] - 1]
        return n[first + 2 * i + d], 1 - block if wave else block

    def wide(i, d, n):
        expert, block = place(i, d, n)
        return (expert, 0, block)

    def low(i, d, n):
        expert, block = place(i, d, n)
        return (expert, block, 0)

    aliased = len(outs)
    return pl.pallas_call(
        functools.partial(unpack_kernel, aliased),
        grid_spec=pltpu.PrefetchScalarGridSpec(
            num_scalar_prefetch=1,
            grid=(count, 2),
            in_specs=[chunk, chunk] + [pl.BlockSpec(memory_space=pl.ANY)] * aliased,
            out_specs=[
                pl.BlockSpec((1, rows, LANES), wide),
                pl.BlockSpec((1, rows, LANES), wide),
                pl.BlockSpec((1, LANES, rows), low),
            ],
        ),
        out_shape=[jax.ShapeDtypeStruct(shape, F32) for shape in shapes],
        input_output_aliases={3 + k: k for k in range(aliased)},
        compiler_params=params(16, "arbitrary", "arbitrary"),
        cost_estimate=SMALL,
        name="unpack",
    )(plan, *chunks, *outs)


def late_chunk_kernel(plan_ref, pack_ref, *refs):
    *came, out_ref = refs
    if came:
        out_ref[...] = (came[0][...].astype(F32) + pack_ref[:, 0].astype(F32)).astype(BF16)
    else:
        out_ref[...] = pack_ref[:, 0]


def late_chunk(plan, at, pack, came):
    halves, _, rows, lanes = pack.shape
    spec = pl.BlockSpec((halves, rows, lanes), lambda i, n: (0, 0, 0))
    return pl.pallas_call(
        late_chunk_kernel,
        grid_spec=pltpu.PrefetchScalarGridSpec(
            num_scalar_prefetch=1,
            grid=(1,),
            in_specs=[pl.BlockSpec((halves, 1, rows, lanes), lambda i, n: (0, n[at], 0, 0))]
            + [spec] * len(came),
            out_specs=spec,
        ),
        out_shape=jax.ShapeDtypeStruct((halves, rows, lanes), BF16),
        compiler_params=params(16, "arbitrary"),
        cost_estimate=SMALL,
        name="late_chunk",
    )(plan, pack, *came)


def unpack_late_kernel(first_step, steps, plan_ref, *refs):
    chunks = refs[0 : 2 * steps]
    sgate, sup, sdown, query, key, value, out, all_ref = refs[2 * steps :]
    rows, features = chunks[0].shape[1], all_ref.shape[2]
    for k in range(2):
        for step in range(steps):
            at = plan_ref[first_step + 2 * step + k] * rows
            for c in range(2):
                all_ref[k, c, pl.ds(pl.multiple_of(at, rows), rows), :] = chunks[
                    steps * k + step
                ][c]
    flipped = plan_ref[plan_ref.shape[0] - 1] != 0
    for c in range(2):
        for b in range(14):
            lanes = slice(b % 7 * LANES, (b % 7 + 1) * LANES)
            first, second = all_ref[0, c, :, lanes], all_ref[1, c, :, lanes]
            if b >= 7:
                first, second = second, first
            block = jnp.where(flipped, second, first).astype(F32)
            if b < 6:
                at = slice((2 * c + b // 3) * LANES, (2 * c + b // 3 + 1) * LANES)
                if b % 3 < 2:
                    (sgate, sup)[b % 3][:, at] = block
                else:
                    for k in range(features // LANES):
                        here = slice(k * LANES, (k + 1) * LANES)
                        sdown[at, here] = block[here, :]
            elif b < 9:
                at = (GROUP_HEADS * c + b - 6) * LANES
                query[:, at : at + LANES] = block
            elif b < 11:
                (key, value)[b - 9][:, c * LANES : (c + 1) * LANES] = block
            else:
                at = (GROUP_HEADS * c + b - 11) * LANES
                out[at : at + LANES, :] = block.T


def unpack_late(plan, first_step, chunks, shapes):
    steps = len(chunks[0])
    halves, rows, lanes = chunks[0][0].shape
    spec = pl.BlockSpec(memory_space=pltpu.VMEM)
    return pl.pallas_call(
        functools.partial(unpack_late_kernel, first_step, steps),
        in_specs=[pl.BlockSpec(memory_space=pltpu.SMEM)] + [spec] * (2 * steps),
        out_specs=[spec] * len(shapes),
        out_shape=[jax.ShapeDtypeStruct(shape, F32) for shape in shapes],
        scratch_shapes=[pltpu.VMEM((2, halves, steps * rows, lanes), BF16)],
        compiler_params=params(48),
        cost_estimate=SMALL,
        name="unpack_late",
    )(plan, *chunks[0], *chunks[1])


def plans(ring, each):
    size = len(ring)
    rows = []
    for member in range(size):
        place = ring.index(member)
        for col in range(2):
            chunks = []
            for step in range(2 * size - 1):
                for which in range(2):
                    sign = 1 if which == col else -1
                    chunks.append((place - sign * step) % size)
            experts = []
            for start in (0, size - 1):
                for step in range(start, start + size):
                    for k in range(each):
                        for which in range(2):
                            second = col if which == 0 else 1 - col
                            experts.append(2 * each * chunks[2 * step + which] + each * second + k)
            rows.append(experts + chunks + [col])
    return np.asarray(rows, np.int32)


LATE_ROUND = 1


def add_rounded(left, right):
    return (left.astype(F32) + right.astype(F32)).astype(BF16)


def body(
    tokens_in,
    norm_gain_attn,
    w_query,
    w_key,
    w_value,
    w_out,
    norm_gain_ffn,
    w_gate,
    w_up,
    w_down,
    w_shared_gate,
    w_shared_up,
    w_shared_down,
    routes,
    gate_weights,
    seq_lengths,
    out_grad,
):
    row = lax.axis_index("row")
    col = lax.axis_index("col")
    dp = lax.axis_index("dp")
    dp_size = lax.axis_size("dp")
    local_rows, local_features = tokens_in.shape
    experts = w_gate.shape[0]
    group_width = GROUP_HEADS * DH
    col_ref = col.reshape(1)

    ring_size = min(8, dp_size)
    ring = ring_of(ring_size)
    starts = range(0, dp_size, ring_size)
    rights = [
        (g + ring[k], g + ring[(k + 1) % ring_size]) for g in starts for k in range(ring_size)
    ]
    lefts = [(b, a) for a, b in rights]
    routes_of = [
        [(2 * a, 2 * b) for a, b in ways[0]] + [(2 * a + 1, 2 * b + 1) for a, b in ways[1]]
        for ways in ((rights, lefts), (lefts, rights))
    ]
    experts_each = experts // (2 * ring_size)
    plan = jnp.asarray(plans(ring, experts_each))
    plan = lax.dynamic_slice(
        plan, (2 * (dp % ring_size) + col, jnp.int32(0)), (1, plan.shape[1])
    ).reshape(-1)

    def send(values, which):
        if ring_size == 1:
            return values
        return lax.ppermute(values, ("dp", "col"), routes_of[which])

    def chunk_at(step, which):
        return plan[2 * experts + 2 * step + which]

    def across_rings(values):
        if len(starts) == 1:
            return values
        peers = [[g + k for g in starts] for k in range(ring_size)]
        return lax.psum(values, "dp", axis_index_groups=peers)

    where = jnp.stack([row, seq_lengths[0], col])
    tokens_y = swap(tokens_in, "row")
    tokens_c = swap(tokens_in, "col")
    count = min(ring_size, 4)
    member = dp % count
    there, out_y = their_columns(
        jnp.stack([col, member]), w_query, w_key, w_value, w_out, count
    )
    gains = jnp.stack([norm_gain_attn, norm_gain_ffn])
    there = swap(there, "col")
    gains_c = swap(gains, "col")

    def project_half(own, other):
        return project(col_ref, own, other, gains, gains_c, w_query, w_key, w_value, there)

    near = project_half(tokens_in, tokens_c)
    gate_c = swap(w_gate, "col")
    out_y = swap(out_y, "row")
    tokens_y = after(tokens_y, near[2], out_y)
    tokens_yc = swap(tokens_y, "col")
    grad_cut = local_rows // 8 * 5
    grad_y = swap(after(out_grad[:grad_cut], tokens_y), "row")
    far = project_half(tokens_y, tokens_yc)

    shares = [out_y]
    for k in range(1, count):
        part = out_y if k == 1 else after(out_y, far[2])
        shares.append(lax.ppermute(part, "dp", [(m, m ^ k) for m in range(dp_size)]))
    where = after(where, grad_y, *shares)

    w_sgate, w_sup, w_sdown = w_shared_gate[None], w_shared_up[None], w_shared_down[None]
    up_c = swap(after(w_up, gate_c, tokens_yc), "col")

    attended = attend(where, near[2], far[2])
    attended_y = swap(attended, "row")
    attended_c = swap(attended, "col")
    out_c = swap(after(w_out, tokens_yc), "col")
    before = hidden_before(
        where,
        [tokens_in, tokens_c, tokens_y, tokens_yc],
        [attended, attended_c],
        w_out,
        out_c,
    )
    down_c = swap(after(w_down, tokens_yc), "col")
    rest_y = swap(after(out_grad[grad_cut:], attended_c), "row")
    attended_y = after(attended_y, before[0])
    out_y = join(member, *shares)
    out_yc = swap(out_y, "col")
    attended_yc = swap(attended_y, "col")
    grad_own = join(row, out_grad, jnp.concatenate([grad_y, rest_y], axis=0))
    grad_other = swap(grad_own, "col")
    hidden, x_own, x_other, scale_ffn = hidden_after(
        where, before, [attended_y, attended_yc], out_y, out_yc, gains, gains_c
    )
    sgate_c, sup_c, sdown_c = (
        swap(after(w, attended_yc), "col") for w in (w_sgate, w_sup, w_sdown)
    )

    choices = jnp.arange(experts, dtype=jnp.int32)[:, None]
    dense = sum(
        jnp.where(routes[:, k][None, :] == choices, gate_weights[:, k][None, :], 0.0)
        for k in range(routes.shape[1])
    )
    gates = []
    for _ in range(3):
        gates.append(lax.reduce_precision(dense, 8, 7))
        dense = dense - gates[-1]
    gates = jnp.concatenate(gates, axis=0).astype(BF16)

    each = experts_each
    order = plan
    pairs_total = experts // 2
    routed = [w_gate, w_up, gate_c, up_c, w_down, down_c]
    shared = [w_sgate, w_sup, sgate_c, sup_c, w_sdown, sdown_c]

    def run(first, last, order, kept):
        return expert_grads(
            order,
            first,
            last,
            pairs_total,
            [x_own, x_other],
            [grad_own, grad_other],
            gates,
            routed,
            kept,
        )

    first = run(0, each, order, ())
    kept = first[2:]
    sums = [first[0], first[1]]
    runs = {}
    mixed = {}

    def work_experts(first, last):
        def work(order):
            nonlocal kept
            result = run(first, last, order, tuple(kept))
            kept = result[2:]
            for at in range(first, last):
                runs[at] = (result[0], result[1], at - first)
            return kept[0]

        return work

    def work_shared(order):
        runs["shared"] = expert_grads(
            order, 0, 1, None, [x_own, x_other], [grad_own, grad_other], gates, shared, ()
        )
        return runs["shared"][2]

    def work_mix(back, half):
        def work(order):
            pick = slice(2 * half, 2 * half + 2) if back else slice(4 + half, 5 + half)
            mixed[back, half] = mix(
                back,
                BF16 if half else F32,
                order,
                kept[0 if back else 1],
                runs["shared"][2 if back else 3],
                routed[pick],
                shared[pick],
            )
            return mixed[back, half]

        return work

    start = row * local_rows

    def my_rows(values):
        return lax.dynamic_slice_in_dim(values, start, local_rows, axis=0)

    def their_rows(values):
        return lax.dynamic_slice_in_dim(values, local_rows - start, local_rows, axis=0)

    normed = {}

    def work_hidden(order):
        normed_grad = mixed[True, 0] + swap(mixed[True, 1], "col").astype(F32)
        came = swap(normed_grad.astype(BF16), "row")
        normed_grad = normed_grad + after(came, order).astype(F32)
        scaled = normed_grad * norm_gain_ffn
        products = jnp.sum(scaled * hidden, axis=1, keepdims=True)
        mean = (products + swap(products, "col")) / D
        normed["gain"] = jnp.sum(my_rows(normed_grad * hidden * scale_ffn), axis=0)
        normed["hidden"] = (
            grad_own.astype(F32) + scale_ffn * scaled - hidden * scale_ffn**3 * mean
        )
        normed["grad"] = normed["hidden"].astype(BF16)
        normed["grad_c"] = swap(normed["grad"], "col")
        return normed["grad"]

    def work_attend(order):
        normed["qkv"] = attend_back(
            after(where, order), near[2], far[2], normed["grad"], normed["grad_c"], w_out, out_c
        )
        return normed["qkv"]

    tasks = [work_experts(at, at + each) for at in range(each, pairs_total, each)]
    tasks += [work_shared, work_mix(True, 1), work_mix(True, 0), work_mix(False, 1), work_mix(False, 0)]
    tasks += [None] * (2 * ring_size - 3 - len(tasks)) + [work_hidden, work_attend]
    got = [None, None]
    if ring_size > 1:
        got[0] = send(sums[0], 0)
        tasks.pop(0)(after(order, *sums))
        got[1] = send(after(sums[1], kept[0]), 1)
    for s in range(1, ring_size):
        for k in range(2):
            last = sums
            task = tasks.pop(0) if tasks else None
            if task:
                last = [task(after(order, *last))]
            got[k] = after(got[k], *last)
            parts = [runs[at] for at in range(each * s, each * s + each)]
            mine = [p[k][p[2] : p[2] + 1] for p in parts]
            mine = mine[0] if each == 1 else jnp.concatenate(mine, axis=0)
            sums[k] = add_rounded(got[k], mine)
            if s + 1 < ring_size:
                got[k] = send(sums[k], k)
    for task in tasks:
        if task:
            task(after(order, *sums))
    sums = [across_rings(total) for total in sums]
    waves = [[total[:, :local_features] for total in sums]]
    crossed = [swap(total[:, local_features:], "col") for total in sums]
    waves.append([crossed[1], crossed[0]])

    hidden_grad, attn_grad, attn_grad_c = normed["hidden"], normed["grad"], normed["grad_c"]
    gain_ffn_part, qkv_grad = normed["gain"], normed["qkv"]
    packs = late_grads(
        where,
        near[0:2],
        far[0:2],
        qkv_grad,
        attended,
        attn_grad,
        attn_grad_c,
        runs["shared"][0:2],
    )

    packs = [
        pack.reshape(2, ring_size, local_features // ring_size, pack.shape[2]) for pack in packs
    ]
    chunks_first = 2 * experts
    late = [late_chunk(plan, chunks_first + k, packs[k], ()) for k in range(2)]
    late_out = [[], []]
    late_done = 0
    late_total = 2 * (ring_size - 1)

    def late_turn():
        totals = [across_rings(values) for values in late]
        others = [swap(values[1], "col") for values in totals]
        for k in range(2):
            late[k] = in_order(totals[k][0:1], others[1 - k][None], col, 0)
            late_out[k].append(late[k])

    def late_finish(k, values):
        if late_done < ring_size:
            at = chunks_first + 2 * late_done + k
            late[k] = late_chunk(plan, at, packs[k], (values,))
        else:
            late[k] = values
            late_out[k].append(values)

    shapes = [w_gate.shape, w_up.shape, w_down.shape]
    placed = ()

    def place_chunks(wave, step, chunks, placed):
        return unpack(plan, experts + 2 * each * step, wave, chunks, shapes, placed)

    if late_total == 0:
        late_turn()
    rounds = [(wave, step) for wave in range(2) for step in range(ring_size - 1)]
    late_got = None
    last = list(sums)
    for number, (wave, step) in enumerate(rounds):
        if step == 0:
            came = list(got) if number else None
            got = list(waves[wave])
        late_done += late_got is not None
        chunks = [None, None]
        for k in range(2):
            chunks[k] = after(got[k], *last)
            got[k] = send(chunks[k], k)
            last = [chunks[k]]
            if late_got is not None:
                late_finish(k, after(late_got[k], *last))
                last = [late[k]]
        if late_got is not None and late_done == ring_size - 1:
            late_turn()
        if number >= LATE_ROUND and late_done < late_total:
            late_got = [send(after(late[k], *chunks), k) for k in range(2)]
        else:
            late_got = None
        if step == 0 and number:
            placed = place_chunks(0, ring_size - 1, came, placed)
        placed = place_chunks(wave, step, chunks, placed)
        last = placed[0:1]
        if number == LATE_ROUND + 3:
            qkv_grad = after(qkv_grad, *last)
    if rounds:
        placed = place_chunks(1, ring_size - 1, [after(got[k], *last) for k in range(2)], placed)
        last = placed[0:1]
    while late_got is not None:
        late_done += 1
        for k in range(2):
            late_finish(k, after(late_got[k], *last))
        if late_done == ring_size - 1:
            late_turn()
        late_got = [send(late[k], k) for k in range(2)] if late_done < late_total else None
    if not rounds:
        for wave in range(2):
            placed = place_chunks(wave, 0, waves[wave], placed)
    gate_grad, up_grad, down_grad = placed
    shapes = [w.shape for w in (w_shared_gate, w_shared_up, w_shared_down)]
    shapes += [w.shape for w in (w_query, w_key, w_value, w_out)]
    finals = unpack_late(plan, chunks_first + late_total, late_out, shapes)
    shared_gate_grad, shared_up_grad, shared_down_grad = finals[0:3]
    query_grad, key_grad, value_grad, out_proj_grad = finals[3:7]

    ffn_sum = mixed[False, 0] + swap(mixed[False, 1], "col").astype(F32)
    ffn_rows = my_rows(ffn_sum) + swap(their_rows(ffn_sum).astype(BF16), "row").astype(F32)
    block_out = (my_rows(hidden) + ffn_rows).astype(BF16)

    here = jnp.concatenate(
        [halves(w, 1, col)[0] for w in (w_query, w_key, w_value)], axis=1
    )
    tokens_back = dot_nt(qkv_grad, here) + swap(
        dot_nt(qkv_grad, there).astype(BF16), "col"
    ).astype(F32)
    tokens_back = my_rows(tokens_back) + swap(
        their_rows(tokens_back).astype(BF16), "row"
    ).astype(F32)
    scale_attn = near[3]
    tokens_f32 = tokens_in.astype(F32)
    gain_attn_part = jnp.sum(tokens_back * tokens_f32 * scale_attn, axis=0)
    scaled = tokens_back * norm_gain_attn
    products = jnp.sum(scaled * tokens_f32, axis=1, keepdims=True)
    mean = (products + swap(products, "col")) / D
    tokens_grad = (
        my_rows(hidden_grad) + scale_attn * scaled - tokens_f32 * scale_attn**3 * mean
    ).astype(BF16)

    gain_parts = jnp.stack([gain_attn_part, gain_ffn_part])
    bit = 1
    while bit < ring_size:
        pairs = [(g + k, g + (k ^ bit)) for g in starts for k in range(ring_size)]
        gain_parts = gain_parts + lax.ppermute(gain_parts, "dp", pairs)
        bit *= 2
    gain_parts = across_rings(gain_parts + swap(gain_parts, "row"))

    return (
        block_out,
        tokens_grad,
        gain_parts[0],
        query_grad,
        key_grad,
        value_grad,
        out_proj_grad,
        gain_parts[1],
        gate_grad,
        up_grad,
        down_grad,
        shared_gate_grad,
        shared_up_grad,
        shared_down_grad,
    )


def solution(mesh):
    in_specs = (
        P(("dp", "row"), "col"),
        P("col"),
        P("col", "row"),
        P("col", "row"),
        P("col", "row"),
        P("row", "col"),
        P("col"),
        P(None, "col", "row"),
        P(None, "col", "row"),
        P(None, "row", "col"),
        P("col", "row"),
        P("col", "row"),
        P("row", "col"),
        P("dp", None),
        P("dp", None),
        P("dp"),
        P(("dp", "row"), "col"),
    )
    out_specs = (
        P(("dp", "row"), "col"),
        P(("dp", "row"), "col"),
        P("col"),
        P("col", "row"),
        P("col", "row"),
        P("col", "row"),
        P("row", "col"),
        P("col"),
        P(None, "col", "row"),
        P(None, "col", "row"),
        P(None, "row", "col"),
        P("col", "row"),
        P("col", "row"),
        P("row", "col"),
    )
    return jax.shard_map(body, mesh=mesh, in_specs=in_specs, out_specs=out_specs, check_vma=False)
```

```python
import functools

import jax
import jax.numpy as jnp
import numpy as np
from jax import lax
from jax.experimental import pallas as pl
from jax.experimental.pallas import tpu as pltpu
from jax.sharding import PartitionSpec as P

D = 1536
HQ = 12
HK = 4
DH = 128
GROUP_HEADS = HQ // HK
LANES = 128

EPSILON = 1e-05
F32 = jnp.float32
BF16 = jnp.bfloat16
MIB = 1024 * 1024
SMALL = pl.CostEstimate(flops=0, bytes_accessed=0, transcendentals=0)


def params(mib, *semantics):
    return pltpu.CompilerParams(
        dimension_semantics=semantics or None, vmem_limit_bytes=mib * MIB
    )


def dot(left, right):
    return jnp.dot(left, right, preferred_element_type=F32)


def dot_nt(left, right):
    return lax.dot_general(left, right, (((1,), (1,)), ((), ())), preferred_element_type=F32)


def dot_tn(left, right):
    return lax.dot_general(left, right, (((0,), (0,)), ((), ())), preferred_element_type=F32)


def after(values, *others):
    return lax.optimization_barrier((values, *others))[0]


def swap(values, axis):
    return lax.ppermute(values, axis, [(0, 1), (1, 0)])


def halves(values, axis, mine):
    size = values.shape[axis] // 2
    low = lax.slice_in_dim(values, 0, size, axis=axis)
    high = lax.slice_in_dim(values, size, 2 * size, axis=axis)
    return jnp.where(mine == 0, low, high), jnp.where(mine == 0, high, low)


def in_order(own, other, mine, axis):
    return jnp.concatenate(
        [jnp.where(mine == 0, own, other), jnp.where(mine == 0, other, own)], axis=axis
    )


def gather_rows(place_ref, own_ref, other_ref, all_ref):
    row = place_ref[0]
    rows = own_ref.shape[0]
    all_ref[pl.ds(pl.multiple_of(row * rows, rows), rows), :] = own_ref[...]
    all_ref[pl.ds(pl.multiple_of((1 - row) * rows, rows), rows), :] = other_ref[...]


def head_rows(ref, first, block):
    return jnp.concatenate(
        [ref[first : first + block, h * DH : (h + 1) * DH] for h in range(GROUP_HEADS)], axis=0
    )


def key_probs(query, key, first, length):
    block, keys = query.shape[0] // GROUP_HEADS, key.shape[0]
    scores = dot_nt(query, key) * DH ** (-0.5)
    shape = (block, keys)
    query_at = lax.broadcasted_iota(jnp.int32, shape, 0) + first
    key_at = lax.broadcasted_iota(jnp.int32, shape, 1)
    allowed = (key_at <= query_at) & (key_at < length)
    allowed = jnp.concatenate([allowed] * GROUP_HEADS, axis=0)
    scores = jnp.where(allowed, scores, -1e30)
    weights = jnp.exp(scores - jnp.max(scores, axis=1, keepdims=True))
    return weights * (1.0 / jnp.sum(weights, axis=1, keepdims=True))


def attend_kernel(place_ref, own_ref, other_ref, out_ref, all_ref):
    gather_rows(place_ref, own_ref, other_ref, all_ref)
    rows = own_ref.shape[0]
    block = 256
    width = GROUP_HEADS * DH
    for at in range(2 * rows // block):
        first, keys = at * block, (at + 1) * block
        query = head_rows(all_ref, first, block)
        key = all_ref[0:keys, width : width + DH]
        value = all_ref[0:keys, width + DH : width + 2 * DH]
        probs = key_probs(query, key, first, place_ref[1])
        result = dot(probs.astype(BF16), value).astype(BF16)
        for h in range(GROUP_HEADS):
            out_ref[first : first + block, h * DH : (h + 1) * DH] = result[
                h * block : (h + 1) * block
            ]


def attend(place, own, other):
    rows, width = own.shape
    spec = pl.BlockSpec(memory_space=pltpu.VMEM)
    return pl.pallas_call(
        attend_kernel,
        out_shape=jax.ShapeDtypeStruct((2 * rows, GROUP_HEADS * DH), BF16),
        in_specs=[pl.BlockSpec(memory_space=pltpu.SMEM), spec, spec],
        out_specs=spec,
        scratch_shapes=[pltpu.VMEM((2 * rows, width), BF16)],
        compiler_params=params(32),
        cost_estimate=SMALL,
        name="attend",
    )(place, own, other)


def attend_back_kernel(
    place_ref, own_ref, other_ref, grad_ref, grad_c_ref, out_ref, out_c_ref, result_ref, all_ref, total_ref
):
    gather_rows(place_ref, own_ref, other_ref, all_ref)
    rows = own_ref.shape[0]
    block = 256
    width = GROUP_HEADS * DH
    group = pl.ds(pl.multiple_of(place_ref[2] * width, width), width)
    blocks = 2 * rows // block
    for at in reversed(range(blocks)):
        first, keys = at * block, (at + 1) * block
        query = head_rows(all_ref, first, block)
        key = all_ref[0:keys, width : width + DH]
        value = all_ref[0:keys, width + DH : width + 2 * DH]
        probs = key_probs(query, key, first, place_ref[1])
        grad = dot_nt(grad_ref[first:keys, :], out_ref[group, :])
        grad = (grad + dot_nt(grad_c_ref[first:keys, :], out_c_ref[group, :])).astype(BF16)
        grad = jnp.concatenate(
            [grad[:, h * DH : (h + 1) * DH] for h in range(GROUP_HEADS)], axis=0
        )
        probs_grad = dot_nt(grad, value)
        carried = jnp.sum(probs * probs_grad, axis=1, keepdims=True)
        score_grad = (probs * (probs_grad - carried)).astype(BF16)
        query_back = (dot(score_grad, key) * DH ** (-0.5)).astype(BF16)
        for h in range(GROUP_HEADS):
            result_ref[first:keys, h * DH : (h + 1) * DH] = query_back[
                h * block : (h + 1) * block
            ]
        key_back = dot_tn(score_grad, query)
        value_back = dot_tn(probs.astype(BF16), grad)
        if at == blocks - 1:
            total_ref[:, 0:DH] = key_back
            total_ref[:, DH:] = value_back
        else:
            total_ref[0:keys, 0:DH] += key_back
            total_ref[0:keys, DH:] += value_back
    result_ref[:, width : width + DH] = (total_ref[:, 0:DH] * DH ** (-0.5)).astype(BF16)
    result_ref[:, width + DH :] = total_ref[:, DH:].astype(BF16)


def attend_back(place, own, other, grad, grad_c, w_out, out_c):
    rows, width = own.shape
    spec = pl.BlockSpec(memory_space=pltpu.VMEM)
    return pl.pallas_call(
        attend_back_kernel,
        out_shape=jax.ShapeDtypeStruct((2 * rows, width), BF16),
        in_specs=[pl.BlockSpec(memory_space=pltpu.SMEM)] + [spec] * 6,
        out_specs=spec,
        scratch_shapes=[
            pltpu.VMEM((2 * rows, width), BF16),
            pltpu.VMEM((2 * rows, 2 * DH), F32),
        ],
        compiler_params=params(60),
        cost_estimate=SMALL,
        name="attend_back",
    )(place, own, other, grad, grad_c, w_out, out_c)


def late_kernel(place_ref, *refs):
    near, near_c, far, far_c, qkv_ref, attended_ref, grad_ref, grad_c_ref = refs[0:8]
    shared = refs[8:10]
    outs = refs[10:12]
    rows, features = near.shape
    own_rows = pl.ds(pl.multiple_of(place_ref[0] * rows, rows), rows)
    far_rows = pl.ds(pl.multiple_of((1 - place_ref[0]) * rows, rows), rows)
    split = 7 * LANES

    def store(h, at, values):
        values = values.astype(BF16)
        for part in range(2):
            low, high = max(at, part * split), min(at + values.shape[1], (part + 1) * split)
            if low < high:
                piece = values[:, low - at : high - at]
                to = slice(low - part * split, high - part * split)

                @pl.when(place_ref[2] == 0)
                def _(part=part, to=to, piece=piece):
                    outs[part][h, :, to] = piece

                @pl.when(place_ref[2] != 0)
                def _(part=part, to=to, piece=piece):
                    outs[1 - part][h, :, to] = piece

    for h, (x, y, grad) in enumerate(((near, far, grad_ref), (near_c, far_c, grad_c_ref))):
        for k in range(2):
            store(h, 3 * LANES * k, shared[k][0, h * features : (h + 1) * features, :])
        project = dot_tn(x[...], qkv_ref[own_rows, :]) + dot_tn(y[...], qkv_ref[far_rows, :])
        store(h, 6 * LANES, project)
        store(h, 11 * LANES, dot_tn(grad[...], attended_ref[...]))


def late_grads(place, near, far, qkv_grad, attended, grad, grad_c, shared):
    features = near[0].shape[1]
    spec = pl.BlockSpec(memory_space=pltpu.VMEM)
    return pl.pallas_call(
        late_kernel,
        out_shape=[jax.ShapeDtypeStruct((2, features, 7 * LANES), BF16)] * 2,
        in_specs=[pl.BlockSpec(memory_space=pltpu.SMEM)] + [spec] * 10,
        out_specs=[spec] * 2,
        compiler_params=params(60),
        cost_estimate=SMALL,
        name="late_grads",
    )(place, *near, *far, qkv_grad, attended, grad, grad_c, *shared)


def columns_kernel(
    place_ref, query_ref, key_ref, value_ref, w_out_ref, out_ref, share_ref
):
    share_ref[...] = w_out_ref[...]
    width = GROUP_HEADS * DH
    out_ref[:, 0:width] = query_ref[...]
    out_ref[:, width : width + DH] = key_ref[...]
    out_ref[:, width + DH :] = value_ref[...]


def their_columns(place, w_query, w_key, w_value, w_out, shares):
    rows = w_query.shape[0]
    width = GROUP_HEADS * DH + 2 * DH

    def theirs(width):
        return pl.BlockSpec((rows, width), lambda i, c: (0, 1 - c[0]))

    return pl.pallas_call(
        columns_kernel,
        grid_spec=pltpu.PrefetchScalarGridSpec(
            num_scalar_prefetch=1,
            grid=(1,),
            in_specs=[theirs(GROUP_HEADS * DH), theirs(DH), theirs(DH)]
            + [pl.BlockSpec((rows // shares, rows), lambda i, c: (c[1], 0))],
            out_specs=[
                pl.BlockSpec((rows, width), lambda i, c: (0, 0)),
                pl.BlockSpec((rows // shares, rows), lambda i, c: (0, 0)),
            ],
        ),
        out_shape=[
            jax.ShapeDtypeStruct((rows, width), BF16),
            jax.ShapeDtypeStruct((rows // shares, rows), BF16),
        ],
        compiler_params=params(60, "arbitrary"),
        cost_estimate=SMALL,
        name="their_columns",
    )(place, w_query, w_key, w_value, w_out)


def join_kernel(mine_ref, *refs):
    *parts, out_ref = refs
    rows = parts[0].shape[0]
    for k, part in enumerate(parts):
        at = jnp.bitwise_xor(mine_ref[0], k)
        out_ref[pl.ds(pl.multiple_of(at * rows, rows), rows), :] = part[...]


def join(mine, *parts):
    rows, width = parts[0].shape
    spec = pl.BlockSpec(memory_space=pltpu.VMEM)
    return pl.pallas_call(
        join_kernel,
        out_shape=jax.ShapeDtypeStruct((len(parts) * rows, width), parts[0].dtype),
        in_specs=[pl.BlockSpec(memory_space=pltpu.SMEM)] + [spec] * len(parts),
        out_specs=spec,
        compiler_params=params(16),
        cost_estimate=SMALL,
        name="join",
    )(mine.reshape(1), *parts)


def project_kernel(col_ref, own_ref, other_ref, gains_ref, gains_c_ref, query_ref, key_ref, value_ref, there_ref, x_own_ref, x_other_ref, qkv_ref, scale_ref):
    own = own_ref[...].astype(F32)
    other = other_ref[...].astype(F32)
    total = jnp.sum(own * own, axis=1, keepdims=True)
    total = total + jnp.sum(other * other, axis=1, keepdims=True)
    scale = lax.rsqrt(total / D + EPSILON)
    own = (own * scale * gains_ref[0:1, :]).astype(BF16)
    other = (other * scale * gains_c_ref[0:1, :]).astype(BF16)
    x_own_ref[...] = own
    x_other_ref[...] = other
    scale_ref[...] = scale
    here = jnp.concatenate([query_ref[...], key_ref[...], value_ref[...]], axis=1)
    qkv_ref[...] = (dot(own, here) + dot(other, there_ref[...])).astype(BF16)


def project(col, own, other, gains, gains_c, w_query, w_key, w_value, there):
    rows, features = own.shape
    width = there.shape[1]
    group = GROUP_HEADS * DH
    tile = rows // 2

    def whole(*shape):
        return pl.BlockSpec(shape, lambda i, c: (0,) * len(shape))

    def mine(width):
        return pl.BlockSpec((features, width), lambda i, c: (0, c[0]))

    def rowwise(width):
        return pl.BlockSpec((tile, width), lambda i, c: (i, 0))

    return pl.pallas_call(
        project_kernel,
        grid_spec=pltpu.PrefetchScalarGridSpec(
            num_scalar_prefetch=1,
            grid=(rows // tile,),
            in_specs=[
                rowwise(features),
                rowwise(features),
                whole(2, features),
                whole(2, features),
                mine(group),
                mine(DH),
                mine(DH),
                whole(features, width),
            ],
            out_specs=[rowwise(features), rowwise(features), rowwise(width), rowwise(1)],
        ),
        out_shape=[
            jax.ShapeDtypeStruct((rows, features), BF16),
            jax.ShapeDtypeStruct((rows, features), BF16),
            jax.ShapeDtypeStruct((rows, width), BF16),
            jax.ShapeDtypeStruct((rows, 1), F32),
        ],
        compiler_params=params(60, "arbitrary"),
        cost_estimate=SMALL,
        name="project",
    )(col, own, other, gains, gains_c, w_query, w_key, w_value, there)


def head_pair(col_ref, own, other):
    first, second = own[...], other[...]
    flipped = col_ref != 0
    return jnp.concatenate(
        [jnp.where(flipped, second, first), jnp.where(flipped, first, second)], axis=1
    )


def before_kernel(tiles, place_ref, *refs):
    near, near_c, far, far_c, attended, attended_c, here, there, own_ref, other_ref = refs
    is_near = (pl.program_id(0) >= tiles // 2).astype(jnp.int32) == place_ref[0]
    heads = head_pair(place_ref[2], attended, attended_c)
    own = jnp.where(is_near, near[...], far[...]).astype(F32)
    other = jnp.where(is_near, near_c[...], far_c[...]).astype(F32)
    own_ref[...] = own + dot(heads, here[...])
    other_ref[...] = other + dot(heads, there[...])


def after_kernel(place_ref, *refs):
    own_ref, other_ref, attended, attended_c, here, there, gains_ref, gains_c_ref = refs[0:8]
    hidden_ref, x_own_ref, x_other_ref, scale_ref = refs[8:12]
    heads = head_pair(place_ref[2], attended, attended_c)
    own = own_ref[...] + dot(heads, here[...])
    other = other_ref[...] + dot(heads, there[...])
    total = jnp.sum(own * own, axis=1, keepdims=True)
    total = total + jnp.sum(other * other, axis=1, keepdims=True)
    scale = lax.rsqrt(total / D + EPSILON)
    hidden_ref[...] = own
    scale_ref[...] = scale
    x_own_ref[...] = (own * scale * gains_ref[1:2, :]).astype(BF16)
    x_other_ref[...] = (other * scale * gains_c_ref[1:2, :]).astype(BF16)


TOKEN_TILE = 256


def rowwise(width):
    return pl.BlockSpec((TOKEN_TILE, width), lambda i, p: (i, 0))


def whole(*shape):
    return pl.BlockSpec(shape, lambda i, p: (0,) * len(shape))


def hidden_before(place, tokens, attended, here, there):
    half, features = tokens[0].shape
    rows, heads = attended[0].shape
    tiles = rows // TOKEN_TILE
    per_half = half // TOKEN_TILE
    halfwise = pl.BlockSpec((TOKEN_TILE, features), lambda i, p: (i % per_half, 0))
    return pl.pallas_call(
        functools.partial(before_kernel, tiles),
        grid_spec=pltpu.PrefetchScalarGridSpec(
            num_scalar_prefetch=1,
            grid=(tiles,),
            in_specs=[halfwise] * 4 + [rowwise(heads)] * 2 + [whole(2 * heads, features)] * 2,
            out_specs=[rowwise(features)] * 2,
        ),
        out_shape=[jax.ShapeDtypeStruct((rows, features), F32)] * 2,
        compiler_params=params(56, "arbitrary"),
        cost_estimate=pl.CostEstimate(
            flops=8 * rows * features * heads,
            bytes_accessed=16 * rows * features,
            transcendentals=0,
        ),
        name="hidden_before",
    )(place, *tokens, *attended, here, there)


def hidden_after(place, before, attended, here, there, gains, gains_c):
    rows, features = before[0].shape
    heads = attended[0].shape[1]
    return pl.pallas_call(
        after_kernel,
        grid_spec=pltpu.PrefetchScalarGridSpec(
            num_scalar_prefetch=1,
            grid=(rows // TOKEN_TILE,),
            in_specs=[rowwise(features)] * 2
            + [rowwise(heads)] * 2
            + [whole(2 * heads, features)] * 2
            + [whole(2, features)] * 2,
            out_specs=[rowwise(features)] * 3 + [rowwise(1)],
        ),
        out_shape=[
            jax.ShapeDtypeStruct((rows, features), F32),
            jax.ShapeDtypeStruct((rows, features), BF16),
            jax.ShapeDtypeStruct((rows, features), BF16),
            jax.ShapeDtypeStruct((rows, 1), F32),
        ],
        compiler_params=params(56, "arbitrary"),
        cost_estimate=SMALL,
        name="hidden_after",
    )(place, *before, *attended, here, there, gains, gains_c)


def expert_kernel(shared, aliased, first, order_ref, *refs):
    x_own, x_other, o_own, o_other, gates_ref = refs[0:5]
    weights = refs[5:17]
    grads = refs[17 + aliased : 19 + aliased]
    pair_ref, inner_ref = refs[19 + aliased : 21 + aliased]
    step = pl.program_id(0) + first
    rows, features = x_own.shape
    tile = 512
    up_own = jnp.concatenate([weights[k][0] for k in (0, 1, 6, 7)], axis=1)
    up_other = jnp.concatenate([weights[k][0] for k in (2, 3, 8, 9)], axis=1)
    down_own = jnp.concatenate([weights[k][0] for k in (4, 10)], axis=0)
    down_other = jnp.concatenate([weights[k][0] for k in (5, 11)], axis=0)

    def token_tile(t, carry):
        at = pl.ds(pl.multiple_of(t * tile, tile), tile)
        pre = dot(x_own[at, :], up_own) + dot(x_other[at, :], up_other)
        back = dot_nt(o_own[at, :], down_own) + dot_nt(o_other[at, :], down_other)
        for k in range(2):
            pre_gate = pre[:, 2 * k * LANES : (2 * k + 1) * LANES]
            pre_up = pre[:, (2 * k + 1) * LANES : (2 * k + 2) * LANES]
            inner_grad = back[:, k * LANES : (k + 1) * LANES]
            sigmoid = 1.0 / (1.0 + jnp.exp(-pre_gate))
            silu = pre_gate * sigmoid
            inner = silu * pre_up
            if not shared:
                shape = (gates_ref.shape[0], LANES)
                expert = lax.broadcasted_iota(jnp.int32, shape, 0) % (gates_ref.shape[0] // 3)
                chosen = (expert == order_ref[2 * step + k]).astype(F32).astype(BF16)
                gate = dot_tn(gates_ref[:, at], chosen)
                inner = gate * inner
                inner_grad = gate * inner_grad
            gate_grad = inner_grad * pre_up * (sigmoid * (1.0 + pre_gate * (1.0 - sigmoid)))
            inner_ref[0, at, k * LANES : (k + 1) * LANES] = inner.astype(BF16)
            pair_ref[0, at, 2 * k * LANES : (2 * k + 1) * LANES] = gate_grad.astype(BF16)
            pair_ref[0, at, (2 * k + 1) * LANES : (2 * k + 2) * LANES] = (
                inner_grad * silu
            ).astype(BF16)
        return carry

    lax.fori_loop(0, rows // tile, token_tile, 0)
    pairs = pair_ref[0]
    for h, x in enumerate((x_own, x_other)):
        wide = dot_tn(x[...], pairs).astype(BF16)
        for k in range(2):
            grads[k][0, h * features : (h + 1) * features, 0 : 2 * LANES] = wide[
                :, 2 * k * LANES : (2 * k + 2) * LANES
            ]
    inner = inner_ref[0]
    tile = 256
    for h, o in enumerate((o_own, o_other)):
        for j in range(features // tile):
            low = dot_tn(inner, o[:, j * tile : (j + 1) * tile]).astype(BF16)
            for k in range(2):
                for b in range(tile // LANES):
                    at = h * features + j * tile + b * LANES
                    grads[k][0, at : at + LANES, 2 * LANES :] = low[
                        k * LANES : (k + 1) * LANES, b * LANES : (b + 1) * LANES
                    ]


def expert_specs(features, place, wide, low):
    specs = []
    if wide:
        block = pl.BlockSpec((1, features, LANES), lambda i, o: (place(i, o)[0], 0, place(i, o)[1]))
        specs += [block] * 4
    if low:
        block = pl.BlockSpec((1, LANES, features), lambda i, o: (*place(i, o), 0))
        specs += [block] * 2
    return specs


def expert_grads(order, first, last, total, x, o, gates, weights, kept):
    shared = total is None
    steps = last - first
    rows, features = x[0].shape
    aliased = len(kept)

    def fixed(*shape):
        return pl.BlockSpec(shape, lambda i, o: (0,) * len(shape))

    def stepped(*shape):
        return pl.BlockSpec((1, *shape), lambda i, o: (i, 0, 0))

    def placed(*shape):
        return pl.BlockSpec((1, *shape), lambda i, o: (i + first, 0, 0))

    specs = []
    for k in range(2):
        if shared:

            def picked(i, o, k=k):
                return 0, 2 * o[o.shape[0] - 1] + k

        else:

            def picked(i, o, k=k):
                return o[2 * (i + first) + k], o[o.shape[0] - 1]

        specs += expert_specs(features, picked, True, True)
    total = steps if shared else total
    return pl.pallas_call(
        functools.partial(expert_kernel, shared, aliased, first),
        grid_spec=pltpu.PrefetchScalarGridSpec(
            num_scalar_prefetch=1,
            grid=(steps,),
            in_specs=[fixed(rows, features)] * 4
            + [fixed(*gates.shape)]
            + specs
            + [pl.BlockSpec(memory_space=pl.ANY)] * aliased,
            out_specs=[stepped(2 * features, 3 * LANES)] * 2
            + [placed(rows, 4 * LANES), placed(rows, 2 * LANES)],
        ),
        out_shape=[jax.ShapeDtypeStruct((steps, 2 * features, 3 * LANES), BF16)] * 2
        + [
            jax.ShapeDtypeStruct((total, rows, 4 * LANES), BF16),
            jax.ShapeDtypeStruct((total, rows, 2 * LANES), BF16),
        ],
        input_output_aliases={18 + k: 2 + k for k in range(aliased)},
        compiler_params=params(40, "arbitrary"),
        cost_estimate=SMALL,
        name="expert_grads",
    )(order, *x, *o, gates, *weights, *weights, *kept)


def mix_back_kernel(group, order_ref, *refs):
    acts_ref, shared_ref = refs[0:2]
    count = 8 * group
    weights, shared = refs[2 : 2 + count], refs[2 + count : 10 + count]
    own_ref, other_ref, total_ref = refs[10 + count :]
    step = pl.program_id(0)

    def gathered(parts, half):
        picked = [p[0] for k in range(len(parts) // 4) for p in parts[4 * k + 2 * half :][:2]]
        return jnp.concatenate(picked, axis=1)

    acts = jnp.concatenate([acts_ref[g] for g in range(group)], axis=1)
    for half in range(2):
        term = dot_nt(acts, gathered(weights, half))

        @pl.when(step == 0)
        def _(half=half, term=term):
            total_ref[half] = term + dot_nt(shared_ref[0], gathered(shared, half))

        @pl.when(step > 0)
        def _(half=half, term=term):
            total_ref[half] += term

    @pl.when(step == pl.num_programs(0) - 1)
    def _():
        own_ref[...] = total_ref[0]
        other_ref[...] = total_ref[1].astype(BF16)


def mix_back(part, order, acts, shared_acts, weights, shared_weights):
    pairs, rows, width = acts.shape
    rows = rows // 2
    features = weights[0].shape[1]
    group = 2 if pairs % 2 == 0 else 1

    def spec(place):
        return pl.BlockSpec(
            (1, features, LANES), lambda i, o: (place(i, o)[0], 0, place(i, o)[1])
        )

    def routed(k):
        return spec(lambda i, o: (o[2 * group * i + k], o[o.shape[0] - 1]))

    def common(k):
        return spec(lambda i, o: (0, 2 * o[o.shape[0] - 1] + k))

    whole = pl.BlockSpec((rows, features), lambda i, o: (0, 0))
    return pl.pallas_call(
        functools.partial(mix_back_kernel, group),
        grid_spec=pltpu.PrefetchScalarGridSpec(
            num_scalar_prefetch=1,
            grid=(pairs // group,),
            in_specs=[
                pl.BlockSpec((group, rows, width), lambda i, o: (i, part, 0)),
                pl.BlockSpec((1, rows, width), lambda i, o: (0, part, 0)),
            ]
            + [routed(k) for k in range(2 * group) for _ in weights]
            + [common(k) for k in range(2) for _ in weights],
            out_specs=[whole, whole],
            scratch_shapes=[pltpu.VMEM((2, rows, features), F32)],
        ),
        out_shape=[
            jax.ShapeDtypeStruct((rows, features), F32),
            jax.ShapeDtypeStruct((rows, features), BF16),
        ],
        compiler_params=params(48, "arbitrary"),
        cost_estimate=SMALL,
        name="mix_back",
    )(order, acts, shared_acts, *weights * (2 * group), *shared_weights * 2)


def mix_out_kernel(group, order_ref, *refs):
    acts_ref, shared_ref = refs[0:2]
    count = 2 * group
    weights, shared = refs[2 : 2 + count], refs[2 + count : 4 + count]
    out_ref, total_ref = refs[4 + count :]
    step = pl.program_id(0)
    rows = out_ref.shape[0]
    tile = 512

    @pl.when(step == 0)
    def _():
        both = jnp.concatenate([w[0] for w in shared], axis=0)
        for t in range(rows // tile):
            at = slice(t * tile, (t + 1) * tile)
            total_ref[at, :] = dot(shared_ref[0, at, :], both)

    both = jnp.concatenate([w[0] for w in weights], axis=0)
    for t in range(rows // tile):
        at = slice(t * tile, (t + 1) * tile)
        acts = jnp.concatenate([acts_ref[g, at, :] for g in range(group)], axis=1)
        total_ref[at, :] += dot(acts, both)

    @pl.when(step == pl.num_programs(0) - 1)
    def _():
        out_ref[...] = total_ref[...].astype(out_ref.dtype)


def mix_out(dtype, order, acts, shared_acts, weights, shared_weights):
    pairs, rows, width = acts.shape
    features = weights.shape[2]
    group = 4 if pairs % 4 == 0 else 1

    def spec(place):
        return pl.BlockSpec((1, LANES, features), lambda i, o: (*place(i, o), 0))

    def routed(k):
        return spec(lambda i, o: (o[2 * group * i + k], o[o.shape[0] - 1]))

    def common(k):
        return spec(lambda i, o: (0, 2 * o[o.shape[0] - 1] + k))

    return pl.pallas_call(
        functools.partial(mix_out_kernel, group),
        grid_spec=pltpu.PrefetchScalarGridSpec(
            num_scalar_prefetch=1,
            grid=(pairs // group,),
            in_specs=[
                pl.BlockSpec((group, rows, width), lambda i, o: (i, 0, 0)),
                pl.BlockSpec((1, rows, width), lambda i, o: (0, 0, 0)),
            ]
            + [routed(k) for k in range(2 * group)]
            + [common(k) for k in range(2)],
            out_specs=pl.BlockSpec((rows, features), lambda i, o: (0, 0)),
            scratch_shapes=[pltpu.VMEM((rows, features), F32)],
        ),
        out_shape=jax.ShapeDtypeStruct((rows, features), dtype),
        compiler_params=params(48, "arbitrary"),
        cost_estimate=SMALL,
        name="mix_out",
    )(order, acts, shared_acts, *[weights] * (2 * group), *[shared_weights] * 2)


def chip_sum_kernel(own_ref, other_ref, total_ref, rounded_ref):
    total = own_ref[...] + other_ref[...].astype(F32)
    total_ref[...] = total
    rounded_ref[...] = total.astype(BF16)


def chip_sum(own, other):
    rows, features = own.shape
    spec = pl.BlockSpec((TOKEN_TILE, features), lambda i: (i, 0))
    return pl.pallas_call(
        chip_sum_kernel,
        grid=(rows // TOKEN_TILE,),
        out_shape=[
            jax.ShapeDtypeStruct((rows, features), F32),
            jax.ShapeDtypeStruct((rows, features), BF16),
        ],
        in_specs=[spec, spec],
        out_specs=[spec, spec],
        compiler_params=params(16, "arbitrary"),
        cost_estimate=SMALL,
        name="chip_sum",
    )(own, other)


def norm_back_kernel(tiles, place_ref, *refs):
    sums, came = refs[0:2], refs[2:4]
    hidden_ref, scale_ref, gains_ref = refs[4:7]
    grad_ref, product_ref, gain_ref = refs[7:10]
    step = pl.program_id(0)
    part = (step >= tiles // 2).astype(jnp.int32)
    terms = [sums[k][...] + came[k][...].astype(F32) for k in range(2)]
    grad = jnp.where(part == 0, terms[0], terms[1])
    hidden = hidden_ref[...]
    grad_ref[...] = grad
    product_ref[...] = jnp.sum(grad * gains_ref[1:2, :] * hidden, axis=1, keepdims=True)

    @pl.when(step == 0)
    def _():
        gain_ref[...] = jnp.zeros_like(gain_ref)

    @pl.when(part == place_ref[0])
    def _():
        gain_ref[...] += jnp.sum(grad * hidden * scale_ref[...], axis=0, keepdims=True)


def norm_back(place, sums, came, hidden, scale, gains):
    rows, features = hidden.shape
    tiles = rows // TOKEN_TILE
    halfwise = pl.BlockSpec((TOKEN_TILE, features), lambda i, p: (i % (tiles // 2), 0))
    return pl.pallas_call(
        functools.partial(norm_back_kernel, tiles),
        grid_spec=pltpu.PrefetchScalarGridSpec(
            num_scalar_prefetch=1,
            grid=(tiles,),
            in_specs=[halfwise] * 4 + [rowwise(features), rowwise(1), whole(2, features)],
            out_specs=[rowwise(features), rowwise(1), whole(1, features)],
        ),
        out_shape=[
            jax.ShapeDtypeStruct((rows, features), F32),
            jax.ShapeDtypeStruct((rows, 1), F32),
            jax.ShapeDtypeStruct((1, features), F32),
        ],
        compiler_params=params(48, "arbitrary"),
        cost_estimate=SMALL,
        name="norm_back",
    )(place, *sums, *came, hidden, scale, gains)


def norm_back_end_kernel(grad_ref, own_ref, other_ref, hidden_ref, scale_ref, gains_ref, out_grad_ref, hidden_grad_ref, rounded_ref):
    scale = scale_ref[...]
    mean = (own_ref[...] + other_ref[...]) * (1.0 / D)
    result = out_grad_ref[...].astype(F32) + scale * (grad_ref[...] * gains_ref[1:2, :])
    result = result - hidden_ref[...] * (scale * scale * scale * mean)
    hidden_grad_ref[...] = result
    rounded_ref[...] = result.astype(BF16)


def norm_back_end(grad, products, products_c, hidden, scale, gains, out_grad):
    rows, features = hidden.shape
    tile = pl.BlockSpec((TOKEN_TILE, features), lambda i: (i, 0))
    column = pl.BlockSpec((TOKEN_TILE, 1), lambda i: (i, 0))
    return pl.pallas_call(
        norm_back_end_kernel,
        grid=(rows // TOKEN_TILE,),
        in_specs=[tile, column, column, tile, column, pl.BlockSpec(gains.shape, lambda i: (0, 0)), tile],
        out_specs=[tile, tile],
        out_shape=[
            jax.ShapeDtypeStruct((rows, features), F32),
            jax.ShapeDtypeStruct((rows, features), BF16),
        ],
        compiler_params=params(48, "arbitrary"),
        cost_estimate=SMALL,
        name="norm_back_end",
    )(grad, products, products_c, hidden, scale, gains, out_grad)


def ring_of(size):
    return list(range(0, size, 2)) + list(range(1, size, 2))[::-1]


def unpack_kernel(aliased, plan_ref, *refs):
    chunks = refs[0:2]
    gate_ref, up_ref, down_ref = refs[2 + aliased : 5 + aliased]
    blocks = chunks[0].shape[1] // LANES

    def write(chunk_ref):
        gate_ref[0] = chunk_ref[0, :, 0:LANES].astype(F32)
        up_ref[0] = chunk_ref[0, :, LANES : 2 * LANES].astype(F32)
        for b in range(blocks):
            at = slice(b * LANES, (b + 1) * LANES)
            down_ref[0, :, at] = chunk_ref[0, at, 2 * LANES :].astype(F32)

    for k in range(2):
        pl.when(pl.program_id(1) == k)(lambda k=k: write(chunks[k]))


def unpack(plan, first, wave, chunks, shapes, outs):
    count, rows, width = chunks[0].shape
    chunk = pl.BlockSpec((1, rows, width), lambda i, d, n: (i, 0, 0))

    def place(i, d, n):
        block = n[n.shape[0] - 1]
        return n[first + 2 * i + d], 1 - block if wave else block

    def wide(i, d, n):
        expert, block = place(i, d, n)
        return (expert, 0, block)

    def low(i, d, n):
        expert, block = place(i, d, n)
        return (expert, block, 0)

    aliased = len(outs)
    return pl.pallas_call(
        functools.partial(unpack_kernel, aliased),
        grid_spec=pltpu.PrefetchScalarGridSpec(
            num_scalar_prefetch=1,
            grid=(count, 2),
            in_specs=[chunk, chunk] + [pl.BlockSpec(memory_space=pl.ANY)] * aliased,
            out_specs=[
                pl.BlockSpec((1, rows, LANES), wide),
                pl.BlockSpec((1, rows, LANES), wide),
                pl.BlockSpec((1, LANES, rows), low),
            ],
        ),
        out_shape=[jax.ShapeDtypeStruct(shape, F32) for shape in shapes],
        input_output_aliases={3 + k: k for k in range(aliased)},
        compiler_params=params(16, "arbitrary", "arbitrary"),
        cost_estimate=SMALL,
        name="unpack",
    )(plan, *chunks, *outs)


def ring_sum_kernel(came_ref, mine_ref, *outs):
    total = (came_ref[...].astype(F32) + mine_ref[...].astype(F32)).astype(BF16)
    if len(outs) == 1:
        outs[0][...] = total
    else:
        half = pl.program_id(1) // (pl.num_programs(1) // 2)
        for k, out_ref in enumerate(outs):

            @pl.when(half == k)
            def _(out_ref=out_ref):
                out_ref[...] = total


def ring_sum(came, mine, halved):
    count, rows, lanes = came.shape
    tiles = 4
    spec = pl.BlockSpec((1, rows // tiles, lanes), lambda i, j: (i, j, 0))

    def half(k):
        first = k * tiles // 2
        last = tiles // 2 - 1
        return pl.BlockSpec(
            (1, rows // tiles, lanes), lambda i, j: (i, jnp.clip(j - first, 0, last), 0)
        )

    shapes = [jax.ShapeDtypeStruct((count, rows // 2, lanes), BF16)] * 2
    return pl.pallas_call(
        ring_sum_kernel,
        grid=(count, tiles),
        in_specs=[spec, spec],
        out_specs=[half(0), half(1)] if halved else spec,
        out_shape=shapes if halved else jax.ShapeDtypeStruct(came.shape, BF16),
        compiler_params=params(16, "arbitrary", "arbitrary"),
        cost_estimate=SMALL,
        name="ring_sum",
    )(came, mine)


def late_chunk_kernel(came, plan_ref, pack_ref, *refs):
    values = pack_ref[:, 0]
    if came:
        values = (refs[0][...].astype(F32) + values.astype(F32)).astype(BF16)
    outs = refs[came:]
    if len(outs) == 1:
        outs[0][...] = values
    else:
        for k, out_ref in enumerate(outs):
            out_ref[...] = values[k]


def late_chunk(plan, at, pack, came, halved):
    halves, _, rows, lanes = pack.shape
    spec = pl.BlockSpec((halves, rows, lanes), lambda i, n: (0, 0, 0))
    half = pl.BlockSpec((rows, lanes), lambda i, n: (0, 0))
    halfs = [jax.ShapeDtypeStruct((rows, lanes), BF16)] * 2
    return pl.pallas_call(
        functools.partial(late_chunk_kernel, len(came)),
        grid_spec=pltpu.PrefetchScalarGridSpec(
            num_scalar_prefetch=1,
            grid=(1,),
            in_specs=[pl.BlockSpec((halves, 1, rows, lanes), lambda i, n: (0, n[at], 0, 0))]
            + [spec] * len(came),
            out_specs=[half] * 2 if halved else spec,
        ),
        out_shape=halfs if halved else jax.ShapeDtypeStruct((halves, rows, lanes), BF16),
        compiler_params=params(16, "arbitrary"),
        cost_estimate=SMALL,
        name="late_chunk",
    )(plan, pack, *came)


def unpack_late_kernel(first_step, steps, plan_ref, *refs):
    chunks = refs[0 : 2 * steps]
    sgate, sup, sdown, query, key, value, out, all_ref = refs[2 * steps :]
    rows, features = chunks[0].shape[0] // 2, all_ref.shape[2]
    for k in range(2):
        for step in range(steps):
            at = plan_ref[first_step + 2 * step + k] * rows
            for c in range(2):
                all_ref[k, c, pl.ds(pl.multiple_of(at, rows), rows), :] = chunks[
                    steps * k + step
                ][c * rows : (c + 1) * rows, :]
    flipped = plan_ref[plan_ref.shape[0] - 1] != 0
    for c in range(2):
        for b in range(14):
            lanes = slice(b % 7 * LANES, (b % 7 + 1) * LANES)
            first, second = all_ref[0, c, :, lanes], all_ref[1, c, :, lanes]
            if b >= 7:
                first, second = second, first
            block = jnp.where(flipped, second, first).astype(F32)
            if b < 6:
                at = slice((2 * c + b // 3) * LANES, (2 * c + b // 3 + 1) * LANES)
                if b % 3 < 2:
                    (sgate, sup)[b % 3][:, at] = block
                else:
                    for k in range(features // LANES):
                        here = slice(k * LANES, (k + 1) * LANES)
                        sdown[at, here] = block[here, :]
            elif b < 9:
                at = (GROUP_HEADS * c + b - 6) * LANES
                query[:, at : at + LANES] = block
            elif b < 11:
                (key, value)[b - 9][:, c * LANES : (c + 1) * LANES] = block
            else:
                at = (GROUP_HEADS * c + b - 11) * LANES
                out[at : at + LANES, :] = block.T


def unpack_late(plan, first_step, chunks, shapes):
    steps = len(chunks[0])
    rows, lanes = chunks[0][0].shape[0] // 2, chunks[0][0].shape[1]
    spec = pl.BlockSpec(memory_space=pltpu.VMEM)
    return pl.pallas_call(
        functools.partial(unpack_late_kernel, first_step, steps),
        in_specs=[pl.BlockSpec(memory_space=pltpu.SMEM)] + [spec] * (2 * steps),
        out_specs=[spec] * len(shapes),
        out_shape=[jax.ShapeDtypeStruct(shape, F32) for shape in shapes],
        scratch_shapes=[pltpu.VMEM((2, 2, steps * rows, lanes), BF16)],
        compiler_params=params(48),
        cost_estimate=SMALL,
        name="unpack_late",
    )(plan, *chunks[0], *chunks[1])


def plans(ring, each):
    size = len(ring)
    rows = []
    for member in range(size):
        place = ring.index(member)
        for col in range(2):
            chunks = []
            for step in range(2 * size - 1):
                for which in range(2):
                    sign = 1 if which == col else -1
                    chunks.append((place - sign * step) % size)
            experts = []
            for start in (0, size - 1):
                for step in range(start, start + size):
                    for k in range(each):
                        for which in range(2):
                            second = col if which == 0 else 1 - col
                            experts.append(2 * each * chunks[2 * step + which] + each * second + k)
            rows.append(experts + chunks + [col])
    return np.asarray(rows, np.int32)


LATE_ROUND = 0


def body(
    tokens_in,
    norm_gain_attn,
    w_query,
    w_key,
    w_value,
    w_out,
    norm_gain_ffn,
    w_gate,
    w_up,
    w_down,
    w_shared_gate,
    w_shared_up,
    w_shared_down,
    routes,
    gate_weights,
    seq_lengths,
    out_grad,
):
    row = lax.axis_index("row")
    col = lax.axis_index("col")
    dp = lax.axis_index("dp")
    dp_size = lax.axis_size("dp")
    local_rows, local_features = tokens_in.shape
    experts = w_gate.shape[0]
    group_width = GROUP_HEADS * DH
    col_ref = col.reshape(1)

    ring_size = min(8, dp_size)
    ring = ring_of(ring_size)
    starts = range(0, dp_size, ring_size)
    rights = [
        (g + ring[k], g + ring[(k + 1) % ring_size]) for g in starts for k in range(ring_size)
    ]
    lefts = [(b, a) for a, b in rights]
    routes_of = [
        [(2 * a, 2 * b) for a, b in ways[0]] + [(2 * a + 1, 2 * b + 1) for a, b in ways[1]]
        for ways in ((rights, lefts), (lefts, rights))
    ]
    experts_each = experts // (2 * ring_size)
    plan = jnp.asarray(plans(ring, experts_each))
    plan = lax.dynamic_slice(
        plan, (2 * (dp % ring_size) + col, jnp.int32(0)), (1, plan.shape[1])
    ).reshape(-1)

    def send(values, which):
        if ring_size == 1:
            return values
        return lax.ppermute(values, ("dp", "col"), routes_of[which])

    def chunk_at(step, which):
        return plan[2 * experts + 2 * step + which]

    def across_rings(values):
        if len(starts) == 1:
            return values
        peers = [[g + k for g in starts] for k in range(ring_size)]
        return lax.psum(values, "dp", axis_index_groups=peers)

    where = jnp.stack([row, seq_lengths[0], col])
    tokens_y = swap(tokens_in, "row")
    tokens_c = swap(tokens_in, "col")
    count = min(ring_size, 4)
    member = dp % count
    there, out_y = their_columns(
        jnp.stack([col, member]), w_query, w_key, w_value, w_out, count
    )
    gains = jnp.stack([norm_gain_attn, norm_gain_ffn])
    there = swap(there, "col")
    gains_c = swap(gains, "col")

    def project_half(own, other):
        return project(col_ref, own, other, gains, gains_c, w_query, w_key, w_value, there)

    near = project_half(tokens_in, tokens_c)
    gate_c = swap(w_gate, "col")
    out_y = swap(out_y, "row")
    tokens_y = after(tokens_y, near[2], out_y)
    tokens_yc = swap(tokens_y, "col")
    grad_y = swap(after(out_grad, tokens_y), "row")
    far = project_half(tokens_y, tokens_yc)
    shares = [out_y]
    for k in range(1, count):
        part = out_y if k < 3 else after(out_y, far[2])
        shares.append(lax.ppermute(part, "dp", [(m, m ^ k) for m in range(dp_size)]))
    where = after(where, grad_y, *shares)

    w_sgate, w_sup, w_sdown = w_shared_gate[None], w_shared_up[None], w_shared_down[None]
    up_c = swap(after(w_up, gate_c, tokens_yc), "col")

    attended = attend(where, near[2], far[2])
    attended_y = swap(attended, "row")
    attended_c = swap(attended, "col")
    out_c = swap(after(w_out, tokens_yc), "col")
    before = hidden_before(
        where,
        [tokens_in, tokens_c, tokens_y, tokens_yc],
        [attended, attended_c],
        w_out,
        out_c,
    )
    down_c = swap(after(w_down, tokens_yc), "col")
    attended_y = after(attended_y, before[0])
    out_y = join(member, *shares)
    out_yc = swap(out_y, "col")
    attended_yc = swap(attended_y, "col")
    grad_own = join(row, out_grad, grad_y)
    grad_other = swap(grad_own, "col")
    hidden, x_own, x_other, scale_ffn = hidden_after(
        where, before, [attended_y, attended_yc], out_y, out_yc, gains, gains_c
    )
    sgate_c, sup_c, sdown_c = (
        swap(after(w, attended_yc), "col") for w in (w_sgate, w_sup, w_sdown)
    )

    choices = jnp.arange(experts, dtype=jnp.int32)[:, None]
    dense = sum(
        jnp.where(routes[:, k][None, :] == choices, gate_weights[:, k][None, :], 0.0)
        for k in range(routes.shape[1])
    )
    gates = []
    for _ in range(3):
        gates.append(lax.reduce_precision(dense, 8, 7))
        dense = dense - gates[-1]
    gates = jnp.concatenate(gates, axis=0).astype(BF16)

    each = experts_each
    order = plan
    pairs_total = experts // 2
    routed = [w_gate, w_up, gate_c, up_c, w_down, down_c]
    shared = [w_sgate, w_sup, sgate_c, sup_c, w_sdown, sdown_c]

    def run(first, last, order, kept):
        return expert_grads(
            order,
            first,
            last,
            pairs_total,
            [x_own, x_other],
            [grad_own, grad_other],
            gates,
            routed,
            kept,
        )

    first = run(0, each, order, ())
    kept = first[2:]
    sums = [first[0], first[1]]
    runs = {}
    mixed = {}

    def work_experts(first, last):
        def work(order):
            nonlocal kept
            result = run(first, last, order, tuple(kept))
            kept = result[2:]
            runs[first] = result[0:2]
            return kept[0]

        return work

    def work_shared(order):
        runs["shared"] = expert_grads(
            order, 0, 1, None, [x_own, x_other], [grad_own, grad_other], gates, shared, ()
        )
        return runs["shared"][2]

    def work_back(part):
        def work(order):
            mixed[True, part] = mix_back(
                part, order, kept[0], runs["shared"][2], routed[:4], shared[:4]
            )
            return mixed[True, part][1]

        return work

    def work_out(half):
        def work(order):
            mixed[False, half] = mix_out(
                BF16 if half else F32,
                order,
                kept[1],
                runs["shared"][3],
                routed[4 + half],
                shared[4 + half],
            )
            return mixed[False, half]

        return work

    start = row * local_rows

    def my_rows(values):
        return lax.dynamic_slice_in_dim(values, start, local_rows, axis=0)

    def their_rows(values):
        return lax.dynamic_slice_in_dim(values, local_rows - start, local_rows, axis=0)

    normed = {}

    def row_sums(part):
        own, other = mixed[True, part]
        both = chip_sum(own, swap(other, "col"))
        return both, swap(both[1], "row")

    def work_hidden(order):
        both, came = zip(*(normed["sums"][part] for part in range(2)), strict=True)
        grads, products, normed["gain"] = norm_back(
            where, [b[0] for b in both], [after(c, order) for c in came], hidden, scale_ffn, gains
        )
        products_c = swap(products, "col")
        normed["hidden"], normed["grad"] = norm_back_end(
            grads, products, products_c, hidden, scale_ffn, gains, grad_own
        )
        normed["grad_c"] = swap(normed["grad"], "col")
        return normed["grad"]

    def work_attend(order):
        normed["qkv"] = attend_back(
            after(where, order), near[2], far[2], normed["grad"], normed["grad_c"], w_out, out_c
        )
        return normed["qkv"]

    def work_late(order):
        normed["packs"] = late_grads(
            after(where, order),
            near[0:2],
            far[0:2],
            normed["qkv"],
            attended,
            normed["grad"],
            normed["grad_c"],
            runs["shared"][0:2],
        )
        return normed["packs"][0]

    def with_sums(part):
        def work(order):
            result = work_back(part)(order)
            normed.setdefault("sums", {})[part] = row_sums(part)
            return result

        return work

    tasks = [work_experts(at, at + each) for at in range(each, pairs_total, each)]
    tasks += [work_shared, with_sums(0), with_sums(1), work_out(1), work_out(0)]
    ends = [work_hidden, work_attend, work_late]
    tasks += [None] * (2 * ring_size - 1 - len(tasks) - len(ends)) + ends
    got = [None, None]
    if ring_size > 1:
        got[0] = send(sums[0], 0)
        tasks.pop(0)(after(order, *sums))
        got[1] = send(after(sums[1], kept[0]), 1)
    for s in range(1, ring_size):
        for k in range(2):
            last = sums
            task = tasks.pop(0) if tasks else None
            if task:
                last = [task(after(order, *last))]
            sums[k] = ring_sum(after(got[k], *last), runs[each * s][k], s + 1 == ring_size)
            if s + 1 < ring_size:
                got[k] = send(sums[k], k)
            else:
                sums[k], got[k] = sums[k]
    for task in tasks:
        if task:
            task(after(order, *sums))
    if ring_size == 1:
        got = [total[:, local_features:] for total in sums]
        sums = [total[:, :local_features] for total in sums]
    waves = [[across_rings(total) for total in sums]]
    crossed = [swap(across_rings(total), "col") for total in got]
    waves.append([crossed[1], crossed[0]])

    hidden_grad, attn_grad, attn_grad_c = normed["hidden"], normed["grad"], normed["grad_c"]
    gain_ffn_part, qkv_grad = normed["gain"], normed["qkv"]
    packs = normed["packs"]

    packs = [
        pack.reshape(2, ring_size, local_features // ring_size, pack.shape[2]) for pack in packs
    ]
    chunks_first = 2 * experts
    late_total = 2 * (ring_size - 1)
    late = [
        late_chunk(plan, chunks_first + k, packs[k], (), late_total == 0) for k in range(2)
    ]
    late_out = [[], []]
    late_done = 0

    def late_turn():
        owns = [across_rings(values[0]) for values in late]
        others = [swap(across_rings(values[1]), "col") for values in late]
        for k in range(2):
            late[k] = join(col, owns[k], others[1 - k])
            late_out[k].append(late[k])

    def late_finish(k, values):
        if late_done < ring_size:
            at = chunks_first + 2 * late_done + k
            late[k] = late_chunk(plan, at, packs[k], (values,), late_done == ring_size - 1)
        else:
            late[k] = values
            late_out[k].append(values)

    shapes = [w_gate.shape, w_up.shape, w_down.shape]
    placed = ()

    def place_chunks(wave, step, chunks, placed):
        return unpack(plan, experts + 2 * each * step, wave, chunks, shapes, placed)

    if late_total == 0:
        late_turn()
    rounds = [(wave, step) for wave in range(2) for step in range(ring_size - 1)]
    late_got = None
    last = []
    for number, (wave, step) in enumerate(rounds):
        if step == 0:
            came = list(got) if number else None
            got = list(waves[wave])
        late_done += late_got is not None
        chunks = [None, None]
        for k in range(2):
            chunks[k] = after(got[k], *last) if last else got[k]
            got[k] = send(chunks[k], k)
            last = [chunks[k]]
            if late_got is not None:
                late_finish(k, after(late_got[k], *last))
                last = list(late[k]) if late_done == ring_size - 1 else [late[k]]
        if late_got is not None and late_done == ring_size - 1:
            late_turn()
        late_got = None
        if number >= LATE_ROUND and late_done < late_total:
            late_got = [send(late[k], k) for k in range(2)]
        if step == 0 and number:
            placed = place_chunks(0, ring_size - 1, came, placed)
        placed = place_chunks(wave, step, chunks, placed)
        last = placed[0:1]
        if number == LATE_ROUND + 3:
            qkv_grad = after(qkv_grad, *last)
    if rounds:
        placed = place_chunks(1, ring_size - 1, [after(got[k], *last) for k in range(2)], placed)
        last = placed[0:1]
    while late_got is not None:
        late_done += 1
        for k in range(2):
            late_finish(k, after(late_got[k], *last))
        if late_done == ring_size - 1:
            late_turn()
        late_got = [send(late[k], k) for k in range(2)] if late_done < late_total else None
    if not rounds:
        for wave in range(2):
            placed = place_chunks(wave, 0, waves[wave], placed)
    gate_grad, up_grad, down_grad = placed
    shapes = [w.shape for w in (w_shared_gate, w_shared_up, w_shared_down)]
    shapes += [w.shape for w in (w_query, w_key, w_value, w_out)]
    finals = unpack_late(plan, chunks_first + late_total, late_out, shapes)
    shared_gate_grad, shared_up_grad, shared_down_grad = finals[0:3]
    query_grad, key_grad, value_grad, out_proj_grad = finals[3:7]

    ffn_sum = mixed[False, 0] + swap(mixed[False, 1], "col").astype(F32)
    ffn_rows = my_rows(ffn_sum) + swap(their_rows(ffn_sum).astype(BF16), "row").astype(F32)
    block_out = (my_rows(hidden) + ffn_rows).astype(BF16)

    here = jnp.concatenate(
        [halves(w, 1, col)[0] for w in (w_query, w_key, w_value)], axis=1
    )
    tokens_back = dot_nt(qkv_grad, here) + swap(
        dot_nt(qkv_grad, there).astype(BF16), "col"
    ).astype(F32)
    tokens_back = my_rows(tokens_back) + swap(
        their_rows(tokens_back).astype(BF16), "row"
    ).astype(F32)
    scale_attn = near[3]
    tokens_f32 = tokens_in.astype(F32)
    gain_attn_part = jnp.sum(tokens_back * tokens_f32 * scale_attn, axis=0)
    scaled = tokens_back * norm_gain_attn
    products = jnp.sum(scaled * tokens_f32, axis=1, keepdims=True)
    mean = (products + swap(products, "col")) / D
    tokens_grad = (
        my_rows(hidden_grad) + scale_attn * scaled - tokens_f32 * scale_attn**3 * mean
    ).astype(BF16)

    gain_parts = jnp.concatenate([gain_attn_part[None], gain_ffn_part], axis=0)
    bit = 1
    while bit < ring_size:
        pairs = [(g + k, g + (k ^ bit)) for g in starts for k in range(ring_size)]
        gain_parts = gain_parts + lax.ppermute(gain_parts, "dp", pairs)
        bit *= 2
    gain_parts = across_rings(gain_parts + swap(gain_parts, "row"))

    return (
        block_out,
        tokens_grad,
        gain_parts[0],
        query_grad,
        key_grad,
        value_grad,
        out_proj_grad,
        gain_parts[1],
        gate_grad,
        up_grad,
        down_grad,
        shared_gate_grad,
        shared_up_grad,
        shared_down_grad,
    )


def solution(mesh):
    in_specs = (
        P(("dp", "row"), "col"),
        P("col"),
        P("col", "row"),
        P("col", "row"),
        P("col", "row"),
        P("row", "col"),
        P("col"),
        P(None, "col", "row"),
        P(None, "col", "row"),
        P(None, "row", "col"),
        P("col", "row"),
        P("col", "row"),
        P("row", "col"),
        P("dp", None),
        P("dp", None),
        P("dp"),
        P(("dp", "row"), "col"),
    )
    out_specs = (
        P(("dp", "row"), "col"),
        P(("dp", "row"), "col"),
        P("col"),
        P("col", "row"),
        P("col", "row"),
        P("col", "row"),
        P("row", "col"),
        P("col"),
        P(None, "col", "row"),
        P(None, "col", "row"),
        P(None, "row", "col"),
        P("col", "row"),
        P("col", "row"),
        P("row", "col"),
    )
    return jax.shard_map(body, mesh=mesh, in_specs=in_specs, out_specs=out_specs, check_vma=False)
```

```python
import functools

import jax
import jax.numpy as jnp
import numpy as np
from jax import lax
from jax.experimental import pallas as pl
from jax.experimental.pallas import tpu as pltpu
from jax.sharding import PartitionSpec as P

D = 1536
HQ = 12
HK = 4
DH = 128
GROUP_HEADS = HQ // HK
LANES = 128

EPSILON = 1e-05
F32 = jnp.float32
BF16 = jnp.bfloat16
MIB = 1024 * 1024
SMALL = pl.CostEstimate(flops=0, bytes_accessed=0, transcendentals=0)


def params(mib, *semantics):
    return pltpu.CompilerParams(
        dimension_semantics=semantics or None, vmem_limit_bytes=mib * MIB
    )


def dot(left, right):
    return jnp.dot(left, right, preferred_element_type=F32)


def dot_nt(left, right):
    return lax.dot_general(left, right, (((1,), (1,)), ((), ())), preferred_element_type=F32)


def dot_tn(left, right):
    return lax.dot_general(left, right, (((0,), (0,)), ((), ())), preferred_element_type=F32)


def after(values, *others):
    return lax.optimization_barrier((values, *others))[0]


def swap(values, axis):
    return lax.ppermute(values, axis, [(0, 1), (1, 0)])


def halves(values, axis, mine):
    size = values.shape[axis] // 2
    low = lax.slice_in_dim(values, 0, size, axis=axis)
    high = lax.slice_in_dim(values, size, 2 * size, axis=axis)
    return jnp.where(mine == 0, low, high), jnp.where(mine == 0, high, low)


def in_order(own, other, mine, axis):
    return jnp.concatenate(
        [jnp.where(mine == 0, own, other), jnp.where(mine == 0, other, own)], axis=axis
    )


def gather_rows(place_ref, own_ref, other_ref, all_ref):
    row = place_ref[0]
    rows = own_ref.shape[0]
    all_ref[pl.ds(pl.multiple_of(row * rows, rows), rows), :] = own_ref[...]
    all_ref[pl.ds(pl.multiple_of((1 - row) * rows, rows), rows), :] = other_ref[...]


def head_rows(ref, first, block):
    return jnp.concatenate(
        [ref[first : first + block, h * DH : (h + 1) * DH] for h in range(GROUP_HEADS)], axis=0
    )


def key_probs(query, key, first, length):
    block, keys = query.shape[0] // GROUP_HEADS, key.shape[0]
    scores = dot_nt(query, key) * DH ** (-0.5)
    shape = (block, keys)
    query_at = lax.broadcasted_iota(jnp.int32, shape, 0) + first
    key_at = lax.broadcasted_iota(jnp.int32, shape, 1)
    allowed = (key_at <= query_at) & (key_at < length)
    allowed = jnp.concatenate([allowed] * GROUP_HEADS, axis=0)
    scores = jnp.where(allowed, scores, -1e30)
    weights = jnp.exp(scores - jnp.max(scores, axis=1, keepdims=True))
    return weights * (1.0 / jnp.sum(weights, axis=1, keepdims=True))


def attend_kernel(place_ref, own_ref, other_ref, out_ref, all_ref):
    gather_rows(place_ref, own_ref, other_ref, all_ref)
    rows = own_ref.shape[0]
    block = 256
    width = GROUP_HEADS * DH
    for at in range(2 * rows // block):
        first, keys = at * block, (at + 1) * block
        query = head_rows(all_ref, first, block)
        key = all_ref[0:keys, width : width + DH]
        value = all_ref[0:keys, width + DH : width + 2 * DH]
        probs = key_probs(query, key, first, place_ref[1])
        result = dot(probs.astype(BF16), value).astype(BF16)
        for h in range(GROUP_HEADS):
            out_ref[first : first + block, h * DH : (h + 1) * DH] = result[
                h * block : (h + 1) * block
            ]


def attend(place, own, other):
    rows, width = own.shape
    spec = pl.BlockSpec(memory_space=pltpu.VMEM)
    return pl.pallas_call(
        attend_kernel,
        out_shape=jax.ShapeDtypeStruct((2 * rows, GROUP_HEADS * DH), BF16),
        in_specs=[pl.BlockSpec(memory_space=pltpu.SMEM), spec, spec],
        out_specs=spec,
        scratch_shapes=[pltpu.VMEM((2 * rows, width), BF16)],
        compiler_params=params(32),
        cost_estimate=SMALL,
        name="attend",
    )(place, own, other)


def attend_back_kernel(
    place_ref, own_ref, other_ref, grad_ref, grad_c_ref, out_ref, out_c_ref, result_ref, all_ref, total_ref
):
    gather_rows(place_ref, own_ref, other_ref, all_ref)
    rows = own_ref.shape[0]
    block = 256
    width = GROUP_HEADS * DH
    group = pl.ds(pl.multiple_of(place_ref[2] * width, width), width)
    blocks = 2 * rows // block
    for at in reversed(range(blocks)):
        first, keys = at * block, (at + 1) * block
        query = head_rows(all_ref, first, block)
        key = all_ref[0:keys, width : width + DH]
        value = all_ref[0:keys, width + DH : width + 2 * DH]
        probs = key_probs(query, key, first, place_ref[1])
        grad = dot_nt(grad_ref[first:keys, :], out_ref[group, :])
        grad = (grad + dot_nt(grad_c_ref[first:keys, :], out_c_ref[group, :])).astype(BF16)
        grad = jnp.concatenate(
            [grad[:, h * DH : (h + 1) * DH] for h in range(GROUP_HEADS)], axis=0
        )
        probs_grad = dot_nt(grad, value)
        carried = jnp.sum(probs * probs_grad, axis=1, keepdims=True)
        score_grad = (probs * (probs_grad - carried)).astype(BF16)
        query_back = (dot(score_grad, key) * DH ** (-0.5)).astype(BF16)
        for h in range(GROUP_HEADS):
            result_ref[first:keys, h * DH : (h + 1) * DH] = query_back[
                h * block : (h + 1) * block
            ]
        key_back = dot_tn(score_grad, query)
        value_back = dot_tn(probs.astype(BF16), grad)
        if at == blocks - 1:
            total_ref[:, 0:DH] = key_back
            total_ref[:, DH:] = value_back
        else:
            total_ref[0:keys, 0:DH] += key_back
            total_ref[0:keys, DH:] += value_back
    result_ref[:, width : width + DH] = (total_ref[:, 0:DH] * DH ** (-0.5)).astype(BF16)
    result_ref[:, width + DH :] = total_ref[:, DH:].astype(BF16)


def attend_back(place, own, other, grad, grad_c, w_out, out_c):
    rows, width = own.shape
    spec = pl.BlockSpec(memory_space=pltpu.VMEM)
    return pl.pallas_call(
        attend_back_kernel,
        out_shape=jax.ShapeDtypeStruct((2 * rows, width), BF16),
        in_specs=[pl.BlockSpec(memory_space=pltpu.SMEM)] + [spec] * 6,
        out_specs=spec,
        scratch_shapes=[
            pltpu.VMEM((2 * rows, width), BF16),
            pltpu.VMEM((2 * rows, 2 * DH), F32),
        ],
        compiler_params=params(60),
        cost_estimate=SMALL,
        name="attend_back",
    )(place, own, other, grad, grad_c, w_out, out_c)


def late_kernel(place_ref, *refs):
    near, near_c, far, far_c, qkv_ref, attended_ref, grad_ref, grad_c_ref = refs[0:8]
    shared = refs[8:10]
    outs = refs[10:12]
    rows, features = near.shape
    own_rows = pl.ds(pl.multiple_of(place_ref[0] * rows, rows), rows)
    far_rows = pl.ds(pl.multiple_of((1 - place_ref[0]) * rows, rows), rows)
    split = 7 * LANES

    def store(h, at, values):
        values = values.astype(BF16)
        for part in range(2):
            low, high = max(at, part * split), min(at + values.shape[1], (part + 1) * split)
            if low < high:
                piece = values[:, low - at : high - at]
                to = slice(low - part * split, high - part * split)

                @pl.when(place_ref[2] == 0)
                def _(part=part, to=to, piece=piece):
                    outs[part][h, :, to] = piece

                @pl.when(place_ref[2] != 0)
                def _(part=part, to=to, piece=piece):
                    outs[1 - part][h, :, to] = piece

    for h, (x, y, grad) in enumerate(((near, far, grad_ref), (near_c, far_c, grad_c_ref))):
        for k in range(2):
            store(h, 3 * LANES * k, shared[k][0, h * features : (h + 1) * features, :])
        project = dot_tn(x[...], qkv_ref[own_rows, :]) + dot_tn(y[...], qkv_ref[far_rows, :])
        store(h, 6 * LANES, project)
        store(h, 11 * LANES, dot_tn(grad[...], attended_ref[...]))


def late_grads(place, near, far, qkv_grad, attended, grad, grad_c, shared):
    features = near[0].shape[1]
    spec = pl.BlockSpec(memory_space=pltpu.VMEM)
    return pl.pallas_call(
        late_kernel,
        out_shape=[jax.ShapeDtypeStruct((2, features, 7 * LANES), BF16)] * 2,
        in_specs=[pl.BlockSpec(memory_space=pltpu.SMEM)] + [spec] * 10,
        out_specs=[spec] * 2,
        compiler_params=params(60),
        cost_estimate=SMALL,
        name="late_grads",
    )(place, *near, *far, qkv_grad, attended, grad, grad_c, *shared)


def columns_kernel(
    place_ref, query_ref, key_ref, value_ref, w_out_ref, out_ref, share_ref
):
    share_ref[...] = w_out_ref[...]
    width = GROUP_HEADS * DH
    out_ref[:, 0:width] = query_ref[...]
    out_ref[:, width : width + DH] = key_ref[...]
    out_ref[:, width + DH :] = value_ref[...]


def their_columns(place, w_query, w_key, w_value, w_out, shares):
    rows = w_query.shape[0]
    width = GROUP_HEADS * DH + 2 * DH

    def theirs(width):
        return pl.BlockSpec((rows, width), lambda i, c: (0, 1 - c[0]))

    return pl.pallas_call(
        columns_kernel,
        grid_spec=pltpu.PrefetchScalarGridSpec(
            num_scalar_prefetch=1,
            grid=(1,),
            in_specs=[theirs(GROUP_HEADS * DH), theirs(DH), theirs(DH)]
            + [pl.BlockSpec((rows // shares, rows), lambda i, c: (c[1], 0))],
            out_specs=[
                pl.BlockSpec((rows, width), lambda i, c: (0, 0)),
                pl.BlockSpec((rows // shares, rows), lambda i, c: (0, 0)),
            ],
        ),
        out_shape=[
            jax.ShapeDtypeStruct((rows, width), BF16),
            jax.ShapeDtypeStruct((rows // shares, rows), BF16),
        ],
        compiler_params=params(60, "arbitrary"),
        cost_estimate=SMALL,
        name="their_columns",
    )(place, w_query, w_key, w_value, w_out)


def join_kernel(mine_ref, *refs):
    *parts, out_ref = refs
    rows = parts[0].shape[0]
    for k, part in enumerate(parts):
        at = jnp.bitwise_xor(mine_ref[0], k)
        out_ref[pl.ds(pl.multiple_of(at * rows, rows), rows), :] = part[...]


def join(mine, *parts):
    rows, width = parts[0].shape
    spec = pl.BlockSpec(memory_space=pltpu.VMEM)
    return pl.pallas_call(
        join_kernel,
        out_shape=jax.ShapeDtypeStruct((len(parts) * rows, width), parts[0].dtype),
        in_specs=[pl.BlockSpec(memory_space=pltpu.SMEM)] + [spec] * len(parts),
        out_specs=spec,
        compiler_params=params(16),
        cost_estimate=SMALL,
        name="join",
    )(mine.reshape(1), *parts)


def project_kernel(col_ref, own_ref, other_ref, gains_ref, gains_c_ref, query_ref, key_ref, value_ref, there_ref, x_own_ref, x_other_ref, qkv_ref, scale_ref):
    own = own_ref[...].astype(F32)
    other = other_ref[...].astype(F32)
    total = jnp.sum(own * own, axis=1, keepdims=True)
    total = total + jnp.sum(other * other, axis=1, keepdims=True)
    scale = lax.rsqrt(total / D + EPSILON)
    own = (own * scale * gains_ref[0:1, :]).astype(BF16)
    other = (other * scale * gains_c_ref[0:1, :]).astype(BF16)
    x_own_ref[...] = own
    x_other_ref[...] = other
    scale_ref[...] = scale
    here = jnp.concatenate([query_ref[...], key_ref[...], value_ref[...]], axis=1)
    qkv_ref[...] = (dot(own, here) + dot(other, there_ref[...])).astype(BF16)


def project(col, own, other, gains, gains_c, w_query, w_key, w_value, there):
    rows, features = own.shape
    width = there.shape[1]
    group = GROUP_HEADS * DH
    tile = rows // 2

    def whole(*shape):
        return pl.BlockSpec(shape, lambda i, c: (0,) * len(shape))

    def mine(width):
        return pl.BlockSpec((features, width), lambda i, c: (0, c[0]))

    def rowwise(width):
        return pl.BlockSpec((tile, width), lambda i, c: (i, 0))

    return pl.pallas_call(
        project_kernel,
        grid_spec=pltpu.PrefetchScalarGridSpec(
            num_scalar_prefetch=1,
            grid=(rows // tile,),
            in_specs=[
                rowwise(features),
                rowwise(features),
                whole(2, features),
                whole(2, features),
                mine(group),
                mine(DH),
                mine(DH),
                whole(features, width),
            ],
            out_specs=[rowwise(features), rowwise(features), rowwise(width), rowwise(1)],
        ),
        out_shape=[
            jax.ShapeDtypeStruct((rows, features), BF16),
            jax.ShapeDtypeStruct((rows, features), BF16),
            jax.ShapeDtypeStruct((rows, width), BF16),
            jax.ShapeDtypeStruct((rows, 1), F32),
        ],
        compiler_params=params(60, "arbitrary"),
        cost_estimate=SMALL,
        name="project",
    )(col, own, other, gains, gains_c, w_query, w_key, w_value, there)


def head_pair(col_ref, own, other):
    first, second = own[...], other[...]
    flipped = col_ref != 0
    return jnp.concatenate(
        [jnp.where(flipped, second, first), jnp.where(flipped, first, second)], axis=1
    )


def before_kernel(tiles, place_ref, *refs):
    near, near_c, far, far_c, attended, attended_c, here, there, own_ref, other_ref = refs
    is_near = (pl.program_id(0) >= tiles // 2).astype(jnp.int32) == place_ref[0]
    heads = head_pair(place_ref[2], attended, attended_c)
    own = jnp.where(is_near, near[...], far[...]).astype(F32)
    other = jnp.where(is_near, near_c[...], far_c[...]).astype(F32)
    own_ref[...] = own + dot(heads, here[...])
    other_ref[...] = other + dot(heads, there[...])


def after_kernel(place_ref, *refs):
    own_ref, other_ref, attended, attended_c, here, there, gains_ref, gains_c_ref = refs[0:8]
    hidden_ref, x_own_ref, x_other_ref, scale_ref = refs[8:12]
    heads = head_pair(place_ref[2], attended, attended_c)
    own = own_ref[...] + dot(heads, here[...])
    other = other_ref[...] + dot(heads, there[...])
    total = jnp.sum(own * own, axis=1, keepdims=True)
    total = total + jnp.sum(other * other, axis=1, keepdims=True)
    scale = lax.rsqrt(total / D + EPSILON)
    hidden_ref[...] = own
    scale_ref[...] = scale
    x_own_ref[...] = (own * scale * gains_ref[1:2, :]).astype(BF16)
    x_other_ref[...] = (other * scale * gains_c_ref[1:2, :]).astype(BF16)


TOKEN_TILE = 256


def rowwise(width):
    return pl.BlockSpec((TOKEN_TILE, width), lambda i, p: (i, 0))


def whole(*shape):
    return pl.BlockSpec(shape, lambda i, p: (0,) * len(shape))


def hidden_before(place, tokens, attended, here, there):
    half, features = tokens[0].shape
    rows, heads = attended[0].shape
    tiles = rows // TOKEN_TILE
    per_half = half // TOKEN_TILE
    halfwise = pl.BlockSpec((TOKEN_TILE, features), lambda i, p: (i % per_half, 0))
    return pl.pallas_call(
        functools.partial(before_kernel, tiles),
        grid_spec=pltpu.PrefetchScalarGridSpec(
            num_scalar_prefetch=1,
            grid=(tiles,),
            in_specs=[halfwise] * 4 + [rowwise(heads)] * 2 + [whole(2 * heads, features)] * 2,
            out_specs=[rowwise(features)] * 2,
        ),
        out_shape=[jax.ShapeDtypeStruct((rows, features), F32)] * 2,
        compiler_params=params(56, "arbitrary"),
        cost_estimate=pl.CostEstimate(
            flops=8 * rows * features * heads,
            bytes_accessed=16 * rows * features,
            transcendentals=0,
        ),
        name="hidden_before",
    )(place, *tokens, *attended, here, there)


def hidden_after(place, before, attended, here, there, gains, gains_c):
    rows, features = before[0].shape
    heads = attended[0].shape[1]
    return pl.pallas_call(
        after_kernel,
        grid_spec=pltpu.PrefetchScalarGridSpec(
            num_scalar_prefetch=1,
            grid=(rows // TOKEN_TILE,),
            in_specs=[rowwise(features)] * 2
            + [rowwise(heads)] * 2
            + [whole(2 * heads, features)] * 2
            + [whole(2, features)] * 2,
            out_specs=[rowwise(features)] * 3 + [rowwise(1)],
        ),
        out_shape=[
            jax.ShapeDtypeStruct((rows, features), F32),
            jax.ShapeDtypeStruct((rows, features), BF16),
            jax.ShapeDtypeStruct((rows, features), BF16),
            jax.ShapeDtypeStruct((rows, 1), F32),
        ],
        compiler_params=params(56, "arbitrary"),
        cost_estimate=SMALL,
        name="hidden_after",
    )(place, *before, *attended, here, there, gains, gains_c)


def expert_kernel(shared, aliased, first, order_ref, *refs):
    x_own, x_other, o_own, o_other, gates_ref = refs[0:5]
    weights = refs[5:17]
    grads = refs[17 + aliased : 19 + aliased]
    pair_ref, inner_ref = refs[19 + aliased : 21 + aliased]
    step = pl.program_id(0) + first
    rows, features = x_own.shape
    tile = 512
    up_own = jnp.concatenate([weights[k][0] for k in (0, 1, 6, 7)], axis=1)
    up_other = jnp.concatenate([weights[k][0] for k in (2, 3, 8, 9)], axis=1)
    down_own = jnp.concatenate([weights[k][0] for k in (4, 10)], axis=0)
    down_other = jnp.concatenate([weights[k][0] for k in (5, 11)], axis=0)

    def token_tile(t, carry):
        at = pl.ds(pl.multiple_of(t * tile, tile), tile)
        pre = dot(x_own[at, :], up_own) + dot(x_other[at, :], up_other)
        back = dot_nt(o_own[at, :], down_own) + dot_nt(o_other[at, :], down_other)
        for k in range(2):
            pre_gate = pre[:, 2 * k * LANES : (2 * k + 1) * LANES]
            pre_up = pre[:, (2 * k + 1) * LANES : (2 * k + 2) * LANES]
            inner_grad = back[:, k * LANES : (k + 1) * LANES]
            sigmoid = 1.0 / (1.0 + jnp.exp(-pre_gate))
            silu = pre_gate * sigmoid
            inner = silu * pre_up
            if not shared:
                shape = (gates_ref.shape[0], LANES)
                expert = lax.broadcasted_iota(jnp.int32, shape, 0) % (gates_ref.shape[0] // 3)
                chosen = (expert == order_ref[2 * step + k]).astype(F32).astype(BF16)
                gate = dot_tn(gates_ref[:, at], chosen)
                inner = gate * inner
                inner_grad = gate * inner_grad
            gate_grad = inner_grad * pre_up * (sigmoid * (1.0 + pre_gate * (1.0 - sigmoid)))
            inner_ref[0, at, k * LANES : (k + 1) * LANES] = inner.astype(BF16)
            pair_ref[0, at, 2 * k * LANES : (2 * k + 1) * LANES] = gate_grad.astype(BF16)
            pair_ref[0, at, (2 * k + 1) * LANES : (2 * k + 2) * LANES] = (
                inner_grad * silu
            ).astype(BF16)
        return carry

    lax.fori_loop(0, rows // tile, token_tile, 0)
    pairs = pair_ref[0]
    for h, x in enumerate((x_own, x_other)):
        wide = dot_tn(x[...], pairs).astype(BF16)
        for k in range(2):
            grads[k][0, h * features : (h + 1) * features, 0 : 2 * LANES] = wide[
                :, 2 * k * LANES : (2 * k + 2) * LANES
            ]
    inner = inner_ref[0]
    tile = 256
    for h, o in enumerate((o_own, o_other)):
        for j in range(features // tile):
            low = dot_tn(inner, o[:, j * tile : (j + 1) * tile]).astype(BF16)
            for k in range(2):
                for b in range(tile // LANES):
                    at = h * features + j * tile + b * LANES
                    grads[k][0, at : at + LANES, 2 * LANES :] = low[
                        k * LANES : (k + 1) * LANES, b * LANES : (b + 1) * LANES
                    ]


def expert_specs(features, place, wide, low):
    specs = []
    if wide:
        block = pl.BlockSpec((1, features, LANES), lambda i, o: (place(i, o)[0], 0, place(i, o)[1]))
        specs += [block] * 4
    if low:
        block = pl.BlockSpec((1, LANES, features), lambda i, o: (*place(i, o), 0))
        specs += [block] * 2
    return specs


def expert_grads(order, first, last, total, x, o, gates, weights, kept):
    shared = total is None
    steps = last - first
    rows, features = x[0].shape
    aliased = len(kept)

    def fixed(*shape):
        return pl.BlockSpec(shape, lambda i, o: (0,) * len(shape))

    def stepped(*shape):
        return pl.BlockSpec((1, *shape), lambda i, o: (i, 0, 0))

    def placed(*shape):
        return pl.BlockSpec((1, *shape), lambda i, o: (i + first, 0, 0))

    specs = []
    for k in range(2):
        if shared:

            def picked(i, o, k=k):
                return 0, 2 * o[o.shape[0] - 1] + k

        else:

            def picked(i, o, k=k):
                return o[2 * (i + first) + k], o[o.shape[0] - 1]

        specs += expert_specs(features, picked, True, True)
    total = steps if shared else total
    return pl.pallas_call(
        functools.partial(expert_kernel, shared, aliased, first),
        grid_spec=pltpu.PrefetchScalarGridSpec(
            num_scalar_prefetch=1,
            grid=(steps,),
            in_specs=[fixed(rows, features)] * 4
            + [fixed(*gates.shape)]
            + specs
            + [pl.BlockSpec(memory_space=pl.ANY)] * aliased,
            out_specs=[stepped(2 * features, 3 * LANES)] * 2
            + [placed(rows, 4 * LANES), placed(rows, 2 * LANES)],
        ),
        out_shape=[jax.ShapeDtypeStruct((steps, 2 * features, 3 * LANES), BF16)] * 2
        + [
            jax.ShapeDtypeStruct((total, rows, 4 * LANES), BF16),
            jax.ShapeDtypeStruct((total, rows, 2 * LANES), BF16),
        ],
        input_output_aliases={18 + k: 2 + k for k in range(aliased)},
        compiler_params=params(40, "arbitrary"),
        cost_estimate=SMALL,
        name="expert_grads",
    )(order, *x, *o, gates, *weights, *weights, *kept)


def mix_kernel(back, group, order_ref, *refs):
    acts_ref, shared_ref = refs[0:2]
    each = 2 if back else 1
    count = 2 * group * each
    weights = refs[2 : 2 + count]
    shared = refs[2 + count : 2 + count + 2 * each]
    out_ref, total_ref = refs[2 + count + 2 * each :]
    step = pl.program_id(0)
    rows = out_ref.shape[0]
    tile = 512
    times = dot_nt if back else dot
    along = 1 if back else 0

    @pl.when(step == 0)
    def _():
        both = jnp.concatenate([w[0] for w in shared], axis=along)
        for t in range(rows // tile):
            at = slice(t * tile, (t + 1) * tile)
            total_ref[at, :] = times(shared_ref[0, at, :], both)

    both = jnp.concatenate([w[0] for w in weights], axis=along)
    for t in range(rows // tile):
        at = slice(t * tile, (t + 1) * tile)
        acts = jnp.concatenate([acts_ref[g, at, :] for g in range(group)], axis=1)
        total_ref[at, :] += times(acts, both)

    @pl.when(step == pl.num_programs(0) - 1)
    def _():
        out_ref[...] = total_ref[...].astype(out_ref.dtype)


def mix(back, dtype, order, acts, shared_acts, weights, shared_weights):
    pairs, rows, width = acts.shape
    features = weights[0].shape[1] if back else weights[0].shape[2]
    group = 4 if pairs % 4 == 0 else 1

    def spec(place):
        if back:
            return pl.BlockSpec((1, features, LANES), lambda i, o: (place(i, o)[0], 0, place(i, o)[1]))
        return pl.BlockSpec((1, LANES, features), lambda i, o: (*place(i, o), 0))

    def routed(k):
        return spec(lambda i, o: (o[2 * group * i + k], o[o.shape[0] - 1]))

    def common(k):
        return spec(lambda i, o: (0, 2 * o[o.shape[0] - 1] + k))

    return pl.pallas_call(
        functools.partial(mix_kernel, back, group),
        grid_spec=pltpu.PrefetchScalarGridSpec(
            num_scalar_prefetch=1,
            grid=(pairs // group,),
            in_specs=[
                pl.BlockSpec((group, rows, width), lambda i, o: (i, 0, 0)),
                pl.BlockSpec((1, rows, width), lambda i, o: (0, 0, 0)),
            ]
            + [routed(k) for k in range(2 * group) for _ in weights]
            + [common(k) for k in range(2) for _ in weights],
            out_specs=pl.BlockSpec((rows, features), lambda i, o: (0, 0)),
            scratch_shapes=[pltpu.VMEM((rows, features), F32)],
        ),
        out_shape=jax.ShapeDtypeStruct((rows, features), dtype),
        compiler_params=params(48, "arbitrary"),
        cost_estimate=SMALL,
        name="mix",
    )(order, acts, shared_acts, *weights * (2 * group), *shared_weights * 2)


def chip_sum_kernel(own_ref, other_ref, total_ref, rounded_ref):
    total = own_ref[...] + other_ref[...].astype(F32)
    total_ref[...] = total
    rounded_ref[...] = total.astype(BF16)


def chip_sum(own, other):
    rows, features = own.shape
    spec = pl.BlockSpec((TOKEN_TILE, features), lambda i: (i, 0))
    return pl.pallas_call(
        chip_sum_kernel,
        grid=(rows // TOKEN_TILE,),
        out_shape=[
            jax.ShapeDtypeStruct((rows, features), F32),
            jax.ShapeDtypeStruct((rows, features), BF16),
        ],
        in_specs=[spec, spec],
        out_specs=[spec, spec],
        compiler_params=params(16, "arbitrary"),
        cost_estimate=SMALL,
        name="chip_sum",
    )(own, other)


def norm_back_kernel(tiles, place_ref, *refs):
    sum_ref, came_ref, hidden_ref, scale_ref, gains_ref, grad_ref, product_ref, gain_ref = refs
    step = pl.program_id(0)
    part = (step >= tiles // 2).astype(jnp.int32)
    grad = sum_ref[...] + came_ref[...].astype(F32)
    hidden = hidden_ref[...]
    grad_ref[...] = grad
    product_ref[...] = jnp.sum(grad * gains_ref[1:2, :] * hidden, axis=1, keepdims=True)

    @pl.when(step == 0)
    def _():
        gain_ref[...] = jnp.zeros_like(gain_ref)

    @pl.when(part == place_ref[0])
    def _():
        gain_ref[...] += jnp.sum(grad * hidden * scale_ref[...], axis=0, keepdims=True)


def norm_back(place, sums, came, hidden, scale, gains):
    rows, features = hidden.shape
    tiles = rows // TOKEN_TILE
    return pl.pallas_call(
        functools.partial(norm_back_kernel, tiles),
        grid_spec=pltpu.PrefetchScalarGridSpec(
            num_scalar_prefetch=1,
            grid=(tiles,),
            in_specs=[rowwise(features)] * 3 + [rowwise(1), whole(2, features)],
            out_specs=[rowwise(features), rowwise(1), whole(1, features)],
        ),
        out_shape=[
            jax.ShapeDtypeStruct((rows, features), F32),
            jax.ShapeDtypeStruct((rows, 1), F32),
            jax.ShapeDtypeStruct((1, features), F32),
        ],
        compiler_params=params(48, "arbitrary"),
        cost_estimate=SMALL,
        name="norm_back",
    )(place, sums, came, hidden, scale, gains)


def norm_back_end_kernel(grad_ref, own_ref, other_ref, hidden_ref, scale_ref, gains_ref, out_grad_ref, hidden_grad_ref, rounded_ref):
    scale = scale_ref[...]
    mean = (own_ref[...] + other_ref[...]) * (1.0 / D)
    result = out_grad_ref[...].astype(F32) + scale * (grad_ref[...] * gains_ref[1:2, :])
    result = result - hidden_ref[...] * (scale * scale * scale * mean)
    hidden_grad_ref[...] = result
    rounded_ref[...] = result.astype(BF16)


def norm_back_end(grad, products, products_c, hidden, scale, gains, out_grad):
    rows, features = hidden.shape
    tile = pl.BlockSpec((TOKEN_TILE, features), lambda i: (i, 0))
    column = pl.BlockSpec((TOKEN_TILE, 1), lambda i: (i, 0))
    return pl.pallas_call(
        norm_back_end_kernel,
        grid=(rows // TOKEN_TILE,),
        in_specs=[tile, column, column, tile, column, pl.BlockSpec(gains.shape, lambda i: (0, 0)), tile],
        out_specs=[tile, tile],
        out_shape=[
            jax.ShapeDtypeStruct((rows, features), F32),
            jax.ShapeDtypeStruct((rows, features), BF16),
        ],
        compiler_params=params(48, "arbitrary"),
        cost_estimate=SMALL,
        name="norm_back_end",
    )(grad, products, products_c, hidden, scale, gains, out_grad)


def ring_of(size):
    return list(range(0, size, 2)) + list(range(1, size, 2))[::-1]


def unpack_kernel(aliased, plan_ref, *refs):
    chunks = refs[0:2]
    gate_ref, up_ref, down_ref = refs[2 + aliased : 5 + aliased]
    blocks = chunks[0].shape[1] // LANES

    def write(chunk_ref):
        gate_ref[0] = chunk_ref[0, :, 0:LANES].astype(F32)
        up_ref[0] = chunk_ref[0, :, LANES : 2 * LANES].astype(F32)
        for b in range(blocks):
            at = slice(b * LANES, (b + 1) * LANES)
            down_ref[0, :, at] = chunk_ref[0, at, 2 * LANES :].astype(F32)

    for k in range(2):
        pl.when(pl.program_id(1) == k)(lambda k=k: write(chunks[k]))


def unpack(plan, first, wave, chunks, shapes, outs):
    count, rows, width = chunks[0].shape
    chunk = pl.BlockSpec((1, rows, width), lambda i, d, n: (i, 0, 0))

    def place(i, d, n):
        block = n[n.shape[0] - 1]
        return n[first + 2 * i + d], 1 - block if wave else block

    def wide(i, d, n):
        expert, block = place(i, d, n)
        return (expert, 0, block)

    def low(i, d, n):
        expert, block = place(i, d, n)
        return (expert, block, 0)

    aliased = len(outs)
    return pl.pallas_call(
        functools.partial(unpack_kernel, aliased),
        grid_spec=pltpu.PrefetchScalarGridSpec(
            num_scalar_prefetch=1,
            grid=(count, 2),
            in_specs=[chunk, chunk] + [pl.BlockSpec(memory_space=pl.ANY)] * aliased,
            out_specs=[
                pl.BlockSpec((1, rows, LANES), wide),
                pl.BlockSpec((1, rows, LANES), wide),
                pl.BlockSpec((1, LANES, rows), low),
            ],
        ),
        out_shape=[jax.ShapeDtypeStruct(shape, F32) for shape in shapes],
        input_output_aliases={3 + k: k for k in range(aliased)},
        compiler_params=params(16, "arbitrary", "arbitrary"),
        cost_estimate=SMALL,
        name="unpack",
    )(plan, *chunks, *outs)


def ring_sum_kernel(came_ref, mine_ref, *outs):
    total = (came_ref[...].astype(F32) + mine_ref[...].astype(F32)).astype(BF16)
    if len(outs) == 1:
        outs[0][...] = total
    else:
        half = pl.program_id(1) // (pl.num_programs(1) // 2)
        for k, out_ref in enumerate(outs):

            @pl.when(half == k)
            def _(out_ref=out_ref):
                out_ref[...] = total


def ring_sum(came, mine, halved):
    count, rows, lanes = came.shape
    tiles = 4
    spec = pl.BlockSpec((1, rows // tiles, lanes), lambda i, j: (i, j, 0))

    def half(k):
        first = k * tiles // 2
        last = tiles // 2 - 1
        return pl.BlockSpec(
            (1, rows // tiles, lanes), lambda i, j: (i, jnp.clip(j - first, 0, last), 0)
        )

    shapes = [jax.ShapeDtypeStruct((count, rows // 2, lanes), BF16)] * 2
    return pl.pallas_call(
        ring_sum_kernel,
        grid=(count, tiles),
        in_specs=[spec, spec],
        out_specs=[half(0), half(1)] if halved else spec,
        out_shape=shapes if halved else jax.ShapeDtypeStruct(came.shape, BF16),
        compiler_params=params(16, "arbitrary", "arbitrary"),
        cost_estimate=SMALL,
        name="ring_sum",
    )(came, mine)


def late_chunk_kernel(came, plan_ref, pack_ref, *refs):
    values = pack_ref[:, 0]
    if came:
        values = (refs[0][...].astype(F32) + values.astype(F32)).astype(BF16)
    outs = refs[came:]
    if len(outs) == 1:
        outs[0][...] = values
    else:
        for k, out_ref in enumerate(outs):
            out_ref[...] = values[k]


def late_chunk(plan, at, pack, came, halved):
    halves, _, rows, lanes = pack.shape
    spec = pl.BlockSpec((halves, rows, lanes), lambda i, n: (0, 0, 0))
    half = pl.BlockSpec((rows, lanes), lambda i, n: (0, 0))
    halfs = [jax.ShapeDtypeStruct((rows, lanes), BF16)] * 2
    return pl.pallas_call(
        functools.partial(late_chunk_kernel, len(came)),
        grid_spec=pltpu.PrefetchScalarGridSpec(
            num_scalar_prefetch=1,
            grid=(1,),
            in_specs=[pl.BlockSpec((halves, 1, rows, lanes), lambda i, n: (0, n[at], 0, 0))]
            + [spec] * len(came),
            out_specs=[half] * 2 if halved else spec,
        ),
        out_shape=halfs if halved else jax.ShapeDtypeStruct((halves, rows, lanes), BF16),
        compiler_params=params(16, "arbitrary"),
        cost_estimate=SMALL,
        name="late_chunk",
    )(plan, pack, *came)


def unpack_late_kernel(first_step, steps, plan_ref, *refs):
    chunks = refs[0 : 2 * steps]
    sgate, sup, sdown, query, key, value, out, all_ref = refs[2 * steps :]
    rows, features = chunks[0].shape[0] // 2, all_ref.shape[2]
    for k in range(2):
        for step in range(steps):
            at = plan_ref[first_step + 2 * step + k] * rows
            for c in range(2):
                all_ref[k, c, pl.ds(pl.multiple_of(at, rows), rows), :] = chunks[
                    steps * k + step
                ][c * rows : (c + 1) * rows, :]
    flipped = plan_ref[plan_ref.shape[0] - 1] != 0
    for c in range(2):
        for b in range(14):
            lanes = slice(b % 7 * LANES, (b % 7 + 1) * LANES)
            first, second = all_ref[0, c, :, lanes], all_ref[1, c, :, lanes]
            if b >= 7:
                first, second = second, first
            block = jnp.where(flipped, second, first).astype(F32)
            if b < 6:
                at = slice((2 * c + b // 3) * LANES, (2 * c + b // 3 + 1) * LANES)
                if b % 3 < 2:
                    (sgate, sup)[b % 3][:, at] = block
                else:
                    for k in range(features // LANES):
                        here = slice(k * LANES, (k + 1) * LANES)
                        sdown[at, here] = block[here, :]
            elif b < 9:
                at = (GROUP_HEADS * c + b - 6) * LANES
                query[:, at : at + LANES] = block
            elif b < 11:
                (key, value)[b - 9][:, c * LANES : (c + 1) * LANES] = block
            else:
                at = (GROUP_HEADS * c + b - 11) * LANES
                out[at : at + LANES, :] = block.T


def unpack_late(plan, first_step, chunks, shapes):
    steps = len(chunks[0])
    rows, lanes = chunks[0][0].shape[0] // 2, chunks[0][0].shape[1]
    spec = pl.BlockSpec(memory_space=pltpu.VMEM)
    return pl.pallas_call(
        functools.partial(unpack_late_kernel, first_step, steps),
        in_specs=[pl.BlockSpec(memory_space=pltpu.SMEM)] + [spec] * (2 * steps),
        out_specs=[spec] * len(shapes),
        out_shape=[jax.ShapeDtypeStruct(shape, F32) for shape in shapes],
        scratch_shapes=[pltpu.VMEM((2, 2, steps * rows, lanes), BF16)],
        compiler_params=params(48),
        cost_estimate=SMALL,
        name="unpack_late",
    )(plan, *chunks[0], *chunks[1])


def plans(ring, each):
    size = len(ring)
    rows = []
    for member in range(size):
        place = ring.index(member)
        for col in range(2):
            chunks = []
            for step in range(2 * size - 1):
                for which in range(2):
                    sign = 1 if which == col else -1
                    chunks.append((place - sign * step) % size)
            experts = []
            for start in (0, size - 1):
                for step in range(start, start + size):
                    for k in range(each):
                        for which in range(2):
                            second = col if which == 0 else 1 - col
                            experts.append(2 * each * chunks[2 * step + which] + each * second + k)
            rows.append(experts + chunks + [col])
    return np.asarray(rows, np.int32)


def body(
    tokens_in,
    norm_gain_attn,
    w_query,
    w_key,
    w_value,
    w_out,
    norm_gain_ffn,
    w_gate,
    w_up,
    w_down,
    w_shared_gate,
    w_shared_up,
    w_shared_down,
    routes,
    gate_weights,
    seq_lengths,
    out_grad,
):
    row = lax.axis_index("row")
    col = lax.axis_index("col")
    dp = lax.axis_index("dp")
    dp_size = lax.axis_size("dp")
    local_rows, local_features = tokens_in.shape
    experts = w_gate.shape[0]
    group_width = GROUP_HEADS * DH
    col_ref = col.reshape(1)

    ring_size = min(8, dp_size)
    ring = ring_of(ring_size)
    starts = range(0, dp_size, ring_size)
    rights = [
        (g + ring[k], g + ring[(k + 1) % ring_size]) for g in starts for k in range(ring_size)
    ]
    lefts = [(b, a) for a, b in rights]
    routes_of = [
        [(2 * a, 2 * b) for a, b in ways[0]] + [(2 * a + 1, 2 * b + 1) for a, b in ways[1]]
        for ways in ((rights, lefts), (lefts, rights))
    ]
    experts_each = experts // (2 * ring_size)
    plan = jnp.asarray(plans(ring, experts_each))
    plan = lax.dynamic_slice(
        plan, (2 * (dp % ring_size) + col, jnp.int32(0)), (1, plan.shape[1])
    ).reshape(-1)

    def send(values, which):
        if ring_size == 1:
            return values
        return lax.ppermute(values, ("dp", "col"), routes_of[which])

    def chunk_at(step, which):
        return plan[2 * experts + 2 * step + which]

    def across_rings(values):
        if len(starts) == 1:
            return values
        peers = [[g + k for g in starts] for k in range(ring_size)]
        return lax.psum(values, "dp", axis_index_groups=peers)

    where = jnp.stack([row, seq_lengths[0], col])
    tokens_y = swap(tokens_in, "row")
    tokens_c = swap(tokens_in, "col")
    count = min(ring_size, 4)
    member = dp % count
    there, out_y = their_columns(
        jnp.stack([col, member]), w_query, w_key, w_value, w_out, count
    )
    gains = jnp.stack([norm_gain_attn, norm_gain_ffn])
    there = swap(there, "col")
    gains_c = swap(gains, "col")

    def project_half(own, other):
        return project(col_ref, own, other, gains, gains_c, w_query, w_key, w_value, there)

    near = project_half(tokens_in, tokens_c)
    gate_c = swap(w_gate, "col")
    out_y = swap(out_y, "row")
    tokens_y = after(tokens_y, near[2], out_y)
    tokens_yc = swap(tokens_y, "col")
    grad_y = swap(after(out_grad, tokens_y), "row")
    far = project_half(tokens_y, tokens_yc)
    shares = [out_y]
    for k in range(1, count):
        part = out_y if k < 3 else after(out_y, far[2])
        shares.append(lax.ppermute(part, "dp", [(m, m ^ k) for m in range(dp_size)]))
    where = after(where, grad_y, *shares)

    w_sgate, w_sup, w_sdown = w_shared_gate[None], w_shared_up[None], w_shared_down[None]
    up_c = swap(after(w_up, gate_c, tokens_yc), "col")

    attended = attend(where, near[2], far[2])
    attended_y = swap(attended, "row")
    attended_c = swap(attended, "col")
    out_c = swap(after(w_out, tokens_yc), "col")
    before = hidden_before(
        where,
        [tokens_in, tokens_c, tokens_y, tokens_yc],
        [attended, attended_c],
        w_out,
        out_c,
    )
    down_c = swap(after(w_down, tokens_yc), "col")
    attended_y = after(attended_y, before[0])
    out_y = join(member, *shares)
    out_yc = swap(out_y, "col")
    attended_yc = swap(attended_y, "col")
    grad_own = join(row, out_grad, grad_y)
    grad_other = swap(grad_own, "col")
    hidden, x_own, x_other, scale_ffn = hidden_after(
        where, before, [attended_y, attended_yc], out_y, out_yc, gains, gains_c
    )
    sgate_c, sup_c, sdown_c = (
        swap(after(w, attended_yc), "col") for w in (w_sgate, w_sup, w_sdown)
    )

    choices = jnp.arange(experts, dtype=jnp.int32)[:, None]
    dense = sum(
        jnp.where(routes[:, k][None, :] == choices, gate_weights[:, k][None, :], 0.0)
        for k in range(routes.shape[1])
    )
    gates = []
    for _ in range(3):
        gates.append(lax.reduce_precision(dense, 8, 7))
        dense = dense - gates[-1]
    gates = jnp.concatenate(gates, axis=0).astype(BF16)

    each = experts_each
    order = plan
    pairs_total = experts // 2
    routed = [w_gate, w_up, gate_c, up_c, w_down, down_c]
    shared = [w_sgate, w_sup, sgate_c, sup_c, w_sdown, sdown_c]

    def run(first, last, order, kept):
        return expert_grads(
            order,
            first,
            last,
            pairs_total,
            [x_own, x_other],
            [grad_own, grad_other],
            gates,
            routed,
            kept,
        )

    first = run(0, each, order, ())
    kept = first[2:]
    sums = [first[0], first[1]]
    runs = {}
    mixed = {}
    normed = {}

    def work_experts(first, last):
        def work(order, ties):
            nonlocal kept
            result = run(first, last, order, tuple(kept))
            kept = result[2:]
            runs[first] = result[0:2]
            return kept[0]

        return work

    def work_shared(order, ties):
        runs["shared"] = expert_grads(
            order, 0, 1, None, [x_own, x_other], [grad_own, grad_other], gates, shared, ()
        )
        return runs["shared"][2]

    def work_back(half):
        def work(order, ties):
            mixed[True, half] = mix(
                True,
                BF16 if half else F32,
                order,
                kept[0],
                runs["shared"][2],
                routed[2 * half : 2 * half + 2],
                shared[2 * half : 2 * half + 2],
            )
            if half:
                normed["other"] = swap(mixed[True, 1], "col")
                return mixed[True, 1]
            normed["sum"] = chip_sum(mixed[True, 0], normed["other"])
            normed["came"] = swap(normed["sum"][1], "row")
            return normed["sum"][1]

        return work

    def work_out(half):
        def work(order, ties):
            mixed[False, half] = mix(
                False,
                BF16 if half else F32,
                order,
                kept[1],
                runs["shared"][3],
                routed[4 + half : 5 + half],
                shared[4 + half : 5 + half],
            )
            return mixed[False, half]

        return work

    start = row * local_rows

    def my_rows(values):
        return lax.dynamic_slice_in_dim(values, start, local_rows, axis=0)

    def their_rows(values):
        return lax.dynamic_slice_in_dim(values, local_rows - start, local_rows, axis=0)

    def work_hidden(order, ties):
        grads, products, normed["gain"] = norm_back(
            after(where, *ties), normed["sum"][0], normed["came"], hidden, scale_ffn, gains
        )
        products_c = swap(products, "col")
        normed["hidden"], normed["grad"] = norm_back_end(
            grads, products, products_c, hidden, scale_ffn, gains, grad_own
        )
        normed["grad_c"] = swap(normed["grad"], "col")
        return normed["grad"]

    def work_attend(order, ties):
        normed["qkv"] = attend_back(
            after(where, *ties), near[2], far[2], normed["grad"], normed["grad_c"], w_out, out_c
        )
        return normed["qkv"]

    def work_late(order, ties):
        normed["packs"] = late_grads(
            where,
            near[0:2],
            far[0:2],
            normed["qkv"],
            attended,
            normed["grad"],
            normed["grad_c"],
            runs["shared"][0:2],
        )
        return normed["packs"][0]

    tasks = [work_experts(at, at + each) for at in range(each, pairs_total, each)]
    tasks += [work_shared, work_back(1), work_back(0), work_out(1), work_out(0)]
    ends = [work_hidden, work_attend]
    tasks += [None] * (2 * ring_size - 1 - len(tasks) - len(ends)) + ends
    got = [None, None]
    if ring_size > 1:
        got[0] = send(sums[0], 0)
        tasks.pop(0)(after(order, *sums), sums)
        got[1] = send(after(sums[1], kept[0]), 1)
    for s in range(1, ring_size):
        for k in range(2):
            last = sums
            task = tasks.pop(0) if tasks else None
            if task:
                last = [task(after(order, *last), last)]
            sums[k] = ring_sum(after(got[k], *last), runs[each * s][k], s + 1 == ring_size)
            if s + 1 < ring_size:
                got[k] = send(sums[k], k)
            else:
                sums[k], got[k] = sums[k]
    for task in tasks:
        if task:
            task(after(order, *sums), sums)
    if ring_size == 1:
        got = [total[:, local_features:] for total in sums]
        sums = [total[:, :local_features] for total in sums]
    waves = [[across_rings(total) for total in sums]]
    crossed = [swap(across_rings(total), "col") for total in got]
    waves.append([crossed[1], crossed[0]])

    hidden_grad, attn_grad, attn_grad_c = normed["hidden"], normed["grad"], normed["grad_c"]
    gain_ffn_part, qkv_grad = normed["gain"], normed["qkv"]
    work_late(order, ())
    packs = normed["packs"]

    packs = [
        pack.reshape(2, ring_size, local_features // ring_size, pack.shape[2]) for pack in packs
    ]
    chunks_first = 2 * experts
    late_total = 2 * (ring_size - 1)
    late = [
        late_chunk(plan, chunks_first + k, packs[k], (), late_total == 0) for k in range(2)
    ]
    late_out = [[], []]
    late_done = 0

    def late_turn():
        owns = [across_rings(values[0]) for values in late]
        others = [swap(across_rings(values[1]), "col") for values in late]
        for k in range(2):
            late[k] = join(col, owns[k], others[1 - k])
            late_out[k].append(late[k])

    def late_finish(k, values):
        if late_done < ring_size:
            at = chunks_first + 2 * late_done + k
            late[k] = late_chunk(plan, at, packs[k], (values,), late_done == ring_size - 1)
        else:
            late[k] = values
            late_out[k].append(values)

    shapes = [w_gate.shape, w_up.shape, w_down.shape]
    placed = ()

    def place_chunks(wave, step, chunks, placed):
        return unpack(plan, experts + 2 * each * step, wave, chunks, shapes, placed)

    if late_total == 0:
        late_turn()
    steps = ring_size - 1
    late_got = None
    last = []
    got = list(waves[0])
    for number in range(2 * steps - 1):
        wave, step = (0, number) if number < steps else (1, number - steps + 1)
        if number == steps:
            came = got
            got = early
        late_done += late_got is not None
        chunks = [None, None]
        for k in range(2):
            chunks[k] = after(got[k], *last) if last else got[k]
            got[k] = send(chunks[k], k)
            last = [chunks[k]]
            if late_got is not None:
                late_finish(k, after(late_got[k], *last))
                last = list(late[k]) if late_done == ring_size - 1 else [late[k]]
        if number == 0:
            early = [send(after(waves[1][k], *chunks), k) for k in range(2)]
        if late_got is not None and late_done == ring_size - 1:
            late_turn()
        late_got = None
        if late_done < late_total:
            late_got = [send(late[k], k) for k in range(2)]
        if number == steps:
            placed = place_chunks(0, steps, came, placed)
            placed = place_chunks(1, 0, waves[1], placed)
        placed = place_chunks(wave, step, [after(chunks[0], *last), chunks[1]], placed)
        last = placed[0:1]
        if number == 3:
            qkv_grad = after(qkv_grad, *last)
    if steps:
        placed = place_chunks(1, steps, [after(got[k], *last) for k in range(2)], placed)
        last = placed[0:1]
    while late_got is not None:
        late_done += 1
        for k in range(2):
            late_finish(k, after(late_got[k], *last))
        if late_done == ring_size - 1:
            late_turn()
        late_got = [send(late[k], k) for k in range(2)] if late_done < late_total else None
    if not steps:
        for wave in range(2):
            placed = place_chunks(wave, 0, waves[wave], placed)
    gate_grad, up_grad, down_grad = placed
    shapes = [w.shape for w in (w_shared_gate, w_shared_up, w_shared_down)]
    shapes += [w.shape for w in (w_query, w_key, w_value, w_out)]
    finals = unpack_late(plan, chunks_first + late_total, late_out, shapes)
    shared_gate_grad, shared_up_grad, shared_down_grad = finals[0:3]
    query_grad, key_grad, value_grad, out_proj_grad = finals[3:7]

    ffn_sum = mixed[False, 0] + swap(mixed[False, 1], "col").astype(F32)
    ffn_rows = my_rows(ffn_sum) + swap(their_rows(ffn_sum).astype(BF16), "row").astype(F32)
    block_out = (my_rows(hidden) + ffn_rows).astype(BF16)

    here = jnp.concatenate(
        [halves(w, 1, col)[0] for w in (w_query, w_key, w_value)], axis=1
    )
    tokens_back = dot_nt(qkv_grad, here) + swap(
        dot_nt(qkv_grad, there).astype(BF16), "col"
    ).astype(F32)
    tokens_back = my_rows(tokens_back) + swap(
        their_rows(tokens_back).astype(BF16), "row"
    ).astype(F32)
    scale_attn = near[3]
    tokens_f32 = tokens_in.astype(F32)
    gain_attn_part = jnp.sum(tokens_back * tokens_f32 * scale_attn, axis=0)
    scaled = tokens_back * norm_gain_attn
    products = jnp.sum(scaled * tokens_f32, axis=1, keepdims=True)
    mean = (products + swap(products, "col")) / D
    tokens_grad = (
        my_rows(hidden_grad) + scale_attn * scaled - tokens_f32 * scale_attn**3 * mean
    ).astype(BF16)

    gain_parts = jnp.concatenate([gain_attn_part[None], gain_ffn_part], axis=0)
    bit = 1
    while bit < ring_size:
        pairs = [(g + k, g + (k ^ bit)) for g in starts for k in range(ring_size)]
        gain_parts = gain_parts + lax.ppermute(gain_parts, "dp", pairs)
        bit *= 2
    gain_parts = across_rings(gain_parts + swap(gain_parts, "row"))

    return (
        block_out,
        tokens_grad,
        gain_parts[0],
        query_grad,
        key_grad,
        value_grad,
        out_proj_grad,
        gain_parts[1],
        gate_grad,
        up_grad,
        down_grad,
        shared_gate_grad,
        shared_up_grad,
        shared_down_grad,
    )


def solution(mesh):
    in_specs = (
        P(("dp", "row"), "col"),
        P("col"),
        P("col", "row"),
        P("col", "row"),
        P("col", "row"),
        P("row", "col"),
        P("col"),
        P(None, "col", "row"),
        P(None, "col", "row"),
        P(None, "row", "col"),
        P("col", "row"),
        P("col", "row"),
        P("row", "col"),
        P("dp", None),
        P("dp", None),
        P("dp"),
        P(("dp", "row"), "col"),
    )
    out_specs = (
        P(("dp", "row"), "col"),
        P(("dp", "row"), "col"),
        P("col"),
        P("col", "row"),
        P("col", "row"),
        P("col", "row"),
        P("row", "col"),
        P("col"),
        P(None, "col", "row"),
        P(None, "col", "row"),
        P(None, "row", "col"),
        P("col", "row"),
        P("col", "row"),
        P("row", "col"),
    )
    return jax.shard_map(body, mesh=mesh, in_specs=in_specs, out_specs=out_specs, check_vma=False)
```

```python
import functools

import jax
import jax.numpy as jnp
import numpy as np
from jax import lax
from jax.experimental import pallas as pl
from jax.experimental.pallas import tpu as pltpu
from jax.sharding import PartitionSpec as P

D = 1536
HQ = 12
HK = 4
DH = 128
GROUP_HEADS = HQ // HK
LANES = 128

EPSILON = 1e-05
F32 = jnp.float32
BF16 = jnp.bfloat16
MIB = 1024 * 1024
GAIN_ROWS = 16
SMALL = pl.CostEstimate(flops=0, bytes_accessed=0, transcendentals=0)


def params(mib, *semantics):
    return pltpu.CompilerParams(
        dimension_semantics=semantics or None, vmem_limit_bytes=mib * MIB
    )


def dot(left, right):
    return jnp.dot(left, right, preferred_element_type=F32)


def dot_nt(left, right):
    return lax.dot_general(left, right, (((1,), (1,)), ((), ())), preferred_element_type=F32)


def dot_tn(left, right):
    return lax.dot_general(left, right, (((0,), (0,)), ((), ())), preferred_element_type=F32)


def after(values, *others):
    return lax.optimization_barrier((values, *others))[0]


def swap(values, axis):
    return lax.ppermute(values, axis, [(0, 1), (1, 0)])


def halves(values, axis, mine):
    size = values.shape[axis] // 2
    low = lax.slice_in_dim(values, 0, size, axis=axis)
    high = lax.slice_in_dim(values, size, 2 * size, axis=axis)
    return jnp.where(mine == 0, low, high), jnp.where(mine == 0, high, low)


def in_order(own, other, mine, axis):
    return jnp.concatenate(
        [jnp.where(mine == 0, own, other), jnp.where(mine == 0, other, own)], axis=axis
    )


def gather_rows(place_ref, own_ref, other_ref, all_ref):
    row = place_ref[0]
    rows = own_ref.shape[0]
    all_ref[pl.ds(pl.multiple_of(row * rows, rows), rows), :] = own_ref[...]
    all_ref[pl.ds(pl.multiple_of((1 - row) * rows, rows), rows), :] = other_ref[...]


def head_rows(ref, first, block):
    return jnp.concatenate(
        [ref[first : first + block, h * DH : (h + 1) * DH] for h in range(GROUP_HEADS)], axis=0
    )


def key_probs(query, key, first, length):
    block, keys = query.shape[0] // GROUP_HEADS, key.shape[0]
    scores = dot_nt(query, key) * DH ** (-0.5)
    shape = (block, keys)
    query_at = lax.broadcasted_iota(jnp.int32, shape, 0) + first
    key_at = lax.broadcasted_iota(jnp.int32, shape, 1)
    allowed = (key_at <= query_at) & (key_at < length)
    allowed = jnp.concatenate([allowed] * GROUP_HEADS, axis=0)
    scores = jnp.where(allowed, scores, -1e30)
    weights = jnp.exp(scores - jnp.max(scores, axis=1, keepdims=True))
    return weights * (1.0 / jnp.sum(weights, axis=1, keepdims=True))


def attend_kernel(place_ref, own_ref, other_ref, out_ref, all_ref):
    gather_rows(place_ref, own_ref, other_ref, all_ref)
    rows = own_ref.shape[0]
    block = 256
    width = GROUP_HEADS * DH
    for at in range(2 * rows // block):
        first, keys = at * block, (at + 1) * block
        query = head_rows(all_ref, first, block)
        key = all_ref[0:keys, width : width + DH]
        value = all_ref[0:keys, width + DH : width + 2 * DH]
        probs = key_probs(query, key, first, place_ref[1])
        result = dot(probs.astype(BF16), value).astype(BF16)
        for h in range(GROUP_HEADS):
            out_ref[first : first + block, h * DH : (h + 1) * DH] = result[
                h * block : (h + 1) * block
            ]


def attend(place, own, other):
    rows, width = own.shape
    spec = pl.BlockSpec(memory_space=pltpu.VMEM)
    return pl.pallas_call(
        attend_kernel,
        out_shape=jax.ShapeDtypeStruct((2 * rows, GROUP_HEADS * DH), BF16),
        in_specs=[pl.BlockSpec(memory_space=pltpu.SMEM), spec, spec],
        out_specs=spec,
        scratch_shapes=[pltpu.VMEM((2 * rows, width), BF16)],
        compiler_params=params(32),
        cost_estimate=SMALL,
        name="attend",
    )(place, own, other)


def attend_back_kernel(
    place_ref, own_ref, other_ref, grad_ref, grad_c_ref, out_ref, out_c_ref, result_ref, all_ref, total_ref
):
    gather_rows(place_ref, own_ref, other_ref, all_ref)
    rows = own_ref.shape[0]
    block = 256
    width = GROUP_HEADS * DH
    group = pl.ds(pl.multiple_of(place_ref[2] * width, width), width)
    blocks = 2 * rows // block
    for at in reversed(range(blocks)):
        first, keys = at * block, (at + 1) * block
        query = head_rows(all_ref, first, block)
        key = all_ref[0:keys, width : width + DH]
        value = all_ref[0:keys, width + DH : width + 2 * DH]
        probs = key_probs(query, key, first, place_ref[1])
        grad = dot_nt(grad_ref[first:keys, :], out_ref[group, :])
        grad = (grad + dot_nt(grad_c_ref[first:keys, :], out_c_ref[group, :])).astype(BF16)
        grad = jnp.concatenate(
            [grad[:, h * DH : (h + 1) * DH] for h in range(GROUP_HEADS)], axis=0
        )
        probs_grad = dot_nt(grad, value)
        carried = jnp.sum(probs * probs_grad, axis=1, keepdims=True)
        score_grad = (probs * (probs_grad - carried)).astype(BF16)
        query_back = (dot(score_grad, key) * DH ** (-0.5)).astype(BF16)
        for h in range(GROUP_HEADS):
            result_ref[first:keys, h * DH : (h + 1) * DH] = query_back[
                h * block : (h + 1) * block
            ]
        key_back = dot_tn(score_grad, query)
        value_back = dot_tn(probs.astype(BF16), grad)
        if at == blocks - 1:
            total_ref[:, 0:DH] = key_back
            total_ref[:, DH:] = value_back
        else:
            total_ref[0:keys, 0:DH] += key_back
            total_ref[0:keys, DH:] += value_back
    result_ref[:, width : width + DH] = (total_ref[:, 0:DH] * DH ** (-0.5)).astype(BF16)
    result_ref[:, width + DH :] = total_ref[:, DH:].astype(BF16)


def attend_back(place, own, other, grad, grad_c, w_out, out_c):
    rows, width = own.shape
    spec = pl.BlockSpec(memory_space=pltpu.VMEM)
    return pl.pallas_call(
        attend_back_kernel,
        out_shape=jax.ShapeDtypeStruct((2 * rows, width), BF16),
        in_specs=[pl.BlockSpec(memory_space=pltpu.SMEM)] + [spec] * 6,
        out_specs=spec,
        scratch_shapes=[
            pltpu.VMEM((2 * rows, width), BF16),
            pltpu.VMEM((2 * rows, 2 * DH), F32),
        ],
        compiler_params=params(60),
        cost_estimate=SMALL,
        name="attend_back",
    )(place, own, other, grad, grad_c, w_out, out_c)


def late_kernel(place_ref, *refs):
    near, near_c, far, far_c, qkv_ref, attended_ref, grad_ref, grad_c_ref = refs[0:8]
    shared = refs[8:10]
    outs = refs[10:12]
    rows, features = near.shape
    own_rows = pl.ds(pl.multiple_of(place_ref[0] * rows, rows), rows)
    far_rows = pl.ds(pl.multiple_of((1 - place_ref[0]) * rows, rows), rows)
    split = 7 * LANES

    def store(h, at, values):
        values = values.astype(BF16)
        for part in range(2):
            low, high = max(at, part * split), min(at + values.shape[1], (part + 1) * split)
            if low < high:
                piece = values[:, low - at : high - at]
                to = slice(low - part * split, high - part * split)

                @pl.when(place_ref[2] == 0)
                def _(part=part, to=to, piece=piece):
                    outs[part][h, :, to] = piece

                @pl.when(place_ref[2] != 0)
                def _(part=part, to=to, piece=piece):
                    outs[1 - part][h, :, to] = piece

    for h, (x, y, grad) in enumerate(((near, far, grad_ref), (near_c, far_c, grad_c_ref))):
        for k in range(2):
            store(h, 3 * LANES * k, shared[k][0, h * features : (h + 1) * features, :])
        project = dot_tn(x[...], qkv_ref[own_rows, :]) + dot_tn(y[...], qkv_ref[far_rows, :])
        store(h, 6 * LANES, project)
        store(h, 11 * LANES, dot_tn(grad[...], attended_ref[...]))


def late_grads(place, near, far, qkv_grad, attended, grad, grad_c, shared):
    features = near[0].shape[1]
    spec = pl.BlockSpec(memory_space=pltpu.VMEM)
    return pl.pallas_call(
        late_kernel,
        out_shape=[jax.ShapeDtypeStruct((2, features, 7 * LANES), BF16)] * 2,
        in_specs=[pl.BlockSpec(memory_space=pltpu.SMEM)] + [spec] * 10,
        out_specs=[spec] * 2,
        compiler_params=params(60),
        cost_estimate=SMALL,
        name="late_grads",
    )(place, *near, *far, qkv_grad, attended, grad, grad_c, *shared)


def columns_kernel(
    place_ref, query_ref, key_ref, value_ref, w_out_ref, out_ref, share_ref
):
    share_ref[...] = w_out_ref[...]
    width = GROUP_HEADS * DH
    out_ref[:, 0:width] = query_ref[...]
    out_ref[:, width : width + DH] = key_ref[...]
    out_ref[:, width + DH :] = value_ref[...]


def their_columns(place, w_query, w_key, w_value, w_out, shares):
    rows = w_query.shape[0]
    width = GROUP_HEADS * DH + 2 * DH

    def theirs(width):
        return pl.BlockSpec((rows, width), lambda i, c: (0, 1 - c[0]))

    return pl.pallas_call(
        columns_kernel,
        grid_spec=pltpu.PrefetchScalarGridSpec(
            num_scalar_prefetch=1,
            grid=(1,),
            in_specs=[theirs(GROUP_HEADS * DH), theirs(DH), theirs(DH)]
            + [pl.BlockSpec((rows // shares, rows), lambda i, c: (c[1], 0))],
            out_specs=[
                pl.BlockSpec((rows, width), lambda i, c: (0, 0)),
                pl.BlockSpec((rows // shares, rows), lambda i, c: (0, 0)),
            ],
        ),
        out_shape=[
            jax.ShapeDtypeStruct((rows, width), BF16),
            jax.ShapeDtypeStruct((rows // shares, rows), BF16),
        ],
        compiler_params=params(60, "arbitrary"),
        cost_estimate=SMALL,
        name="their_columns",
    )(place, w_query, w_key, w_value, w_out)


def join_kernel(mine_ref, *refs):
    *parts, out_ref = refs
    rows = parts[0].shape[0]
    for k, part in enumerate(parts):
        at = jnp.bitwise_xor(mine_ref[0], k)
        out_ref[pl.ds(pl.multiple_of(at * rows, rows), rows), :] = part[...]


def join(mine, *parts):
    rows, width = parts[0].shape
    spec = pl.BlockSpec(memory_space=pltpu.VMEM)
    return pl.pallas_call(
        join_kernel,
        out_shape=jax.ShapeDtypeStruct((len(parts) * rows, width), parts[0].dtype),
        in_specs=[pl.BlockSpec(memory_space=pltpu.SMEM)] + [spec] * len(parts),
        out_specs=spec,
        compiler_params=params(16),
        cost_estimate=SMALL,
        name="join",
    )(mine.reshape(1), *parts)


def project_kernel(col_ref, own_ref, other_ref, gains_ref, gains_c_ref, query_ref, key_ref, value_ref, there_ref, x_own_ref, x_other_ref, qkv_ref, scale_ref):
    own = own_ref[...].astype(F32)
    other = other_ref[...].astype(F32)
    total = jnp.sum(own * own, axis=1, keepdims=True)
    total = total + jnp.sum(other * other, axis=1, keepdims=True)
    scale = lax.rsqrt(total / D + EPSILON)
    own = (own * scale * gains_ref[0:1, :]).astype(BF16)
    other = (other * scale * gains_c_ref[0:1, :]).astype(BF16)
    x_own_ref[...] = own
    x_other_ref[...] = other
    scale_ref[...] = scale
    here = jnp.concatenate([query_ref[...], key_ref[...], value_ref[...]], axis=1)
    qkv_ref[...] = (dot(own, here) + dot(other, there_ref[...])).astype(BF16)


def project(col, own, other, gains, gains_c, w_query, w_key, w_value, there):
    rows, features = own.shape
    width = there.shape[1]
    group = GROUP_HEADS * DH
    tile = rows // 2

    def whole(*shape):
        return pl.BlockSpec(shape, lambda i, c: (0,) * len(shape))

    def mine(width):
        return pl.BlockSpec((features, width), lambda i, c: (0, c[0]))

    def rowwise(width):
        return pl.BlockSpec((tile, width), lambda i, c: (i, 0))

    return pl.pallas_call(
        project_kernel,
        grid_spec=pltpu.PrefetchScalarGridSpec(
            num_scalar_prefetch=1,
            grid=(rows // tile,),
            in_specs=[
                rowwise(features),
                rowwise(features),
                whole(2, features),
                whole(2, features),
                mine(group),
                mine(DH),
                mine(DH),
                whole(features, width),
            ],
            out_specs=[rowwise(features), rowwise(features), rowwise(width), rowwise(1)],
        ),
        out_shape=[
            jax.ShapeDtypeStruct((rows, features), BF16),
            jax.ShapeDtypeStruct((rows, features), BF16),
            jax.ShapeDtypeStruct((rows, width), BF16),
            jax.ShapeDtypeStruct((rows, 1), F32),
        ],
        compiler_params=params(60, "arbitrary"),
        cost_estimate=SMALL,
        name="project",
    )(col, own, other, gains, gains_c, w_query, w_key, w_value, there)


def head_pair(col_ref, own, other):
    first, second = own[...], other[...]
    flipped = col_ref != 0
    return jnp.concatenate(
        [jnp.where(flipped, second, first), jnp.where(flipped, first, second)], axis=1
    )


def before_kernel(tiles, place_ref, *refs):
    near, near_c, far, far_c, attended, attended_c, here, there, own_ref, other_ref = refs
    is_near = (pl.program_id(0) >= tiles // 2).astype(jnp.int32) == place_ref[0]
    heads = head_pair(place_ref[2], attended, attended_c)
    own = jnp.where(is_near, near[...], far[...]).astype(F32)
    other = jnp.where(is_near, near_c[...], far_c[...]).astype(F32)
    own_ref[...] = own + dot(heads, here[...])
    other_ref[...] = other + dot(heads, there[...])


def after_kernel(place_ref, *refs):
    own_ref, other_ref, attended, attended_c, here, there, gains_ref, gains_c_ref = refs[0:8]
    hidden_ref, x_own_ref, x_other_ref, scale_ref = refs[8:12]
    heads = head_pair(place_ref[2], attended, attended_c)
    own = own_ref[...] + dot(heads, here[...])
    other = other_ref[...] + dot(heads, there[...])
    total = jnp.sum(own * own, axis=1, keepdims=True)
    total = total + jnp.sum(other * other, axis=1, keepdims=True)
    scale = lax.rsqrt(total / D + EPSILON)
    hidden_ref[...] = own
    scale_ref[...] = scale
    x_own_ref[...] = (own * scale * gains_ref[1:2, :]).astype(BF16)
    x_other_ref[...] = (other * scale * gains_c_ref[1:2, :]).astype(BF16)


TOKEN_TILE = 256


def rowwise(width):
    return pl.BlockSpec((TOKEN_TILE, width), lambda i, p: (i, 0))


def whole(*shape):
    return pl.BlockSpec(shape, lambda i, p: (0,) * len(shape))


def hidden_before(place, tokens, attended, here, there):
    half, features = tokens[0].shape
    rows, heads = attended[0].shape
    tiles = rows // TOKEN_TILE
    per_half = half // TOKEN_TILE
    halfwise = pl.BlockSpec((TOKEN_TILE, features), lambda i, p: (i % per_half, 0))
    return pl.pallas_call(
        functools.partial(before_kernel, tiles),
        grid_spec=pltpu.PrefetchScalarGridSpec(
            num_scalar_prefetch=1,
            grid=(tiles,),
            in_specs=[halfwise] * 4 + [rowwise(heads)] * 2 + [whole(2 * heads, features)] * 2,
            out_specs=[rowwise(features)] * 2,
        ),
        out_shape=[jax.ShapeDtypeStruct((rows, features), F32)] * 2,
        compiler_params=params(56, "arbitrary"),
        cost_estimate=pl.CostEstimate(
            flops=8 * rows * features * heads,
            bytes_accessed=16 * rows * features,
            transcendentals=0,
        ),
        name="hidden_before",
    )(place, *tokens, *attended, here, there)


def hidden_after(place, before, attended, here, there, gains, gains_c):
    rows, features = before[0].shape
    heads = attended[0].shape[1]
    return pl.pallas_call(
        after_kernel,
        grid_spec=pltpu.PrefetchScalarGridSpec(
            num_scalar_prefetch=1,
            grid=(rows // TOKEN_TILE,),
            in_specs=[rowwise(features)] * 2
            + [rowwise(heads)] * 2
            + [whole(2 * heads, features)] * 2
            + [whole(2, features)] * 2,
            out_specs=[rowwise(features)] * 3 + [rowwise(1)],
        ),
        out_shape=[
            jax.ShapeDtypeStruct((rows, features), F32),
            jax.ShapeDtypeStruct((rows, features), BF16),
            jax.ShapeDtypeStruct((rows, features), BF16),
            jax.ShapeDtypeStruct((rows, 1), F32),
        ],
        compiler_params=params(56, "arbitrary"),
        cost_estimate=SMALL,
        name="hidden_after",
    )(place, *before, *attended, here, there, gains, gains_c)


def expert_kernel(shared, aliased, first, order_ref, *refs):
    x_own, x_other, o_own, o_other, gates_ref = refs[0:5]
    weights = refs[5:17]
    grads = refs[17 + aliased : 19 + aliased]
    pair_ref, inner_ref = refs[19 + aliased : 21 + aliased]
    step = pl.program_id(0) + first
    rows, features = x_own.shape
    tile = 512
    up_own = jnp.concatenate([weights[k][0] for k in (0, 1, 6, 7)], axis=1)
    up_other = jnp.concatenate([weights[k][0] for k in (2, 3, 8, 9)], axis=1)
    down_own = jnp.concatenate([weights[k][0] for k in (4, 10)], axis=0)
    down_other = jnp.concatenate([weights[k][0] for k in (5, 11)], axis=0)

    def token_tile(t, carry):
        at = pl.ds(pl.multiple_of(t * tile, tile), tile)
        pre = dot(x_own[at, :], up_own) + dot(x_other[at, :], up_other)
        back = dot_nt(o_own[at, :], down_own) + dot_nt(o_other[at, :], down_other)
        for k in range(2):
            pre_gate = pre[:, 2 * k * LANES : (2 * k + 1) * LANES]
            pre_up = pre[:, (2 * k + 1) * LANES : (2 * k + 2) * LANES]
            inner_grad = back[:, k * LANES : (k + 1) * LANES]
            sigmoid = 1.0 / (1.0 + jnp.exp(-pre_gate))
            silu = pre_gate * sigmoid
            inner = silu * pre_up
            if not shared:
                shape = (gates_ref.shape[0], LANES)
                expert = lax.broadcasted_iota(jnp.int32, shape, 0) % (gates_ref.shape[0] // 3)
                chosen = (expert == order_ref[2 * step + k]).astype(F32).astype(BF16)
                gate = dot_tn(gates_ref[:, at], chosen)
                inner = gate * inner
                inner_grad = gate * inner_grad
            gate_grad = inner_grad * pre_up * (sigmoid * (1.0 + pre_gate * (1.0 - sigmoid)))
            inner_ref[0, at, k * LANES : (k + 1) * LANES] = inner.astype(BF16)
            pair_ref[0, at, 2 * k * LANES : (2 * k + 1) * LANES] = gate_grad.astype(BF16)
            pair_ref[0, at, (2 * k + 1) * LANES : (2 * k + 2) * LANES] = (
                inner_grad * silu
            ).astype(BF16)
        return carry

    lax.fori_loop(0, rows // tile, token_tile, 0)
    pairs = pair_ref[0]
    for h, x in enumerate((x_own, x_other)):
        wide = dot_tn(x[...], pairs).astype(BF16)
        for k in range(2):
            grads[k][0, h * features : (h + 1) * features, 0 : 2 * LANES] = wide[
                :, 2 * k * LANES : (2 * k + 2) * LANES
            ]
    inner = inner_ref[0]
    tile = 256
    for h, o in enumerate((o_own, o_other)):
        for j in range(features // tile):
            low = dot_tn(inner, o[:, j * tile : (j + 1) * tile]).astype(BF16)
            for k in range(2):
                for b in range(tile // LANES):
                    at = h * features + j * tile + b * LANES
                    grads[k][0, at : at + LANES, 2 * LANES :] = low[
                        k * LANES : (k + 1) * LANES, b * LANES : (b + 1) * LANES
                    ]


def expert_specs(features, place, wide, low):
    specs = []
    if wide:
        block = pl.BlockSpec((1, features, LANES), lambda i, o: (place(i, o)[0], 0, place(i, o)[1]))
        specs += [block] * 4
    if low:
        block = pl.BlockSpec((1, LANES, features), lambda i, o: (*place(i, o), 0))
        specs += [block] * 2
    return specs


def expert_grads(order, first, last, total, x, o, gates, weights, kept):
    shared = total is None
    steps = last - first
    rows, features = x[0].shape
    aliased = len(kept)

    def fixed(*shape):
        return pl.BlockSpec(shape, lambda i, o: (0,) * len(shape))

    def stepped(*shape):
        return pl.BlockSpec((1, *shape), lambda i, o: (i, 0, 0))

    def placed(*shape):
        return pl.BlockSpec((1, *shape), lambda i, o: (i + first, 0, 0))

    specs = []
    for k in range(2):
        if shared:

            def picked(i, o, k=k):
                return 0, 2 * o[o.shape[0] - 1] + k

        else:

            def picked(i, o, k=k):
                return o[2 * (i + first) + k], o[o.shape[0] - 1]

        specs += expert_specs(features, picked, True, True)
    total = steps if shared else total
    return pl.pallas_call(
        functools.partial(expert_kernel, shared, aliased, first),
        grid_spec=pltpu.PrefetchScalarGridSpec(
            num_scalar_prefetch=1,
            grid=(steps,),
            in_specs=[fixed(rows, features)] * 4
            + [fixed(*gates.shape)]
            + specs
            + [pl.BlockSpec(memory_space=pl.ANY)] * aliased,
            out_specs=[stepped(2 * features, 3 * LANES)] * 2
            + [placed(rows, 4 * LANES), placed(rows, 2 * LANES)],
        ),
        out_shape=[jax.ShapeDtypeStruct((steps, 2 * features, 3 * LANES), BF16)] * 2
        + [
            jax.ShapeDtypeStruct((total, rows, 4 * LANES), BF16),
            jax.ShapeDtypeStruct((total, rows, 2 * LANES), BF16),
        ],
        input_output_aliases={18 + k: 2 + k for k in range(aliased)},
        compiler_params=params(40, "arbitrary"),
        cost_estimate=SMALL,
        name="expert_grads",
    )(order, *x, *o, gates, *weights, *weights, *kept)


def mix_kernel(back, group, order_ref, *refs):
    acts_ref, shared_ref = refs[0:2]
    each = 2 if back else 1
    count = 2 * group * each
    weights = refs[2 : 2 + count]
    shared = refs[2 + count : 2 + count + 2 * each]
    out_ref, total_ref = refs[2 + count + 2 * each :]
    step = pl.program_id(0)
    rows = out_ref.shape[0]
    tile = 512
    times = dot_nt if back else dot
    along = 1 if back else 0

    @pl.when(step == 0)
    def _():
        both = jnp.concatenate([w[0] for w in shared], axis=along)
        for t in range(rows // tile):
            at = slice(t * tile, (t + 1) * tile)
            total_ref[at, :] = times(shared_ref[0, at, :], both)

    both = jnp.concatenate([w[0] for w in weights], axis=along)
    for t in range(rows // tile):
        at = slice(t * tile, (t + 1) * tile)
        acts = jnp.concatenate([acts_ref[g, at, :] for g in range(group)], axis=1)
        total_ref[at, :] += times(acts, both)

    @pl.when(step == pl.num_programs(0) - 1)
    def _():
        out_ref[...] = total_ref[...].astype(out_ref.dtype)


def mix(back, dtype, order, acts, shared_acts, weights, shared_weights):
    pairs, rows, width = acts.shape
    features = weights[0].shape[1] if back else weights[0].shape[2]
    group = 4 if pairs % 4 == 0 else 1

    def spec(place):
        if back:
            return pl.BlockSpec((1, features, LANES), lambda i, o: (place(i, o)[0], 0, place(i, o)[1]))
        return pl.BlockSpec((1, LANES, features), lambda i, o: (*place(i, o), 0))

    def routed(k):
        return spec(lambda i, o: (o[2 * group * i + k], o[o.shape[0] - 1]))

    def common(k):
        return spec(lambda i, o: (0, 2 * o[o.shape[0] - 1] + k))

    return pl.pallas_call(
        functools.partial(mix_kernel, back, group),
        grid_spec=pltpu.PrefetchScalarGridSpec(
            num_scalar_prefetch=1,
            grid=(pairs // group,),
            in_specs=[
                pl.BlockSpec((group, rows, width), lambda i, o: (i, 0, 0)),
                pl.BlockSpec((1, rows, width), lambda i, o: (0, 0, 0)),
            ]
            + [routed(k) for k in range(2 * group) for _ in weights]
            + [common(k) for k in range(2) for _ in weights],
            out_specs=pl.BlockSpec((rows, features), lambda i, o: (0, 0)),
            scratch_shapes=[pltpu.VMEM((rows, features), F32)],
        ),
        out_shape=jax.ShapeDtypeStruct((rows, features), dtype),
        compiler_params=params(48, "arbitrary"),
        cost_estimate=SMALL,
        name="mix",
    )(order, acts, shared_acts, *weights * (2 * group), *shared_weights * 2)


def chip_sum_kernel(own_ref, other_ref, total_ref, rounded_ref):
    total = own_ref[...] + other_ref[...].astype(F32)
    total_ref[...] = total
    rounded_ref[...] = total.astype(BF16)


def chip_sum(own, other):
    rows, features = own.shape
    spec = pl.BlockSpec((TOKEN_TILE, features), lambda i: (i, 0))
    return pl.pallas_call(
        chip_sum_kernel,
        grid=(rows // TOKEN_TILE,),
        out_shape=[
            jax.ShapeDtypeStruct((rows, features), F32),
            jax.ShapeDtypeStruct((rows, features), BF16),
        ],
        in_specs=[spec, spec],
        out_specs=[spec, spec],
        compiler_params=params(16, "arbitrary"),
        cost_estimate=SMALL,
        name="chip_sum",
    )(own, other)


def norm_back_kernel(tiles, place_ref, *refs):
    sum_ref, came_ref, hidden_ref, scale_ref, gains_ref, grad_ref, product_ref, gain_ref = refs
    step = pl.program_id(0)
    part = (step >= tiles // 2).astype(jnp.int32)
    grad = sum_ref[...] + came_ref[...].astype(F32)
    hidden = hidden_ref[...]
    grad_ref[...] = grad
    product_ref[...] = jnp.sum(grad * gains_ref[1:2, :] * hidden, axis=1, keepdims=True)

    @pl.when(step == 0)
    def _():
        gain_ref[...] = jnp.zeros_like(gain_ref)

    @pl.when(part == place_ref[0])
    def _():
        gain_ref[...] += jnp.sum(grad * hidden * scale_ref[...], axis=0, keepdims=True)


def norm_back(place, sums, came, hidden, scale, gains):
    rows, features = hidden.shape
    tiles = rows // TOKEN_TILE
    return pl.pallas_call(
        functools.partial(norm_back_kernel, tiles),
        grid_spec=pltpu.PrefetchScalarGridSpec(
            num_scalar_prefetch=1,
            grid=(tiles,),
            in_specs=[rowwise(features)] * 3 + [rowwise(1), whole(2, features)],
            out_specs=[rowwise(features), rowwise(1), whole(1, features)],
        ),
        out_shape=[
            jax.ShapeDtypeStruct((rows, features), F32),
            jax.ShapeDtypeStruct((rows, 1), F32),
            jax.ShapeDtypeStruct((1, features), F32),
        ],
        compiler_params=params(48, "arbitrary"),
        cost_estimate=SMALL,
        name="norm_back",
    )(place, sums, came, hidden, scale, gains)


def norm_back_end_kernel(grad_ref, own_ref, other_ref, hidden_ref, scale_ref, gains_ref, out_grad_ref, hidden_grad_ref, rounded_ref):
    scale = scale_ref[...]
    mean = (own_ref[...] + other_ref[...]) * (1.0 / D)
    result = out_grad_ref[...].astype(F32) + scale * (grad_ref[...] * gains_ref[1:2, :])
    result = result - hidden_ref[...] * (scale * scale * scale * mean)
    hidden_grad_ref[...] = result
    rounded_ref[...] = result.astype(BF16)


def norm_back_end(grad, products, products_c, hidden, scale, gains, out_grad):
    rows, features = hidden.shape
    tile = pl.BlockSpec((TOKEN_TILE, features), lambda i: (i, 0))
    column = pl.BlockSpec((TOKEN_TILE, 1), lambda i: (i, 0))
    return pl.pallas_call(
        norm_back_end_kernel,
        grid=(rows // TOKEN_TILE,),
        in_specs=[tile, column, column, tile, column, pl.BlockSpec(gains.shape, lambda i: (0, 0)), tile],
        out_specs=[tile, tile],
        out_shape=[
            jax.ShapeDtypeStruct((rows, features), F32),
            jax.ShapeDtypeStruct((rows, features), BF16),
        ],
        compiler_params=params(48, "arbitrary"),
        cost_estimate=SMALL,
        name="norm_back_end",
    )(grad, products, products_c, hidden, scale, gains, out_grad)


def ring_of(size):
    return list(range(0, size, 2)) + list(range(1, size, 2))[::-1]


def unpack_kernel(aliased, plan_ref, *refs):
    chunks = refs[0:2]
    gate_ref, up_ref, down_ref = refs[2 + aliased : 5 + aliased]
    blocks = chunks[0].shape[1] // LANES

    def write(chunk_ref):
        gate_ref[0] = chunk_ref[0, :, 0:LANES].astype(F32)
        up_ref[0] = chunk_ref[0, :, LANES : 2 * LANES].astype(F32)
        for b in range(blocks):
            at = slice(b * LANES, (b + 1) * LANES)
            down_ref[0, :, at] = chunk_ref[0, at, 2 * LANES :].astype(F32)

    for k in range(2):
        pl.when(pl.program_id(1) == k)(lambda k=k: write(chunks[k]))


def unpack(plan, first, wave, chunks, shapes, outs):
    count, rows, width = chunks[0].shape
    chunk = pl.BlockSpec((1, rows, width), lambda i, d, n: (i, 0, 0))

    def place(i, d, n):
        block = n[n.shape[0] - 1]
        return n[first + 2 * i + d], 1 - block if wave else block

    def wide(i, d, n):
        expert, block = place(i, d, n)
        return (expert, 0, block)

    def low(i, d, n):
        expert, block = place(i, d, n)
        return (expert, block, 0)

    aliased = len(outs)
    return pl.pallas_call(
        functools.partial(unpack_kernel, aliased),
        grid_spec=pltpu.PrefetchScalarGridSpec(
            num_scalar_prefetch=1,
            grid=(count, 2),
            in_specs=[chunk, chunk] + [pl.BlockSpec(memory_space=pl.ANY)] * aliased,
            out_specs=[
                pl.BlockSpec((1, rows, LANES), wide),
                pl.BlockSpec((1, rows, LANES), wide),
                pl.BlockSpec((1, LANES, rows), low),
            ],
        ),
        out_shape=[jax.ShapeDtypeStruct(shape, F32) for shape in shapes],
        input_output_aliases={3 + k: k for k in range(aliased)},
        compiler_params=params(16, "arbitrary", "arbitrary"),
        cost_estimate=SMALL,
        name="unpack",
    )(plan, *chunks, *outs)


def ring_sum_kernel(came_ref, mine_ref, *outs):
    total = (came_ref[...].astype(F32) + mine_ref[...].astype(F32)).astype(BF16)
    if len(outs) == 1:
        outs[0][...] = total
    else:
        half = pl.program_id(1) // (pl.num_programs(1) // 2)
        for k, out_ref in enumerate(outs):

            @pl.when(half == k)
            def _(out_ref=out_ref):
                out_ref[...] = total


def ring_sum(came, mine, halved):
    count, rows, lanes = came.shape
    tiles = 4
    spec = pl.BlockSpec((1, rows // tiles, lanes), lambda i, j: (i, j, 0))

    def half(k):
        first = k * tiles // 2
        last = tiles // 2 - 1
        return pl.BlockSpec(
            (1, rows // tiles, lanes), lambda i, j: (i, jnp.clip(j - first, 0, last), 0)
        )

    shapes = [jax.ShapeDtypeStruct((count, rows // 2, lanes), BF16)] * 2
    return pl.pallas_call(
        ring_sum_kernel,
        grid=(count, tiles),
        in_specs=[spec, spec],
        out_specs=[half(0), half(1)] if halved else spec,
        out_shape=shapes if halved else jax.ShapeDtypeStruct(came.shape, BF16),
        compiler_params=params(16, "arbitrary", "arbitrary"),
        cost_estimate=SMALL,
        name="ring_sum",
    )(came, mine)


def late_chunk_kernel(came, plan_ref, pack_ref, *refs):
    values = pack_ref[:, 0]
    if came:
        values = (refs[0][...].astype(F32) + values.astype(F32)).astype(BF16)
    outs = refs[came:]
    if len(outs) == 1:
        outs[0][...] = values
    else:
        for k, out_ref in enumerate(outs):
            out_ref[...] = values[k]


def late_chunk(plan, at, pack, came, halved):
    halves, _, rows, lanes = pack.shape
    spec = pl.BlockSpec((halves, rows, lanes), lambda i, n: (0, 0, 0))
    half = pl.BlockSpec((rows, lanes), lambda i, n: (0, 0))
    halfs = [jax.ShapeDtypeStruct((rows, lanes), BF16)] * 2
    return pl.pallas_call(
        functools.partial(late_chunk_kernel, len(came)),
        grid_spec=pltpu.PrefetchScalarGridSpec(
            num_scalar_prefetch=1,
            grid=(1,),
            in_specs=[pl.BlockSpec((halves, 1, rows, lanes), lambda i, n: (0, n[at], 0, 0))]
            + [spec] * len(came),
            out_specs=[half] * 2 if halved else spec,
        ),
        out_shape=halfs if halved else jax.ShapeDtypeStruct((halves, rows, lanes), BF16),
        compiler_params=params(16, "arbitrary"),
        cost_estimate=SMALL,
        name="late_chunk",
    )(plan, pack, *came)


def late_join_kernel(col_ref, own_ref, other_ref, gains_ref, out_ref):
    rows = own_ref.shape[0]
    features = gains_ref.shape[1]
    out_ref[pl.ds(pl.multiple_of(col_ref[0] * rows, rows), rows), :] = own_ref[...]
    out_ref[pl.ds(pl.multiple_of((1 - col_ref[0]) * rows, rows), rows), :] = other_ref[...]
    out_ref[2 * rows :, :] = jnp.zeros((GAIN_ROWS, own_ref.shape[1]), BF16)
    pad = jnp.zeros((GAIN_ROWS - 2, features), F32)
    out_ref[2 * rows :, 0:features] = jnp.concatenate([gains_ref[...], pad], axis=0).astype(BF16)


def late_join(col, own, other, gains):
    rows, lanes = own.shape
    spec = pl.BlockSpec(memory_space=pltpu.VMEM)
    return pl.pallas_call(
        late_join_kernel,
        out_shape=jax.ShapeDtypeStruct((2 * rows + GAIN_ROWS, lanes), BF16),
        in_specs=[pl.BlockSpec(memory_space=pltpu.SMEM)] + [spec] * 3,
        out_specs=spec,
        compiler_params=params(16),
        cost_estimate=SMALL,
        name="late_join",
    )(col, own, other, gains)


def unpack_late_kernel(first_step, steps, plan_ref, *refs):
    chunks = refs[0 : 2 * steps]
    sgate, sup, sdown, query, key, value, out, gains, all_ref, gain_ref = refs[2 * steps :]
    rows, features = (chunks[0].shape[0] - GAIN_ROWS) // 2, all_ref.shape[2]
    for k in range(2):
        for step in range(steps):
            at = plan_ref[first_step + 2 * step + k] * rows
            for c in range(2):
                all_ref[k, c, pl.ds(pl.multiple_of(at, rows), rows), :] = chunks[
                    steps * k + step
                ][c * rows : (c + 1) * rows, :]
    for step in range(steps):
        at = plan_ref[first_step + 2 * step] * GAIN_ROWS
        gain_ref[pl.ds(pl.multiple_of(at, GAIN_ROWS), GAIN_ROWS), :] = chunks[step][2 * rows :, :]
    total = jnp.zeros((GAIN_ROWS, features), F32)
    for step in range(steps):
        rows_of = slice(step * GAIN_ROWS, (step + 1) * GAIN_ROWS)
        total = total + gain_ref[rows_of, 0:features].astype(F32)
    gains[...] = total[0:2]
    flipped = plan_ref[plan_ref.shape[0] - 1] != 0
    for c in range(2):
        for b in range(14):
            lanes = slice(b % 7 * LANES, (b % 7 + 1) * LANES)
            first, second = all_ref[0, c, :, lanes], all_ref[1, c, :, lanes]
            if b >= 7:
                first, second = second, first
            block = jnp.where(flipped, second, first).astype(F32)
            if b < 6:
                at = slice((2 * c + b // 3) * LANES, (2 * c + b // 3 + 1) * LANES)
                if b % 3 < 2:
                    (sgate, sup)[b % 3][:, at] = block
                else:
                    for k in range(features // LANES):
                        here = slice(k * LANES, (k + 1) * LANES)
                        sdown[at, here] = block[here, :]
            elif b < 9:
                at = (GROUP_HEADS * c + b - 6) * LANES
                query[:, at : at + LANES] = block
            elif b < 11:
                (key, value)[b - 9][:, c * LANES : (c + 1) * LANES] = block
            else:
                at = (GROUP_HEADS * c + b - 11) * LANES
                out[at : at + LANES, :] = block.T


def unpack_late(plan, first_step, chunks, shapes):
    steps = len(chunks[0])
    rows, lanes = (chunks[0][0].shape[0] - GAIN_ROWS) // 2, chunks[0][0].shape[1]
    spec = pl.BlockSpec(memory_space=pltpu.VMEM)
    return pl.pallas_call(
        functools.partial(unpack_late_kernel, first_step, steps),
        in_specs=[pl.BlockSpec(memory_space=pltpu.SMEM)] + [spec] * (2 * steps),
        out_specs=[spec] * len(shapes),
        out_shape=[jax.ShapeDtypeStruct(shape, F32) for shape in shapes],
        scratch_shapes=[
            pltpu.VMEM((2, 2, steps * rows, lanes), BF16),
            pltpu.VMEM((steps * GAIN_ROWS, lanes), BF16),
        ],
        compiler_params=params(48),
        cost_estimate=SMALL,
        name="unpack_late",
    )(plan, *chunks[0], *chunks[1])


def plans(ring, each):
    size = len(ring)
    rows = []
    for member in range(size):
        place = ring.index(member)
        for col in range(2):
            chunks = []
            for step in range(2 * size - 1):
                for which in range(2):
                    sign = 1 if which == col else -1
                    chunks.append((place - sign * step) % size)
            experts = []
            for start in (0, size - 1):
                for step in range(start, start + size):
                    for k in range(each):
                        for which in range(2):
                            second = col if which == 0 else 1 - col
                            experts.append(2 * each * chunks[2 * step + which] + each * second + k)
            rows.append(experts + chunks + [col])
    return np.asarray(rows, np.int32)


def body(
    tokens_in,
    norm_gain_attn,
    w_query,
    w_key,
    w_value,
    w_out,
    norm_gain_ffn,
    w_gate,
    w_up,
    w_down,
    w_shared_gate,
    w_shared_up,
    w_shared_down,
    routes,
    gate_weights,
    seq_lengths,
    out_grad,
):
    row = lax.axis_index("row")
    col = lax.axis_index("col")
    dp = lax.axis_index("dp")
    dp_size = lax.axis_size("dp")
    local_rows, local_features = tokens_in.shape
    experts = w_gate.shape[0]
    group_width = GROUP_HEADS * DH
    col_ref = col.reshape(1)

    ring_size = min(8, dp_size)
    ring = ring_of(ring_size)
    starts = range(0, dp_size, ring_size)
    rights = [
        (g + ring[k], g + ring[(k + 1) % ring_size]) for g in starts for k in range(ring_size)
    ]
    lefts = [(b, a) for a, b in rights]
    routes_of = [
        [(2 * a, 2 * b) for a, b in ways[0]] + [(2 * a + 1, 2 * b + 1) for a, b in ways[1]]
        for ways in ((rights, lefts), (lefts, rights))
    ]
    experts_each = experts // (2 * ring_size)
    plan = jnp.asarray(plans(ring, experts_each))
    plan = lax.dynamic_slice(
        plan, (2 * (dp % ring_size) + col, jnp.int32(0)), (1, plan.shape[1])
    ).reshape(-1)

    def send(values, which):
        if ring_size == 1:
            return values
        return lax.ppermute(values, ("dp", "col"), routes_of[which])

    def chunk_at(step, which):
        return plan[2 * experts + 2 * step + which]

    def across_rings(values):
        if len(starts) == 1:
            return values
        peers = [[g + k for g in starts] for k in range(ring_size)]
        return lax.psum(values, "dp", axis_index_groups=peers)

    where = jnp.stack([row, seq_lengths[0], col])
    tokens_y = swap(tokens_in, "row")
    tokens_c = swap(tokens_in, "col")
    count = min(ring_size, 4)
    member = dp % count
    there, out_y = their_columns(
        jnp.stack([col, member]), w_query, w_key, w_value, w_out, count
    )
    gains = jnp.stack([norm_gain_attn, norm_gain_ffn])
    there = swap(there, "col")
    gains_c = swap(gains, "col")

    def project_half(own, other):
        return project(col_ref, own, other, gains, gains_c, w_query, w_key, w_value, there)

    near = project_half(tokens_in, tokens_c)
    gate_c = swap(w_gate, "col")
    out_y = swap(out_y, "row")
    tokens_y = after(tokens_y, near[2], out_y)
    tokens_yc = swap(tokens_y, "col")
    grad_y = swap(after(out_grad, tokens_y), "row")
    far = project_half(tokens_y, tokens_yc)
    shares = [out_y]
    for k in range(1, count):
        part = out_y if k < 3 else after(out_y, far[2])
        shares.append(lax.ppermute(part, "dp", [(m, m ^ k) for m in range(dp_size)]))
    where = after(where, grad_y, *shares)

    w_sgate, w_sup, w_sdown = w_shared_gate[None], w_shared_up[None], w_shared_down[None]
    up_c = swap(after(w_up, gate_c, tokens_yc), "col")

    attended = attend(where, near[2], far[2])
    attended_y = swap(attended, "row")
    attended_c = swap(attended, "col")
    out_c = swap(after(w_out, tokens_yc), "col")
    before = hidden_before(
        where,
        [tokens_in, tokens_c, tokens_y, tokens_yc],
        [attended, attended_c],
        w_out,
        out_c,
    )
    down_c = swap(after(w_down, tokens_yc), "col")
    attended_y = after(attended_y, before[0])
    out_y = join(member, *shares)
    out_yc = swap(out_y, "col")
    attended_yc = swap(attended_y, "col")
    grad_own = join(row, out_grad, grad_y)
    grad_other = swap(grad_own, "col")
    hidden, x_own, x_other, scale_ffn = hidden_after(
        where, before, [attended_y, attended_yc], out_y, out_yc, gains, gains_c
    )
    sgate_c, sup_c, sdown_c = (
        swap(after(w, attended_yc), "col") for w in (w_sgate, w_sup, w_sdown)
    )

    choices = jnp.arange(experts, dtype=jnp.int32)[:, None]
    dense = sum(
        jnp.where(routes[:, k][None, :] == choices, gate_weights[:, k][None, :], 0.0)
        for k in range(routes.shape[1])
    )
    gates = []
    for _ in range(3):
        gates.append(lax.reduce_precision(dense, 8, 7))
        dense = dense - gates[-1]
    gates = jnp.concatenate(gates, axis=0).astype(BF16)

    each = experts_each
    order = plan
    pairs_total = experts // 2
    routed = [w_gate, w_up, gate_c, up_c, w_down, down_c]
    shared = [w_sgate, w_sup, sgate_c, sup_c, w_sdown, sdown_c]

    def run(first, last, order, kept):
        return expert_grads(
            order,
            first,
            last,
            pairs_total,
            [x_own, x_other],
            [grad_own, grad_other],
            gates,
            routed,
            kept,
        )

    first = run(0, each, order, ())
    kept = first[2:]
    sums = [first[0], first[1]]
    runs = {}
    mixed = {}
    normed = {}

    def work_experts(first, last):
        def work(order, ties):
            nonlocal kept
            result = run(first, last, order, tuple(kept))
            kept = result[2:]
            runs[first] = result[0:2]
            return [kept[0]]

        return work

    def work_shared(order, ties):
        runs["shared"] = expert_grads(
            order, 0, 1, None, [x_own, x_other], [grad_own, grad_other], gates, shared, ()
        )
        return [runs["shared"][2]]

    def work_back(half):
        def work(order, ties):
            mixed[True, half] = mix(
                True,
                BF16 if half else F32,
                order,
                kept[0],
                runs["shared"][2],
                routed[2 * half : 2 * half + 2],
                shared[2 * half : 2 * half + 2],
            )
            if half:
                normed["other"] = swap(mixed[True, 1], "col")
                return [mixed[True, 1]]
            normed["sum"] = chip_sum(mixed[True, 0], normed["other"])
            normed["came"] = swap(normed["sum"][1], "row")
            return [mixed[True, 0]]

        return work

    def work_out(half):
        def work(order, ties):
            mixed[False, half] = mix(
                False,
                BF16 if half else F32,
                order,
                kept[1],
                runs["shared"][3],
                routed[4 + half : 5 + half],
                shared[4 + half : 5 + half],
            )
            return [mixed[False, half]] + ([] if half else [normed["sum"][1]])

        return work

    start = row * local_rows

    def my_rows(values):
        return lax.dynamic_slice_in_dim(values, start, local_rows, axis=0)

    def their_rows(values):
        return lax.dynamic_slice_in_dim(values, local_rows - start, local_rows, axis=0)

    def work_hidden(order, ties):
        grads, products, normed["gain"] = norm_back(
            after(where, *ties), normed["sum"][0], normed["came"], hidden, scale_ffn, gains
        )
        products_c = swap(products, "col")
        normed["hidden"], normed["grad"] = norm_back_end(
            grads, products, products_c, hidden, scale_ffn, gains, grad_own
        )
        normed["grad_c"] = swap(normed["grad"], "col")
        return [normed["grad"]]

    def work_attend(order, ties):
        normed["qkv"] = attend_back(
            after(where, *ties), near[2], far[2], normed["grad"], normed["grad_c"], w_out, out_c
        )
        return [normed["qkv"]]

    def work_late(order, ties):
        normed["packs"] = late_grads(
            after(where, *ties),
            near[0:2],
            far[0:2],
            normed["qkv"],
            attended,
            normed["grad"],
            normed["grad_c"],
            runs["shared"][0:2],
        )
        return normed["packs"]

    tasks = [work_experts(at, at + each) for at in range(each, pairs_total, each)]
    tasks += [work_shared, work_back(1), work_back(0), work_out(1), work_out(0)]
    later = [work_hidden, work_attend, work_late]
    got = [None, None]
    if ring_size > 1:
        got[0] = send(sums[0], 0)
        tasks.pop(0)(after(order, *sums), sums)
        got[1] = send(after(sums[1], kept[0]), 1)
    for s in range(1, ring_size):
        for k in range(2):
            last = sums
            task = tasks.pop(0) if tasks else None
            if task:
                last = task(after(order, *last), last)
            sums[k] = ring_sum(after(got[k], *last), runs[each * s][k], s + 1 == ring_size)
            if s + 1 < ring_size:
                got[k] = send(sums[k], k)
            else:
                sums[k], got[k] = sums[k]
    for task in tasks:
        if task:
            task(after(order, *sums), sums)
    if ring_size == 1:
        got = [total[:, local_features:] for total in sums]
        sums = [total[:, :local_features] for total in sums]
    waves = [[across_rings(total) for total in sums]]
    crossed = [swap(across_rings(total), "col") for total in got]
    waves.append([crossed[1], crossed[0]])

    chunks_first = 2 * experts
    late_total = 2 * (ring_size - 1)
    packs, late = [None, None], [None, None]

    def late_begin():
        for k in range(2):
            pack = normed["packs"][k]
            packs[k] = pack.reshape(2, ring_size, local_features // ring_size, pack.shape[2])
            late[k] = late_chunk(plan, chunks_first + k, packs[k], (), late_total == 0)

    def back_to_tokens(ties):
        hidden_grad = normed["hidden"]
        qkv_grad = after(normed["qkv"], *ties)
        ffn_sum = mixed[False, 0] + swap(mixed[False, 1], "col").astype(F32)
        ffn_rows = my_rows(ffn_sum) + swap(their_rows(ffn_sum).astype(BF16), "row").astype(F32)
        block_out = (my_rows(hidden) + ffn_rows).astype(BF16)
        here = jnp.concatenate(
            [halves(w, 1, col)[0] for w in (w_query, w_key, w_value)], axis=1
        )
        tokens_back = dot_nt(qkv_grad, here) + swap(
            dot_nt(qkv_grad, there).astype(BF16), "col"
        ).astype(F32)
        tokens_back = my_rows(tokens_back) + swap(
            their_rows(tokens_back).astype(BF16), "row"
        ).astype(F32)
        scale_attn = near[3]
        tokens_f32 = tokens_in.astype(F32)
        gain_attn_part = jnp.sum(tokens_back * tokens_f32 * scale_attn, axis=0)
        scaled = tokens_back * norm_gain_attn
        products = jnp.sum(scaled * tokens_f32, axis=1, keepdims=True)
        mean = (products + swap(products, "col")) / D
        tokens_grad = (
            my_rows(hidden_grad) + scale_attn * scaled - tokens_f32 * scale_attn**3 * mean
        ).astype(BF16)

        gain_parts = jnp.concatenate([gain_attn_part[None], normed["gain"]], axis=0)
        normed["gains"] = across_rings(gain_parts + swap(gain_parts, "row"))
        normed["outs"] = (block_out, tokens_grad)

    def gain_sums():
        return normed["gains"]

    late_out = [[], []]
    late_done = 0

    def late_turn():
        owns = [across_rings(values[0]) for values in late]
        others = [swap(across_rings(values[1]), "col") for values in late]
        for k in range(2):
            late[k] = late_join(col_ref, owns[k], others[1 - k], gain_sums())
            late_out[k].append(late[k])

    def late_finish(k, values):
        if late_done < ring_size:
            at = chunks_first + 2 * late_done + k
            late[k] = late_chunk(plan, at, packs[k], (values,), late_done == ring_size - 1)
        else:
            late[k] = values
            late_out[k].append(values)

    shapes = [w_gate.shape, w_up.shape, w_down.shape]
    placed = ()

    def place_chunks(wave, step, chunks, placed):
        return unpack(plan, experts + 2 * each * step, wave, chunks, shapes, placed)

    steps = ring_size - 1
    late_got = None
    last = []
    got = list(waves[0])
    for number in range(2 * steps - 1):
        wave, step = (0, number) if number < steps else (1, number - steps + 1)
        if number == steps:
            came = got
            got = early
        chunks = [None, None]
        for k in range(2):
            chunks[k] = after(got[k], *last) if last else got[k]
            got[k] = send(chunks[k], k)
            last = [chunks[k]]
        if number == 0:
            early = [send(after(waves[1][k], *chunks), k) for k in range(2)]
        if late_got is not None:
            late_done += 1
            for k in range(2):
                late_finish(k, after(late_got[k], *last))
                last = list(late[k]) if late_done == ring_size - 1 else [late[k]]
            if late_done == ring_size - 1:
                late_turn()
        if number < len(later):
            last = later[number](after(order, *last), last)
        late_got = None
        if number + 1 >= len(later) and late_done < late_total:
            if late_done == 0:
                late_begin()
            late_got = [send(late[k], k) for k in range(2)]
        if number == steps:
            placed = place_chunks(0, steps, came, placed)
            placed = place_chunks(1, 0, waves[1], placed)
        placed = place_chunks(wave, step, [after(chunks[0], *last), chunks[1]], placed)
        last = placed[0:1]
        if number == 3:
            back_to_tokens(last)
    if steps:
        placed = place_chunks(1, steps, [after(got[k], *last) for k in range(2)], placed)
        last = placed[0:1]
    else:
        for work in later:
            work(order, ())
        late_begin()
        back_to_tokens(())
        late_turn()
    while late_got is not None:
        late_done += 1
        for k in range(2):
            late_finish(k, after(late_got[k], *last))
        if late_done == ring_size - 1:
            late_turn()
        late_got = [send(late[k], k) for k in range(2)] if late_done < late_total else None
    if not steps:
        for wave in range(2):
            placed = place_chunks(wave, 0, waves[wave], placed)
    gate_grad, up_grad, down_grad = placed
    shapes = [w.shape for w in (w_shared_gate, w_shared_up, w_shared_down)]
    shapes += [w.shape for w in (w_query, w_key, w_value, w_out)] + [gains.shape]
    finals = unpack_late(plan, chunks_first + late_total, late_out, shapes)
    shared_gate_grad, shared_up_grad, shared_down_grad = finals[0:3]
    query_grad, key_grad, value_grad, out_proj_grad, gain_grads = finals[3:8]


    return (
        *normed["outs"],
        gain_grads[0],
        query_grad,
        key_grad,
        value_grad,
        out_proj_grad,
        gain_grads[1],
        gate_grad,
        up_grad,
        down_grad,
        shared_gate_grad,
        shared_up_grad,
        shared_down_grad,
    )


def solution(mesh):
    in_specs = (
        P(("dp", "row"), "col"),
        P("col"),
        P("col", "row"),
        P("col", "row"),
        P("col", "row"),
        P("row", "col"),
        P("col"),
        P(None, "col", "row"),
        P(None, "col", "row"),
        P(None, "row", "col"),
        P("col", "row"),
        P("col", "row"),
        P("row", "col"),
        P("dp", None),
        P("dp", None),
        P("dp"),
        P(("dp", "row"), "col"),
    )
    out_specs = (
        P(("dp", "row"), "col"),
        P(("dp", "row"), "col"),
        P("col"),
        P("col", "row"),
        P("col", "row"),
        P("col", "row"),
        P("row", "col"),
        P("col"),
        P(None, "col", "row"),
        P(None, "col", "row"),
        P(None, "row", "col"),
        P("col", "row"),
        P("col", "row"),
        P("row", "col"),
    )
    return jax.shard_map(body, mesh=mesh, in_specs=in_specs, out_specs=out_specs, check_vma=False)
```

```python
import functools

import jax
import jax.numpy as jnp
import numpy as np
from jax import lax
from jax.experimental import pallas as pl
from jax.experimental.pallas import tpu as pltpu
from jax.sharding import PartitionSpec as P

D = 1536
HQ = 12
HK = 4
DH = 128
GROUP_HEADS = HQ // HK
LANES = 128

EPSILON = 1e-05
F32 = jnp.float32
BF16 = jnp.bfloat16
MIB = 1024 * 1024
GAIN_ROWS = 16
RING = 8
LATE_BLOCKS = 5
SMALL = pl.CostEstimate(flops=0, bytes_accessed=0, transcendentals=0)


def params(mib, *semantics):
    return pltpu.CompilerParams(
        dimension_semantics=semantics or None, vmem_limit_bytes=mib * MIB
    )


def dot(left, right):
    return jnp.dot(left, right, preferred_element_type=F32)


def dot_nt(left, right):
    return lax.dot_general(left, right, (((1,), (1,)), ((), ())), preferred_element_type=F32)


def dot_tn(left, right):
    return lax.dot_general(left, right, (((0,), (0,)), ((), ())), preferred_element_type=F32)


def after(values, *others):
    return lax.optimization_barrier((values, *others))[0]


def swap(values, axis):
    return lax.ppermute(values, axis, [(0, 1), (1, 0)])


def halves(values, axis, mine):
    size = values.shape[axis] // 2
    low = lax.slice_in_dim(values, 0, size, axis=axis)
    high = lax.slice_in_dim(values, size, 2 * size, axis=axis)
    return jnp.where(mine == 0, low, high), jnp.where(mine == 0, high, low)


def in_order(own, other, mine, axis):
    return jnp.concatenate(
        [jnp.where(mine == 0, own, other), jnp.where(mine == 0, other, own)], axis=axis
    )


def gather_rows(place_ref, own_ref, other_ref, all_ref):
    row = place_ref[0]
    rows = own_ref.shape[0]
    all_ref[pl.ds(pl.multiple_of(row * rows, rows), rows), :] = own_ref[...]
    all_ref[pl.ds(pl.multiple_of((1 - row) * rows, rows), rows), :] = other_ref[...]


def head_rows(ref, first, block):
    return jnp.concatenate(
        [ref[first : first + block, h * DH : (h + 1) * DH] for h in range(GROUP_HEADS)], axis=0
    )


def key_probs(query, key, first, length):
    block, keys = query.shape[0] // GROUP_HEADS, key.shape[0]
    scores = dot_nt(query, key) * DH ** (-0.5)
    shape = (block, keys)
    query_at = lax.broadcasted_iota(jnp.int32, shape, 0) + first
    key_at = lax.broadcasted_iota(jnp.int32, shape, 1)
    allowed = (key_at <= query_at) & (key_at < length)
    allowed = jnp.concatenate([allowed] * GROUP_HEADS, axis=0)
    scores = jnp.where(allowed, scores, -1e30)
    weights = jnp.exp(scores - jnp.max(scores, axis=1, keepdims=True))
    return weights * (1.0 / jnp.sum(weights, axis=1, keepdims=True))


def attend_kernel(place_ref, own_ref, other_ref, out_ref, all_ref):
    gather_rows(place_ref, own_ref, other_ref, all_ref)
    rows = own_ref.shape[0]
    block = 256
    width = GROUP_HEADS * DH
    for at in range(2 * rows // block):
        first, keys = at * block, (at + 1) * block
        query = head_rows(all_ref, first, block)
        key = all_ref[0:keys, width : width + DH]
        value = all_ref[0:keys, width + DH : width + 2 * DH]
        probs = key_probs(query, key, first, place_ref[1])
        result = dot(probs.astype(BF16), value).astype(BF16)
        for h in range(GROUP_HEADS):
            out_ref[first : first + block, h * DH : (h + 1) * DH] = result[
                h * block : (h + 1) * block
            ]


def attend(place, own, other):
    rows, width = own.shape
    spec = pl.BlockSpec(memory_space=pltpu.VMEM)
    return pl.pallas_call(
        attend_kernel,
        out_shape=jax.ShapeDtypeStruct((2 * rows, GROUP_HEADS * DH), BF16),
        in_specs=[pl.BlockSpec(memory_space=pltpu.SMEM), spec, spec],
        out_specs=spec,
        scratch_shapes=[pltpu.VMEM((2 * rows, width), BF16)],
        compiler_params=params(32),
        cost_estimate=SMALL,
        name="attend",
    )(place, own, other)


def attend_back_kernel(
    place_ref, own_ref, other_ref, grad_ref, grad_c_ref, out_ref, out_c_ref, result_ref, all_ref, total_ref
):
    gather_rows(place_ref, own_ref, other_ref, all_ref)
    rows = own_ref.shape[0]
    block = 256
    width = GROUP_HEADS * DH
    group = pl.ds(pl.multiple_of(place_ref[2] * width, width), width)
    blocks = 2 * rows // block
    for at in reversed(range(blocks)):
        first, keys = at * block, (at + 1) * block
        query = head_rows(all_ref, first, block)
        key = all_ref[0:keys, width : width + DH]
        value = all_ref[0:keys, width + DH : width + 2 * DH]
        probs = key_probs(query, key, first, place_ref[1])
        grad = dot_nt(grad_ref[first:keys, :], out_ref[group, :])
        grad = (grad + dot_nt(grad_c_ref[first:keys, :], out_c_ref[group, :])).astype(BF16)
        grad = jnp.concatenate(
            [grad[:, h * DH : (h + 1) * DH] for h in range(GROUP_HEADS)], axis=0
        )
        probs_grad = dot_nt(grad, value)
        carried = jnp.sum(probs * probs_grad, axis=1, keepdims=True)
        score_grad = (probs * (probs_grad - carried)).astype(BF16)
        query_back = (dot(score_grad, key) * DH ** (-0.5)).astype(BF16)
        for h in range(GROUP_HEADS):
            result_ref[first:keys, h * DH : (h + 1) * DH] = query_back[
                h * block : (h + 1) * block
            ]
        key_back = dot_tn(score_grad, query)
        value_back = dot_tn(probs.astype(BF16), grad)
        if at == blocks - 1:
            total_ref[:, 0:DH] = key_back
            total_ref[:, DH:] = value_back
        else:
            total_ref[0:keys, 0:DH] += key_back
            total_ref[0:keys, DH:] += value_back
    result_ref[:, width : width + DH] = (total_ref[:, 0:DH] * DH ** (-0.5)).astype(BF16)
    result_ref[:, width + DH :] = total_ref[:, DH:].astype(BF16)


def attend_back(place, own, other, grad, grad_c, w_out, out_c):
    rows, width = own.shape
    spec = pl.BlockSpec(memory_space=pltpu.VMEM)
    return pl.pallas_call(
        attend_back_kernel,
        out_shape=jax.ShapeDtypeStruct((2 * rows, width), BF16),
        in_specs=[pl.BlockSpec(memory_space=pltpu.SMEM)] + [spec] * 6,
        out_specs=spec,
        scratch_shapes=[
            pltpu.VMEM((2 * rows, width), BF16),
            pltpu.VMEM((2 * rows, 2 * DH), F32),
        ],
        compiler_params=params(60),
        cost_estimate=SMALL,
        name="attend_back",
    )(place, own, other, grad, grad_c, w_out, out_c)


def unit_slices(unit, share):
    row, lane = divmod(unit, 3)
    return slice(row * share, (row + 1) * share), slice(lane * LANES, (lane + 1) * LANES)


def late_kernel(place_ref, *refs):
    near, near_c, far, far_c, qkv_ref, attended_ref, grad_ref, grad_c_ref = refs[0:8]
    shared = refs[8:10]
    outs = refs[10:12]
    rows, features = near.shape
    own_rows = pl.ds(pl.multiple_of(place_ref[0] * rows, rows), rows)
    far_rows = pl.ds(pl.multiple_of((1 - place_ref[0]) * rows, rows), rows)
    split = 7 * LANES

    chunks = outs[0].shape[0]
    share = features // chunks

    def store(h, at, values):
        values = values.astype(BF16)
        for b in range(values.shape[1] // LANES):
            part, unit = divmod(at // LANES + b, split // LANES)
            to_rows, to_lanes = unit_slices(h * (split // LANES) + unit, share)

            def write(out_ref, b=b, to_rows=to_rows, to_lanes=to_lanes):
                for chunk in range(chunks):
                    out_ref[chunk, to_rows, to_lanes] = values[
                        chunk * share : (chunk + 1) * share, b * LANES : (b + 1) * LANES
                    ]

            pl.when(place_ref[2] == 0)(lambda part=part, write=write: write(outs[part]))
            pl.when(place_ref[2] != 0)(lambda part=part, write=write: write(outs[1 - part]))

    for out_ref in outs:
        to_rows, to_lanes = unit_slices(2 * (split // LANES), share)
        for chunk in range(chunks):
            out_ref[chunk, to_rows, to_lanes] = jnp.zeros((share, LANES), BF16)

    for h, (x, y, grad) in enumerate(((near, far, grad_ref), (near_c, far_c, grad_c_ref))):
        for k in range(2):
            store(h, 3 * LANES * k, shared[k][0, h * features : (h + 1) * features, :])
        project = dot_tn(x[...], qkv_ref[own_rows, :]) + dot_tn(y[...], qkv_ref[far_rows, :])
        store(h, 6 * LANES, project)
        store(h, 11 * LANES, dot_tn(grad[...], attended_ref[...]))


def late_grads(place, near, far, qkv_grad, attended, grad, grad_c, shared):
    features = near[0].shape[1]
    rows = LATE_BLOCKS * (features // RING)
    spec = pl.BlockSpec(memory_space=pltpu.VMEM)
    return pl.pallas_call(
        late_kernel,
        out_shape=[jax.ShapeDtypeStruct((RING, rows, 3 * LANES), BF16)] * 2,
        in_specs=[pl.BlockSpec(memory_space=pltpu.SMEM)] + [spec] * 10,
        out_specs=[spec] * 2,
        compiler_params=params(60),
        cost_estimate=SMALL,
        name="late_grads",
    )(place, *near, *far, qkv_grad, attended, grad, grad_c, *shared)


def columns_kernel(
    place_ref, query_ref, key_ref, value_ref, w_out_ref, out_ref, share_ref
):
    share_ref[...] = w_out_ref[...]
    width = GROUP_HEADS * DH
    out_ref[:, 0:width] = query_ref[...]
    out_ref[:, width : width + DH] = key_ref[...]
    out_ref[:, width + DH :] = value_ref[...]


def their_columns(place, w_query, w_key, w_value, w_out, shares):
    rows = w_query.shape[0]
    width = GROUP_HEADS * DH + 2 * DH

    def theirs(width):
        return pl.BlockSpec((rows, width), lambda i, c: (0, 1 - c[0]))

    return pl.pallas_call(
        columns_kernel,
        grid_spec=pltpu.PrefetchScalarGridSpec(
            num_scalar_prefetch=1,
            grid=(1,),
            in_specs=[theirs(GROUP_HEADS * DH), theirs(DH), theirs(DH)]
            + [pl.BlockSpec((rows // shares, rows), lambda i, c: (c[1], 0))],
            out_specs=[
                pl.BlockSpec((rows, width), lambda i, c: (0, 0)),
                pl.BlockSpec((rows // shares, rows), lambda i, c: (0, 0)),
            ],
        ),
        out_shape=[
            jax.ShapeDtypeStruct((rows, width), BF16),
            jax.ShapeDtypeStruct((rows // shares, rows), BF16),
        ],
        compiler_params=params(60, "arbitrary"),
        cost_estimate=SMALL,
        name="their_columns",
    )(place, w_query, w_key, w_value, w_out)


def join_kernel(mine_ref, *refs):
    *parts, out_ref = refs
    rows = parts[0].shape[0]
    for k, part in enumerate(parts):
        at = jnp.bitwise_xor(mine_ref[0], k)
        out_ref[pl.ds(pl.multiple_of(at * rows, rows), rows), :] = part[...]


def join(mine, *parts):
    rows, width = parts[0].shape
    spec = pl.BlockSpec(memory_space=pltpu.VMEM)
    return pl.pallas_call(
        join_kernel,
        out_shape=jax.ShapeDtypeStruct((len(parts) * rows, width), parts[0].dtype),
        in_specs=[pl.BlockSpec(memory_space=pltpu.SMEM)] + [spec] * len(parts),
        out_specs=spec,
        compiler_params=params(16),
        cost_estimate=SMALL,
        name="join",
    )(mine.reshape(1), *parts)


def project_kernel(col_ref, own_ref, other_ref, gains_ref, gains_c_ref, query_ref, key_ref, value_ref, there_ref, x_own_ref, x_other_ref, qkv_ref, scale_ref):
    own = own_ref[...].astype(F32)
    other = other_ref[...].astype(F32)
    total = jnp.sum(own * own, axis=1, keepdims=True)
    total = total + jnp.sum(other * other, axis=1, keepdims=True)
    scale = lax.rsqrt(total / D + EPSILON)
    own = (own * scale * gains_ref[0:1, :]).astype(BF16)
    other = (other * scale * gains_c_ref[0:1, :]).astype(BF16)
    x_own_ref[...] = own
    x_other_ref[...] = other
    scale_ref[...] = scale
    here = jnp.concatenate([query_ref[...], key_ref[...], value_ref[...]], axis=1)
    qkv_ref[...] = (dot(own, here) + dot(other, there_ref[...])).astype(BF16)


def project(col, own, other, gains, gains_c, w_query, w_key, w_value, there):
    rows, features = own.shape
    width = there.shape[1]
    group = GROUP_HEADS * DH
    tile = rows // 2

    def whole(*shape):
        return pl.BlockSpec(shape, lambda i, c: (0,) * len(shape))

    def mine(width):
        return pl.BlockSpec((features, width), lambda i, c: (0, c[0]))

    def rowwise(width):
        return pl.BlockSpec((tile, width), lambda i, c: (i, 0))

    return pl.pallas_call(
        project_kernel,
        grid_spec=pltpu.PrefetchScalarGridSpec(
            num_scalar_prefetch=1,
            grid=(rows // tile,),
            in_specs=[
                rowwise(features),
                rowwise(features),
                whole(2, features),
                whole(2, features),
                mine(group),
                mine(DH),
                mine(DH),
                whole(features, width),
            ],
            out_specs=[rowwise(features), rowwise(features), rowwise(width), rowwise(1)],
        ),
        out_shape=[
            jax.ShapeDtypeStruct((rows, features), BF16),
            jax.ShapeDtypeStruct((rows, features), BF16),
            jax.ShapeDtypeStruct((rows, width), BF16),
            jax.ShapeDtypeStruct((rows, 1), F32),
        ],
        compiler_params=params(60, "arbitrary"),
        cost_estimate=SMALL,
        name="project",
    )(col, own, other, gains, gains_c, w_query, w_key, w_value, there)


def head_pair(col_ref, own, other):
    first, second = own[...], other[...]
    flipped = col_ref != 0
    return jnp.concatenate(
        [jnp.where(flipped, second, first), jnp.where(flipped, first, second)], axis=1
    )


def before_kernel(tiles, place_ref, *refs):
    near, near_c, far, far_c, attended, attended_c, here, there, own_ref, other_ref = refs
    is_near = (pl.program_id(0) >= tiles // 2).astype(jnp.int32) == place_ref[0]
    heads = head_pair(place_ref[2], attended, attended_c)
    own = jnp.where(is_near, near[...], far[...]).astype(F32)
    other = jnp.where(is_near, near_c[...], far_c[...]).astype(F32)
    own_ref[...] = own + dot(heads, here[...])
    other_ref[...] = other + dot(heads, there[...])


def after_kernel(place_ref, *refs):
    own_ref, other_ref, attended, attended_c, here, there, gains_ref, gains_c_ref = refs[0:8]
    hidden_ref, x_own_ref, x_other_ref, scale_ref = refs[8:12]
    heads = head_pair(place_ref[2], attended, attended_c)
    own = own_ref[...] + dot(heads, here[...])
    other = other_ref[...] + dot(heads, there[...])
    total = jnp.sum(own * own, axis=1, keepdims=True)
    total = total + jnp.sum(other * other, axis=1, keepdims=True)
    scale = lax.rsqrt(total / D + EPSILON)
    hidden_ref[...] = own
    scale_ref[...] = scale
    x_own_ref[...] = (own * scale * gains_ref[1:2, :]).astype(BF16)
    x_other_ref[...] = (other * scale * gains_c_ref[1:2, :]).astype(BF16)


TOKEN_TILE = 256


def rowwise(width):
    return pl.BlockSpec((TOKEN_TILE, width), lambda i, p: (i, 0))


def whole(*shape):
    return pl.BlockSpec(shape, lambda i, p: (0,) * len(shape))


def hidden_before(place, tokens, attended, here, there):
    half, features = tokens[0].shape
    rows, heads = attended[0].shape
    tiles = rows // TOKEN_TILE
    per_half = half // TOKEN_TILE
    halfwise = pl.BlockSpec((TOKEN_TILE, features), lambda i, p: (i % per_half, 0))
    return pl.pallas_call(
        functools.partial(before_kernel, tiles),
        grid_spec=pltpu.PrefetchScalarGridSpec(
            num_scalar_prefetch=1,
            grid=(tiles,),
            in_specs=[halfwise] * 4 + [rowwise(heads)] * 2 + [whole(2 * heads, features)] * 2,
            out_specs=[rowwise(features)] * 2,
        ),
        out_shape=[jax.ShapeDtypeStruct((rows, features), F32)] * 2,
        compiler_params=params(56, "arbitrary"),
        cost_estimate=pl.CostEstimate(
            flops=8 * rows * features * heads,
            bytes_accessed=16 * rows * features,
            transcendentals=0,
        ),
        name="hidden_before",
    )(place, *tokens, *attended, here, there)


def hidden_after(place, before, attended, here, there, gains, gains_c):
    rows, features = before[0].shape
    heads = attended[0].shape[1]
    return pl.pallas_call(
        after_kernel,
        grid_spec=pltpu.PrefetchScalarGridSpec(
            num_scalar_prefetch=1,
            grid=(rows // TOKEN_TILE,),
            in_specs=[rowwise(features)] * 2
            + [rowwise(heads)] * 2
            + [whole(2 * heads, features)] * 2
            + [whole(2, features)] * 2,
            out_specs=[rowwise(features)] * 3 + [rowwise(1)],
        ),
        out_shape=[
            jax.ShapeDtypeStruct((rows, features), F32),
            jax.ShapeDtypeStruct((rows, features), BF16),
            jax.ShapeDtypeStruct((rows, features), BF16),
            jax.ShapeDtypeStruct((rows, 1), F32),
        ],
        compiler_params=params(56, "arbitrary"),
        cost_estimate=SMALL,
        name="hidden_after",
    )(place, *before, *attended, here, there, gains, gains_c)


def expert_kernel(shared, aliased, first, order_ref, *refs):
    x_own, x_other, o_own, o_other, gates_ref = refs[0:5]
    weights = refs[5:17]
    grads = refs[17 + aliased : 19 + aliased]
    pair_ref, inner_ref = refs[19 + aliased : 21 + aliased]
    step = pl.program_id(0) + first
    rows, features = x_own.shape
    tile = 512
    up_own = jnp.concatenate([weights[k][0] for k in (0, 1, 6, 7)], axis=1)
    up_other = jnp.concatenate([weights[k][0] for k in (2, 3, 8, 9)], axis=1)
    down_own = jnp.concatenate([weights[k][0] for k in (4, 10)], axis=0)
    down_other = jnp.concatenate([weights[k][0] for k in (5, 11)], axis=0)

    def token_tile(t, carry):
        at = pl.ds(pl.multiple_of(t * tile, tile), tile)
        pre = dot(x_own[at, :], up_own) + dot(x_other[at, :], up_other)
        back = dot_nt(o_own[at, :], down_own) + dot_nt(o_other[at, :], down_other)
        for k in range(2):
            pre_gate = pre[:, 2 * k * LANES : (2 * k + 1) * LANES]
            pre_up = pre[:, (2 * k + 1) * LANES : (2 * k + 2) * LANES]
            inner_grad = back[:, k * LANES : (k + 1) * LANES]
            sigmoid = 1.0 / (1.0 + jnp.exp(-pre_gate))
            silu = pre_gate * sigmoid
            inner = silu * pre_up
            if not shared:
                shape = (gates_ref.shape[0], LANES)
                expert = lax.broadcasted_iota(jnp.int32, shape, 0) % (gates_ref.shape[0] // 3)
                chosen = (expert == order_ref[2 * step + k]).astype(F32).astype(BF16)
                gate = dot_tn(gates_ref[:, at], chosen)
                inner = gate * inner
                inner_grad = gate * inner_grad
            gate_grad = inner_grad * pre_up * (sigmoid * (1.0 + pre_gate * (1.0 - sigmoid)))
            inner_ref[0, at, k * LANES : (k + 1) * LANES] = inner.astype(BF16)
            pair_ref[0, at, 2 * k * LANES : (2 * k + 1) * LANES] = gate_grad.astype(BF16)
            pair_ref[0, at, (2 * k + 1) * LANES : (2 * k + 2) * LANES] = (
                inner_grad * silu
            ).astype(BF16)
        return carry

    lax.fori_loop(0, rows // tile, token_tile, 0)
    pairs = pair_ref[0]
    for h, x in enumerate((x_own, x_other)):
        wide = dot_tn(x[...], pairs).astype(BF16)
        for k in range(2):
            grads[k][0, h * features : (h + 1) * features, 0 : 2 * LANES] = wide[
                :, 2 * k * LANES : (2 * k + 2) * LANES
            ]
    inner = inner_ref[0]
    tile = 256
    for h, o in enumerate((o_own, o_other)):
        for j in range(features // tile):
            low = dot_tn(inner, o[:, j * tile : (j + 1) * tile]).astype(BF16)
            for k in range(2):
                for b in range(tile // LANES):
                    at = h * features + j * tile + b * LANES
                    grads[k][0, at : at + LANES, 2 * LANES :] = low[
                        k * LANES : (k + 1) * LANES, b * LANES : (b + 1) * LANES
                    ]


def expert_specs(features, place, wide, low):
    specs = []
    if wide:
        block = pl.BlockSpec((1, features, LANES), lambda i, o: (place(i, o)[0], 0, place(i, o)[1]))
        specs += [block] * 4
    if low:
        block = pl.BlockSpec((1, LANES, features), lambda i, o: (*place(i, o), 0))
        specs += [block] * 2
    return specs


def expert_grads(order, first, last, total, x, o, gates, weights, kept):
    shared = total is None
    steps = last - first
    rows, features = x[0].shape
    aliased = len(kept)

    def fixed(*shape):
        return pl.BlockSpec(shape, lambda i, o: (0,) * len(shape))

    def stepped(*shape):
        return pl.BlockSpec((1, *shape), lambda i, o: (i, 0, 0))

    def placed(*shape):
        return pl.BlockSpec((1, *shape), lambda i, o: (i + first, 0, 0))

    specs = []
    for k in range(2):
        if shared:

            def picked(i, o, k=k):
                return 0, 2 * o[o.shape[0] - 1] + k

        else:

            def picked(i, o, k=k):
                return o[2 * (i + first) + k], o[o.shape[0] - 1]

        specs += expert_specs(features, picked, True, True)
    total = steps if shared else total
    return pl.pallas_call(
        functools.partial(expert_kernel, shared, aliased, first),
        grid_spec=pltpu.PrefetchScalarGridSpec(
            num_scalar_prefetch=1,
            grid=(steps,),
            in_specs=[fixed(rows, features)] * 4
            + [fixed(*gates.shape)]
            + specs
            + [pl.BlockSpec(memory_space=pl.ANY)] * aliased,
            out_specs=[stepped(2 * features, 3 * LANES)] * 2
            + [placed(rows, 4 * LANES), placed(rows, 2 * LANES)],
        ),
        out_shape=[jax.ShapeDtypeStruct((steps, 2 * features, 3 * LANES), BF16)] * 2
        + [
            jax.ShapeDtypeStruct((total, rows, 4 * LANES), BF16),
            jax.ShapeDtypeStruct((total, rows, 2 * LANES), BF16),
        ],
        input_output_aliases={18 + k: 2 + k for k in range(aliased)},
        compiler_params=params(40, "arbitrary"),
        cost_estimate=SMALL,
        name="expert_grads",
    )(order, *x, *o, gates, *weights, *weights, *kept)


def mix_kernel(back, group, order_ref, *refs):
    acts_ref, shared_ref = refs[0:2]
    each = 2 if back else 1
    count = 2 * group * each
    weights = refs[2 : 2 + count]
    shared = refs[2 + count : 2 + count + 2 * each]
    out_ref, total_ref = refs[2 + count + 2 * each :]
    step = pl.program_id(0)
    rows = out_ref.shape[0]
    tile = 512
    times = dot_nt if back else dot
    along = 1 if back else 0

    @pl.when(step == 0)
    def _():
        both = jnp.concatenate([w[0] for w in shared], axis=along)
        for t in range(rows // tile):
            at = slice(t * tile, (t + 1) * tile)
            total_ref[at, :] = times(shared_ref[0, at, :], both)

    both = jnp.concatenate([w[0] for w in weights], axis=along)
    for t in range(rows // tile):
        at = slice(t * tile, (t + 1) * tile)
        acts = jnp.concatenate([acts_ref[g, at, :] for g in range(group)], axis=1)
        total_ref[at, :] += times(acts, both)

    @pl.when(step == pl.num_programs(0) - 1)
    def _():
        out_ref[...] = total_ref[...].astype(out_ref.dtype)


def mix(back, dtype, order, acts, shared_acts, weights, shared_weights):
    pairs, rows, width = acts.shape
    features = weights[0].shape[1] if back else weights[0].shape[2]
    group = 4 if pairs % 4 == 0 else 1

    def spec(place):
        if back:
            return pl.BlockSpec((1, features, LANES), lambda i, o: (place(i, o)[0], 0, place(i, o)[1]))
        return pl.BlockSpec((1, LANES, features), lambda i, o: (*place(i, o), 0))

    def routed(k):
        return spec(lambda i, o: (o[2 * group * i + k], o[o.shape[0] - 1]))

    def common(k):
        return spec(lambda i, o: (0, 2 * o[o.shape[0] - 1] + k))

    return pl.pallas_call(
        functools.partial(mix_kernel, back, group),
        grid_spec=pltpu.PrefetchScalarGridSpec(
            num_scalar_prefetch=1,
            grid=(pairs // group,),
            in_specs=[
                pl.BlockSpec((group, rows, width), lambda i, o: (i, 0, 0)),
                pl.BlockSpec((1, rows, width), lambda i, o: (0, 0, 0)),
            ]
            + [routed(k) for k in range(2 * group) for _ in weights]
            + [common(k) for k in range(2) for _ in weights],
            out_specs=pl.BlockSpec((rows, features), lambda i, o: (0, 0)),
            scratch_shapes=[pltpu.VMEM((rows, features), F32)],
        ),
        out_shape=jax.ShapeDtypeStruct((rows, features), dtype),
        compiler_params=params(48, "arbitrary"),
        cost_estimate=SMALL,
        name="mix",
    )(order, acts, shared_acts, *weights * (2 * group), *shared_weights * 2)


def chip_sum_kernel(own_ref, other_ref, hidden_ref, gains_ref, total_ref, rounded_ref, product_ref):
    total = own_ref[...] + other_ref[...].astype(F32)
    total_ref[...] = total
    rounded_ref[...] = total.astype(BF16)
    product_ref[...] = lax.dot_general(
        jnp.ones((8, total.shape[1]), F32),
        total * gains_ref[1:2, :] * hidden_ref[...],
        (((1,), (1,)), ((), ())),
        precision=lax.Precision.HIGHEST,
        preferred_element_type=F32,
    )


def chip_sum(own, other, hidden, gains):
    rows, features = own.shape
    spec = pl.BlockSpec((TOKEN_TILE, features), lambda i: (i, 0))
    return pl.pallas_call(
        chip_sum_kernel,
        grid=(rows // TOKEN_TILE,),
        out_shape=[
            jax.ShapeDtypeStruct((rows, features), F32),
            jax.ShapeDtypeStruct((rows, features), BF16),
            jax.ShapeDtypeStruct((8, rows), F32),
        ],
        in_specs=[spec, spec, spec, pl.BlockSpec(gains.shape, lambda i: (0, 0))],
        out_specs=[spec, spec, pl.BlockSpec((8, TOKEN_TILE), lambda i: (0, i))],
        compiler_params=params(24, "arbitrary"),
        cost_estimate=SMALL,
        name="chip_sum",
    )(own, other, hidden, gains)


def norm_back_kernel(tiles, place_ref, *refs):
    sum_ref, came_ref, hidden_ref, scale_ref, out_grad_ref, gains_ref = refs[0:6]
    products = refs[6:10]
    hidden_grad_ref, rounded_ref, gain_ref = refs[10:13]
    step = pl.program_id(0)
    part = (step >= tiles // 2).astype(jnp.int32)
    grad = sum_ref[...] + came_ref[...].astype(F32)
    hidden = hidden_ref[...]
    scale = scale_ref[...]
    total = (products[0][...] + products[1][...]) + (products[2][...] + products[3][...])
    mean = lax.dot_general(
        total,
        jnp.full((8, LANES), 1.0 / (8 * D), F32),
        (((0,), (0,)), ((), ())),
        precision=lax.Precision.HIGHEST,
        preferred_element_type=F32,
    )[:, 0:1]
    result = out_grad_ref[...].astype(F32) + scale * (grad * gains_ref[1:2, :])
    result = result - hidden * (scale * scale * scale * mean)
    hidden_grad_ref[...] = result
    rounded_ref[...] = result.astype(BF16)

    @pl.when(step == 0)
    def _():
        gain_ref[...] = jnp.zeros_like(gain_ref)

    @pl.when(part == place_ref[0])
    def _():
        gain_ref[...] += jnp.sum(grad * hidden * scale, axis=0, keepdims=True)


def norm_back(place, sums, came, hidden, scale, out_grad, gains, products):
    rows, features = hidden.shape
    tiles = rows // TOKEN_TILE
    lanes = pl.BlockSpec((8, TOKEN_TILE), lambda i, p: (0, i))
    return pl.pallas_call(
        functools.partial(norm_back_kernel, tiles),
        grid_spec=pltpu.PrefetchScalarGridSpec(
            num_scalar_prefetch=1,
            grid=(tiles,),
            in_specs=[rowwise(features)] * 3
            + [rowwise(1), rowwise(features), whole(2, features)]
            + [lanes] * 4,
            out_specs=[rowwise(features)] * 2 + [whole(1, features)],
        ),
        out_shape=[
            jax.ShapeDtypeStruct((rows, features), F32),
            jax.ShapeDtypeStruct((rows, features), BF16),
            jax.ShapeDtypeStruct((1, features), F32),
        ],
        compiler_params=params(48, "arbitrary"),
        cost_estimate=SMALL,
        name="norm_back",
    )(place, sums, came, hidden, scale, out_grad, gains, *products)


def ring_of(size):
    return list(range(0, size, 2)) + list(range(1, size, 2))[::-1]


def unpack_kernel(aliased, plan_ref, *refs):
    chunks = refs[0:2]
    gate_ref, up_ref, down_ref = refs[2 + aliased : 5 + aliased]
    rows = gate_ref.shape[1]

    def write(chunk_ref):
        first = chunk_ref.shape[0] - rows
        gate_ref[0] = chunk_ref[first:, 0:LANES].astype(F32)
        up_ref[0] = chunk_ref[first:, LANES : 2 * LANES].astype(F32)
        for b in range(rows // LANES):
            at = slice(first + b * LANES, first + (b + 1) * LANES)
            down_ref[0, :, b * LANES : (b + 1) * LANES] = chunk_ref[at, 2 * LANES :].astype(F32)

    for k in range(2):
        pl.when(pl.program_id(0) == k)(lambda k=k: write(chunks[k]))


def unpack(plan, first, wave, chunks, shapes, outs):
    rows = shapes[0][1]

    def place(d, n):
        block = n[n.shape[0] - 1]
        return n[first + d], 1 - block if wave else block

    def wide(d, n):
        expert, block = place(d, n)
        return (expert, 0, block)

    def low(d, n):
        expert, block = place(d, n)
        return (expert, block, 0)

    aliased = len(outs)
    return pl.pallas_call(
        functools.partial(unpack_kernel, aliased),
        grid_spec=pltpu.PrefetchScalarGridSpec(
            num_scalar_prefetch=1,
            grid=(2,),
            in_specs=[pl.BlockSpec(chunk.shape, lambda d, n: (0, 0)) for chunk in chunks]
            + [pl.BlockSpec(memory_space=pl.ANY)] * aliased,
            out_specs=[
                pl.BlockSpec((1, rows, LANES), wide),
                pl.BlockSpec((1, rows, LANES), wide),
                pl.BlockSpec((1, LANES, rows), low),
            ],
        ),
        out_shape=[jax.ShapeDtypeStruct(shape, F32) for shape in shapes],
        input_output_aliases={3 + k: k for k in range(aliased)},
        compiler_params=params(16, "arbitrary"),
        cost_estimate=SMALL,
        name="unpack",
    )(plan, *chunks, *outs)


def ring_sum_kernel(came_ref, mine_ref, *outs):
    total = (came_ref[...].astype(F32) + mine_ref[...].astype(F32)).astype(BF16)
    if len(outs) == 1:
        outs[0][...] = total
    else:
        half = pl.program_id(1) // (pl.num_programs(1) // 2)
        for k, out_ref in enumerate(outs):

            @pl.when(half == k)
            def _(out_ref=out_ref):
                out_ref[...] = total


def ring_sum(came, mine, halved):
    count, rows, lanes = came.shape
    tiles = 4
    spec = pl.BlockSpec((1, rows // tiles, lanes), lambda i, j: (i, j, 0))

    def half(k):
        first = k * tiles // 2
        last = tiles // 2 - 1
        return pl.BlockSpec(
            (1, rows // tiles, lanes), lambda i, j: (i, jnp.clip(j - first, 0, last), 0)
        )

    shapes = [jax.ShapeDtypeStruct((count, rows // 2, lanes), BF16)] * 2
    return pl.pallas_call(
        ring_sum_kernel,
        grid=(count, tiles),
        in_specs=[spec, spec],
        out_specs=[half(0), half(1)] if halved else spec,
        out_shape=shapes if halved else jax.ShapeDtypeStruct(came.shape, BF16),
        compiler_params=params(16, "arbitrary", "arbitrary"),
        cost_estimate=SMALL,
        name="ring_sum",
    )(came, mine)


def late_load_kernel(plan_ref, pack_ref, main_ref, out_ref):
    rows = pack_ref.shape[1]
    out_ref[0:rows, :] = pack_ref[0]
    out_ref[rows:, :] = main_ref[...]


def late_load(plan, at, pack, main):
    rows, lanes = pack.shape[1:]
    total = rows + main.shape[0]
    return pl.pallas_call(
        late_load_kernel,
        grid_spec=pltpu.PrefetchScalarGridSpec(
            num_scalar_prefetch=1,
            grid=(1,),
            in_specs=[
                pl.BlockSpec((1, rows, lanes), lambda i, n: (n[at], 0, 0)),
                pl.BlockSpec(main.shape, lambda i, n: (0, 0)),
            ],
            out_specs=pl.BlockSpec((total, lanes), lambda i, n: (0, 0)),
        ),
        out_shape=jax.ShapeDtypeStruct((total, lanes), BF16),
        compiler_params=params(16, "arbitrary"),
        cost_estimate=SMALL,
        name="late_load",
    )(plan, pack, main)


def late_add_kernel(plan_ref, pack_ref, came_ref, *outs):
    total = (came_ref[...].astype(F32) + pack_ref[0].astype(F32)).astype(BF16)
    for out_ref in outs:
        out_ref[...] = total


def late_add(plan, at, pack, came, copied=False):
    rows, lanes = pack.shape[1:]
    spec = pl.BlockSpec((rows, lanes), lambda i, n: (0, 0))
    shape = jax.ShapeDtypeStruct(came.shape, BF16)
    return pl.pallas_call(
        late_add_kernel,
        grid_spec=pltpu.PrefetchScalarGridSpec(
            num_scalar_prefetch=1,
            grid=(1,),
            in_specs=[pl.BlockSpec((1, rows, lanes), lambda i, n: (n[at], 0, 0)), spec],
            out_specs=[spec] * 2 if copied else spec,
        ),
        out_shape=[shape, jax.ShapeDtypeStruct((rows, lanes), BF16)] if copied else shape,
        input_output_aliases={2: 0},
        compiler_params=params(16, "arbitrary"),
        cost_estimate=SMALL,
        name="late_add",
    )(plan, pack, came)


def late_main_kernel(main_ref, all_ref, out_ref):
    out_ref[...] = main_ref[...]


def late_main(rows_all, main):
    lanes = main.shape[1]
    share = main.shape[0] // RING
    first = (rows_all.shape[0] - main.shape[0]) // share
    return pl.pallas_call(
        late_main_kernel,
        grid=(RING,),
        in_specs=[
            pl.BlockSpec((share, lanes), lambda i: (i, 0)),
            pl.BlockSpec(memory_space=pl.ANY),
        ],
        out_specs=pl.BlockSpec((share, lanes), lambda i: (first + i, 0)),
        out_shape=jax.ShapeDtypeStruct(rows_all.shape, BF16),
        input_output_aliases={1: 0},
        compiler_params=params(16, "arbitrary"),
        cost_estimate=SMALL,
        name="late_main",
    )(main, rows_all)


def late_join_kernel(col_ref, mine_ref, other_ref, gains_ref, out_ref):
    units = 7
    share = mine_ref.shape[0] // LATE_BLOCKS
    to_rows, to_lanes = unit_slices(2 * units, share)
    blocks = gains_ref.shape[1] // LANES
    gains = [
        gains_ref[g : g + 1, b * LANES : (b + 1) * LANES] for g in range(2) for b in range(blocks)
    ]
    gains = jnp.concatenate(gains + [jnp.zeros((share - len(gains), LANES), F32)], axis=0)
    own = [mine_ref[unit_slices(b, share)] for b in range(units)]
    other = [other_ref[unit_slices(units + b, share)] for b in range(units)]
    for b in range(units):
        first, second = own[b], other[b]
        flipped = col_ref[0] != 0
        out_ref[unit_slices(b, share)] = jnp.where(flipped, second, first)
        out_ref[unit_slices(units + b, share)] = jnp.where(flipped, first, second)
    out_ref[to_rows, to_lanes] = gains.astype(BF16)


def late_join(col, rows_all, other, gains):
    rows, lanes = other.shape
    spec = pl.BlockSpec((rows, lanes), lambda i, c: (0, 0))
    return pl.pallas_call(
        late_join_kernel,
        grid_spec=pltpu.PrefetchScalarGridSpec(
            num_scalar_prefetch=1,
            grid=(1,),
            in_specs=[spec, spec, pl.BlockSpec(gains.shape, lambda i, c: (0, 0))],
            out_specs=spec,
        ),
        out_shape=jax.ShapeDtypeStruct(rows_all.shape, BF16),
        input_output_aliases={1: 0},
        compiler_params=params(16, "arbitrary"),
        cost_estimate=SMALL,
        name="late_join",
    )(col, rows_all, other, gains)


def unpack_late_kernel(first_step, steps, plan_ref, *refs):
    chunks = refs[0 : 2 * steps]
    sgate, sup, sdown, query, key, value, out, gains, all_ref, gain_ref = refs[2 * steps :]
    share, features = chunks[0].shape[0] // LATE_BLOCKS, all_ref.shape[2]
    for k in range(2):
        for step in range(steps):
            at = plan_ref[first_step + 2 * step + k]
            chunk = chunks[steps * k + step]
            to_rows = pl.ds(pl.multiple_of(at * share, share), share)
            for unit in range(14):
                lanes = slice(unit % 7 * LANES, (unit % 7 + 1) * LANES)
                all_ref[k, unit // 7, to_rows, lanes] = chunk[unit_slices(unit, share)]
            if k == 0:
                to_rows = pl.ds(pl.multiple_of(at * GAIN_ROWS, GAIN_ROWS), GAIN_ROWS)
                rows, lanes = unit_slices(14, share)
                gain_ref[to_rows, :] = chunk[rows.start : rows.start + GAIN_ROWS, lanes]
    total = jnp.zeros((GAIN_ROWS, LANES), F32)
    for step in range(steps):
        total = total + gain_ref[step * GAIN_ROWS : (step + 1) * GAIN_ROWS, :].astype(F32)
    blocks = features // LANES
    for row in range(2 * blocks):
        gains[row // blocks : row // blocks + 1, row % blocks * LANES : (row % blocks + 1) * LANES] = (
            total[row : row + 1, :]
        )
    flipped = plan_ref[plan_ref.shape[0] - 1] != 0
    for c in range(2):
        for b in range(14):
            lanes = slice(b % 7 * LANES, (b % 7 + 1) * LANES)
            first, second = all_ref[0, c, :, lanes], all_ref[1, c, :, lanes]
            if b >= 7:
                first, second = second, first
            block = jnp.where(flipped, second, first).astype(F32)
            if b < 6:
                at = slice((2 * c + b // 3) * LANES, (2 * c + b // 3 + 1) * LANES)
                if b % 3 < 2:
                    (sgate, sup)[b % 3][:, at] = block
                else:
                    for k in range(features // LANES):
                        here = slice(k * LANES, (k + 1) * LANES)
                        sdown[at, here] = block[here, :]
            elif b < 9:
                at = (GROUP_HEADS * c + b - 6) * LANES
                query[:, at : at + LANES] = block
            elif b < 11:
                (key, value)[b - 9][:, c * LANES : (c + 1) * LANES] = block
            else:
                at = (GROUP_HEADS * c + b - 11) * LANES
                out[at : at + LANES, :] = block.T


def unpack_late(plan, first_step, chunks, shapes):
    steps = len(chunks[0])
    features = shapes[0][0]
    share = features // steps
    chunk = pl.BlockSpec((LATE_BLOCKS * share, 3 * LANES), lambda i, n: (0, 0))
    return pl.pallas_call(
        functools.partial(unpack_late_kernel, first_step, steps),
        grid_spec=pltpu.PrefetchScalarGridSpec(
            num_scalar_prefetch=1,
            grid=(1,),
            in_specs=[chunk] * (2 * steps),
            out_specs=[pl.BlockSpec(shape, lambda i, n: (0, 0)) for shape in shapes],
            scratch_shapes=[
                pltpu.VMEM((2, 2, features, 7 * LANES), BF16),
                pltpu.VMEM((steps * GAIN_ROWS, LANES), BF16),
            ],
        ),
        out_shape=[jax.ShapeDtypeStruct(shape, F32) for shape in shapes],
        compiler_params=params(48, "arbitrary"),
        cost_estimate=SMALL,
        name="unpack_late",
    )(plan, *chunks[0], *chunks[1])


def plans(ring, each):
    size = len(ring)
    rows = []
    for member in range(size):
        place = ring.index(member)
        for col in range(2):
            chunks = []
            for step in range(2 * size - 1):
                for which in range(2):
                    sign = 1 if which == col else -1
                    chunks.append((place - sign * step) % size)
            experts = []
            for start in (0, size - 1):
                for step in range(start, start + size):
                    for k in range(each):
                        for which in range(2):
                            second = col if which == 0 else 1 - col
                            experts.append(2 * each * chunks[2 * step + which] + each * second + k)
            rows.append(experts + chunks + [col])
    return np.asarray(rows, np.int32)


def body(
    tokens_in,
    norm_gain_attn,
    w_query,
    w_key,
    w_value,
    w_out,
    norm_gain_ffn,
    w_gate,
    w_up,
    w_down,
    w_shared_gate,
    w_shared_up,
    w_shared_down,
    routes,
    gate_weights,
    seq_lengths,
    out_grad,
):
    row = lax.axis_index("row")
    col = lax.axis_index("col")
    dp = lax.axis_index("dp")
    dp_size = lax.axis_size("dp")
    local_rows, local_features = tokens_in.shape
    experts = w_gate.shape[0]
    group_width = GROUP_HEADS * DH
    col_ref = col.reshape(1)

    ring_size = RING
    ring = ring_of(ring_size)
    starts = range(0, dp_size, ring_size)
    rights = [
        (g + ring[k], g + ring[(k + 1) % ring_size]) for g in starts for k in range(ring_size)
    ]
    lefts = [(b, a) for a, b in rights]
    routes_of = [
        [(2 * a, 2 * b) for a, b in ways[0]] + [(2 * a + 1, 2 * b + 1) for a, b in ways[1]]
        for ways in ((rights, lefts), (lefts, rights))
    ]
    experts_each = experts // (2 * ring_size)
    plan = jnp.asarray(plans(ring, experts_each))
    plan = lax.dynamic_slice(
        plan, (2 * (dp % ring_size) + col, jnp.int32(0)), (1, plan.shape[1])
    ).reshape(-1)

    def send(values, which):
        return lax.ppermute(values, ("dp", "col"), routes_of[which])

    def chunk_at(step, which):
        return plan[2 * experts + 2 * step + which]

    def across_rings(values):
        if len(starts) == 1:
            return values
        peers = [[g + k for g in starts] for k in range(ring_size)]
        return lax.psum(values, "dp", axis_index_groups=peers)

    where = jnp.stack([row, seq_lengths[0], col])
    tokens_y = swap(tokens_in, "row")
    tokens_c = swap(tokens_in, "col")
    count = 4
    member = dp % count
    there, out_y = their_columns(
        jnp.stack([col, member]), w_query, w_key, w_value, w_out, count
    )
    gains = jnp.stack([norm_gain_attn, norm_gain_ffn])
    there = swap(there, "col")
    gains_c = swap(gains, "col")

    def project_half(own, other):
        return project(col_ref, own, other, gains, gains_c, w_query, w_key, w_value, there)

    near = project_half(tokens_in, tokens_c)
    gate_c = swap(w_gate, "col")
    out_y = swap(out_y, "row")
    tokens_y = after(tokens_y, near[2], out_y)
    tokens_yc = swap(tokens_y, "col")
    grad_y = swap(after(out_grad, tokens_y), "row")
    far = project_half(tokens_y, tokens_yc)
    shares = [out_y]
    for k in range(1, count):
        part = out_y if k < 3 else after(out_y, far[2])
        shares.append(lax.ppermute(part, "dp", [(m, m ^ k) for m in range(dp_size)]))
    where = after(where, grad_y, *shares)

    w_sgate, w_sup, w_sdown = w_shared_gate[None], w_shared_up[None], w_shared_down[None]
    up_c = swap(after(w_up, gate_c, tokens_yc), "col")

    attended = attend(where, near[2], far[2])
    attended_y = swap(attended, "row")
    attended_c = swap(attended, "col")
    out_c = swap(after(w_out, tokens_yc), "col")
    before = hidden_before(
        where,
        [tokens_in, tokens_c, tokens_y, tokens_yc],
        [attended, attended_c],
        w_out,
        out_c,
    )
    down_c = swap(after(w_down, tokens_yc), "col")
    attended_y = after(attended_y, before[0])
    out_y = join(member, *shares)
    out_yc = swap(out_y, "col")
    attended_yc = swap(attended_y, "col")
    grad_own = join(row, out_grad, grad_y)
    grad_other = swap(grad_own, "col")
    hidden, x_own, x_other, scale_ffn = hidden_after(
        where, before, [attended_y, attended_yc], out_y, out_yc, gains, gains_c
    )
    sgate_c, sup_c, sdown_c = (
        swap(after(w, attended_yc), "col") for w in (w_sgate, w_sup, w_sdown)
    )

    choices = jnp.arange(experts, dtype=jnp.int32)[:, None]
    dense = sum(
        jnp.where(routes[:, k][None, :] == choices, gate_weights[:, k][None, :], 0.0)
        for k in range(routes.shape[1])
    )
    gates = []
    for _ in range(3):
        gates.append(lax.reduce_precision(dense, 8, 7))
        dense = dense - gates[-1]
    gates = jnp.concatenate(gates, axis=0).astype(BF16)

    each = experts_each
    order = plan
    pairs_total = experts // 2
    routed = [w_gate, w_up, gate_c, up_c, w_down, down_c]
    shared = [w_sgate, w_sup, sgate_c, sup_c, w_sdown, sdown_c]

    def run(first, last, order, kept):
        return expert_grads(
            order,
            first,
            last,
            pairs_total,
            [x_own, x_other],
            [grad_own, grad_other],
            gates,
            routed,
            kept,
        )

    first = run(0, each, order, ())
    kept = first[2:]
    sums = [first[0], first[1]]
    runs = {}
    mixed = {}
    normed = {}

    def work_experts(first, last):
        def work(order, ties):
            nonlocal kept
            result = run(first, last, order, tuple(kept))
            kept = result[2:]
            runs[first] = result[0:2]
            return [kept[0]]

        return work

    def work_shared(order, ties):
        runs["shared"] = expert_grads(
            order, 0, 1, None, [x_own, x_other], [grad_own, grad_other], gates, shared, ()
        )
        return [runs["shared"][2]]

    def work_back(half):
        def work(order, ties):
            mixed[True, half] = mix(
                True,
                BF16 if half else F32,
                order,
                kept[0],
                runs["shared"][2],
                routed[2 * half : 2 * half + 2],
                shared[2 * half : 2 * half + 2],
            )
            if half:
                normed["other"] = swap(mixed[True, 1], "col")
                return [mixed[True, 1]]
            total, rounded, product = chip_sum(mixed[True, 0], normed["other"], hidden, gains)
            product_c = swap(product, "col")
            normed["sum"] = total
            normed["tie"] = rounded
            normed["came"] = swap(rounded, "row")
            normed["products"] = [product, product_c, swap(product, "row"), swap(product_c, "row")]
            return [mixed[True, 0]]

        return work

    def work_out(half):
        def work(order, ties):
            mixed[False, half] = mix(
                False,
                BF16 if half else F32,
                order,
                kept[1],
                runs["shared"][3],
                routed[4 + half : 5 + half],
                shared[4 + half : 5 + half],
            )
            return [mixed[False, half]] + ([] if half else [normed["tie"]])

        return work

    start = row * local_rows

    def my_rows(values):
        return lax.dynamic_slice_in_dim(values, start, local_rows, axis=0)

    def their_rows(values):
        return lax.dynamic_slice_in_dim(values, local_rows - start, local_rows, axis=0)

    def work_hidden(order, ties):
        normed["hidden"], normed["grad"], normed["gain"] = norm_back(
            after(where, *ties),
            normed["sum"],
            normed["came"],
            hidden,
            scale_ffn,
            grad_own,
            gains,
            normed["products"],
        )
        normed["grad_c"] = swap(normed["grad"], "col")
        return [normed["grad"]]

    def work_attend(order, ties):
        normed["qkv"] = attend_back(
            after(where, *ties), near[2], far[2], normed["grad"], normed["grad_c"], w_out, out_c
        )
        return [normed["qkv"]]

    def work_late(order, ties):
        normed["packs"] = late_grads(
            after(where, *ties),
            near[0:2],
            far[0:2],
            normed["qkv"],
            attended,
            normed["grad"],
            normed["grad_c"],
            runs["shared"][0:2],
        )
        return normed["packs"]

    tasks = [work_experts(at, at + each) for at in range(each, pairs_total, each)]
    tasks += [work_shared, work_back(1), work_back(0), work_out(1), work_out(0)]
    later = [[work_hidden, work_attend], [work_late]]
    got = [None, None]
    got[0] = send(sums[0], 0)
    tasks.pop(0)(after(order, *sums), sums)
    got[1] = send(after(sums[1], kept[0]), 1)
    for s in range(1, ring_size):
        for k in range(2):
            last = sums
            task = tasks.pop(0) if tasks else None
            if task:
                last = task(after(order, *last), last)
            sums[k] = ring_sum(after(got[k], *last), runs[each * s][k], s + 1 == ring_size)
            if s + 1 < ring_size:
                got[k] = send(sums[k], k)
            else:
                sums[k], got[k] = sums[k]
    crossed = [swap(across_rings(total), "col") for total in got]
    waves = [[across_rings(total)[0] for total in sums], [crossed[1][0], crossed[0][0]]]

    chunks_first = 2 * experts
    late_total = 2 * (ring_size - 1)

    def back_to_tokens(ties):
        hidden_grad = normed["hidden"]
        qkv_grad = after(normed["qkv"], *ties)
        ffn_sum = mixed[False, 0] + swap(mixed[False, 1], "col").astype(F32)
        ffn_rows = my_rows(ffn_sum) + swap(their_rows(ffn_sum).astype(BF16), "row").astype(F32)
        block_out = (my_rows(hidden) + ffn_rows).astype(BF16)
        here = jnp.concatenate(
            [halves(w, 1, col)[0] for w in (w_query, w_key, w_value)], axis=1
        )
        tokens_back = dot_nt(qkv_grad, here) + swap(
            dot_nt(qkv_grad, there).astype(BF16), "col"
        ).astype(F32)
        tokens_back = my_rows(tokens_back) + swap(
            their_rows(tokens_back).astype(BF16), "row"
        ).astype(F32)
        scale_attn = near[3]
        tokens_f32 = tokens_in.astype(F32)
        gain_attn_part = jnp.sum(tokens_back * tokens_f32 * scale_attn, axis=0)
        scaled = tokens_back * norm_gain_attn
        products = jnp.sum(scaled * tokens_f32, axis=1, keepdims=True)
        mean = (products + swap(products, "col")) / D
        tokens_grad = (
            my_rows(hidden_grad) + scale_attn * scaled - tokens_f32 * scale_attn**3 * mean
        ).astype(BF16)

        gain_parts = jnp.concatenate([gain_attn_part[None], normed["gain"]], axis=0)
        normed["gains"] = across_rings(gain_parts + swap(gain_parts, "row"))
        normed["outs"] = (block_out, tokens_grad)

    shapes = [w_gate.shape, w_up.shape, w_down.shape]
    placed = ()
    late_out = [[], []]
    late_start = len(later)
    last, got = [], [None, None]
    moves = [(wave, step) for wave in range(2) for step in range(wave, ring_size - 1)]
    for number, (wave, step) in enumerate(moves):
        late_step = number - late_start
        current = [None, None]
        copies = [None, None]
        for k in range(2):
            if number == 0:
                current[k] = after(waves[0][k], *last) if last else waves[0][k]
                got[k] = send(current[k], k)
                last = [current[k]]
                continue
            current[k] = after(got[k], *last)
            if late_step < 0:
                got[k] = send(current[k], k)
                last = [current[k]]
                continue
            at = chunks_first + 2 * late_step + k
            if late_step == 0:
                current[k] = late_load(plan, at, normed["packs"][k], current[k])
            elif late_step < ring_size - 1:
                current[k] = late_add(plan, at, normed["packs"][k], current[k])
            elif late_step == ring_size - 1:
                current[k], copies[k] = late_add(plan, at, normed["packs"][k], current[k], True)
            last = [current[k]]
            if not (wave == 1 and step == 1) and late_step != ring_size - 1:
                got[k] = send(current[k], k)
                if late_step >= ring_size:
                    late_out[k].append(current[k])
        switch = wave == 1 and step == 1
        if switch or late_step == ring_size - 1:
            if late_step == ring_size - 1:
                others = [swap(across_rings(values), "col") for values in copies]
                current = [
                    late_join(col_ref, current[k], others[1 - k], normed["gains"])
                    for k in range(2)
                ]
            if switch:
                placed = unpack(
                    plan, experts + 2 * (ring_size - 1), 0, current, shapes, placed
                )
                placed = unpack(plan, experts, 1, waves[1], shapes, placed)
                current = [late_main(after(current[k], placed[0]), early[k]) for k in range(2)]
            for k in range(2):
                got[k] = send(current[k], k)
                if late_step >= ring_size - 1:
                    late_out[k].append(current[k])
            last = [current[1]]
        if number == 0:
            early = [send(after(waves[1][k], *current), k) for k in range(2)]
        if number < len(later):
            for work in later[number]:
                if number == 1:
                    last = [*last, *early]
                last = work(after(order, *last), last)
        placed = unpack(
            plan, experts + 2 * step, wave, [after(current[0], *last), current[1]], shapes, placed
        )
        last = placed[0:1]
        if number == 3:
            back_to_tokens(last)
    for late_step in range(len(moves) - late_start, late_total + 1):
        for k in range(2):
            values = after(got[k], *last)
            late_out[k].append(values)
            if late_step < late_total:
                got[k] = send(values[: LATE_BLOCKS * (local_features // ring_size)], k)
            last = [values]
        if late_step == len(moves) - late_start:
            whole_chunks = [late_out[k][-1] for k in range(2)]
            placed = unpack(
                plan, experts + 2 * (ring_size - 1), 1, whole_chunks, shapes, placed
            )
    gate_grad, up_grad, down_grad = placed
    shapes = [w.shape for w in (w_shared_gate, w_shared_up, w_shared_down)]
    shapes += [w.shape for w in (w_query, w_key, w_value, w_out)] + [gains.shape]
    finals = unpack_late(plan, chunks_first + late_total, late_out, shapes)
    shared_gate_grad, shared_up_grad, shared_down_grad = finals[0:3]
    query_grad, key_grad, value_grad, out_proj_grad, gain_grads = finals[3:8]


    return (
        *normed["outs"],
        gain_grads[0],
        query_grad,
        key_grad,
        value_grad,
        out_proj_grad,
        gain_grads[1],
        gate_grad,
        up_grad,
        down_grad,
        shared_gate_grad,
        shared_up_grad,
        shared_down_grad,
    )


def solution(mesh):
    in_specs = (
        P(("dp", "row"), "col"),
        P("col"),
        P("col", "row"),
        P("col", "row"),
        P("col", "row"),
        P("row", "col"),
        P("col"),
        P(None, "col", "row"),
        P(None, "col", "row"),
        P(None, "row", "col"),
        P("col", "row"),
        P("col", "row"),
        P("row", "col"),
        P("dp", None),
        P("dp", None),
        P("dp"),
        P(("dp", "row"), "col"),
    )
    out_specs = (
        P(("dp", "row"), "col"),
        P(("dp", "row"), "col"),
        P("col"),
        P("col", "row"),
        P("col", "row"),
        P("col", "row"),
        P("row", "col"),
        P("col"),
        P(None, "col", "row"),
        P(None, "col", "row"),
        P(None, "row", "col"),
        P("col", "row"),
        P("col", "row"),
        P("row", "col"),
    )
    return jax.shard_map(body, mesh=mesh, in_specs=in_specs, out_specs=out_specs, check_vma=False)
```

```python
import functools

import jax
import jax.numpy as jnp
import numpy as np
from jax import lax
from jax.experimental import pallas as pl
from jax.experimental.pallas import tpu as pltpu
from jax.sharding import PartitionSpec as P

D = 1536
HQ = 12
HK = 4
DH = 128
GROUP_HEADS = HQ // HK
LANES = 128

EPSILON = 1e-05
F32 = jnp.float32
BF16 = jnp.bfloat16
MIB = 1024 * 1024
GAIN_ROWS = 16
RING = 8
LATE_BLOCKS = 5
SMALL = pl.CostEstimate(flops=0, bytes_accessed=0, transcendentals=0)


def params(mib, *semantics):
    return pltpu.CompilerParams(
        dimension_semantics=semantics or None, vmem_limit_bytes=mib * MIB
    )


def dot(left, right):
    return jnp.dot(left, right, preferred_element_type=F32)


def dot_nt(left, right):
    return lax.dot_general(left, right, (((1,), (1,)), ((), ())), preferred_element_type=F32)


def dot_tn(left, right):
    return lax.dot_general(left, right, (((0,), (0,)), ((), ())), preferred_element_type=F32)


def after(values, *others):
    return lax.optimization_barrier((values, *others))[0]


def swap(values, axis):
    return lax.ppermute(values, axis, [(0, 1), (1, 0)])


def halves(values, axis, mine):
    size = values.shape[axis] // 2
    low = lax.slice_in_dim(values, 0, size, axis=axis)
    high = lax.slice_in_dim(values, size, 2 * size, axis=axis)
    return jnp.where(mine == 0, low, high), jnp.where(mine == 0, high, low)


def in_order(own, other, mine, axis):
    return jnp.concatenate(
        [jnp.where(mine == 0, own, other), jnp.where(mine == 0, other, own)], axis=axis
    )


def gather_rows(place_ref, own_ref, other_ref, all_ref):
    row = place_ref[0]
    rows = own_ref.shape[0]
    all_ref[pl.ds(pl.multiple_of(row * rows, rows), rows), :] = own_ref[...]
    all_ref[pl.ds(pl.multiple_of((1 - row) * rows, rows), rows), :] = other_ref[...]


def head_rows(ref, first, block):
    return jnp.concatenate(
        [ref[first : first + block, h * DH : (h + 1) * DH] for h in range(GROUP_HEADS)], axis=0
    )


def key_probs(query, key, first, length):
    block, keys = query.shape[0] // GROUP_HEADS, key.shape[0]
    scores = dot_nt(query, key) * DH ** (-0.5)
    shape = (block, keys)
    query_at = lax.broadcasted_iota(jnp.int32, shape, 0) + first
    key_at = lax.broadcasted_iota(jnp.int32, shape, 1)
    allowed = (key_at <= query_at) & (key_at < length)
    allowed = jnp.concatenate([allowed] * GROUP_HEADS, axis=0)
    scores = jnp.where(allowed, scores, -1e30)
    weights = jnp.exp(scores - jnp.max(scores, axis=1, keepdims=True))
    return weights * (1.0 / jnp.sum(weights, axis=1, keepdims=True))


def attend_kernel(place_ref, own_ref, other_ref, out_ref, all_ref):
    gather_rows(place_ref, own_ref, other_ref, all_ref)
    rows = own_ref.shape[0]
    block = 256
    width = GROUP_HEADS * DH
    for at in range(2 * rows // block):
        first, keys = at * block, (at + 1) * block
        query = head_rows(all_ref, first, block)
        key = all_ref[0:keys, width : width + DH]
        value = all_ref[0:keys, width + DH : width + 2 * DH]
        probs = key_probs(query, key, first, place_ref[1])
        result = dot(probs.astype(BF16), value).astype(BF16)
        for h in range(GROUP_HEADS):
            out_ref[first : first + block, h * DH : (h + 1) * DH] = result[
                h * block : (h + 1) * block
            ]


def attend(place, own, other):
    rows, width = own.shape
    spec = pl.BlockSpec(memory_space=pltpu.VMEM)
    return pl.pallas_call(
        attend_kernel,
        out_shape=jax.ShapeDtypeStruct((2 * rows, GROUP_HEADS * DH), BF16),
        in_specs=[pl.BlockSpec(memory_space=pltpu.SMEM), spec, spec],
        out_specs=spec,
        scratch_shapes=[pltpu.VMEM((2 * rows, width), BF16)],
        compiler_params=params(32),
        cost_estimate=SMALL,
        name="attend",
    )(place, own, other)


def attend_back_kernel(
    place_ref, own_ref, other_ref, grad_ref, grad_c_ref, out_ref, out_c_ref, result_ref, all_ref, total_ref
):
    gather_rows(place_ref, own_ref, other_ref, all_ref)
    rows = own_ref.shape[0]
    block = 256
    width = GROUP_HEADS * DH
    group = pl.ds(pl.multiple_of(place_ref[2] * width, width), width)
    blocks = 2 * rows // block
    for at in reversed(range(blocks)):
        first, keys = at * block, (at + 1) * block
        query = head_rows(all_ref, first, block)
        key = all_ref[0:keys, width : width + DH]
        value = all_ref[0:keys, width + DH : width + 2 * DH]
        probs = key_probs(query, key, first, place_ref[1])
        grad = dot_nt(grad_ref[first:keys, :], out_ref[group, :])
        grad = (grad + dot_nt(grad_c_ref[first:keys, :], out_c_ref[group, :])).astype(BF16)
        grad = jnp.concatenate(
            [grad[:, h * DH : (h + 1) * DH] for h in range(GROUP_HEADS)], axis=0
        )
        probs_grad = dot_nt(grad, value)
        carried = jnp.sum(probs * probs_grad, axis=1, keepdims=True)
        score_grad = (probs * (probs_grad - carried)).astype(BF16)
        query_back = (dot(score_grad, key) * DH ** (-0.5)).astype(BF16)
        for h in range(GROUP_HEADS):
            result_ref[first:keys, h * DH : (h + 1) * DH] = query_back[
                h * block : (h + 1) * block
            ]
        key_back = dot_tn(score_grad, query)
        value_back = dot_tn(probs.astype(BF16), grad)
        if at == blocks - 1:
            total_ref[:, 0:DH] = key_back
            total_ref[:, DH:] = value_back
        else:
            total_ref[0:keys, 0:DH] += key_back
            total_ref[0:keys, DH:] += value_back
    result_ref[:, width : width + DH] = (total_ref[:, 0:DH] * DH ** (-0.5)).astype(BF16)
    result_ref[:, width + DH :] = total_ref[:, DH:].astype(BF16)


def attend_back(place, own, other, grad, grad_c, w_out, out_c):
    rows, width = own.shape
    spec = pl.BlockSpec(memory_space=pltpu.VMEM)
    return pl.pallas_call(
        attend_back_kernel,
        out_shape=jax.ShapeDtypeStruct((2 * rows, width), BF16),
        in_specs=[pl.BlockSpec(memory_space=pltpu.SMEM)] + [spec] * 6,
        out_specs=spec,
        scratch_shapes=[
            pltpu.VMEM((2 * rows, width), BF16),
            pltpu.VMEM((2 * rows, 2 * DH), F32),
        ],
        compiler_params=params(60),
        cost_estimate=SMALL,
        name="attend_back",
    )(place, own, other, grad, grad_c, w_out, out_c)


def unit_slices(unit, share):
    row, lane = divmod(unit, 3)
    return slice(row * share, (row + 1) * share), slice(lane * LANES, (lane + 1) * LANES)


def late_kernel(place_ref, *refs):
    near, near_c, far, far_c, qkv_ref, attended_ref, grad_ref, grad_c_ref = refs[0:8]
    shared = refs[8:10]
    outs = refs[10:12]
    rows, features = near.shape
    own_rows = pl.ds(pl.multiple_of(place_ref[0] * rows, rows), rows)
    far_rows = pl.ds(pl.multiple_of((1 - place_ref[0]) * rows, rows), rows)
    split = 7 * LANES

    chunks = outs[0].shape[0]
    share = features // chunks

    def store(h, at, values):
        values = values.astype(BF16)
        for b in range(values.shape[1] // LANES):
            part, unit = divmod(at // LANES + b, split // LANES)
            to_rows, to_lanes = unit_slices(h * (split // LANES) + unit, share)

            def write(out_ref, b=b, to_rows=to_rows, to_lanes=to_lanes):
                for chunk in range(chunks):
                    out_ref[chunk, to_rows, to_lanes] = values[
                        chunk * share : (chunk + 1) * share, b * LANES : (b + 1) * LANES
                    ]

            pl.when(place_ref[2] == 0)(lambda part=part, write=write: write(outs[part]))
            pl.when(place_ref[2] != 0)(lambda part=part, write=write: write(outs[1 - part]))

    for out_ref in outs:
        to_rows, to_lanes = unit_slices(2 * (split // LANES), share)
        for chunk in range(chunks):
            out_ref[chunk, to_rows, to_lanes] = jnp.zeros((share, LANES), BF16)

    for h, (x, y, grad) in enumerate(((near, far, grad_ref), (near_c, far_c, grad_c_ref))):
        for k in range(2):
            store(h, 3 * LANES * k, shared[k][0, h * features : (h + 1) * features, :])
        project = dot_tn(x[...], qkv_ref[own_rows, :]) + dot_tn(y[...], qkv_ref[far_rows, :])
        store(h, 6 * LANES, project)
        store(h, 11 * LANES, dot_tn(grad[...], attended_ref[...]))


def late_grads(place, near, far, qkv_grad, attended, grad, grad_c, shared):
    features = near[0].shape[1]
    rows = LATE_BLOCKS * (features // RING)
    spec = pl.BlockSpec(memory_space=pltpu.VMEM)
    return pl.pallas_call(
        late_kernel,
        out_shape=[jax.ShapeDtypeStruct((RING, rows, 3 * LANES), BF16)] * 2,
        in_specs=[pl.BlockSpec(memory_space=pltpu.SMEM)] + [spec] * 10,
        out_specs=[spec] * 2,
        compiler_params=params(60),
        cost_estimate=SMALL,
        name="late_grads",
    )(place, *near, *far, qkv_grad, attended, grad, grad_c, *shared)


def columns_kernel(
    place_ref, query_ref, key_ref, value_ref, w_out_ref, out_ref, share_ref
):
    share_ref[...] = w_out_ref[...]
    width = GROUP_HEADS * DH
    out_ref[:, 0:width] = query_ref[...]
    out_ref[:, width : width + DH] = key_ref[...]
    out_ref[:, width + DH :] = value_ref[...]


def their_columns(place, w_query, w_key, w_value, w_out, shares):
    rows = w_query.shape[0]
    width = GROUP_HEADS * DH + 2 * DH

    def theirs(width):
        return pl.BlockSpec((rows, width), lambda i, c: (0, 1 - c[0]))

    return pl.pallas_call(
        columns_kernel,
        grid_spec=pltpu.PrefetchScalarGridSpec(
            num_scalar_prefetch=1,
            grid=(1,),
            in_specs=[theirs(GROUP_HEADS * DH), theirs(DH), theirs(DH)]
            + [pl.BlockSpec((rows // shares, rows), lambda i, c: (c[1], 0))],
            out_specs=[
                pl.BlockSpec((rows, width), lambda i, c: (0, 0)),
                pl.BlockSpec((rows // shares, rows), lambda i, c: (0, 0)),
            ],
        ),
        out_shape=[
            jax.ShapeDtypeStruct((rows, width), BF16),
            jax.ShapeDtypeStruct((rows // shares, rows), BF16),
        ],
        compiler_params=params(60, "arbitrary"),
        cost_estimate=SMALL,
        name="their_columns",
    )(place, w_query, w_key, w_value, w_out)


def join_kernel(mine_ref, *refs):
    *parts, out_ref = refs
    rows = parts[0].shape[0]
    for k, part in enumerate(parts):
        at = jnp.bitwise_xor(mine_ref[0], k)
        out_ref[pl.ds(pl.multiple_of(at * rows, rows), rows), :] = part[...]


def join(mine, *parts):
    rows, width = parts[0].shape
    spec = pl.BlockSpec(memory_space=pltpu.VMEM)
    return pl.pallas_call(
        join_kernel,
        out_shape=jax.ShapeDtypeStruct((len(parts) * rows, width), parts[0].dtype),
        in_specs=[pl.BlockSpec(memory_space=pltpu.SMEM)] + [spec] * len(parts),
        out_specs=spec,
        compiler_params=params(16),
        cost_estimate=SMALL,
        name="join",
    )(mine.reshape(1), *parts)


def project_kernel(col_ref, own_ref, other_ref, gains_ref, gains_c_ref, query_ref, key_ref, value_ref, there_ref, x_own_ref, x_other_ref, qkv_ref, scale_ref):
    own = own_ref[...].astype(F32)
    other = other_ref[...].astype(F32)
    total = jnp.sum(own * own, axis=1, keepdims=True)
    total = total + jnp.sum(other * other, axis=1, keepdims=True)
    scale = lax.rsqrt(total / D + EPSILON)
    own = (own * scale * gains_ref[0:1, :]).astype(BF16)
    other = (other * scale * gains_c_ref[0:1, :]).astype(BF16)
    x_own_ref[...] = own
    x_other_ref[...] = other
    scale_ref[...] = scale
    here = jnp.concatenate([query_ref[...], key_ref[...], value_ref[...]], axis=1)
    qkv_ref[...] = (dot(own, here) + dot(other, there_ref[...])).astype(BF16)


def project(col, own, other, gains, gains_c, w_query, w_key, w_value, there):
    rows, features = own.shape
    width = there.shape[1]
    group = GROUP_HEADS * DH
    tile = rows // 2

    def whole(*shape):
        return pl.BlockSpec(shape, lambda i, c: (0,) * len(shape))

    def mine(width):
        return pl.BlockSpec((features, width), lambda i, c: (0, c[0]))

    def rowwise(width):
        return pl.BlockSpec((tile, width), lambda i, c: (i, 0))

    return pl.pallas_call(
        project_kernel,
        grid_spec=pltpu.PrefetchScalarGridSpec(
            num_scalar_prefetch=1,
            grid=(rows // tile,),
            in_specs=[
                rowwise(features),
                rowwise(features),
                whole(2, features),
                whole(2, features),
                mine(group),
                mine(DH),
                mine(DH),
                whole(features, width),
            ],
            out_specs=[rowwise(features), rowwise(features), rowwise(width), rowwise(1)],
        ),
        out_shape=[
            jax.ShapeDtypeStruct((rows, features), BF16),
            jax.ShapeDtypeStruct((rows, features), BF16),
            jax.ShapeDtypeStruct((rows, width), BF16),
            jax.ShapeDtypeStruct((rows, 1), F32),
        ],
        compiler_params=params(60, "arbitrary"),
        cost_estimate=SMALL,
        name="project",
    )(col, own, other, gains, gains_c, w_query, w_key, w_value, there)


def head_pair(col_ref, own, other):
    first, second = own[...], other[...]
    flipped = col_ref != 0
    return jnp.concatenate(
        [jnp.where(flipped, second, first), jnp.where(flipped, first, second)], axis=1
    )


def before_kernel(tiles, place_ref, *refs):
    near, near_c, far, far_c, attended, attended_c, here, there, own_ref, other_ref = refs
    is_near = (pl.program_id(0) >= tiles // 2).astype(jnp.int32) == place_ref[0]
    heads = head_pair(place_ref[2], attended, attended_c)
    own = jnp.where(is_near, near[...], far[...]).astype(F32)
    other = jnp.where(is_near, near_c[...], far_c[...]).astype(F32)
    own_ref[...] = own + dot(heads, here[...])
    other_ref[...] = other + dot(heads, there[...])


def after_kernel(place_ref, *refs):
    own_ref, other_ref, attended, attended_c, here, there, gains_ref, gains_c_ref = refs[0:8]
    hidden_ref, x_own_ref, x_other_ref, scale_ref = refs[8:12]
    heads = head_pair(place_ref[2], attended, attended_c)
    own = own_ref[...] + dot(heads, here[...])
    other = other_ref[...] + dot(heads, there[...])
    total = jnp.sum(own * own, axis=1, keepdims=True)
    total = total + jnp.sum(other * other, axis=1, keepdims=True)
    scale = lax.rsqrt(total / D + EPSILON)
    hidden_ref[...] = own
    scale_ref[...] = scale
    x_own_ref[...] = (own * scale * gains_ref[1:2, :]).astype(BF16)
    x_other_ref[...] = (other * scale * gains_c_ref[1:2, :]).astype(BF16)


TOKEN_TILE = 256


def rowwise(width):
    return pl.BlockSpec((TOKEN_TILE, width), lambda i, p: (i, 0))


def whole(*shape):
    return pl.BlockSpec(shape, lambda i, p: (0,) * len(shape))


def hidden_before(place, tokens, attended, here, there):
    half, features = tokens[0].shape
    rows, heads = attended[0].shape
    tiles = rows // TOKEN_TILE
    per_half = half // TOKEN_TILE
    halfwise = pl.BlockSpec((TOKEN_TILE, features), lambda i, p: (i % per_half, 0))
    return pl.pallas_call(
        functools.partial(before_kernel, tiles),
        grid_spec=pltpu.PrefetchScalarGridSpec(
            num_scalar_prefetch=1,
            grid=(tiles,),
            in_specs=[halfwise] * 4 + [rowwise(heads)] * 2 + [whole(2 * heads, features)] * 2,
            out_specs=[rowwise(features)] * 2,
        ),
        out_shape=[jax.ShapeDtypeStruct((rows, features), F32)] * 2,
        compiler_params=params(56, "arbitrary"),
        cost_estimate=pl.CostEstimate(
            flops=8 * rows * features * heads,
            bytes_accessed=16 * rows * features,
            transcendentals=0,
        ),
        name="hidden_before",
    )(place, *tokens, *attended, here, there)


def hidden_after(place, before, attended, here, there, gains, gains_c):
    rows, features = before[0].shape
    heads = attended[0].shape[1]
    return pl.pallas_call(
        after_kernel,
        grid_spec=pltpu.PrefetchScalarGridSpec(
            num_scalar_prefetch=1,
            grid=(rows // TOKEN_TILE,),
            in_specs=[rowwise(features)] * 2
            + [rowwise(heads)] * 2
            + [whole(2 * heads, features)] * 2
            + [whole(2, features)] * 2,
            out_specs=[rowwise(features)] * 3 + [rowwise(1)],
        ),
        out_shape=[
            jax.ShapeDtypeStruct((rows, features), F32),
            jax.ShapeDtypeStruct((rows, features), BF16),
            jax.ShapeDtypeStruct((rows, features), BF16),
            jax.ShapeDtypeStruct((rows, 1), F32),
        ],
        compiler_params=params(56, "arbitrary"),
        cost_estimate=SMALL,
        name="hidden_after",
    )(place, *before, *attended, here, there, gains, gains_c)


def expert_kernel(shared, aliased, first, order_ref, *refs):
    x_own, x_other, o_own, o_other, gates_ref = refs[0:5]
    weights = refs[5:17]
    grads = refs[17 + aliased : 19 + aliased]
    pair_ref, inner_ref = refs[19 + aliased : 21 + aliased]
    step = pl.program_id(0) + first
    rows, features = x_own.shape
    tile = 512
    up_own = jnp.concatenate([weights[k][0] for k in (0, 1, 6, 7)], axis=1)
    up_other = jnp.concatenate([weights[k][0] for k in (2, 3, 8, 9)], axis=1)
    down_own = jnp.concatenate([weights[k][0] for k in (4, 10)], axis=0)
    down_other = jnp.concatenate([weights[k][0] for k in (5, 11)], axis=0)

    def token_tile(t, carry):
        at = pl.ds(pl.multiple_of(t * tile, tile), tile)
        pre = dot(x_own[at, :], up_own) + dot(x_other[at, :], up_other)
        back = dot_nt(o_own[at, :], down_own) + dot_nt(o_other[at, :], down_other)
        for k in range(2):
            pre_gate = pre[:, 2 * k * LANES : (2 * k + 1) * LANES]
            pre_up = pre[:, (2 * k + 1) * LANES : (2 * k + 2) * LANES]
            inner_grad = back[:, k * LANES : (k + 1) * LANES]
            sigmoid = 1.0 / (1.0 + jnp.exp(-pre_gate))
            silu = pre_gate * sigmoid
            inner = silu * pre_up
            if not shared:
                shape = (gates_ref.shape[0], LANES)
                expert = lax.broadcasted_iota(jnp.int32, shape, 0) % (gates_ref.shape[0] // 3)
                chosen = (expert == order_ref[2 * step + k]).astype(F32).astype(BF16)
                gate = dot_tn(gates_ref[:, at], chosen)
                inner = gate * inner
                inner_grad = gate * inner_grad
            gate_grad = inner_grad * pre_up * (sigmoid * (1.0 + pre_gate * (1.0 - sigmoid)))
            inner_ref[0, at, k * LANES : (k + 1) * LANES] = inner.astype(BF16)
            pair_ref[0, at, 2 * k * LANES : (2 * k + 1) * LANES] = gate_grad.astype(BF16)
            pair_ref[0, at, (2 * k + 1) * LANES : (2 * k + 2) * LANES] = (
                inner_grad * silu
            ).astype(BF16)
        return carry

    lax.fori_loop(0, rows // tile, token_tile, 0)
    pairs = pair_ref[0]
    for h, x in enumerate((x_own, x_other)):
        wide = dot_tn(x[...], pairs).astype(BF16)
        for k in range(2):
            grads[k][0, h * features : (h + 1) * features, 0 : 2 * LANES] = wide[
                :, 2 * k * LANES : (2 * k + 2) * LANES
            ]
    inner = inner_ref[0]
    tile = 256
    for h, o in enumerate((o_own, o_other)):
        for j in range(features // tile):
            low = dot_tn(inner, o[:, j * tile : (j + 1) * tile]).astype(BF16)
            for k in range(2):
                for b in range(tile // LANES):
                    at = h * features + j * tile + b * LANES
                    grads[k][0, at : at + LANES, 2 * LANES :] = low[
                        k * LANES : (k + 1) * LANES, b * LANES : (b + 1) * LANES
                    ]


def expert_specs(features, place, wide, low):
    specs = []
    if wide:
        block = pl.BlockSpec((1, features, LANES), lambda i, o: (place(i, o)[0], 0, place(i, o)[1]))
        specs += [block] * 4
    if low:
        block = pl.BlockSpec((1, LANES, features), lambda i, o: (*place(i, o), 0))
        specs += [block] * 2
    return specs


def expert_grads(order, first, last, total, x, o, gates, weights, kept):
    shared = total is None
    steps = last - first
    rows, features = x[0].shape
    aliased = len(kept)

    def fixed(*shape):
        return pl.BlockSpec(shape, lambda i, o: (0,) * len(shape))

    def stepped(*shape):
        return pl.BlockSpec((1, *shape), lambda i, o: (i, 0, 0))

    def placed(*shape):
        return pl.BlockSpec((1, *shape), lambda i, o: (i + first, 0, 0))

    specs = []
    for k in range(2):
        if shared:

            def picked(i, o, k=k):
                return 0, 2 * o[o.shape[0] - 1] + k

        else:

            def picked(i, o, k=k):
                return o[2 * (i + first) + k], o[o.shape[0] - 1]

        specs += expert_specs(features, picked, True, True)
    total = steps if shared else total
    return pl.pallas_call(
        functools.partial(expert_kernel, shared, aliased, first),
        grid_spec=pltpu.PrefetchScalarGridSpec(
            num_scalar_prefetch=1,
            grid=(steps,),
            in_specs=[fixed(rows, features)] * 4
            + [fixed(*gates.shape)]
            + specs
            + [pl.BlockSpec(memory_space=pl.ANY)] * aliased,
            out_specs=[stepped(2 * features, 3 * LANES)] * 2
            + [placed(rows, 4 * LANES), placed(rows, 2 * LANES)],
        ),
        out_shape=[jax.ShapeDtypeStruct((steps, 2 * features, 3 * LANES), BF16)] * 2
        + [
            jax.ShapeDtypeStruct((total, rows, 4 * LANES), BF16),
            jax.ShapeDtypeStruct((total, rows, 2 * LANES), BF16),
        ],
        input_output_aliases={18 + k: 2 + k for k in range(aliased)},
        compiler_params=params(40, "arbitrary"),
        cost_estimate=SMALL,
        name="expert_grads",
    )(order, *x, *o, gates, *weights, *weights, *kept)


def mix_kernel(back, group, order_ref, *refs):
    acts_ref, shared_ref = refs[0:2]
    each = 2 if back else 1
    count = 2 * group * each
    weights = refs[2 : 2 + count]
    shared = refs[2 + count : 2 + count + 2 * each]
    out_ref, total_ref = refs[2 + count + 2 * each :]
    step = pl.program_id(0)
    rows = out_ref.shape[0]
    tile = 512
    times = dot_nt if back else dot
    along = 1 if back else 0

    @pl.when(step == 0)
    def _():
        both = jnp.concatenate([w[0] for w in shared], axis=along)
        for t in range(rows // tile):
            at = slice(t * tile, (t + 1) * tile)
            total_ref[at, :] = times(shared_ref[0, at, :], both)

    both = jnp.concatenate([w[0] for w in weights], axis=along)
    for t in range(rows // tile):
        at = slice(t * tile, (t + 1) * tile)
        acts = jnp.concatenate([acts_ref[g, at, :] for g in range(group)], axis=1)
        total_ref[at, :] += times(acts, both)

    @pl.when(step == pl.num_programs(0) - 1)
    def _():
        out_ref[...] = total_ref[...].astype(out_ref.dtype)


def mix(back, dtype, order, acts, shared_acts, weights, shared_weights):
    pairs, rows, width = acts.shape
    features = weights[0].shape[1] if back else weights[0].shape[2]
    group = 4 if pairs % 4 == 0 else 1

    def spec(place):
        if back:
            return pl.BlockSpec((1, features, LANES), lambda i, o: (place(i, o)[0], 0, place(i, o)[1]))
        return pl.BlockSpec((1, LANES, features), lambda i, o: (*place(i, o), 0))

    def routed(k):
        return spec(lambda i, o: (o[2 * group * i + k], o[o.shape[0] - 1]))

    def common(k):
        return spec(lambda i, o: (0, 2 * o[o.shape[0] - 1] + k))

    return pl.pallas_call(
        functools.partial(mix_kernel, back, group),
        grid_spec=pltpu.PrefetchScalarGridSpec(
            num_scalar_prefetch=1,
            grid=(pairs // group,),
            in_specs=[
                pl.BlockSpec((group, rows, width), lambda i, o: (i, 0, 0)),
                pl.BlockSpec((1, rows, width), lambda i, o: (0, 0, 0)),
            ]
            + [routed(k) for k in range(2 * group) for _ in weights]
            + [common(k) for k in range(2) for _ in weights],
            out_specs=pl.BlockSpec((rows, features), lambda i, o: (0, 0)),
            scratch_shapes=[pltpu.VMEM((rows, features), F32)],
        ),
        out_shape=jax.ShapeDtypeStruct((rows, features), dtype),
        compiler_params=params(48, "arbitrary"),
        cost_estimate=SMALL,
        name="mix",
    )(order, acts, shared_acts, *weights * (2 * group), *shared_weights * 2)


def chip_sum_kernel(own_ref, other_ref, hidden_ref, gains_ref, total_ref, rounded_ref, product_ref):
    total = own_ref[...] + other_ref[...].astype(F32)
    total_ref[...] = total
    rounded_ref[...] = total.astype(BF16)
    product_ref[...] = lax.dot_general(
        jnp.ones((8, total.shape[1]), F32),
        total * gains_ref[1:2, :] * hidden_ref[...],
        (((1,), (1,)), ((), ())),
        precision=lax.Precision.HIGHEST,
        preferred_element_type=F32,
    )


def chip_sum(own, other, hidden, gains):
    rows, features = own.shape
    spec = pl.BlockSpec((TOKEN_TILE, features), lambda i: (i, 0))
    return pl.pallas_call(
        chip_sum_kernel,
        grid=(rows // TOKEN_TILE,),
        out_shape=[
            jax.ShapeDtypeStruct((rows, features), F32),
            jax.ShapeDtypeStruct((rows, features), BF16),
            jax.ShapeDtypeStruct((8, rows), F32),
        ],
        in_specs=[spec, spec, spec, pl.BlockSpec(gains.shape, lambda i: (0, 0))],
        out_specs=[spec, spec, pl.BlockSpec((8, TOKEN_TILE), lambda i: (0, i))],
        compiler_params=params(24, "arbitrary"),
        cost_estimate=SMALL,
        name="chip_sum",
    )(own, other, hidden, gains)


def norm_back_kernel(tiles, place_ref, *refs):
    sum_ref, came_ref, hidden_ref, scale_ref, out_grad_ref, gains_ref = refs[0:6]
    products = refs[6:10]
    hidden_grad_ref, rounded_ref, gain_ref = refs[10:13]
    step = pl.program_id(0)
    part = (step >= tiles // 2).astype(jnp.int32)
    grad = sum_ref[...] + came_ref[...].astype(F32)
    hidden = hidden_ref[...]
    scale = scale_ref[...]
    total = (products[0][...] + products[1][...]) + (products[2][...] + products[3][...])
    mean = lax.dot_general(
        total,
        jnp.full((8, LANES), 1.0 / (8 * D), F32),
        (((0,), (0,)), ((), ())),
        precision=lax.Precision.HIGHEST,
        preferred_element_type=F32,
    )[:, 0:1]
    result = out_grad_ref[...].astype(F32) + scale * (grad * gains_ref[1:2, :])
    result = result - hidden * (scale * scale * scale * mean)
    hidden_grad_ref[...] = result
    rounded_ref[...] = result.astype(BF16)

    @pl.when(step == 0)
    def _():
        gain_ref[...] = jnp.zeros_like(gain_ref)

    @pl.when(part == place_ref[0])
    def _():
        gain_ref[...] += jnp.sum(grad * hidden * scale, axis=0, keepdims=True)


def norm_back(place, sums, came, hidden, scale, out_grad, gains, products):
    rows, features = hidden.shape
    tiles = rows // TOKEN_TILE
    lanes = pl.BlockSpec((8, TOKEN_TILE), lambda i, p: (0, i))
    return pl.pallas_call(
        functools.partial(norm_back_kernel, tiles),
        grid_spec=pltpu.PrefetchScalarGridSpec(
            num_scalar_prefetch=1,
            grid=(tiles,),
            in_specs=[rowwise(features)] * 3
            + [rowwise(1), rowwise(features), whole(2, features)]
            + [lanes] * 4,
            out_specs=[rowwise(features)] * 2 + [whole(1, features)],
        ),
        out_shape=[
            jax.ShapeDtypeStruct((rows, features), F32),
            jax.ShapeDtypeStruct((rows, features), BF16),
            jax.ShapeDtypeStruct((1, features), F32),
        ],
        compiler_params=params(48, "arbitrary"),
        cost_estimate=SMALL,
        name="norm_back",
    )(place, sums, came, hidden, scale, out_grad, gains, *products)


def ring_of(size):
    return list(range(0, size, 2)) + list(range(1, size, 2))[::-1]


def unpack_kernel(aliased, plan_ref, *refs):
    chunks = refs[0:2]
    gate_ref, up_ref, down_ref = refs[2 + aliased : 5 + aliased]
    rows = gate_ref.shape[1]

    def write(chunk_ref):
        first = chunk_ref.shape[0] - rows
        gate_ref[0] = chunk_ref[first:, 0:LANES].astype(F32)
        up_ref[0] = chunk_ref[first:, LANES : 2 * LANES].astype(F32)
        for b in range(rows // LANES):
            at = slice(first + b * LANES, first + (b + 1) * LANES)
            down_ref[0, :, b * LANES : (b + 1) * LANES] = chunk_ref[at, 2 * LANES :].astype(F32)

    for k in range(2):
        pl.when(pl.program_id(0) == k)(lambda k=k: write(chunks[k]))


def unpack(plan, first, wave, chunks, shapes, outs):
    rows = shapes[0][1]

    def place(d, n):
        block = n[n.shape[0] - 1]
        return n[first + d], 1 - block if wave else block

    def wide(d, n):
        expert, block = place(d, n)
        return (expert, 0, block)

    def low(d, n):
        expert, block = place(d, n)
        return (expert, block, 0)

    aliased = len(outs)
    return pl.pallas_call(
        functools.partial(unpack_kernel, aliased),
        grid_spec=pltpu.PrefetchScalarGridSpec(
            num_scalar_prefetch=1,
            grid=(2,),
            in_specs=[pl.BlockSpec(chunk.shape, lambda d, n: (0, 0)) for chunk in chunks]
            + [pl.BlockSpec(memory_space=pl.ANY)] * aliased,
            out_specs=[
                pl.BlockSpec((1, rows, LANES), wide),
                pl.BlockSpec((1, rows, LANES), wide),
                pl.BlockSpec((1, LANES, rows), low),
            ],
        ),
        out_shape=[jax.ShapeDtypeStruct(shape, F32) for shape in shapes],
        input_output_aliases={3 + k: k for k in range(aliased)},
        compiler_params=params(16, "arbitrary"),
        cost_estimate=SMALL,
        name="unpack",
    )(plan, *chunks, *outs)


def ring_sum_kernel(came_ref, mine_ref, *outs):
    total = (came_ref[...].astype(F32) + mine_ref[...].astype(F32)).astype(BF16)
    if len(outs) == 1:
        outs[0][...] = total
    else:
        half = pl.program_id(1) // (pl.num_programs(1) // 2)
        for k, out_ref in enumerate(outs):

            @pl.when(half == k)
            def _(out_ref=out_ref):
                out_ref[...] = total


def ring_sum(came, mine, first, halved):
    count, rows, lanes = came.shape
    tiles = 4
    spec = pl.BlockSpec((1, rows // tiles, lanes), lambda i, j: (i, j, 0))
    term = pl.BlockSpec((1, rows // tiles, lanes), lambda i, j: (first + i, j, 0))

    def half(k):
        first = k * tiles // 2
        last = tiles // 2 - 1
        return pl.BlockSpec(
            (1, rows // tiles, lanes), lambda i, j: (i, jnp.clip(j - first, 0, last), 0)
        )

    shapes = [jax.ShapeDtypeStruct((count, rows // 2, lanes), BF16)] * 2
    return pl.pallas_call(
        ring_sum_kernel,
        grid=(count, tiles),
        in_specs=[spec, term],
        out_specs=[half(0), half(1)] if halved else spec,
        out_shape=shapes if halved else jax.ShapeDtypeStruct(came.shape, BF16),
        compiler_params=params(16, "arbitrary", "arbitrary"),
        cost_estimate=SMALL,
        name="ring_sum",
    )(came, mine)


def late_load_kernel(plan_ref, pack_ref, main_ref, out_ref):
    rows = pack_ref.shape[1]
    out_ref[0:rows, :] = pack_ref[0]
    out_ref[rows:, :] = main_ref[...]


def late_load(plan, at, pack, main):
    rows, lanes = pack.shape[1:]
    total = rows + main.shape[0]
    return pl.pallas_call(
        late_load_kernel,
        grid_spec=pltpu.PrefetchScalarGridSpec(
            num_scalar_prefetch=1,
            grid=(1,),
            in_specs=[
                pl.BlockSpec((1, rows, lanes), lambda i, n: (n[at], 0, 0)),
                pl.BlockSpec(main.shape, lambda i, n: (0, 0)),
            ],
            out_specs=pl.BlockSpec((total, lanes), lambda i, n: (0, 0)),
        ),
        out_shape=jax.ShapeDtypeStruct((total, lanes), BF16),
        compiler_params=params(16, "arbitrary"),
        cost_estimate=SMALL,
        name="late_load",
    )(plan, pack, main)


def late_add_kernel(plan_ref, pack_ref, came_ref, *outs):
    total = (came_ref[...].astype(F32) + pack_ref[0].astype(F32)).astype(BF16)
    for out_ref in outs:
        out_ref[...] = total


def late_add(plan, at, pack, came, copied=False):
    rows, lanes = pack.shape[1:]
    spec = pl.BlockSpec((rows, lanes), lambda i, n: (0, 0))
    shape = jax.ShapeDtypeStruct(came.shape, BF16)
    return pl.pallas_call(
        late_add_kernel,
        grid_spec=pltpu.PrefetchScalarGridSpec(
            num_scalar_prefetch=1,
            grid=(1,),
            in_specs=[pl.BlockSpec((1, rows, lanes), lambda i, n: (n[at], 0, 0)), spec],
            out_specs=[spec] * 2 if copied else spec,
        ),
        out_shape=[shape, jax.ShapeDtypeStruct((rows, lanes), BF16)] if copied else shape,
        input_output_aliases={2: 0},
        compiler_params=params(16, "arbitrary"),
        cost_estimate=SMALL,
        name="late_add",
    )(plan, pack, came)


def late_join_kernel(col_ref, mine_ref, other_ref, gains_ref, main_ref, out_ref):
    units = 7
    out_ref[mine_ref.shape[0] :, :] = main_ref[...]
    share = mine_ref.shape[0] // LATE_BLOCKS
    to_rows, to_lanes = unit_slices(2 * units, share)
    blocks = gains_ref.shape[1] // LANES
    gains = [
        gains_ref[g : g + 1, b * LANES : (b + 1) * LANES] for g in range(2) for b in range(blocks)
    ]
    gains = jnp.concatenate(gains + [jnp.zeros((share - len(gains), LANES), F32)], axis=0)
    own = [mine_ref[unit_slices(b, share)] for b in range(units)]
    other = [other_ref[unit_slices(units + b, share)] for b in range(units)]
    for b in range(units):
        first, second = own[b], other[b]
        flipped = col_ref[0] != 0
        out_ref[unit_slices(b, share)] = jnp.where(flipped, second, first)
        out_ref[unit_slices(units + b, share)] = jnp.where(flipped, first, second)
    out_ref[to_rows, to_lanes] = gains.astype(BF16)


def late_join(col, mine, other, gains, main):
    rows, lanes = mine.shape
    total = rows + main.shape[0]

    def all_of(*shape):
        return pl.BlockSpec(shape, lambda i, c: (0, 0))

    return pl.pallas_call(
        late_join_kernel,
        grid_spec=pltpu.PrefetchScalarGridSpec(
            num_scalar_prefetch=1,
            grid=(1,),
            in_specs=[all_of(rows, lanes)] * 2 + [all_of(*gains.shape), all_of(*main.shape)],
            out_specs=all_of(total, lanes),
        ),
        out_shape=jax.ShapeDtypeStruct((total, lanes), BF16),
        compiler_params=params(16, "arbitrary"),
        cost_estimate=SMALL,
        name="late_join",
    )(col, mine, other, gains, main)


def unpack_late_kernel(first_step, steps, plan_ref, *refs):
    chunks = refs[0 : 2 * steps]
    sgate, sup, sdown, query, key, value, out, gains, all_ref, gain_ref = refs[2 * steps :]
    share, features = chunks[0].shape[0] // LATE_BLOCKS, all_ref.shape[2]
    for k in range(2):
        for step in range(steps):
            at = plan_ref[first_step + 2 * step + k]
            chunk = chunks[steps * k + step]
            to_rows = pl.ds(pl.multiple_of(at * share, share), share)
            for unit in range(14):
                lanes = slice(unit % 7 * LANES, (unit % 7 + 1) * LANES)
                all_ref[k, unit // 7, to_rows, lanes] = chunk[unit_slices(unit, share)]
            if k == 0:
                to_rows = pl.ds(pl.multiple_of(at * GAIN_ROWS, GAIN_ROWS), GAIN_ROWS)
                rows, lanes = unit_slices(14, share)
                gain_ref[to_rows, :] = chunk[rows.start : rows.start + GAIN_ROWS, lanes]
    total = jnp.zeros((GAIN_ROWS, LANES), F32)
    for step in range(steps):
        total = total + gain_ref[step * GAIN_ROWS : (step + 1) * GAIN_ROWS, :].astype(F32)
    blocks = features // LANES
    for row in range(2 * blocks):
        gains[row // blocks : row // blocks + 1, row % blocks * LANES : (row % blocks + 1) * LANES] = (
            total[row : row + 1, :]
        )
    flipped = plan_ref[plan_ref.shape[0] - 1] != 0
    for c in range(2):
        for b in range(14):
            lanes = slice(b % 7 * LANES, (b % 7 + 1) * LANES)
            first, second = all_ref[0, c, :, lanes], all_ref[1, c, :, lanes]
            if b >= 7:
                first, second = second, first
            block = jnp.where(flipped, second, first).astype(F32)
            if b < 6:
                at = slice((2 * c + b // 3) * LANES, (2 * c + b // 3 + 1) * LANES)
                if b % 3 < 2:
                    (sgate, sup)[b % 3][:, at] = block
                else:
                    for k in range(features // LANES):
                        here = slice(k * LANES, (k + 1) * LANES)
                        sdown[at, here] = block[here, :]
            elif b < 9:
                at = (GROUP_HEADS * c + b - 6) * LANES
                query[:, at : at + LANES] = block
            elif b < 11:
                (key, value)[b - 9][:, c * LANES : (c + 1) * LANES] = block
            else:
                at = (GROUP_HEADS * c + b - 11) * LANES
                out[at : at + LANES, :] = block.T


def unpack_late(plan, first_step, chunks, shapes):
    steps = len(chunks[0])
    features = shapes[0][0]
    share = features // steps
    chunk = pl.BlockSpec((LATE_BLOCKS * share, 3 * LANES), lambda i, n: (0, 0))
    return pl.pallas_call(
        functools.partial(unpack_late_kernel, first_step, steps),
        grid_spec=pltpu.PrefetchScalarGridSpec(
            num_scalar_prefetch=1,
            grid=(1,),
            in_specs=[chunk] * (2 * steps),
            out_specs=[pl.BlockSpec(shape, lambda i, n: (0, 0)) for shape in shapes],
            scratch_shapes=[
                pltpu.VMEM((2, 2, features, 7 * LANES), BF16),
                pltpu.VMEM((steps * GAIN_ROWS, LANES), BF16),
            ],
        ),
        out_shape=[jax.ShapeDtypeStruct(shape, F32) for shape in shapes],
        compiler_params=params(48, "arbitrary"),
        cost_estimate=SMALL,
        name="unpack_late",
    )(plan, *chunks[0], *chunks[1])


def plans(ring, each):
    size = len(ring)
    rows = []
    for member in range(size):
        place = ring.index(member)
        for col in range(2):
            chunks = []
            for step in range(2 * size - 1):
                for which in range(2):
                    sign = 1 if which == col else -1
                    chunks.append((place - sign * step) % size)
            experts = []
            for start in (0, size - 1):
                for step in range(start, start + size):
                    for k in range(each):
                        for which in range(2):
                            second = col if which == 0 else 1 - col
                            experts.append(2 * each * chunks[2 * step + which] + each * second + k)
            rows.append(experts + chunks + [col])
    return np.asarray(rows, np.int32)


def body(
    tokens_in,
    norm_gain_attn,
    w_query,
    w_key,
    w_value,
    w_out,
    norm_gain_ffn,
    w_gate,
    w_up,
    w_down,
    w_shared_gate,
    w_shared_up,
    w_shared_down,
    routes,
    gate_weights,
    seq_lengths,
    out_grad,
):
    row = lax.axis_index("row")
    col = lax.axis_index("col")
    dp = lax.axis_index("dp")
    dp_size = lax.axis_size("dp")
    local_rows, local_features = tokens_in.shape
    experts = w_gate.shape[0]
    group_width = GROUP_HEADS * DH
    col_ref = col.reshape(1)

    ring_size = RING
    ring = ring_of(ring_size)
    starts = range(0, dp_size, ring_size)
    rights = [
        (g + ring[k], g + ring[(k + 1) % ring_size]) for g in starts for k in range(ring_size)
    ]
    lefts = [(b, a) for a, b in rights]
    routes_of = [
        [(2 * a, 2 * b) for a, b in ways[0]] + [(2 * a + 1, 2 * b + 1) for a, b in ways[1]]
        for ways in ((rights, lefts), (lefts, rights))
    ]
    experts_each = experts // (2 * ring_size)
    plan = jnp.asarray(plans(ring, experts_each))
    plan = lax.dynamic_slice(
        plan, (2 * (dp % ring_size) + col, jnp.int32(0)), (1, plan.shape[1])
    ).reshape(-1)

    def send(values, which):
        return lax.ppermute(values, ("dp", "col"), routes_of[which])

    def chunk_at(step, which):
        return plan[2 * experts + 2 * step + which]

    def across_rings(values):
        if len(starts) == 1:
            return values
        peers = [[g + k for g in starts] for k in range(ring_size)]
        return lax.psum(values, "dp", axis_index_groups=peers)

    where = jnp.stack([row, seq_lengths[0], col])
    tokens_y = swap(tokens_in, "row")
    tokens_c = swap(tokens_in, "col")
    count = 4
    member = dp % count
    there, out_y = their_columns(
        jnp.stack([col, member]), w_query, w_key, w_value, w_out, count
    )
    gains = jnp.stack([norm_gain_attn, norm_gain_ffn])
    there = swap(there, "col")
    gains_c = swap(gains, "col")

    def project_half(own, other):
        return project(col_ref, own, other, gains, gains_c, w_query, w_key, w_value, there)

    near = project_half(tokens_in, tokens_c)
    gate_c = swap(w_gate, "col")
    out_y = swap(out_y, "row")
    tokens_y = after(tokens_y, near[2], out_y)
    tokens_yc = swap(tokens_y, "col")
    grad_y = swap(after(out_grad, tokens_y), "row")
    far = project_half(tokens_y, tokens_yc)
    shares = [out_y]
    for k in range(1, count):
        part = out_y if k < 3 else after(out_y, far[2])
        shares.append(lax.ppermute(part, "dp", [(m, m ^ k) for m in range(dp_size)]))
    where = after(where, grad_y, *shares)

    w_sgate, w_sup, w_sdown = w_shared_gate[None], w_shared_up[None], w_shared_down[None]
    up_c = swap(after(w_up, gate_c, tokens_yc), "col")

    attended = attend(where, near[2], far[2])
    attended_y = swap(attended, "row")
    attended_c = swap(attended, "col")
    out_c = swap(after(w_out, tokens_yc), "col")
    before = hidden_before(
        where,
        [tokens_in, tokens_c, tokens_y, tokens_yc],
        [attended, attended_c],
        w_out,
        out_c,
    )
    down_c = swap(after(w_down, tokens_yc), "col")
    attended_y = after(attended_y, before[0])
    out_y = join(member, *shares)
    out_yc = swap(out_y, "col")
    attended_yc = swap(attended_y, "col")
    grad_own = join(row, out_grad, grad_y)
    grad_other = swap(grad_own, "col")
    hidden, x_own, x_other, scale_ffn = hidden_after(
        where, before, [attended_y, attended_yc], out_y, out_yc, gains, gains_c
    )
    sgate_c, sup_c, sdown_c = (
        swap(after(w, attended_yc), "col") for w in (w_sgate, w_sup, w_sdown)
    )

    choices = jnp.arange(experts, dtype=jnp.int32)[:, None]
    dense = sum(
        jnp.where(routes[:, k][None, :] == choices, gate_weights[:, k][None, :], 0.0)
        for k in range(routes.shape[1])
    )
    gates = []
    for _ in range(3):
        gates.append(lax.reduce_precision(dense, 8, 7))
        dense = dense - gates[-1]
    gates = jnp.concatenate(gates, axis=0).astype(BF16)

    each = experts_each
    order = plan
    pairs_total = experts // 2
    routed = [w_gate, w_up, gate_c, up_c, w_down, down_c]
    shared = [w_sgate, w_sup, sgate_c, sup_c, w_sdown, sdown_c]

    def run(first, last, order, kept):
        return expert_grads(
            order,
            first,
            last,
            pairs_total,
            [x_own, x_other],
            [grad_own, grad_other],
            gates,
            routed,
            kept,
        )

    first = run(0, 1, order, ())
    kept = first[2:]
    sums = [first[0], first[1]]
    runs = {}
    mixed = {}
    normed = {}

    def work_experts(first, last):
        def work(order, ties):
            nonlocal kept
            result = run(first, last, order, tuple(kept))
            kept = result[2:]
            for at in range(first, last):
                runs[at] = (*result[0:2], at - first)
            return [kept[0]]

        return work

    def work_shared(order, ties):
        runs["shared"] = expert_grads(
            order, 0, 1, None, [x_own, x_other], [grad_own, grad_other], gates, shared, ()
        )
        return [runs["shared"][2]]

    def work_back(half):
        def work(order, ties):
            mixed[True, half] = mix(
                True,
                BF16 if half else F32,
                order,
                kept[0],
                runs["shared"][2],
                routed[2 * half : 2 * half + 2],
                shared[2 * half : 2 * half + 2],
            )
            if half:
                normed["other"] = swap(mixed[True, 1], "col")
                return [mixed[True, 1]]
            total, rounded, product = chip_sum(mixed[True, 0], normed["other"], hidden, gains)
            product_c = swap(product, "col")
            normed["sum"] = total
            normed["tie"] = rounded
            normed["came"] = swap(rounded, "row")
            normed["products"] = [product, product_c, swap(product, "row"), swap(product_c, "row")]
            return [mixed[True, 0]]

        return work

    def work_out(half):
        def work(order, ties):
            mixed[False, half] = mix(
                False,
                BF16 if half else F32,
                order,
                kept[1],
                runs["shared"][3],
                routed[4 + half : 5 + half],
                shared[4 + half : 5 + half],
            )
            return [mixed[False, half]]

        return work

    start = row * local_rows

    def my_rows(values):
        return lax.dynamic_slice_in_dim(values, start, local_rows, axis=0)

    def their_rows(values):
        return lax.dynamic_slice_in_dim(values, local_rows - start, local_rows, axis=0)

    def work_hidden(order, ties):
        normed["hidden"], normed["grad"], normed["gain"] = norm_back(
            after(where, *ties),
            normed["sum"],
            normed["came"],
            hidden,
            scale_ffn,
            grad_own,
            gains,
            normed["products"],
        )
        normed["grad_c"] = swap(normed["grad"], "col")
        return [normed["grad"]]

    def work_attend(order, ties):
        normed["qkv"] = attend_back(
            after(where, *ties), near[2], far[2], normed["grad"], normed["grad_c"], w_out, out_c
        )
        return [normed["qkv"]]

    def work_late(order, ties):
        normed["packs"] = late_grads(
            after(where, *ties),
            near[0:2],
            far[0:2],
            normed["qkv"],
            attended,
            normed["grad"],
            normed["grad_c"],
            runs["shared"][0:2],
        )
        return normed["packs"]

    def work_tie(order, ties):
        return [normed["tie"]]

    tasks = [work_experts(at, min(at + 2, pairs_total)) for at in range(1, pairs_total, 2)]
    tasks += [work_shared, work_back(1), work_back(0), None, work_out(0), work_tie]
    ends = [work_hidden, work_attend, work_late]
    tasks += [None] * (2 * ring_size - 2 - len(tasks) - len(ends)) + ends
    got = [None, None]
    got[0] = send(sums[0], 0)
    tasks.pop(0)(after(order, *sums), sums)
    got[1] = send(after(sums[1], kept[0]), 1)
    for s in range(1, ring_size):
        for k in range(2):
            last = sums
            task = tasks.pop(0) if tasks else None
            if task:
                last = task(after(order, *last), last)
            mine = runs[s]
            sums[k] = ring_sum(after(got[k], *last), mine[k], mine[2], s + 1 == ring_size)
            if s + 1 < ring_size:
                got[k] = send(sums[k], k)
            else:
                sums[k], got[k] = sums[k]
    crossed = [swap(across_rings(total), "col") for total in got]
    waves = [[across_rings(total)[0] for total in sums], [crossed[1][0], crossed[0][0]]]

    chunks_first = 2 * experts
    late_total = 2 * (ring_size - 1)

    def back_to_tokens(ties):
        hidden_grad = normed["hidden"]
        qkv_grad = after(normed["qkv"], *ties)
        here = jnp.concatenate(
            [halves(w, 1, col)[0] for w in (w_query, w_key, w_value)], axis=1
        )
        tokens_back = dot_nt(qkv_grad, here) + swap(
            dot_nt(qkv_grad, there).astype(BF16), "col"
        ).astype(F32)
        tokens_back = my_rows(tokens_back) + swap(
            their_rows(tokens_back).astype(BF16), "row"
        ).astype(F32)
        scale_attn = near[3]
        tokens_f32 = tokens_in.astype(F32)
        gain_attn_part = jnp.sum(tokens_back * tokens_f32 * scale_attn, axis=0)
        scaled = tokens_back * norm_gain_attn
        products = jnp.sum(scaled * tokens_f32, axis=1, keepdims=True)
        mean = (products + swap(products, "col")) / D
        tokens_grad = (
            my_rows(hidden_grad) + scale_attn * scaled - tokens_f32 * scale_attn**3 * mean
        ).astype(BF16)

        gain_parts = jnp.concatenate([gain_attn_part[None], normed["gain"]], axis=0)
        normed["gains"] = across_rings(gain_parts + swap(gain_parts, "row"))
        normed["tokens_grad"] = tokens_grad

    def block_rows(ties):
        ffn_sum = after(mixed[False, 0], *ties) + swap(mixed[False, 1], "col").astype(F32)
        ffn_rows = my_rows(ffn_sum) + swap(their_rows(ffn_sum).astype(BF16), "row").astype(F32)
        block_out = (my_rows(hidden) + ffn_rows).astype(BF16)
        normed["block_out"] = block_out

    shapes = [w_gate.shape, w_up.shape, w_down.shape]
    placed = ()
    late_out = [[], []]
    last, got = [], [None, None]
    moves = [(wave, step) for wave in range(2) for step in range(ring_size - 1)]
    for number, (wave, step) in enumerate(moves):
        current = [None, None]
        copies = [None, None]
        turn = number == ring_size - 1
        for k in range(2):
            at = chunks_first + 2 * number + k
            pack = normed["packs"][k]
            if number == 0:
                current[k] = late_load(plan, at, pack, after(waves[0][k], *last))
            elif number < ring_size - 1:
                current[k] = late_add(plan, at, pack, after(got[k], *last))
            elif turn:
                current[k], copies[k] = late_add(plan, at, pack, after(got[k], *last), True)
            else:
                current[k] = after(got[k], *last)
            last = [current[k]]
            if not turn:
                got[k] = send(current[k], k)
        if turn:
            placed = unpack(plan, experts + 2 * (ring_size - 1), 0, current, shapes, placed)
            others = [swap(across_rings(values), "col") for values in copies]
            for k in range(2):
                current[k] = late_join(
                    col_ref, after(copies[k], *last), others[1 - k], normed["gains"], waves[1][k]
                )
                got[k] = send(current[k], k)
                last = work_out(1)(after(order, current[k]), ()) if k == 0 else [current[k]]
        if number >= ring_size - 1:
            for k in range(2):
                late_out[k].append(current[k])
        placed = unpack(
            plan, experts + 2 * step, wave, [after(current[0], *last), current[1]], shapes, placed
        )
        last = placed[0:1]
        if number == 2:
            back_to_tokens(last)
        if number == ring_size + 1:
            block_rows(last)
    for k in range(2):
        late_out[k].append(after(got[k], *last))
        last = [late_out[k][-1]]
    placed = unpack(
        plan,
        experts + 2 * (ring_size - 1),
        1,
        [late_out[k][-1] for k in range(2)],
        shapes,
        placed,
    )
    gate_grad, up_grad, down_grad = placed
    shapes = [w.shape for w in (w_shared_gate, w_shared_up, w_shared_down)]
    shapes += [w.shape for w in (w_query, w_key, w_value, w_out)] + [gains.shape]
    finals = unpack_late(plan, chunks_first + late_total, late_out, shapes)
    shared_gate_grad, shared_up_grad, shared_down_grad = finals[0:3]
    query_grad, key_grad, value_grad, out_proj_grad, gain_grads = finals[3:8]


    return (
        normed["block_out"],
        normed["tokens_grad"],
        gain_grads[0],
        query_grad,
        key_grad,
        value_grad,
        out_proj_grad,
        gain_grads[1],
        gate_grad,
        up_grad,
        down_grad,
        shared_gate_grad,
        shared_up_grad,
        shared_down_grad,
    )


def solution(mesh):
    in_specs = (
        P(("dp", "row"), "col"),
        P("col"),
        P("col", "row"),
        P("col", "row"),
        P("col", "row"),
        P("row", "col"),
        P("col"),
        P(None, "col", "row"),
        P(None, "col", "row"),
        P(None, "row", "col"),
        P("col", "row"),
        P("col", "row"),
        P("row", "col"),
        P("dp", None),
        P("dp", None),
        P("dp"),
        P(("dp", "row"), "col"),
    )
    out_specs = (
        P(("dp", "row"), "col"),
        P(("dp", "row"), "col"),
        P("col"),
        P("col", "row"),
        P("col", "row"),
        P("col", "row"),
        P("row", "col"),
        P("col"),
        P(None, "col", "row"),
        P(None, "col", "row"),
        P(None, "row", "col"),
        P("col", "row"),
        P("col", "row"),
        P("row", "col"),
    )
    return jax.shard_map(body, mesh=mesh, in_specs=in_specs, out_specs=out_specs, check_vma=False)
```

```python
import functools

import jax
import jax.numpy as jnp
import numpy as np
from jax import lax
from jax.experimental import pallas as pl
from jax.experimental.pallas import tpu as pltpu
from jax.sharding import PartitionSpec as P

D = 1536
HQ = 12
HK = 4
DH = 128
GROUP_HEADS = HQ // HK
LANES = 128

EPSILON = 1e-05
F32 = jnp.float32
BF16 = jnp.bfloat16
MIB = 1024 * 1024
GAIN_ROWS = 16
RING = 8
LATE_BLOCKS = 5
SMALL = pl.CostEstimate(flops=0, bytes_accessed=0, transcendentals=0)


def params(mib, *semantics):
    return pltpu.CompilerParams(
        dimension_semantics=semantics or None, vmem_limit_bytes=mib * MIB
    )


def dot(left, right):
    return jnp.dot(left, right, preferred_element_type=F32)


def dot_nt(left, right):
    return lax.dot_general(left, right, (((1,), (1,)), ((), ())), preferred_element_type=F32)


def dot_tn(left, right):
    return lax.dot_general(left, right, (((0,), (0,)), ((), ())), preferred_element_type=F32)


def after(values, *others):
    return lax.optimization_barrier((values, *others))[0]


def swap(values, axis):
    return lax.ppermute(values, axis, [(0, 1), (1, 0)])


def halves(values, axis, mine):
    size = values.shape[axis] // 2
    low = lax.slice_in_dim(values, 0, size, axis=axis)
    high = lax.slice_in_dim(values, size, 2 * size, axis=axis)
    return jnp.where(mine == 0, low, high), jnp.where(mine == 0, high, low)


def in_order(own, other, mine, axis):
    return jnp.concatenate(
        [jnp.where(mine == 0, own, other), jnp.where(mine == 0, other, own)], axis=axis
    )


def gather_rows(place_ref, own_ref, other_ref, all_ref):
    row = place_ref[0]
    rows = own_ref.shape[0]
    all_ref[pl.ds(pl.multiple_of(row * rows, rows), rows), :] = own_ref[...]
    all_ref[pl.ds(pl.multiple_of((1 - row) * rows, rows), rows), :] = other_ref[...]


def head_rows(ref, first, block):
    return jnp.concatenate(
        [ref[first : first + block, h * DH : (h + 1) * DH] for h in range(GROUP_HEADS)], axis=0
    )


def key_probs(query, key, first, length):
    block, keys = query.shape[0] // GROUP_HEADS, key.shape[0]
    scores = dot_nt(query, key) * DH ** (-0.5)
    shape = (block, keys)
    query_at = lax.broadcasted_iota(jnp.int32, shape, 0) + first
    key_at = lax.broadcasted_iota(jnp.int32, shape, 1)
    allowed = (key_at <= query_at) & (key_at < length)
    allowed = jnp.concatenate([allowed] * GROUP_HEADS, axis=0)
    scores = jnp.where(allowed, scores, -1e30)
    weights = jnp.exp(scores - jnp.max(scores, axis=1, keepdims=True))
    return weights * (1.0 / jnp.sum(weights, axis=1, keepdims=True))


def attend_kernel(place_ref, own_ref, other_ref, out_ref, all_ref):
    gather_rows(place_ref, own_ref, other_ref, all_ref)
    rows = own_ref.shape[0]
    block = 256
    width = GROUP_HEADS * DH
    for at in range(2 * rows // block):
        first, keys = at * block, (at + 1) * block
        query = head_rows(all_ref, first, block)
        key = all_ref[0:keys, width : width + DH]
        value = all_ref[0:keys, width + DH : width + 2 * DH]
        probs = key_probs(query, key, first, place_ref[1])
        result = dot(probs.astype(BF16), value).astype(BF16)
        for h in range(GROUP_HEADS):
            out_ref[first : first + block, h * DH : (h + 1) * DH] = result[
                h * block : (h + 1) * block
            ]


def attend(place, own, other):
    rows, width = own.shape
    spec = pl.BlockSpec(memory_space=pltpu.VMEM)
    return pl.pallas_call(
        attend_kernel,
        out_shape=jax.ShapeDtypeStruct((2 * rows, GROUP_HEADS * DH), BF16),
        in_specs=[pl.BlockSpec(memory_space=pltpu.SMEM), spec, spec],
        out_specs=spec,
        scratch_shapes=[pltpu.VMEM((2 * rows, width), BF16)],
        compiler_params=params(32),
        cost_estimate=SMALL,
        name="attend",
    )(place, own, other)


def attend_back_kernel(
    place_ref, own_ref, other_ref, *refs
):
    grad_refs, grad_c_refs = refs[0:2], refs[2:4]
    out_ref, out_c_ref, result_ref, all_ref, total_ref = refs[4:9]
    gather_rows(place_ref, own_ref, other_ref, all_ref)
    rows = own_ref.shape[0]
    block = 256
    width = GROUP_HEADS * DH
    group = pl.ds(pl.multiple_of(place_ref[2] * width, width), width)
    blocks = 2 * rows // block
    for at in reversed(range(blocks)):
        first, keys = at * block, (at + 1) * block
        query = head_rows(all_ref, first, block)
        key = all_ref[0:keys, width : width + DH]
        value = all_ref[0:keys, width + DH : width + 2 * DH]
        probs = key_probs(query, key, first, place_ref[1])
        half, in_half = divmod(first, rows)
        piece = slice(in_half, in_half + block)
        grad = dot_nt(grad_refs[half][piece, :], out_ref[group, :])
        grad = (grad + dot_nt(grad_c_refs[half][piece, :], out_c_ref[group, :])).astype(BF16)
        grad = jnp.concatenate(
            [grad[:, h * DH : (h + 1) * DH] for h in range(GROUP_HEADS)], axis=0
        )
        probs_grad = dot_nt(grad, value)
        carried = jnp.sum(probs * probs_grad, axis=1, keepdims=True)
        score_grad = (probs * (probs_grad - carried)).astype(BF16)
        query_back = (dot(score_grad, key) * DH ** (-0.5)).astype(BF16)
        for h in range(GROUP_HEADS):
            result_ref[first:keys, h * DH : (h + 1) * DH] = query_back[
                h * block : (h + 1) * block
            ]
        key_back = dot_tn(score_grad, query)
        value_back = dot_tn(probs.astype(BF16), grad)
        if at == blocks - 1:
            total_ref[:, 0:DH] = key_back
            total_ref[:, DH:] = value_back
        else:
            total_ref[0:keys, 0:DH] += key_back
            total_ref[0:keys, DH:] += value_back
    result_ref[:, width : width + DH] = (total_ref[:, 0:DH] * DH ** (-0.5)).astype(BF16)
    result_ref[:, width + DH :] = total_ref[:, DH:].astype(BF16)


def attend_back(place, own, other, grad, grad_c, w_out, out_c):
    rows, width = own.shape
    spec = pl.BlockSpec(memory_space=pltpu.VMEM)
    return pl.pallas_call(
        attend_back_kernel,
        out_shape=jax.ShapeDtypeStruct((2 * rows, width), BF16),
        in_specs=[pl.BlockSpec(memory_space=pltpu.SMEM)] + [spec] * 8,
        out_specs=spec,
        scratch_shapes=[
            pltpu.VMEM((2 * rows, width), BF16),
            pltpu.VMEM((2 * rows, 2 * DH), F32),
        ],
        compiler_params=params(60),
        cost_estimate=SMALL,
        name="attend_back",
    )(place, own, other, *grad, *grad_c, w_out, out_c)


def unit_slices(unit, share):
    row, lane = divmod(unit, 3)
    return slice(row * share, (row + 1) * share), slice(lane * LANES, (lane + 1) * LANES)


def late_kernel(place_ref, *refs):
    near, near_c, far, far_c, qkv_ref, attended_ref = refs[0:6]
    grad_refs, grad_c_refs, shared, outs = refs[6:8], refs[8:10], refs[10:12], refs[12:14]
    rows, features = near.shape
    own_rows = pl.ds(pl.multiple_of(place_ref[0] * rows, rows), rows)
    far_rows = pl.ds(pl.multiple_of((1 - place_ref[0]) * rows, rows), rows)
    split = 7 * LANES

    chunks = outs[0].shape[0]
    share = features // chunks

    def store(h, at, values):
        values = values.astype(BF16)
        for b in range(values.shape[1] // LANES):
            part, unit = divmod(at // LANES + b, split // LANES)
            to_rows, to_lanes = unit_slices(h * (split // LANES) + unit, share)

            def write(out_ref, b=b, to_rows=to_rows, to_lanes=to_lanes):
                for chunk in range(chunks):
                    out_ref[chunk, to_rows, to_lanes] = values[
                        chunk * share : (chunk + 1) * share, b * LANES : (b + 1) * LANES
                    ]

            pl.when(place_ref[2] == 0)(lambda part=part, write=write: write(outs[part]))
            pl.when(place_ref[2] != 0)(lambda part=part, write=write: write(outs[1 - part]))

    for out_ref in outs:
        to_rows, to_lanes = unit_slices(2 * (split // LANES), share)
        for chunk in range(chunks):
            out_ref[chunk, to_rows, to_lanes] = jnp.zeros((share, LANES), BF16)

    for h, (x, y, grad) in enumerate(((near, far, grad_refs), (near_c, far_c, grad_c_refs))):
        for k in range(2):
            store(h, 3 * LANES * k, shared[k][0, h * features : (h + 1) * features, :])
        project = dot_tn(x[...], qkv_ref[own_rows, :]) + dot_tn(y[...], qkv_ref[far_rows, :])
        store(h, 6 * LANES, project)
        out = [dot_tn(grad[k][...], attended_ref[k * rows : (k + 1) * rows, :]) for k in range(2)]
        store(h, 11 * LANES, out[0] + out[1])


def late_grads(place, near, far, qkv_grad, attended, grad, grad_c, shared):
    features = near[0].shape[1]
    rows = LATE_BLOCKS * (features // RING)
    spec = pl.BlockSpec(memory_space=pltpu.VMEM)
    return pl.pallas_call(
        late_kernel,
        out_shape=[jax.ShapeDtypeStruct((RING, rows, 3 * LANES), BF16)] * 2,
        in_specs=[pl.BlockSpec(memory_space=pltpu.SMEM)] + [spec] * 12,
        out_specs=[spec] * 2,
        compiler_params=params(60),
        cost_estimate=SMALL,
        name="late_grads",
    )(place, *near, *far, qkv_grad, attended, *grad, *grad_c, *shared)


def columns_kernel(
    place_ref, query_ref, key_ref, value_ref, w_out_ref, out_ref, share_ref
):
    share_ref[...] = w_out_ref[...]
    width = GROUP_HEADS * DH
    out_ref[:, 0:width] = query_ref[...]
    out_ref[:, width : width + DH] = key_ref[...]
    out_ref[:, width + DH :] = value_ref[...]


def their_columns(place, w_query, w_key, w_value, w_out, shares):
    rows = w_query.shape[0]
    width = GROUP_HEADS * DH + 2 * DH

    def theirs(width):
        return pl.BlockSpec((rows, width), lambda i, c: (0, 1 - c[0]))

    return pl.pallas_call(
        columns_kernel,
        grid_spec=pltpu.PrefetchScalarGridSpec(
            num_scalar_prefetch=1,
            grid=(1,),
            in_specs=[theirs(GROUP_HEADS * DH), theirs(DH), theirs(DH)]
            + [pl.BlockSpec((rows // shares, rows), lambda i, c: (c[1], 0))],
            out_specs=[
                pl.BlockSpec((rows, width), lambda i, c: (0, 0)),
                pl.BlockSpec((rows // shares, rows), lambda i, c: (0, 0)),
            ],
        ),
        out_shape=[
            jax.ShapeDtypeStruct((rows, width), BF16),
            jax.ShapeDtypeStruct((rows // shares, rows), BF16),
        ],
        compiler_params=params(60, "arbitrary"),
        cost_estimate=SMALL,
        name="their_columns",
    )(place, w_query, w_key, w_value, w_out)


def join_kernel(mine_ref, *refs):
    *parts, out_ref = refs
    rows = parts[0].shape[0]
    for k, part in enumerate(parts):
        at = jnp.bitwise_xor(mine_ref[0], k)
        out_ref[pl.ds(pl.multiple_of(at * rows, rows), rows), :] = part[...]


def join(mine, *parts):
    rows, width = parts[0].shape
    spec = pl.BlockSpec(memory_space=pltpu.VMEM)
    return pl.pallas_call(
        join_kernel,
        out_shape=jax.ShapeDtypeStruct((len(parts) * rows, width), parts[0].dtype),
        in_specs=[pl.BlockSpec(memory_space=pltpu.SMEM)] + [spec] * len(parts),
        out_specs=spec,
        compiler_params=params(16),
        cost_estimate=SMALL,
        name="join",
    )(mine.reshape(1), *parts)


def project_kernel(col_ref, own_ref, other_ref, gains_ref, gains_c_ref, query_ref, key_ref, value_ref, there_ref, x_own_ref, x_other_ref, qkv_ref, scale_ref):
    own = own_ref[...].astype(F32)
    other = other_ref[...].astype(F32)
    total = jnp.sum(own * own, axis=1, keepdims=True)
    total = total + jnp.sum(other * other, axis=1, keepdims=True)
    scale = lax.rsqrt(total / D + EPSILON)
    own = (own * scale * gains_ref[0:1, :]).astype(BF16)
    other = (other * scale * gains_c_ref[0:1, :]).astype(BF16)
    x_own_ref[...] = own
    x_other_ref[...] = other
    scale_ref[...] = scale
    here = jnp.concatenate([query_ref[...], key_ref[...], value_ref[...]], axis=1)
    qkv_ref[...] = (dot(own, here) + dot(other, there_ref[...])).astype(BF16)


def project(col, own, other, gains, gains_c, w_query, w_key, w_value, there):
    rows, features = own.shape
    width = there.shape[1]
    group = GROUP_HEADS * DH
    tile = rows // 2

    def whole(*shape):
        return pl.BlockSpec(shape, lambda i, c: (0,) * len(shape))

    def mine(width):
        return pl.BlockSpec((features, width), lambda i, c: (0, c[0]))

    def rowwise(width):
        return pl.BlockSpec((tile, width), lambda i, c: (i, 0))

    return pl.pallas_call(
        project_kernel,
        grid_spec=pltpu.PrefetchScalarGridSpec(
            num_scalar_prefetch=1,
            grid=(rows // tile,),
            in_specs=[
                rowwise(features),
                rowwise(features),
                whole(2, features),
                whole(2, features),
                mine(group),
                mine(DH),
                mine(DH),
                whole(features, width),
            ],
            out_specs=[rowwise(features), rowwise(features), rowwise(width), rowwise(1)],
        ),
        out_shape=[
            jax.ShapeDtypeStruct((rows, features), BF16),
            jax.ShapeDtypeStruct((rows, features), BF16),
            jax.ShapeDtypeStruct((rows, width), BF16),
            jax.ShapeDtypeStruct((rows, 1), F32),
        ],
        compiler_params=params(60, "arbitrary"),
        cost_estimate=SMALL,
        name="project",
    )(col, own, other, gains, gains_c, w_query, w_key, w_value, there)


def head_pair(col_ref, own, other):
    first, second = own[...], other[...]
    flipped = col_ref != 0
    return jnp.concatenate(
        [jnp.where(flipped, second, first), jnp.where(flipped, first, second)], axis=1
    )


def before_kernel(tiles, place_ref, *refs):
    near, near_c, far, far_c, attended, attended_c, here, there, own_ref, other_ref = refs
    is_near = (pl.program_id(0) >= tiles // 2).astype(jnp.int32) == place_ref[0]
    heads = head_pair(place_ref[2], attended, attended_c)
    own = jnp.where(is_near, near[...], far[...]).astype(F32)
    other = jnp.where(is_near, near_c[...], far_c[...]).astype(F32)
    own_ref[...] = own + dot(heads, here[...])
    other_ref[...] = other + dot(heads, there[...])


def after_kernel(place_ref, *refs):
    own_ref, other_ref, attended, attended_c, here, there, gains_ref, gains_c_ref = refs[0:8]
    hidden_ref, x_own_ref, x_other_ref, scale_ref = refs[8:12]
    heads = head_pair(place_ref[2], attended, attended_c)
    own = own_ref[...] + dot(heads, here[...])
    other = other_ref[...] + dot(heads, there[...])
    total = jnp.sum(own * own, axis=1, keepdims=True)
    total = total + jnp.sum(other * other, axis=1, keepdims=True)
    scale = lax.rsqrt(total / D + EPSILON)
    hidden_ref[...] = own
    scale_ref[...] = scale
    x_own_ref[...] = (own * scale * gains_ref[1:2, :]).astype(BF16)
    x_other_ref[...] = (other * scale * gains_c_ref[1:2, :]).astype(BF16)


TOKEN_TILE = 256


def rowwise(width):
    return pl.BlockSpec((TOKEN_TILE, width), lambda i, p: (i, 0))


def whole(*shape):
    return pl.BlockSpec(shape, lambda i, p: (0,) * len(shape))


def hidden_before(place, tokens, attended, here, there):
    half, features = tokens[0].shape
    rows, heads = attended[0].shape
    tiles = rows // TOKEN_TILE
    per_half = half // TOKEN_TILE
    halfwise = pl.BlockSpec((TOKEN_TILE, features), lambda i, p: (i % per_half, 0))
    return pl.pallas_call(
        functools.partial(before_kernel, tiles),
        grid_spec=pltpu.PrefetchScalarGridSpec(
            num_scalar_prefetch=1,
            grid=(tiles,),
            in_specs=[halfwise] * 4 + [rowwise(heads)] * 2 + [whole(2 * heads, features)] * 2,
            out_specs=[rowwise(features)] * 2,
        ),
        out_shape=[jax.ShapeDtypeStruct((rows, features), F32)] * 2,
        compiler_params=params(56, "arbitrary"),
        cost_estimate=pl.CostEstimate(
            flops=8 * rows * features * heads,
            bytes_accessed=16 * rows * features,
            transcendentals=0,
        ),
        name="hidden_before",
    )(place, *tokens, *attended, here, there)


def hidden_after(place, before, attended, here, there, gains, gains_c):
    rows, features = before[0].shape
    heads = attended[0].shape[1]
    return pl.pallas_call(
        after_kernel,
        grid_spec=pltpu.PrefetchScalarGridSpec(
            num_scalar_prefetch=1,
            grid=(rows // TOKEN_TILE,),
            in_specs=[rowwise(features)] * 2
            + [rowwise(heads)] * 2
            + [whole(2 * heads, features)] * 2
            + [whole(2, features)] * 2,
            out_specs=[rowwise(features)] * 3 + [rowwise(1)],
        ),
        out_shape=[
            jax.ShapeDtypeStruct((rows, features), F32),
            jax.ShapeDtypeStruct((rows, features), BF16),
            jax.ShapeDtypeStruct((rows, features), BF16),
            jax.ShapeDtypeStruct((rows, 1), F32),
        ],
        compiler_params=params(56, "arbitrary"),
        cost_estimate=SMALL,
        name="hidden_after",
    )(place, *before, *attended, here, there, gains, gains_c)


def expert_kernel(shared, aliased, first, order_ref, *refs):
    x_own, x_other, o_own, o_other, gates_ref = refs[0:5]
    weights = refs[5:17]
    grads = refs[17 + aliased : 19 + aliased]
    pair_ref, inner_ref = refs[19 + aliased : 21 + aliased]
    step = pl.program_id(0) + first
    rows, features = x_own.shape
    tile = 512
    up_own = jnp.concatenate([weights[k][0] for k in (0, 1, 6, 7)], axis=1)
    up_other = jnp.concatenate([weights[k][0] for k in (2, 3, 8, 9)], axis=1)
    down_own = jnp.concatenate([weights[k][0] for k in (4, 10)], axis=0)
    down_other = jnp.concatenate([weights[k][0] for k in (5, 11)], axis=0)

    def token_tile(t, carry):
        at = pl.ds(pl.multiple_of(t * tile, tile), tile)
        pre = dot(x_own[at, :], up_own) + dot(x_other[at, :], up_other)
        back = dot_nt(o_own[at, :], down_own) + dot_nt(o_other[at, :], down_other)
        for k in range(2):
            pre_gate = pre[:, 2 * k * LANES : (2 * k + 1) * LANES]
            pre_up = pre[:, (2 * k + 1) * LANES : (2 * k + 2) * LANES]
            inner_grad = back[:, k * LANES : (k + 1) * LANES]
            sigmoid = 1.0 / (1.0 + jnp.exp(-pre_gate))
            silu = pre_gate * sigmoid
            inner = silu * pre_up
            if not shared:
                shape = (gates_ref.shape[0], LANES)
                expert = lax.broadcasted_iota(jnp.int32, shape, 0) % (gates_ref.shape[0] // 3)
                chosen = (expert == order_ref[2 * step + k]).astype(F32).astype(BF16)
                gate = dot_tn(gates_ref[:, at], chosen)
                inner = gate * inner
                inner_grad = gate * inner_grad
            gate_grad = inner_grad * pre_up * (sigmoid * (1.0 + pre_gate * (1.0 - sigmoid)))
            inner_ref[0, at, k * LANES : (k + 1) * LANES] = inner.astype(BF16)
            pair_ref[0, at, 2 * k * LANES : (2 * k + 1) * LANES] = gate_grad.astype(BF16)
            pair_ref[0, at, (2 * k + 1) * LANES : (2 * k + 2) * LANES] = (
                inner_grad * silu
            ).astype(BF16)
        return carry

    lax.fori_loop(0, rows // tile, token_tile, 0)
    pairs = pair_ref[0]
    for h, x in enumerate((x_own, x_other)):
        wide = dot_tn(x[...], pairs).astype(BF16)
        for k in range(2):
            grads[k][0, h * features : (h + 1) * features, 0 : 2 * LANES] = wide[
                :, 2 * k * LANES : (2 * k + 2) * LANES
            ]
    inner = inner_ref[0]
    tile = 256
    for h, o in enumerate((o_own, o_other)):
        for j in range(features // tile):
            low = dot_tn(inner, o[:, j * tile : (j + 1) * tile]).astype(BF16)
            for k in range(2):
                for b in range(tile // LANES):
                    at = h * features + j * tile + b * LANES
                    grads[k][0, at : at + LANES, 2 * LANES :] = low[
                        k * LANES : (k + 1) * LANES, b * LANES : (b + 1) * LANES
                    ]


def expert_specs(features, place, wide, low):
    specs = []
    if wide:
        block = pl.BlockSpec((1, features, LANES), lambda i, o: (place(i, o)[0], 0, place(i, o)[1]))
        specs += [block] * 4
    if low:
        block = pl.BlockSpec((1, LANES, features), lambda i, o: (*place(i, o), 0))
        specs += [block] * 2
    return specs


def expert_grads(order, first, last, total, x, o, gates, weights, kept):
    shared = total is None
    steps = last - first
    rows, features = x[0].shape
    aliased = len(kept)

    def fixed(*shape):
        return pl.BlockSpec(shape, lambda i, o: (0,) * len(shape))

    def stepped(*shape):
        return pl.BlockSpec((1, *shape), lambda i, o: (i, 0, 0))

    def placed(*shape):
        return pl.BlockSpec((1, *shape), lambda i, o: (i + first, 0, 0))

    specs = []
    for k in range(2):
        if shared:

            def picked(i, o, k=k):
                return 0, 2 * o[o.shape[0] - 1] + k

        else:

            def picked(i, o, k=k):
                return o[2 * (i + first) + k], o[o.shape[0] - 1]

        specs += expert_specs(features, picked, True, True)
    total = steps if shared else total
    return pl.pallas_call(
        functools.partial(expert_kernel, shared, aliased, first),
        grid_spec=pltpu.PrefetchScalarGridSpec(
            num_scalar_prefetch=1,
            grid=(steps,),
            in_specs=[fixed(rows, features)] * 4
            + [fixed(*gates.shape)]
            + specs
            + [pl.BlockSpec(memory_space=pl.ANY)] * aliased,
            out_specs=[stepped(2 * features, 3 * LANES)] * 2
            + [placed(rows, 4 * LANES), placed(rows, 2 * LANES)],
        ),
        out_shape=[jax.ShapeDtypeStruct((steps, 2 * features, 3 * LANES), BF16)] * 2
        + [
            jax.ShapeDtypeStruct((total, rows, 4 * LANES), BF16),
            jax.ShapeDtypeStruct((total, rows, 2 * LANES), BF16),
        ],
        input_output_aliases={18 + k: 2 + k for k in range(aliased)},
        compiler_params=params(40, "arbitrary"),
        cost_estimate=SMALL,
        name="expert_grads",
    )(order, *x, *o, gates, *weights, *weights, *kept)


def mix_kernel(back, group, pieces, order_ref, *refs):
    acts_ref, shared_ref = refs[0:2]
    each = 2 if back else 1
    count = 2 * group * each
    weights = refs[2 : 2 + count]
    shared = refs[2 + count : 2 + count + 2 * each]
    *outs, total_ref = refs[2 + count + 2 * each :]
    step = pl.program_id(0)
    rows = total_ref.shape[0]
    tile = 512
    times = dot_nt if back else dot
    along = 1 if back else 0

    @pl.when(step == 0)
    def _():
        both = jnp.concatenate([w[0] for w in shared], axis=along)
        for t in range(rows // tile):
            at = slice(t * tile, (t + 1) * tile)
            total_ref[at, :] = times(shared_ref[0, at, :], both)

    both = jnp.concatenate([w[0] for w in weights], axis=along)
    for t in range(rows // tile):
        at = slice(t * tile, (t + 1) * tile)
        acts = jnp.concatenate([acts_ref[g, at, :] for g in range(group)], axis=1)
        total_ref[at, :] += times(acts, both)

    @pl.when(step == pl.num_programs(0) - 1)
    def _():
        part = rows // pieces
        for k, out_ref in enumerate(outs):
            out_ref[...] = total_ref[k * part : (k + 1) * part, :].astype(out_ref.dtype)


def mix(back, dtype, pieces, order, acts, shared_acts, weights, shared_weights):
    pairs, rows, width = acts.shape
    features = weights[0].shape[1] if back else weights[0].shape[2]
    group = 4 if pairs % 4 == 0 else 1

    def spec(place):
        if back:
            return pl.BlockSpec((1, features, LANES), lambda i, o: (place(i, o)[0], 0, place(i, o)[1]))
        return pl.BlockSpec((1, LANES, features), lambda i, o: (*place(i, o), 0))

    def routed(k):
        return spec(lambda i, o: (o[2 * group * i + k], o[o.shape[0] - 1]))

    def common(k):
        return spec(lambda i, o: (0, 2 * o[o.shape[0] - 1] + k))

    outs = pl.pallas_call(
        functools.partial(mix_kernel, back, group, pieces),
        grid_spec=pltpu.PrefetchScalarGridSpec(
            num_scalar_prefetch=1,
            grid=(pairs // group,),
            in_specs=[
                pl.BlockSpec((group, rows, width), lambda i, o: (i, 0, 0)),
                pl.BlockSpec((1, rows, width), lambda i, o: (0, 0, 0)),
            ]
            + [routed(k) for k in range(2 * group) for _ in weights]
            + [common(k) for k in range(2) for _ in weights],
            out_specs=[pl.BlockSpec((rows // pieces, features), lambda i, o: (0, 0))] * pieces,
            scratch_shapes=[pltpu.VMEM((rows, features), F32)],
        ),
        out_shape=[jax.ShapeDtypeStruct((rows // pieces, features), dtype)] * pieces,
        compiler_params=params(48, "arbitrary"),
        cost_estimate=SMALL,
        name="mix",
    )(order, acts, shared_acts, *weights * (2 * group), *shared_weights * 2)
    return outs if pieces > 1 else outs[0]


def chip_sum_kernel(tiles, own_ref, first_ref, second_ref, hidden_ref, gains_ref, total_ref, rounded_ref, product_ref):
    is_first = pl.program_id(0) < tiles // 2
    other = jnp.where(is_first, first_ref[...], second_ref[...])
    total = own_ref[...] + other.astype(F32)
    total_ref[...] = total
    rounded_ref[...] = total.astype(BF16)
    product_ref[...] = lax.dot_general(
        jnp.ones((8, total.shape[1]), F32),
        total * gains_ref[1:2, :] * hidden_ref[...],
        (((1,), (1,)), ((), ())),
        precision=lax.Precision.HIGHEST,
        preferred_element_type=F32,
    )


def chip_sum(own, other, hidden, gains):
    rows, features = own.shape
    spec = pl.BlockSpec((TOKEN_TILE, features), lambda i: (i, 0))
    tiles = rows // TOKEN_TILE
    piece = pl.BlockSpec((TOKEN_TILE, features), lambda i: (i % (tiles // 2), 0))
    return pl.pallas_call(
        functools.partial(chip_sum_kernel, tiles),
        grid=(tiles,),
        out_shape=[
            jax.ShapeDtypeStruct((rows, features), F32),
            jax.ShapeDtypeStruct((rows, features), BF16),
            jax.ShapeDtypeStruct((8, rows), F32),
        ],
        in_specs=[spec, piece, piece, spec, pl.BlockSpec(gains.shape, lambda i: (0, 0))],
        out_specs=[spec, spec, pl.BlockSpec((8, TOKEN_TILE), lambda i: (0, i))],
        compiler_params=params(24, "arbitrary"),
        cost_estimate=SMALL,
        name="chip_sum",
    )(own, *other, hidden, gains)


def norm_back_kernel(tiles, place_ref, *refs):
    sum_ref, came_ref, hidden_ref, scale_ref, out_grad_ref, gains_ref = refs[0:6]
    products = refs[6:10]
    hidden_grad_ref, first_ref, second_ref, gain_ref = refs[10:14]
    step = pl.program_id(0)
    part = (step >= tiles // 2).astype(jnp.int32)
    grad = sum_ref[...] + came_ref[...].astype(F32)
    hidden = hidden_ref[...]
    scale = scale_ref[...]
    total = (products[0][...] + products[1][...]) + (products[2][...] + products[3][...])
    mean = lax.dot_general(
        total,
        jnp.full((8, LANES), 1.0 / (8 * D), F32),
        (((0,), (0,)), ((), ())),
        precision=lax.Precision.HIGHEST,
        preferred_element_type=F32,
    )[:, 0:1]
    result = out_grad_ref[...].astype(F32) + scale * (grad * gains_ref[1:2, :])
    result = result - hidden * (scale * scale * scale * mean)
    hidden_grad_ref[...] = result
    for k, rounded_ref in enumerate((first_ref, second_ref)):

        @pl.when(part == k)
        def _(rounded_ref=rounded_ref):
            rounded_ref[...] = result.astype(BF16)

    @pl.when(step == 0)
    def _():
        gain_ref[...] = jnp.zeros_like(gain_ref)

    @pl.when(part == place_ref[0])
    def _():
        gain_ref[...] += jnp.sum(grad * hidden * scale, axis=0, keepdims=True)


def norm_back(place, sums, came, hidden, scale, out_grad, gains, products):
    rows, features = hidden.shape
    tiles = rows // TOKEN_TILE
    lanes = pl.BlockSpec((8, TOKEN_TILE), lambda i, p: (0, i))

    def piece(k):
        last = tiles // 2 - 1
        return pl.BlockSpec(
            (TOKEN_TILE, features), lambda i, p: (jnp.clip(i - k * tiles // 2, 0, last), 0)
        )

    return pl.pallas_call(
        functools.partial(norm_back_kernel, tiles),
        grid_spec=pltpu.PrefetchScalarGridSpec(
            num_scalar_prefetch=1,
            grid=(tiles,),
            in_specs=[rowwise(features)] * 3
            + [rowwise(1), rowwise(features), whole(2, features)]
            + [lanes] * 4,
            out_specs=[rowwise(features), piece(0), piece(1), whole(1, features)],
        ),
        out_shape=[
            jax.ShapeDtypeStruct((rows, features), F32),
            jax.ShapeDtypeStruct((rows // 2, features), BF16),
            jax.ShapeDtypeStruct((rows // 2, features), BF16),
            jax.ShapeDtypeStruct((1, features), F32),
        ],
        compiler_params=params(48, "arbitrary"),
        cost_estimate=SMALL,
        name="norm_back",
    )(place, sums, came, hidden, scale, out_grad, gains, *products)


def ring_of(size):
    return list(range(0, size, 2)) + list(range(1, size, 2))[::-1]


def unpack_kernel(aliased, plan_ref, *refs):
    chunks = refs[0:2]
    gate_ref, up_ref, down_ref = refs[2 + aliased : 5 + aliased]
    rows = gate_ref.shape[1]

    def write(chunk_ref):
        first = chunk_ref.shape[0] - rows
        gate_ref[0] = chunk_ref[first:, 0:LANES].astype(F32)
        up_ref[0] = chunk_ref[first:, LANES : 2 * LANES].astype(F32)
        for b in range(rows // LANES):
            at = slice(first + b * LANES, first + (b + 1) * LANES)
            down_ref[0, :, b * LANES : (b + 1) * LANES] = chunk_ref[at, 2 * LANES :].astype(F32)

    for k in range(2):
        pl.when(pl.program_id(0) == k)(lambda k=k: write(chunks[k]))


def unpack(plan, first, wave, chunks, shapes, outs):
    rows = shapes[0][1]

    def place(d, n):
        block = n[n.shape[0] - 1]
        return n[first + d], 1 - block if wave else block

    def wide(d, n):
        expert, block = place(d, n)
        return (expert, 0, block)

    def low(d, n):
        expert, block = place(d, n)
        return (expert, block, 0)

    aliased = len(outs)
    return pl.pallas_call(
        functools.partial(unpack_kernel, aliased),
        grid_spec=pltpu.PrefetchScalarGridSpec(
            num_scalar_prefetch=1,
            grid=(2,),
            in_specs=[pl.BlockSpec(chunk.shape, lambda d, n: (0, 0)) for chunk in chunks]
            + [pl.BlockSpec(memory_space=pl.ANY)] * aliased,
            out_specs=[
                pl.BlockSpec((1, rows, LANES), wide),
                pl.BlockSpec((1, rows, LANES), wide),
                pl.BlockSpec((1, LANES, rows), low),
            ],
        ),
        out_shape=[jax.ShapeDtypeStruct(shape, F32) for shape in shapes],
        input_output_aliases={3 + k: k for k in range(aliased)},
        compiler_params=params(16, "arbitrary"),
        cost_estimate=SMALL,
        name="unpack",
    )(plan, *chunks, *outs)


def ring_sum_kernel(came_ref, mine_ref, *outs):
    total = (came_ref[...].astype(F32) + mine_ref[...].astype(F32)).astype(BF16)
    if len(outs) == 1:
        outs[0][...] = total
    else:
        half = pl.program_id(1) // (pl.num_programs(1) // 2)
        for k, out_ref in enumerate(outs):

            @pl.when(half == k)
            def _(out_ref=out_ref):
                out_ref[...] = total


def ring_sum(came, mine, first, halved):
    count, rows, lanes = came.shape
    tiles = 4
    spec = pl.BlockSpec((1, rows // tiles, lanes), lambda i, j: (i, j, 0))
    term = pl.BlockSpec((1, rows // tiles, lanes), lambda i, j: (first + i, j, 0))

    def half(k):
        first = k * tiles // 2
        last = tiles // 2 - 1
        return pl.BlockSpec(
            (1, rows // tiles, lanes), lambda i, j: (i, jnp.clip(j - first, 0, last), 0)
        )

    shapes = [jax.ShapeDtypeStruct((count, rows // 2, lanes), BF16)] * 2
    return pl.pallas_call(
        ring_sum_kernel,
        grid=(count, tiles),
        in_specs=[spec, term],
        out_specs=[half(0), half(1)] if halved else spec,
        out_shape=shapes if halved else jax.ShapeDtypeStruct(came.shape, BF16),
        compiler_params=params(16, "arbitrary", "arbitrary"),
        cost_estimate=SMALL,
        name="ring_sum",
    )(came, mine)


def late_load_kernel(plan_ref, pack_ref, main_ref, out_ref):
    rows = pack_ref.shape[1]
    out_ref[0:rows, :] = pack_ref[0]
    out_ref[rows:, :] = main_ref[...]


def late_load(plan, at, pack, main):
    rows, lanes = pack.shape[1:]
    total = rows + main.shape[0]
    return pl.pallas_call(
        late_load_kernel,
        grid_spec=pltpu.PrefetchScalarGridSpec(
            num_scalar_prefetch=1,
            grid=(1,),
            in_specs=[
                pl.BlockSpec((1, rows, lanes), lambda i, n: (n[at], 0, 0)),
                pl.BlockSpec(main.shape, lambda i, n: (0, 0)),
            ],
            out_specs=pl.BlockSpec((total, lanes), lambda i, n: (0, 0)),
        ),
        out_shape=jax.ShapeDtypeStruct((total, lanes), BF16),
        compiler_params=params(16, "arbitrary"),
        cost_estimate=SMALL,
        name="late_load",
    )(plan, pack, main)


def late_add_kernel(plan_ref, pack_ref, came_ref, *outs):
    total = (came_ref[...].astype(F32) + pack_ref[0].astype(F32)).astype(BF16)
    for out_ref in outs:
        out_ref[...] = total


def late_add(plan, at, pack, came, copied=False):
    rows, lanes = pack.shape[1:]
    spec = pl.BlockSpec((rows, lanes), lambda i, n: (0, 0))
    shape = jax.ShapeDtypeStruct(came.shape, BF16)
    return pl.pallas_call(
        late_add_kernel,
        grid_spec=pltpu.PrefetchScalarGridSpec(
            num_scalar_prefetch=1,
            grid=(1,),
            in_specs=[pl.BlockSpec((1, rows, lanes), lambda i, n: (n[at], 0, 0)), spec],
            out_specs=[spec] * 2 if copied else spec,
        ),
        out_shape=[shape, jax.ShapeDtypeStruct((rows, lanes), BF16)] if copied else shape,
        input_output_aliases={2: 0},
        compiler_params=params(16, "arbitrary"),
        cost_estimate=SMALL,
        name="late_add",
    )(plan, pack, came)


def late_join_kernel(col_ref, mine_ref, other_ref, gains_ref, main_ref, out_ref):
    units = 7
    out_ref[mine_ref.shape[0] :, :] = main_ref[...]
    share = mine_ref.shape[0] // LATE_BLOCKS
    to_rows, to_lanes = unit_slices(2 * units, share)
    blocks = gains_ref.shape[1] // LANES
    gains = [
        gains_ref[g : g + 1, b * LANES : (b + 1) * LANES] for g in range(2) for b in range(blocks)
    ]
    gains = jnp.concatenate(gains + [jnp.zeros((share - len(gains), LANES), F32)], axis=0)
    own = [mine_ref[unit_slices(b, share)] for b in range(units)]
    other = [other_ref[unit_slices(units + b, share)] for b in range(units)]
    for b in range(units):
        first, second = own[b], other[b]
        flipped = col_ref[0] != 0
        out_ref[unit_slices(b, share)] = jnp.where(flipped, second, first)
        out_ref[unit_slices(units + b, share)] = jnp.where(flipped, first, second)
    out_ref[to_rows, to_lanes] = gains.astype(BF16)


def late_join(col, mine, other, gains, main):
    rows, lanes = mine.shape
    total = rows + main.shape[0]

    def all_of(*shape):
        return pl.BlockSpec(shape, lambda i, c: (0, 0))

    return pl.pallas_call(
        late_join_kernel,
        grid_spec=pltpu.PrefetchScalarGridSpec(
            num_scalar_prefetch=1,
            grid=(1,),
            in_specs=[all_of(rows, lanes)] * 2 + [all_of(*gains.shape), all_of(*main.shape)],
            out_specs=all_of(total, lanes),
        ),
        out_shape=jax.ShapeDtypeStruct((total, lanes), BF16),
        compiler_params=params(16, "arbitrary"),
        cost_estimate=SMALL,
        name="late_join",
    )(col, mine, other, gains, main)


def unpack_late_kernel(first_step, steps, plan_ref, *refs):
    chunks = refs[0 : 2 * steps]
    sgate, sup, sdown, query, key, value, out, gains, all_ref, gain_ref = refs[2 * steps :]
    share, features = chunks[0].shape[0] // LATE_BLOCKS, all_ref.shape[2]
    for k in range(2):
        for step in range(steps):
            at = plan_ref[first_step + 2 * step + k]
            chunk = chunks[steps * k + step]
            to_rows = pl.ds(pl.multiple_of(at * share, share), share)
            for unit in range(14):
                lanes = slice(unit % 7 * LANES, (unit % 7 + 1) * LANES)
                all_ref[k, unit // 7, to_rows, lanes] = chunk[unit_slices(unit, share)]
            if k == 0:
                to_rows = pl.ds(pl.multiple_of(at * GAIN_ROWS, GAIN_ROWS), GAIN_ROWS)
                rows, lanes = unit_slices(14, share)
                gain_ref[to_rows, :] = chunk[rows.start : rows.start + GAIN_ROWS, lanes]
    total = jnp.zeros((GAIN_ROWS, LANES), F32)
    for step in range(steps):
        total = total + gain_ref[step * GAIN_ROWS : (step + 1) * GAIN_ROWS, :].astype(F32)
    blocks = features // LANES
    for row in range(2 * blocks):
        gains[row // blocks : row // blocks + 1, row % blocks * LANES : (row % blocks + 1) * LANES] = (
            total[row : row + 1, :]
        )
    flipped = plan_ref[plan_ref.shape[0] - 1] != 0
    for c in range(2):
        for b in range(14):
            lanes = slice(b % 7 * LANES, (b % 7 + 1) * LANES)
            first, second = all_ref[0, c, :, lanes], all_ref[1, c, :, lanes]
            if b >= 7:
                first, second = second, first
            block = jnp.where(flipped, second, first).astype(F32)
            if b < 6:
                at = slice((2 * c + b // 3) * LANES, (2 * c + b // 3 + 1) * LANES)
                if b % 3 < 2:
                    (sgate, sup)[b % 3][:, at] = block
                else:
                    for k in range(features // LANES):
                        here = slice(k * LANES, (k + 1) * LANES)
                        sdown[at, here] = block[here, :]
            elif b < 9:
                at = (GROUP_HEADS * c + b - 6) * LANES
                query[:, at : at + LANES] = block
            elif b < 11:
                (key, value)[b - 9][:, c * LANES : (c + 1) * LANES] = block
            else:
                at = (GROUP_HEADS * c + b - 11) * LANES
                out[at : at + LANES, :] = block.T


def unpack_late(plan, first_step, chunks, shapes):
    steps = len(chunks[0])
    features = shapes[0][0]
    share = features // steps
    chunk = pl.BlockSpec((LATE_BLOCKS * share, 3 * LANES), lambda i, n: (0, 0))
    return pl.pallas_call(
        functools.partial(unpack_late_kernel, first_step, steps),
        grid_spec=pltpu.PrefetchScalarGridSpec(
            num_scalar_prefetch=1,
            grid=(1,),
            in_specs=[chunk] * (2 * steps),
            out_specs=[pl.BlockSpec(shape, lambda i, n: (0, 0)) for shape in shapes],
            scratch_shapes=[
                pltpu.VMEM((2, 2, features, 7 * LANES), BF16),
                pltpu.VMEM((steps * GAIN_ROWS, LANES), BF16),
            ],
        ),
        out_shape=[jax.ShapeDtypeStruct(shape, F32) for shape in shapes],
        compiler_params=params(48, "arbitrary"),
        cost_estimate=SMALL,
        name="unpack_late",
    )(plan, *chunks[0], *chunks[1])


def plans(ring, each):
    size = len(ring)
    rows = []
    for member in range(size):
        place = ring.index(member)
        for col in range(2):
            chunks = []
            for step in range(2 * size - 1):
                for which in range(2):
                    sign = 1 if which == col else -1
                    chunks.append((place - sign * step) % size)
            experts = []
            for start in (0, size - 1):
                for step in range(start, start + size):
                    for k in range(each):
                        for which in range(2):
                            second = col if which == 0 else 1 - col
                            experts.append(2 * each * chunks[2 * step + which] + each * second + k)
            rows.append(experts + chunks + [col])
    return np.asarray(rows, np.int32)


def body(
    tokens_in,
    norm_gain_attn,
    w_query,
    w_key,
    w_value,
    w_out,
    norm_gain_ffn,
    w_gate,
    w_up,
    w_down,
    w_shared_gate,
    w_shared_up,
    w_shared_down,
    routes,
    gate_weights,
    seq_lengths,
    out_grad,
):
    row = lax.axis_index("row")
    col = lax.axis_index("col")
    dp = lax.axis_index("dp")
    dp_size = lax.axis_size("dp")
    local_rows, local_features = tokens_in.shape
    experts = w_gate.shape[0]
    group_width = GROUP_HEADS * DH
    col_ref = col.reshape(1)

    ring_size = RING
    ring = ring_of(ring_size)
    starts = range(0, dp_size, ring_size)
    rights = [
        (g + ring[k], g + ring[(k + 1) % ring_size]) for g in starts for k in range(ring_size)
    ]
    lefts = [(b, a) for a, b in rights]
    routes_of = [
        [(2 * a, 2 * b) for a, b in ways[0]] + [(2 * a + 1, 2 * b + 1) for a, b in ways[1]]
        for ways in ((rights, lefts), (lefts, rights))
    ]
    experts_each = experts // (2 * ring_size)
    plan = jnp.asarray(plans(ring, experts_each))
    plan = lax.dynamic_slice(
        plan, (2 * (dp % ring_size) + col, jnp.int32(0)), (1, plan.shape[1])
    ).reshape(-1)

    def send(values, which):
        return lax.ppermute(values, ("dp", "col"), routes_of[which])

    def chunk_at(step, which):
        return plan[2 * experts + 2 * step + which]

    def across_rings(values):
        if len(starts) == 1:
            return values
        peers = [[g + k for g in starts] for k in range(ring_size)]
        return lax.psum(values, "dp", axis_index_groups=peers)

    where = jnp.stack([row, seq_lengths[0], col])
    tokens_y = swap(tokens_in, "row")
    tokens_c = swap(tokens_in, "col")
    count = 4
    member = dp % count
    there, out_y = their_columns(
        jnp.stack([col, member]), w_query, w_key, w_value, w_out, count
    )
    gains = jnp.stack([norm_gain_attn, norm_gain_ffn])
    there = swap(there, "col")
    gains_c = swap(gains, "col")

    def project_half(own, other):
        return project(col_ref, own, other, gains, gains_c, w_query, w_key, w_value, there)

    near = project_half(tokens_in, tokens_c)
    gate_c = swap(w_gate, "col")
    out_y = swap(out_y, "row")
    tokens_y = after(tokens_y, near[2], out_y)
    tokens_yc = swap(tokens_y, "col")
    grad_y = swap(after(out_grad, tokens_y), "row")
    far = project_half(tokens_y, tokens_yc)
    shares = [out_y]
    for k in range(1, count):
        part = out_y if k < 3 else after(out_y, far[2])
        shares.append(lax.ppermute(part, "dp", [(m, m ^ k) for m in range(dp_size)]))
    where = after(where, grad_y, *shares)

    w_sgate, w_sup, w_sdown = w_shared_gate[None], w_shared_up[None], w_shared_down[None]
    up_c = swap(after(w_up, gate_c, tokens_yc), "col")

    attended = attend(where, near[2], far[2])
    attended_y = swap(attended, "row")
    attended_c = swap(attended, "col")
    out_c = swap(after(w_out, tokens_yc), "col")
    before = hidden_before(
        where,
        [tokens_in, tokens_c, tokens_y, tokens_yc],
        [attended, attended_c],
        w_out,
        out_c,
    )
    down_c = swap(after(w_down, tokens_yc), "col")
    attended_y = after(attended_y, before[0])
    out_y = join(member, *shares)
    out_yc = swap(out_y, "col")
    attended_yc = swap(attended_y, "col")
    grad_own = join(row, out_grad, grad_y)
    grad_other = swap(grad_own, "col")
    hidden, x_own, x_other, scale_ffn = hidden_after(
        where, before, [attended_y, attended_yc], out_y, out_yc, gains, gains_c
    )
    sgate_c, sup_c, sdown_c = (
        swap(after(w, attended_yc), "col") for w in (w_sgate, w_sup, w_sdown)
    )

    choices = jnp.arange(experts, dtype=jnp.int32)[:, None]
    dense = sum(
        jnp.where(routes[:, k][None, :] == choices, gate_weights[:, k][None, :], 0.0)
        for k in range(routes.shape[1])
    )
    gates = []
    for _ in range(3):
        gates.append(lax.reduce_precision(dense, 8, 7))
        dense = dense - gates[-1]
    gates = jnp.concatenate(gates, axis=0).astype(BF16)

    each = experts_each
    order = plan
    pairs_total = experts // 2
    routed = [w_gate, w_up, gate_c, up_c, w_down, down_c]
    shared = [w_sgate, w_sup, sgate_c, sup_c, w_sdown, sdown_c]

    def run(first, last, order, kept):
        return expert_grads(
            order,
            first,
            last,
            pairs_total,
            [x_own, x_other],
            [grad_own, grad_other],
            gates,
            routed,
            kept,
        )

    first = run(0, 1, order, ())
    kept = first[2:]
    sums = [first[0], first[1]]
    runs = {}
    mixed = {}
    normed = {}

    def work_experts(first, last):
        def work(order, ties):
            nonlocal kept
            result = run(first, last, order, tuple(kept))
            kept = result[2:]
            for at in range(first, last):
                runs[at] = (*result[0:2], at - first)
            return [kept[0]]

        return work

    def work_shared(order, ties):
        runs["shared"] = expert_grads(
            order, 0, 1, None, [x_own, x_other], [grad_own, grad_other], gates, shared, ()
        )
        return [runs["shared"][2]]

    def work_back(half):
        def work(order, ties):
            mixed[True, half] = mix(
                True,
                BF16 if half else F32,
                1 + half,
                order,
                kept[0],
                runs["shared"][2],
                routed[2 * half : 2 * half + 2],
                shared[2 * half : 2 * half + 2],
            )
            if half:
                normed["other"] = [swap(part, "col") for part in mixed[True, 1]]
                return list(mixed[True, 1])
            total, rounded, product = chip_sum(
                mixed[True, 0], normed["other"], hidden, gains
            )
            product_c = swap(product, "col")
            normed["sum"] = total
            normed["tie"] = rounded
            normed["came"] = swap(rounded, "row")
            normed["products"] = [product, product_c, swap(product, "row"), swap(product_c, "row")]
            return [mixed[True, 0]]

        return work

    def work_out(half):
        def work(order, ties):
            mixed[False, half] = mix(
                False,
                BF16 if half else F32,
                1,
                order,
                kept[1],
                runs["shared"][3],
                routed[4 + half : 5 + half],
                shared[4 + half : 5 + half],
            )
            return [mixed[False, half]]

        return work

    start = row * local_rows

    def my_rows(values):
        return lax.dynamic_slice_in_dim(values, start, local_rows, axis=0)

    def their_rows(values):
        return lax.dynamic_slice_in_dim(values, local_rows - start, local_rows, axis=0)

    def work_hidden(order, ties):
        normed["hidden"], *grad, normed["gain"] = norm_back(
            after(where, *ties),
            normed["sum"],
            normed["came"],
            hidden,
            scale_ffn,
            grad_own,
            gains,
            normed["products"],
        )
        normed["grad"] = grad
        normed["grad_c"] = [swap(part, "col") for part in grad]
        return grad

    def work_attend(order, ties):
        normed["qkv"] = attend_back(
            after(where, *ties), near[2], far[2], normed["grad"], normed["grad_c"], w_out, out_c
        )
        return [normed["qkv"]]

    def work_late(order, ties):
        normed["packs"] = late_grads(
            after(where, *ties),
            near[0:2],
            far[0:2],
            normed["qkv"],
            attended,
            normed["grad"],
            normed["grad_c"],
            runs["shared"][0:2],
        )
        return normed["packs"]

    def work_tie(order, ties):
        return [normed["tie"]]

    tasks = [work_experts(at, min(at + 2, pairs_total)) for at in range(1, pairs_total, 2)]
    tasks += [work_shared, work_back(1), work_back(0), None, work_out(0), work_tie]
    ends = [work_hidden, work_attend, work_late]
    tasks += [None] * (2 * ring_size - 2 - len(tasks) - len(ends)) + ends
    got = [None, None]
    got[0] = send(sums[0], 0)
    tasks.pop(0)(after(order, *sums), sums)
    got[1] = send(after(sums[1], kept[0]), 1)
    for s in range(1, ring_size):
        for k in range(2):
            last = sums
            task = tasks.pop(0) if tasks else None
            if task:
                last = task(after(order, *last), last)
            mine = runs[s]
            sums[k] = ring_sum(after(got[k], *last), mine[k], mine[2], s + 1 == ring_size)
            if s + 1 < ring_size:
                got[k] = send(sums[k], k)
            else:
                sums[k], got[k] = sums[k]
    crossed = [swap(across_rings(total), "col") for total in got]
    waves = [[across_rings(total)[0] for total in sums], [crossed[1][0], crossed[0][0]]]

    chunks_first = 2 * experts
    late_total = 2 * (ring_size - 1)

    def back_to_tokens(ties):
        hidden_grad = normed["hidden"]
        qkv_grad = after(normed["qkv"], *ties)
        here = jnp.concatenate(
            [halves(w, 1, col)[0] for w in (w_query, w_key, w_value)], axis=1
        )
        tokens_back = dot_nt(qkv_grad, here) + swap(
            dot_nt(qkv_grad, there).astype(BF16), "col"
        ).astype(F32)
        tokens_back = my_rows(tokens_back) + swap(
            their_rows(tokens_back).astype(BF16), "row"
        ).astype(F32)
        scale_attn = near[3]
        tokens_f32 = tokens_in.astype(F32)
        gain_attn_part = jnp.sum(tokens_back * tokens_f32 * scale_attn, axis=0)
        scaled = tokens_back * norm_gain_attn
        products = jnp.sum(scaled * tokens_f32, axis=1, keepdims=True)
        mean = (products + swap(products, "col")) / D
        tokens_grad = (
            my_rows(hidden_grad) + scale_attn * scaled - tokens_f32 * scale_attn**3 * mean
        ).astype(BF16)

        gain_parts = jnp.concatenate([gain_attn_part[None], normed["gain"]], axis=0)
        normed["gains"] = across_rings(gain_parts + swap(gain_parts, "row"))
        normed["tokens_grad"] = tokens_grad

    def block_rows(ties):
        ffn_sum = after(mixed[False, 0], *ties) + swap(mixed[False, 1], "col").astype(F32)
        ffn_rows = my_rows(ffn_sum) + swap(their_rows(ffn_sum).astype(BF16), "row").astype(F32)
        block_out = (my_rows(hidden) + ffn_rows).astype(BF16)
        normed["block_out"] = block_out

    shapes = [w_gate.shape, w_up.shape, w_down.shape]
    placed = ()
    late_out = [[], []]
    last, got = [], [None, None]
    moves = [(wave, step) for wave in range(2) for step in range(ring_size - 1)]
    for number, (wave, step) in enumerate(moves):
        current = [None, None]
        copies = [None, None]
        turn = number == ring_size - 1
        for k in range(2):
            at = chunks_first + 2 * number + k
            pack = normed["packs"][k]
            if number == 0:
                current[k] = late_load(plan, at, pack, after(waves[0][k], *last))
            elif number < ring_size - 1:
                current[k] = late_add(plan, at, pack, after(got[k], *last))
            elif turn:
                current[k], copies[k] = late_add(plan, at, pack, after(got[k], *last), True)
            else:
                current[k] = after(got[k], *last)
            last = [current[k]]
            if not turn:
                got[k] = send(current[k], k)
        if turn:
            placed = unpack(plan, experts + 2 * (ring_size - 1), 0, current, shapes, placed)
            others = [swap(across_rings(values), "col") for values in copies]
            for k in range(2):
                current[k] = late_join(
                    col_ref, after(copies[k], *last), others[1 - k], normed["gains"], waves[1][k]
                )
                got[k] = send(current[k], k)
                last = work_out(1)(after(order, current[k]), ()) if k == 0 else [current[k]]
        if number >= ring_size - 1:
            for k in range(2):
                late_out[k].append(current[k])
        placed = unpack(
            plan, experts + 2 * step, wave, [after(current[0], *last), current[1]], shapes, placed
        )
        last = placed[0:1]
        if number == 2:
            back_to_tokens(last)
        if number == ring_size + 1:
            block_rows(last)
    for k in range(2):
        late_out[k].append(after(got[k], *last))
        last = [late_out[k][-1]]
    placed = unpack(
        plan,
        experts + 2 * (ring_size - 1),
        1,
        [late_out[k][-1] for k in range(2)],
        shapes,
        placed,
    )
    gate_grad, up_grad, down_grad = placed
    shapes = [w.shape for w in (w_shared_gate, w_shared_up, w_shared_down)]
    shapes += [w.shape for w in (w_query, w_key, w_value, w_out)] + [gains.shape]
    finals = unpack_late(plan, chunks_first + late_total, late_out, shapes)
    shared_gate_grad, shared_up_grad, shared_down_grad = finals[0:3]
    query_grad, key_grad, value_grad, out_proj_grad, gain_grads = finals[3:8]


    return (
        normed["block_out"],
        normed["tokens_grad"],
        gain_grads[0],
        query_grad,
        key_grad,
        value_grad,
        out_proj_grad,
        gain_grads[1],
        gate_grad,
        up_grad,
        down_grad,
        shared_gate_grad,
        shared_up_grad,
        shared_down_grad,
    )


def solution(mesh):
    in_specs = (
        P(("dp", "row"), "col"),
        P("col"),
        P("col", "row"),
        P("col", "row"),
        P("col", "row"),
        P("row", "col"),
        P("col"),
        P(None, "col", "row"),
        P(None, "col", "row"),
        P(None, "row", "col"),
        P("col", "row"),
        P("col", "row"),
        P("row", "col"),
        P("dp", None),
        P("dp", None),
        P("dp"),
        P(("dp", "row"), "col"),
    )
    out_specs = (
        P(("dp", "row"), "col"),
        P(("dp", "row"), "col"),
        P("col"),
        P("col", "row"),
        P("col", "row"),
        P("col", "row"),
        P("row", "col"),
        P("col"),
        P(None, "col", "row"),
        P(None, "col", "row"),
        P(None, "row", "col"),
        P("col", "row"),
        P("col", "row"),
        P("row", "col"),
    )
    return jax.shard_map(body, mesh=mesh, in_specs=in_specs, out_specs=out_specs, check_vma=False)
```

```python
import functools

import jax
import jax.numpy as jnp
import numpy as np
from jax import lax
from jax.experimental import pallas as pl
from jax.experimental.pallas import tpu as pltpu
from jax.sharding import PartitionSpec as P

D = 1536
HQ = 12
HK = 4
DH = 128
GROUP_HEADS = HQ // HK
LANES = 128

EPSILON = 1e-05
F32 = jnp.float32
BF16 = jnp.bfloat16
MIB = 1024 * 1024
GAIN_ROWS = 16
RING = 8
LATE_BLOCKS = 5
SMALL = pl.CostEstimate(flops=0, bytes_accessed=0, transcendentals=0)


def params(mib, *semantics):
    return pltpu.CompilerParams(
        dimension_semantics=semantics or None, vmem_limit_bytes=mib * MIB
    )


def dot(left, right):
    return jnp.dot(left, right, preferred_element_type=F32)


def dot_nt(left, right):
    return lax.dot_general(left, right, (((1,), (1,)), ((), ())), preferred_element_type=F32)


def dot_tn(left, right):
    return lax.dot_general(left, right, (((0,), (0,)), ((), ())), preferred_element_type=F32)


def after(values, *others):
    return lax.optimization_barrier((values, *others))[0]


def swap(values, axis):
    return lax.ppermute(values, axis, [(0, 1), (1, 0)])


def halves(values, axis, mine):
    size = values.shape[axis] // 2
    low = lax.slice_in_dim(values, 0, size, axis=axis)
    high = lax.slice_in_dim(values, size, 2 * size, axis=axis)
    return jnp.where(mine == 0, low, high), jnp.where(mine == 0, high, low)


def in_order(own, other, mine, axis):
    return jnp.concatenate(
        [jnp.where(mine == 0, own, other), jnp.where(mine == 0, other, own)], axis=axis
    )


def gather_rows(place_ref, own_ref, other_ref, all_ref):
    row = place_ref[0]
    rows = own_ref.shape[0]
    all_ref[pl.ds(pl.multiple_of(row * rows, rows), rows), :] = own_ref[...]
    all_ref[pl.ds(pl.multiple_of((1 - row) * rows, rows), rows), :] = other_ref[...]


def head_rows(ref, first, block):
    return jnp.concatenate(
        [ref[first : first + block, h * DH : (h + 1) * DH] for h in range(GROUP_HEADS)], axis=0
    )


def key_probs(query, key, first, length):
    block, keys = query.shape[0] // GROUP_HEADS, key.shape[0]
    scores = dot_nt(query, key) * DH ** (-0.5)
    shape = (block, keys)
    query_at = lax.broadcasted_iota(jnp.int32, shape, 0) + first
    key_at = lax.broadcasted_iota(jnp.int32, shape, 1)
    allowed = (key_at <= query_at) & (key_at < length)
    allowed = jnp.concatenate([allowed] * GROUP_HEADS, axis=0)
    scores = jnp.where(allowed, scores, -1e30)
    weights = jnp.exp(scores - jnp.max(scores, axis=1, keepdims=True))
    return weights * (1.0 / jnp.sum(weights, axis=1, keepdims=True))


def attend_kernel(place_ref, own_ref, other_ref, out_ref, all_ref):
    gather_rows(place_ref, own_ref, other_ref, all_ref)
    rows = own_ref.shape[0]
    block = 256
    width = GROUP_HEADS * DH
    for at in range(2 * rows // block):
        first, keys = at * block, (at + 1) * block
        query = head_rows(all_ref, first, block)
        key = all_ref[0:keys, width : width + DH]
        value = all_ref[0:keys, width + DH : width + 2 * DH]
        probs = key_probs(query, key, first, place_ref[1])
        result = dot(probs.astype(BF16), value).astype(BF16)
        for h in range(GROUP_HEADS):
            out_ref[first : first + block, h * DH : (h + 1) * DH] = result[
                h * block : (h + 1) * block
            ]


def attend(place, own, other):
    rows, width = own.shape
    spec = pl.BlockSpec(memory_space=pltpu.VMEM)
    return pl.pallas_call(
        attend_kernel,
        out_shape=jax.ShapeDtypeStruct((2 * rows, GROUP_HEADS * DH), BF16),
        in_specs=[pl.BlockSpec(memory_space=pltpu.SMEM), spec, spec],
        out_specs=spec,
        scratch_shapes=[pltpu.VMEM((2 * rows, width), BF16)],
        compiler_params=params(32),
        cost_estimate=SMALL,
        name="attend",
    )(place, own, other)


def attend_back_kernel(
    place_ref, own_ref, other_ref, *refs
):
    grad_refs, grad_c_refs = refs[0:2], refs[2:4]
    out_ref, out_c_ref, result_ref, all_ref, total_ref = refs[4:9]
    gather_rows(place_ref, own_ref, other_ref, all_ref)
    rows = own_ref.shape[0]
    block = 256
    width = GROUP_HEADS * DH
    group = pl.ds(pl.multiple_of(place_ref[2] * width, width), width)
    blocks = 2 * rows // block
    for at in reversed(range(blocks)):
        first, keys = at * block, (at + 1) * block
        query = head_rows(all_ref, first, block)
        key = all_ref[0:keys, width : width + DH]
        value = all_ref[0:keys, width + DH : width + 2 * DH]
        probs = key_probs(query, key, first, place_ref[1])
        half, in_half = divmod(first, rows)
        piece = slice(in_half, in_half + block)
        grad = dot_nt(grad_refs[half][piece, :], out_ref[group, :])
        grad = (grad + dot_nt(grad_c_refs[half][piece, :], out_c_ref[group, :])).astype(BF16)
        grad = jnp.concatenate(
            [grad[:, h * DH : (h + 1) * DH] for h in range(GROUP_HEADS)], axis=0
        )
        probs_grad = dot_nt(grad, value)
        carried = jnp.sum(probs * probs_grad, axis=1, keepdims=True)
        score_grad = (probs * (probs_grad - carried)).astype(BF16)
        query_back = (dot(score_grad, key) * DH ** (-0.5)).astype(BF16)
        for h in range(GROUP_HEADS):
            result_ref[first:keys, h * DH : (h + 1) * DH] = query_back[
                h * block : (h + 1) * block
            ]
        key_back = dot_tn(score_grad, query)
        value_back = dot_tn(probs.astype(BF16), grad)
        if at == blocks - 1:
            total_ref[:, 0:DH] = key_back
            total_ref[:, DH:] = value_back
        else:
            total_ref[0:keys, 0:DH] += key_back
            total_ref[0:keys, DH:] += value_back
    result_ref[:, width : width + DH] = (total_ref[:, 0:DH] * DH ** (-0.5)).astype(BF16)
    result_ref[:, width + DH :] = total_ref[:, DH:].astype(BF16)


def attend_back(place, own, other, grad, grad_c, w_out, out_c):
    rows, width = own.shape
    spec = pl.BlockSpec(memory_space=pltpu.VMEM)
    return pl.pallas_call(
        attend_back_kernel,
        out_shape=jax.ShapeDtypeStruct((2 * rows, width), BF16),
        in_specs=[pl.BlockSpec(memory_space=pltpu.SMEM)] + [spec] * 8,
        out_specs=spec,
        scratch_shapes=[
            pltpu.VMEM((2 * rows, width), BF16),
            pltpu.VMEM((2 * rows, 2 * DH), F32),
        ],
        compiler_params=params(60),
        cost_estimate=SMALL,
        name="attend_back",
    )(place, own, other, *grad, *grad_c, w_out, out_c)


def unit_slices(unit, share):
    row, lane = divmod(unit, 3)
    return slice(row * share, (row + 1) * share), slice(lane * LANES, (lane + 1) * LANES)


def late_kernel(place_ref, *refs):
    near, near_c, far, far_c, qkv_ref, attended_ref = refs[0:6]
    grad_refs, grad_c_refs, shared, outs = refs[6:8], refs[8:10], refs[10:12], refs[12:14]
    rows, features = near.shape
    own_rows = pl.ds(pl.multiple_of(place_ref[0] * rows, rows), rows)
    far_rows = pl.ds(pl.multiple_of((1 - place_ref[0]) * rows, rows), rows)
    split = 7 * LANES

    chunks = outs[0].shape[0]
    share = features // chunks

    def store(h, at, values):
        values = values.astype(BF16)
        for b in range(values.shape[1] // LANES):
            part, unit = divmod(at // LANES + b, split // LANES)
            to_rows, to_lanes = unit_slices(h * (split // LANES) + unit, share)

            def write(out_ref, b=b, to_rows=to_rows, to_lanes=to_lanes):
                for chunk in range(chunks):
                    out_ref[chunk, to_rows, to_lanes] = values[
                        chunk * share : (chunk + 1) * share, b * LANES : (b + 1) * LANES
                    ]

            pl.when(place_ref[2] == 0)(lambda part=part, write=write: write(outs[part]))
            pl.when(place_ref[2] != 0)(lambda part=part, write=write: write(outs[1 - part]))

    for out_ref in outs:
        to_rows, to_lanes = unit_slices(2 * (split // LANES), share)
        for chunk in range(chunks):
            out_ref[chunk, to_rows, to_lanes] = jnp.zeros((share, LANES), BF16)

    for h, (x, y, grad) in enumerate(((near, far, grad_refs), (near_c, far_c, grad_c_refs))):
        for k in range(2):
            store(h, 3 * LANES * k, shared[k][0, h * features : (h + 1) * features, :])
        project = dot_tn(x[...], qkv_ref[own_rows, :]) + dot_tn(y[...], qkv_ref[far_rows, :])
        store(h, 6 * LANES, project)
        out = [dot_tn(grad[k][...], attended_ref[k * rows : (k + 1) * rows, :]) for k in range(2)]
        store(h, 11 * LANES, out[0] + out[1])


def late_grads(place, near, far, qkv_grad, attended, grad, grad_c, shared):
    features = near[0].shape[1]
    rows = LATE_BLOCKS * (features // RING)
    spec = pl.BlockSpec(memory_space=pltpu.VMEM)
    return pl.pallas_call(
        late_kernel,
        out_shape=[jax.ShapeDtypeStruct((RING, rows, 3 * LANES), BF16)] * 2,
        in_specs=[pl.BlockSpec(memory_space=pltpu.SMEM)] + [spec] * 12,
        out_specs=[spec] * 2,
        compiler_params=params(60),
        cost_estimate=SMALL,
        name="late_grads",
    )(place, *near, *far, qkv_grad, attended, *grad, *grad_c, *shared)


def columns_kernel(
    place_ref, query_ref, key_ref, value_ref, w_out_ref, out_ref, share_ref
):
    share_ref[...] = w_out_ref[...]
    width = GROUP_HEADS * DH
    out_ref[:, 0:width] = query_ref[...]
    out_ref[:, width : width + DH] = key_ref[...]
    out_ref[:, width + DH :] = value_ref[...]


def their_columns(place, w_query, w_key, w_value, w_out, shares):
    rows = w_query.shape[0]
    width = GROUP_HEADS * DH + 2 * DH

    def theirs(width):
        return pl.BlockSpec((rows, width), lambda i, c: (0, 1 - c[0]))

    return pl.pallas_call(
        columns_kernel,
        grid_spec=pltpu.PrefetchScalarGridSpec(
            num_scalar_prefetch=1,
            grid=(1,),
            in_specs=[theirs(GROUP_HEADS * DH), theirs(DH), theirs(DH)]
            + [pl.BlockSpec((rows // shares, rows), lambda i, c: (c[1], 0))],
            out_specs=[
                pl.BlockSpec((rows, width), lambda i, c: (0, 0)),
                pl.BlockSpec((rows // shares, rows), lambda i, c: (0, 0)),
            ],
        ),
        out_shape=[
            jax.ShapeDtypeStruct((rows, width), BF16),
            jax.ShapeDtypeStruct((rows // shares, rows), BF16),
        ],
        compiler_params=params(60, "arbitrary"),
        cost_estimate=SMALL,
        name="their_columns",
    )(place, w_query, w_key, w_value, w_out)


def join_kernel(mine_ref, *refs):
    *parts, out_ref = refs
    rows = parts[0].shape[0]
    for k, part in enumerate(parts):
        at = jnp.bitwise_xor(mine_ref[0], k)
        out_ref[pl.ds(pl.multiple_of(at * rows, rows), rows), :] = part[...]


def join(mine, *parts):
    rows, width = parts[0].shape
    spec = pl.BlockSpec(memory_space=pltpu.VMEM)
    return pl.pallas_call(
        join_kernel,
        out_shape=jax.ShapeDtypeStruct((len(parts) * rows, width), parts[0].dtype),
        in_specs=[pl.BlockSpec(memory_space=pltpu.SMEM)] + [spec] * len(parts),
        out_specs=spec,
        compiler_params=params(16),
        cost_estimate=SMALL,
        name="join",
    )(mine.reshape(1), *parts)


def project_kernel(col_ref, own_ref, other_ref, gains_ref, gains_c_ref, query_ref, key_ref, value_ref, there_ref, x_own_ref, x_other_ref, qkv_ref, scale_ref):
    own = own_ref[...].astype(F32)
    other = other_ref[...].astype(F32)
    total = jnp.sum(own * own, axis=1, keepdims=True)
    total = total + jnp.sum(other * other, axis=1, keepdims=True)
    scale = lax.rsqrt(total / D + EPSILON)
    own = (own * scale * gains_ref[0:1, :]).astype(BF16)
    other = (other * scale * gains_c_ref[0:1, :]).astype(BF16)
    x_own_ref[...] = own
    x_other_ref[...] = other
    scale_ref[...] = scale
    here = jnp.concatenate([query_ref[...], key_ref[...], value_ref[...]], axis=1)
    qkv_ref[...] = (dot(own, here) + dot(other, there_ref[...])).astype(BF16)


def project(col, own, other, gains, gains_c, w_query, w_key, w_value, there):
    rows, features = own.shape
    width = there.shape[1]
    group = GROUP_HEADS * DH
    tile = rows // 2

    def whole(*shape):
        return pl.BlockSpec(shape, lambda i, c: (0,) * len(shape))

    def mine(width):
        return pl.BlockSpec((features, width), lambda i, c: (0, c[0]))

    def rowwise(width):
        return pl.BlockSpec((tile, width), lambda i, c: (i, 0))

    return pl.pallas_call(
        project_kernel,
        grid_spec=pltpu.PrefetchScalarGridSpec(
            num_scalar_prefetch=1,
            grid=(rows // tile,),
            in_specs=[
                rowwise(features),
                rowwise(features),
                whole(2, features),
                whole(2, features),
                mine(group),
                mine(DH),
                mine(DH),
                whole(features, width),
            ],
            out_specs=[rowwise(features), rowwise(features), rowwise(width), rowwise(1)],
        ),
        out_shape=[
            jax.ShapeDtypeStruct((rows, features), BF16),
            jax.ShapeDtypeStruct((rows, features), BF16),
            jax.ShapeDtypeStruct((rows, width), BF16),
            jax.ShapeDtypeStruct((rows, 1), F32),
        ],
        compiler_params=params(60, "arbitrary"),
        cost_estimate=SMALL,
        name="project",
    )(col, own, other, gains, gains_c, w_query, w_key, w_value, there)


def head_pair(col_ref, own, other):
    first, second = own[...], other[...]
    flipped = col_ref != 0
    return jnp.concatenate(
        [jnp.where(flipped, second, first), jnp.where(flipped, first, second)], axis=1
    )


def before_kernel(tiles, place_ref, *refs):
    near, near_c, far, far_c, attended, attended_c, here, there, own_ref, other_ref = refs
    is_near = (pl.program_id(0) >= tiles // 2).astype(jnp.int32) == place_ref[0]
    heads = head_pair(place_ref[2], attended, attended_c)
    own = jnp.where(is_near, near[...], far[...]).astype(F32)
    other = jnp.where(is_near, near_c[...], far_c[...]).astype(F32)
    own_ref[...] = own + dot(heads, here[...])
    other_ref[...] = other + dot(heads, there[...])


def after_kernel(place_ref, *refs):
    own_ref, other_ref, attended, attended_c, here, there, gains_ref, gains_c_ref = refs[0:8]
    hidden_ref, x_own_ref, x_other_ref, scale_ref = refs[8:12]
    heads = head_pair(place_ref[2], attended, attended_c)
    own = own_ref[...] + dot(heads, here[...])
    other = other_ref[...] + dot(heads, there[...])
    total = jnp.sum(own * own, axis=1, keepdims=True)
    total = total + jnp.sum(other * other, axis=1, keepdims=True)
    scale = lax.rsqrt(total / D + EPSILON)
    hidden_ref[...] = own
    scale_ref[...] = scale
    x_own_ref[...] = (own * scale * gains_ref[1:2, :]).astype(BF16)
    x_other_ref[...] = (other * scale * gains_c_ref[1:2, :]).astype(BF16)


TOKEN_TILE = 256


def rowwise(width):
    return pl.BlockSpec((TOKEN_TILE, width), lambda i, p: (i, 0))


def whole(*shape):
    return pl.BlockSpec(shape, lambda i, p: (0,) * len(shape))


def hidden_before(place, tokens, attended, here, there):
    half, features = tokens[0].shape
    rows, heads = attended[0].shape
    tiles = rows // TOKEN_TILE
    per_half = half // TOKEN_TILE
    halfwise = pl.BlockSpec((TOKEN_TILE, features), lambda i, p: (i % per_half, 0))
    return pl.pallas_call(
        functools.partial(before_kernel, tiles),
        grid_spec=pltpu.PrefetchScalarGridSpec(
            num_scalar_prefetch=1,
            grid=(tiles,),
            in_specs=[halfwise] * 4 + [rowwise(heads)] * 2 + [whole(2 * heads, features)] * 2,
            out_specs=[rowwise(features)] * 2,
        ),
        out_shape=[jax.ShapeDtypeStruct((rows, features), F32)] * 2,
        compiler_params=params(56, "arbitrary"),
        cost_estimate=pl.CostEstimate(
            flops=8 * rows * features * heads,
            bytes_accessed=16 * rows * features,
            transcendentals=0,
        ),
        name="hidden_before",
    )(place, *tokens, *attended, here, there)


def hidden_after(place, before, attended, here, there, gains, gains_c):
    rows, features = before[0].shape
    heads = attended[0].shape[1]
    return pl.pallas_call(
        after_kernel,
        grid_spec=pltpu.PrefetchScalarGridSpec(
            num_scalar_prefetch=1,
            grid=(rows // TOKEN_TILE,),
            in_specs=[rowwise(features)] * 2
            + [rowwise(heads)] * 2
            + [whole(2 * heads, features)] * 2
            + [whole(2, features)] * 2,
            out_specs=[rowwise(features)] * 3 + [rowwise(1)],
        ),
        out_shape=[
            jax.ShapeDtypeStruct((rows, features), F32),
            jax.ShapeDtypeStruct((rows, features), BF16),
            jax.ShapeDtypeStruct((rows, features), BF16),
            jax.ShapeDtypeStruct((rows, 1), F32),
        ],
        compiler_params=params(56, "arbitrary"),
        cost_estimate=SMALL,
        name="hidden_after",
    )(place, *before, *attended, here, there, gains, gains_c)


def expert_kernel(shared, aliased, first, order_ref, *refs):
    x_own, x_other, o_own, o_other, gates_ref = refs[0:5]
    weights = refs[5:17]
    grads = refs[17 + aliased : 19 + aliased]
    pair_ref, inner_ref = refs[19 + aliased : 21 + aliased]
    step = pl.program_id(0) + first
    rows, features = x_own.shape
    tile = 512
    up_own = jnp.concatenate([weights[k][0] for k in (0, 1, 6, 7)], axis=1)
    up_other = jnp.concatenate([weights[k][0] for k in (2, 3, 8, 9)], axis=1)
    down_own = jnp.concatenate([weights[k][0] for k in (4, 10)], axis=0)
    down_other = jnp.concatenate([weights[k][0] for k in (5, 11)], axis=0)

    def token_tile(t, carry):
        at = pl.ds(pl.multiple_of(t * tile, tile), tile)
        pre = dot(x_own[at, :], up_own) + dot(x_other[at, :], up_other)
        back = dot_nt(o_own[at, :], down_own) + dot_nt(o_other[at, :], down_other)
        for k in range(2):
            pre_gate = pre[:, 2 * k * LANES : (2 * k + 1) * LANES]
            pre_up = pre[:, (2 * k + 1) * LANES : (2 * k + 2) * LANES]
            inner_grad = back[:, k * LANES : (k + 1) * LANES]
            sigmoid = 1.0 / (1.0 + jnp.exp(-pre_gate))
            silu = pre_gate * sigmoid
            inner = silu * pre_up
            if not shared:
                shape = (gates_ref.shape[0], LANES)
                expert = lax.broadcasted_iota(jnp.int32, shape, 0) % (gates_ref.shape[0] // 3)
                chosen = (expert == order_ref[2 * step + k]).astype(F32).astype(BF16)
                gate = dot_tn(gates_ref[:, at], chosen)
                inner = gate * inner
                inner_grad = gate * inner_grad
            gate_grad = inner_grad * pre_up * (sigmoid * (1.0 + pre_gate * (1.0 - sigmoid)))
            inner_ref[0, at, k * LANES : (k + 1) * LANES] = inner.astype(BF16)
            pair_ref[0, at, 2 * k * LANES : (2 * k + 1) * LANES] = gate_grad.astype(BF16)
            pair_ref[0, at, (2 * k + 1) * LANES : (2 * k + 2) * LANES] = (
                inner_grad * silu
            ).astype(BF16)
        return carry

    lax.fori_loop(0, rows // tile, token_tile, 0)
    pairs = pair_ref[0]
    for h, x in enumerate((x_own, x_other)):
        wide = dot_tn(x[...], pairs).astype(BF16)
        for k in range(2):
            grads[k][0, h * features : (h + 1) * features, 0 : 2 * LANES] = wide[
                :, 2 * k * LANES : (2 * k + 2) * LANES
            ]
    inner = inner_ref[0]
    tile = 256
    for h, o in enumerate((o_own, o_other)):
        for j in range(features // tile):
            low = dot_tn(inner, o[:, j * tile : (j + 1) * tile]).astype(BF16)
            for k in range(2):
                for b in range(tile // LANES):
                    at = h * features + j * tile + b * LANES
                    grads[k][0, at : at + LANES, 2 * LANES :] = low[
                        k * LANES : (k + 1) * LANES, b * LANES : (b + 1) * LANES
                    ]


def expert_specs(features, place, wide, low):
    specs = []
    if wide:
        block = pl.BlockSpec((1, features, LANES), lambda i, o: (place(i, o)[0], 0, place(i, o)[1]))
        specs += [block] * 4
    if low:
        block = pl.BlockSpec((1, LANES, features), lambda i, o: (*place(i, o), 0))
        specs += [block] * 2
    return specs


def expert_grads(order, first, last, total, x, o, gates, weights, kept):
    shared = total is None
    steps = last - first
    rows, features = x[0].shape
    aliased = len(kept)

    def fixed(*shape):
        return pl.BlockSpec(shape, lambda i, o: (0,) * len(shape))

    def stepped(*shape):
        return pl.BlockSpec((1, *shape), lambda i, o: (i, 0, 0))

    def placed(*shape):
        return pl.BlockSpec((1, *shape), lambda i, o: (i + first, 0, 0))

    specs = []
    for k in range(2):
        if shared:

            def picked(i, o, k=k):
                return 0, 2 * o[o.shape[0] - 1] + k

        else:

            def picked(i, o, k=k):
                return o[2 * (i + first) + k], o[o.shape[0] - 1]

        specs += expert_specs(features, picked, True, True)
    total = steps if shared else total
    return pl.pallas_call(
        functools.partial(expert_kernel, shared, aliased, first),
        grid_spec=pltpu.PrefetchScalarGridSpec(
            num_scalar_prefetch=1,
            grid=(steps,),
            in_specs=[fixed(rows, features)] * 4
            + [fixed(*gates.shape)]
            + specs
            + [pl.BlockSpec(memory_space=pl.ANY)] * aliased,
            out_specs=[stepped(2 * features, 3 * LANES)] * 2
            + [placed(rows, 4 * LANES), placed(rows, 2 * LANES)],
        ),
        out_shape=[jax.ShapeDtypeStruct((steps, 2 * features, 3 * LANES), BF16)] * 2
        + [
            jax.ShapeDtypeStruct((total, rows, 4 * LANES), BF16),
            jax.ShapeDtypeStruct((total, rows, 2 * LANES), BF16),
        ],
        input_output_aliases={18 + k: 2 + k for k in range(aliased)},
        compiler_params=params(40, "arbitrary"),
        cost_estimate=SMALL,
        name="expert_grads",
    )(order, *x, *o, gates, *weights, *weights, *kept)


def mix_kernel(back, group, pieces, order_ref, *refs):
    acts_ref, shared_ref = refs[0:2]
    each = 2 if back else 1
    count = 2 * group * each
    weights = refs[2 : 2 + count]
    shared = refs[2 + count : 2 + count + 2 * each]
    *outs, total_ref = refs[2 + count + 2 * each :]
    step = pl.program_id(0)
    rows = total_ref.shape[0]
    tile = 512
    times = dot_nt if back else dot
    along = 1 if back else 0

    @pl.when(step == 0)
    def _():
        both = jnp.concatenate([w[0] for w in shared], axis=along)
        for t in range(rows // tile):
            at = slice(t * tile, (t + 1) * tile)
            total_ref[at, :] = times(shared_ref[0, at, :], both)

    both = jnp.concatenate([w[0] for w in weights], axis=along)
    for t in range(rows // tile):
        at = slice(t * tile, (t + 1) * tile)
        acts = jnp.concatenate([acts_ref[g, at, :] for g in range(group)], axis=1)
        total_ref[at, :] += times(acts, both)

    @pl.when(step == pl.num_programs(0) - 1)
    def _():
        part = rows // pieces
        for k, out_ref in enumerate(outs):
            out_ref[...] = total_ref[k * part : (k + 1) * part, :].astype(out_ref.dtype)


def mix(back, dtype, pieces, order, acts, shared_acts, weights, shared_weights):
    pairs, rows, width = acts.shape
    features = weights[0].shape[1] if back else weights[0].shape[2]
    group = 4 if pairs % 4 == 0 else 1

    def spec(place):
        if back:
            return pl.BlockSpec((1, features, LANES), lambda i, o: (place(i, o)[0], 0, place(i, o)[1]))
        return pl.BlockSpec((1, LANES, features), lambda i, o: (*place(i, o), 0))

    def routed(k):
        return spec(lambda i, o: (o[2 * group * i + k], o[o.shape[0] - 1]))

    def common(k):
        return spec(lambda i, o: (0, 2 * o[o.shape[0] - 1] + k))

    outs = pl.pallas_call(
        functools.partial(mix_kernel, back, group, pieces),
        grid_spec=pltpu.PrefetchScalarGridSpec(
            num_scalar_prefetch=1,
            grid=(pairs // group,),
            in_specs=[
                pl.BlockSpec((group, rows, width), lambda i, o: (i, 0, 0)),
                pl.BlockSpec((1, rows, width), lambda i, o: (0, 0, 0)),
            ]
            + [routed(k) for k in range(2 * group) for _ in weights]
            + [common(k) for k in range(2) for _ in weights],
            out_specs=[pl.BlockSpec((rows // pieces, features), lambda i, o: (0, 0))] * pieces,
            scratch_shapes=[pltpu.VMEM((rows, features), F32)],
        ),
        out_shape=[jax.ShapeDtypeStruct((rows // pieces, features), dtype)] * pieces,
        compiler_params=params(48, "arbitrary"),
        cost_estimate=SMALL,
        name="mix",
    )(order, acts, shared_acts, *weights * (2 * group), *shared_weights * 2)
    return outs if pieces > 1 else outs[0]


def chip_sum_kernel(tiles, own_ref, first_ref, second_ref, hidden_ref, gains_ref, total_ref, rounded_ref, product_ref):
    is_first = pl.program_id(0) < tiles // 2
    other = jnp.where(is_first, first_ref[...], second_ref[...])
    total = own_ref[...] + other.astype(F32)
    total_ref[...] = total
    rounded_ref[...] = total.astype(BF16)
    product_ref[...] = lax.dot_general(
        jnp.ones((8, total.shape[1]), F32),
        total * gains_ref[1:2, :] * hidden_ref[...],
        (((1,), (1,)), ((), ())),
        precision=lax.Precision.HIGHEST,
        preferred_element_type=F32,
    )


def chip_sum(own, other, hidden, gains):
    rows, features = own.shape
    spec = pl.BlockSpec((TOKEN_TILE, features), lambda i: (i, 0))
    tiles = rows // TOKEN_TILE
    piece = pl.BlockSpec((TOKEN_TILE, features), lambda i: (i % (tiles // 2), 0))
    return pl.pallas_call(
        functools.partial(chip_sum_kernel, tiles),
        grid=(tiles,),
        out_shape=[
            jax.ShapeDtypeStruct((rows, features), F32),
            jax.ShapeDtypeStruct((rows, features), BF16),
            jax.ShapeDtypeStruct((8, rows), F32),
        ],
        in_specs=[spec, piece, piece, spec, pl.BlockSpec(gains.shape, lambda i: (0, 0))],
        out_specs=[spec, spec, pl.BlockSpec((8, TOKEN_TILE), lambda i: (0, i))],
        compiler_params=params(24, "arbitrary"),
        cost_estimate=SMALL,
        name="chip_sum",
    )(own, *other, hidden, gains)


def norm_back_kernel(tiles, place_ref, *refs):
    sum_ref, came_ref, hidden_ref, scale_ref, out_grad_ref, gains_ref = refs[0:6]
    products = refs[6:10]
    hidden_grad_ref, first_ref, second_ref, gain_ref = refs[10:14]
    step = pl.program_id(0)
    part = (step >= tiles // 2).astype(jnp.int32)
    grad = sum_ref[...] + came_ref[...].astype(F32)
    hidden = hidden_ref[...]
    scale = scale_ref[...]
    total = (products[0][...] + products[1][...]) + (products[2][...] + products[3][...])
    mean = lax.dot_general(
        total,
        jnp.full((8, LANES), 1.0 / (8 * D), F32),
        (((0,), (0,)), ((), ())),
        precision=lax.Precision.HIGHEST,
        preferred_element_type=F32,
    )[:, 0:1]
    result = out_grad_ref[...].astype(F32) + scale * (grad * gains_ref[1:2, :])
    result = result - hidden * (scale * scale * scale * mean)
    hidden_grad_ref[...] = result
    for k, rounded_ref in enumerate((first_ref, second_ref)):

        @pl.when(part == k)
        def _(rounded_ref=rounded_ref):
            rounded_ref[...] = result.astype(BF16)

    @pl.when(step == 0)
    def _():
        gain_ref[...] = jnp.zeros_like(gain_ref)

    @pl.when(part == place_ref[0])
    def _():
        gain_ref[...] += jnp.sum(grad * hidden * scale, axis=0, keepdims=True)


def norm_back(place, sums, came, hidden, scale, out_grad, gains, products):
    rows, features = hidden.shape
    tiles = rows // TOKEN_TILE
    lanes = pl.BlockSpec((8, TOKEN_TILE), lambda i, p: (0, i))

    def piece(k):
        last = tiles // 2 - 1
        return pl.BlockSpec(
            (TOKEN_TILE, features), lambda i, p: (jnp.clip(i - k * tiles // 2, 0, last), 0)
        )

    return pl.pallas_call(
        functools.partial(norm_back_kernel, tiles),
        grid_spec=pltpu.PrefetchScalarGridSpec(
            num_scalar_prefetch=1,
            grid=(tiles,),
            in_specs=[rowwise(features)] * 3
            + [rowwise(1), rowwise(features), whole(2, features)]
            + [lanes] * 4,
            out_specs=[rowwise(features), piece(0), piece(1), whole(1, features)],
        ),
        out_shape=[
            jax.ShapeDtypeStruct((rows, features), F32),
            jax.ShapeDtypeStruct((rows // 2, features), BF16),
            jax.ShapeDtypeStruct((rows // 2, features), BF16),
            jax.ShapeDtypeStruct((1, features), F32),
        ],
        compiler_params=params(48, "arbitrary"),
        cost_estimate=SMALL,
        name="norm_back",
    )(place, sums, came, hidden, scale, out_grad, gains, *products)


def ring_of(size):
    return list(range(0, size, 2)) + list(range(1, size, 2))[::-1]


def unpack_kernel(aliased, plan_ref, *refs):
    chunks = refs[0:2]
    gate_ref, up_ref, down_ref = refs[2 + aliased : 5 + aliased]
    rows = gate_ref.shape[1]

    def write(chunk_ref):
        first = chunk_ref.shape[0] - rows
        gate_ref[0] = chunk_ref[first:, 0:LANES].astype(F32)
        up_ref[0] = chunk_ref[first:, LANES : 2 * LANES].astype(F32)
        for b in range(rows // LANES):
            at = slice(first + b * LANES, first + (b + 1) * LANES)
            down_ref[0, :, b * LANES : (b + 1) * LANES] = chunk_ref[at, 2 * LANES :].astype(F32)

    for k in range(2):
        pl.when(pl.program_id(0) == k)(lambda k=k: write(chunks[k]))


def unpack(plan, first, wave, chunks, shapes, outs):
    rows = shapes[0][1]

    def place(d, n):
        block = n[n.shape[0] - 1]
        return n[first + d], 1 - block if wave else block

    def wide(d, n):
        expert, block = place(d, n)
        return (expert, 0, block)

    def low(d, n):
        expert, block = place(d, n)
        return (expert, block, 0)

    aliased = len(outs)
    return pl.pallas_call(
        functools.partial(unpack_kernel, aliased),
        grid_spec=pltpu.PrefetchScalarGridSpec(
            num_scalar_prefetch=1,
            grid=(2,),
            in_specs=[pl.BlockSpec(chunk.shape, lambda d, n: (0, 0)) for chunk in chunks]
            + [pl.BlockSpec(memory_space=pl.ANY)] * aliased,
            out_specs=[
                pl.BlockSpec((1, rows, LANES), wide),
                pl.BlockSpec((1, rows, LANES), wide),
                pl.BlockSpec((1, LANES, rows), low),
            ],
        ),
        out_shape=[jax.ShapeDtypeStruct(shape, F32) for shape in shapes],
        input_output_aliases={3 + k: k for k in range(aliased)},
        compiler_params=params(16, "arbitrary"),
        cost_estimate=SMALL,
        name="unpack",
    )(plan, *chunks, *outs)


def ring_sum_kernel(came_ref, mine_ref, *outs):
    total = (came_ref[...].astype(F32) + mine_ref[...].astype(F32)).astype(BF16)
    if len(outs) == 1:
        outs[0][...] = total
    else:
        half = pl.program_id(1) // (pl.num_programs(1) // 2)
        for k, out_ref in enumerate(outs):

            @pl.when(half == k)
            def _(out_ref=out_ref):
                out_ref[...] = total


def ring_sum(came, mine, first, halved):
    count, rows, lanes = came.shape
    tiles = 2
    spec = pl.BlockSpec((1, rows // tiles, lanes), lambda i, j: (i, j, 0))
    term = pl.BlockSpec((1, rows // tiles, lanes), lambda i, j: (first + i, j, 0))

    def half(k):
        first = k * tiles // 2
        last = tiles // 2 - 1
        return pl.BlockSpec(
            (1, rows // tiles, lanes), lambda i, j: (i, jnp.clip(j - first, 0, last), 0)
        )

    shapes = [jax.ShapeDtypeStruct((count, rows // 2, lanes), BF16)] * 2
    return pl.pallas_call(
        ring_sum_kernel,
        grid=(count, tiles),
        in_specs=[spec, term],
        out_specs=[half(0), half(1)] if halved else spec,
        out_shape=shapes if halved else jax.ShapeDtypeStruct(came.shape, BF16),
        compiler_params=params(60, "arbitrary", "arbitrary"),
        cost_estimate=SMALL,
        name="ring_sum",
    )(came, mine)


def late_load_kernel(plan_ref, pack_ref, main_ref, out_ref):
    rows = pack_ref.shape[1]
    out_ref[0:rows, :] = pack_ref[0]
    out_ref[rows:, :] = main_ref[...]


def late_load(plan, at, pack, main):
    rows, lanes = pack.shape[1:]
    total = rows + main.shape[0]
    return pl.pallas_call(
        late_load_kernel,
        grid_spec=pltpu.PrefetchScalarGridSpec(
            num_scalar_prefetch=1,
            grid=(1,),
            in_specs=[
                pl.BlockSpec((1, rows, lanes), lambda i, n: (n[at], 0, 0)),
                pl.BlockSpec(main.shape, lambda i, n: (0, 0)),
            ],
            out_specs=pl.BlockSpec((total, lanes), lambda i, n: (0, 0)),
        ),
        out_shape=jax.ShapeDtypeStruct((total, lanes), BF16),
        compiler_params=params(16, "arbitrary"),
        cost_estimate=SMALL,
        name="late_load",
    )(plan, pack, main)


def late_add_kernel(plan_ref, pack_ref, came_ref, *outs):
    total = (came_ref[...].astype(F32) + pack_ref[0].astype(F32)).astype(BF16)
    for out_ref in outs:
        out_ref[...] = total


def late_add(plan, at, pack, came, copied=False):
    rows, lanes = pack.shape[1:]
    spec = pl.BlockSpec((rows, lanes), lambda i, n: (0, 0))
    shape = jax.ShapeDtypeStruct(came.shape, BF16)
    return pl.pallas_call(
        late_add_kernel,
        grid_spec=pltpu.PrefetchScalarGridSpec(
            num_scalar_prefetch=1,
            grid=(1,),
            in_specs=[pl.BlockSpec((1, rows, lanes), lambda i, n: (n[at], 0, 0)), spec],
            out_specs=[spec] * 2 if copied else spec,
        ),
        out_shape=[shape, jax.ShapeDtypeStruct((rows, lanes), BF16)] if copied else shape,
        input_output_aliases={2: 0},
        compiler_params=params(16, "arbitrary"),
        cost_estimate=SMALL,
        name="late_add",
    )(plan, pack, came)


def late_join_kernel(col_ref, mine_ref, other_ref, gains_ref, main_ref, out_ref):
    units = 7
    out_ref[mine_ref.shape[0] :, :] = main_ref[...]
    share = mine_ref.shape[0] // LATE_BLOCKS
    to_rows, to_lanes = unit_slices(2 * units, share)
    blocks = gains_ref.shape[1] // LANES
    gains = [
        gains_ref[g : g + 1, b * LANES : (b + 1) * LANES] for g in range(2) for b in range(blocks)
    ]
    gains = jnp.concatenate(gains + [jnp.zeros((share - len(gains), LANES), F32)], axis=0)
    own = [mine_ref[unit_slices(b, share)] for b in range(units)]
    other = [other_ref[unit_slices(units + b, share)] for b in range(units)]
    for b in range(units):
        first, second = own[b], other[b]
        flipped = col_ref[0] != 0
        out_ref[unit_slices(b, share)] = jnp.where(flipped, second, first)
        out_ref[unit_slices(units + b, share)] = jnp.where(flipped, first, second)
    out_ref[to_rows, to_lanes] = gains.astype(BF16)


def late_join(col, mine, other, gains, main):
    rows, lanes = mine.shape
    total = rows + main.shape[0]

    def all_of(*shape):
        return pl.BlockSpec(shape, lambda i, c: (0, 0))

    return pl.pallas_call(
        late_join_kernel,
        grid_spec=pltpu.PrefetchScalarGridSpec(
            num_scalar_prefetch=1,
            grid=(1,),
            in_specs=[all_of(rows, lanes)] * 2 + [all_of(*gains.shape), all_of(*main.shape)],
            out_specs=all_of(total, lanes),
        ),
        out_shape=jax.ShapeDtypeStruct((total, lanes), BF16),
        compiler_params=params(16, "arbitrary"),
        cost_estimate=SMALL,
        name="late_join",
    )(col, mine, other, gains, main)


def unpack_late_kernel(first_step, steps, plan_ref, *refs):
    chunks = refs[0 : 2 * steps]
    sgate, sup, sdown, query, key, value, out, gains, all_ref, gain_ref = refs[2 * steps :]
    share, features = chunks[0].shape[0] // LATE_BLOCKS, all_ref.shape[2]
    for k in range(2):
        for step in range(steps):
            at = plan_ref[first_step + 2 * step + k]
            chunk = chunks[steps * k + step]
            to_rows = pl.ds(pl.multiple_of(at * share, share), share)
            for unit in range(14):
                lanes = slice(unit % 7 * LANES, (unit % 7 + 1) * LANES)
                all_ref[k, unit // 7, to_rows, lanes] = chunk[unit_slices(unit, share)]
            if k == 0:
                to_rows = pl.ds(pl.multiple_of(at * GAIN_ROWS, GAIN_ROWS), GAIN_ROWS)
                rows, lanes = unit_slices(14, share)
                gain_ref[to_rows, :] = chunk[rows.start : rows.start + GAIN_ROWS, lanes]
    total = jnp.zeros((GAIN_ROWS, LANES), F32)
    for step in range(steps):
        total = total + gain_ref[step * GAIN_ROWS : (step + 1) * GAIN_ROWS, :].astype(F32)
    blocks = features // LANES
    for row in range(2 * blocks):
        gains[row // blocks : row // blocks + 1, row % blocks * LANES : (row % blocks + 1) * LANES] = (
            total[row : row + 1, :]
        )
    flipped = plan_ref[plan_ref.shape[0] - 1] != 0
    for c in range(2):
        for b in range(14):
            lanes = slice(b % 7 * LANES, (b % 7 + 1) * LANES)
            first, second = all_ref[0, c, :, lanes], all_ref[1, c, :, lanes]
            if b >= 7:
                first, second = second, first
            block = jnp.where(flipped, second, first).astype(F32)
            if b < 6:
                at = slice((2 * c + b // 3) * LANES, (2 * c + b // 3 + 1) * LANES)
                if b % 3 < 2:
                    (sgate, sup)[b % 3][:, at] = block
                else:
                    for k in range(features // LANES):
                        here = slice(k * LANES, (k + 1) * LANES)
                        sdown[at, here] = block[here, :]
            elif b < 9:
                at = (GROUP_HEADS * c + b - 6) * LANES
                query[:, at : at + LANES] = block
            elif b < 11:
                (key, value)[b - 9][:, c * LANES : (c + 1) * LANES] = block
            else:
                at = (GROUP_HEADS * c + b - 11) * LANES
                out[at : at + LANES, :] = block.T


def unpack_late(plan, first_step, chunks, shapes):
    steps = len(chunks[0])
    features = shapes[0][0]
    share = features // steps
    chunk = pl.BlockSpec((LATE_BLOCKS * share, 3 * LANES), lambda i, n: (0, 0))
    return pl.pallas_call(
        functools.partial(unpack_late_kernel, first_step, steps),
        grid_spec=pltpu.PrefetchScalarGridSpec(
            num_scalar_prefetch=1,
            grid=(1,),
            in_specs=[chunk] * (2 * steps),
            out_specs=[pl.BlockSpec(shape, lambda i, n: (0, 0)) for shape in shapes],
            scratch_shapes=[
                pltpu.VMEM((2, 2, features, 7 * LANES), BF16),
                pltpu.VMEM((steps * GAIN_ROWS, LANES), BF16),
            ],
        ),
        out_shape=[jax.ShapeDtypeStruct(shape, F32) for shape in shapes],
        compiler_params=params(48, "arbitrary"),
        cost_estimate=SMALL,
        name="unpack_late",
    )(plan, *chunks[0], *chunks[1])


def plans(ring, each):
    size = len(ring)
    rows = []
    for member in range(size):
        place = ring.index(member)
        for col in range(2):
            chunks = []
            for step in range(2 * size - 1):
                for which in range(2):
                    sign = 1 if which == col else -1
                    chunks.append((place - sign * step) % size)
            experts = []
            for start in (0, size - 1):
                for step in range(start, start + size):
                    for k in range(each):
                        for which in range(2):
                            second = col if which == 0 else 1 - col
                            experts.append(2 * each * chunks[2 * step + which] + each * second + k)
            rows.append(experts + chunks + [col])
    return np.asarray(rows, np.int32)


def body(
    tokens_in,
    norm_gain_attn,
    w_query,
    w_key,
    w_value,
    w_out,
    norm_gain_ffn,
    w_gate,
    w_up,
    w_down,
    w_shared_gate,
    w_shared_up,
    w_shared_down,
    routes,
    gate_weights,
    seq_lengths,
    out_grad,
):
    row = lax.axis_index("row")
    col = lax.axis_index("col")
    dp = lax.axis_index("dp")
    dp_size = lax.axis_size("dp")
    local_rows, local_features = tokens_in.shape
    experts = w_gate.shape[0]
    group_width = GROUP_HEADS * DH
    col_ref = col.reshape(1)

    ring_size = RING
    ring = ring_of(ring_size)
    starts = range(0, dp_size, ring_size)
    rights = [
        (g + ring[k], g + ring[(k + 1) % ring_size]) for g in starts for k in range(ring_size)
    ]
    lefts = [(b, a) for a, b in rights]
    routes_of = [
        [(2 * a, 2 * b) for a, b in ways[0]] + [(2 * a + 1, 2 * b + 1) for a, b in ways[1]]
        for ways in ((rights, lefts), (lefts, rights))
    ]
    experts_each = experts // (2 * ring_size)
    plan = jnp.asarray(plans(ring, experts_each))
    plan = lax.dynamic_slice(
        plan, (2 * (dp % ring_size) + col, jnp.int32(0)), (1, plan.shape[1])
    ).reshape(-1)

    def send(values, which):
        return lax.ppermute(values, ("dp", "col"), routes_of[which])

    def chunk_at(step, which):
        return plan[2 * experts + 2 * step + which]

    def across_rings(values):
        if len(starts) == 1:
            return values
        peers = [[g + k for g in starts] for k in range(ring_size)]
        return lax.psum(values, "dp", axis_index_groups=peers)

    where = jnp.stack([row, seq_lengths[0], col])
    tokens_y = swap(tokens_in, "row")
    tokens_c = swap(tokens_in, "col")
    count = 4
    member = dp % count
    there, out_y = their_columns(
        jnp.stack([col, member]), w_query, w_key, w_value, w_out, count
    )
    gains = jnp.stack([norm_gain_attn, norm_gain_ffn])
    there = swap(there, "col")
    gains_c = swap(gains, "col")

    def project_half(own, other):
        return project(col_ref, own, other, gains, gains_c, w_query, w_key, w_value, there)

    near = project_half(tokens_in, tokens_c)
    gate_c = swap(w_gate, "col")
    out_y = swap(out_y, "row")
    tokens_y = after(tokens_y, near[2], out_y)
    tokens_yc = swap(tokens_y, "col")
    grad_y = swap(after(out_grad, tokens_y), "row")
    far = project_half(tokens_y, tokens_yc)
    shares = [out_y]
    for k in range(1, count):
        part = out_y if k < 3 else after(out_y, far[2])
        shares.append(lax.ppermute(part, "dp", [(m, m ^ k) for m in range(dp_size)]))
    where = after(where, grad_y, *shares)

    w_sgate, w_sup, w_sdown = w_shared_gate[None], w_shared_up[None], w_shared_down[None]
    up_c = swap(after(w_up, gate_c, tokens_yc), "col")

    attended = attend(where, near[2], far[2])
    attended_y = swap(attended, "row")
    attended_c = swap(attended, "col")
    out_c = swap(after(w_out, tokens_yc), "col")
    before = hidden_before(
        where,
        [tokens_in, tokens_c, tokens_y, tokens_yc],
        [attended, attended_c],
        w_out,
        out_c,
    )
    down_c = swap(after(w_down, tokens_yc), "col")
    attended_y = after(attended_y, before[0])
    out_y = join(member, *shares)
    out_yc = swap(out_y, "col")
    attended_yc = swap(attended_y, "col")
    grad_own = join(row, out_grad, grad_y)
    grad_other = swap(grad_own, "col")
    hidden, x_own, x_other, scale_ffn = hidden_after(
        where, before, [attended_y, attended_yc], out_y, out_yc, gains, gains_c
    )
    sgate_c, sup_c, sdown_c = (
        swap(after(w, attended_yc), "col") for w in (w_sgate, w_sup, w_sdown)
    )

    choices = jnp.arange(experts, dtype=jnp.int32)[:, None]
    dense = sum(
        jnp.where(routes[:, k][None, :] == choices, gate_weights[:, k][None, :], 0.0)
        for k in range(routes.shape[1])
    )
    gates = []
    for _ in range(3):
        gates.append(lax.reduce_precision(dense, 8, 7))
        dense = dense - gates[-1]
    gates = jnp.concatenate(gates, axis=0).astype(BF16)

    each = experts_each
    order = plan
    pairs_total = experts // 2
    routed = [w_gate, w_up, gate_c, up_c, w_down, down_c]
    shared = [w_sgate, w_sup, sgate_c, sup_c, w_sdown, sdown_c]

    def run(first, last, order, kept):
        return expert_grads(
            order,
            first,
            last,
            pairs_total,
            [x_own, x_other],
            [grad_own, grad_other],
            gates,
            routed,
            kept,
        )

    first = run(0, 1, order, ())
    kept = first[2:]
    sums = [first[0], first[1]]
    runs = {}
    mixed = {}
    normed = {}

    def work_experts(first, last):
        def work(order, ties):
            nonlocal kept
            result = run(first, last, order, tuple(kept))
            kept = result[2:]
            for at in range(first, last):
                runs[at] = (*result[0:2], at - first)
            return [kept[0]]

        return work

    def work_shared(order, ties):
        runs["shared"] = expert_grads(
            order, 0, 1, None, [x_own, x_other], [grad_own, grad_other], gates, shared, ()
        )
        return [runs["shared"][2]]

    def work_back(half):
        def work(order, ties):
            mixed[True, half] = mix(
                True,
                BF16 if half else F32,
                1 + half,
                order,
                kept[0],
                runs["shared"][2],
                routed[2 * half : 2 * half + 2],
                shared[2 * half : 2 * half + 2],
            )
            if half:
                normed["other"] = [swap(part, "col") for part in mixed[True, 1]]
                return list(mixed[True, 1])
            total, rounded, product = chip_sum(
                mixed[True, 0], normed["other"], hidden, gains
            )
            product_c = swap(product, "col")
            normed["sum"] = total
            normed["tie"] = rounded
            normed["came"] = swap(rounded, "row")
            normed["products"] = [product, product_c, swap(product, "row"), swap(product_c, "row")]
            return [mixed[True, 0]]

        return work

    def work_out(half):
        def work(order, ties):
            mixed[False, half] = mix(
                False,
                BF16 if half else F32,
                1,
                order,
                kept[1],
                runs["shared"][3],
                routed[4 + half : 5 + half],
                shared[4 + half : 5 + half],
            )
            return [mixed[False, half]]

        return work

    start = row * local_rows

    def my_rows(values):
        return lax.dynamic_slice_in_dim(values, start, local_rows, axis=0)

    def their_rows(values):
        return lax.dynamic_slice_in_dim(values, local_rows - start, local_rows, axis=0)

    def work_hidden(order, ties):
        normed["hidden"], *grad, normed["gain"] = norm_back(
            after(where, *ties),
            normed["sum"],
            normed["came"],
            hidden,
            scale_ffn,
            grad_own,
            gains,
            normed["products"],
        )
        normed["grad"] = grad
        normed["grad_c"] = [swap(part, "col") for part in grad]
        return grad

    def work_attend(order, ties):
        normed["qkv"] = attend_back(
            after(where, *ties), near[2], far[2], normed["grad"], normed["grad_c"], w_out, out_c
        )
        return [normed["qkv"]]

    def work_late(order, ties):
        normed["packs"] = late_grads(
            after(where, *ties),
            near[0:2],
            far[0:2],
            normed["qkv"],
            attended,
            normed["grad"],
            normed["grad_c"],
            runs["shared"][0:2],
        )
        return normed["packs"]

    def work_tie(order, ties):
        return [normed["tie"]]

    tasks = [work_experts(at, min(at + 2, pairs_total)) for at in range(1, pairs_total, 2)]
    tasks += [work_shared, work_back(1), work_back(0), None, None, work_tie]
    ends = [work_hidden, work_attend, work_late]
    tasks += [None] * (2 * ring_size - 2 - len(tasks) - len(ends)) + ends
    got = [None, None]
    got[0] = send(sums[0], 0)
    tasks.pop(0)(after(order, *sums), sums)
    got[1] = send(after(sums[1], kept[0]), 1)
    for s in range(1, ring_size):
        for k in range(2):
            last = sums
            task = tasks.pop(0) if tasks else None
            if task:
                last = task(after(order, *last), last)
            mine = runs[s]
            sums[k] = ring_sum(after(got[k], *last), mine[k], mine[2], s + 1 == ring_size)
            if s + 1 < ring_size:
                got[k] = send(sums[k], k)
            else:
                sums[k], got[k] = sums[k]
    crossed = [swap(across_rings(total), "col") for total in got]
    waves = [[across_rings(total)[0] for total in sums], [crossed[1][0], crossed[0][0]]]

    chunks_first = 2 * experts
    late_total = 2 * (ring_size - 1)

    def back_to_tokens(ties):
        hidden_grad = normed["hidden"]
        qkv_grad = after(normed["qkv"], *ties)
        here = jnp.concatenate(
            [halves(w, 1, col)[0] for w in (w_query, w_key, w_value)], axis=1
        )
        tokens_back = dot_nt(qkv_grad, here) + swap(
            dot_nt(qkv_grad, there).astype(BF16), "col"
        ).astype(F32)
        tokens_back = my_rows(tokens_back) + swap(
            their_rows(tokens_back).astype(BF16), "row"
        ).astype(F32)
        scale_attn = near[3]
        tokens_f32 = tokens_in.astype(F32)
        gain_attn_part = jnp.sum(tokens_back * tokens_f32 * scale_attn, axis=0)
        scaled = tokens_back * norm_gain_attn
        products = jnp.sum(scaled * tokens_f32, axis=1, keepdims=True)
        mean = (products + swap(products, "col")) / D
        tokens_grad = (
            my_rows(hidden_grad) + scale_attn * scaled - tokens_f32 * scale_attn**3 * mean
        ).astype(BF16)

        gain_parts = jnp.concatenate([gain_attn_part[None], normed["gain"]], axis=0)
        normed["gains"] = across_rings(gain_parts + swap(gain_parts, "row"))
        normed["tokens_grad"] = tokens_grad

    def block_rows(ties):
        ffn_sum = after(mixed[False, 0], *ties) + swap(mixed[False, 1], "col").astype(F32)
        ffn_rows = my_rows(ffn_sum) + swap(their_rows(ffn_sum).astype(BF16), "row").astype(F32)
        block_out = (my_rows(hidden) + ffn_rows).astype(BF16)
        normed["block_out"] = block_out

    shapes = [w_gate.shape, w_up.shape, w_down.shape]
    placed = ()
    late_out = [[], []]
    last, got = [], [None, None]
    moves = [(wave, step) for wave in range(2) for step in range(ring_size - 1)]
    for number, (wave, step) in enumerate(moves):
        current = [None, None]
        copies = [None, None]
        turn = number == ring_size - 1
        for k in range(2):
            at = chunks_first + 2 * number + k
            pack = normed["packs"][k]
            if number == 0:
                current[k] = late_load(plan, at, pack, after(waves[0][k], *last))
            elif number < ring_size - 1:
                current[k] = late_add(plan, at, pack, after(got[k], *last))
            elif turn:
                current[k], copies[k] = late_add(plan, at, pack, after(got[k], *last), True)
            else:
                current[k] = after(got[k], *last)
            last = [current[k]]
            if not turn:
                got[k] = send(current[k], k)
            if number == 0 and k == 0:
                last = work_out(0)(after(order, *last), ())
        if turn:
            placed = unpack(plan, experts + 2 * (ring_size - 1), 0, current, shapes, placed)
            others = [swap(across_rings(values), "col") for values in copies]
            for k in range(2):
                current[k] = late_join(
                    col_ref, after(copies[k], *last), others[1 - k], normed["gains"], waves[1][k]
                )
                got[k] = send(current[k], k)
                last = work_out(1)(after(order, current[k]), ()) if k == 0 else [current[k]]
        if number >= ring_size - 1:
            for k in range(2):
                late_out[k].append(current[k])
        placed = unpack(
            plan, experts + 2 * step, wave, [after(current[0], *last), current[1]], shapes, placed
        )
        last = placed[0:1]
        if number == 0:
            back_to_tokens(last)
        if number == 4:
            last = [*last, normed["gains"]]
        if number == ring_size + 1:
            block_rows(last)
    for k in range(2):
        late_out[k].append(after(got[k], *last))
        last = [late_out[k][-1]]
    placed = unpack(
        plan,
        experts + 2 * (ring_size - 1),
        1,
        [late_out[k][-1] for k in range(2)],
        shapes,
        placed,
    )
    gate_grad, up_grad, down_grad = placed
    shapes = [w.shape for w in (w_shared_gate, w_shared_up, w_shared_down)]
    shapes += [w.shape for w in (w_query, w_key, w_value, w_out)] + [gains.shape]
    finals = unpack_late(plan, chunks_first + late_total, late_out, shapes)
    shared_gate_grad, shared_up_grad, shared_down_grad = finals[0:3]
    query_grad, key_grad, value_grad, out_proj_grad, gain_grads = finals[3:8]


    return (
        normed["block_out"],
        normed["tokens_grad"],
        gain_grads[0],
        query_grad,
        key_grad,
        value_grad,
        out_proj_grad,
        gain_grads[1],
        gate_grad,
        up_grad,
        down_grad,
        shared_gate_grad,
        shared_up_grad,
        shared_down_grad,
    )


def solution(mesh):
    in_specs = (
        P(("dp", "row"), "col"),
        P("col"),
        P("col", "row"),
        P("col", "row"),
        P("col", "row"),
        P("row", "col"),
        P("col"),
        P(None, "col", "row"),
        P(None, "col", "row"),
        P(None, "row", "col"),
        P("col", "row"),
        P("col", "row"),
        P("row", "col"),
        P("dp", None),
        P("dp", None),
        P("dp"),
        P(("dp", "row"), "col"),
    )
    out_specs = (
        P(("dp", "row"), "col"),
        P(("dp", "row"), "col"),
        P("col"),
        P("col", "row"),
        P("col", "row"),
        P("col", "row"),
        P("row", "col"),
        P("col"),
        P(None, "col", "row"),
        P(None, "col", "row"),
        P(None, "row", "col"),
        P("col", "row"),
        P("col", "row"),
        P("row", "col"),
    )
    return jax.shard_map(body, mesh=mesh, in_specs=in_specs, out_specs=out_specs, check_vma=False)
```

```python
import functools

import jax
import jax.numpy as jnp
import numpy as np
from jax import lax
from jax.experimental import pallas as pl
from jax.experimental.pallas import tpu as pltpu
from jax.sharding import PartitionSpec as P

D = 1536
HQ = 12
HK = 4
DH = 128
GROUP_HEADS = HQ // HK
LANES = 128

EPSILON = 1e-05
F32 = jnp.float32
BF16 = jnp.bfloat16
MIB = 1024 * 1024
GAIN_ROWS = 16
RING = 8
LATE_BLOCKS = 5
SMALL = pl.CostEstimate(flops=0, bytes_accessed=0, transcendentals=0)


def params(mib, *semantics):
    return pltpu.CompilerParams(
        dimension_semantics=semantics or None, vmem_limit_bytes=mib * MIB
    )


def dot(left, right):
    return jnp.dot(left, right, preferred_element_type=F32)


def dot_nt(left, right):
    return lax.dot_general(left, right, (((1,), (1,)), ((), ())), preferred_element_type=F32)


def dot_tn(left, right):
    return lax.dot_general(left, right, (((0,), (0,)), ((), ())), preferred_element_type=F32)


def after(values, *others):
    return lax.optimization_barrier((values, *others))[0]


def swap(values, axis):
    return lax.ppermute(values, axis, [(0, 1), (1, 0)])


def halves(values, axis, mine):
    size = values.shape[axis] // 2
    low = lax.slice_in_dim(values, 0, size, axis=axis)
    high = lax.slice_in_dim(values, size, 2 * size, axis=axis)
    return jnp.where(mine == 0, low, high), jnp.where(mine == 0, high, low)


def in_order(own, other, mine, axis):
    return jnp.concatenate(
        [jnp.where(mine == 0, own, other), jnp.where(mine == 0, other, own)], axis=axis
    )


def gather_rows(place_ref, own_ref, other_ref, all_ref):
    row = place_ref[0]
    rows = own_ref.shape[0]
    all_ref[pl.ds(pl.multiple_of(row * rows, rows), rows), :] = own_ref[...]
    all_ref[pl.ds(pl.multiple_of((1 - row) * rows, rows), rows), :] = other_ref[...]


def head_rows(ref, first, block):
    return jnp.concatenate(
        [ref[first : first + block, h * DH : (h + 1) * DH] for h in range(GROUP_HEADS)], axis=0
    )


def key_probs(query, key, first, length):
    block, keys = query.shape[0] // GROUP_HEADS, key.shape[0]
    scores = dot_nt(query, key) * DH ** (-0.5)
    shape = (block, keys)
    query_at = lax.broadcasted_iota(jnp.int32, shape, 0) + first
    key_at = lax.broadcasted_iota(jnp.int32, shape, 1)
    allowed = (key_at <= query_at) & (key_at < length)
    allowed = jnp.concatenate([allowed] * GROUP_HEADS, axis=0)
    scores = jnp.where(allowed, scores, -1e30)
    weights = jnp.exp(scores - jnp.max(scores, axis=1, keepdims=True))
    return weights * (1.0 / jnp.sum(weights, axis=1, keepdims=True))


def attend_kernel(place_ref, own_ref, other_ref, out_ref, all_ref):
    gather_rows(place_ref, own_ref, other_ref, all_ref)
    rows = own_ref.shape[0]
    block = 256
    width = GROUP_HEADS * DH
    for at in range(2 * rows // block):
        first, keys = at * block, (at + 1) * block
        query = head_rows(all_ref, first, block)
        key = all_ref[0:keys, width : width + DH]
        value = all_ref[0:keys, width + DH : width + 2 * DH]
        probs = key_probs(query, key, first, place_ref[1])
        result = dot(probs.astype(BF16), value).astype(BF16)
        for h in range(GROUP_HEADS):
            out_ref[first : first + block, h * DH : (h + 1) * DH] = result[
                h * block : (h + 1) * block
            ]


def attend(place, own, other):
    rows, width = own.shape
    spec = pl.BlockSpec(memory_space=pltpu.VMEM)
    return pl.pallas_call(
        attend_kernel,
        out_shape=jax.ShapeDtypeStruct((2 * rows, GROUP_HEADS * DH), BF16),
        in_specs=[pl.BlockSpec(memory_space=pltpu.SMEM), spec, spec],
        out_specs=spec,
        scratch_shapes=[pltpu.VMEM((2 * rows, width), BF16)],
        compiler_params=params(32),
        cost_estimate=SMALL,
        name="attend",
    )(place, own, other)


def attend_back_kernel(
    place_ref, own_ref, other_ref, *refs
):
    grad_refs, grad_c_refs = refs[0:2], refs[2:4]
    out_ref, out_c_ref, result_ref, all_ref, total_ref = refs[4:9]
    gather_rows(place_ref, own_ref, other_ref, all_ref)
    rows = own_ref.shape[0]
    block = 256
    width = GROUP_HEADS * DH
    group = pl.ds(pl.multiple_of(place_ref[2] * width, width), width)
    blocks = 2 * rows // block
    for at in reversed(range(blocks)):
        first, keys = at * block, (at + 1) * block
        query = head_rows(all_ref, first, block)
        key = all_ref[0:keys, width : width + DH]
        value = all_ref[0:keys, width + DH : width + 2 * DH]
        probs = key_probs(query, key, first, place_ref[1])
        half, in_half = divmod(first, rows)
        piece = slice(in_half, in_half + block)
        grad = dot_nt(grad_refs[half][piece, :], out_ref[group, :])
        grad = (grad + dot_nt(grad_c_refs[half][piece, :], out_c_ref[group, :])).astype(BF16)
        grad = jnp.concatenate(
            [grad[:, h * DH : (h + 1) * DH] for h in range(GROUP_HEADS)], axis=0
        )
        probs_grad = dot_nt(grad, value)
        carried = jnp.sum(probs * probs_grad, axis=1, keepdims=True)
        score_grad = (probs * (probs_grad - carried)).astype(BF16)
        query_back = (dot(score_grad, key) * DH ** (-0.5)).astype(BF16)
        for h in range(GROUP_HEADS):
            result_ref[first:keys, h * DH : (h + 1) * DH] = query_back[
                h * block : (h + 1) * block
            ]
        key_back = dot_tn(score_grad, query)
        value_back = dot_tn(probs.astype(BF16), grad)
        if at == blocks - 1:
            total_ref[:, 0:DH] = key_back
            total_ref[:, DH:] = value_back
        else:
            total_ref[0:keys, 0:DH] += key_back
            total_ref[0:keys, DH:] += value_back
    result_ref[:, width : width + DH] = (total_ref[:, 0:DH] * DH ** (-0.5)).astype(BF16)
    result_ref[:, width + DH :] = total_ref[:, DH:].astype(BF16)


def attend_back(place, own, other, grad, grad_c, w_out, out_c):
    rows, width = own.shape
    spec = pl.BlockSpec(memory_space=pltpu.VMEM)
    return pl.pallas_call(
        attend_back_kernel,
        out_shape=jax.ShapeDtypeStruct((2 * rows, width), BF16),
        in_specs=[pl.BlockSpec(memory_space=pltpu.SMEM)] + [spec] * 8,
        out_specs=spec,
        scratch_shapes=[
            pltpu.VMEM((2 * rows, width), BF16),
            pltpu.VMEM((2 * rows, 2 * DH), F32),
        ],
        compiler_params=params(60),
        cost_estimate=SMALL,
        name="attend_back",
    )(place, own, other, *grad, *grad_c, w_out, out_c)


def unit_slices(unit, share):
    row, lane = divmod(unit, 3)
    return slice(row * share, (row + 1) * share), slice(lane * LANES, (lane + 1) * LANES)


def late_kernel(place_ref, *refs):
    near, near_c, far, far_c, qkv_ref, attended_ref = refs[0:6]
    grad_refs, grad_c_refs, shared, outs = refs[6:8], refs[8:10], refs[10:12], refs[12:14]
    rows, features = near.shape
    own_rows = pl.ds(pl.multiple_of(place_ref[0] * rows, rows), rows)
    far_rows = pl.ds(pl.multiple_of((1 - place_ref[0]) * rows, rows), rows)
    split = 7 * LANES

    chunks = outs[0].shape[0]
    share = features // chunks

    def store(h, at, values):
        values = values.astype(BF16)
        for b in range(values.shape[1] // LANES):
            part, unit = divmod(at // LANES + b, split // LANES)
            to_rows, to_lanes = unit_slices(h * (split // LANES) + unit, share)

            def write(out_ref, b=b, to_rows=to_rows, to_lanes=to_lanes):
                for chunk in range(chunks):
                    out_ref[chunk, to_rows, to_lanes] = values[
                        chunk * share : (chunk + 1) * share, b * LANES : (b + 1) * LANES
                    ]

            pl.when(place_ref[2] == 0)(lambda part=part, write=write: write(outs[part]))
            pl.when(place_ref[2] != 0)(lambda part=part, write=write: write(outs[1 - part]))

    for out_ref in outs:
        to_rows, to_lanes = unit_slices(2 * (split // LANES), share)
        for chunk in range(chunks):
            out_ref[chunk, to_rows, to_lanes] = jnp.zeros((share, LANES), BF16)

    for h, (x, y, grad) in enumerate(((near, far, grad_refs), (near_c, far_c, grad_c_refs))):
        for k in range(2):
            store(h, 3 * LANES * k, shared[k][0, h * features : (h + 1) * features, :])
        project = dot_tn(x[...], qkv_ref[own_rows, :]) + dot_tn(y[...], qkv_ref[far_rows, :])
        store(h, 6 * LANES, project)
        out = [dot_tn(grad[k][...], attended_ref[k * rows : (k + 1) * rows, :]) for k in range(2)]
        store(h, 11 * LANES, out[0] + out[1])


def late_grads(place, near, far, qkv_grad, attended, grad, grad_c, shared):
    features = near[0].shape[1]
    rows = LATE_BLOCKS * (features // RING)
    spec = pl.BlockSpec(memory_space=pltpu.VMEM)
    return pl.pallas_call(
        late_kernel,
        out_shape=[jax.ShapeDtypeStruct((RING, rows, 3 * LANES), BF16)] * 2,
        in_specs=[pl.BlockSpec(memory_space=pltpu.SMEM)] + [spec] * 12,
        out_specs=[spec] * 2,
        compiler_params=params(60),
        cost_estimate=SMALL,
        name="late_grads",
    )(place, *near, *far, qkv_grad, attended, *grad, *grad_c, *shared)


def columns_kernel(
    place_ref, query_ref, key_ref, value_ref, w_out_ref, out_ref, share_ref
):
    share_ref[...] = w_out_ref[...]
    width = GROUP_HEADS * DH
    out_ref[:, 0:width] = query_ref[...]
    out_ref[:, width : width + DH] = key_ref[...]
    out_ref[:, width + DH :] = value_ref[...]


def their_columns(place, w_query, w_key, w_value, w_out, shares):
    rows = w_query.shape[0]
    width = GROUP_HEADS * DH + 2 * DH

    def theirs(width):
        return pl.BlockSpec((rows, width), lambda i, c: (0, 1 - c[0]))

    return pl.pallas_call(
        columns_kernel,
        grid_spec=pltpu.PrefetchScalarGridSpec(
            num_scalar_prefetch=1,
            grid=(1,),
            in_specs=[theirs(GROUP_HEADS * DH), theirs(DH), theirs(DH)]
            + [pl.BlockSpec((rows // shares, rows), lambda i, c: (c[1], 0))],
            out_specs=[
                pl.BlockSpec((rows, width), lambda i, c: (0, 0)),
                pl.BlockSpec((rows // shares, rows), lambda i, c: (0, 0)),
            ],
        ),
        out_shape=[
            jax.ShapeDtypeStruct((rows, width), BF16),
            jax.ShapeDtypeStruct((rows // shares, rows), BF16),
        ],
        compiler_params=params(60, "arbitrary"),
        cost_estimate=SMALL,
        name="their_columns",
    )(place, w_query, w_key, w_value, w_out)


def join_kernel(mine_ref, *refs):
    *parts, out_ref = refs
    rows = parts[0].shape[0]
    for k, part in enumerate(parts):
        at = jnp.bitwise_xor(mine_ref[0], k)
        out_ref[pl.ds(pl.multiple_of(at * rows, rows), rows), :] = part[...]


def join(mine, *parts):
    rows, width = parts[0].shape
    spec = pl.BlockSpec(memory_space=pltpu.VMEM)
    return pl.pallas_call(
        join_kernel,
        out_shape=jax.ShapeDtypeStruct((len(parts) * rows, width), parts[0].dtype),
        in_specs=[pl.BlockSpec(memory_space=pltpu.SMEM)] + [spec] * len(parts),
        out_specs=spec,
        compiler_params=params(16),
        cost_estimate=SMALL,
        name="join",
    )(mine.reshape(1), *parts)


def project_kernel(col_ref, own_ref, other_ref, gains_ref, gains_c_ref, query_ref, key_ref, value_ref, there_ref, x_own_ref, x_other_ref, qkv_ref, scale_ref):
    own = own_ref[...].astype(F32)
    other = other_ref[...].astype(F32)
    total = jnp.sum(own * own, axis=1, keepdims=True)
    total = total + jnp.sum(other * other, axis=1, keepdims=True)
    scale = lax.rsqrt(total / D + EPSILON)
    own = (own * scale * gains_ref[0:1, :]).astype(BF16)
    other = (other * scale * gains_c_ref[0:1, :]).astype(BF16)
    x_own_ref[...] = own
    x_other_ref[...] = other
    scale_ref[...] = scale
    here = jnp.concatenate([query_ref[...], key_ref[...], value_ref[...]], axis=1)
    qkv_ref[...] = (dot(own, here) + dot(other, there_ref[...])).astype(BF16)


def project(col, own, other, gains, gains_c, w_query, w_key, w_value, there):
    rows, features = own.shape
    width = there.shape[1]
    group = GROUP_HEADS * DH
    tile = rows // 2

    def whole(*shape):
        return pl.BlockSpec(shape, lambda i, c: (0,) * len(shape))

    def mine(width):
        return pl.BlockSpec((features, width), lambda i, c: (0, c[0]))

    def rowwise(width):
        return pl.BlockSpec((tile, width), lambda i, c: (i, 0))

    return pl.pallas_call(
        project_kernel,
        grid_spec=pltpu.PrefetchScalarGridSpec(
            num_scalar_prefetch=1,
            grid=(rows // tile,),
            in_specs=[
                rowwise(features),
                rowwise(features),
                whole(2, features),
                whole(2, features),
                mine(group),
                mine(DH),
                mine(DH),
                whole(features, width),
            ],
            out_specs=[rowwise(features), rowwise(features), rowwise(width), rowwise(1)],
        ),
        out_shape=[
            jax.ShapeDtypeStruct((rows, features), BF16),
            jax.ShapeDtypeStruct((rows, features), BF16),
            jax.ShapeDtypeStruct((rows, width), BF16),
            jax.ShapeDtypeStruct((rows, 1), F32),
        ],
        compiler_params=params(60, "arbitrary"),
        cost_estimate=SMALL,
        name="project",
    )(col, own, other, gains, gains_c, w_query, w_key, w_value, there)


def head_pair(col_ref, own, other):
    first, second = own[...], other[...]
    flipped = col_ref != 0
    return jnp.concatenate(
        [jnp.where(flipped, second, first), jnp.where(flipped, first, second)], axis=1
    )


def before_kernel(tiles, place_ref, *refs):
    near, near_c, far, far_c, attended, attended_c, here, there, own_ref, other_ref = refs
    is_near = (pl.program_id(0) >= tiles // 2).astype(jnp.int32) == place_ref[0]
    heads = head_pair(place_ref[2], attended, attended_c)
    own = jnp.where(is_near, near[...], far[...]).astype(F32)
    other = jnp.where(is_near, near_c[...], far_c[...]).astype(F32)
    own_ref[...] = own + dot(heads, here[...])
    other_ref[...] = other + dot(heads, there[...])


def after_kernel(place_ref, *refs):
    own_ref, other_ref, attended, attended_c, here, there, gains_ref, gains_c_ref = refs[0:8]
    hidden_ref, x_own_ref, x_other_ref, scale_ref = refs[8:12]
    heads = head_pair(place_ref[2], attended, attended_c)
    own = own_ref[...] + dot(heads, here[...])
    other = other_ref[...] + dot(heads, there[...])
    total = jnp.sum(own * own, axis=1, keepdims=True)
    total = total + jnp.sum(other * other, axis=1, keepdims=True)
    scale = lax.rsqrt(total / D + EPSILON)
    hidden_ref[...] = own
    scale_ref[...] = scale
    x_own_ref[...] = (own * scale * gains_ref[1:2, :]).astype(BF16)
    x_other_ref[...] = (other * scale * gains_c_ref[1:2, :]).astype(BF16)


TOKEN_TILE = 256


def rowwise(width):
    return pl.BlockSpec((TOKEN_TILE, width), lambda i, p: (i, 0))


def whole(*shape):
    return pl.BlockSpec(shape, lambda i, p: (0,) * len(shape))


def hidden_before(place, tokens, attended, here, there):
    half, features = tokens[0].shape
    rows, heads = attended[0].shape
    tiles = rows // TOKEN_TILE
    per_half = half // TOKEN_TILE
    halfwise = pl.BlockSpec((TOKEN_TILE, features), lambda i, p: (i % per_half, 0))
    return pl.pallas_call(
        functools.partial(before_kernel, tiles),
        grid_spec=pltpu.PrefetchScalarGridSpec(
            num_scalar_prefetch=1,
            grid=(tiles,),
            in_specs=[halfwise] * 4 + [rowwise(heads)] * 2 + [whole(2 * heads, features)] * 2,
            out_specs=[rowwise(features)] * 2,
        ),
        out_shape=[jax.ShapeDtypeStruct((rows, features), F32)] * 2,
        compiler_params=params(56, "arbitrary"),
        cost_estimate=pl.CostEstimate(
            flops=8 * rows * features * heads,
            bytes_accessed=16 * rows * features,
            transcendentals=0,
        ),
        name="hidden_before",
    )(place, *tokens, *attended, here, there)


def hidden_after(place, before, attended, here, there, gains, gains_c):
    rows, features = before[0].shape
    heads = attended[0].shape[1]
    return pl.pallas_call(
        after_kernel,
        grid_spec=pltpu.PrefetchScalarGridSpec(
            num_scalar_prefetch=1,
            grid=(rows // TOKEN_TILE,),
            in_specs=[rowwise(features)] * 2
            + [rowwise(heads)] * 2
            + [whole(2 * heads, features)] * 2
            + [whole(2, features)] * 2,
            out_specs=[rowwise(features)] * 3 + [rowwise(1)],
        ),
        out_shape=[
            jax.ShapeDtypeStruct((rows, features), F32),
            jax.ShapeDtypeStruct((rows, features), BF16),
            jax.ShapeDtypeStruct((rows, features), BF16),
            jax.ShapeDtypeStruct((rows, 1), F32),
        ],
        compiler_params=params(56, "arbitrary"),
        cost_estimate=SMALL,
        name="hidden_after",
    )(place, *before, *attended, here, there, gains, gains_c)


def expert_kernel(shared, aliased, first, order_ref, *refs):
    x_own, x_other, o_own, o_other, gates_ref = refs[0:5]
    weights = refs[5:17]
    grads = refs[17 + aliased : 19 + aliased]
    pair_ref, inner_ref = refs[19 + aliased : 21 + aliased]
    step = pl.program_id(0) + first
    rows, features = x_own.shape
    tile = 512
    up_own = jnp.concatenate([weights[k][0] for k in (0, 1, 6, 7)], axis=1)
    up_other = jnp.concatenate([weights[k][0] for k in (2, 3, 8, 9)], axis=1)
    down_own = jnp.concatenate([weights[k][0] for k in (4, 10)], axis=0)
    down_other = jnp.concatenate([weights[k][0] for k in (5, 11)], axis=0)

    def token_tile(t, carry):
        at = pl.ds(pl.multiple_of(t * tile, tile), tile)
        pre = dot(x_own[at, :], up_own) + dot(x_other[at, :], up_other)
        back = dot_nt(o_own[at, :], down_own) + dot_nt(o_other[at, :], down_other)
        for k in range(2):
            pre_gate = pre[:, 2 * k * LANES : (2 * k + 1) * LANES]
            pre_up = pre[:, (2 * k + 1) * LANES : (2 * k + 2) * LANES]
            inner_grad = back[:, k * LANES : (k + 1) * LANES]
            sigmoid = 1.0 / (1.0 + jnp.exp(-pre_gate))
            silu = pre_gate * sigmoid
            inner = silu * pre_up
            if not shared:
                shape = (gates_ref.shape[0], LANES)
                expert = lax.broadcasted_iota(jnp.int32, shape, 0) % (gates_ref.shape[0] // 3)
                chosen = (expert == order_ref[2 * step + k]).astype(F32).astype(BF16)
                gate = dot_tn(gates_ref[:, at], chosen)
                inner = gate * inner
                inner_grad = gate * inner_grad
            gate_grad = inner_grad * pre_up * (sigmoid * (1.0 + pre_gate * (1.0 - sigmoid)))
            inner_ref[0, at, k * LANES : (k + 1) * LANES] = inner.astype(BF16)
            pair_ref[0, at, 2 * k * LANES : (2 * k + 1) * LANES] = gate_grad.astype(BF16)
            pair_ref[0, at, (2 * k + 1) * LANES : (2 * k + 2) * LANES] = (
                inner_grad * silu
            ).astype(BF16)
        return carry

    lax.fori_loop(0, rows // tile, token_tile, 0)
    pairs = pair_ref[0]
    for h, x in enumerate((x_own, x_other)):
        wide = dot_tn(x[...], pairs).astype(BF16)
        for k in range(2):
            grads[k][0, h * features : (h + 1) * features, 0 : 2 * LANES] = wide[
                :, 2 * k * LANES : (2 * k + 2) * LANES
            ]
    inner = inner_ref[0]
    tile = 256
    for h, o in enumerate((o_own, o_other)):
        for j in range(features // tile):
            low = dot_tn(inner, o[:, j * tile : (j + 1) * tile]).astype(BF16)
            for k in range(2):
                for b in range(tile // LANES):
                    at = h * features + j * tile + b * LANES
                    grads[k][0, at : at + LANES, 2 * LANES :] = low[
                        k * LANES : (k + 1) * LANES, b * LANES : (b + 1) * LANES
                    ]


def expert_specs(features, place, wide, low):
    specs = []
    if wide:
        block = pl.BlockSpec((1, features, LANES), lambda i, o: (place(i, o)[0], 0, place(i, o)[1]))
        specs += [block] * 4
    if low:
        block = pl.BlockSpec((1, LANES, features), lambda i, o: (*place(i, o), 0))
        specs += [block] * 2
    return specs


def expert_grads(order, first, last, total, x, o, gates, weights, kept):
    shared = total is None
    steps = last - first
    rows, features = x[0].shape
    aliased = len(kept)

    def fixed(*shape):
        return pl.BlockSpec(shape, lambda i, o: (0,) * len(shape))

    def stepped(*shape):
        return pl.BlockSpec((1, *shape), lambda i, o: (i, 0, 0))

    def placed(*shape):
        return pl.BlockSpec((1, *shape), lambda i, o: (i + first, 0, 0))

    specs = []
    for k in range(2):
        if shared:

            def picked(i, o, k=k):
                return 0, 2 * o[o.shape[0] - 1] + k

        else:

            def picked(i, o, k=k):
                return o[2 * (i + first) + k], o[o.shape[0] - 1]

        specs += expert_specs(features, picked, True, True)
    total = steps if shared else total
    return pl.pallas_call(
        functools.partial(expert_kernel, shared, aliased, first),
        grid_spec=pltpu.PrefetchScalarGridSpec(
            num_scalar_prefetch=1,
            grid=(steps,),
            in_specs=[fixed(rows, features)] * 4
            + [fixed(*gates.shape)]
            + specs
            + [pl.BlockSpec(memory_space=pl.ANY)] * aliased,
            out_specs=[stepped(2 * features, 3 * LANES)] * 2
            + [placed(rows, 4 * LANES), placed(rows, 2 * LANES)],
        ),
        out_shape=[jax.ShapeDtypeStruct((steps, 2 * features, 3 * LANES), BF16)] * 2
        + [
            jax.ShapeDtypeStruct((total, rows, 4 * LANES), BF16),
            jax.ShapeDtypeStruct((total, rows, 2 * LANES), BF16),
        ],
        input_output_aliases={18 + k: 2 + k for k in range(aliased)},
        compiler_params=params(40, "arbitrary"),
        cost_estimate=SMALL,
        name="expert_grads",
    )(order, *x, *o, gates, *weights, *weights, *kept)


def mix_kernel(back, group, pieces, order_ref, *refs):
    acts_ref, shared_ref = refs[0:2]
    each = 2 if back else 1
    count = 2 * group * each
    weights = refs[2 : 2 + count]
    shared = refs[2 + count : 2 + count + 2 * each]
    *outs, total_ref = refs[2 + count + 2 * each :]
    step = pl.program_id(0)
    rows = total_ref.shape[0]
    tile = 512
    times = dot_nt if back else dot
    along = 1 if back else 0

    @pl.when(step == 0)
    def _():
        both = jnp.concatenate([w[0] for w in shared], axis=along)
        for t in range(rows // tile):
            at = slice(t * tile, (t + 1) * tile)
            total_ref[at, :] = times(shared_ref[0, at, :], both)

    both = jnp.concatenate([w[0] for w in weights], axis=along)
    for t in range(rows // tile):
        at = slice(t * tile, (t + 1) * tile)
        acts = jnp.concatenate([acts_ref[g, at, :] for g in range(group)], axis=1)
        total_ref[at, :] += times(acts, both)

    @pl.when(step == pl.num_programs(0) - 1)
    def _():
        part = rows // pieces
        for k, out_ref in enumerate(outs):
            out_ref[...] = total_ref[k * part : (k + 1) * part, :].astype(out_ref.dtype)


def mix(back, dtype, pieces, order, acts, shared_acts, weights, shared_weights):
    pairs, rows, width = acts.shape
    features = weights[0].shape[1] if back else weights[0].shape[2]
    group = 4 if pairs % 4 == 0 else 1

    def spec(place):
        if back:
            return pl.BlockSpec((1, features, LANES), lambda i, o: (place(i, o)[0], 0, place(i, o)[1]))
        return pl.BlockSpec((1, LANES, features), lambda i, o: (*place(i, o), 0))

    def routed(k):
        return spec(lambda i, o: (o[2 * group * i + k], o[o.shape[0] - 1]))

    def common(k):
        return spec(lambda i, o: (0, 2 * o[o.shape[0] - 1] + k))

    outs = pl.pallas_call(
        functools.partial(mix_kernel, back, group, pieces),
        grid_spec=pltpu.PrefetchScalarGridSpec(
            num_scalar_prefetch=1,
            grid=(pairs // group,),
            in_specs=[
                pl.BlockSpec((group, rows, width), lambda i, o: (i, 0, 0)),
                pl.BlockSpec((1, rows, width), lambda i, o: (0, 0, 0)),
            ]
            + [routed(k) for k in range(2 * group) for _ in weights]
            + [common(k) for k in range(2) for _ in weights],
            out_specs=[pl.BlockSpec((rows // pieces, features), lambda i, o: (0, 0))] * pieces,
            scratch_shapes=[pltpu.VMEM((rows, features), F32)],
        ),
        out_shape=[jax.ShapeDtypeStruct((rows // pieces, features), dtype)] * pieces,
        compiler_params=params(48, "arbitrary"),
        cost_estimate=SMALL,
        name="mix",
    )(order, acts, shared_acts, *weights * (2 * group), *shared_weights * 2)
    return outs if pieces > 1 else outs[0]


def chip_sum_kernel(tiles, own_ref, first_ref, second_ref, hidden_ref, gains_ref, total_ref, rounded_ref, product_ref):
    is_first = pl.program_id(0) < tiles // 2
    other = jnp.where(is_first, first_ref[...], second_ref[...])
    total = own_ref[...] + other.astype(F32)
    total_ref[...] = total
    rounded_ref[...] = total.astype(BF16)
    product_ref[...] = lax.dot_general(
        jnp.ones((8, total.shape[1]), F32),
        total * gains_ref[1:2, :] * hidden_ref[...],
        (((1,), (1,)), ((), ())),
        precision=lax.Precision.HIGHEST,
        preferred_element_type=F32,
    )


def chip_sum(own, other, hidden, gains):
    rows, features = own.shape
    spec = pl.BlockSpec((TOKEN_TILE, features), lambda i: (i, 0))
    tiles = rows // TOKEN_TILE
    piece = pl.BlockSpec((TOKEN_TILE, features), lambda i: (i % (tiles // 2), 0))
    return pl.pallas_call(
        functools.partial(chip_sum_kernel, tiles),
        grid=(tiles,),
        out_shape=[
            jax.ShapeDtypeStruct((rows, features), F32),
            jax.ShapeDtypeStruct((rows, features), BF16),
            jax.ShapeDtypeStruct((8, rows), F32),
        ],
        in_specs=[spec, piece, piece, spec, pl.BlockSpec(gains.shape, lambda i: (0, 0))],
        out_specs=[spec, spec, pl.BlockSpec((8, TOKEN_TILE), lambda i: (0, i))],
        compiler_params=params(24, "arbitrary"),
        cost_estimate=SMALL,
        name="chip_sum",
    )(own, *other, hidden, gains)


def norm_back_kernel(tiles, place_ref, *refs):
    sum_ref, came_ref, hidden_ref, scale_ref, out_grad_ref, gains_ref = refs[0:6]
    products = refs[6:10]
    hidden_grad_ref, first_ref, second_ref, gain_ref = refs[10:14]
    step = pl.program_id(0)
    part = (step >= tiles // 2).astype(jnp.int32)
    grad = sum_ref[...] + came_ref[...].astype(F32)
    hidden = hidden_ref[...]
    scale = scale_ref[...]
    total = (products[0][...] + products[1][...]) + (products[2][...] + products[3][...])
    mean = lax.dot_general(
        total,
        jnp.full((8, LANES), 1.0 / (8 * D), F32),
        (((0,), (0,)), ((), ())),
        precision=lax.Precision.HIGHEST,
        preferred_element_type=F32,
    )[:, 0:1]
    result = out_grad_ref[...].astype(F32) + scale * (grad * gains_ref[1:2, :])
    result = result - hidden * (scale * scale * scale * mean)
    hidden_grad_ref[...] = result
    for k, rounded_ref in enumerate((first_ref, second_ref)):

        @pl.when(part == k)
        def _(rounded_ref=rounded_ref):
            rounded_ref[...] = result.astype(BF16)

    @pl.when(step == 0)
    def _():
        gain_ref[...] = jnp.zeros_like(gain_ref)

    @pl.when(part == place_ref[0])
    def _():
        gain_ref[...] += jnp.sum(grad * hidden * scale, axis=0, keepdims=True)


def norm_back(place, sums, came, hidden, scale, out_grad, gains, products):
    rows, features = hidden.shape
    tiles = rows // TOKEN_TILE
    lanes = pl.BlockSpec((8, TOKEN_TILE), lambda i, p: (0, i))

    def piece(k):
        last = tiles // 2 - 1
        return pl.BlockSpec(
            (TOKEN_TILE, features), lambda i, p: (jnp.clip(i - k * tiles // 2, 0, last), 0)
        )

    return pl.pallas_call(
        functools.partial(norm_back_kernel, tiles),
        grid_spec=pltpu.PrefetchScalarGridSpec(
            num_scalar_prefetch=1,
            grid=(tiles,),
            in_specs=[rowwise(features)] * 3
            + [rowwise(1), rowwise(features), whole(2, features)]
            + [lanes] * 4,
            out_specs=[rowwise(features), piece(0), piece(1), whole(1, features)],
        ),
        out_shape=[
            jax.ShapeDtypeStruct((rows, features), F32),
            jax.ShapeDtypeStruct((rows // 2, features), BF16),
            jax.ShapeDtypeStruct((rows // 2, features), BF16),
            jax.ShapeDtypeStruct((1, features), F32),
        ],
        compiler_params=params(48, "arbitrary"),
        cost_estimate=SMALL,
        name="norm_back",
    )(place, sums, came, hidden, scale, out_grad, gains, *products)


def ring_of(size):
    return list(range(0, size, 2)) + list(range(1, size, 2))[::-1]


def unpack_kernel(aliased, plan_ref, *refs):
    chunks = refs[0:2]
    gate_ref, up_ref, down_ref = refs[2 + aliased : 5 + aliased]
    rows = gate_ref.shape[1]

    def write(chunk_ref):
        first = chunk_ref.shape[0] - rows
        gate_ref[0] = chunk_ref[first:, 0:LANES].astype(F32)
        up_ref[0] = chunk_ref[first:, LANES : 2 * LANES].astype(F32)
        for b in range(rows // LANES):
            at = slice(first + b * LANES, first + (b + 1) * LANES)
            down_ref[0, :, b * LANES : (b + 1) * LANES] = chunk_ref[at, 2 * LANES :].astype(F32)

    for k in range(2):
        pl.when(pl.program_id(0) == k)(lambda k=k: write(chunks[k]))


def unpack(plan, first, wave, chunks, shapes, outs):
    rows = shapes[0][1]

    def place(d, n):
        block = n[n.shape[0] - 1]
        return n[first + d], 1 - block if wave else block

    def wide(d, n):
        expert, block = place(d, n)
        return (expert, 0, block)

    def low(d, n):
        expert, block = place(d, n)
        return (expert, block, 0)

    aliased = len(outs)
    return pl.pallas_call(
        functools.partial(unpack_kernel, aliased),
        grid_spec=pltpu.PrefetchScalarGridSpec(
            num_scalar_prefetch=1,
            grid=(2,),
            in_specs=[pl.BlockSpec(chunk.shape, lambda d, n: (0, 0)) for chunk in chunks]
            + [pl.BlockSpec(memory_space=pl.ANY)] * aliased,
            out_specs=[
                pl.BlockSpec((1, rows, LANES), wide),
                pl.BlockSpec((1, rows, LANES), wide),
                pl.BlockSpec((1, LANES, rows), low),
            ],
        ),
        out_shape=[jax.ShapeDtypeStruct(shape, F32) for shape in shapes],
        input_output_aliases={3 + k: k for k in range(aliased)},
        compiler_params=params(16, "arbitrary"),
        cost_estimate=SMALL,
        name="unpack",
    )(plan, *chunks, *outs)


def ring_sum_kernel(came_ref, mine_ref, *outs):
    total = (came_ref[...].astype(F32) + mine_ref[...].astype(F32)).astype(BF16)
    if len(outs) == 1:
        outs[0][...] = total
    else:
        half = pl.program_id(1) // (pl.num_programs(1) // 2)
        for k, out_ref in enumerate(outs):

            @pl.when(half == k)
            def _(out_ref=out_ref):
                out_ref[...] = total


def ring_sum(came, mine, first, halved):
    count, rows, lanes = came.shape
    tiles = 4
    spec = pl.BlockSpec((1, rows // tiles, lanes), lambda i, j: (i, j, 0))
    term = pl.BlockSpec((1, rows // tiles, lanes), lambda i, j: (first + i, j, 0))

    def half(k):
        first = k * tiles // 2
        last = tiles // 2 - 1
        return pl.BlockSpec(
            (1, rows // tiles, lanes), lambda i, j: (i, jnp.clip(j - first, 0, last), 0)
        )

    shapes = [jax.ShapeDtypeStruct((count, rows // 2, lanes), BF16)] * 2
    return pl.pallas_call(
        ring_sum_kernel,
        grid=(count, tiles),
        in_specs=[spec, term],
        out_specs=[half(0), half(1)] if halved else spec,
        out_shape=shapes if halved else jax.ShapeDtypeStruct(came.shape, BF16),
        compiler_params=params(16, "arbitrary", "arbitrary"),
        cost_estimate=SMALL,
        name="ring_sum",
    )(came, mine)


def late_add_kernel(came, plan_ref, pack_ref, *refs):
    values = pack_ref[0]
    if came:
        values = (refs[0][...].astype(F32) + values.astype(F32)).astype(BF16)
    refs[came][...] = values


def late_chunk(plan, at, pack, *came):
    rows, lanes = pack.shape[1:]
    spec = pl.BlockSpec((rows, lanes), lambda i, n: (0, 0))
    return pl.pallas_call(
        functools.partial(late_add_kernel, len(came)),
        grid_spec=pltpu.PrefetchScalarGridSpec(
            num_scalar_prefetch=1,
            grid=(1,),
            in_specs=[pl.BlockSpec((1, rows, lanes), lambda i, n: (n[at], 0, 0))]
            + [spec] * len(came),
            out_specs=spec,
        ),
        out_shape=jax.ShapeDtypeStruct((rows, lanes), BF16),
        compiler_params=params(16, "arbitrary"),
        cost_estimate=SMALL,
        name="late_chunk",
    )(plan, pack, *came)


def late_pick(plan, at, pack):
    return late_chunk(plan, at, pack)


def late_add(plan, at, pack, came):
    return late_chunk(plan, at, pack, came)


def late_join_kernel(col_ref, mine_ref, other_ref, gains_ref, out_ref):
    units = 7
    share = mine_ref.shape[0] // LATE_BLOCKS
    to_rows, to_lanes = unit_slices(2 * units, share)
    blocks = gains_ref.shape[1] // LANES
    gains = [
        gains_ref[g : g + 1, b * LANES : (b + 1) * LANES] for g in range(2) for b in range(blocks)
    ]
    gains = jnp.concatenate(gains + [jnp.zeros((share - len(gains), LANES), F32)], axis=0)
    own = [mine_ref[unit_slices(b, share)] for b in range(units)]
    other = [other_ref[unit_slices(units + b, share)] for b in range(units)]
    for b in range(units):
        first, second = own[b], other[b]
        flipped = col_ref[0] != 0
        out_ref[unit_slices(b, share)] = jnp.where(flipped, second, first)
        out_ref[unit_slices(units + b, share)] = jnp.where(flipped, first, second)
    out_ref[to_rows, to_lanes] = gains.astype(BF16)


def late_join(col, mine, other, gains):
    rows, lanes = mine.shape

    def all_of(*shape):
        return pl.BlockSpec(shape, lambda i, c: (0, 0))

    return pl.pallas_call(
        late_join_kernel,
        grid_spec=pltpu.PrefetchScalarGridSpec(
            num_scalar_prefetch=1,
            grid=(1,),
            in_specs=[all_of(rows, lanes)] * 2 + [all_of(*gains.shape)],
            out_specs=all_of(rows, lanes),
        ),
        out_shape=jax.ShapeDtypeStruct((rows, lanes), BF16),
        compiler_params=params(16, "arbitrary"),
        cost_estimate=SMALL,
        name="late_join",
    )(col, mine, other, gains)


def unpack_late_kernel(first_step, steps, plan_ref, *refs):
    chunks = refs[0 : 2 * steps]
    sgate, sup, sdown, query, key, value, out, gains, all_ref, gain_ref = refs[2 * steps :]
    share, features = chunks[0].shape[0] // LATE_BLOCKS, all_ref.shape[2]
    for k in range(2):
        for step in range(steps):
            at = plan_ref[first_step + 2 * step + k]
            chunk = chunks[steps * k + step]
            to_rows = pl.ds(pl.multiple_of(at * share, share), share)
            for unit in range(14):
                lanes = slice(unit % 7 * LANES, (unit % 7 + 1) * LANES)
                all_ref[k, unit // 7, to_rows, lanes] = chunk[unit_slices(unit, share)]
            if k == 0:
                to_rows = pl.ds(pl.multiple_of(at * GAIN_ROWS, GAIN_ROWS), GAIN_ROWS)
                rows, lanes = unit_slices(14, share)
                gain_ref[to_rows, :] = chunk[rows.start : rows.start + GAIN_ROWS, lanes]
    total = jnp.zeros((GAIN_ROWS, LANES), F32)
    for step in range(steps):
        total = total + gain_ref[step * GAIN_ROWS : (step + 1) * GAIN_ROWS, :].astype(F32)
    blocks = features // LANES
    for row in range(2 * blocks):
        gains[row // blocks : row // blocks + 1, row % blocks * LANES : (row % blocks + 1) * LANES] = (
            total[row : row + 1, :]
        )
    flipped = plan_ref[plan_ref.shape[0] - 1] != 0
    for c in range(2):
        for b in range(14):
            lanes = slice(b % 7 * LANES, (b % 7 + 1) * LANES)
            first, second = all_ref[0, c, :, lanes], all_ref[1, c, :, lanes]
            if b >= 7:
                first, second = second, first
            block = jnp.where(flipped, second, first).astype(F32)
            if b < 6:
                at = slice((2 * c + b // 3) * LANES, (2 * c + b // 3 + 1) * LANES)
                if b % 3 < 2:
                    (sgate, sup)[b % 3][:, at] = block
                else:
                    for k in range(features // LANES):
                        here = slice(k * LANES, (k + 1) * LANES)
                        sdown[at, here] = block[here, :]
            elif b < 9:
                at = (GROUP_HEADS * c + b - 6) * LANES
                query[:, at : at + LANES] = block
            elif b < 11:
                (key, value)[b - 9][:, c * LANES : (c + 1) * LANES] = block
            else:
                at = (GROUP_HEADS * c + b - 11) * LANES
                out[at : at + LANES, :] = block.T


def unpack_late(plan, first_step, chunks, shapes):
    steps = len(chunks[0])
    features = shapes[0][0]
    share = features // steps
    chunk = pl.BlockSpec((LATE_BLOCKS * share, 3 * LANES), lambda i, n: (0, 0))
    return pl.pallas_call(
        functools.partial(unpack_late_kernel, first_step, steps),
        grid_spec=pltpu.PrefetchScalarGridSpec(
            num_scalar_prefetch=1,
            grid=(1,),
            in_specs=[chunk] * (2 * steps),
            out_specs=[pl.BlockSpec(shape, lambda i, n: (0, 0)) for shape in shapes],
            scratch_shapes=[
                pltpu.VMEM((2, 2, features, 7 * LANES), BF16),
                pltpu.VMEM((steps * GAIN_ROWS, LANES), BF16),
            ],
        ),
        out_shape=[jax.ShapeDtypeStruct(shape, F32) for shape in shapes],
        compiler_params=params(48, "arbitrary"),
        cost_estimate=SMALL,
        name="unpack_late",
    )(plan, *chunks[0], *chunks[1])


def plans(ring, each):
    size = len(ring)
    rows = []
    for member in range(size):
        place = ring.index(member)
        for col in range(2):
            chunks = []
            for step in range(2 * size - 1):
                for which in range(2):
                    sign = 1 if which == col else -1
                    chunks.append((place - sign * step) % size)
            experts = []
            for start in (0, size - 1):
                for step in range(start, start + size):
                    for k in range(each):
                        for which in range(2):
                            second = col if which == 0 else 1 - col
                            experts.append(2 * each * chunks[2 * step + which] + each * second + k)
            rows.append(experts + chunks + [col])
    return np.asarray(rows, np.int32)


def body(
    tokens_in,
    norm_gain_attn,
    w_query,
    w_key,
    w_value,
    w_out,
    norm_gain_ffn,
    w_gate,
    w_up,
    w_down,
    w_shared_gate,
    w_shared_up,
    w_shared_down,
    routes,
    gate_weights,
    seq_lengths,
    out_grad,
):
    row = lax.axis_index("row")
    col = lax.axis_index("col")
    dp = lax.axis_index("dp")
    dp_size = lax.axis_size("dp")
    local_rows, local_features = tokens_in.shape
    experts = w_gate.shape[0]
    group_width = GROUP_HEADS * DH
    col_ref = col.reshape(1)

    ring_size = RING
    ring = ring_of(ring_size)
    starts = range(0, dp_size, ring_size)
    rights = [
        (g + ring[k], g + ring[(k + 1) % ring_size]) for g in starts for k in range(ring_size)
    ]
    lefts = [(b, a) for a, b in rights]
    routes_of = [
        [(2 * a, 2 * b) for a, b in ways[0]] + [(2 * a + 1, 2 * b + 1) for a, b in ways[1]]
        for ways in ((rights, lefts), (lefts, rights))
    ]
    experts_each = experts // (2 * ring_size)
    plan = jnp.asarray(plans(ring, experts_each))
    plan = lax.dynamic_slice(
        plan, (2 * (dp % ring_size) + col, jnp.int32(0)), (1, plan.shape[1])
    ).reshape(-1)

    def send(values, which):
        return lax.ppermute(values, ("dp", "col"), routes_of[which])

    def chunk_at(step, which):
        return plan[2 * experts + 2 * step + which]

    def across_rings(values):
        if len(starts) == 1:
            return values
        peers = [[g + k for g in starts] for k in range(ring_size)]
        return lax.psum(values, "dp", axis_index_groups=peers)

    where = jnp.stack([row, seq_lengths[0], col])
    tokens_y = swap(tokens_in, "row")
    tokens_c = swap(tokens_in, "col")
    count = 4
    member = dp % count
    there, out_y = their_columns(
        jnp.stack([col, member]), w_query, w_key, w_value, w_out, count
    )
    gains = jnp.stack([norm_gain_attn, norm_gain_ffn])
    there = swap(there, "col")
    gains_c = swap(gains, "col")

    def project_half(own, other):
        return project(col_ref, own, other, gains, gains_c, w_query, w_key, w_value, there)

    near = project_half(tokens_in, tokens_c)
    gate_c = swap(w_gate, "col")
    out_y = swap(out_y, "row")
    tokens_y = after(tokens_y, near[2], out_y)
    tokens_yc = swap(tokens_y, "col")
    grad_y = swap(after(out_grad, tokens_y), "row")
    far = project_half(tokens_y, tokens_yc)
    shares = [out_y]
    for k in range(1, count):
        part = out_y if k < 3 else after(out_y, far[2])
        shares.append(lax.ppermute(part, "dp", [(m, m ^ k) for m in range(dp_size)]))
    where = after(where, grad_y, *shares)

    w_sgate, w_sup, w_sdown = w_shared_gate[None], w_shared_up[None], w_shared_down[None]
    up_c = swap(after(w_up, gate_c, tokens_yc), "col")

    attended = attend(where, near[2], far[2])
    attended_y = swap(attended, "row")
    attended_c = swap(attended, "col")
    out_c = swap(after(w_out, tokens_yc), "col")
    before = hidden_before(
        where,
        [tokens_in, tokens_c, tokens_y, tokens_yc],
        [attended, attended_c],
        w_out,
        out_c,
    )
    down_c = swap(after(w_down, tokens_yc), "col")
    attended_y = after(attended_y, before[0])
    out_y = join(member, *shares)
    out_yc = swap(out_y, "col")
    attended_yc = swap(attended_y, "col")
    grad_own = join(row, out_grad, grad_y)
    grad_other = swap(grad_own, "col")
    hidden, x_own, x_other, scale_ffn = hidden_after(
        where, before, [attended_y, attended_yc], out_y, out_yc, gains, gains_c
    )
    sgate_c, sup_c, sdown_c = (
        swap(after(w, attended_yc), "col") for w in (w_sgate, w_sup, w_sdown)
    )

    choices = jnp.arange(experts, dtype=jnp.int32)[:, None]
    dense = sum(
        jnp.where(routes[:, k][None, :] == choices, gate_weights[:, k][None, :], 0.0)
        for k in range(routes.shape[1])
    )
    gates = []
    for _ in range(3):
        gates.append(lax.reduce_precision(dense, 8, 7))
        dense = dense - gates[-1]
    gates = jnp.concatenate(gates, axis=0).astype(BF16)

    each = experts_each
    order = plan
    pairs_total = experts // 2
    routed = [w_gate, w_up, gate_c, up_c, w_down, down_c]
    shared = [w_sgate, w_sup, sgate_c, sup_c, w_sdown, sdown_c]

    def run(first, last, order, kept):
        return expert_grads(
            order,
            first,
            last,
            pairs_total,
            [x_own, x_other],
            [grad_own, grad_other],
            gates,
            routed,
            kept,
        )

    first = run(0, 1, order, ())
    kept = first[2:]
    sums = [first[0], first[1]]
    runs = {}
    mixed = {}
    normed = {}

    def work_experts(first, last):
        def work(order, ties):
            nonlocal kept
            result = run(first, last, order, tuple(kept))
            kept = result[2:]
            for at in range(first, last):
                runs[at] = (*result[0:2], at - first)
            return [kept[0]]

        return work

    def work_shared(order, ties):
        runs["shared"] = expert_grads(
            order, 0, 1, None, [x_own, x_other], [grad_own, grad_other], gates, shared, ()
        )
        return [runs["shared"][2]]

    def work_back(half):
        def work(order, ties):
            mixed[True, half] = mix(
                True,
                BF16 if half else F32,
                1 + half,
                order,
                kept[0],
                runs["shared"][2],
                routed[2 * half : 2 * half + 2],
                shared[2 * half : 2 * half + 2],
            )
            if half:
                normed["other"] = [swap(part, "col") for part in mixed[True, 1]]
                return list(mixed[True, 1])
            total, rounded, product = chip_sum(
                mixed[True, 0], normed["other"], hidden, gains
            )
            product_c = swap(product, "col")
            normed["sum"] = total
            normed["tie"] = rounded
            normed["came"] = swap(rounded, "row")
            normed["products"] = [product, product_c, swap(product, "row"), swap(product_c, "row")]
            return [mixed[True, 0]]

        return work

    def work_out(half):
        def work(order, ties):
            mixed[False, half] = mix(
                False,
                BF16 if half else F32,
                1,
                order,
                kept[1],
                runs["shared"][3],
                routed[4 + half : 5 + half],
                shared[4 + half : 5 + half],
            )
            return [mixed[False, half]]

        return work

    start = row * local_rows

    def my_rows(values):
        return lax.dynamic_slice_in_dim(values, start, local_rows, axis=0)

    def their_rows(values):
        return lax.dynamic_slice_in_dim(values, local_rows - start, local_rows, axis=0)

    def work_hidden(order, ties):
        normed["hidden"], *grad, normed["gain"] = norm_back(
            after(where, *ties),
            normed["sum"],
            normed["came"],
            hidden,
            scale_ffn,
            grad_own,
            gains,
            normed["products"],
        )
        normed["grad"] = grad
        normed["grad_c"] = [swap(part, "col") for part in grad]
        return grad

    def work_attend(order, ties):
        normed["qkv"] = attend_back(
            after(where, *ties), near[2], far[2], normed["grad"], normed["grad_c"], w_out, out_c
        )
        return [normed["qkv"]]

    def work_late(order, ties):
        normed["packs"] = late_grads(
            after(where, *ties),
            near[0:2],
            far[0:2],
            normed["qkv"],
            attended,
            normed["grad"],
            normed["grad_c"],
            runs["shared"][0:2],
        )
        return normed["packs"]

    def work_tie(order, ties):
        return [normed["tie"]]

    tasks = [work_experts(at, min(at + 2, pairs_total)) for at in range(1, pairs_total, 2)]
    tasks += [work_shared, work_back(1), work_back(0), work_out(1), work_out(0), work_tie]
    ends = [work_hidden, work_attend, work_late]
    tasks += [None] * (2 * ring_size - 2 - len(tasks) - len(ends)) + ends
    got = [None, None]
    got[0] = send(sums[0], 0)
    tasks.pop(0)(after(order, *sums), sums)
    got[1] = send(after(sums[1], kept[0]), 1)
    for s in range(1, ring_size):
        for k in range(2):
            last = sums
            task = tasks.pop(0) if tasks else None
            if task:
                last = task(after(order, *last), last)
            mine = runs[s]
            sums[k] = ring_sum(after(got[k], *last), mine[k], mine[2], s + 1 == ring_size)
            if s + 1 < ring_size:
                got[k] = send(sums[k], k)
            else:
                sums[k], got[k] = sums[k]
    crossed = [swap(across_rings(total), "col") for total in got]
    waves = [[across_rings(total)[0] for total in sums], [crossed[1][0], crossed[0][0]]]

    chunks_first = 2 * experts
    late_total = 2 * (ring_size - 1)

    def back_to_tokens(ties):
        hidden_grad = normed["hidden"]
        qkv_grad = after(normed["qkv"], *ties)
        here = jnp.concatenate(
            [halves(w, 1, col)[0] for w in (w_query, w_key, w_value)], axis=1
        )
        tokens_back = dot_nt(qkv_grad, here) + swap(
            dot_nt(qkv_grad, there).astype(BF16), "col"
        ).astype(F32)
        tokens_back = my_rows(tokens_back) + swap(
            their_rows(tokens_back).astype(BF16), "row"
        ).astype(F32)
        scale_attn = near[3]
        tokens_f32 = tokens_in.astype(F32)
        gain_attn_part = jnp.sum(tokens_back * tokens_f32 * scale_attn, axis=0)
        scaled = tokens_back * norm_gain_attn
        products = jnp.sum(scaled * tokens_f32, axis=1, keepdims=True)
        mean = (products + swap(products, "col")) / D
        tokens_grad = (
            my_rows(hidden_grad) + scale_attn * scaled - tokens_f32 * scale_attn**3 * mean
        ).astype(BF16)

        gain_parts = jnp.concatenate([gain_attn_part[None], normed["gain"]], axis=0)
        normed["gains"] = across_rings(gain_parts + swap(gain_parts, "row"))
        normed["tokens_grad"] = tokens_grad

    def block_rows(ties):
        ffn_sum = after(mixed[False, 0], *ties) + swap(mixed[False, 1], "col").astype(F32)
        ffn_rows = my_rows(ffn_sum) + swap(their_rows(ffn_sum).astype(BF16), "row").astype(F32)
        block_out = (my_rows(hidden) + ffn_rows).astype(BF16)
        normed["block_out"] = block_out

    shapes = [w_gate.shape, w_up.shape, w_down.shape]
    placed = ()
    late, late_out, late_done = [None, None], [[], []], 0

    def late_turn():
        others = [swap(across_rings(values), "col") for values in late]
        for k in range(2):
            late[k] = late_join(col_ref, across_rings(late[k]), others[1 - k], normed["gains"])
            late_out[k].append(late[k])

    def late_finish(k, values):
        if late_done < ring_size:
            at = chunks_first + 2 * late_done + k
            late[k] = late_add(plan, at, normed["packs"][k], values)
        else:
            late[k] = values
            late_out[k].append(values)

    late = [late_pick(plan, chunks_first + k, normed["packs"][k]) for k in range(2)]
    late_got = None
    last, got = [], [None, None]
    moves = [(wave, step) for wave in range(2) for step in range(ring_size - 1)]
    for number, (wave, step) in enumerate(moves):
        if step == 0:
            came = list(got)
            got = list(waves[wave])
        late_done += late_got is not None
        chunks = [None, None]
        for k in range(2):
            chunks[k] = after(got[k], *last) if last else got[k]
            got[k] = send(chunks[k], k)
            last = [chunks[k]]
            if late_got is not None:
                late_finish(k, after(late_got[k], *last))
                last = [late[k]]
        if late_done == ring_size - 1 and late_got is not None:
            late_turn()
        late_got = [send(late[k], k) for k in range(2)] if late_done < late_total else None
        if wave and step == 0:
            placed = unpack(plan, experts + 2 * (ring_size - 1), 0, came, shapes, placed)
        placed = unpack(plan, experts + 2 * step, wave, chunks, shapes, placed)
        last = placed[0:1]
        if number == 3:
            back_to_tokens(last)
        if number == 9:
            block_rows(last)
    placed = unpack(
        plan,
        experts + 2 * (ring_size - 1),
        1,
        [after(got[k], *last) for k in range(2)],
        shapes,
        placed,
    )
    last = placed[0:1]
    while late_got is not None:
        late_done += 1
        for k in range(2):
            late_finish(k, after(late_got[k], *last))
        late_got = [send(late[k], k) for k in range(2)] if late_done < late_total else None
    gate_grad, up_grad, down_grad = placed
    shapes = [w.shape for w in (w_shared_gate, w_shared_up, w_shared_down)]
    shapes += [w.shape for w in (w_query, w_key, w_value, w_out)] + [gains.shape]
    finals = unpack_late(plan, chunks_first + late_total, late_out, shapes)
    shared_gate_grad, shared_up_grad, shared_down_grad = finals[0:3]
    query_grad, key_grad, value_grad, out_proj_grad, gain_grads = finals[3:8]


    return (
        normed["block_out"],
        normed["tokens_grad"],
        gain_grads[0],
        query_grad,
        key_grad,
        value_grad,
        out_proj_grad,
        gain_grads[1],
        gate_grad,
        up_grad,
        down_grad,
        shared_gate_grad,
        shared_up_grad,
        shared_down_grad,
    )


def solution(mesh):
    in_specs = (
        P(("dp", "row"), "col"),
        P("col"),
        P("col", "row"),
        P("col", "row"),
        P("col", "row"),
        P("row", "col"),
        P("col"),
        P(None, "col", "row"),
        P(None, "col", "row"),
        P(None, "row", "col"),
        P("col", "row"),
        P("col", "row"),
        P("row", "col"),
        P("dp", None),
        P("dp", None),
        P("dp"),
        P(("dp", "row"), "col"),
    )
    out_specs = (
        P(("dp", "row"), "col"),
        P(("dp", "row"), "col"),
        P("col"),
        P("col", "row"),
        P("col", "row"),
        P("col", "row"),
        P("row", "col"),
        P("col"),
        P(None, "col", "row"),
        P(None, "col", "row"),
        P(None, "row", "col"),
        P("col", "row"),
        P("col", "row"),
        P("row", "col"),
    )
    return jax.shard_map(body, mesh=mesh, in_specs=in_specs, out_specs=out_specs, check_vma=False)
```

```python
import functools

import jax
import jax.numpy as jnp
import numpy as np
from jax import lax
from jax.experimental import pallas as pl
from jax.experimental.pallas import tpu as pltpu
from jax.sharding import PartitionSpec as P

D = 1536
HQ = 12
HK = 4
DH = 128
GROUP_HEADS = HQ // HK
LANES = 128

EPSILON = 1e-05
F32 = jnp.float32
BF16 = jnp.bfloat16
MIB = 1024 * 1024
GAIN_ROWS = 16
RING = 8
LATE_BLOCKS = 5
SMALL = pl.CostEstimate(flops=0, bytes_accessed=0, transcendentals=0)


def params(mib, *semantics):
    return pltpu.CompilerParams(
        dimension_semantics=semantics or None, vmem_limit_bytes=mib * MIB
    )


def dot(left, right):
    return jnp.dot(left, right, preferred_element_type=F32)


def dot_nt(left, right):
    return lax.dot_general(left, right, (((1,), (1,)), ((), ())), preferred_element_type=F32)


def dot_tn(left, right):
    return lax.dot_general(left, right, (((0,), (0,)), ((), ())), preferred_element_type=F32)


def after(values, *others):
    return lax.optimization_barrier((values, *others))[0]


def swap(values, axis):
    return lax.ppermute(values, axis, [(0, 1), (1, 0)])


def halves(values, axis, mine):
    size = values.shape[axis] // 2
    low = lax.slice_in_dim(values, 0, size, axis=axis)
    high = lax.slice_in_dim(values, size, 2 * size, axis=axis)
    return jnp.where(mine == 0, low, high), jnp.where(mine == 0, high, low)


def in_order(own, other, mine, axis):
    return jnp.concatenate(
        [jnp.where(mine == 0, own, other), jnp.where(mine == 0, other, own)], axis=axis
    )


def gather_rows(place_ref, own_ref, other_ref, all_ref):
    row = place_ref[0]
    rows = own_ref.shape[0]
    all_ref[pl.ds(pl.multiple_of(row * rows, rows), rows), :] = own_ref[...]
    all_ref[pl.ds(pl.multiple_of((1 - row) * rows, rows), rows), :] = other_ref[...]


def head_rows(ref, first, block):
    return jnp.concatenate(
        [ref[first : first + block, h * DH : (h + 1) * DH] for h in range(GROUP_HEADS)], axis=0
    )


def key_probs(query, key, first, length):
    block, keys = query.shape[0] // GROUP_HEADS, key.shape[0]
    scores = dot_nt(query, key) * DH ** (-0.5)
    shape = (block, keys)
    query_at = lax.broadcasted_iota(jnp.int32, shape, 0) + first
    key_at = lax.broadcasted_iota(jnp.int32, shape, 1)
    allowed = (key_at <= query_at) & (key_at < length)
    allowed = jnp.concatenate([allowed] * GROUP_HEADS, axis=0)
    scores = jnp.where(allowed, scores, -1e30)
    weights = jnp.exp(scores - jnp.max(scores, axis=1, keepdims=True))
    return weights * (1.0 / jnp.sum(weights, axis=1, keepdims=True))


def attend_kernel(place_ref, own_ref, other_ref, out_ref, all_ref):
    gather_rows(place_ref, own_ref, other_ref, all_ref)
    rows = own_ref.shape[0]
    block = 256
    width = GROUP_HEADS * DH
    for at in range(2 * rows // block):
        first, keys = at * block, (at + 1) * block
        query = head_rows(all_ref, first, block)
        key = all_ref[0:keys, width : width + DH]
        value = all_ref[0:keys, width + DH : width + 2 * DH]
        probs = key_probs(query, key, first, place_ref[1])
        result = dot(probs.astype(BF16), value).astype(BF16)
        for h in range(GROUP_HEADS):
            out_ref[first : first + block, h * DH : (h + 1) * DH] = result[
                h * block : (h + 1) * block
            ]


def attend(place, own, other):
    rows, width = own.shape
    spec = pl.BlockSpec(memory_space=pltpu.VMEM)
    return pl.pallas_call(
        attend_kernel,
        out_shape=jax.ShapeDtypeStruct((2 * rows, GROUP_HEADS * DH), BF16),
        in_specs=[pl.BlockSpec(memory_space=pltpu.SMEM), spec, spec],
        out_specs=spec,
        scratch_shapes=[pltpu.VMEM((2 * rows, width), BF16)],
        compiler_params=params(32),
        cost_estimate=SMALL,
        name="attend",
    )(place, own, other)


def attend_back_kernel(
    place_ref, own_ref, other_ref, *refs
):
    grad_refs, grad_c_refs = refs[0:2], refs[2:4]
    out_ref, out_c_ref, result_ref, all_ref, total_ref = refs[4:9]
    gather_rows(place_ref, own_ref, other_ref, all_ref)
    rows = own_ref.shape[0]
    block = 256
    width = GROUP_HEADS * DH
    group = pl.ds(pl.multiple_of(place_ref[2] * width, width), width)
    blocks = 2 * rows // block
    for at in reversed(range(blocks)):
        first, keys = at * block, (at + 1) * block
        query = head_rows(all_ref, first, block)
        key = all_ref[0:keys, width : width + DH]
        value = all_ref[0:keys, width + DH : width + 2 * DH]
        probs = key_probs(query, key, first, place_ref[1])
        half, in_half = divmod(first, rows)
        piece = slice(in_half, in_half + block)
        grad = dot_nt(grad_refs[half][piece, :], out_ref[group, :])
        grad = (grad + dot_nt(grad_c_refs[half][piece, :], out_c_ref[group, :])).astype(BF16)
        grad = jnp.concatenate(
            [grad[:, h * DH : (h + 1) * DH] for h in range(GROUP_HEADS)], axis=0
        )
        probs_grad = dot_nt(grad, value)
        carried = jnp.sum(probs * probs_grad, axis=1, keepdims=True)
        score_grad = (probs * (probs_grad - carried)).astype(BF16)
        query_back = (dot(score_grad, key) * DH ** (-0.5)).astype(BF16)
        for h in range(GROUP_HEADS):
            result_ref[first:keys, h * DH : (h + 1) * DH] = query_back[
                h * block : (h + 1) * block
            ]
        key_back = dot_tn(score_grad, query)
        value_back = dot_tn(probs.astype(BF16), grad)
        if at == blocks - 1:
            total_ref[:, 0:DH] = key_back
            total_ref[:, DH:] = value_back
        else:
            total_ref[0:keys, 0:DH] += key_back
            total_ref[0:keys, DH:] += value_back
    result_ref[:, width : width + DH] = (total_ref[:, 0:DH] * DH ** (-0.5)).astype(BF16)
    result_ref[:, width + DH :] = total_ref[:, DH:].astype(BF16)


def attend_back(place, own, other, grad, grad_c, w_out, out_c):
    rows, width = own.shape
    spec = pl.BlockSpec(memory_space=pltpu.VMEM)
    return pl.pallas_call(
        attend_back_kernel,
        out_shape=jax.ShapeDtypeStruct((2 * rows, width), BF16),
        in_specs=[pl.BlockSpec(memory_space=pltpu.SMEM)] + [spec] * 8,
        out_specs=spec,
        scratch_shapes=[
            pltpu.VMEM((2 * rows, width), BF16),
            pltpu.VMEM((2 * rows, 2 * DH), F32),
        ],
        compiler_params=params(60),
        cost_estimate=SMALL,
        name="attend_back",
    )(place, own, other, *grad, *grad_c, w_out, out_c)


def unit_slices(unit, share):
    row, lane = divmod(unit, 3)
    return slice(row * share, (row + 1) * share), slice(lane * LANES, (lane + 1) * LANES)


def late_kernel(place_ref, *refs):
    near, near_c, far, far_c, qkv_ref, attended_ref = refs[0:6]
    grad_refs, grad_c_refs, shared, outs = refs[6:8], refs[8:10], refs[10:12], refs[12:14]
    rows, features = near.shape
    own_rows = pl.ds(pl.multiple_of(place_ref[0] * rows, rows), rows)
    far_rows = pl.ds(pl.multiple_of((1 - place_ref[0]) * rows, rows), rows)
    split = 7 * LANES

    chunks = outs[0].shape[0]
    share = features // chunks

    def store(h, at, values):
        values = values.astype(BF16)
        for b in range(values.shape[1] // LANES):
            part, unit = divmod(at // LANES + b, split // LANES)
            to_rows, to_lanes = unit_slices(h * (split // LANES) + unit, share)

            def write(out_ref, b=b, to_rows=to_rows, to_lanes=to_lanes):
                for chunk in range(chunks):
                    out_ref[chunk, to_rows, to_lanes] = values[
                        chunk * share : (chunk + 1) * share, b * LANES : (b + 1) * LANES
                    ]

            pl.when(place_ref[2] == 0)(lambda part=part, write=write: write(outs[part]))
            pl.when(place_ref[2] != 0)(lambda part=part, write=write: write(outs[1 - part]))

    for out_ref in outs:
        to_rows, to_lanes = unit_slices(2 * (split // LANES), share)
        for chunk in range(chunks):
            out_ref[chunk, to_rows, to_lanes] = jnp.zeros((share, LANES), BF16)

    for h, (x, y, grad) in enumerate(((near, far, grad_refs), (near_c, far_c, grad_c_refs))):
        for k in range(2):
            store(h, 3 * LANES * k, shared[k][0, h * features : (h + 1) * features, :])
        project = dot_tn(x[...], qkv_ref[own_rows, :]) + dot_tn(y[...], qkv_ref[far_rows, :])
        store(h, 6 * LANES, project)
        out = [dot_tn(grad[k][...], attended_ref[k * rows : (k + 1) * rows, :]) for k in range(2)]
        store(h, 11 * LANES, out[0] + out[1])


def late_grads(place, near, far, qkv_grad, attended, grad, grad_c, shared):
    features = near[0].shape[1]
    rows = LATE_BLOCKS * (features // RING)
    spec = pl.BlockSpec(memory_space=pltpu.VMEM)
    return pl.pallas_call(
        late_kernel,
        out_shape=[jax.ShapeDtypeStruct((RING, rows, 3 * LANES), BF16)] * 2,
        in_specs=[pl.BlockSpec(memory_space=pltpu.SMEM)] + [spec] * 12,
        out_specs=[spec] * 2,
        compiler_params=params(60),
        cost_estimate=SMALL,
        name="late_grads",
    )(place, *near, *far, qkv_grad, attended, *grad, *grad_c, *shared)


def columns_kernel(
    place_ref, query_ref, key_ref, value_ref, w_out_ref, out_ref, share_ref
):
    share_ref[...] = w_out_ref[...]
    width = GROUP_HEADS * DH
    out_ref[:, 0:width] = query_ref[...]
    out_ref[:, width : width + DH] = key_ref[...]
    out_ref[:, width + DH :] = value_ref[...]


def their_columns(place, w_query, w_key, w_value, w_out, shares):
    rows = w_query.shape[0]
    width = GROUP_HEADS * DH + 2 * DH

    def theirs(width):
        return pl.BlockSpec((rows, width), lambda i, c: (0, 1 - c[0]))

    return pl.pallas_call(
        columns_kernel,
        grid_spec=pltpu.PrefetchScalarGridSpec(
            num_scalar_prefetch=1,
            grid=(1,),
            in_specs=[theirs(GROUP_HEADS * DH), theirs(DH), theirs(DH)]
            + [pl.BlockSpec((rows // shares, rows), lambda i, c: (c[1], 0))],
            out_specs=[
                pl.BlockSpec((rows, width), lambda i, c: (0, 0)),
                pl.BlockSpec((rows // shares, rows), lambda i, c: (0, 0)),
            ],
        ),
        out_shape=[
            jax.ShapeDtypeStruct((rows, width), BF16),
            jax.ShapeDtypeStruct((rows // shares, rows), BF16),
        ],
        compiler_params=params(60, "arbitrary"),
        cost_estimate=SMALL,
        name="their_columns",
    )(place, w_query, w_key, w_value, w_out)


def join_kernel(mine_ref, *refs):
    *parts, out_ref = refs
    rows = parts[0].shape[0]
    for k, part in enumerate(parts):
        at = jnp.bitwise_xor(mine_ref[0], k)
        out_ref[pl.ds(pl.multiple_of(at * rows, rows), rows), :] = part[...]


def join(mine, *parts):
    rows, width = parts[0].shape
    spec = pl.BlockSpec(memory_space=pltpu.VMEM)
    return pl.pallas_call(
        join_kernel,
        out_shape=jax.ShapeDtypeStruct((len(parts) * rows, width), parts[0].dtype),
        in_specs=[pl.BlockSpec(memory_space=pltpu.SMEM)] + [spec] * len(parts),
        out_specs=spec,
        compiler_params=params(16),
        cost_estimate=SMALL,
        name="join",
    )(mine.reshape(1), *parts)


def project_kernel(col_ref, own_ref, other_ref, gains_ref, gains_c_ref, query_ref, key_ref, value_ref, there_ref, x_own_ref, x_other_ref, qkv_ref, scale_ref):
    own = own_ref[...].astype(F32)
    other = other_ref[...].astype(F32)
    total = jnp.sum(own * own, axis=1, keepdims=True)
    total = total + jnp.sum(other * other, axis=1, keepdims=True)
    scale = lax.rsqrt(total / D + EPSILON)
    own = (own * scale * gains_ref[0:1, :]).astype(BF16)
    other = (other * scale * gains_c_ref[0:1, :]).astype(BF16)
    x_own_ref[...] = own
    x_other_ref[...] = other
    scale_ref[...] = scale
    here = jnp.concatenate([query_ref[...], key_ref[...], value_ref[...]], axis=1)
    qkv_ref[...] = (dot(own, here) + dot(other, there_ref[...])).astype(BF16)


def project(col, own, other, gains, gains_c, w_query, w_key, w_value, there):
    rows, features = own.shape
    width = there.shape[1]
    group = GROUP_HEADS * DH
    tile = rows // 2

    def whole(*shape):
        return pl.BlockSpec(shape, lambda i, c: (0,) * len(shape))

    def mine(width):
        return pl.BlockSpec((features, width), lambda i, c: (0, c[0]))

    def rowwise(width):
        return pl.BlockSpec((tile, width), lambda i, c: (i, 0))

    return pl.pallas_call(
        project_kernel,
        grid_spec=pltpu.PrefetchScalarGridSpec(
            num_scalar_prefetch=1,
            grid=(rows // tile,),
            in_specs=[
                rowwise(features),
                rowwise(features),
                whole(2, features),
                whole(2, features),
                mine(group),
                mine(DH),
                mine(DH),
                whole(features, width),
            ],
            out_specs=[rowwise(features), rowwise(features), rowwise(width), rowwise(1)],
        ),
        out_shape=[
            jax.ShapeDtypeStruct((rows, features), BF16),
            jax.ShapeDtypeStruct((rows, features), BF16),
            jax.ShapeDtypeStruct((rows, width), BF16),
            jax.ShapeDtypeStruct((rows, 1), F32),
        ],
        compiler_params=params(60, "arbitrary"),
        cost_estimate=SMALL,
        name="project",
    )(col, own, other, gains, gains_c, w_query, w_key, w_value, there)


def head_pair(col_ref, own, other):
    first, second = own[...], other[...]
    flipped = col_ref != 0
    return jnp.concatenate(
        [jnp.where(flipped, second, first), jnp.where(flipped, first, second)], axis=1
    )


def before_kernel(tiles, place_ref, *refs):
    near, near_c, far, far_c, attended, attended_c, here, there, own_ref, other_ref = refs
    is_near = (pl.program_id(0) >= tiles // 2).astype(jnp.int32) == place_ref[0]
    heads = head_pair(place_ref[2], attended, attended_c)
    own = jnp.where(is_near, near[...], far[...]).astype(F32)
    other = jnp.where(is_near, near_c[...], far_c[...]).astype(F32)
    own_ref[...] = own + dot(heads, here[...])
    other_ref[...] = other + dot(heads, there[...])


def after_kernel(place_ref, *refs):
    own_ref, other_ref, attended, attended_c, here, there, gains_ref, gains_c_ref = refs[0:8]
    hidden_ref, x_own_ref, x_other_ref, scale_ref = refs[8:12]
    heads = head_pair(place_ref[2], attended, attended_c)
    own = own_ref[...] + dot(heads, here[...])
    other = other_ref[...] + dot(heads, there[...])
    total = jnp.sum(own * own, axis=1, keepdims=True)
    total = total + jnp.sum(other * other, axis=1, keepdims=True)
    scale = lax.rsqrt(total / D + EPSILON)
    hidden_ref[...] = own
    scale_ref[...] = scale
    x_own_ref[...] = (own * scale * gains_ref[1:2, :]).astype(BF16)
    x_other_ref[...] = (other * scale * gains_c_ref[1:2, :]).astype(BF16)


TOKEN_TILE = 256


def rowwise(width):
    return pl.BlockSpec((TOKEN_TILE, width), lambda i, p: (i, 0))


def whole(*shape):
    return pl.BlockSpec(shape, lambda i, p: (0,) * len(shape))


def hidden_before(place, tokens, attended, here, there):
    half, features = tokens[0].shape
    rows, heads = attended[0].shape
    tiles = rows // TOKEN_TILE
    per_half = half // TOKEN_TILE
    halfwise = pl.BlockSpec((TOKEN_TILE, features), lambda i, p: (i % per_half, 0))
    return pl.pallas_call(
        functools.partial(before_kernel, tiles),
        grid_spec=pltpu.PrefetchScalarGridSpec(
            num_scalar_prefetch=1,
            grid=(tiles,),
            in_specs=[halfwise] * 4 + [rowwise(heads)] * 2 + [whole(2 * heads, features)] * 2,
            out_specs=[rowwise(features)] * 2,
        ),
        out_shape=[jax.ShapeDtypeStruct((rows, features), F32)] * 2,
        compiler_params=params(56, "arbitrary"),
        cost_estimate=pl.CostEstimate(
            flops=8 * rows * features * heads,
            bytes_accessed=16 * rows * features,
            transcendentals=0,
        ),
        name="hidden_before",
    )(place, *tokens, *attended, here, there)


def hidden_after(place, before, attended, here, there, gains, gains_c):
    rows, features = before[0].shape
    heads = attended[0].shape[1]
    return pl.pallas_call(
        after_kernel,
        grid_spec=pltpu.PrefetchScalarGridSpec(
            num_scalar_prefetch=1,
            grid=(rows // TOKEN_TILE,),
            in_specs=[rowwise(features)] * 2
            + [rowwise(heads)] * 2
            + [whole(2 * heads, features)] * 2
            + [whole(2, features)] * 2,
            out_specs=[rowwise(features)] * 3 + [rowwise(1)],
        ),
        out_shape=[
            jax.ShapeDtypeStruct((rows, features), F32),
            jax.ShapeDtypeStruct((rows, features), BF16),
            jax.ShapeDtypeStruct((rows, features), BF16),
            jax.ShapeDtypeStruct((rows, 1), F32),
        ],
        compiler_params=params(56, "arbitrary"),
        cost_estimate=SMALL,
        name="hidden_after",
    )(place, *before, *attended, here, there, gains, gains_c)


def expert_kernel(shared, aliased, first, order_ref, *refs):
    x_own, x_other, o_own, o_other, gates_ref = refs[0:5]
    weights = refs[5:17]
    grads = refs[17 + aliased : 19 + aliased]
    pair_ref, inner_ref = refs[19 + aliased : 21 + aliased]
    step = pl.program_id(0) + first
    rows, features = x_own.shape
    tile = 512
    up_own = jnp.concatenate([weights[k][0] for k in (0, 1, 6, 7)], axis=1)
    up_other = jnp.concatenate([weights[k][0] for k in (2, 3, 8, 9)], axis=1)
    down_own = jnp.concatenate([weights[k][0] for k in (4, 10)], axis=0)
    down_other = jnp.concatenate([weights[k][0] for k in (5, 11)], axis=0)

    def token_tile(t, carry):
        at = pl.ds(pl.multiple_of(t * tile, tile), tile)
        pre = dot(x_own[at, :], up_own) + dot(x_other[at, :], up_other)
        back = dot_nt(o_own[at, :], down_own) + dot_nt(o_other[at, :], down_other)
        for k in range(2):
            pre_gate = pre[:, 2 * k * LANES : (2 * k + 1) * LANES]
            pre_up = pre[:, (2 * k + 1) * LANES : (2 * k + 2) * LANES]
            inner_grad = back[:, k * LANES : (k + 1) * LANES]
            sigmoid = 1.0 / (1.0 + jnp.exp(-pre_gate))
            silu = pre_gate * sigmoid
            inner = silu * pre_up
            if not shared:
                shape = (gates_ref.shape[0], LANES)
                expert = lax.broadcasted_iota(jnp.int32, shape, 0) % (gates_ref.shape[0] // 3)
                chosen = (expert == order_ref[2 * step + k]).astype(F32).astype(BF16)
                gate = dot_tn(gates_ref[:, at], chosen)
                inner = gate * inner
                inner_grad = gate * inner_grad
            gate_grad = inner_grad * pre_up * (sigmoid * (1.0 + pre_gate * (1.0 - sigmoid)))
            inner_ref[0, at, k * LANES : (k + 1) * LANES] = inner.astype(BF16)
            pair_ref[0, at, 2 * k * LANES : (2 * k + 1) * LANES] = gate_grad.astype(BF16)
            pair_ref[0, at, (2 * k + 1) * LANES : (2 * k + 2) * LANES] = (
                inner_grad * silu
            ).astype(BF16)
        return carry

    lax.fori_loop(0, rows // tile, token_tile, 0)
    pairs = pair_ref[0]
    for h, x in enumerate((x_own, x_other)):
        wide = dot_tn(x[...], pairs).astype(BF16)
        for k in range(2):
            grads[k][0, h * features : (h + 1) * features, 0 : 2 * LANES] = wide[
                :, 2 * k * LANES : (2 * k + 2) * LANES
            ]
    inner = inner_ref[0]
    tile = 256
    for h, o in enumerate((o_own, o_other)):
        for j in range(features // tile):
            low = dot_tn(inner, o[:, j * tile : (j + 1) * tile]).astype(BF16)
            for k in range(2):
                for b in range(tile // LANES):
                    at = h * features + j * tile + b * LANES
                    grads[k][0, at : at + LANES, 2 * LANES :] = low[
                        k * LANES : (k + 1) * LANES, b * LANES : (b + 1) * LANES
                    ]


def expert_specs(features, place, wide, low):
    specs = []
    if wide:
        block = pl.BlockSpec((1, features, LANES), lambda i, o: (place(i, o)[0], 0, place(i, o)[1]))
        specs += [block] * 4
    if low:
        block = pl.BlockSpec((1, LANES, features), lambda i, o: (*place(i, o), 0))
        specs += [block] * 2
    return specs


def expert_grads(order, first, last, total, x, o, gates, weights, kept):
    shared = total is None
    steps = last - first
    rows, features = x[0].shape
    aliased = len(kept)

    def fixed(*shape):
        return pl.BlockSpec(shape, lambda i, o: (0,) * len(shape))

    def stepped(*shape):
        return pl.BlockSpec((1, *shape), lambda i, o: (i, 0, 0))

    def placed(*shape):
        return pl.BlockSpec((1, *shape), lambda i, o: (i + first, 0, 0))

    specs = []
    for k in range(2):
        if shared:

            def picked(i, o, k=k):
                return 0, 2 * o[o.shape[0] - 1] + k

        else:

            def picked(i, o, k=k):
                return o[2 * (i + first) + k], o[o.shape[0] - 1]

        specs += expert_specs(features, picked, True, True)
    total = steps if shared else total
    return pl.pallas_call(
        functools.partial(expert_kernel, shared, aliased, first),
        grid_spec=pltpu.PrefetchScalarGridSpec(
            num_scalar_prefetch=1,
            grid=(steps,),
            in_specs=[fixed(rows, features)] * 4
            + [fixed(*gates.shape)]
            + specs
            + [pl.BlockSpec(memory_space=pl.ANY)] * aliased,
            out_specs=[stepped(2 * features, 3 * LANES)] * 2
            + [placed(rows, 4 * LANES), placed(rows, 2 * LANES)],
        ),
        out_shape=[jax.ShapeDtypeStruct((steps, 2 * features, 3 * LANES), BF16)] * 2
        + [
            jax.ShapeDtypeStruct((total, rows, 4 * LANES), BF16),
            jax.ShapeDtypeStruct((total, rows, 2 * LANES), BF16),
        ],
        input_output_aliases={18 + k: 2 + k for k in range(aliased)},
        compiler_params=params(40, "arbitrary"),
        cost_estimate=SMALL,
        name="expert_grads",
    )(order, *x, *o, gates, *weights, *weights, *kept)


def mix_kernel(back, group, pieces, order_ref, *refs):
    acts_ref, shared_ref = refs[0:2]
    each = 2 if back else 1
    count = 2 * group * each
    weights = refs[2 : 2 + count]
    shared = refs[2 + count : 2 + count + 2 * each]
    *outs, total_ref = refs[2 + count + 2 * each :]
    step = pl.program_id(0)
    rows = total_ref.shape[0]
    tile = 512
    times = dot_nt if back else dot
    along = 1 if back else 0

    @pl.when(step == 0)
    def _():
        both = jnp.concatenate([w[0] for w in shared], axis=along)
        for t in range(rows // tile):
            at = slice(t * tile, (t + 1) * tile)
            total_ref[at, :] = times(shared_ref[0, at, :], both)

    both = jnp.concatenate([w[0] for w in weights], axis=along)
    for t in range(rows // tile):
        at = slice(t * tile, (t + 1) * tile)
        acts = jnp.concatenate([acts_ref[g, at, :] for g in range(group)], axis=1)
        total_ref[at, :] += times(acts, both)

    @pl.when(step == pl.num_programs(0) - 1)
    def _():
        part = rows // pieces
        for k, out_ref in enumerate(outs):
            out_ref[...] = total_ref[k * part : (k + 1) * part, :].astype(out_ref.dtype)


def mix(back, dtype, pieces, order, acts, shared_acts, weights, shared_weights):
    pairs, rows, width = acts.shape
    features = weights[0].shape[1] if back else weights[0].shape[2]
    group = 4 if pairs % 4 == 0 else 1

    def spec(place):
        if back:
            return pl.BlockSpec((1, features, LANES), lambda i, o: (place(i, o)[0], 0, place(i, o)[1]))
        return pl.BlockSpec((1, LANES, features), lambda i, o: (*place(i, o), 0))

    def routed(k):
        return spec(lambda i, o: (o[2 * group * i + k], o[o.shape[0] - 1]))

    def common(k):
        return spec(lambda i, o: (0, 2 * o[o.shape[0] - 1] + k))

    outs = pl.pallas_call(
        functools.partial(mix_kernel, back, group, pieces),
        grid_spec=pltpu.PrefetchScalarGridSpec(
            num_scalar_prefetch=1,
            grid=(pairs // group,),
            in_specs=[
                pl.BlockSpec((group, rows, width), lambda i, o: (i, 0, 0)),
                pl.BlockSpec((1, rows, width), lambda i, o: (0, 0, 0)),
            ]
            + [routed(k) for k in range(2 * group) for _ in weights]
            + [common(k) for k in range(2) for _ in weights],
            out_specs=[pl.BlockSpec((rows // pieces, features), lambda i, o: (0, 0))] * pieces,
            scratch_shapes=[pltpu.VMEM((rows, features), F32)],
        ),
        out_shape=[jax.ShapeDtypeStruct((rows // pieces, features), dtype)] * pieces,
        compiler_params=params(48, "arbitrary"),
        cost_estimate=SMALL,
        name="mix",
    )(order, acts, shared_acts, *weights * (2 * group), *shared_weights * 2)
    return outs if pieces > 1 else outs[0]


def chip_sum_kernel(tiles, own_ref, first_ref, second_ref, hidden_ref, gains_ref, total_ref, rounded_ref, product_ref):
    is_first = pl.program_id(0) < tiles // 2
    other = jnp.where(is_first, first_ref[...], second_ref[...])
    total = own_ref[...] + other.astype(F32)
    total_ref[...] = total
    rounded_ref[...] = total.astype(BF16)
    product_ref[...] = lax.dot_general(
        jnp.ones((8, total.shape[1]), F32),
        total * gains_ref[1:2, :] * hidden_ref[...],
        (((1,), (1,)), ((), ())),
        precision=lax.Precision.HIGHEST,
        preferred_element_type=F32,
    )


def chip_sum(own, other, hidden, gains):
    rows, features = own.shape
    spec = pl.BlockSpec((TOKEN_TILE, features), lambda i: (i, 0))
    tiles = rows // TOKEN_TILE
    piece = pl.BlockSpec((TOKEN_TILE, features), lambda i: (i % (tiles // 2), 0))
    return pl.pallas_call(
        functools.partial(chip_sum_kernel, tiles),
        grid=(tiles,),
        out_shape=[
            jax.ShapeDtypeStruct((rows, features), F32),
            jax.ShapeDtypeStruct((rows, features), BF16),
            jax.ShapeDtypeStruct((8, rows), F32),
        ],
        in_specs=[spec, piece, piece, spec, pl.BlockSpec(gains.shape, lambda i: (0, 0))],
        out_specs=[spec, spec, pl.BlockSpec((8, TOKEN_TILE), lambda i: (0, i))],
        compiler_params=params(24, "arbitrary"),
        cost_estimate=SMALL,
        name="chip_sum",
    )(own, *other, hidden, gains)


def norm_back_kernel(tiles, place_ref, *refs):
    sum_ref, came_ref, hidden_ref, scale_ref, out_grad_ref, gains_ref = refs[0:6]
    products = refs[6:10]
    hidden_grad_ref, first_ref, second_ref, gain_ref = refs[10:14]
    step = pl.program_id(0)
    part = (step >= tiles // 2).astype(jnp.int32)
    grad = sum_ref[...] + came_ref[...].astype(F32)
    hidden = hidden_ref[...]
    scale = scale_ref[...]
    total = (products[0][...] + products[1][...]) + (products[2][...] + products[3][...])
    mean = lax.dot_general(
        total,
        jnp.full((8, LANES), 1.0 / (8 * D), F32),
        (((0,), (0,)), ((), ())),
        precision=lax.Precision.HIGHEST,
        preferred_element_type=F32,
    )[:, 0:1]
    result = out_grad_ref[...].astype(F32) + scale * (grad * gains_ref[1:2, :])
    result = result - hidden * (scale * scale * scale * mean)
    hidden_grad_ref[...] = result
    for k, rounded_ref in enumerate((first_ref, second_ref)):

        @pl.when(part == k)
        def _(rounded_ref=rounded_ref):
            rounded_ref[...] = result.astype(BF16)

    @pl.when(step == 0)
    def _():
        gain_ref[...] = jnp.zeros_like(gain_ref)

    @pl.when(part == place_ref[0])
    def _():
        gain_ref[...] += jnp.sum(grad * hidden * scale, axis=0, keepdims=True)


def norm_back(place, sums, came, hidden, scale, out_grad, gains, products):
    rows, features = hidden.shape
    tiles = rows // TOKEN_TILE
    lanes = pl.BlockSpec((8, TOKEN_TILE), lambda i, p: (0, i))

    def piece(k):
        last = tiles // 2 - 1
        return pl.BlockSpec(
            (TOKEN_TILE, features), lambda i, p: (jnp.clip(i - k * tiles // 2, 0, last), 0)
        )

    return pl.pallas_call(
        functools.partial(norm_back_kernel, tiles),
        grid_spec=pltpu.PrefetchScalarGridSpec(
            num_scalar_prefetch=1,
            grid=(tiles,),
            in_specs=[rowwise(features)] * 3
            + [rowwise(1), rowwise(features), whole(2, features)]
            + [lanes] * 4,
            out_specs=[rowwise(features), piece(0), piece(1), whole(1, features)],
        ),
        out_shape=[
            jax.ShapeDtypeStruct((rows, features), F32),
            jax.ShapeDtypeStruct((rows // 2, features), BF16),
            jax.ShapeDtypeStruct((rows // 2, features), BF16),
            jax.ShapeDtypeStruct((1, features), F32),
        ],
        compiler_params=params(48, "arbitrary"),
        cost_estimate=SMALL,
        name="norm_back",
    )(place, sums, came, hidden, scale, out_grad, gains, *products)


def ring_of(size):
    return list(range(0, size, 2)) + list(range(1, size, 2))[::-1]


def unpack_kernel(aliased, plan_ref, *refs):
    chunks = refs[0:2]
    gate_ref, up_ref, down_ref = refs[2 + aliased : 5 + aliased]
    rows = gate_ref.shape[1]

    def write(chunk_ref):
        first = chunk_ref.shape[0] - rows
        gate_ref[0] = chunk_ref[first:, 0:LANES].astype(F32)
        up_ref[0] = chunk_ref[first:, LANES : 2 * LANES].astype(F32)
        for b in range(rows // LANES):
            at = slice(first + b * LANES, first + (b + 1) * LANES)
            down_ref[0, :, b * LANES : (b + 1) * LANES] = chunk_ref[at, 2 * LANES :].astype(F32)

    for k in range(2):
        pl.when(pl.program_id(0) == k)(lambda k=k: write(chunks[k]))


def unpack(plan, first, wave, chunks, shapes, outs):
    rows = shapes[0][1]

    def place(d, n):
        block = n[n.shape[0] - 1]
        return n[first + d], 1 - block if wave else block

    def wide(d, n):
        expert, block = place(d, n)
        return (expert, 0, block)

    def low(d, n):
        expert, block = place(d, n)
        return (expert, block, 0)

    aliased = len(outs)
    return pl.pallas_call(
        functools.partial(unpack_kernel, aliased),
        grid_spec=pltpu.PrefetchScalarGridSpec(
            num_scalar_prefetch=1,
            grid=(2,),
            in_specs=[pl.BlockSpec(chunk.shape, lambda d, n: (0, 0)) for chunk in chunks]
            + [pl.BlockSpec(memory_space=pl.ANY)] * aliased,
            out_specs=[
                pl.BlockSpec((1, rows, LANES), wide),
                pl.BlockSpec((1, rows, LANES), wide),
                pl.BlockSpec((1, LANES, rows), low),
            ],
        ),
        out_shape=[jax.ShapeDtypeStruct(shape, F32) for shape in shapes],
        input_output_aliases={3 + k: k for k in range(aliased)},
        compiler_params=params(16, "arbitrary"),
        cost_estimate=SMALL,
        name="unpack",
    )(plan, *chunks, *outs)


def ring_sum_kernel(came_ref, mine_ref, *outs):
    total = (came_ref[...].astype(F32) + mine_ref[...].astype(F32)).astype(BF16)
    if len(outs) == 1:
        outs[0][...] = total
    else:
        half = pl.program_id(1) // (pl.num_programs(1) // 2)
        for k, out_ref in enumerate(outs):

            @pl.when(half == k)
            def _(out_ref=out_ref):
                out_ref[...] = total


def ring_sum(came, mine, first, halved):
    count, rows, lanes = came.shape
    tiles = 4
    spec = pl.BlockSpec((1, rows // tiles, lanes), lambda i, j: (i, j, 0))
    term = pl.BlockSpec((1, rows // tiles, lanes), lambda i, j: (first + i, j, 0))

    def half(k):
        first = k * tiles // 2
        last = tiles // 2 - 1
        return pl.BlockSpec(
            (1, rows // tiles, lanes), lambda i, j: (i, jnp.clip(j - first, 0, last), 0)
        )

    shapes = [jax.ShapeDtypeStruct((count, rows // 2, lanes), BF16)] * 2
    return pl.pallas_call(
        ring_sum_kernel,
        grid=(count, tiles),
        in_specs=[spec, term],
        out_specs=[half(0), half(1)] if halved else spec,
        out_shape=shapes if halved else jax.ShapeDtypeStruct(came.shape, BF16),
        compiler_params=params(16, "arbitrary", "arbitrary"),
        cost_estimate=SMALL,
        name="ring_sum",
    )(came, mine)


def late_add_kernel(came, plan_ref, pack_ref, *refs):
    values = pack_ref[0]
    if came:
        values = (refs[0][...].astype(F32) + values.astype(F32)).astype(BF16)
    refs[came][...] = values


def late_chunk(plan, at, pack, *came):
    rows, lanes = pack.shape[1:]
    spec = pl.BlockSpec((rows, lanes), lambda i, n: (0, 0))
    return pl.pallas_call(
        functools.partial(late_add_kernel, len(came)),
        grid_spec=pltpu.PrefetchScalarGridSpec(
            num_scalar_prefetch=1,
            grid=(1,),
            in_specs=[pl.BlockSpec((1, rows, lanes), lambda i, n: (n[at], 0, 0))]
            + [spec] * len(came),
            out_specs=spec,
        ),
        out_shape=jax.ShapeDtypeStruct((rows, lanes), BF16),
        compiler_params=params(16, "arbitrary"),
        cost_estimate=SMALL,
        name="late_chunk",
    )(plan, pack, *came)


def late_pick(plan, at, pack):
    return late_chunk(plan, at, pack)


def late_add(plan, at, pack, came):
    return late_chunk(plan, at, pack, came)


def late_join_kernel(col_ref, mine_ref, other_ref, gains_ref, out_ref):
    units = 7
    share = mine_ref.shape[0] // LATE_BLOCKS
    to_rows, to_lanes = unit_slices(2 * units, share)
    blocks = gains_ref.shape[1] // LANES
    gains = [
        gains_ref[g : g + 1, b * LANES : (b + 1) * LANES] for g in range(2) for b in range(blocks)
    ]
    gains = jnp.concatenate(gains + [jnp.zeros((share - len(gains), LANES), F32)], axis=0)
    own = [mine_ref[unit_slices(b, share)] for b in range(units)]
    other = [other_ref[unit_slices(units + b, share)] for b in range(units)]
    for b in range(units):
        first, second = own[b], other[b]
        flipped = col_ref[0] != 0
        out_ref[unit_slices(b, share)] = jnp.where(flipped, second, first)
        out_ref[unit_slices(units + b, share)] = jnp.where(flipped, first, second)
    out_ref[to_rows, to_lanes] = gains.astype(BF16)


def late_join(col, mine, other, gains):
    rows, lanes = mine.shape

    def all_of(*shape):
        return pl.BlockSpec(shape, lambda i, c: (0, 0))

    return pl.pallas_call(
        late_join_kernel,
        grid_spec=pltpu.PrefetchScalarGridSpec(
            num_scalar_prefetch=1,
            grid=(1,),
            in_specs=[all_of(rows, lanes)] * 2 + [all_of(*gains.shape)],
            out_specs=all_of(rows, lanes),
        ),
        out_shape=jax.ShapeDtypeStruct((rows, lanes), BF16),
        compiler_params=params(16, "arbitrary"),
        cost_estimate=SMALL,
        name="late_join",
    )(col, mine, other, gains)


def unpack_late_kernel(first_step, steps, plan_ref, *refs):
    chunks = refs[0 : 2 * steps]
    sgate, sup, sdown, query, key, value, out, gains, all_ref, gain_ref = refs[2 * steps :]
    share, features = chunks[0].shape[0] // LATE_BLOCKS, all_ref.shape[2]
    for k in range(2):
        for step in range(steps):
            at = plan_ref[first_step + 2 * step + k]
            chunk = chunks[steps * k + step]
            to_rows = pl.ds(pl.multiple_of(at * share, share), share)
            for unit in range(14):
                lanes = slice(unit % 7 * LANES, (unit % 7 + 1) * LANES)
                all_ref[k, unit // 7, to_rows, lanes] = chunk[unit_slices(unit, share)]
            if k == 0:
                to_rows = pl.ds(pl.multiple_of(at * GAIN_ROWS, GAIN_ROWS), GAIN_ROWS)
                rows, lanes = unit_slices(14, share)
                gain_ref[to_rows, :] = chunk[rows.start : rows.start + GAIN_ROWS, lanes]
    total = jnp.zeros((GAIN_ROWS, LANES), F32)
    for step in range(steps):
        total = total + gain_ref[step * GAIN_ROWS : (step + 1) * GAIN_ROWS, :].astype(F32)
    blocks = features // LANES
    for row in range(2 * blocks):
        gains[row // blocks : row // blocks + 1, row % blocks * LANES : (row % blocks + 1) * LANES] = (
            total[row : row + 1, :]
        )
    flipped = plan_ref[plan_ref.shape[0] - 1] != 0
    for c in range(2):
        for b in range(14):
            lanes = slice(b % 7 * LANES, (b % 7 + 1) * LANES)
            first, second = all_ref[0, c, :, lanes], all_ref[1, c, :, lanes]
            if b >= 7:
                first, second = second, first
            block = jnp.where(flipped, second, first).astype(F32)
            if b < 6:
                at = slice((2 * c + b // 3) * LANES, (2 * c + b // 3 + 1) * LANES)
                if b % 3 < 2:
                    (sgate, sup)[b % 3][:, at] = block
                else:
                    for k in range(features // LANES):
                        here = slice(k * LANES, (k + 1) * LANES)
                        sdown[at, here] = block[here, :]
            elif b < 9:
                at = (GROUP_HEADS * c + b - 6) * LANES
                query[:, at : at + LANES] = block
            elif b < 11:
                (key, value)[b - 9][:, c * LANES : (c + 1) * LANES] = block
            else:
                at = (GROUP_HEADS * c + b - 11) * LANES
                out[at : at + LANES, :] = block.T


def unpack_late(plan, first_step, chunks, shapes):
    steps = len(chunks[0])
    features = shapes[0][0]
    share = features // steps
    chunk = pl.BlockSpec((LATE_BLOCKS * share, 3 * LANES), lambda i, n: (0, 0))
    return pl.pallas_call(
        functools.partial(unpack_late_kernel, first_step, steps),
        grid_spec=pltpu.PrefetchScalarGridSpec(
            num_scalar_prefetch=1,
            grid=(1,),
            in_specs=[chunk] * (2 * steps),
            out_specs=[pl.BlockSpec(shape, lambda i, n: (0, 0)) for shape in shapes],
            scratch_shapes=[
                pltpu.VMEM((2, 2, features, 7 * LANES), BF16),
                pltpu.VMEM((steps * GAIN_ROWS, LANES), BF16),
            ],
        ),
        out_shape=[jax.ShapeDtypeStruct(shape, F32) for shape in shapes],
        compiler_params=params(48, "arbitrary"),
        cost_estimate=SMALL,
        name="unpack_late",
    )(plan, *chunks[0], *chunks[1])


def plans(ring, each):
    size = len(ring)
    rows = []
    for member in range(size):
        place = ring.index(member)
        for col in range(2):
            chunks = []
            for step in range(2 * size - 1):
                for which in range(2):
                    sign = 1 if which == col else -1
                    chunks.append((place - sign * step) % size)
            experts = []
            for start in (0, size - 1):
                for step in range(start, start + size):
                    for k in range(each):
                        for which in range(2):
                            second = col if which == 0 else 1 - col
                            experts.append(2 * each * chunks[2 * step + which] + each * second + k)
            rows.append(experts + chunks + [col])
    return np.asarray(rows, np.int32)


def body(
    tokens_in,
    norm_gain_attn,
    w_query,
    w_key,
    w_value,
    w_out,
    norm_gain_ffn,
    w_gate,
    w_up,
    w_down,
    w_shared_gate,
    w_shared_up,
    w_shared_down,
    routes,
    gate_weights,
    seq_lengths,
    out_grad,
):
    row = lax.axis_index("row")
    col = lax.axis_index("col")
    dp = lax.axis_index("dp")
    dp_size = lax.axis_size("dp")
    local_rows, local_features = tokens_in.shape
    experts = w_gate.shape[0]
    group_width = GROUP_HEADS * DH
    col_ref = col.reshape(1)

    ring_size = RING
    ring = ring_of(ring_size)
    starts = range(0, dp_size, ring_size)
    rights = [
        (g + ring[k], g + ring[(k + 1) % ring_size]) for g in starts for k in range(ring_size)
    ]
    lefts = [(b, a) for a, b in rights]
    routes_of = [
        [(2 * a, 2 * b) for a, b in ways[0]] + [(2 * a + 1, 2 * b + 1) for a, b in ways[1]]
        for ways in ((rights, lefts), (lefts, rights))
    ]
    experts_each = experts // (2 * ring_size)
    plan = jnp.asarray(plans(ring, experts_each))
    plan = lax.dynamic_slice(
        plan, (2 * (dp % ring_size) + col, jnp.int32(0)), (1, plan.shape[1])
    ).reshape(-1)

    def send(values, which):
        return lax.ppermute(values, ("dp", "col"), routes_of[which])

    def chunk_at(step, which):
        return plan[2 * experts + 2 * step + which]

    def across_rings(values):
        if len(starts) == 1:
            return values
        peers = [[g + k for g in starts] for k in range(ring_size)]
        return lax.psum(values, "dp", axis_index_groups=peers)

    where = jnp.stack([row, seq_lengths[0], col])
    tokens_y = swap(tokens_in, "row")
    tokens_c = swap(tokens_in, "col")
    count = 4
    member = dp % count
    there, out_y = their_columns(
        jnp.stack([col, member]), w_query, w_key, w_value, w_out, count
    )
    gains = jnp.stack([norm_gain_attn, norm_gain_ffn])
    there = swap(there, "col")
    gains_c = swap(gains, "col")

    def project_half(own, other):
        return project(col_ref, own, other, gains, gains_c, w_query, w_key, w_value, there)

    near = project_half(tokens_in, tokens_c)
    gate_c = swap(w_gate, "col")
    out_y = swap(out_y, "row")
    tokens_y = after(tokens_y, near[2], out_y)
    tokens_yc = swap(tokens_y, "col")
    grad_y = swap(after(out_grad, tokens_y), "row")
    far = project_half(tokens_y, tokens_yc)
    shares = [out_y]
    for k in range(1, count):
        part = out_y if k < 3 else after(out_y, far[2])
        shares.append(lax.ppermute(part, "dp", [(m, m ^ k) for m in range(dp_size)]))
    where = after(where, grad_y, *shares)

    w_sgate, w_sup, w_sdown = w_shared_gate[None], w_shared_up[None], w_shared_down[None]
    up_c = swap(after(w_up, gate_c, tokens_yc), "col")

    attended = attend(where, near[2], far[2])
    attended_y = swap(attended, "row")
    attended_c = swap(attended, "col")
    out_c = swap(after(w_out, tokens_yc), "col")
    before = hidden_before(
        where,
        [tokens_in, tokens_c, tokens_y, tokens_yc],
        [attended, attended_c],
        w_out,
        out_c,
    )
    down_c = swap(after(w_down, tokens_yc), "col")
    attended_y = after(attended_y, before[0])
    out_y = join(member, *shares)
    out_yc = swap(out_y, "col")
    attended_yc = swap(attended_y, "col")
    grad_own = join(row, out_grad, grad_y)
    grad_other = swap(grad_own, "col")
    hidden, x_own, x_other, scale_ffn = hidden_after(
        where, before, [attended_y, attended_yc], out_y, out_yc, gains, gains_c
    )
    sgate_c, sup_c, sdown_c = (
        swap(after(w, attended_yc), "col") for w in (w_sgate, w_sup, w_sdown)
    )

    choices = jnp.arange(experts, dtype=jnp.int32)[:, None]
    dense = sum(
        jnp.where(routes[:, k][None, :] == choices, gate_weights[:, k][None, :], 0.0)
        for k in range(routes.shape[1])
    )
    gates = []
    for _ in range(3):
        gates.append(lax.reduce_precision(dense, 8, 7))
        dense = dense - gates[-1]
    gates = jnp.concatenate(gates, axis=0).astype(BF16)

    each = experts_each
    order = plan
    pairs_total = experts // 2
    routed = [w_gate, w_up, gate_c, up_c, w_down, down_c]
    shared = [w_sgate, w_sup, sgate_c, sup_c, w_sdown, sdown_c]

    def run(first, last, order, kept):
        return expert_grads(
            order,
            first,
            last,
            pairs_total,
            [x_own, x_other],
            [grad_own, grad_other],
            gates,
            routed,
            kept,
        )

    first = run(0, 1, order, ())
    kept = first[2:]
    sums = [first[0], first[1]]
    runs = {}
    mixed = {}
    normed = {}

    def work_experts(first, last):
        def work(order, ties):
            nonlocal kept
            result = run(first, last, order, tuple(kept))
            kept = result[2:]
            for at in range(first, last):
                runs[at] = (*result[0:2], at - first)
            return [kept[0]]

        return work

    def work_shared(order, ties):
        runs["shared"] = expert_grads(
            order, 0, 1, None, [x_own, x_other], [grad_own, grad_other], gates, shared, ()
        )
        return [runs["shared"][2]]

    def work_back(half):
        def work(order, ties):
            mixed[True, half] = mix(
                True,
                BF16 if half else F32,
                1 + half,
                order,
                kept[0],
                runs["shared"][2],
                routed[2 * half : 2 * half + 2],
                shared[2 * half : 2 * half + 2],
            )
            if half:
                normed["other"] = [swap(part, "col") for part in mixed[True, 1]]
                return list(mixed[True, 1])
            total, rounded, product = chip_sum(
                mixed[True, 0], normed["other"], hidden, gains
            )
            product_c = swap(product, "col")
            normed["sum"] = total
            normed["tie"] = rounded
            normed["came"] = swap(rounded, "row")
            normed["products"] = [product, product_c, swap(product, "row"), swap(product_c, "row")]
            return [mixed[True, 0]]

        return work

    def work_out(half):
        def work(order, ties):
            mixed[False, half] = mix(
                False,
                BF16 if half else F32,
                1,
                order,
                kept[1],
                runs["shared"][3],
                routed[4 + half : 5 + half],
                shared[4 + half : 5 + half],
            )
            return [mixed[False, half]]

        return work

    start = row * local_rows

    def my_rows(values):
        return lax.dynamic_slice_in_dim(values, start, local_rows, axis=0)

    def their_rows(values):
        return lax.dynamic_slice_in_dim(values, local_rows - start, local_rows, axis=0)

    def work_hidden(order, ties):
        normed["hidden"], *grad, normed["gain"] = norm_back(
            after(where, *ties),
            normed["sum"],
            normed["came"],
            hidden,
            scale_ffn,
            grad_own,
            gains,
            normed["products"],
        )
        normed["grad"] = grad
        normed["grad_c"] = [swap(part, "col") for part in grad]
        return grad

    def work_attend(order, ties):
        normed["qkv"] = attend_back(
            after(where, *ties), near[2], far[2], normed["grad"], normed["grad_c"], w_out, out_c
        )
        return [normed["qkv"]]

    def work_late(order, ties):
        normed["packs"] = late_grads(
            after(where, *ties),
            near[0:2],
            far[0:2],
            normed["qkv"],
            attended,
            normed["grad"],
            normed["grad_c"],
            runs["shared"][0:2],
        )
        return normed["packs"]

    def work_tie(order, ties):
        return [normed["tie"]]

    tasks = [work_experts(at, min(at + 2, pairs_total)) for at in range(1, pairs_total, 2)]
    tasks += [work_shared, work_back(1), work_back(0), work_out(1), work_out(0), work_tie]
    ends = [work_hidden, work_attend, work_late]
    tasks += [None] * (2 * ring_size - 2 - len(tasks) - len(ends)) + ends
    got = [None, None]
    got[0] = send(sums[0], 0)
    tasks.pop(0)(after(order, *sums), sums)
    got[1] = send(after(sums[1], kept[0]), 1)
    for s in range(1, ring_size):
        for k in range(2):
            last = sums
            task = tasks.pop(0) if tasks else None
            if task:
                last = task(after(order, *last), last)
            mine = runs[s]
            sums[k] = ring_sum(after(got[k], *last), mine[k], mine[2], s + 1 == ring_size)
            if s + 1 < ring_size:
                got[k] = send(sums[k], k)
            else:
                sums[k], got[k] = sums[k]
    crossed = [swap(across_rings(total), "col") for total in got]
    waves = [[across_rings(total)[0] for total in sums], [crossed[1][0], crossed[0][0]]]

    chunks_first = 2 * experts
    late_total = 2 * (ring_size - 1)

    def back_to_tokens(ties):
        hidden_grad = normed["hidden"]
        qkv_grad = after(normed["qkv"], *ties)
        here = jnp.concatenate(
            [halves(w, 1, col)[0] for w in (w_query, w_key, w_value)], axis=1
        )
        tokens_back = dot_nt(qkv_grad, here) + swap(
            dot_nt(qkv_grad, there).astype(BF16), "col"
        ).astype(F32)
        came = swap(their_rows(tokens_back).astype(BF16), "row")
        normed["tokens_came"] = came
        tokens_back = my_rows(tokens_back) + came.astype(F32)
        scale_attn = near[3]
        tokens_f32 = tokens_in.astype(F32)
        gain_attn_part = jnp.sum(tokens_back * tokens_f32 * scale_attn, axis=0)
        scaled = tokens_back * norm_gain_attn
        products = jnp.sum(scaled * tokens_f32, axis=1, keepdims=True)
        mean = (products + swap(products, "col")) / D
        tokens_grad = (
            my_rows(hidden_grad) + scale_attn * scaled - tokens_f32 * scale_attn**3 * mean
        ).astype(BF16)

        gain_parts = jnp.concatenate([gain_attn_part[None], normed["gain"]], axis=0)
        normed["gains"] = across_rings(gain_parts + swap(gain_parts, "row"))
        normed["tokens_grad"] = tokens_grad

    def block_rows(ties):
        ffn_sum = after(mixed[False, 0], *ties) + swap(mixed[False, 1], "col").astype(F32)
        ffn_rows = my_rows(ffn_sum) + swap(their_rows(ffn_sum).astype(BF16), "row").astype(F32)
        block_out = (my_rows(hidden) + ffn_rows).astype(BF16)
        normed["block_out"] = block_out

    shapes = [w_gate.shape, w_up.shape, w_down.shape]
    placed = ()
    late, late_out, late_done = [None, None], [[], []], 0

    def late_turn():
        others = [swap(across_rings(values), "col") for values in late]
        for k in range(2):
            late[k] = late_join(col_ref, across_rings(late[k]), others[1 - k], normed["gains"])
            late_out[k].append(late[k])

    def late_finish(k, values):
        if late_done < ring_size:
            at = chunks_first + 2 * late_done + k
            late[k] = late_add(plan, at, normed["packs"][k], values)
        else:
            late[k] = values
            late_out[k].append(values)

    late = [late_pick(plan, chunks_first + k, normed["packs"][k]) for k in range(2)]
    late_got = None
    last, got = [], [None, None]
    moves = [(wave, step) for wave in range(2) for step in range(ring_size - 1)]
    for number, (wave, step) in enumerate(moves):
        if step == 0:
            came = list(got)
            got = [after(waves[wave][k], came[k]) if wave else waves[wave][k] for k in range(2)]
        late_done += late_got is not None
        chunks = [None, None]
        for k in range(2):
            chunks[k] = after(got[k], *last) if last else got[k]
            got[k] = send(chunks[k], k)
            last = [chunks[k]]
            if late_got is not None:
                late_finish(k, after(late_got[k], *last))
                last = [late[k]]
        if late_done == ring_size - 1 and late_got is not None:
            late_turn()
        late_got = [send(late[k], k) for k in range(2)] if late_done < late_total else None
        if wave and step == 0:
            placed = unpack(plan, experts + 2 * (ring_size - 1), 0, came, shapes, placed)
        ties = {
            1: [*waves[1], *late],
            5: [normed.get("tokens_came")],
            6: [normed.get("gains")],
            7: late,
            8: late,
        }
        chunks = [after(chunks[0], *ties.get(number, ())), chunks[1]]
        placed = unpack(plan, experts + 2 * step, wave, chunks, shapes, placed)
        last = placed[0:1]
        if number == 2:
            back_to_tokens(last)
        if number == 9:
            block_rows(last)
    placed = unpack(
        plan,
        experts + 2 * (ring_size - 1),
        1,
        [after(got[k], *last) for k in range(2)],
        shapes,
        placed,
    )
    last = placed[0:1]
    while late_got is not None:
        late_done += 1
        for k in range(2):
            late_finish(k, after(late_got[k], *last))
        late_got = [send(late[k], k) for k in range(2)] if late_done < late_total else None
    gate_grad, up_grad, down_grad = placed
    shapes = [w.shape for w in (w_shared_gate, w_shared_up, w_shared_down)]
    shapes += [w.shape for w in (w_query, w_key, w_value, w_out)] + [gains.shape]
    finals = unpack_late(plan, chunks_first + late_total, late_out, shapes)
    shared_gate_grad, shared_up_grad, shared_down_grad = finals[0:3]
    query_grad, key_grad, value_grad, out_proj_grad, gain_grads = finals[3:8]


    return (
        normed["block_out"],
        normed["tokens_grad"],
        gain_grads[0],
        query_grad,
        key_grad,
        value_grad,
        out_proj_grad,
        gain_grads[1],
        gate_grad,
        up_grad,
        down_grad,
        shared_gate_grad,
        shared_up_grad,
        shared_down_grad,
    )


def solution(mesh):
    in_specs = (
        P(("dp", "row"), "col"),
        P("col"),
        P("col", "row"),
        P("col", "row"),
        P("col", "row"),
        P("row", "col"),
        P("col"),
        P(None, "col", "row"),
        P(None, "col", "row"),
        P(None, "row", "col"),
        P("col", "row"),
        P("col", "row"),
        P("row", "col"),
        P("dp", None),
        P("dp", None),
        P("dp"),
        P(("dp", "row"), "col"),
    )
    out_specs = (
        P(("dp", "row"), "col"),
        P(("dp", "row"), "col"),
        P("col"),
        P("col", "row"),
        P("col", "row"),
        P("col", "row"),
        P("row", "col"),
        P("col"),
        P(None, "col", "row"),
        P(None, "col", "row"),
        P(None, "row", "col"),
        P("col", "row"),
        P("col", "row"),
        P("row", "col"),
    )
    return jax.shard_map(body, mesh=mesh, in_specs=in_specs, out_specs=out_specs, check_vma=False)
```

```python
import functools

import jax
import jax.numpy as jnp
import numpy as np
from jax import lax
from jax.experimental import pallas as pl
from jax.experimental.pallas import tpu as pltpu
from jax.sharding import PartitionSpec as P

D = 1536
HQ = 12
HK = 4
DH = 128
GROUP_HEADS = HQ // HK
LANES = 128

EPSILON = 1e-05
F32 = jnp.float32
BF16 = jnp.bfloat16
MIB = 1024 * 1024
SMALL = pl.CostEstimate(flops=0, bytes_accessed=0, transcendentals=0)


def params(mib, *semantics):
    return pltpu.CompilerParams(
        dimension_semantics=semantics or None, vmem_limit_bytes=mib * MIB
    )


def dot(left, right):
    return jnp.dot(left, right, preferred_element_type=F32)


def dot_nt(left, right):
    return lax.dot_general(left, right, (((1,), (1,)), ((), ())), preferred_element_type=F32)


def dot_tn(left, right):
    return lax.dot_general(left, right, (((0,), (0,)), ((), ())), preferred_element_type=F32)


def after(values, *others):
    return lax.optimization_barrier((values, *others))[0]


def swap(values, axis):
    return lax.ppermute(values, axis, [(0, 1), (1, 0)])


def halves(values, axis, mine):
    size = values.shape[axis] // 2
    low = lax.slice_in_dim(values, 0, size, axis=axis)
    high = lax.slice_in_dim(values, size, 2 * size, axis=axis)
    return jnp.where(mine == 0, low, high), jnp.where(mine == 0, high, low)


def in_order(own, other, mine, axis):
    return jnp.concatenate(
        [jnp.where(mine == 0, own, other), jnp.where(mine == 0, other, own)], axis=axis
    )


def gather_rows(place_ref, own_ref, other_ref, all_ref):
    row = place_ref[0]
    rows = own_ref.shape[0]
    all_ref[pl.ds(pl.multiple_of(row * rows, rows), rows), :] = own_ref[...]
    all_ref[pl.ds(pl.multiple_of((1 - row) * rows, rows), rows), :] = other_ref[...]


def head_rows(ref, first, block):
    return jnp.concatenate(
        [ref[first : first + block, h * DH : (h + 1) * DH] for h in range(GROUP_HEADS)], axis=0
    )


def key_probs(query, key, first, length):
    block, keys = query.shape[0] // GROUP_HEADS, key.shape[0]
    scores = dot_nt(query, key) * DH ** (-0.5)
    shape = (block, keys)
    query_at = lax.broadcasted_iota(jnp.int32, shape, 0) + first
    key_at = lax.broadcasted_iota(jnp.int32, shape, 1)
    allowed = (key_at <= query_at) & (key_at < length)
    allowed = jnp.concatenate([allowed] * GROUP_HEADS, axis=0)
    scores = jnp.where(allowed, scores, -1e30)
    weights = jnp.exp(scores - jnp.max(scores, axis=1, keepdims=True))
    return weights * (1.0 / jnp.sum(weights, axis=1, keepdims=True))


def attend_kernel(place_ref, own_ref, other_ref, out_ref, all_ref):
    gather_rows(place_ref, own_ref, other_ref, all_ref)
    rows = own_ref.shape[0]
    block = 256
    width = GROUP_HEADS * DH
    for at in range(2 * rows // block):
        first, keys = at * block, (at + 1) * block
        query = head_rows(all_ref, first, block)
        key = all_ref[0:keys, width : width + DH]
        value = all_ref[0:keys, width + DH : width + 2 * DH]
        probs = key_probs(query, key, first, place_ref[1])
        result = dot(probs.astype(BF16), value).astype(BF16)
        for h in range(GROUP_HEADS):
            out_ref[first : first + block, h * DH : (h + 1) * DH] = result[
                h * block : (h + 1) * block
            ]


def attend(place, own, other):
    rows, width = own.shape
    spec = pl.BlockSpec(memory_space=pltpu.VMEM)
    return pl.pallas_call(
        attend_kernel,
        out_shape=jax.ShapeDtypeStruct((2 * rows, GROUP_HEADS * DH), BF16),
        in_specs=[pl.BlockSpec(memory_space=pltpu.SMEM), spec, spec],
        out_specs=spec,
        scratch_shapes=[pltpu.VMEM((2 * rows, width), BF16)],
        compiler_params=params(32),
        cost_estimate=SMALL,
        name="attend",
    )(place, own, other)


def attend_back_kernel(
    place_ref, own_ref, other_ref, grad_ref, grad_c_ref, out_ref, out_c_ref, result_ref, all_ref, total_ref
):
    gather_rows(place_ref, own_ref, other_ref, all_ref)
    rows = own_ref.shape[0]
    block = 256
    width = GROUP_HEADS * DH
    group = pl.ds(pl.multiple_of(place_ref[2] * width, width), width)
    blocks = 2 * rows // block
    for at in reversed(range(blocks)):
        first, keys = at * block, (at + 1) * block
        query = head_rows(all_ref, first, block)
        key = all_ref[0:keys, width : width + DH]
        value = all_ref[0:keys, width + DH : width + 2 * DH]
        probs = key_probs(query, key, first, place_ref[1])
        grad = dot_nt(grad_ref[first:keys, :], out_ref[group, :])
        grad = (grad + dot_nt(grad_c_ref[first:keys, :], out_c_ref[group, :])).astype(BF16)
        grad = jnp.concatenate(
            [grad[:, h * DH : (h + 1) * DH] for h in range(GROUP_HEADS)], axis=0
        )
        probs_grad = dot_nt(grad, value)
        carried = jnp.sum(probs * probs_grad, axis=1, keepdims=True)
        score_grad = (probs * (probs_grad - carried)).astype(BF16)
        query_back = (dot(score_grad, key) * DH ** (-0.5)).astype(BF16)
        for h in range(GROUP_HEADS):
            result_ref[first:keys, h * DH : (h + 1) * DH] = query_back[
                h * block : (h + 1) * block
            ]
        key_back = dot_tn(score_grad, query)
        value_back = dot_tn(probs.astype(BF16), grad)
        if at == blocks - 1:
            total_ref[:, 0:DH] = key_back
            total_ref[:, DH:] = value_back
        else:
            total_ref[0:keys, 0:DH] += key_back
            total_ref[0:keys, DH:] += value_back
    result_ref[:, width : width + DH] = (total_ref[:, 0:DH] * DH ** (-0.5)).astype(BF16)
    result_ref[:, width + DH :] = total_ref[:, DH:].astype(BF16)


def attend_back(place, own, other, grad, grad_c, w_out, out_c):
    rows, width = own.shape
    spec = pl.BlockSpec(memory_space=pltpu.VMEM)
    return pl.pallas_call(
        attend_back_kernel,
        out_shape=jax.ShapeDtypeStruct((2 * rows, width), BF16),
        in_specs=[pl.BlockSpec(memory_space=pltpu.SMEM)] + [spec] * 6,
        out_specs=spec,
        scratch_shapes=[
            pltpu.VMEM((2 * rows, width), BF16),
            pltpu.VMEM((2 * rows, 2 * DH), F32),
        ],
        compiler_params=params(60),
        cost_estimate=SMALL,
        name="attend_back",
    )(place, own, other, grad, grad_c, w_out, out_c)


def late_kernel(place_ref, *refs):
    near, near_c, far, far_c, qkv_ref, attended_ref, grad_ref, grad_c_ref = refs[0:8]
    shared = refs[8:10]
    outs = refs[10:12]
    rows, features = near.shape
    own_rows = pl.ds(pl.multiple_of(place_ref[0] * rows, rows), rows)
    far_rows = pl.ds(pl.multiple_of((1 - place_ref[0]) * rows, rows), rows)
    split = 7 * LANES

    def store(h, at, values):
        values = values.astype(BF16)
        for part in range(2):
            low, high = max(at, part * split), min(at + values.shape[1], (part + 1) * split)
            if low < high:
                piece = values[:, low - at : high - at]
                to = slice(low - part * split, high - part * split)

                @pl.when(place_ref[2] == 0)
                def _(part=part, to=to, piece=piece):
                    outs[part][h, :, to] = piece

                @pl.when(place_ref[2] != 0)
                def _(part=part, to=to, piece=piece):
                    outs[1 - part][h, :, to] = piece

    for h, (x, y, grad) in enumerate(((near, far, grad_ref), (near_c, far_c, grad_c_ref))):
        for k in range(2):
            store(h, 3 * LANES * k, shared[k][0, h * features : (h + 1) * features, :])
        project = dot_tn(x[...], qkv_ref[own_rows, :]) + dot_tn(y[...], qkv_ref[far_rows, :])
        store(h, 6 * LANES, project)
        store(h, 11 * LANES, dot_tn(grad[...], attended_ref[...]))


def late_grads(place, near, far, qkv_grad, attended, grad, grad_c, shared):
    features = near[0].shape[1]
    spec = pl.BlockSpec(memory_space=pltpu.VMEM)
    return pl.pallas_call(
        late_kernel,
        out_shape=[jax.ShapeDtypeStruct((2, features, 7 * LANES), BF16)] * 2,
        in_specs=[pl.BlockSpec(memory_space=pltpu.SMEM)] + [spec] * 10,
        out_specs=[spec] * 2,
        compiler_params=params(60),
        cost_estimate=SMALL,
        name="late_grads",
    )(place, *near, *far, qkv_grad, attended, grad, grad_c, *shared)


def columns_kernel(
    place_ref, query_ref, key_ref, value_ref, w_out_ref, out_ref, share_ref
):
    share_ref[...] = w_out_ref[...]
    width = GROUP_HEADS * DH
    out_ref[:, 0:width] = query_ref[...]
    out_ref[:, width : width + DH] = key_ref[...]
    out_ref[:, width + DH :] = value_ref[...]


def their_columns(place, w_query, w_key, w_value, w_out, shares):
    rows = w_query.shape[0]
    width = GROUP_HEADS * DH + 2 * DH

    def theirs(width):
        return pl.BlockSpec((rows, width), lambda i, c: (0, 1 - c[0]))

    return pl.pallas_call(
        columns_kernel,
        grid_spec=pltpu.PrefetchScalarGridSpec(
            num_scalar_prefetch=1,
            grid=(1,),
            in_specs=[theirs(GROUP_HEADS * DH), theirs(DH), theirs(DH)]
            + [pl.BlockSpec((rows // shares, rows), lambda i, c: (c[1], 0))],
            out_specs=[
                pl.BlockSpec((rows, width), lambda i, c: (0, 0)),
                pl.BlockSpec((rows // shares, rows), lambda i, c: (0, 0)),
            ],
        ),
        out_shape=[
            jax.ShapeDtypeStruct((rows, width), BF16),
            jax.ShapeDtypeStruct((rows // shares, rows), BF16),
        ],
        compiler_params=params(60, "arbitrary"),
        cost_estimate=SMALL,
        name="their_columns",
    )(place, w_query, w_key, w_value, w_out)


def join_kernel(mine_ref, *refs):
    *parts, out_ref = refs
    rows = parts[0].shape[0]
    for k, part in enumerate(parts):
        at = jnp.bitwise_xor(mine_ref[0], k)
        out_ref[pl.ds(pl.multiple_of(at * rows, rows), rows), :] = part[...]


def join(mine, *parts):
    rows, width = parts[0].shape
    spec = pl.BlockSpec(memory_space=pltpu.VMEM)
    return pl.pallas_call(
        join_kernel,
        out_shape=jax.ShapeDtypeStruct((len(parts) * rows, width), parts[0].dtype),
        in_specs=[pl.BlockSpec(memory_space=pltpu.SMEM)] + [spec] * len(parts),
        out_specs=spec,
        compiler_params=params(16),
        cost_estimate=SMALL,
        name="join",
    )(mine.reshape(1), *parts)


def project_kernel(col_ref, own_ref, other_ref, gains_ref, gains_c_ref, query_ref, key_ref, value_ref, there_ref, x_own_ref, x_other_ref, qkv_ref, scale_ref):
    own = own_ref[...].astype(F32)
    other = other_ref[...].astype(F32)
    total = jnp.sum(own * own, axis=1, keepdims=True)
    total = total + jnp.sum(other * other, axis=1, keepdims=True)
    scale = lax.rsqrt(total / D + EPSILON)
    own = (own * scale * gains_ref[0:1, :]).astype(BF16)
    other = (other * scale * gains_c_ref[0:1, :]).astype(BF16)
    x_own_ref[...] = own
    x_other_ref[...] = other
    scale_ref[...] = scale
    here = jnp.concatenate([query_ref[...], key_ref[...], value_ref[...]], axis=1)
    qkv_ref[...] = (dot(own, here) + dot(other, there_ref[...])).astype(BF16)


def project(col, own, other, gains, gains_c, w_query, w_key, w_value, there):
    rows, features = own.shape
    width = there.shape[1]
    group = GROUP_HEADS * DH
    tile = rows // 2

    def whole(*shape):
        return pl.BlockSpec(shape, lambda i, c: (0,) * len(shape))

    def mine(width):
        return pl.BlockSpec((features, width), lambda i, c: (0, c[0]))

    def rowwise(width):
        return pl.BlockSpec((tile, width), lambda i, c: (i, 0))

    return pl.pallas_call(
        project_kernel,
        grid_spec=pltpu.PrefetchScalarGridSpec(
            num_scalar_prefetch=1,
            grid=(rows // tile,),
            in_specs=[
                rowwise(features),
                rowwise(features),
                whole(2, features),
                whole(2, features),
                mine(group),
                mine(DH),
                mine(DH),
                whole(features, width),
            ],
            out_specs=[rowwise(features), rowwise(features), rowwise(width), rowwise(1)],
        ),
        out_shape=[
            jax.ShapeDtypeStruct((rows, features), BF16),
            jax.ShapeDtypeStruct((rows, features), BF16),
            jax.ShapeDtypeStruct((rows, width), BF16),
            jax.ShapeDtypeStruct((rows, 1), F32),
        ],
        compiler_params=params(60, "arbitrary"),
        cost_estimate=SMALL,
        name="project",
    )(col, own, other, gains, gains_c, w_query, w_key, w_value, there)


def head_pair(col_ref, own, other):
    first, second = own[...], other[...]
    flipped = col_ref != 0
    return jnp.concatenate(
        [jnp.where(flipped, second, first), jnp.where(flipped, first, second)], axis=1
    )


def before_kernel(tiles, place_ref, *refs):
    near, near_c, far, far_c, attended, attended_c, here, there, own_ref, other_ref = refs
    is_near = (pl.program_id(0) >= tiles // 2).astype(jnp.int32) == place_ref[0]
    heads = head_pair(place_ref[2], attended, attended_c)
    own = jnp.where(is_near, near[...], far[...]).astype(F32)
    other = jnp.where(is_near, near_c[...], far_c[...]).astype(F32)
    own_ref[...] = own + dot(heads, here[...])
    other_ref[...] = other + dot(heads, there[...])


def after_kernel(place_ref, *refs):
    own_ref, other_ref, attended, attended_c, here, there, gains_ref, gains_c_ref = refs[0:8]
    hidden_ref, x_own_ref, x_other_ref, scale_ref = refs[8:12]
    heads = head_pair(place_ref[2], attended, attended_c)
    own = own_ref[...] + dot(heads, here[...])
    other = other_ref[...] + dot(heads, there[...])
    total = jnp.sum(own * own, axis=1, keepdims=True)
    total = total + jnp.sum(other * other, axis=1, keepdims=True)
    scale = lax.rsqrt(total / D + EPSILON)
    hidden_ref[...] = own
    scale_ref[...] = scale
    x_own_ref[...] = (own * scale * gains_ref[1:2, :]).astype(BF16)
    x_other_ref[...] = (other * scale * gains_c_ref[1:2, :]).astype(BF16)


TOKEN_TILE = 256


def rowwise(width):
    return pl.BlockSpec((TOKEN_TILE, width), lambda i, p: (i, 0))


def whole(*shape):
    return pl.BlockSpec(shape, lambda i, p: (0,) * len(shape))


def hidden_before(place, tokens, attended, here, there):
    half, features = tokens[0].shape
    rows, heads = attended[0].shape
    tiles = rows // TOKEN_TILE
    per_half = half // TOKEN_TILE
    halfwise = pl.BlockSpec((TOKEN_TILE, features), lambda i, p: (i % per_half, 0))
    return pl.pallas_call(
        functools.partial(before_kernel, tiles),
        grid_spec=pltpu.PrefetchScalarGridSpec(
            num_scalar_prefetch=1,
            grid=(tiles,),
            in_specs=[halfwise] * 4 + [rowwise(heads)] * 2 + [whole(2 * heads, features)] * 2,
            out_specs=[rowwise(features)] * 2,
        ),
        out_shape=[jax.ShapeDtypeStruct((rows, features), F32)] * 2,
        compiler_params=params(56, "arbitrary"),
        cost_estimate=pl.CostEstimate(
            flops=8 * rows * features * heads,
            bytes_accessed=16 * rows * features,
            transcendentals=0,
        ),
        name="hidden_before",
    )(place, *tokens, *attended, here, there)


def hidden_after(place, before, attended, here, there, gains, gains_c):
    rows, features = before[0].shape
    heads = attended[0].shape[1]
    return pl.pallas_call(
        after_kernel,
        grid_spec=pltpu.PrefetchScalarGridSpec(
            num_scalar_prefetch=1,
            grid=(rows // TOKEN_TILE,),
            in_specs=[rowwise(features)] * 2
            + [rowwise(heads)] * 2
            + [whole(2 * heads, features)] * 2
            + [whole(2, features)] * 2,
            out_specs=[rowwise(features)] * 3 + [rowwise(1)],
        ),
        out_shape=[
            jax.ShapeDtypeStruct((rows, features), F32),
            jax.ShapeDtypeStruct((rows, features), BF16),
            jax.ShapeDtypeStruct((rows, features), BF16),
            jax.ShapeDtypeStruct((rows, 1), F32),
        ],
        compiler_params=params(56, "arbitrary"),
        cost_estimate=SMALL,
        name="hidden_after",
    )(place, *before, *attended, here, there, gains, gains_c)


def expert_kernel(shared, aliased, first, order_ref, *refs):
    x_own, x_other, o_own, o_other, gates_ref = refs[0:5]
    weights = refs[5:17]
    grads = refs[17 + aliased : 19 + aliased]
    pair_ref, inner_ref = refs[19 + aliased : 21 + aliased]
    step = pl.program_id(0) + first
    rows, features = x_own.shape
    tile = 512
    up_own = jnp.concatenate([weights[k][0] for k in (0, 1, 6, 7)], axis=1)
    up_other = jnp.concatenate([weights[k][0] for k in (2, 3, 8, 9)], axis=1)
    down_own = jnp.concatenate([weights[k][0] for k in (4, 10)], axis=0)
    down_other = jnp.concatenate([weights[k][0] for k in (5, 11)], axis=0)

    def token_tile(t, carry):
        at = pl.ds(pl.multiple_of(t * tile, tile), tile)
        pre = dot(x_own[at, :], up_own) + dot(x_other[at, :], up_other)
        back = dot_nt(o_own[at, :], down_own) + dot_nt(o_other[at, :], down_other)
        for k in range(2):
            pre_gate = pre[:, 2 * k * LANES : (2 * k + 1) * LANES]
            pre_up = pre[:, (2 * k + 1) * LANES : (2 * k + 2) * LANES]
            inner_grad = back[:, k * LANES : (k + 1) * LANES]
            sigmoid = 1.0 / (1.0 + jnp.exp(-pre_gate))
            silu = pre_gate * sigmoid
            inner = silu * pre_up
            if not shared:
                shape = (gates_ref.shape[0], LANES)
                expert = lax.broadcasted_iota(jnp.int32, shape, 0) % (gates_ref.shape[0] // 3)
                chosen = (expert == order_ref[2 * step + k]).astype(F32).astype(BF16)
                gate = dot_tn(gates_ref[:, at], chosen)
                inner = gate * inner
                inner_grad = gate * inner_grad
            gate_grad = inner_grad * pre_up * (sigmoid * (1.0 + pre_gate * (1.0 - sigmoid)))
            inner_ref[0, at, k * LANES : (k + 1) * LANES] = inner.astype(BF16)
            pair_ref[0, at, 2 * k * LANES : (2 * k + 1) * LANES] = gate_grad.astype(BF16)
            pair_ref[0, at, (2 * k + 1) * LANES : (2 * k + 2) * LANES] = (
                inner_grad * silu
            ).astype(BF16)
        return carry

    lax.fori_loop(0, rows // tile, token_tile, 0)
    pairs = pair_ref[0]
    for h, x in enumerate((x_own, x_other)):
        wide = dot_tn(x[...], pairs).astype(BF16)
        for k in range(2):
            grads[k][0, h * features : (h + 1) * features, 0 : 2 * LANES] = wide[
                :, 2 * k * LANES : (2 * k + 2) * LANES
            ]
    inner = inner_ref[0]
    tile = 256
    for h, o in enumerate((o_own, o_other)):
        for j in range(features // tile):
            low = dot_tn(inner, o[:, j * tile : (j + 1) * tile]).astype(BF16)
            for k in range(2):
                for b in range(tile // LANES):
                    at = h * features + j * tile + b * LANES
                    grads[k][0, at : at + LANES, 2 * LANES :] = low[
                        k * LANES : (k + 1) * LANES, b * LANES : (b + 1) * LANES
                    ]


def expert_specs(features, place, wide, low):
    specs = []
    if wide:
        block = pl.BlockSpec((1, features, LANES), lambda i, o: (place(i, o)[0], 0, place(i, o)[1]))
        specs += [block] * 4
    if low:
        block = pl.BlockSpec((1, LANES, features), lambda i, o: (*place(i, o), 0))
        specs += [block] * 2
    return specs


def expert_grads(order, first, last, total, x, o, gates, weights, kept):
    shared = total is None
    steps = last - first
    rows, features = x[0].shape
    aliased = len(kept)

    def fixed(*shape):
        return pl.BlockSpec(shape, lambda i, o: (0,) * len(shape))

    def stepped(*shape):
        return pl.BlockSpec((1, *shape), lambda i, o: (i, 0, 0))

    def placed(*shape):
        return pl.BlockSpec((1, *shape), lambda i, o: (i + first, 0, 0))

    specs = []
    for k in range(2):
        if shared:

            def picked(i, o, k=k):
                return 0, 2 * o[o.shape[0] - 1] + k

        else:

            def picked(i, o, k=k):
                return o[2 * (i + first) + k], o[o.shape[0] - 1]

        specs += expert_specs(features, picked, True, True)
    total = steps if shared else total
    return pl.pallas_call(
        functools.partial(expert_kernel, shared, aliased, first),
        grid_spec=pltpu.PrefetchScalarGridSpec(
            num_scalar_prefetch=1,
            grid=(steps,),
            in_specs=[fixed(rows, features)] * 4
            + [fixed(*gates.shape)]
            + specs
            + [pl.BlockSpec(memory_space=pl.ANY)] * aliased,
            out_specs=[stepped(2 * features, 3 * LANES)] * 2
            + [placed(rows, 4 * LANES), placed(rows, 2 * LANES)],
        ),
        out_shape=[jax.ShapeDtypeStruct((steps, 2 * features, 3 * LANES), BF16)] * 2
        + [
            jax.ShapeDtypeStruct((total, rows, 4 * LANES), BF16),
            jax.ShapeDtypeStruct((total, rows, 2 * LANES), BF16),
        ],
        input_output_aliases={18 + k: 2 + k for k in range(aliased)},
        compiler_params=params(40, "arbitrary"),
        cost_estimate=SMALL,
        name="expert_grads",
    )(order, *x, *o, gates, *weights, *weights, *kept)


def mix_kernel(back, group, order_ref, *refs):
    acts_ref, shared_ref = refs[0:2]
    each = 2 if back else 1
    count = 2 * group * each
    weights = refs[2 : 2 + count]
    shared = refs[2 + count : 2 + count + 2 * each]
    out_ref, total_ref = refs[2 + count + 2 * each :]
    step = pl.program_id(0)
    rows = out_ref.shape[0]
    tile = 512
    times = dot_nt if back else dot
    along = 1 if back else 0

    @pl.when(step == 0)
    def _():
        both = jnp.concatenate([w[0] for w in shared], axis=along)
        for t in range(rows // tile):
            at = slice(t * tile, (t + 1) * tile)
            total_ref[at, :] = times(shared_ref[0, at, :], both)

    both = jnp.concatenate([w[0] for w in weights], axis=along)
    for t in range(rows // tile):
        at = slice(t * tile, (t + 1) * tile)
        acts = jnp.concatenate([acts_ref[g, at, :] for g in range(group)], axis=1)
        total_ref[at, :] += times(acts, both)

    @pl.when(step == pl.num_programs(0) - 1)
    def _():
        out_ref[...] = total_ref[...].astype(out_ref.dtype)


def mix(back, dtype, order, acts, shared_acts, weights, shared_weights):
    pairs, rows, width = acts.shape
    features = weights[0].shape[1] if back else weights[0].shape[2]
    group = 4 if pairs % 4 == 0 else 1

    def spec(place):
        if back:
            return pl.BlockSpec((1, features, LANES), lambda i, o: (place(i, o)[0], 0, place(i, o)[1]))
        return pl.BlockSpec((1, LANES, features), lambda i, o: (*place(i, o), 0))

    def routed(k):
        return spec(lambda i, o: (o[2 * group * i + k], o[o.shape[0] - 1]))

    def common(k):
        return spec(lambda i, o: (0, 2 * o[o.shape[0] - 1] + k))

    return pl.pallas_call(
        functools.partial(mix_kernel, back, group),
        grid_spec=pltpu.PrefetchScalarGridSpec(
            num_scalar_prefetch=1,
            grid=(pairs // group,),
            in_specs=[
                pl.BlockSpec((group, rows, width), lambda i, o: (i, 0, 0)),
                pl.BlockSpec((1, rows, width), lambda i, o: (0, 0, 0)),
            ]
            + [routed(k) for k in range(2 * group) for _ in weights]
            + [common(k) for k in range(2) for _ in weights],
            out_specs=pl.BlockSpec((rows, features), lambda i, o: (0, 0)),
            scratch_shapes=[pltpu.VMEM((rows, features), F32)],
        ),
        out_shape=jax.ShapeDtypeStruct((rows, features), dtype),
        compiler_params=params(48, "arbitrary"),
        cost_estimate=SMALL,
        name="mix",
    )(order, acts, shared_acts, *weights * (2 * group), *shared_weights * 2)


def ring_of(size):
    return list(range(0, size, 2)) + list(range(1, size, 2))[::-1]


def unpack_kernel(aliased, plan_ref, *refs):
    chunks = refs[0:2]
    gate_ref, up_ref, down_ref = refs[2 + aliased : 5 + aliased]
    blocks = chunks[0].shape[1] // LANES

    def write(chunk_ref):
        gate_ref[0] = chunk_ref[0, :, 0:LANES].astype(F32)
        up_ref[0] = chunk_ref[0, :, LANES : 2 * LANES].astype(F32)
        for b in range(blocks):
            at = slice(b * LANES, (b + 1) * LANES)
            down_ref[0, :, at] = chunk_ref[0, at, 2 * LANES :].astype(F32)

    for k in range(2):
        pl.when(pl.program_id(1) == k)(lambda k=k: write(chunks[k]))


def unpack(plan, first, wave, chunks, shapes, outs):
    count, rows, width = chunks[0].shape
    chunk = pl.BlockSpec((1, rows, width), lambda i, d, n: (i, 0, 0))

    def place(i, d, n):
        block = n[n.shape[0] - 1]
        return n[first + 2 * i + d], 1 - block if wave else block

    def wide(i, d, n):
        expert, block = place(i, d, n)
        return (expert, 0, block)

    def low(i, d, n):
        expert, block = place(i, d, n)
        return (expert, block, 0)

    aliased = len(outs)
    return pl.pallas_call(
        functools.partial(unpack_kernel, aliased),
        grid_spec=pltpu.PrefetchScalarGridSpec(
            num_scalar_prefetch=1,
            grid=(count, 2),
            in_specs=[chunk, chunk] + [pl.BlockSpec(memory_space=pl.ANY)] * aliased,
            out_specs=[
                pl.BlockSpec((1, rows, LANES), wide),
                pl.BlockSpec((1, rows, LANES), wide),
                pl.BlockSpec((1, LANES, rows), low),
            ],
        ),
        out_shape=[jax.ShapeDtypeStruct(shape, F32) for shape in shapes],
        input_output_aliases={3 + k: k for k in range(aliased)},
        compiler_params=params(16, "arbitrary", "arbitrary"),
        cost_estimate=SMALL,
        name="unpack",
    )(plan, *chunks, *outs)


def late_chunk_kernel(plan_ref, pack_ref, *refs):
    *came, out_ref = refs
    if came:
        out_ref[...] = (came[0][...].astype(F32) + pack_ref[:, 0].astype(F32)).astype(BF16)
    else:
        out_ref[...] = pack_ref[:, 0]


def late_chunk(plan, at, pack, came):
    halves, _, rows, lanes = pack.shape
    spec = pl.BlockSpec((halves, rows, lanes), lambda i, n: (0, 0, 0))
    return pl.pallas_call(
        late_chunk_kernel,
        grid_spec=pltpu.PrefetchScalarGridSpec(
            num_scalar_prefetch=1,
            grid=(1,),
            in_specs=[pl.BlockSpec((halves, 1, rows, lanes), lambda i, n: (0, n[at], 0, 0))]
            + [spec] * len(came),
            out_specs=spec,
        ),
        out_shape=jax.ShapeDtypeStruct((halves, rows, lanes), BF16),
        compiler_params=params(16, "arbitrary"),
        cost_estimate=SMALL,
        name="late_chunk",
    )(plan, pack, *came)


def unpack_late_kernel(first_step, steps, plan_ref, *refs):
    chunks = refs[0 : 2 * steps]
    sgate, sup, sdown, query, key, value, out, all_ref = refs[2 * steps :]
    rows, features = chunks[0].shape[1], all_ref.shape[2]
    for k in range(2):
        for step in range(steps):
            at = plan_ref[first_step + 2 * step + k] * rows
            for c in range(2):
                all_ref[k, c, pl.ds(pl.multiple_of(at, rows), rows), :] = chunks[
                    steps * k + step
                ][c]
    flipped = plan_ref[plan_ref.shape[0] - 1] != 0
    for c in range(2):
        for b in range(14):
            lanes = slice(b % 7 * LANES, (b % 7 + 1) * LANES)
            first, second = all_ref[0, c, :, lanes], all_ref[1, c, :, lanes]
            if b >= 7:
                first, second = second, first
            block = jnp.where(flipped, second, first).astype(F32)
            if b < 6:
                at = slice((2 * c + b // 3) * LANES, (2 * c + b // 3 + 1) * LANES)
                if b % 3 < 2:
                    (sgate, sup)[b % 3][:, at] = block
                else:
                    for k in range(features // LANES):
                        here = slice(k * LANES, (k + 1) * LANES)
                        sdown[at, here] = block[here, :]
            elif b < 9:
                at = (GROUP_HEADS * c + b - 6) * LANES
                query[:, at : at + LANES] = block
            elif b < 11:
                (key, value)[b - 9][:, c * LANES : (c + 1) * LANES] = block
            else:
                at = (GROUP_HEADS * c + b - 11) * LANES
                out[at : at + LANES, :] = block.T


def unpack_late(plan, first_step, chunks, shapes):
    steps = len(chunks[0])
    halves, rows, lanes = chunks[0][0].shape
    spec = pl.BlockSpec(memory_space=pltpu.VMEM)
    return pl.pallas_call(
        functools.partial(unpack_late_kernel, first_step, steps),
        in_specs=[pl.BlockSpec(memory_space=pltpu.SMEM)] + [spec] * (2 * steps),
        out_specs=[spec] * len(shapes),
        out_shape=[jax.ShapeDtypeStruct(shape, F32) for shape in shapes],
        scratch_shapes=[pltpu.VMEM((2, halves, steps * rows, lanes), BF16)],
        compiler_params=params(48),
        cost_estimate=SMALL,
        name="unpack_late",
    )(plan, *chunks[0], *chunks[1])


def plans(ring, each):
    size = len(ring)
    rows = []
    for member in range(size):
        place = ring.index(member)
        for col in range(2):
            chunks = []
            for step in range(2 * size - 1):
                for which in range(2):
                    sign = 1 if which == col else -1
                    chunks.append((place - sign * step) % size)
            experts = []
            for start in (0, size - 1):
                for step in range(start, start + size):
                    for k in range(each):
                        for which in range(2):
                            second = col if which == 0 else 1 - col
                            experts.append(2 * each * chunks[2 * step + which] + each * second + k)
            rows.append(experts + chunks + [col])
    return np.asarray(rows, np.int32)


LATE_ROUND = 1


def add_rounded(left, right):
    return (left.astype(F32) + right.astype(F32)).astype(BF16)


def body(
    tokens_in,
    norm_gain_attn,
    w_query,
    w_key,
    w_value,
    w_out,
    norm_gain_ffn,
    w_gate,
    w_up,
    w_down,
    w_shared_gate,
    w_shared_up,
    w_shared_down,
    routes,
    gate_weights,
    seq_lengths,
    out_grad,
):
    row = lax.axis_index("row")
    col = lax.axis_index("col")
    dp = lax.axis_index("dp")
    dp_size = lax.axis_size("dp")
    local_rows, local_features = tokens_in.shape
    experts = w_gate.shape[0]
    group_width = GROUP_HEADS * DH
    col_ref = col.reshape(1)

    ring_size = min(8, dp_size)
    ring = ring_of(ring_size)
    starts = range(0, dp_size, ring_size)
    rights = [
        (g + ring[k], g + ring[(k + 1) % ring_size]) for g in starts for k in range(ring_size)
    ]
    lefts = [(b, a) for a, b in rights]
    routes_of = [
        [(2 * a, 2 * b) for a, b in ways[0]] + [(2 * a + 1, 2 * b + 1) for a, b in ways[1]]
        for ways in ((rights, lefts), (lefts, rights))
    ]
    experts_each = experts // (2 * ring_size)
    plan = jnp.asarray(plans(ring, experts_each))
    plan = lax.dynamic_slice(
        plan, (2 * (dp % ring_size) + col, jnp.int32(0)), (1, plan.shape[1])
    ).reshape(-1)

    def send(values, which):
        if ring_size == 1:
            return values
        return lax.ppermute(values, ("dp", "col"), routes_of[which])

    def chunk_at(step, which):
        return plan[2 * experts + 2 * step + which]

    def across_rings(values):
        if len(starts) == 1:
            return values
        peers = [[g + k for g in starts] for k in range(ring_size)]
        return lax.psum(values, "dp", axis_index_groups=peers)

    where = jnp.stack([row, seq_lengths[0], col])
    tokens_y = swap(tokens_in, "row")
    tokens_c = swap(tokens_in, "col")
    count = min(ring_size, 4)
    member = dp % count
    there, out_y = their_columns(
        jnp.stack([col, member]), w_query, w_key, w_value, w_out, count
    )
    gains = jnp.stack([norm_gain_attn, norm_gain_ffn])
    there = swap(there, "col")
    gains_c = swap(gains, "col")

    def project_half(own, other):
        return project(col_ref, own, other, gains, gains_c, w_query, w_key, w_value, there)

    near = project_half(tokens_in, tokens_c)
    gate_c = swap(w_gate, "col")
    out_y = swap(out_y, "row")
    tokens_y = after(tokens_y, near[2], out_y)
    tokens_yc = swap(tokens_y, "col")
    grad_y = swap(after(out_grad, tokens_y), "row")
    far = project_half(tokens_y, tokens_yc)
    shares = [out_y]
    for k in range(1, count):
        part = out_y if k < 3 else after(out_y, far[2])
        shares.append(lax.ppermute(part, "dp", [(m, m ^ k) for m in range(dp_size)]))
    where = after(where, grad_y, *shares)

    w_sgate, w_sup, w_sdown = w_shared_gate[None], w_shared_up[None], w_shared_down[None]
    up_c = swap(after(w_up, gate_c, tokens_yc), "col")

    attended = attend(where, near[2], far[2])
    attended_y = swap(attended, "row")
    attended_c = swap(attended, "col")
    out_c = swap(after(w_out, tokens_yc), "col")
    before = hidden_before(
        where,
        [tokens_in, tokens_c, tokens_y, tokens_yc],
        [attended, attended_c],
        w_out,
        out_c,
    )
    down_c = swap(after(w_down, tokens_yc), "col")
    attended_y = after(attended_y, before[0])
    out_y = join(member, *shares)
    out_yc = swap(out_y, "col")
    attended_yc = swap(attended_y, "col")
    grad_own = join(row, out_grad, grad_y)
    grad_other = swap(grad_own, "col")
    hidden, x_own, x_other, scale_ffn = hidden_after(
        where, before, [attended_y, attended_yc], out_y, out_yc, gains, gains_c
    )
    sgate_c, sup_c, sdown_c = (
        swap(after(w, attended_yc), "col") for w in (w_sgate, w_sup, w_sdown)
    )

    choices = jnp.arange(experts, dtype=jnp.int32)[:, None]
    dense = sum(
        jnp.where(routes[:, k][None, :] == choices, gate_weights[:, k][None, :], 0.0)
        for k in range(routes.shape[1])
    )
    gates = []
    for _ in range(3):
        gates.append(lax.reduce_precision(dense, 8, 7))
        dense = dense - gates[-1]
    gates = jnp.concatenate(gates, axis=0).astype(BF16)

    each = experts_each
    order = plan
    pairs_total = experts // 2
    routed = [w_gate, w_up, gate_c, up_c, w_down, down_c]
    shared = [w_sgate, w_sup, sgate_c, sup_c, w_sdown, sdown_c]

    def run(first, last, order, kept):
        return expert_grads(
            order,
            first,
            last,
            pairs_total,
            [x_own, x_other],
            [grad_own, grad_other],
            gates,
            routed,
            kept,
        )

    first = run(0, each, order, ())
    kept = first[2:]
    sums = [first[0], first[1]]
    runs = {}
    mixed = {}

    def work_experts(first, last):
        def work(order):
            nonlocal kept
            result = run(first, last, order, tuple(kept))
            kept = result[2:]
            for at in range(first, last):
                runs[at] = (result[0], result[1], at - first)
            return kept[0]

        return work

    def work_shared(order):
        runs["shared"] = expert_grads(
            order, 0, 1, None, [x_own, x_other], [grad_own, grad_other], gates, shared, ()
        )
        return runs["shared"][2]

    def work_mix(back, half):
        def work(order):
            pick = slice(2 * half, 2 * half + 2) if back else slice(4 + half, 5 + half)
            mixed[back, half] = mix(
                back,
                BF16 if half else F32,
                order,
                kept[0 if back else 1],
                runs["shared"][2 if back else 3],
                routed[pick],
                shared[pick],
            )
            return mixed[back, half]

        return work

    start = row * local_rows

    def my_rows(values):
        return lax.dynamic_slice_in_dim(values, start, local_rows, axis=0)

    def their_rows(values):
        return lax.dynamic_slice_in_dim(values, local_rows - start, local_rows, axis=0)

    normed = {}

    def work_hidden(order):
        normed_grad = mixed[True, 0] + swap(mixed[True, 1], "col").astype(F32)
        came = swap(normed_grad.astype(BF16), "row")
        normed_grad = normed_grad + after(came, order).astype(F32)
        scaled = normed_grad * norm_gain_ffn
        products = jnp.sum(scaled * hidden, axis=1, keepdims=True)
        mean = (products + swap(products, "col")) / D
        normed["gain"] = jnp.sum(my_rows(normed_grad * hidden * scale_ffn), axis=0)
        normed["hidden"] = (
            grad_own.astype(F32) + scale_ffn * scaled - hidden * scale_ffn**3 * mean
        )
        normed["grad"] = normed["hidden"].astype(BF16)
        normed["grad_c"] = swap(normed["grad"], "col")
        return normed["grad"]

    def work_attend(order):
        normed["qkv"] = attend_back(
            after(where, order), near[2], far[2], normed["grad"], normed["grad_c"], w_out, out_c
        )
        return normed["qkv"]

    tasks = [work_experts(at, at + each) for at in range(each, pairs_total, each)]
    tasks += [work_shared, work_mix(True, 1), work_mix(True, 0), work_mix(False, 1), work_mix(False, 0)]
    tasks += [None] * (2 * ring_size - 3 - len(tasks)) + [work_hidden, work_attend]
    got = [None, None]
    if ring_size > 1:
        got[0] = send(sums[0], 0)
        tasks.pop(0)(after(order, *sums))
        got[1] = send(after(sums[1], kept[0]), 1)
    for s in range(1, ring_size):
        for k in range(2):
            last = sums
            task = tasks.pop(0) if tasks else None
            if task:
                last = [task(after(order, *last))]
            got[k] = after(got[k], *last)
            parts = [runs[at] for at in range(each * s, each * s + each)]
            mine = [p[k][p[2] : p[2] + 1] for p in parts]
            mine = mine[0] if each == 1 else jnp.concatenate(mine, axis=0)
            sums[k] = add_rounded(got[k], mine)
            if s + 1 < ring_size:
                got[k] = send(sums[k], k)
    for task in tasks:
        if task:
            task(after(order, *sums))
    sums = [across_rings(total) for total in sums]
    waves = [[total[:, :local_features] for total in sums]]
    crossed = [swap(total[:, local_features:], "col") for total in sums]
    waves.append([crossed[1], crossed[0]])

    hidden_grad, attn_grad, attn_grad_c = normed["hidden"], normed["grad"], normed["grad_c"]
    gain_ffn_part, qkv_grad = normed["gain"], normed["qkv"]
    packs = late_grads(
        where,
        near[0:2],
        far[0:2],
        qkv_grad,
        attended,
        attn_grad,
        attn_grad_c,
        runs["shared"][0:2],
    )

    packs = [
        pack.reshape(2, ring_size, local_features // ring_size, pack.shape[2]) for pack in packs
    ]
    chunks_first = 2 * experts
    late = [late_chunk(plan, chunks_first + k, packs[k], ()) for k in range(2)]
    late_out = [[], []]
    late_done = 0
    late_total = 2 * (ring_size - 1)

    def late_turn():
        totals = [across_rings(values) for values in late]
        others = [swap(values[1], "col") for values in totals]
        for k in range(2):
            late[k] = in_order(totals[k][0:1], others[1 - k][None], col, 0)
            late_out[k].append(late[k])

    def late_finish(k, values):
        if late_done < ring_size:
            at = chunks_first + 2 * late_done + k
            late[k] = late_chunk(plan, at, packs[k], (values,))
        else:
            late[k] = values
            late_out[k].append(values)

    shapes = [w_gate.shape, w_up.shape, w_down.shape]
    placed = ()

    def place_chunks(wave, step, chunks, placed):
        return unpack(plan, experts + 2 * each * step, wave, chunks, shapes, placed)

    if late_total == 0:
        late_turn()
    rounds = [(wave, step) for wave in range(2) for step in range(ring_size - 1)]
    late_got = None
    last = list(sums)
    for number, (wave, step) in enumerate(rounds):
        if step == 0:
            came = list(got) if number else None
            got = list(waves[wave])
        late_done += late_got is not None
        chunks = [None, None]
        for k in range(2):
            chunks[k] = after(got[k], *last)
            got[k] = send(chunks[k], k)
            last = [chunks[k]]
            if late_got is not None:
                late_finish(k, after(late_got[k], *last))
                last = [late[k]]
        if late_got is not None and late_done == ring_size - 1:
            late_turn()
        if number >= LATE_ROUND and late_done < late_total:
            late_got = [send(after(late[k], *chunks), k) for k in range(2)]
        else:
            late_got = None
        if step == 0 and number:
            placed = place_chunks(0, ring_size - 1, came, placed)
        placed = place_chunks(wave, step, chunks, placed)
        last = placed[0:1]
        if number == LATE_ROUND + 3:
            qkv_grad = after(qkv_grad, *last)
    if rounds:
        placed = place_chunks(1, ring_size - 1, [after(got[k], *last) for k in range(2)], placed)
        last = placed[0:1]
    while late_got is not None:
        late_done += 1
        for k in range(2):
            late_finish(k, after(late_got[k], *last))
        if late_done == ring_size - 1:
            late_turn()
        late_got = [send(late[k], k) for k in range(2)] if late_done < late_total else None
    if not rounds:
        for wave in range(2):
            placed = place_chunks(wave, 0, waves[wave], placed)
    gate_grad, up_grad, down_grad = placed
    shapes = [w.shape for w in (w_shared_gate, w_shared_up, w_shared_down)]
    shapes += [w.shape for w in (w_query, w_key, w_value, w_out)]
    finals = unpack_late(plan, chunks_first + late_total, late_out, shapes)
    shared_gate_grad, shared_up_grad, shared_down_grad = finals[0:3]
    query_grad, key_grad, value_grad, out_proj_grad = finals[3:7]

    ffn_sum = mixed[False, 0] + swap(mixed[False, 1], "col").astype(F32)
    ffn_rows = my_rows(ffn_sum) + swap(their_rows(ffn_sum).astype(BF16), "row").astype(F32)
    block_out = (my_rows(hidden) + ffn_rows).astype(BF16)

    here = jnp.concatenate(
        [halves(w, 1, col)[0] for w in (w_query, w_key, w_value)], axis=1
    )
    tokens_back = dot_nt(qkv_grad, here) + swap(
        dot_nt(qkv_grad, there).astype(BF16), "col"
    ).astype(F32)
    tokens_back = my_rows(tokens_back) + swap(
        their_rows(tokens_back).astype(BF16), "row"
    ).astype(F32)
    scale_attn = near[3]
    tokens_f32 = tokens_in.astype(F32)
    gain_attn_part = jnp.sum(tokens_back * tokens_f32 * scale_attn, axis=0)
    scaled = tokens_back * norm_gain_attn
    products = jnp.sum(scaled * tokens_f32, axis=1, keepdims=True)
    mean = (products + swap(products, "col")) / D
    tokens_grad = (
        my_rows(hidden_grad) + scale_attn * scaled - tokens_f32 * scale_attn**3 * mean
    ).astype(BF16)

    gain_parts = jnp.stack([gain_attn_part, gain_ffn_part])
    bit = 1
    while bit < ring_size:
        pairs = [(g + k, g + (k ^ bit)) for g in starts for k in range(ring_size)]
        gain_parts = gain_parts + lax.ppermute(gain_parts, "dp", pairs)
        bit *= 2
    gain_parts = across_rings(gain_parts + swap(gain_parts, "row"))

    return (
        block_out,
        tokens_grad,
        gain_parts[0],
        query_grad,
        key_grad,
        value_grad,
        out_proj_grad,
        gain_parts[1],
        gate_grad,
        up_grad,
        down_grad,
        shared_gate_grad,
        shared_up_grad,
        shared_down_grad,
    )


def solution(mesh):
    in_specs = (
        P(("dp", "row"), "col"),
        P("col"),
        P("col", "row"),
        P("col", "row"),
        P("col", "row"),
        P("row", "col"),
        P("col"),
        P(None, "col", "row"),
        P(None, "col", "row"),
        P(None, "row", "col"),
        P("col", "row"),
        P("col", "row"),
        P("row", "col"),
        P("dp", None),
        P("dp", None),
        P("dp"),
        P(("dp", "row"), "col"),
    )
    out_specs = (
        P(("dp", "row"), "col"),
        P(("dp", "row"), "col"),
        P("col"),
        P("col", "row"),
        P("col", "row"),
        P("col", "row"),
        P("row", "col"),
        P("col"),
        P(None, "col", "row"),
        P(None, "col", "row"),
        P(None, "row", "col"),
        P("col", "row"),
        P("col", "row"),
        P("row", "col"),
    )
    return jax.shard_map(body, mesh=mesh, in_specs=in_specs, out_specs=out_specs, check_vma=False)
```

```python
import functools

import jax
import jax.numpy as jnp
import numpy as np
from jax import lax
from jax.experimental import pallas as pl
from jax.experimental.pallas import tpu as pltpu
from jax.sharding import PartitionSpec as P

D = 1536
HQ = 12
HK = 4
DH = 128
GROUP_HEADS = HQ // HK
LANES = 128

EPSILON = 1e-05
F32 = jnp.float32
BF16 = jnp.bfloat16
MIB = 1024 * 1024
SMALL = pl.CostEstimate(flops=0, bytes_accessed=0, transcendentals=0)


def params(mib, *semantics):
    return pltpu.CompilerParams(
        dimension_semantics=semantics or None, vmem_limit_bytes=mib * MIB
    )


def dot(left, right):
    return jnp.dot(left, right, preferred_element_type=F32)


def dot_nt(left, right):
    return lax.dot_general(left, right, (((1,), (1,)), ((), ())), preferred_element_type=F32)


def dot_tn(left, right):
    return lax.dot_general(left, right, (((0,), (0,)), ((), ())), preferred_element_type=F32)


def after(values, *others):
    return lax.optimization_barrier((values, *others))[0]


def swap(values, axis):
    return lax.ppermute(values, axis, [(0, 1), (1, 0)])


def swap_halves(values):
    half = values.shape[0] // 2
    parts = [swap(values[:half], "col"), swap(values[half:], "col")]
    return jnp.concatenate(parts, axis=0)


def halves(values, axis, mine):
    size = values.shape[axis] // 2
    low = lax.slice_in_dim(values, 0, size, axis=axis)
    high = lax.slice_in_dim(values, size, 2 * size, axis=axis)
    return jnp.where(mine == 0, low, high), jnp.where(mine == 0, high, low)


def in_order(own, other, mine, axis):
    return jnp.concatenate(
        [jnp.where(mine == 0, own, other), jnp.where(mine == 0, other, own)], axis=axis
    )


def gather_rows(place_ref, own_ref, other_ref, all_ref):
    row = place_ref[0]
    rows = own_ref.shape[0]
    all_ref[pl.ds(pl.multiple_of(row * rows, rows), rows), :] = own_ref[...]
    all_ref[pl.ds(pl.multiple_of((1 - row) * rows, rows), rows), :] = other_ref[...]


def head_rows(ref, first, block):
    return jnp.concatenate(
        [ref[first : first + block, h * DH : (h + 1) * DH] for h in range(GROUP_HEADS)], axis=0
    )


def key_probs(query, key, first, length):
    block, keys = query.shape[0] // GROUP_HEADS, key.shape[0]
    scores = dot_nt(query, key) * DH ** (-0.5)
    shape = (block, keys)
    query_at = lax.broadcasted_iota(jnp.int32, shape, 0) + first
    key_at = lax.broadcasted_iota(jnp.int32, shape, 1)
    allowed = (key_at <= query_at) & (key_at < length)
    allowed = jnp.concatenate([allowed] * GROUP_HEADS, axis=0)
    scores = jnp.where(allowed, scores, -1e30)
    weights = jnp.exp(scores - jnp.max(scores, axis=1, keepdims=True))
    return weights * (1.0 / jnp.sum(weights, axis=1, keepdims=True))


def attend_kernel(place_ref, own_ref, other_ref, out_ref, all_ref):
    gather_rows(place_ref, own_ref, other_ref, all_ref)
    rows = own_ref.shape[0]
    block = 256
    width = GROUP_HEADS * DH
    for at in range(2 * rows // block):
        first, keys = at * block, (at + 1) * block
        query = head_rows(all_ref, first, block)
        key = all_ref[0:keys, width : width + DH]
        value = all_ref[0:keys, width + DH : width + 2 * DH]
        probs = key_probs(query, key, first, place_ref[1])
        result = dot(probs.astype(BF16), value).astype(BF16)
        for h in range(GROUP_HEADS):
            out_ref[first : first + block, h * DH : (h + 1) * DH] = result[
                h * block : (h + 1) * block
            ]


def attend(place, own, other):
    rows, width = own.shape
    spec = pl.BlockSpec(memory_space=pltpu.VMEM)
    return pl.pallas_call(
        attend_kernel,
        out_shape=jax.ShapeDtypeStruct((2 * rows, GROUP_HEADS * DH), BF16),
        in_specs=[pl.BlockSpec(memory_space=pltpu.SMEM), spec, spec],
        out_specs=spec,
        scratch_shapes=[pltpu.VMEM((2 * rows, width), BF16)],
        compiler_params=params(32),
        cost_estimate=SMALL,
        name="attend",
    )(place, own, other)


def attend_back_kernel(
    place_ref, own_ref, other_ref, grad_ref, grad_c_ref, out_ref, out_c_ref, result_ref, all_ref, total_ref
):
    gather_rows(place_ref, own_ref, other_ref, all_ref)
    rows = own_ref.shape[0]
    block = 256
    width = GROUP_HEADS * DH
    group = pl.ds(pl.multiple_of(place_ref[2] * width, width), width)
    blocks = 2 * rows // block
    for at in reversed(range(blocks)):
        first, keys = at * block, (at + 1) * block
        query = head_rows(all_ref, first, block)
        key = all_ref[0:keys, width : width + DH]
        value = all_ref[0:keys, width + DH : width + 2 * DH]
        probs = key_probs(query, key, first, place_ref[1])
        grad = dot_nt(grad_ref[first:keys, :], out_ref[group, :])
        grad = (grad + dot_nt(grad_c_ref[first:keys, :], out_c_ref[group, :])).astype(BF16)
        grad = jnp.concatenate(
            [grad[:, h * DH : (h + 1) * DH] for h in range(GROUP_HEADS)], axis=0
        )
        probs_grad = dot_nt(grad, value)
        carried = jnp.sum(probs * probs_grad, axis=1, keepdims=True)
        score_grad = (probs * (probs_grad - carried)).astype(BF16)
        query_back = (dot(score_grad, key) * DH ** (-0.5)).astype(BF16)
        for h in range(GROUP_HEADS):
            result_ref[first:keys, h * DH : (h + 1) * DH] = query_back[
                h * block : (h + 1) * block
            ]
        key_back = dot_tn(score_grad, query)
        value_back = dot_tn(probs.astype(BF16), grad)
        if at == blocks - 1:
            total_ref[:, 0:DH] = key_back
            total_ref[:, DH:] = value_back
        else:
            total_ref[0:keys, 0:DH] += key_back
            total_ref[0:keys, DH:] += value_back
    result_ref[:, width : width + DH] = (total_ref[:, 0:DH] * DH ** (-0.5)).astype(BF16)
    result_ref[:, width + DH :] = total_ref[:, DH:].astype(BF16)


def attend_back(place, own, other, grad, grad_c, w_out, out_c):
    rows, width = own.shape
    spec = pl.BlockSpec(memory_space=pltpu.VMEM)
    return pl.pallas_call(
        attend_back_kernel,
        out_shape=jax.ShapeDtypeStruct((2 * rows, width), BF16),
        in_specs=[pl.BlockSpec(memory_space=pltpu.SMEM)] + [spec] * 6,
        out_specs=spec,
        scratch_shapes=[
            pltpu.VMEM((2 * rows, width), BF16),
            pltpu.VMEM((2 * rows, 2 * DH), F32),
        ],
        compiler_params=params(60),
        cost_estimate=SMALL,
        name="attend_back",
    )(place, own, other, grad, grad_c, w_out, out_c)


def late_kernel(place_ref, *refs):
    near, near_c, far, far_c, qkv_ref, attended_ref, grad_ref, grad_c_ref = refs[0:8]
    shared = refs[8:10]
    outs = refs[10:12]
    rows, features = near.shape
    own_rows = pl.ds(pl.multiple_of(place_ref[0] * rows, rows), rows)
    far_rows = pl.ds(pl.multiple_of((1 - place_ref[0]) * rows, rows), rows)
    split = 7 * LANES

    def store(h, at, values):
        values = values.astype(BF16)
        for part in range(2):
            low, high = max(at, part * split), min(at + values.shape[1], (part + 1) * split)
            if low < high:
                piece = values[:, low - at : high - at]
                to = slice(low - part * split, high - part * split)

                @pl.when(place_ref[2] == 0)
                def _(part=part, to=to, piece=piece):
                    outs[part][h, :, to] = piece

                @pl.when(place_ref[2] != 0)
                def _(part=part, to=to, piece=piece):
                    outs[1 - part][h, :, to] = piece

    for h, (x, y, grad) in enumerate(((near, far, grad_ref), (near_c, far_c, grad_c_ref))):
        for k in range(2):
            store(h, 3 * LANES * k, shared[k][0, h * features : (h + 1) * features, :])
        project = dot_tn(x[...], qkv_ref[own_rows, :]) + dot_tn(y[...], qkv_ref[far_rows, :])
        store(h, 6 * LANES, project)
        store(h, 11 * LANES, dot_tn(grad[...], attended_ref[...]))


def late_grads(place, near, far, qkv_grad, attended, grad, grad_c, shared):
    features = near[0].shape[1]
    spec = pl.BlockSpec(memory_space=pltpu.VMEM)
    return pl.pallas_call(
        late_kernel,
        out_shape=[jax.ShapeDtypeStruct((2, features, 7 * LANES), BF16)] * 2,
        in_specs=[pl.BlockSpec(memory_space=pltpu.SMEM)] + [spec] * 10,
        out_specs=[spec] * 2,
        compiler_params=params(60),
        cost_estimate=SMALL,
        name="late_grads",
    )(place, *near, *far, qkv_grad, attended, grad, grad_c, *shared)


def columns_kernel(
    place_ref, query_ref, key_ref, value_ref, w_out_ref, out_ref, share_ref
):
    share_ref[...] = w_out_ref[...]
    width = GROUP_HEADS * DH
    out_ref[:, 0:width] = query_ref[...]
    out_ref[:, width : width + DH] = key_ref[...]
    out_ref[:, width + DH :] = value_ref[...]


def their_columns(place, w_query, w_key, w_value, w_out, shares):
    rows = w_query.shape[0]
    width = GROUP_HEADS * DH + 2 * DH

    def theirs(width):
        return pl.BlockSpec((rows, width), lambda i, c: (0, 1 - c[0]))

    return pl.pallas_call(
        columns_kernel,
        grid_spec=pltpu.PrefetchScalarGridSpec(
            num_scalar_prefetch=1,
            grid=(1,),
            in_specs=[theirs(GROUP_HEADS * DH), theirs(DH), theirs(DH)]
            + [pl.BlockSpec((rows // shares, rows), lambda i, c: (c[1], 0))],
            out_specs=[
                pl.BlockSpec((rows, width), lambda i, c: (0, 0)),
                pl.BlockSpec((rows // shares, rows), lambda i, c: (0, 0)),
            ],
        ),
        out_shape=[
            jax.ShapeDtypeStruct((rows, width), BF16),
            jax.ShapeDtypeStruct((rows // shares, rows), BF16),
        ],
        compiler_params=params(60, "arbitrary"),
        cost_estimate=SMALL,
        name="their_columns",
    )(place, w_query, w_key, w_value, w_out)


def join_kernel(mine_ref, *refs):
    *parts, out_ref = refs
    rows = parts[0].shape[0]
    for k, part in enumerate(parts):
        at = jnp.bitwise_xor(mine_ref[0], k)
        out_ref[pl.ds(pl.multiple_of(at * rows, rows), rows), :] = part[...]


def join(mine, *parts):
    rows, width = parts[0].shape
    spec = pl.BlockSpec(memory_space=pltpu.VMEM)
    return pl.pallas_call(
        join_kernel,
        out_shape=jax.ShapeDtypeStruct((len(parts) * rows, width), parts[0].dtype),
        in_specs=[pl.BlockSpec(memory_space=pltpu.SMEM)] + [spec] * len(parts),
        out_specs=spec,
        compiler_params=params(16),
        cost_estimate=SMALL,
        name="join",
    )(mine.reshape(1), *parts)


def project_kernel(col_ref, own_ref, other_ref, gains_ref, gains_c_ref, query_ref, key_ref, value_ref, there_ref, x_own_ref, x_other_ref, qkv_ref, scale_ref):
    own = own_ref[...].astype(F32)
    other = other_ref[...].astype(F32)
    total = jnp.sum(own * own, axis=1, keepdims=True)
    total = total + jnp.sum(other * other, axis=1, keepdims=True)
    scale = lax.rsqrt(total / D + EPSILON)
    own = (own * scale * gains_ref[0:1, :]).astype(BF16)
    other = (other * scale * gains_c_ref[0:1, :]).astype(BF16)
    x_own_ref[...] = own
    x_other_ref[...] = other
    scale_ref[...] = scale
    here = jnp.concatenate([query_ref[...], key_ref[...], value_ref[...]], axis=1)
    qkv_ref[...] = (dot(own, here) + dot(other, there_ref[...])).astype(BF16)


def project(col, own, other, gains, gains_c, w_query, w_key, w_value, there):
    rows, features = own.shape
    width = there.shape[1]
    group = GROUP_HEADS * DH
    tile = rows // 2

    def whole(*shape):
        return pl.BlockSpec(shape, lambda i, c: (0,) * len(shape))

    def mine(width):
        return pl.BlockSpec((features, width), lambda i, c: (0, c[0]))

    def rowwise(width):
        return pl.BlockSpec((tile, width), lambda i, c: (i, 0))

    return pl.pallas_call(
        project_kernel,
        grid_spec=pltpu.PrefetchScalarGridSpec(
            num_scalar_prefetch=1,
            grid=(rows // tile,),
            in_specs=[
                rowwise(features),
                rowwise(features),
                whole(2, features),
                whole(2, features),
                mine(group),
                mine(DH),
                mine(DH),
                whole(features, width),
            ],
            out_specs=[rowwise(features), rowwise(features), rowwise(width), rowwise(1)],
        ),
        out_shape=[
            jax.ShapeDtypeStruct((rows, features), BF16),
            jax.ShapeDtypeStruct((rows, features), BF16),
            jax.ShapeDtypeStruct((rows, width), BF16),
            jax.ShapeDtypeStruct((rows, 1), F32),
        ],
        compiler_params=params(60, "arbitrary"),
        cost_estimate=SMALL,
        name="project",
    )(col, own, other, gains, gains_c, w_query, w_key, w_value, there)


def head_pair(col_ref, own, other):
    first, second = own[...], other[...]
    flipped = col_ref != 0
    return jnp.concatenate(
        [jnp.where(flipped, second, first), jnp.where(flipped, first, second)], axis=1
    )


def before_kernel(tiles, place_ref, *refs):
    near, near_c, far, far_c, attended, attended_c, here, there, own_ref, other_ref = refs
    is_near = (pl.program_id(0) >= tiles // 2).astype(jnp.int32) == place_ref[0]
    heads = head_pair(place_ref[2], attended, attended_c)
    own = jnp.where(is_near, near[...], far[...]).astype(F32)
    other = jnp.where(is_near, near_c[...], far_c[...]).astype(F32)
    own_ref[...] = own + dot(heads, here[...])
    other_ref[...] = other + dot(heads, there[...])


def after_kernel(place_ref, *refs):
    own_ref, other_ref, attended, attended_c, here, there, gains_ref, gains_c_ref = refs[0:8]
    hidden_ref, x_own_ref, x_other_ref, scale_ref = refs[8:12]
    heads = head_pair(place_ref[2], attended, attended_c)
    own = own_ref[...] + dot(heads, here[...])
    other = other_ref[...] + dot(heads, there[...])
    total = jnp.sum(own * own, axis=1, keepdims=True)
    total = total + jnp.sum(other * other, axis=1, keepdims=True)
    scale = lax.rsqrt(total / D + EPSILON)
    hidden_ref[...] = own
    scale_ref[...] = scale
    x_own_ref[...] = (own * scale * gains_ref[1:2, :]).astype(BF16)
    x_other_ref[...] = (other * scale * gains_c_ref[1:2, :]).astype(BF16)


TOKEN_TILE = 256


def rowwise(width):
    return pl.BlockSpec((TOKEN_TILE, width), lambda i, p: (i, 0))


def whole(*shape):
    return pl.BlockSpec(shape, lambda i, p: (0,) * len(shape))


def hidden_before(place, tokens, attended, here, there):
    half, features = tokens[0].shape
    rows, heads = attended[0].shape
    tiles = rows // TOKEN_TILE
    per_half = half // TOKEN_TILE
    halfwise = pl.BlockSpec((TOKEN_TILE, features), lambda i, p: (i % per_half, 0))
    return pl.pallas_call(
        functools.partial(before_kernel, tiles),
        grid_spec=pltpu.PrefetchScalarGridSpec(
            num_scalar_prefetch=1,
            grid=(tiles,),
            in_specs=[halfwise] * 4 + [rowwise(heads)] * 2 + [whole(2 * heads, features)] * 2,
            out_specs=[rowwise(features)] * 2,
        ),
        out_shape=[jax.ShapeDtypeStruct((rows, features), F32)] * 2,
        compiler_params=params(56, "arbitrary"),
        cost_estimate=pl.CostEstimate(
            flops=8 * rows * features * heads,
            bytes_accessed=16 * rows * features,
            transcendentals=0,
        ),
        name="hidden_before",
    )(place, *tokens, *attended, here, there)


def hidden_after(place, before, attended, here, there, gains, gains_c):
    rows, features = before[0].shape
    heads = attended[0].shape[1]
    return pl.pallas_call(
        after_kernel,
        grid_spec=pltpu.PrefetchScalarGridSpec(
            num_scalar_prefetch=1,
            grid=(rows // TOKEN_TILE,),
            in_specs=[rowwise(features)] * 2
            + [rowwise(heads)] * 2
            + [whole(2 * heads, features)] * 2
            + [whole(2, features)] * 2,
            out_specs=[rowwise(features)] * 3 + [rowwise(1)],
        ),
        out_shape=[
            jax.ShapeDtypeStruct((rows, features), F32),
            jax.ShapeDtypeStruct((rows, features), BF16),
            jax.ShapeDtypeStruct((rows, features), BF16),
            jax.ShapeDtypeStruct((rows, 1), F32),
        ],
        compiler_params=params(56, "arbitrary"),
        cost_estimate=SMALL,
        name="hidden_after",
    )(place, *before, *attended, here, there, gains, gains_c)


def expert_kernel(shared, aliased, first, order_ref, *refs):
    x_own, x_other, o_own, o_other, gates_ref = refs[0:5]
    weights = refs[5:17]
    grads = refs[17 + aliased : 19 + aliased]
    pair_ref, inner_ref = refs[19 + aliased : 21 + aliased]
    step = pl.program_id(0) + first
    rows, features = x_own.shape
    tile = 512
    up_own = jnp.concatenate([weights[k][0] for k in (0, 1, 6, 7)], axis=1)
    up_other = jnp.concatenate([weights[k][0] for k in (2, 3, 8, 9)], axis=1)
    down_own = jnp.concatenate([weights[k][0] for k in (4, 10)], axis=0)
    down_other = jnp.concatenate([weights[k][0] for k in (5, 11)], axis=0)

    def token_tile(t, carry):
        at = pl.ds(pl.multiple_of(t * tile, tile), tile)
        pre = dot(x_own[at, :], up_own) + dot(x_other[at, :], up_other)
        back = dot_nt(o_own[at, :], down_own) + dot_nt(o_other[at, :], down_other)
        for k in range(2):
            pre_gate = pre[:, 2 * k * LANES : (2 * k + 1) * LANES]
            pre_up = pre[:, (2 * k + 1) * LANES : (2 * k + 2) * LANES]
            inner_grad = back[:, k * LANES : (k + 1) * LANES]
            sigmoid = 1.0 / (1.0 + jnp.exp(-pre_gate))
            silu = pre_gate * sigmoid
            inner = silu * pre_up
            if not shared:
                shape = (gates_ref.shape[0], LANES)
                expert = lax.broadcasted_iota(jnp.int32, shape, 0) % (gates_ref.shape[0] // 3)
                chosen = (expert == order_ref[2 * step + k]).astype(F32).astype(BF16)
                gate = dot_tn(gates_ref[:, at], chosen)
                inner = gate * inner
                inner_grad = gate * inner_grad
            gate_grad = inner_grad * pre_up * (sigmoid * (1.0 + pre_gate * (1.0 - sigmoid)))
            inner_ref[0, at, k * LANES : (k + 1) * LANES] = inner.astype(BF16)
            pair_ref[0, at, 2 * k * LANES : (2 * k + 1) * LANES] = gate_grad.astype(BF16)
            pair_ref[0, at, (2 * k + 1) * LANES : (2 * k + 2) * LANES] = (
                inner_grad * silu
            ).astype(BF16)
        return carry

    lax.fori_loop(0, rows // tile, token_tile, 0)
    pairs = pair_ref[0]
    for h, x in enumerate((x_own, x_other)):
        wide = dot_tn(x[...], pairs).astype(BF16)
        for k in range(2):
            grads[k][0, h * features : (h + 1) * features, 0 : 2 * LANES] = wide[
                :, 2 * k * LANES : (2 * k + 2) * LANES
            ]
    inner = inner_ref[0]
    tile = 256
    for h, o in enumerate((o_own, o_other)):
        for j in range(features // tile):
            low = dot_tn(inner, o[:, j * tile : (j + 1) * tile]).astype(BF16)
            for k in range(2):
                for b in range(tile // LANES):
                    at = h * features + j * tile + b * LANES
                    grads[k][0, at : at + LANES, 2 * LANES :] = low[
                        k * LANES : (k + 1) * LANES, b * LANES : (b + 1) * LANES
                    ]


def expert_specs(features, place, wide, low):
    specs = []
    if wide:
        block = pl.BlockSpec((1, features, LANES), lambda i, o: (place(i, o)[0], 0, place(i, o)[1]))
        specs += [block] * 4
    if low:
        block = pl.BlockSpec((1, LANES, features), lambda i, o: (*place(i, o), 0))
        specs += [block] * 2
    return specs


def expert_grads(order, first, last, total, x, o, gates, weights, kept):
    shared = total is None
    steps = last - first
    rows, features = x[0].shape
    aliased = len(kept)

    def fixed(*shape):
        return pl.BlockSpec(shape, lambda i, o: (0,) * len(shape))

    def stepped(*shape):
        return pl.BlockSpec((1, *shape), lambda i, o: (i, 0, 0))

    def placed(*shape):
        return pl.BlockSpec((1, *shape), lambda i, o: (i + first, 0, 0))

    specs = []
    for k in range(2):
        if shared:

            def picked(i, o, k=k):
                return 0, 2 * o[o.shape[0] - 1] + k

        else:

            def picked(i, o, k=k):
                return o[2 * (i + first) + k], o[o.shape[0] - 1]

        specs += expert_specs(features, picked, True, True)
    total = steps if shared else total
    return pl.pallas_call(
        functools.partial(expert_kernel, shared, aliased, first),
        grid_spec=pltpu.PrefetchScalarGridSpec(
            num_scalar_prefetch=1,
            grid=(steps,),
            in_specs=[fixed(rows, features)] * 4
            + [fixed(*gates.shape)]
            + specs
            + [pl.BlockSpec(memory_space=pl.ANY)] * aliased,
            out_specs=[stepped(2 * features, 3 * LANES)] * 2
            + [placed(rows, 4 * LANES), placed(rows, 2 * LANES)],
        ),
        out_shape=[jax.ShapeDtypeStruct((steps, 2 * features, 3 * LANES), BF16)] * 2
        + [
            jax.ShapeDtypeStruct((total, rows, 4 * LANES), BF16),
            jax.ShapeDtypeStruct((total, rows, 2 * LANES), BF16),
        ],
        input_output_aliases={18 + k: 2 + k for k in range(aliased)},
        compiler_params=params(40, "arbitrary"),
        cost_estimate=SMALL,
        name="expert_grads",
    )(order, *x, *o, gates, *weights, *weights, *kept)


def mix_kernel(back, group, order_ref, *refs):
    acts_ref, shared_ref = refs[0:2]
    each = 2 if back else 1
    count = 2 * group * each
    weights = refs[2 : 2 + count]
    shared = refs[2 + count : 2 + count + 2 * each]
    out_ref, total_ref = refs[2 + count + 2 * each :]
    step = pl.program_id(0)
    rows = out_ref.shape[0]
    tile = 512
    times = dot_nt if back else dot
    along = 1 if back else 0

    @pl.when(step == 0)
    def _():
        both = jnp.concatenate([w[0] for w in shared], axis=along)
        for t in range(rows // tile):
            at = slice(t * tile, (t + 1) * tile)
            total_ref[at, :] = times(shared_ref[0, at, :], both)

    both = jnp.concatenate([w[0] for w in weights], axis=along)
    for t in range(rows // tile):
        at = slice(t * tile, (t + 1) * tile)
        acts = jnp.concatenate([acts_ref[g, at, :] for g in range(group)], axis=1)
        total_ref[at, :] += times(acts, both)

    @pl.when(step == pl.num_programs(0) - 1)
    def _():
        out_ref[...] = total_ref[...].astype(out_ref.dtype)


def mix(back, dtype, order, acts, shared_acts, weights, shared_weights):
    pairs, rows, width = acts.shape
    features = weights[0].shape[1] if back else weights[0].shape[2]
    group = 4 if pairs % 4 == 0 else 1

    def spec(place):
        if back:
            return pl.BlockSpec((1, features, LANES), lambda i, o: (place(i, o)[0], 0, place(i, o)[1]))
        return pl.BlockSpec((1, LANES, features), lambda i, o: (*place(i, o), 0))

    def routed(k):
        return spec(lambda i, o: (o[2 * group * i + k], o[o.shape[0] - 1]))

    def common(k):
        return spec(lambda i, o: (0, 2 * o[o.shape[0] - 1] + k))

    return pl.pallas_call(
        functools.partial(mix_kernel, back, group),
        grid_spec=pltpu.PrefetchScalarGridSpec(
            num_scalar_prefetch=1,
            grid=(pairs // group,),
            in_specs=[
                pl.BlockSpec((group, rows, width), lambda i, o: (i, 0, 0)),
                pl.BlockSpec((1, rows, width), lambda i, o: (0, 0, 0)),
            ]
            + [routed(k) for k in range(2 * group) for _ in weights]
            + [common(k) for k in range(2) for _ in weights],
            out_specs=pl.BlockSpec((rows, features), lambda i, o: (0, 0)),
            scratch_shapes=[pltpu.VMEM((rows, features), F32)],
        ),
        out_shape=jax.ShapeDtypeStruct((rows, features), dtype),
        compiler_params=params(48, "arbitrary"),
        cost_estimate=SMALL,
        name="mix",
    )(order, acts, shared_acts, *weights * (2 * group), *shared_weights * 2)


def ring_of(size):
    return list(range(0, size, 2)) + list(range(1, size, 2))[::-1]


def unpack_kernel(aliased, plan_ref, *refs):
    chunks = refs[0:2]
    gate_ref, up_ref, down_ref = refs[2 + aliased : 5 + aliased]
    blocks = chunks[0].shape[1] // LANES

    def write(chunk_ref):
        gate_ref[0] = chunk_ref[0, :, 0:LANES].astype(F32)
        up_ref[0] = chunk_ref[0, :, LANES : 2 * LANES].astype(F32)
        for b in range(blocks):
            at = slice(b * LANES, (b + 1) * LANES)
            down_ref[0, :, at] = chunk_ref[0, at, 2 * LANES :].astype(F32)

    for k in range(2):
        pl.when(pl.program_id(1) == k)(lambda k=k: write(chunks[k]))


def unpack(plan, first, wave, chunks, shapes, outs):
    count, rows, width = chunks[0].shape
    chunk = pl.BlockSpec((1, rows, width), lambda i, d, n: (i, 0, 0))

    def place(i, d, n):
        block = n[n.shape[0] - 1]
        return n[first + 2 * i + d], 1 - block if wave else block

    def wide(i, d, n):
        expert, block = place(i, d, n)
        return (expert, 0, block)

    def low(i, d, n):
        expert, block = place(i, d, n)
        return (expert, block, 0)

    aliased = len(outs)
    return pl.pallas_call(
        functools.partial(unpack_kernel, aliased),
        grid_spec=pltpu.PrefetchScalarGridSpec(
            num_scalar_prefetch=1,
            grid=(count, 2),
            in_specs=[chunk, chunk] + [pl.BlockSpec(memory_space=pl.ANY)] * aliased,
            out_specs=[
                pl.BlockSpec((1, rows, LANES), wide),
                pl.BlockSpec((1, rows, LANES), wide),
                pl.BlockSpec((1, LANES, rows), low),
            ],
        ),
        out_shape=[jax.ShapeDtypeStruct(shape, F32) for shape in shapes],
        input_output_aliases={3 + k: k for k in range(aliased)},
        compiler_params=params(16, "arbitrary", "arbitrary"),
        cost_estimate=SMALL,
        name="unpack",
    )(plan, *chunks, *outs)


def late_chunk_kernel(plan_ref, pack_ref, *refs):
    *came, out_ref = refs
    if came:
        out_ref[...] = (came[0][...].astype(F32) + pack_ref[:, 0].astype(F32)).astype(BF16)
    else:
        out_ref[...] = pack_ref[:, 0]


def late_chunk(plan, at, pack, came):
    halves, _, rows, lanes = pack.shape
    spec = pl.BlockSpec((halves, rows, lanes), lambda i, n: (0, 0, 0))
    return pl.pallas_call(
        late_chunk_kernel,
        grid_spec=pltpu.PrefetchScalarGridSpec(
            num_scalar_prefetch=1,
            grid=(1,),
            in_specs=[pl.BlockSpec((halves, 1, rows, lanes), lambda i, n: (0, n[at], 0, 0))]
            + [spec] * len(came),
            out_specs=spec,
        ),
        out_shape=jax.ShapeDtypeStruct((halves, rows, lanes), BF16),
        compiler_params=params(16, "arbitrary"),
        cost_estimate=SMALL,
        name="late_chunk",
    )(plan, pack, *came)


def unpack_late_kernel(first_step, steps, plan_ref, *refs):
    chunks = refs[0 : 2 * steps]
    sgate, sup, sdown, query, key, value, out, all_ref = refs[2 * steps :]
    rows, features = chunks[0].shape[1], all_ref.shape[2]
    for k in range(2):
        for step in range(steps):
            at = plan_ref[first_step + 2 * step + k] * rows
            for c in range(2):
                all_ref[k, c, pl.ds(pl.multiple_of(at, rows), rows), :] = chunks[
                    steps * k + step
                ][c]
    flipped = plan_ref[plan_ref.shape[0] - 1] != 0
    for c in range(2):
        for b in range(14):
            lanes = slice(b % 7 * LANES, (b % 7 + 1) * LANES)
            first, second = all_ref[0, c, :, lanes], all_ref[1, c, :, lanes]
            if b >= 7:
                first, second = second, first
            block = jnp.where(flipped, second, first).astype(F32)
            if b < 6:
                at = slice((2 * c + b // 3) * LANES, (2 * c + b // 3 + 1) * LANES)
                if b % 3 < 2:
                    (sgate, sup)[b % 3][:, at] = block
                else:
                    for k in range(features // LANES):
                        here = slice(k * LANES, (k + 1) * LANES)
                        sdown[at, here] = block[here, :]
            elif b < 9:
                at = (GROUP_HEADS * c + b - 6) * LANES
                query[:, at : at + LANES] = block
            elif b < 11:
                (key, value)[b - 9][:, c * LANES : (c + 1) * LANES] = block
            else:
                at = (GROUP_HEADS * c + b - 11) * LANES
                out[at : at + LANES, :] = block.T


def unpack_late(plan, first_step, chunks, shapes):
    steps = len(chunks[0])
    halves, rows, lanes = chunks[0][0].shape
    spec = pl.BlockSpec(memory_space=pltpu.VMEM)
    return pl.pallas_call(
        functools.partial(unpack_late_kernel, first_step, steps),
        in_specs=[pl.BlockSpec(memory_space=pltpu.SMEM)] + [spec] * (2 * steps),
        out_specs=[spec] * len(shapes),
        out_shape=[jax.ShapeDtypeStruct(shape, F32) for shape in shapes],
        scratch_shapes=[pltpu.VMEM((2, halves, steps * rows, lanes), BF16)],
        compiler_params=params(48),
        cost_estimate=SMALL,
        name="unpack_late",
    )(plan, *chunks[0], *chunks[1])


def plans(ring, each):
    size = len(ring)
    rows = []
    for member in range(size):
        place = ring.index(member)
        for col in range(2):
            chunks = []
            for step in range(2 * size - 1):
                for which in range(2):
                    sign = 1 if which == col else -1
                    chunks.append((place - sign * step) % size)
            experts = []
            for start in (0, size - 1):
                for step in range(start, start + size):
                    for k in range(each):
                        for which in range(2):
                            second = col if which == 0 else 1 - col
                            experts.append(2 * each * chunks[2 * step + which] + each * second + k)
            rows.append(experts + chunks + [col])
    return np.asarray(rows, np.int32)


LATE_ROUND = 1


def add_rounded(left, right):
    return (left.astype(F32) + right.astype(F32)).astype(BF16)


def body(
    tokens_in,
    norm_gain_attn,
    w_query,
    w_key,
    w_value,
    w_out,
    norm_gain_ffn,
    w_gate,
    w_up,
    w_down,
    w_shared_gate,
    w_shared_up,
    w_shared_down,
    routes,
    gate_weights,
    seq_lengths,
    out_grad,
):
    row = lax.axis_index("row")
    col = lax.axis_index("col")
    dp = lax.axis_index("dp")
    dp_size = lax.axis_size("dp")
    local_rows, local_features = tokens_in.shape
    experts = w_gate.shape[0]
    group_width = GROUP_HEADS * DH
    col_ref = col.reshape(1)

    ring_size = min(8, dp_size)
    ring = ring_of(ring_size)
    starts = range(0, dp_size, ring_size)
    rights = [
        (g + ring[k], g + ring[(k + 1) % ring_size]) for g in starts for k in range(ring_size)
    ]
    lefts = [(b, a) for a, b in rights]
    routes_of = [
        [(2 * a, 2 * b) for a, b in ways[0]] + [(2 * a + 1, 2 * b + 1) for a, b in ways[1]]
        for ways in ((rights, lefts), (lefts, rights))
    ]
    experts_each = experts // (2 * ring_size)
    plan = jnp.asarray(plans(ring, experts_each))
    plan = lax.dynamic_slice(
        plan, (2 * (dp % ring_size) + col, jnp.int32(0)), (1, plan.shape[1])
    ).reshape(-1)

    def send(values, which):
        if ring_size == 1:
            return values
        return lax.ppermute(values, ("dp", "col"), routes_of[which])

    def chunk_at(step, which):
        return plan[2 * experts + 2 * step + which]

    def across_rings(values):
        if len(starts) == 1:
            return values
        peers = [[g + k for g in starts] for k in range(ring_size)]
        return lax.psum(values, "dp", axis_index_groups=peers)

    where = jnp.stack([row, seq_lengths[0], col])
    tokens_y = swap(tokens_in, "row")
    tokens_c = swap(tokens_in, "col")
    count = min(ring_size, 4)
    member = dp % count
    there, out_y = their_columns(
        jnp.stack([col, member]), w_query, w_key, w_value, w_out, count
    )
    gains = jnp.stack([norm_gain_attn, norm_gain_ffn])
    there = swap(there, "col")
    gains_c = swap(gains, "col")

    def project_half(own, other):
        return project(col_ref, own, other, gains, gains_c, w_query, w_key, w_value, there)

    near = project_half(tokens_in, tokens_c)
    gate_c = swap(w_gate, "col")
    out_y = swap(out_y, "row")
    tokens_y = after(tokens_y, near[2], out_y)
    tokens_yc = swap(tokens_y, "col")
    grad_y = swap(after(out_grad, tokens_y), "row")
    far = project_half(tokens_y, tokens_yc)
    shares = [out_y]
    for k in range(1, count):
        part = out_y if k < 3 else after(out_y, far[2])
        shares.append(lax.ppermute(part, "dp", [(m, m ^ k) for m in range(dp_size)]))
    where = after(where, grad_y, *shares)

    w_sgate, w_sup, w_sdown = w_shared_gate[None], w_shared_up[None], w_shared_down[None]
    up_c = swap(after(w_up, gate_c, tokens_yc), "col")

    attended = attend(where, near[2], far[2])
    attended_y = swap(attended, "row")
    attended_c = swap(attended, "col")
    out_c = swap(after(w_out, tokens_yc), "col")
    before = hidden_before(
        where,
        [tokens_in, tokens_c, tokens_y, tokens_yc],
        [attended, attended_c],
        w_out,
        out_c,
    )
    down_c = swap(after(w_down, tokens_yc), "col")
    attended_y = after(attended_y, before[0])
    out_y = join(member, *shares)
    out_yc = swap(out_y, "col")
    attended_yc = swap(attended_y, "col")
    grad_own = join(row, out_grad, grad_y)
    grad_other = swap(grad_own, "col")
    hidden, x_own, x_other, scale_ffn = hidden_after(
        where, before, [attended_y, attended_yc], out_y, out_yc, gains, gains_c
    )
    sgate_c, sup_c, sdown_c = (
        swap(after(w, attended_yc), "col") for w in (w_sgate, w_sup, w_sdown)
    )

    choices = jnp.arange(experts, dtype=jnp.int32)[:, None]
    dense = sum(
        jnp.where(routes[:, k][None, :] == choices, gate_weights[:, k][None, :], 0.0)
        for k in range(routes.shape[1])
    )
    gates = []
    for _ in range(3):
        gates.append(lax.reduce_precision(dense, 8, 7))
        dense = dense - gates[-1]
    gates = jnp.concatenate(gates, axis=0).astype(BF16)

    each = experts_each
    order = plan
    pairs_total = experts // 2
    routed = [w_gate, w_up, gate_c, up_c, w_down, down_c]
    shared = [w_sgate, w_sup, sgate_c, sup_c, w_sdown, sdown_c]

    def run(first, last, order, kept):
        return expert_grads(
            order,
            first,
            last,
            pairs_total,
            [x_own, x_other],
            [grad_own, grad_other],
            gates,
            routed,
            kept,
        )

    first = run(0, each, order, ())
    kept = first[2:]
    sums = [first[0], first[1]]
    runs = {}
    mixed = {}

    def work_experts(first, last):
        def work(order):
            nonlocal kept
            result = run(first, last, order, tuple(kept))
            kept = result[2:]
            for at in range(first, last):
                runs[at] = (result[0], result[1], at - first)
            return kept[0]

        return work

    def work_shared(order):
        runs["shared"] = expert_grads(
            order, 0, 1, None, [x_own, x_other], [grad_own, grad_other], gates, shared, ()
        )
        return runs["shared"][2]

    def work_mix(back, half):
        def work(order):
            pick = slice(2 * half, 2 * half + 2) if back else slice(4 + half, 5 + half)
            mixed[back, half] = mix(
                back,
                BF16 if half else F32,
                order,
                kept[0 if back else 1],
                runs["shared"][2 if back else 3],
                routed[pick],
                shared[pick],
            )
            return mixed[back, half]

        return work

    start = row * local_rows

    def my_rows(values):
        return lax.dynamic_slice_in_dim(values, start, local_rows, axis=0)

    def their_rows(values):
        return lax.dynamic_slice_in_dim(values, local_rows - start, local_rows, axis=0)

    normed = {}

    def work_hidden(order):
        normed_grad = mixed[True, 0] + swap_halves(mixed[True, 1]).astype(F32)
        came = swap(normed_grad.astype(BF16), "row")
        normed_grad = normed_grad + after(came, order).astype(F32)
        scaled = normed_grad * norm_gain_ffn
        products = jnp.sum(scaled * hidden, axis=1, keepdims=True)
        mean = (products + swap(products, "col")) / D
        normed["gain"] = jnp.sum(my_rows(normed_grad * hidden * scale_ffn), axis=0)
        normed["hidden"] = (
            grad_own.astype(F32) + scale_ffn * scaled - hidden * scale_ffn**3 * mean
        )
        normed["grad"] = normed["hidden"].astype(BF16)
        normed["grad_c"] = swap_halves(normed["grad"])
        return normed["grad"]

    def work_attend(order):
        normed["qkv"] = attend_back(
            after(where, order), near[2], far[2], normed["grad"], normed["grad_c"], w_out, out_c
        )
        return normed["qkv"]

    tasks = [work_experts(at, at + each) for at in range(each, pairs_total, each)]
    tasks += [work_shared, work_mix(True, 1), work_mix(True, 0), work_mix(False, 1), work_mix(False, 0)]
    tasks += [None] * (2 * ring_size - 3 - len(tasks)) + [work_hidden, work_attend]
    got = [None, None]
    if ring_size > 1:
        got[0] = send(sums[0], 0)
        tasks.pop(0)(after(order, *sums))
        got[1] = send(after(sums[1], kept[0]), 1)
    for s in range(1, ring_size):
        for k in range(2):
            last = sums
            task = tasks.pop(0) if tasks else None
            if task:
                last = [task(after(order, *last))]
            got[k] = after(got[k], *last)
            parts = [runs[at] for at in range(each * s, each * s + each)]
            mine = [p[k][p[2] : p[2] + 1] for p in parts]
            mine = mine[0] if each == 1 else jnp.concatenate(mine, axis=0)
            sums[k] = add_rounded(got[k], mine)
            if s + 1 < ring_size:
                got[k] = send(sums[k], k)
    for task in tasks:
        if task:
            task(after(order, *sums))
    sums = [across_rings(total) for total in sums]
    waves = [[total[:, :local_features] for total in sums]]
    crossed = [swap(total[:, local_features:], "col") for total in sums]
    waves.append([crossed[1], crossed[0]])

    hidden_grad, attn_grad, attn_grad_c = normed["hidden"], normed["grad"], normed["grad_c"]
    gain_ffn_part, qkv_grad = normed["gain"], normed["qkv"]
    packs = late_grads(
        where,
        near[0:2],
        far[0:2],
        qkv_grad,
        attended,
        attn_grad,
        attn_grad_c,
        runs["shared"][0:2],
    )

    packs = [
        pack.reshape(2, ring_size, local_features // ring_size, pack.shape[2]) for pack in packs
    ]
    chunks_first = 2 * experts
    late = [late_chunk(plan, chunks_first + k, packs[k], ()) for k in range(2)]
    late_out = [[], []]
    late_done = 0
    late_total = 2 * (ring_size - 1)

    def late_turn():
        totals = [across_rings(values) for values in late]
        others = [swap(values[1], "col") for values in totals]
        for k in range(2):
            late[k] = in_order(totals[k][0:1], others[1 - k][None], col, 0)
            late_out[k].append(late[k])

    def late_finish(k, values):
        if late_done < ring_size:
            at = chunks_first + 2 * late_done + k
            late[k] = late_chunk(plan, at, packs[k], (values,))
        else:
            late[k] = values
            late_out[k].append(values)

    shapes = [w_gate.shape, w_up.shape, w_down.shape]
    placed = ()

    def place_chunks(wave, step, chunks, placed):
        return unpack(plan, experts + 2 * each * step, wave, chunks, shapes, placed)

    if late_total == 0:
        late_turn()
    rounds = [(wave, step) for wave in range(2) for step in range(ring_size - 1)]
    late_got = None
    last = list(sums)
    for number, (wave, step) in enumerate(rounds):
        if step == 0:
            came = list(got) if number else None
            got = list(waves[wave])
        late_done += late_got is not None
        chunks = [None, None]
        for k in range(2):
            chunks[k] = after(got[k], *last)
            got[k] = send(chunks[k], k)
            last = [chunks[k]]
            if late_got is not None:
                late_finish(k, after(late_got[k], *last))
                last = [late[k]]
        if late_got is not None and late_done == ring_size - 1:
            late_turn()
        if number >= LATE_ROUND and late_done < late_total:
            late_got = [send(after(late[k], *chunks), k) for k in range(2)]
        else:
            late_got = None
        if step == 0 and number:
            placed = place_chunks(0, ring_size - 1, came, placed)
        placed = place_chunks(wave, step, chunks, placed)
        last = placed[0:1]
        if number == LATE_ROUND + 3:
            qkv_grad = after(qkv_grad, *last)
    if rounds:
        placed = place_chunks(1, ring_size - 1, [after(got[k], *last) for k in range(2)], placed)
        last = placed[0:1]
    while late_got is not None:
        late_done += 1
        for k in range(2):
            late_finish(k, after(late_got[k], *last))
        if late_done == ring_size - 1:
            late_turn()
        late_got = [send(late[k], k) for k in range(2)] if late_done < late_total else None
    if not rounds:
        for wave in range(2):
            placed = place_chunks(wave, 0, waves[wave], placed)
    gate_grad, up_grad, down_grad = placed
    shapes = [w.shape for w in (w_shared_gate, w_shared_up, w_shared_down)]
    shapes += [w.shape for w in (w_query, w_key, w_value, w_out)]
    finals = unpack_late(plan, chunks_first + late_total, late_out, shapes)
    shared_gate_grad, shared_up_grad, shared_down_grad = finals[0:3]
    query_grad, key_grad, value_grad, out_proj_grad = finals[3:7]

    ffn_sum = mixed[False, 0] + swap(mixed[False, 1], "col").astype(F32)
    ffn_rows = my_rows(ffn_sum) + swap(their_rows(ffn_sum).astype(BF16), "row").astype(F32)
    block_out = (my_rows(hidden) + ffn_rows).astype(BF16)

    here = jnp.concatenate(
        [halves(w, 1, col)[0] for w in (w_query, w_key, w_value)], axis=1
    )
    tokens_back = dot_nt(qkv_grad, here) + swap(
        dot_nt(qkv_grad, there).astype(BF16), "col"
    ).astype(F32)
    tokens_back = my_rows(tokens_back) + swap(
        their_rows(tokens_back).astype(BF16), "row"
    ).astype(F32)
    scale_attn = near[3]
    tokens_f32 = tokens_in.astype(F32)
    gain_attn_part = jnp.sum(tokens_back * tokens_f32 * scale_attn, axis=0)
    scaled = tokens_back * norm_gain_attn
    products = jnp.sum(scaled * tokens_f32, axis=1, keepdims=True)
    mean = (products + swap(products, "col")) / D
    tokens_grad = (
        my_rows(hidden_grad) + scale_attn * scaled - tokens_f32 * scale_attn**3 * mean
    ).astype(BF16)

    gain_parts = jnp.stack([gain_attn_part, gain_ffn_part])
    bit = 1
    while bit < ring_size:
        pairs = [(g + k, g + (k ^ bit)) for g in starts for k in range(ring_size)]
        gain_parts = gain_parts + lax.ppermute(gain_parts, "dp", pairs)
        bit *= 2
    gain_parts = across_rings(gain_parts + swap(gain_parts, "row"))

    return (
        block_out,
        tokens_grad,
        gain_parts[0],
        query_grad,
        key_grad,
        value_grad,
        out_proj_grad,
        gain_parts[1],
        gate_grad,
        up_grad,
        down_grad,
        shared_gate_grad,
        shared_up_grad,
        shared_down_grad,
    )


def solution(mesh):
    in_specs = (
        P(("dp", "row"), "col"),
        P("col"),
        P("col", "row"),
        P("col", "row"),
        P("col", "row"),
        P("row", "col"),
        P("col"),
        P(None, "col", "row"),
        P(None, "col", "row"),
        P(None, "row", "col"),
        P("col", "row"),
        P("col", "row"),
        P("row", "col"),
        P("dp", None),
        P("dp", None),
        P("dp"),
        P(("dp", "row"), "col"),
    )
    out_specs = (
        P(("dp", "row"), "col"),
        P(("dp", "row"), "col"),
        P("col"),
        P("col", "row"),
        P("col", "row"),
        P("col", "row"),
        P("row", "col"),
        P("col"),
        P(None, "col", "row"),
        P(None, "col", "row"),
        P(None, "row", "col"),
        P("col", "row"),
        P("col", "row"),
        P("row", "col"),
    )
    return jax.shard_map(body, mesh=mesh, in_specs=in_specs, out_specs=out_specs, check_vma=False)
```
